32 devices in a mesh: dp: 8 (over y, x, core), mp: 4 (over z).
Axes of the slice: x: 2, y: 2, z: 4, core: 2. Of those that a mesh axis runs over, the one named last changes fastest.
Arguments:
- pixels: bfloat16 [8, 64, 64, 1024], P(None, 'dp', None, 'mp'), may hold values from -6 to 6
- counts: int32 [8], replicated, may hold values from 1 to 1, as said below
- kernel_one: bfloat16 [3, 3, 1024, 512], P(None, None, None, 'mp'), may hold values from -0.0625 to 0.0625
- bias_one: float32 [512], P('mp'), may hold values from -4 to 4
- kernel_two: bfloat16 [3, 3, 512, 512], P(None, None, None, 'mp'), may hold values from -0.09375 to 0.09375
- bias_two: float32 [512], P('mp'), may hold values from -4 to 4
- kernel_three: bfloat16 [3, 3, 512, 512], P(None, None, None, 'mp'), may hold values from -0.09375 to 0.09375
- bias_three: float32 [512], P('mp'), may hold values from -4 to 4
- out_kernel: bfloat16 [512, 2048], P(None, 'mp'), may hold values from -16 to 16
- identity_kernel: bfloat16 [1024, 2048], P(None, 'mp'), may hold values from -0.1875 to 0.1875
- identity_bias: float32 [2048], P('mp'), may hold values from -4 to 4
- cotangent: bfloat16 [8, 32, 32, 2048], P('dp', None, None, 'mp'), may hold values from -6 to 6
Outputs:
- block_out: bfloat16 [8, 32, 32, 2048], P('dp', None, None, 'mp')
- pixels_grad: bfloat16 [8, 64, 64, 1024], P(None, 'dp', None, 'mp')
- kernel_one_grad: float32 [3, 3, 1024, 512], P(None, None, None, 'mp')
- bias_one_grad: float32 [512], P('mp')
- kernel_two_grad: float32 [3, 3, 512, 512], P(None, None, None, 'mp')
- bias_two_grad: float32 [512], P('mp')
- kernel_three_grad: float32 [3, 3, 512, 512], P(None, None, None, 'mp')
- bias_three_grad: float32 [512], P('mp')
- out_kernel_grad: float32 [512, 2048], P(None, 'mp')
- identity_kernel_grad: float32 [1024, 2048], P(None, 'mp')
- identity_bias_grad: float32 [2048], P('mp')
The draws below stay inside these ranges and needn't reach their ends.
Inputs may be any that keep to these rules, and one draw needn't show every extreme that they name: counts[d] is the number of images in the slots of index d of dp; at least one index holds exactly 1.
All inputs are finite; a program needn't handle non-finite values.
Results may differ from the reference program's by a relative error of at most 0.012.
Values may be sent and summed in bfloat16 or wider, within the bound.
No kernel may reach another device: no remote copies, remote signals or barrier semaphores. Data moves between devices by JAX's collectives and lax.ppermute only.
A program may use at most 128 MiB of HBM per device.

```python
import jax
import jax.numpy as jnp
from jax import lax

CIN = 1024
HID = 512
COUT = 2048
GRID = 64
CAP = 1
IMAGES = 8
N_DP = 8


def draw_counts(key, part):
    key = jax.random.fold_in(key, 11)
    first, second = jax.random.split(key)
    drawn = jax.random.randint(first, (N_DP,), 1, CAP + 1)
    chosen = jax.random.randint(second, (), 0, N_DP)
    return jnp.where(jnp.arange(N_DP) == chosen, CAP, drawn).astype(jnp.int32)


def steps_of(rng, extent, cuts, least, high):
    def one(dim, shards_of):
        steps = jax.random.uniform(jax.random.fold_in(jax.random.fold_in(rng, 6), dim), (shards_of,), jnp.float32, least / len(cuts), high / len(cuts))
        return jnp.repeat(jnp.exp(steps), extent[dim] // shards_of).reshape((-1,) + (1,) * (len(extent) - dim - 1))

    level = one(*cuts[0])
    for cut in cuts[1:]:
        level = level * one(*cut)
    return level


def noise(own_key, extent, deviation, limit, shards=(), kind=jnp.bfloat16):
    values = deviation * jax.random.normal(own_key, extent, jnp.float32)
    if shards:
        values = values * steps_of(own_key, extent, shards, -0.22, 0.18)
    return jnp.clip(values, -limit, limit).astype(kind)


def setup_inputs(seed: int = 0) -> dict:
    keys = jax.random.split(jax.random.key(seed), 13)
    pixels = noise(keys[0], (IMAGES, GRID, GRID, CIN), 1.0, 6.0, ((1, 8), (3, 4)))
    counts = draw_counts(jax.random.fold_in(keys[12], 71), 0)
    kernel_one = noise(keys[2], (3, 3, CIN, HID), (9 * CIN) ** -0.5, 0.0625, ((3, 4),))
    bias_one = noise(keys[3], (HID,), 1.0, 4.0, ((0, 4),), jnp.float32)
    kernel_two = noise(keys[4], (3, 3, HID, HID), (9 * HID) ** -0.5, 0.09375, ((3, 4),))
    bias_two = noise(keys[5], (HID,), 1.0, 4.0, ((0, 4),), jnp.float32)
    kernel_three = noise(keys[6], (3, 3, HID, HID), (9 * HID) ** -0.5, 0.09375, ((3, 4),))
    bias_three = noise(keys[7], (HID,), 1.0, 4.0, ((0, 4),), jnp.float32)
    out_kernel = noise(keys[8], (HID, COUT), (64.0 * HID ** -0.5), 16.0, ((1, 4),))
    identity_kernel = noise(keys[9], (CIN, COUT), CIN ** -0.5, 0.1875, ((1, 4),))
    identity_bias = noise(keys[10], (COUT,), 1.0, 4.0, ((0, 4),), jnp.float32)
    cotangent = noise(keys[11], (IMAGES, GRID // 2, GRID // 2, COUT), 1.0, 6.0, ((0, 8), (3, 4)))
    return dict(pixels=pixels, counts=counts, kernel_one=kernel_one, bias_one=bias_one, kernel_two=kernel_two, bias_two=bias_two, kernel_three=kernel_three, bias_three=bias_three, out_kernel=out_kernel, identity_kernel=identity_kernel, identity_bias=identity_bias, cotangent=cotangent)


post_gain = 0.015625

@jax.custom_vjp
def low(v):
    return lax.optimization_barrier(v.astype(jnp.bfloat16)).astype(jnp.float32)

@jax.custom_vjp
def low_back(v):
    return v

def low_keep(v):
    return (low(v), None)

def low_pass(kept, grad):
    return (grad,)

def back_keep(v):
    return (v, None)

def back_low(kept, grad):
    return (low(grad),)
low.defvjp(low_keep, low_pass)
low_back.defvjp(back_keep, back_low)

def convolve(values, kernel):
    return lax.conv_general_dilated(values, kernel, (1, 1), 'SAME', dimension_numbers=('NHWC', 'HWIO', 'NHWC'), precision=lax.Precision.HIGHEST)

def project(values, kernel):
    return jnp.einsum('nhwc,cd->nhwd', values, kernel, precision=lax.Precision.HIGHEST)

def forward(pixels, kernel_one, bias_one, kernel_two, bias_two, kernel_three, bias_three, out_kernel, identity_kernel, identity_bias, valid):
    images = pixels.shape[0]
    side = pixels.shape[1] // 2
    pooled = lax.optimization_barrier(jnp.mean(pixels.reshape(images, side, 2, side, 2, pixels.shape[3]), axis=(2, 4)))
    inputs = low_back(low(pooled))
    act_zero = low(jax.nn.gelu(inputs))
    pre_one = low_back(convolve(act_zero, kernel_one) + bias_one)
    act_one = low(jax.nn.gelu(pre_one))
    pre_two = low_back(convolve(act_one, kernel_two) + bias_two)
    act_two = low(jax.nn.gelu(pre_two))
    pre_three = low_back(convolve(act_two, kernel_three) + bias_three)
    act_three = low(jax.nn.gelu(pre_three))
    identity = project(inputs, identity_kernel)
    branch = project(act_three, out_kernel)
    return (identity + identity_bias + post_gain * branch) * valid

def reference(pixels, counts, kernel_one, bias_one, kernel_two, bias_two, kernel_three, bias_three, out_kernel, identity_kernel, identity_bias, cotangent):
    slots = jnp.arange(IMAGES, dtype=jnp.int32)
    owner = slots // CAP
    valid = (slots % CAP < counts[owner]).astype(jnp.float32)[:, None, None, None]
    params = (pixels.astype(jnp.float32), kernel_one.astype(jnp.float32), bias_one.astype(jnp.float32), kernel_two.astype(jnp.float32), bias_two.astype(jnp.float32), kernel_three.astype(jnp.float32), bias_three.astype(jnp.float32), out_kernel.astype(jnp.float32), identity_kernel.astype(jnp.float32), identity_bias.astype(jnp.float32))

    def apply(*values):
        return forward(*values, valid)
    result, pull = jax.vjp(apply, *params)
    grads = pull(cotangent.astype(jnp.float32))
    return (result.astype(jnp.bfloat16), grads[0].astype(jnp.bfloat16), grads[1], grads[2], grads[3], grads[4], grads[5], grads[6], grads[7], grads[8], grads[9])
```

```python
import jax
import jax.numpy as jnp
from jax import lax
from jax.sharding import PartitionSpec as P

post_gain = 0.015625


def convolve(values, kernel):
    return lax.conv_general_dilated(
        values,
        kernel,
        (1, 1),
        "SAME",
        dimension_numbers=("NHWC", "HWIO", "NHWC"),
        preferred_element_type=jnp.float32,
    )


def transpose_conv(grad_pre, kernel):
    flipped = jnp.transpose(kernel[::-1, ::-1], (0, 1, 3, 2))
    return convolve(grad_pre, flipped)


def kernel_grad(values, grad_pre):
    side = values.shape[1]
    width = values.shape[2]
    padded = jnp.pad(values, ((0, 0), (1, 1), (1, 1), (0, 0)))
    flat_grad = grad_pre.reshape(-1, grad_pre.shape[3])
    layers = []
    for shift_y in range(3):
        across = []
        for shift_x in range(3):
            window = padded[:, shift_y : shift_y + side, shift_x : shift_x + width, :].reshape(
                -1, values.shape[3]
            )
            across.append(
                jnp.einsum("pi,po->io", window, flat_grad, preferred_element_type=jnp.float32)
            )
        layers.append(jnp.stack(across))
    return jnp.stack(layers)


def gelu_back(pre_value, grad):
    return jax.vjp(jax.nn.gelu, pre_value)[1](grad)[0]


def gather_mp(shard, members):
    place = lax.axis_index("mp")
    chans = shard.shape[3]
    up = [shard]
    down = [shard]
    for step in range(1, members):
        up.append(lax.ppermute(up[-1], "mp", [(i, i + 1) for i in range(step - 1, members - 1)]))
        down.append(lax.ppermute(down[-1], "mp", [(i + 1, i) for i in range(members - step)]))
    full = jnp.zeros(shard.shape[:3] + (members * chans,), shard.dtype)
    full = lax.dynamic_update_slice(full, shard, (0, 0, 0, place * chans))
    for step in range(1, members):
        block = jnp.where(place >= step, up[step], down[members - step])
        owner = lax.rem(place - step + members, members)
        full = lax.dynamic_update_slice(full, block, (0, 0, 0, owner * chans))
    return full


def scatter_mp(partial_value, members):
    place = lax.axis_index("mp")
    chans = partial_value.shape[3] // members

    def part(owner):
        owner = jnp.clip(owner, 0, members - 1)
        return lax.dynamic_slice_in_dim(partial_value, owner * chans, chans, 3)

    up = None
    down = None
    for step in range(1, members):
        rise = part(place + members - step)
        fall = part(place - members + step)
        if step > 1:
            rise = rise + up.astype(jnp.float32)
            fall = fall + down.astype(jnp.float32)
        up = lax.ppermute(
            rise.astype(jnp.bfloat16), "mp", [(i, i + 1) for i in range(step)]
        )
        down = lax.ppermute(
            fall.astype(jnp.bfloat16),
            "mp",
            [(i + 1, i) for i in range(members - 1 - step, members - 1)],
        )
    return part(place) + up.astype(jnp.float32) + down.astype(jnp.float32)


def sum_dp(values):
    narrow = lax.psum(tuple(v.astype(jnp.bfloat16) for v in values), "dp")
    return tuple(v.astype(jnp.float32) for v in narrow)


def layer_back(grad_act, pre_value, full_in, kernel):
    grad_pre = gelu_back(pre_value, grad_act).astype(jnp.bfloat16)
    bias_grad = jnp.sum(grad_pre.astype(jnp.float32), axis=(0, 1, 2))
    weight_grad = kernel_grad(full_in, grad_pre)
    grad_in = transpose_conv(grad_pre, kernel)
    return (grad_in, weight_grad, bias_grad)


def local(
    pixels,
    counts,
    kernel_one,
    bias_one,
    kernel_two,
    bias_two,
    kernel_three,
    bias_three,
    out_kernel,
    identity_kernel,
    identity_bias,
    cotangent,
):
    images, rows, width, chans = pixels.shape
    pooled = jnp.mean(
        pixels.astype(jnp.float32).reshape(images, rows // 2, 2, width // 2, 2, chans), axis=(2, 4)
    ).astype(jnp.bfloat16)
    local_x = lax.all_to_all(pooled, "dp", split_axis=0, concat_axis=1, tiled=True)
    slots = local_x.shape[0]
    own_count = lax.dynamic_index_in_dim(counts, lax.axis_index("dp"), 0, keepdims=False)
    live = jnp.arange(slots, dtype=jnp.int32) < own_count
    valid = live.astype(jnp.float32)[:, None, None, None]
    members = lax.axis_size("mp")
    full_x = gather_mp(local_x, members)
    full_float = full_x.astype(jnp.float32)
    act_zero = jax.nn.gelu(full_float).astype(jnp.bfloat16)
    pre_one = convolve(act_zero, kernel_one) + bias_one
    act_one = jax.nn.gelu(pre_one).astype(jnp.bfloat16)
    full_one = gather_mp(act_one, members)
    pre_two = convolve(full_one, kernel_two) + bias_two
    act_two = jax.nn.gelu(pre_two).astype(jnp.bfloat16)
    full_two = gather_mp(act_two, members)
    pre_three = convolve(full_two, kernel_three) + bias_three
    act_three = jax.nn.gelu(pre_three).astype(jnp.bfloat16)
    full_three = gather_mp(act_three, members)
    identity = jnp.einsum(
        "nhwc,cd->nhwd", full_x, identity_kernel, preferred_element_type=jnp.float32
    )
    branch = jnp.einsum("nhwc,cd->nhwd", full_three, out_kernel, preferred_element_type=jnp.float32)
    block_out = ((identity + identity_bias + post_gain * branch) * valid).astype(jnp.bfloat16)
    grad_out = cotangent * valid.astype(jnp.bfloat16)
    identity_bias_grad = jnp.sum(grad_out.astype(jnp.float32), axis=(0, 1, 2))
    identity_kernel_grad = jnp.einsum(
        "nhwc,nhwd->cd", full_x, grad_out, preferred_element_type=jnp.float32
    )
    out_kernel_grad = post_gain * jnp.einsum(
        "nhwc,nhwd->cd", full_three, grad_out, preferred_element_type=jnp.float32
    )
    grad_full_three = post_gain * jnp.einsum(
        "nhwd,cd->nhwc", grad_out, out_kernel, preferred_element_type=jnp.float32
    )
    grad_act_three = scatter_mp(grad_full_three, members)
    grad_next, kernel_three_grad, bias_three_grad = layer_back(
        grad_act_three, pre_three, full_two, kernel_three
    )
    grad_act_two = scatter_mp(grad_next, members)
    grad_next, kernel_two_grad, bias_two_grad = layer_back(
        grad_act_two, pre_two, full_one, kernel_two
    )
    grad_act_one = scatter_mp(grad_next, members)
    grad_act_zero, kernel_one_grad, bias_one_grad = layer_back(
        grad_act_one, pre_one, act_zero, kernel_one
    )
    grad_full_x = gelu_back(full_float, grad_act_zero) + jnp.einsum(
        "nhwd,cd->nhwc", grad_out, identity_kernel, preferred_element_type=jnp.float32
    )
    grad_local_x = scatter_mp(grad_full_x, members).astype(jnp.bfloat16)
    grad_pooled = lax.all_to_all(grad_local_x, "dp", split_axis=1, concat_axis=0, tiled=True)
    quarter = grad_pooled.astype(jnp.float32) * 0.25
    pool_rows = quarter.shape[1]
    pool_cols = quarter.shape[2]
    widened = jnp.broadcast_to(
        quarter[:, :, None, :, None, :], (images, pool_rows, 2, pool_cols, 2, chans)
    )
    pixels_grad = widened.reshape(images, rows, width, chans).astype(jnp.bfloat16)
    outer = sum_dp((out_kernel_grad, identity_kernel_grad))
    third = sum_dp((kernel_three_grad,))
    second = sum_dp((kernel_two_grad,))
    first = sum_dp((kernel_one_grad,))
    small = lax.psum((bias_one_grad, bias_two_grad, bias_three_grad, identity_bias_grad), "dp")
    return (
        block_out,
        pixels_grad,
        first[0],
        small[0],
        second[0],
        small[1],
        third[0],
        small[2],
        outer[0],
        outer[1],
        small[3],
    )


def solution(mesh):
    return jax.shard_map(
        local,
        mesh=mesh,
        in_specs=(
            P(None, "dp", None, "mp"),
            P(),
            P(None, None, None, "mp"),
            P("mp"),
            P(None, None, None, "mp"),
            P("mp"),
            P(None, None, None, "mp"),
            P("mp"),
            P(None, "mp"),
            P(None, "mp"),
            P("mp"),
            P("dp", None, None, "mp"),
        ),
        out_specs=(
            P("dp", None, None, "mp"),
            P(None, "dp", None, "mp"),
            P(None, None, None, "mp"),
            P("mp"),
            P(None, None, None, "mp"),
            P("mp"),
            P(None, None, None, "mp"),
            P("mp"),
            P(None, "mp"),
            P(None, "mp"),
            P("mp"),
        ),
        check_vma=False,
    )
```

```python
import functools

import jax
import jax.numpy as jnp
from jax import lax
from jax.experimental import pallas as pl
from jax.experimental.pallas import tpu as pltpu
from jax.sharding import PartitionSpec as P

post_gain = 0.015625
slope = 0.7978845608028654
cubic = 0.044715
bf16 = jnp.bfloat16
f32 = jnp.float32
NT = (((1,), (1,)), ((), ()))
TN = (((0,), (0,)), ((), ()))
NN = (((1,), (0,)), ((), ()))


def dot(left, right, dims=NN):
    return lax.dot_general(left, right, dims, preferred_element_type=f32)


def gelu(value):
    inner = jnp.tanh(slope * (value + cubic * value * value * value))
    return 0.5 * value * (1.0 + inner)


def gelu_slope(value):
    square = value * value
    inner = jnp.tanh(slope * value * (1.0 + cubic * square))
    climb = slope * (1.0 + 3.0 * cubic * square)
    return 0.5 * (1.0 + inner) + 0.5 * value * (1.0 - inner * inner) * climb


def params(vmem=48):
    return pltpu.CompilerParams(vmem_limit_bytes=vmem << 20)


def cost(flops, moved):
    return pl.CostEstimate(flops=int(flops), bytes_accessed=int(moved), transcendentals=0)


def struct(shape, kind):
    return jax.ShapeDtypeStruct(shape, kind)


def pool_body(x_ref, out_ref):
    rows, width, chans = x_ref.shape[1:]
    half = width // 2
    pixel = lax.broadcasted_iota(jnp.int32, (half, 2 * width), 1)
    place = lax.broadcasted_iota(jnp.int32, (half, 2 * width), 0)
    inside = (lax.rem(pixel, width) >= 2 * place) & (lax.rem(pixel, width) < 2 * place + 2)
    pick = jnp.where(inside, 0.25, 0.0).astype(bf16)
    for row in range(rows // 2):
        window = x_ref[0, 2 * row : 2 * row + 2].reshape(2 * width, chans)
        out_ref[0, row * half : (row + 1) * half, :] = dot(pick, window).astype(bf16)


def pool(pixels):
    images, rows, width, chans = pixels.shape
    pooled = rows * width // 4
    return pl.pallas_call(
        pool_body,
        grid=(images,),
        in_specs=[pl.BlockSpec((1, rows, width, chans), lambda i: (i, 0, 0, 0))],
        out_specs=pl.BlockSpec((1, pooled, chans), lambda i: (i, 0, 0)),
        out_shape=struct((images, pooled, chans), bf16),
        compiler_params=params(),
        cost_estimate=cost(0, pixels.size * 2.5),
        name="pool",
    )(pixels)


def widen_body(g_ref, out_ref):
    rows, width, chans = out_ref.shape[1:]
    half = width // 2
    pixel = lax.broadcasted_iota(jnp.int32, (width, half), 0)
    place = lax.broadcasted_iota(jnp.int32, (width, half), 1)
    inside = (pixel >= 2 * place) & (pixel < 2 * place + 2)
    pick = jnp.where(inside, 0.25, 0.0).astype(bf16)
    for row in range(rows // 2):
        wide = dot(pick, g_ref[0, row * half : (row + 1) * half, :]).astype(bf16)
        out_ref[0, 2 * row] = wide
        out_ref[0, 2 * row + 1] = wide


def widen(grad, rows, width):
    images, _, chans = grad.shape
    return pl.pallas_call(
        widen_body,
        grid=(images,),
        in_specs=[pl.BlockSpec((1,) + grad.shape[1:], lambda i: (i, 0, 0))],
        out_specs=pl.BlockSpec((1, rows, width, chans), lambda i: (i, 0, 0, 0)),
        out_shape=struct((images, rows, width, chans), bf16),
        compiler_params=params(),
        cost_estimate=cost(0, grad.size * 10),
        name="widen",
    )(grad)


def lanes(blocks):
    return blocks[0] if len(blocks) == 1 else jnp.concatenate(blocks, axis=1)


def conv_body(side, steps, first, x_ref, w_ref, b_ref, *rest):
    if first:
        zero_ref, pre_ref, act_ref, acc = rest
    else:
        pre_ref, act_ref, acc = rest
    step = pl.program_id(0)
    pixels = x_ref.shape[1]
    outs = w_ref.shape[2]

    @pl.when(step == 0)
    def _():
        acc[...] = jnp.zeros_like(acc)

    weights = [lanes([w_ref[3 * y + x] for y in range(3)]) for x in range(3)]
    weights = lanes(weights)
    block = 8 * side
    for begin in range(0, pixels, block):
        values = lanes([x_ref[j, begin : begin + block, :] for j in range(x_ref.shape[0])])
        if first:
            values = gelu(values.astype(f32)).astype(bf16)
            zero_ref[0, begin : begin + block, :] = values
        product = dot(values, weights)
        for x in range(3):
            for y in range(3):
                at = begin + side * (2 - y)
                col = (3 * x + y) * outs
                acc[x, at : at + block, :] += product[:, col : col + outs]

    @pl.when(step == steps - 1)
    def _():
        spot = lax.broadcasted_iota(jnp.int32, (block, outs), 0)
        column = lax.rem(spot, side)
        for begin in range(0, pixels, block):
            at = begin + side
            left = pltpu.roll(acc[0, at : at + block, :], 1, 0)
            right = pltpu.roll(acc[2, at : at + block, :], block - 1, 0)
            pre = acc[1, at : at + block, :] + b_ref[...]
            pre = pre + jnp.where(column > 0, left, 0.0)
            pre = pre + jnp.where(column < side - 1, right, 0.0)
            pre_ref[begin : begin + block, :] = pre
            act = gelu(pre).astype(bf16)
            for j in range(act_ref.shape[0]):
                act_ref[j, begin : begin + block, :] = act


def conv(side, gathered, kernel, bias, first=False):
    members, pixels, chans = gathered.shape
    taps, depth, outs = kernel.shape
    joined = max(1, 256 // chans)
    steps = members // joined
    out_shape = [struct((pixels, outs), f32), struct((members, pixels, outs), bf16)]
    out_specs = [
        pl.BlockSpec((pixels, outs), lambda k: (0, 0)),
        pl.BlockSpec((members, pixels, outs), lambda k: (0, 0, 0)),
    ]
    if first:
        out_shape = [struct(gathered.shape, bf16)] + out_shape
        out_specs = [pl.BlockSpec((1, pixels, chans), lambda k: (k, 0, 0))] + out_specs
    return pl.pallas_call(
        functools.partial(conv_body, side, steps, first),
        grid=(steps,),
        in_specs=[
            pl.BlockSpec((joined, pixels, chans), lambda k: (k, 0, 0)),
            pl.BlockSpec((taps, joined * chans, outs), lambda k: (0, k, 0)),
            pl.BlockSpec((1, outs), lambda k: (0, 0)),
        ],
        out_specs=out_specs,
        out_shape=out_shape,
        scratch_shapes=[pltpu.VMEM((3, pixels + 2 * side, outs), f32)],
        compiler_params=params(),
        cost_estimate=cost(2 * pixels * taps * depth * outs, 2 * kernel.size + 4 * gathered.size),
        name="conv",
    )(gathered, kernel, bias.reshape(1, outs))


def spread_taps(side, grad, taps_ref):
    pixels, outs = grad.shape
    spot = lax.broadcasted_iota(jnp.int32, (pixels, outs), 0)
    column = lax.rem(spot, side)
    wide = grad.astype(f32)
    ahead = jnp.where(column < side - 1, pltpu.roll(wide, pixels - 1, 0), 0.0).astype(bf16)
    behind = jnp.where(column > 0, pltpu.roll(wide, 1, 0), 0.0).astype(bf16)
    edge = jnp.zeros((side, 3 * outs), bf16)
    taps_ref[:side, :] = edge
    taps_ref[side + pixels :, :] = edge
    taps_ref[side : side + pixels, :] = jnp.concatenate([ahead, grad, behind], axis=1)


def tap_block(side, taps_ref, begin, block):
    return lanes(
        [taps_ref[begin + side * (2 - y) : begin + side * (2 - y) + block, :] for y in range(3)]
    )


def back_body(side, last, rs_ref, pre_ref, w_ref, *rest):
    if last:
        x_ref, go_ref, idk_ref, gp_ref, bias_ref, gin_ref, taps_ref = rest
    else:
        gp_ref, bias_ref, gin_ref, taps_ref = rest
    pixels = pre_ref.shape[0]
    block = 8 * side

    @pl.when(pl.program_id(0) == 0)
    def _():
        total = rs_ref[0].astype(f32)
        for j in range(1, rs_ref.shape[0]):
            total = total + rs_ref[j].astype(f32)
        grad = (total * gelu_slope(pre_ref[...])).astype(bf16)
        gp_ref[...] = grad
        bias_ref[...] = jnp.sum(grad.astype(f32), axis=0, keepdims=True)
        spread_taps(side, grad, taps_ref)

    weights = lanes([w_ref[t] for t in range(9)])
    for begin in range(0, pixels, block):
        part = dot(tap_block(side, taps_ref, begin, block), weights, NT)
        if last:
            part = part * gelu_slope(x_ref[0, begin : begin + block, :].astype(f32))
            part = part + dot(go_ref[begin : begin + block, :], idk_ref[...], NT)
        gin_ref[0, begin : begin + block, :] = part.astype(bf16)


def back(side, pieces, pre, kernel, extra=()):
    members, pixels, outs = pieces.shape
    taps, depth, _ = kernel.shape
    chans = depth // members
    in_specs = [
        pl.BlockSpec(pieces.shape, lambda k: (0, 0, 0)),
        pl.BlockSpec(pre.shape, lambda k: (0, 0)),
        pl.BlockSpec((taps, chans, outs), lambda k: (0, k, 0)),
    ]
    if extra:
        x, go, idk = extra
        in_specs += [
            pl.BlockSpec((1, pixels, chans), lambda k: (k, 0, 0)),
            pl.BlockSpec(go.shape, lambda k: (0, 0)),
            pl.BlockSpec((chans, idk.shape[1]), lambda k: (k, 0)),
        ]
    return pl.pallas_call(
        functools.partial(back_body, side, bool(extra)),
        grid=(members,),
        in_specs=in_specs,
        out_specs=[
            pl.BlockSpec((pixels, outs), lambda k: (0, 0)),
            pl.BlockSpec((1, outs), lambda k: (0, 0)),
            pl.BlockSpec((1, pixels, chans), lambda k: (k, 0, 0)),
        ],
        out_shape=[
            struct((pixels, outs), bf16),
            struct((1, outs), f32),
            struct((members, pixels, chans), bf16),
        ],
        scratch_shapes=[pltpu.VMEM((pixels + 2 * side, 3 * outs), bf16)],
        compiler_params=params(),
        cost_estimate=cost(2 * pixels * taps * depth * outs, 2 * kernel.size + 2 * pixels * depth),
        name="back",
    )(pieces, pre, kernel, *extra)


def weight_body(side, gp_ref, x_ref, dw_ref, taps_ref):
    pixels, outs = gp_ref.shape

    @pl.when(pl.program_id(0) == 0)
    def _():
        spread_taps(side, gp_ref[...], taps_ref)

    values = lanes([x_ref[j] for j in range(x_ref.shape[0])])
    for y in range(3):
        at = side * (2 - y)
        part = dot(values, taps_ref[at : at + pixels, :], TN)
        for x in range(3):
            dw_ref[3 * y + x] = part[:, x * outs : (x + 1) * outs].astype(bf16)


def weight_grad(side, grad, gathered):
    members, pixels, chans = gathered.shape
    outs = grad.shape[1]
    joined = max(1, 256 // chans)
    steps = members // joined
    return pl.pallas_call(
        functools.partial(weight_body, side),
        grid=(steps,),
        in_specs=[
            pl.BlockSpec(grad.shape, lambda k: (0, 0)),
            pl.BlockSpec((joined, pixels, chans), lambda k: (k, 0, 0)),
        ],
        out_specs=pl.BlockSpec((9, joined * chans, outs), lambda k: (0, k, 0)),
        out_shape=struct((9, members * chans, outs), bf16),
        scratch_shapes=[pltpu.VMEM((pixels + 2 * side, 3 * outs), bf16)],
        compiler_params=params(),
        cost_estimate=cost(18 * pixels * members * chans * outs, 4 * gathered.size),
        name="weight_grad",
    )(grad, gathered)


def outer_body(gain, x_ref, go_ref, out_ref):
    for j in range(x_ref.shape[0]):
        chans = x_ref.shape[2]
        part = dot(x_ref[j], go_ref[...], TN)
        out_ref[j * chans : (j + 1) * chans, :] = (gain * part).astype(bf16)


def outer(gathered, go, gain):
    members, pixels, chans = gathered.shape
    outs = go.shape[1]
    return pl.pallas_call(
        functools.partial(outer_body, gain),
        grid=(members,),
        in_specs=[
            pl.BlockSpec((1, pixels, chans), lambda k: (k, 0, 0)),
            pl.BlockSpec(go.shape, lambda k: (0, 0)),
        ],
        out_specs=pl.BlockSpec((chans, outs), lambda k: (k, 0)),
        out_shape=struct((members * chans, outs), bf16),
        compiler_params=params(),
        cost_estimate=cost(2 * pixels * members * chans * outs, 2 * gathered.size),
        name="outer",
    )(gathered, go)


def start_body(valid_ref, cot_ref, outk_ref, go_ref, bias_ref, ga_ref):
    @pl.when(pl.program_id(0) == 0)
    def _():
        masked = cot_ref[...].astype(f32) * valid_ref[0]
        go_ref[...] = masked.astype(bf16)
        bias_ref[...] = jnp.sum(masked, axis=0, keepdims=True)

    ga_ref[0] = (post_gain * dot(go_ref[...], outk_ref[...], NT)).astype(bf16)


def start_back(valid, cot, outk, members):
    pixels, outs = cot.shape
    chans = outk.shape[0] // members
    return pl.pallas_call(
        start_body,
        grid=(members,),
        in_specs=[
            pl.BlockSpec(memory_space=pltpu.SMEM),
            pl.BlockSpec(cot.shape, lambda k: (0, 0)),
            pl.BlockSpec((chans, outs), lambda k: (k, 0)),
        ],
        out_specs=[
            pl.BlockSpec(cot.shape, lambda k: (0, 0)),
            pl.BlockSpec((1, outs), lambda k: (0, 0)),
            pl.BlockSpec((1, pixels, chans), lambda k: (k, 0, 0)),
        ],
        out_shape=[
            struct(cot.shape, bf16),
            struct((1, outs), f32),
            struct((members, pixels, chans), bf16),
        ],
        compiler_params=params(),
        cost_estimate=cost(2 * pixels * outs * outk.shape[0], 4 * cot.size),
        name="start_back",
    )(valid, cot, outk)


def finish_body(valid_ref, x_ref, act_ref, idk_ref, outk_ref, ib_ref, out_ref):
    members = x_ref.shape[0]
    x = lanes([x_ref[j] for j in range(members)])
    act = lanes([act_ref[j] for j in range(members)])
    identity = dot(x, idk_ref[...]) + ib_ref[...]
    branch = dot(act, outk_ref[...])
    out_ref[...] = ((identity + post_gain * branch) * valid_ref[0]).astype(bf16)


def finish(valid, x, act, idk, outk, ib):
    members, pixels, chans = x.shape
    outs = idk.shape[1]
    block = pixels // 4
    return pl.pallas_call(
        finish_body,
        grid=(4,),
        in_specs=[
            pl.BlockSpec(memory_space=pltpu.SMEM),
            pl.BlockSpec((members, block, chans), lambda k: (0, k, 0)),
            pl.BlockSpec((members, block, act.shape[2]), lambda k: (0, k, 0)),
            pl.BlockSpec(idk.shape, lambda k: (0, 0)),
            pl.BlockSpec(outk.shape, lambda k: (0, 0)),
            pl.BlockSpec((1, outs), lambda k: (0, 0)),
        ],
        out_specs=pl.BlockSpec((block, outs), lambda k: (k, 0)),
        out_shape=struct((pixels, outs), bf16),
        compiler_params=params(),
        cost_estimate=cost(2 * pixels * outs * (idk.shape[0] + outk.shape[0]), 2 * x.size),
        name="finish",
    )(valid, x, act, idk, outk, ib.reshape(1, outs))


def swap(pieces, axis):
    return lax.all_to_all(pieces, axis, split_axis=0, concat_axis=0, tiled=True)


def after(value, other):
    return lax.optimization_barrier((value, other))[0]


def local(
    pixels,
    counts,
    kernel_one,
    bias_one,
    kernel_two,
    bias_two,
    kernel_three,
    bias_three,
    out_kernel,
    identity_kernel,
    identity_bias,
    cotangent,
):
    images, rows, width, chans = pixels.shape
    members = lax.axis_size("mp")
    side = width // 2
    spots = side * side
    outs = cotangent.shape[3]
    taps = lambda kernel: kernel.reshape((9,) + kernel.shape[2:])
    one, two, three = taps(kernel_one), taps(kernel_two), taps(kernel_three)

    own_count = lax.dynamic_index_in_dim(counts, lax.axis_index("dp"), 0, keepdims=True)
    valid = (own_count > 0).astype(f32)

    local_x = swap(pool(pixels), "dp").reshape(spots, chans)
    go, identity_bias_grad, ga_three = start_back(
        valid, cotangent.reshape(spots, outs), out_kernel, members
    )
    copies = jnp.broadcast_to(local_x, (members, spots, chans))
    full_x = swap(copies, "mp")
    act_zero, pre_one, act_one = conv(side, full_x, one, bias_one, True)
    full_one = swap(act_one, "mp")
    pre_two, act_two = conv(side, full_one, two, bias_two)
    full_two = swap(act_two, "mp")
    ga_three = swap(ga_three, "mp")
    pre_three, act_three = conv(side, full_two, three, bias_three)
    gp_three, bias_three_grad, ga_two = back(side, ga_three, pre_three, three)
    ga_two = swap(ga_two, "mp")
    gp_two, bias_two_grad, ga_one = back(side, ga_two, pre_two, two)
    ga_one = swap(ga_one, "mp")
    gp_one, bias_one_grad, gx = back(side, ga_one, pre_one, one, (full_x, go, identity_kernel))
    gx = swap(gx, "mp")
    full_three = swap(act_three, "mp")

    block_out = finish(valid, full_x, full_three, identity_kernel, out_kernel, identity_bias)
    identity_kernel_grad = outer(full_x, go, 1.0)
    out_kernel_grad = outer(full_three, go, post_gain)
    kernel_three_grad = weight_grad(side, gp_three, full_two)
    kernel_two_grad = weight_grad(side, gp_two, full_one)
    kernel_one_grad = weight_grad(side, gp_one, act_zero)

    gx = jnp.sum(gx.astype(f32), axis=0).astype(bf16)
    gx = swap(gx.reshape(images, rows * width // 4, chans), "dp")
    pixels_grad = widen(gx, rows, width)

    identity_kernel_grad = lax.psum(identity_kernel_grad, "dp")
    out_kernel_grad = lax.psum(after(out_kernel_grad, identity_kernel_grad), "dp")
    kernel_three_grad = lax.psum(after(kernel_three_grad, out_kernel_grad), "dp")
    kernel_two_grad = lax.psum(after(kernel_two_grad, kernel_three_grad), "dp")
    small = jnp.concatenate(
        [bias_one_grad, bias_two_grad, bias_three_grad, identity_bias_grad], axis=1
    ).astype(bf16)
    kernel_one_grad, small = lax.psum((after(kernel_one_grad, kernel_two_grad), small), "dp")
    small = small.astype(f32)[0]
    hid = bias_one.shape[0]
    return (
        block_out.reshape(cotangent.shape),
        pixels_grad,
        kernel_one_grad.astype(f32).reshape(kernel_one.shape),
        small[:hid],
        kernel_two_grad.astype(f32).reshape(kernel_two.shape),
        small[hid : 2 * hid],
        kernel_three_grad.astype(f32).reshape(kernel_three.shape),
        small[2 * hid : 3 * hid],
        out_kernel_grad.astype(f32),
        identity_kernel_grad.astype(f32),
        small[3 * hid :],
    )


def solution(mesh):
    return jax.shard_map(
        local,
        mesh=mesh,
        in_specs=(
            P(None, "dp", None, "mp"),
            P(),
            P(None, None, None, "mp"),
            P("mp"),
            P(None, None, None, "mp"),
            P("mp"),
            P(None, None, None, "mp"),
            P("mp"),
            P(None, "mp"),
            P(None, "mp"),
            P("mp"),
            P("dp", None, None, "mp"),
        ),
        out_specs=(
            P("dp", None, None, "mp"),
            P(None, "dp", None, "mp"),
            P(None, None, None, "mp"),
            P("mp"),
            P(None, None, None, "mp"),
            P("mp"),
            P(None, None, None, "mp"),
            P("mp"),
            P(None, "mp"),
            P(None, "mp"),
            P("mp"),
        ),
        check_vma=False,
    )
```

```python
import functools

import jax
import jax.numpy as jnp
from jax import lax
from jax.experimental import pallas as pl
from jax.experimental.pallas import tpu as pltpu
from jax.sharding import Mesh
from jax.sharding import PartitionSpec as P


post_gain = 0.015625
slope = 0.7978845608028654
cubic = 0.044715
halo = 6
bf16 = jnp.bfloat16
f32 = jnp.float32
NT = (((1,), (1,)), ((), ()))
TN = (((0,), (0,)), ((), ()))
NN = (((1,), (0,)), ((), ()))
DP = ("chip", "core")
MP = ("zh", "zl")


def dot(left, right, dims=NN):
    return lax.dot_general(left, right, dims, preferred_element_type=f32)


def gelu(value):
    inner = jnp.tanh(slope * (value + cubic * value * value * value))
    return 0.5 * value * (1.0 + inner)


def gelu_slope(value):
    square = value * value
    inner = jnp.tanh(slope * value * (1.0 + cubic * square))
    climb = slope * (1.0 + 3.0 * cubic * square)
    return 0.5 * (1.0 + inner) + 0.5 * value * (1.0 - inner * inner) * climb


def struct(shape, kind):
    return jax.ShapeDtypeStruct(shape, kind)


def lanes(blocks):
    return blocks[0] if len(blocks) == 1 else jnp.concatenate(blocks, axis=1)


VMEM = pl.BlockSpec(memory_space=pltpu.VMEM)
SMEM = pl.BlockSpec(memory_space=pltpu.SMEM)
FAR = pl.BlockSpec(memory_space=pl.ANY)


def call(body, name, ins, outs, scratch=(), flops=0, **more):
    spaces = [space for space, _ in ins]
    arrays = [array for _, array in ins]
    out_specs = [space for space, _ in outs]
    out_shape = [shape for _, shape in outs]
    moved = sum(a.size * a.dtype.itemsize for a in arrays + out_shape)
    single = len(outs) == 1
    return pl.pallas_call(
        body,
        in_specs=spaces,
        out_specs=out_specs[0] if single else out_specs,
        out_shape=out_shape[0] if single else out_shape,
        scratch_shapes=list(scratch),
        compiler_params=pltpu.CompilerParams(vmem_limit_bytes=60 << 20),
        cost_estimate=pl.CostEstimate(flops=int(flops), bytes_accessed=moved, transcendentals=0),
        name=name,
        **more,
    )(*arrays)


def run_copies(pairs, sems):
    copies = [pltpu.make_async_copy(a, b, sems.at[i]) for i, (a, b) in enumerate(pairs)]
    for copy in copies:
        copy.start()
    for copy in copies:
        copy.wait()


def at(start, size, unit):
    return pl.ds(pl.multiple_of(start, unit), size)


def pool_body(x_ref, out_ref):
    rows, width, chans = x_ref.shape[1:]
    half = width // 2
    pixel = lax.broadcasted_iota(jnp.int32, (half, 2 * width), 1)
    place = lax.broadcasted_iota(jnp.int32, (half, 2 * width), 0)
    inside = (lax.rem(pixel, width) >= 2 * place) & (lax.rem(pixel, width) < 2 * place + 2)
    pick = jnp.where(inside, 0.25, 0.0).astype(bf16)
    for row in range(rows // 2):
        window = x_ref[0, 2 * row : 2 * row + 2].reshape(2 * width, chans)
        out_ref[0, row * half : (row + 1) * half, :] = dot(pick, window).astype(bf16)


def pool(pixels):
    images, rows, width, chans = pixels.shape
    spots = rows * width // 4
    block = pl.BlockSpec((1, rows, width, chans), lambda i: (i, 0, 0, 0))
    out = pl.BlockSpec((1, spots, chans), lambda i: (i, 0, 0))
    return call(
        pool_body,
        "pool",
        [(block, pixels)],
        [(out, struct((images, spots, chans), bf16))],
        grid=(images,),
    )


def widen_body(g_ref, out_ref):
    rows, width, chans = out_ref.shape[1:]
    half = width // 2
    pixel = lax.broadcasted_iota(jnp.int32, (width, half), 0)
    place = lax.broadcasted_iota(jnp.int32, (width, half), 1)
    inside = (pixel >= 2 * place) & (pixel < 2 * place + 2)
    pick = jnp.where(inside, 0.25, 0.0).astype(bf16)
    for row in range(rows // 2):
        wide = dot(pick, g_ref[0, row * half : (row + 1) * half, :]).astype(bf16)
        out_ref[0, 2 * row] = wide
        out_ref[0, 2 * row + 1] = wide


def widen(grad, rows, width):
    images, spots, chans = grad.shape
    block = pl.BlockSpec((1, spots, chans), lambda i: (i, 0, 0))
    out = pl.BlockSpec((1, rows, width, chans), lambda i: (i, 0, 0, 0))
    return call(
        widen_body,
        "widen",
        [(block, grad)],
        [(out, struct((images, rows, width, chans), bf16))],
        grid=(images,),
    )


def conv_body(side, first, idx_ref, *refs):
    zh, zl = idx_ref[2], idx_ref[3]
    if first:
        xl, xa, xh, xd, wl, wo, bl, bo, pre_ref, act_ref, xbuf, wbuf, acc, sems = refs
        chans = xl.shape[1]
        spots = xbuf.shape[0]
        begin = zh * (xl.shape[0] - spots)
        pairs = []
        for source, up, along in ((xl, zh, zl), (xa, zh, 1 - zl), (xh, 1 - zh, zl), (xd, 1 - zh, 1 - zl)):
            if source is xl:
                source = xl.at[at(begin, spots, side), :]
            pairs.append((source, xbuf.at[:, at((2 * up + along) * chans, chans, chans)]))
    else:
        xl, xa, wl, wo, bl, bo, pre_ref, act_ref, xbuf, wbuf, acc, sems = refs
        chans = xl.shape[1] // 2
        spots = xbuf.shape[0]
        pairs = []
        for source, along in ((xl, zl), (xa, 1 - zl)):
            for up in range(2):
                pairs.append(
                    (
                        source.at[:, up * chans : (up + 1) * chans],
                        xbuf.at[:, at((2 * up + along) * chans, chans, chans)],
                    )
                )
    run_copies(pairs + [(wl, wbuf.at[zh]), (wo, wbuf.at[1 - zh])], sems)
    acc[...] = jnp.zeros_like(acc)
    outs = 2 * wl.shape[2]
    block = spots // 2
    for x in range(3):
        weights = lanes([wbuf[u, 3 * y + x] for y in range(3) for u in range(2)])
        for begin in range(0, spots, block):
            values = xbuf[begin : begin + block, :]
            if first:
                values = gelu(values.astype(f32)).astype(bf16)
            product = dot(values, weights)
            for y in range(3):
                place = begin + side * (2 - y)
                acc[x, place : place + block, :] += product[:, y * outs : (y + 1) * outs]
    spot = lax.broadcasted_iota(jnp.int32, (block, outs), 0)
    column = lax.rem(spot, side)
    own, other = bl[...], bo[...]
    bias = lanes([jnp.where(zh == 0, own, other), jnp.where(zh == 0, other, own)])
    for begin in range(0, spots, block):
        place = begin + side
        left = pltpu.roll(acc[0, place : place + block, :], 1, 0)
        right = pltpu.roll(acc[2, place : place + block, :], block - 1, 0)
        pre = acc[1, place : place + block, :] + bias
        pre = pre + jnp.where(column > 0, left, 0.0)
        pre = pre + jnp.where(column < side - 1, right, 0.0)
        pre_ref[begin : begin + block, :] = pre
        act_ref[begin : begin + block, :] = gelu(pre).astype(bf16)


def conv(side, idx, sources, own, other, bias, bias_other, first=False):
    taps, depth, outs = own.shape
    spots = sources[1].shape[0]
    return call(
        functools.partial(conv_body, side, first),
        "conv",
        [(SMEM, idx)]
        + [(FAR, s) for s in sources]
        + [(FAR, own), (FAR, other), (VMEM, bias.reshape(1, outs)), (VMEM, bias_other.reshape(1, outs))],
        [(VMEM, struct((spots, 2 * outs), f32)), (VMEM, struct((spots, 2 * outs), bf16))],
        [
            pltpu.VMEM((spots, depth), bf16),
            pltpu.VMEM((2, taps, depth, outs), bf16),
            pltpu.VMEM((3, spots + 2 * side, 2 * outs), f32),
            pltpu.SemaphoreType.DMA((6,)),
        ],
        flops=4 * spots * taps * depth * outs,
    )


def spread_taps(side, grad, taps_ref):
    pixels, outs = grad.shape
    spot = lax.broadcasted_iota(jnp.int32, (pixels, outs), 0)
    column = lax.rem(spot, side)
    wide = grad.astype(f32)
    ahead = jnp.where(column < side - 1, pltpu.roll(wide, pixels - 1, 0), 0.0).astype(bf16)
    behind = jnp.where(column > 0, pltpu.roll(wide, 1, 0), 0.0).astype(bf16)
    edge = jnp.zeros((side, 3 * outs), bf16)
    taps_ref[:side, :] = edge
    taps_ref[side + pixels :, :] = edge
    taps_ref[side : side + pixels, :] = jnp.concatenate([ahead, grad, behind], axis=1)


def tap_block(side, taps_ref, begin, block):
    return lanes([taps_ref[at(begin + side * (2 - y), block, side), :] for y in range(3)])


def back_body(side, last, idx_ref, keep_ref, recv_ref, pre_ref, wl, wo, *refs):
    zh, zl = idx_ref[2], idx_ref[3]
    if last:
        mine_ref, theirs_ref, own_ref, give_ref, gp_ref, taps_ref, wbuf, sems = refs
    else:
        gp_ref, own_ref, give_ref, taps_ref, wbuf, sems = refs
    copies = [
        pltpu.make_async_copy(wl, wbuf.at[zh], sems.at[0]),
        pltpu.make_async_copy(wo, wbuf.at[1 - zh], sems.at[1]),
    ]
    for copy in copies:
        copy.start()
    total = keep_ref[...] + recv_ref[...].astype(f32)
    grad = (total * gelu_slope(pre_ref[...])).astype(bf16)
    gp_ref[...] = grad
    spread_taps(side, grad, taps_ref)
    depth, outs = wl.shape[1:]
    pixels = pre_ref.shape[0]
    if last:
        start = zh * halo * side
        pixels = mine_ref.shape[0]
        own = gp_ref[at(start, pixels, side), :]
        low, high = own[:, :outs], own[:, outs:]
        mine_ref[...] = jnp.where(zh == 0, low, high)
        theirs_ref[...] = jnp.where(zh == 0, high, low)
    for copy in copies:
        copy.wait()
    block = pixels // 2
    chans = depth // 4

    def rows(index):
        spot = at(index * chans, chans, chans)
        return lanes([wbuf[u, t, spot, :] for t in range(9) for u in range(2)])

    for target, along in ((give_ref, 1 - zl), (own_ref, zl)):
        if last:
            for up in range(2):
                weights = rows(2 * up + along)
                for begin in range(0, pixels, block):
                    part = dot(tap_block(side, taps_ref, start + begin, block), weights, NT)
                    target[up, begin : begin + block, :] = part.astype(target.dtype)
        else:
            weights = jnp.concatenate([rows(along), rows(2 + along)], axis=0)
            for begin in range(0, pixels, block):
                part = dot(tap_block(side, taps_ref, begin, block), weights, NT)
                target[begin : begin + block, :] = part.astype(target.dtype)


def back(side, idx, keep, recv, pre, own, other, half=0):
    taps, depth, outs = own.shape
    spots = pre.shape[0]
    if half:
        shape = (2, half, depth // 4)
        results = [
            (VMEM, struct((half, outs), bf16)),
            (VMEM, struct((half, outs), bf16)),
        ]
    else:
        shape = (spots, depth // 2)
        results = [(VMEM, struct((spots, 2 * outs), bf16))]
    results += [(VMEM, struct(shape, f32)), (VMEM, struct(shape, bf16))]
    scratch = [
        pltpu.VMEM((spots + 2 * side, 6 * outs), bf16),
        pltpu.VMEM((2, taps, depth, outs), bf16),
        pltpu.SemaphoreType.DMA((2,)),
    ]
    if half:
        scratch = [pltpu.VMEM((spots, 2 * outs), bf16)] + scratch
    return call(
        functools.partial(back_body, side, bool(half)),
        "back",
        [(SMEM, idx), (VMEM, keep), (VMEM, recv), (VMEM, pre), (FAR, own), (FAR, other)],
        results,
        scratch,
        flops=4 * spots * taps * depth * outs,
    )


def put_blocks(idx_ref, keep_ref, give_ref, part, tap, first_block, size, *inner):
    chip, core = idx_ref[0], idx_ref[1]
    for b in range(0, part.shape[0] // size, 2):
        even = part[b * size : (b + 1) * size, :]
        odd = part[(b + 1) * size : (b + 2) * size, :]
        slot = chip ^ ((first_block + b) // 2)
        rows = slice(tap * size, (tap + 1) * size)
        keep_ref[(slot,) + inner + (rows, slice(None))] = jnp.where(core == 0, even, odd).astype(bf16)
        give_ref[(slot,) + inner + (rows, slice(None))] = jnp.where(core == 0, odd, even).astype(bf16)


def weight_body(side, half, idx_ref, gp_ref, xl, xa, keep_ref, give_ref, xbuf, taps_ref, sems):
    zh, zl = idx_ref[2], idx_ref[3]
    chans = xl.shape[1] // 2
    pairs = []
    for source, along in ((xl, zl), (xa, 1 - zl)):
        for up in range(2):
            pairs.append(
                (
                    source.at[:, up * chans : (up + 1) * chans],
                    xbuf.at[:, at((2 * up + along) * chans, chans, chans)],
                )
            )
    run_copies(pairs, sems)
    spots, wide = gp_ref.shape
    outs = wide // 2
    spot = lax.broadcasted_iota(jnp.int32, (spots, wide), 0) - zh * halo * side
    grad = jnp.where((spot >= 0) & (spot < half), gp_ref[...].astype(f32), 0.0)
    bias = jnp.sum(grad, axis=0, keepdims=True)
    spread_taps(side, grad.astype(bf16), taps_ref)
    blocks = 2 * keep_ref.shape[0]
    depth = xbuf.shape[1]
    size = depth // blocks
    for begin in range(0, depth, 256):
        values = xbuf[:, begin : begin + 256]
        for y in range(3):
            place = side * (2 - y)
            part = dot(values, taps_ref[place : place + spots, :], TN)
            for x in range(3):
                for u in range(2):
                    col = x * wide + u * outs
                    put_blocks(
                        idx_ref, keep_ref, give_ref, part[:, col : col + outs],
                        3 * y + x, begin // size, size, u,
                    )
    for u in range(2):
        row = jnp.broadcast_to(bias[:, u * outs : (u + 1) * outs], (16, outs)).astype(bf16)
        for j in range(keep_ref.shape[0]):
            keep_ref[j, u, 9 * size :, :] = row
            give_ref[j, u, 9 * size :, :] = row


def weight_grad(side, half, idx, grad, act, act_other, chips):
    spots, wide = grad.shape
    outs = wide // 2
    depth = 2 * act.shape[1]
    rows = 9 * depth // (2 * chips) + 16
    return call(
        functools.partial(weight_body, side, half),
        "weight_grad",
        [(SMEM, idx), (VMEM, grad), (FAR, act), (FAR, act_other)],
        [(VMEM, struct((chips, 2, rows, outs), bf16))] * 2,
        [
            pltpu.VMEM((spots, depth), bf16),
            pltpu.VMEM((spots + 2 * side, 3 * wide), bf16),
            pltpu.SemaphoreType.DMA((4,)),
        ],
        flops=36 * spots * depth * outs,
    )


def weight_one_body(side, idx_ref, mine_ref, theirs_ref, x_ref, keep_ref, give_ref, gp_ref, taps_ref):
    zh = idx_ref[2]
    half, outs = mine_ref.shape
    gp_ref[at(zh * half, half, side), :] = mine_ref[...]
    gp_ref[at((1 - zh) * half, half, side), :] = theirs_ref[...]
    grad = gp_ref[...]
    bias = jnp.sum(grad.astype(f32), axis=0, keepdims=True)
    spread_taps(side, grad, taps_ref)
    blocks = 2 * keep_ref.shape[0]
    spots, depth = x_ref.shape
    size = depth // blocks
    right = tap_block(side, taps_ref, 0, spots)
    for begin in range(0, depth, 256):
        part = dot(x_ref[:, begin : begin + 256], right, TN)
        for tap in range(9):
            put_blocks(
                idx_ref, keep_ref, give_ref, part[:, tap * outs : (tap + 1) * outs],
                tap, begin // size, size,
            )
    row = jnp.broadcast_to(bias, (16, outs)).astype(bf16)
    for j in range(keep_ref.shape[0]):
        keep_ref[j, 9 * size :, :] = row
        give_ref[j, 9 * size :, :] = row


def weight_one_grad(side, idx, mine, theirs, act_zero, chips):
    spots, depth = act_zero.shape
    outs = mine.shape[1]
    rows = 9 * depth // (2 * chips) + 16
    return call(
        functools.partial(weight_one_body, side),
        "weight_one_grad",
        [(SMEM, idx), (VMEM, mine), (VMEM, theirs), (VMEM, act_zero)],
        [(VMEM, struct((chips, rows, outs), bf16))] * 2,
        [
            pltpu.VMEM((spots, outs), bf16),
            pltpu.VMEM((spots + 2 * side, 3 * outs), bf16),
        ],
        flops=18 * spots * depth * outs,
    )


def pair_body(groups, *refs):
    ins, outs = refs[: 2 * groups], refs[2 * groups :]
    for j, out in enumerate(outs):
        for g in range(groups):
            total = (ins[2 * g][j].astype(f32) + ins[2 * g + 1][j].astype(f32)).astype(bf16)
            if groups == 1:
                out[...] = total
            else:
                out[:, g] = total


def pair_sum(*pairs):
    groups = len(pairs) // 2
    chips = pairs[0].shape[0]
    shape = pairs[0].shape[1:]
    if groups > 1:
        shape = shape[:1] + (groups,) + shape[1:]
    return call(
        functools.partial(pair_body, groups),
        "pair_sum",
        [(VMEM, p) for p in pairs],
        [(VMEM, struct(shape, bf16))] * chips,
    )


def chip_body(idx_ref, *refs):
    parts, (keep_ref, give_ref) = refs[:-2], refs[-2:]
    zh = idx_ref[2]
    for target, slot in ((keep_ref, zh), (give_ref, 1 - zh)):
        total = parts[0][slot].astype(f32)
        for part in parts[1:]:
            total = total + part[slot].astype(f32)
        target[...] = total.astype(target.dtype)


def chip_sum(idx, parts):
    shape = parts[0].shape[1:]
    return call(
        chip_body,
        "chip_sum",
        [(SMEM, idx)] + [(VMEM, p) for p in parts],
        [(VMEM, struct(shape, f32)), (VMEM, struct(shape, bf16))],
    )


def place_body(groups, idx_ref, own_ref, sib_ref, *refs):
    chip, core = idx_ref[0], idx_ref[1]
    outs, sems = refs[:-1], refs[-1]
    size = own_ref.shape[-2]
    pairs = []
    for j in range(own_ref.shape[0]):
        for g, out in enumerate(outs):
            for source, owner in ((own_ref, core), (sib_ref, 1 - core)):
                spot = at((2 * (chip ^ j) + owner) * size, size, size)
                pairs.append((source.at[j, g], out.at[:, spot, :]))
    run_copies(pairs, sems)


def place(idx, own, sib):
    chips, groups, taps, size, outs = own.shape
    shape = struct((taps, 2 * chips * size, outs), bf16)
    results = call(
        functools.partial(place_body, groups),
        "place",
        [(SMEM, idx), (FAR, own), (FAR, sib)],
        [(FAR, shape)] * groups,
        [pltpu.SemaphoreType.DMA((2 * chips * groups,))],
    )
    return results if groups > 1 else [results]


def final_body(groups, idx_ref, own_ref, sib_ref, *outs):
    chip, core = idx_ref[0], idx_ref[1]
    size = (own_ref.shape[-2] - 16) // 9
    for g in range(groups):
        grad_ref, bias_ref = outs[2 * g : 2 * g + 2]
        bias_ref[...] = own_ref[0, g, 9 * size : 9 * size + 1, :].astype(f32)
        for j in range(own_ref.shape[0]):
            for source, owner in ((own_ref, core), (sib_ref, 1 - core)):
                spot = at((2 * (chip ^ j) + owner) * size, size, size)
                for tap in range(9):
                    grad_ref[tap, spot, :] = source[j, g, tap * size : (tap + 1) * size, :].astype(f32)


def final_grads(idx, own, sib):
    chips, groups, rows, outs = own.shape
    depth = 2 * chips * ((rows - 16) // 9)
    return call(
        functools.partial(final_body, groups),
        "final_grads",
        [(SMEM, idx), (VMEM, own), (VMEM, sib)],
        [(VMEM, struct((9, depth, outs), f32)), (VMEM, struct((1, outs), f32))] * groups,
    )


def outer_body(gain, x_ref, go_ref, out_ref):
    out_ref[...] = (gain * dot(x_ref[...], go_ref[...], TN)).astype(bf16)


def outer(x, go, gain):
    spots, depth = x.shape
    outs = go.shape[1]
    return call(
        functools.partial(outer_body, gain),
        "outer",
        [
            (pl.BlockSpec((spots, 256), lambda k: (0, k)), x),
            (pl.BlockSpec((spots, outs), lambda k: (0, 0)), go),
        ],
        [(pl.BlockSpec((256, outs), lambda k: (k, 0)), struct((depth, outs), bf16))],
        flops=2 * spots * depth * outs,
        grid=(depth // 256,),
    )


def start_body(idx_ref, valid_ref, cot_ref, outk_ref, go_ref, bias_ref, own_ref, give_ref):
    zl = idx_ref[3]
    masked = cot_ref[...].astype(f32) * valid_ref[0]
    go_ref[...] = masked.astype(bf16)
    bias_ref[...] = jnp.sum(masked, axis=0, keepdims=True).astype(bf16)
    chans = outk_ref.shape[0] // 4
    block = cot_ref.shape[0] // 4
    for target, along in ((give_ref, 1 - zl), (own_ref, zl)):
        weights = jnp.concatenate(
            [outk_ref[at((2 * up + along) * chans, chans, chans), :] for up in range(2)], axis=0
        )
        for begin in range(0, cot_ref.shape[0], block):
            part = post_gain * dot(go_ref[begin : begin + block, :], weights, NT)
            target[begin : begin + block, :] = part.astype(target.dtype)


def start_back(idx, valid, cot, outk):
    spots, outs = cot.shape
    half = outk.shape[0] // 2
    return call(
        start_body,
        "start_back",
        [(SMEM, idx), (SMEM, valid), (VMEM, cot), (VMEM, outk)],
        [
            (VMEM, struct(cot.shape, bf16)),
            (VMEM, struct((1, outs), bf16)),
            (VMEM, struct((spots, half), f32)),
            (VMEM, struct((spots, half), bf16)),
        ],
        flops=4 * spots * outs * half,
    )


def identity_body(idx_ref, go_ref, idk_ref, own_ref, give_ref):
    zl = idx_ref[3]
    chans = idk_ref.shape[0] // 4
    block = go_ref.shape[0] // 4
    for target, along in ((give_ref, 1 - zl), (own_ref, zl)):
        for up in range(2):
            weights = idk_ref[at((2 * up + along) * chans, chans, chans), :]
            for begin in range(0, go_ref.shape[0], block):
                part = dot(go_ref[begin : begin + block, :], weights, NT)
                target[up, begin : begin + block, :] = part.astype(target.dtype)


def identity_back(idx, go, idk):
    spots, outs = go.shape
    chans = idk.shape[0] // 4
    return call(
        identity_body,
        "identity_back",
        [(SMEM, idx), (VMEM, go), (VMEM, idk)],
        [(VMEM, struct((2, spots, chans), f32)), (VMEM, struct((2, spots, chans), bf16))],
        flops=8 * spots * outs * chans,
    )


def rows_body(side, idx_ref, own_ref, recv_ref, keep_ref, give_ref):
    zh = idx_ref[2]
    spots = keep_ref.shape[0]
    apart = own_ref.shape[0] - spots
    for target, begin in ((give_ref, (1 - zh) * apart), (keep_ref, zh * apart)):
        spot = at(begin, spots, side)
        total = own_ref[spot, :] + recv_ref[spot, :].astype(f32)
        target[...] = total.astype(target.dtype)


def rows_sum(side, idx, own, recv, spots):
    shape = (spots, own.shape[1])
    return call(
        functools.partial(rows_body, side),
        "rows_sum",
        [(SMEM, idx), (VMEM, own), (VMEM, recv)],
        [(VMEM, struct(shape, f32)), (VMEM, struct(shape, bf16))],
    )


def slots_body(idx_ref, own_ref, recv_ref, keep_ref, give_ref):
    zh = idx_ref[2]
    for target, slot in ((give_ref, 1 - zh), (keep_ref, zh)):
        total = own_ref[slot] + recv_ref[slot].astype(f32)
        target[...] = total.astype(target.dtype)


def slots_sum(idx, own, recv):
    shape = own.shape[1:]
    return call(
        slots_body,
        "slots_sum",
        [(SMEM, idx), (VMEM, own), (VMEM, recv)],
        [(VMEM, struct(shape, f32)), (VMEM, struct(shape, bf16))],
    )


def input_body(idx_ref, x_ref, keep_ref, recv_ref, id_ref, id_recv_ref, out_ref):
    zh = idx_ref[2]
    half = keep_ref.shape[0]
    for part in range(2):
        rows = slice(part * half, (part + 1) * half)
        conv = jnp.where(zh == part, keep_ref[...], recv_ref[...].astype(f32))
        straight = id_ref[rows, :] + id_recv_ref[rows, :].astype(f32)
        total = conv * gelu_slope(x_ref[rows, :].astype(f32)) + straight
        out_ref[rows, :] = total.astype(bf16)


def input_grad(idx, x, keep, recv, id_keep, id_recv):
    return call(
        input_body,
        "input_grad",
        [(SMEM, idx)] + [(VMEM, a) for a in (x, keep, recv, id_keep, id_recv)],
        [(VMEM, struct(x.shape, bf16))],
    )


def whole_body(side, idx_ref, xl, xa, xh, xd, rh, rl, x_ref, act_ref, sems):
    zh, zl = idx_ref[2], idx_ref[3]
    chans = xl.shape[1]
    spots = xa.shape[0]
    rest = xl.shape[0] - spots
    window, outside = at(zh * rest, spots, side), at((1 - zh) * spots, rest, side)

    def cols(up, along):
        return at((2 * up + along) * chans, chans, chans)

    run_copies(
        [
            (xl, x_ref.at[:, cols(zh, zl)]),
            (xa, x_ref.at[window, cols(zh, 1 - zl)]),
            (xh, x_ref.at[window, cols(1 - zh, zl)]),
            (xd, x_ref.at[window, cols(1 - zh, 1 - zl)]),
            (rl.at[0], x_ref.at[outside, cols(zh, 1 - zl)]),
            (rh, x_ref.at[outside, cols(1 - zh, zl)]),
            (rl.at[1], x_ref.at[outside, cols(1 - zh, 1 - zl)]),
        ],
        sems,
    )
    block = x_ref.shape[0] // 8
    for begin in range(0, x_ref.shape[0], block):
        rows = slice(begin, begin + block)
        act_ref[rows, :] = gelu(x_ref[rows, :].astype(f32)).astype(bf16)


def whole_input(side, idx, *parts):
    spots, chans = parts[0].shape
    return call(
        functools.partial(whole_body, side),
        "whole_input",
        [(SMEM, idx)] + [(FAR, p) for p in parts],
        [(VMEM, struct((spots, 4 * chans), bf16))] * 2,
        [pltpu.SemaphoreType.DMA((7,))],
    )


def join_body(idx_ref, own, recv, out, sems):
    zh, zl = idx_ref[2], idx_ref[3]
    half = own.shape[1]
    chans = own.shape[2] // 2
    pairs = []
    for source, along in ((own, zl), (recv, 1 - zl)):
        for part, up in ((0, zh), (1, 1 - zh)):
            for slot in range(2):
                spot = at((2 * slot + along) * chans, chans, chans)
                pairs.append(
                    (
                        source.at[part, :, slot * chans : (slot + 1) * chans],
                        out.at[at(up * half, half, half), spot],
                    )
                )
    run_copies(pairs, sems)


def join(idx, own, recv):
    _, half, wide = own.shape
    return call(
        join_body,
        "join",
        [(SMEM, idx), (FAR, own), (FAR, recv)],
        [(FAR, struct((2 * half, 2 * wide), bf16))],
        [pltpu.SemaphoreType.DMA((8,))],
    )


def finish_body(valid_ref, x_ref, act_ref, idk_ref, outk_ref, ib_ref, out_ref):
    identity = dot(x_ref[...], idk_ref[...]) + ib_ref[...]
    branch = dot(act_ref[...], outk_ref[...])
    out_ref[...] = ((identity + post_gain * branch) * valid_ref[0]).astype(bf16)


def finish(valid, x, act, idk, outk, ib):
    spots, depth = x.shape
    outs = idk.shape[1]
    block = spots // 4
    by_row = lambda wide: pl.BlockSpec((block, wide), lambda k: (k, 0))
    full = lambda a: pl.BlockSpec(a.shape, lambda k: (0, 0))
    ib = ib.reshape(1, outs)
    return call(
        finish_body,
        "finish",
        [(SMEM, valid), (by_row(depth), x), (by_row(act.shape[1]), act)]
        + [(full(a), a) for a in (idk, outk, ib)],
        [(by_row(outs), struct((spots, outs), bf16))],
        flops=2 * spots * outs * (depth + act.shape[1]),
        grid=(4,),
    )


def flip(value, axis):
    return lax.ppermute(value, axis, [(0, 1), (1, 0)])


def hop(value, j, chips):
    return lax.ppermute(value, "chip", [(i, i ^ j) for i in range(chips)])


def gather_chips(value, chips):
    return [value] + [hop(value, j, chips) for j in range(1, chips)]


def swap(pieces, axis):
    return lax.all_to_all(pieces, axis, split_axis=0, concat_axis=0, tiled=True)


def after(value, other):
    return lax.optimization_barrier((value, other))[0]


def rows_of(value, start, size):
    return lax.dynamic_slice_in_dim(value, start, size, 0)


def local(
    pixels,
    counts,
    kernel_one,
    bias_one,
    kernel_two,
    bias_two,
    kernel_three,
    bias_three,
    out_kernel,
    identity_kernel,
    identity_bias,
    cotangent,
):
    images, rows, width, chans = pixels.shape
    side = width // 2
    spots = side * side
    half = spots // 2
    window = half + halo * side
    outs = cotangent.shape[3]
    chips = lax.axis_size("chip")
    chip, core, zh, zl = [lax.axis_index(a) for a in ("chip", "core", "zh", "zl")]
    idx = jnp.stack([chip, core, zh, zl]).astype(jnp.int32)
    taps = lambda kernel: kernel.reshape((9,) + kernel.shape[2:])
    one, two, three = taps(kernel_one), taps(kernel_two), taps(kernel_three)

    own_count = lax.dynamic_index_in_dim(counts, 2 * chip + core, 0, keepdims=True)
    valid = (own_count > 0).astype(f32)

    def block_of(kernel):
        size = kernel.shape[1] // (2 * chips)
        return lax.dynamic_slice_in_dim(kernel, (2 * chip + core) * size, size, 1)

    def other_kernels(*kernels):
        piece = flip(jnp.stack([block_of(kernel) for kernel in kernels]), "zh")
        own = jnp.stack(gather_chips(piece, chips))
        return place(idx, own, flip(own, "core"))

    (one_other,) = other_kernels(one)
    bias_other = flip(jnp.stack([bias_one, bias_two, bias_three]), "zh")

    xl = swap(pool(pixels), DP).reshape(spots, chans)
    begin = zh * (spots - window)
    begin_other = (1 - zh) * (spots - window)
    xa = flip(rows_of(xl, begin, window), "zl")
    xh = flip(rows_of(xl, begin_other, window), "zh")
    xd = flip(xh, "zl")
    two_other, three_other = other_kernels(two, three)

    go, identity_bias_grad, ga_own, ga_give = start_back(
        idx, valid, cotangent.reshape(spots, outs), out_kernel
    )
    pre_one, act_one = conv(side, idx, (xl, xa, xh, xd), one, one_other, bias_one, bias_other[0], True)
    act_one_other = flip(act_one, "zl")
    pre_two, act_two = conv(side, idx, (act_one, act_one_other), two, two_other, bias_two, bias_other[1])
    act_two_other = flip(act_two, "zl")
    ga_keep, ga_give = rows_sum(side, idx, ga_own, flip(ga_give, "zl"), window)
    ga_recv = flip(ga_give, "zh")
    pre_three, act_three = conv(
        side, idx, (act_two, act_two_other), three, three_other, bias_three, bias_other[2]
    )

    gp_three, ga_own, ga_give = back(side, idx, ga_keep, ga_recv, pre_three, three, three_other)
    ga_recv = flip(ga_give, "zl")
    gp_two, ga_own, ga_give = back(side, idx, ga_own, ga_recv, pre_two, two, two_other)
    ga_recv = flip(ga_give, "zl")
    gp_mine, gp_theirs, gx_own, gx_give = back(
        side, idx, ga_own, ga_recv, pre_one, one, one_other, half
    )
    gp_theirs = flip(gp_theirs, "zh")

    rest = spots - window
    rest_own = rows_of(xl, (1 - zh) * window, rest)
    rest_high = flip(rows_of(xl, zh * window, rest), "zh")
    rest_low = flip(jnp.stack([rest_own, rest_high]), "zl")
    full_x, act_zero = whole_input(side, idx, xl, xa, xh, xd, rest_high, rest_low)

    own_rows = rows_of(act_three, zh * halo * side, half)
    own_rows = jnp.stack([own_rows, flip(own_rows, "zh")])
    full_three = join(idx, own_rows, flip(own_rows, "zl"))
    block_out = finish(valid, full_x, full_three, identity_kernel, out_kernel, identity_bias)

    id_own, id_give = identity_back(idx, go, identity_kernel)
    id_keep, id_give = slots_sum(idx, id_own, flip(id_give, "zl"))
    id_recv = flip(id_give, "zh")

    gx_keep, gx_give = slots_sum(idx, gx_own, flip(gx_give, "zl"))
    gx = input_grad(idx, xl, gx_keep, flip(gx_give, "zh"), id_keep, id_recv)
    gx = swap(gx.reshape(images, rows * width // 4, chans), DP)
    pixels_grad = widen(gx, rows, width)

    identity_kernel_grad = outer(full_x, go, 1.0)
    out_kernel_grad = outer(full_three, go, post_gain)
    bias_rows = jnp.broadcast_to(identity_bias_grad, (16, outs))
    identity_kernel_grad, out_kernel_grad = lax.psum(
        (identity_kernel_grad, jnp.concatenate([out_kernel_grad, bias_rows])), DP
    )
    identity_bias_grad = out_kernel_grad[-1:]
    out_kernel_grad = out_kernel_grad[:-16]

    keep_three, give_three = weight_grad(side, half, idx, gp_three, act_two, act_two_other, chips)
    recv_three = flip(give_three, "core")
    keep_two, give_two = weight_grad(side, half, idx, gp_two, act_one, act_one_other, chips)
    recv_two = flip(give_two, "core")
    parts = pair_sum(keep_two, recv_two, keep_three, recv_three)
    parts = [parts[0]] + [hop(parts[j], j, chips) for j in range(1, chips)]
    keep, give = chip_sum(idx, parts)
    total = (keep + flip(give, "zh").astype(f32)).astype(bf16)
    total = jnp.stack(gather_chips(total, chips))
    kernel_two_grad, bias_two_grad, kernel_three_grad, bias_three_grad = final_grads(
        idx, total, flip(total, "core")
    )

    keep_one, give_one = weight_one_grad(side, idx, gp_mine, gp_theirs, act_zero, chips)
    parts = pair_sum(keep_one, flip(give_one, "core"))
    total = parts[0].astype(f32)
    for j in range(1, chips):
        total = total + hop(parts[j], j, chips).astype(f32)
    total = jnp.stack(gather_chips(total.astype(bf16)[None], chips))
    kernel_one_grad, bias_one_grad = final_grads(idx, total, flip(total, "core"))

    return (
        block_out.reshape(cotangent.shape),
        pixels_grad,
        kernel_one_grad.reshape(kernel_one.shape),
        bias_one_grad[0],
        kernel_two_grad.reshape(kernel_two.shape),
        bias_two_grad[0],
        kernel_three_grad.reshape(kernel_three.shape),
        bias_three_grad[0],
        out_kernel_grad.astype(f32),
        identity_kernel_grad.astype(f32),
        identity_bias_grad.astype(f32)[0],
    )


def solution(mesh):
    members = mesh.devices.size // mesh.shape["mp"]
    fine = Mesh(
        mesh.devices.reshape(members // 2, 2, 2, mesh.shape["mp"] // 2),
        ("chip", "core", "zh", "zl"),
    )
    return jax.shard_map(
        local,
        mesh=fine,
        in_specs=(
            P(None, DP, None, MP),
            P(),
            P(None, None, None, MP),
            P(MP),
            P(None, None, None, MP),
            P(MP),
            P(None, None, None, MP),
            P(MP),
            P(None, MP),
            P(None, MP),
            P(MP),
            P(DP, None, None, MP),
        ),
        out_specs=(
            P(DP, None, None, MP),
            P(None, DP, None, MP),
            P(None, None, None, MP),
            P(MP),
            P(None, None, None, MP),
            P(MP),
            P(None, None, None, MP),
            P(MP),
            P(None, MP),
            P(None, MP),
            P(MP),
        ),
        check_vma=False,
    )
```

```python
import functools

import jax
import jax.numpy as jnp
from jax import lax
from jax.experimental import pallas as pl
from jax.experimental.pallas import tpu as pltpu
from jax.sharding import Mesh
from jax.sharding import PartitionSpec as P


post_gain = 0.015625
slope = 0.7978845608028654
cubic = 0.044715
halo = 6
bf16 = jnp.bfloat16
f32 = jnp.float32
NT = (((1,), (1,)), ((), ()))
TN = (((0,), (0,)), ((), ()))
NN = (((1,), (0,)), ((), ()))
DP = ("chip", "core")
MP = ("zh", "zl")


def dot(left, right, dims=NN):
    return lax.dot_general(left, right, dims, preferred_element_type=f32)


def gelu(value):
    inner = jnp.tanh(slope * (value + cubic * value * value * value))
    return 0.5 * value * (1.0 + inner)


def gelu_slope(value):
    square = value * value
    inner = jnp.tanh(slope * value * (1.0 + cubic * square))
    climb = slope * (1.0 + 3.0 * cubic * square)
    return 0.5 * (1.0 + inner) + 0.5 * value * (1.0 - inner * inner) * climb


def struct(shape, kind):
    return jax.ShapeDtypeStruct(shape, kind)


def lanes(blocks):
    return blocks[0] if len(blocks) == 1 else jnp.concatenate(blocks, axis=1)


VMEM = pl.BlockSpec(memory_space=pltpu.VMEM)
SMEM = pl.BlockSpec(memory_space=pltpu.SMEM)
FAR = pl.BlockSpec(memory_space=pl.ANY)


def call(body, name, ins, outs, scratch=(), flops=0, **more):
    spaces = [space for space, _ in ins]
    arrays = [array for _, array in ins]
    out_specs = [space for space, _ in outs]
    out_shape = [shape for _, shape in outs]
    moved = sum(a.size * a.dtype.itemsize for a in arrays + out_shape)
    single = len(outs) == 1
    return pl.pallas_call(
        body,
        in_specs=spaces,
        out_specs=out_specs[0] if single else out_specs,
        out_shape=out_shape[0] if single else out_shape,
        scratch_shapes=list(scratch),
        compiler_params=pltpu.CompilerParams(vmem_limit_bytes=60 << 20),
        cost_estimate=pl.CostEstimate(flops=int(flops), bytes_accessed=moved, transcendentals=0),
        name=name,
        **more,
    )(*arrays)


def run_copies(pairs, sems):
    copies = [pltpu.make_async_copy(a, b, sems.at[i]) for i, (a, b) in enumerate(pairs)]
    for copy in copies:
        copy.start()
    for copy in copies:
        copy.wait()


def slice_copies(group, idx_ref, own, blocks, sibling, wbuf):
    chip, core, zh = idx_ref[0], idx_ref[1], idx_ref[2]
    size = blocks.shape[-2]
    pairs = [(own, wbuf.at[zh])]
    for j in range(blocks.shape[0]):
        for source, owner in ((blocks, core), (sibling, 1 - core)):
            spot = at((2 * (chip ^ j) + owner) * size, size, size)
            pairs.append((source.at[j, group], wbuf.at[1 - zh, :, spot, :]))
    return pairs


def at(start, size, unit):
    return pl.ds(pl.multiple_of(start, unit), size)


def pool_body(x_ref, out_ref):
    rows, width, chans = x_ref.shape[1:]
    half = width // 2
    pixel = lax.broadcasted_iota(jnp.int32, (half, 2 * width), 1)
    place = lax.broadcasted_iota(jnp.int32, (half, 2 * width), 0)
    inside = (lax.rem(pixel, width) >= 2 * place) & (lax.rem(pixel, width) < 2 * place + 2)
    pick = jnp.where(inside, 0.25, 0.0).astype(bf16)
    for row in range(rows // 2):
        window = x_ref[0, 2 * row : 2 * row + 2].reshape(2 * width, chans)
        out_ref[0, row * half : (row + 1) * half, :] = dot(pick, window).astype(bf16)


def pool(pixels):
    images, rows, width, chans = pixels.shape
    spots = rows * width // 4
    block = pl.BlockSpec((1, rows, width, chans), lambda i: (i, 0, 0, 0))
    out = pl.BlockSpec((1, spots, chans), lambda i: (i, 0, 0))
    return call(
        pool_body,
        "pool",
        [(block, pixels)],
        [(out, struct((images, spots, chans), bf16))],
        grid=(images,),
    )


def widen_body(g_ref, out_ref):
    rows, width, chans = out_ref.shape[1:]
    half = width // 2
    pixel = lax.broadcasted_iota(jnp.int32, (width, half), 0)
    place = lax.broadcasted_iota(jnp.int32, (width, half), 1)
    inside = (pixel >= 2 * place) & (pixel < 2 * place + 2)
    pick = jnp.where(inside, 0.25, 0.0).astype(bf16)
    for row in range(rows // 2):
        wide = dot(pick, g_ref[0, row * half : (row + 1) * half, :]).astype(bf16)
        out_ref[0, 2 * row] = wide
        out_ref[0, 2 * row + 1] = wide


def widen(grad, rows, width):
    images, spots, chans = grad.shape
    block = pl.BlockSpec((1, spots, chans), lambda i: (i, 0, 0))
    out = pl.BlockSpec((1, rows, width, chans), lambda i: (i, 0, 0, 0))
    return call(
        widen_body,
        "widen",
        [(block, grad)],
        [(out, struct((images, rows, width, chans), bf16))],
        grid=(images,),
    )


def conv_body(side, first, group, idx_ref, *refs):
    zh, zl = idx_ref[2], idx_ref[3]
    if first:
        xl, xa, xh, xd, wl, wo, ws, bl, bo, pre_ref, act_ref, xbuf, wbuf, acc, sems = refs
        chans = xl.shape[1]
        spots = xbuf.shape[0]
        begin = zh * (xl.shape[0] - spots)
        pairs = []
        for source, up, along in ((xl, zh, zl), (xa, zh, 1 - zl), (xh, 1 - zh, zl), (xd, 1 - zh, 1 - zl)):
            if source is xl:
                source = xl.at[at(begin, spots, side), :]
            pairs.append((source, xbuf.at[:, at((2 * up + along) * chans, chans, chans)]))
    else:
        xl, xa, wl, wo, ws, bl, bo, pre_ref, act_ref, xbuf, wbuf, acc, sems = refs
        chans = xl.shape[1] // 2
        spots = xbuf.shape[0]
        pairs = []
        for source, along in ((xl, zl), (xa, 1 - zl)):
            for up in range(2):
                pairs.append(
                    (
                        source.at[:, up * chans : (up + 1) * chans],
                        xbuf.at[:, at((2 * up + along) * chans, chans, chans)],
                    )
                )
    run_copies(slice_copies(group, idx_ref, wl, wo, ws, wbuf) + pairs, sems)
    acc[...] = jnp.zeros_like(acc)
    outs = 2 * wl.shape[2]
    block = spots // 2
    for x in range(3):
        weights = lanes([wbuf[u, 3 * y + x] for y in range(3) for u in range(2)])
        for begin in range(0, spots, block):
            values = xbuf[begin : begin + block, :]
            if first:
                values = gelu(values.astype(f32)).astype(bf16)
            product = dot(values, weights)
            for y in range(3):
                place = begin + side * (2 - y)
                acc[x, place : place + block, :] += product[:, y * outs : (y + 1) * outs]
    spot = lax.broadcasted_iota(jnp.int32, (block, outs), 0)
    column = lax.rem(spot, side)
    own, other = bl[...], bo[...]
    bias = lanes([jnp.where(zh == 0, own, other), jnp.where(zh == 0, other, own)])
    for begin in range(0, spots, block):
        place = begin + side
        left = pltpu.roll(acc[0, place : place + block, :], 1, 0)
        right = pltpu.roll(acc[2, place : place + block, :], block - 1, 0)
        pre = acc[1, place : place + block, :] + bias
        pre = pre + jnp.where(column > 0, left, 0.0)
        pre = pre + jnp.where(column < side - 1, right, 0.0)
        pre_ref[begin : begin + block, :] = pre
        act_ref[begin : begin + block, :] = gelu(pre).astype(bf16)


def conv(side, idx, sources, own, other, group, bias, bias_other, first=False):
    taps, depth, outs = own.shape
    spots = sources[1].shape[0]
    return call(
        functools.partial(conv_body, side, first, group),
        "conv",
        [(SMEM, idx)]
        + [(FAR, s) for s in sources]
        + [(FAR, own), (FAR, other[0]), (FAR, other[1])]
        + [(VMEM, bias.reshape(1, outs)), (VMEM, bias_other.reshape(1, outs))],
        [(VMEM, struct((spots, 2 * outs), f32)), (VMEM, struct((spots, 2 * outs), bf16))],
        [
            pltpu.VMEM((spots, depth), bf16),
            pltpu.VMEM((2, taps, depth, outs), bf16),
            pltpu.VMEM((3, spots + 2 * side, 2 * outs), f32),
            pltpu.SemaphoreType.DMA((2 * other[0].shape[0] + 5,)),
        ],
        flops=4 * spots * taps * depth * outs,
    )


def spread_taps(side, grad, taps_ref):
    pixels, outs = grad.shape
    spot = lax.broadcasted_iota(jnp.int32, (pixels, outs), 0)
    column = lax.rem(spot, side)
    wide = grad.astype(f32)
    ahead = jnp.where(column < side - 1, pltpu.roll(wide, pixels - 1, 0), 0.0).astype(bf16)
    behind = jnp.where(column > 0, pltpu.roll(wide, 1, 0), 0.0).astype(bf16)
    edge = jnp.zeros((side, 3 * outs), bf16)
    taps_ref[:side, :] = edge
    taps_ref[side + pixels :, :] = edge
    taps_ref[side : side + pixels, :] = jnp.concatenate([ahead, grad, behind], axis=1)


def tap_block(side, taps_ref, begin, block):
    return lanes([taps_ref[at(begin + side * (2 - y), block, side), :] for y in range(3)])


def back_body(side, last, group, idx_ref, keep_ref, recv_ref, pre_ref, wl, wo, ws, *refs):
    zh, zl = idx_ref[2], idx_ref[3]
    if last:
        mine_ref, theirs_ref, own_ref, give_ref, gp_ref, taps_ref, wbuf, sems = refs
    else:
        gp_ref, own_ref, give_ref, taps_ref, wbuf, sems = refs
    pairs = slice_copies(group, idx_ref, wl, wo, ws, wbuf)
    copies = [pltpu.make_async_copy(a, b, sems.at[i]) for i, (a, b) in enumerate(pairs)]
    for copy in copies:
        copy.start()
    total = keep_ref[...] + recv_ref[...].astype(f32)
    grad = (total * gelu_slope(pre_ref[...])).astype(bf16)
    gp_ref[...] = grad
    spread_taps(side, grad, taps_ref)
    depth, outs = wl.shape[1:]
    pixels = pre_ref.shape[0]
    if last:
        start = zh * halo * side
        pixels = mine_ref.shape[0]
        own = gp_ref[at(start, pixels, side), :]
        low, high = own[:, :outs], own[:, outs:]
        mine_ref[...] = jnp.where(zh == 0, low, high)
        theirs_ref[...] = jnp.where(zh == 0, high, low)
    for copy in copies:
        copy.wait()
    block = pixels // 2
    chans = depth // 4

    def rows(index):
        spot = at(index * chans, chans, chans)
        return lanes([wbuf[u, t, spot, :] for t in range(9) for u in range(2)])

    for target, along in ((give_ref, 1 - zl), (own_ref, zl)):
        if last:
            for up in range(2):
                weights = rows(2 * up + along)
                for begin in range(0, pixels, block):
                    part = dot(tap_block(side, taps_ref, start + begin, block), weights, NT)
                    target[up, begin : begin + block, :] = part.astype(target.dtype)
        else:
            weights = jnp.concatenate([rows(along), rows(2 + along)], axis=0)
            for begin in range(0, pixels, block):
                part = dot(tap_block(side, taps_ref, begin, block), weights, NT)
                target[begin : begin + block, :] = part.astype(target.dtype)


def back(side, idx, keep, recv, pre, own, other, group, half=0):
    taps, depth, outs = own.shape
    spots = pre.shape[0]
    if half:
        shape = (2, half, depth // 4)
        results = [
            (VMEM, struct((half, outs), bf16)),
            (VMEM, struct((half, outs), bf16)),
        ]
    else:
        shape = (spots, depth // 2)
        results = [(VMEM, struct((spots, 2 * outs), bf16))]
    results += [(VMEM, struct(shape, f32)), (VMEM, struct(shape, bf16))]
    scratch = [
        pltpu.VMEM((spots + 2 * side, 6 * outs), bf16),
        pltpu.VMEM((2, taps, depth, outs), bf16),
        pltpu.SemaphoreType.DMA((2 * other[0].shape[0] + 1,)),
    ]
    if half:
        scratch = [pltpu.VMEM((spots, 2 * outs), bf16)] + scratch
    return call(
        functools.partial(back_body, side, bool(half), group),
        "back",
        [(SMEM, idx), (VMEM, keep), (VMEM, recv), (VMEM, pre)]
        + [(FAR, own), (FAR, other[0]), (FAR, other[1])],
        results,
        scratch,
        flops=4 * spots * taps * depth * outs,
    )


def put_blocks(idx_ref, keep_ref, give_ref, part, tap, first_block, size, *inner):
    chip, core = idx_ref[0], idx_ref[1]
    for b in range(0, part.shape[0] // size, 2):
        even = part[b * size : (b + 1) * size, :]
        odd = part[(b + 1) * size : (b + 2) * size, :]
        slot = chip ^ ((first_block + b) // 2)
        rows = slice(tap * size, (tap + 1) * size)
        keep_ref[(slot,) + inner + (rows, slice(None))] = jnp.where(core == 0, even, odd).astype(bf16)
        give_ref[(slot,) + inner + (rows, slice(None))] = jnp.where(core == 0, odd, even).astype(bf16)


def weight_body(side, half, idx_ref, gp_ref, xl, xa, keep_ref, give_ref, xbuf, taps_ref, sems):
    zh, zl = idx_ref[2], idx_ref[3]
    chans = xl.shape[1] // 2
    pairs = []
    for source, along in ((xl, zl), (xa, 1 - zl)):
        for up in range(2):
            pairs.append(
                (
                    source.at[:, up * chans : (up + 1) * chans],
                    xbuf.at[:, at((2 * up + along) * chans, chans, chans)],
                )
            )
    run_copies(pairs, sems)
    spots, wide = gp_ref.shape
    outs = wide // 2
    spot = lax.broadcasted_iota(jnp.int32, (spots, wide), 0) - zh * halo * side
    grad = jnp.where((spot >= 0) & (spot < half), gp_ref[...].astype(f32), 0.0)
    bias = jnp.sum(grad, axis=0, keepdims=True)
    spread_taps(side, grad.astype(bf16), taps_ref)
    blocks = 2 * keep_ref.shape[0]
    depth = xbuf.shape[1]
    size = depth // blocks
    for begin in range(0, depth, 256):
        values = xbuf[:, begin : begin + 256]
        for y in range(3):
            place = side * (2 - y)
            part = dot(values, taps_ref[place : place + spots, :], TN)
            for x in range(3):
                for u in range(2):
                    col = x * wide + u * outs
                    put_blocks(
                        idx_ref, keep_ref, give_ref, part[:, col : col + outs],
                        3 * y + x, begin // size, size, u,
                    )
    for u in range(2):
        row = jnp.broadcast_to(bias[:, u * outs : (u + 1) * outs], (16, outs)).astype(bf16)
        for j in range(keep_ref.shape[0]):
            keep_ref[j, u, 9 * size :, :] = row
            give_ref[j, u, 9 * size :, :] = row


def weight_grad(side, half, idx, grad, act, act_other, chips):
    spots, wide = grad.shape
    outs = wide // 2
    depth = 2 * act.shape[1]
    rows = 9 * depth // (2 * chips) + 16
    return call(
        functools.partial(weight_body, side, half),
        "weight_grad",
        [(SMEM, idx), (VMEM, grad), (FAR, act), (FAR, act_other)],
        [(VMEM, struct((chips, 2, rows, outs), bf16))] * 2,
        [
            pltpu.VMEM((spots, depth), bf16),
            pltpu.VMEM((spots + 2 * side, 3 * wide), bf16),
            pltpu.SemaphoreType.DMA((4,)),
        ],
        flops=36 * spots * depth * outs,
    )


def weight_one_body(side, idx_ref, mine_ref, theirs_ref, x_ref, keep_ref, give_ref, gp_ref, taps_ref):
    zh = idx_ref[2]
    half, outs = mine_ref.shape
    gp_ref[at(zh * half, half, side), :] = mine_ref[...]
    gp_ref[at((1 - zh) * half, half, side), :] = theirs_ref[...]
    grad = gp_ref[...]
    bias = jnp.sum(grad.astype(f32), axis=0, keepdims=True)
    spread_taps(side, grad, taps_ref)
    blocks = 2 * keep_ref.shape[0]
    spots, depth = x_ref.shape
    size = depth // blocks
    right = tap_block(side, taps_ref, 0, spots)
    for begin in range(0, depth, 256):
        part = dot(x_ref[:, begin : begin + 256], right, TN)
        for tap in range(9):
            put_blocks(
                idx_ref, keep_ref, give_ref, part[:, tap * outs : (tap + 1) * outs],
                tap, begin // size, size,
            )
    row = jnp.broadcast_to(bias, (16, outs)).astype(bf16)
    for j in range(keep_ref.shape[0]):
        keep_ref[j, 9 * size :, :] = row
        give_ref[j, 9 * size :, :] = row


def weight_one_grad(side, idx, mine, theirs, act_zero, chips):
    spots, depth = act_zero.shape
    outs = mine.shape[1]
    rows = 9 * depth // (2 * chips) + 16
    return call(
        functools.partial(weight_one_body, side),
        "weight_one_grad",
        [(SMEM, idx), (VMEM, mine), (VMEM, theirs), (VMEM, act_zero)],
        [(VMEM, struct((chips, rows, outs), bf16))] * 2,
        [
            pltpu.VMEM((spots, outs), bf16),
            pltpu.VMEM((spots + 2 * side, 3 * outs), bf16),
        ],
        flops=18 * spots * depth * outs,
    )


def pair_body(groups, *refs):
    ins, outs = refs[: 2 * groups], refs[2 * groups :]
    for j, out in enumerate(outs):
        for g in range(groups):
            total = (ins[2 * g][j].astype(f32) + ins[2 * g + 1][j].astype(f32)).astype(bf16)
            if groups == 1:
                out[...] = total
            else:
                out[:, g] = total


def pair_sum(*pairs):
    groups = len(pairs) // 2
    chips = pairs[0].shape[0]
    shape = pairs[0].shape[1:]
    if groups > 1:
        shape = shape[:1] + (groups,) + shape[1:]
    return call(
        functools.partial(pair_body, groups),
        "pair_sum",
        [(VMEM, p) for p in pairs],
        [(VMEM, struct(shape, bf16))] * chips,
    )


def chip_body(idx_ref, *refs):
    parts, (keep_ref, give_ref) = refs[:-2], refs[-2:]
    zh = idx_ref[2]
    for target, slot in ((keep_ref, zh), (give_ref, 1 - zh)):
        total = parts[0][slot].astype(f32)
        for part in parts[1:]:
            total = total + part[slot].astype(f32)
        target[...] = total.astype(target.dtype)


def chip_sum(idx, parts):
    shape = parts[0].shape[1:]
    return call(
        chip_body,
        "chip_sum",
        [(SMEM, idx)] + [(VMEM, p) for p in parts],
        [(VMEM, struct(shape, f32)), (VMEM, struct(shape, bf16))],
    )


def final_body(groups, idx_ref, own_ref, sib_ref, *outs):
    chip, core = idx_ref[0], idx_ref[1]
    size = (own_ref.shape[-2] - 16) // 9
    for g in range(groups):
        grad_ref, bias_ref = outs[2 * g : 2 * g + 2]
        bias_ref[...] = own_ref[0, g, 9 * size : 9 * size + 1, :].astype(f32)
        for j in range(own_ref.shape[0]):
            for source, owner in ((own_ref, core), (sib_ref, 1 - core)):
                spot = at((2 * (chip ^ j) + owner) * size, size, size)
                for tap in range(9):
                    grad_ref[tap, spot, :] = source[j, g, tap * size : (tap + 1) * size, :].astype(f32)


def final_grads(idx, own, sib):
    chips, groups, rows, outs = own.shape
    depth = 2 * chips * ((rows - 16) // 9)
    return call(
        functools.partial(final_body, groups),
        "final_grads",
        [(SMEM, idx), (VMEM, own), (VMEM, sib)],
        [(VMEM, struct((9, depth, outs), f32)), (VMEM, struct((1, outs), f32))] * groups,
    )


def outer_body(gain, x_ref, go_ref, out_ref):
    out_ref[...] = (gain * dot(x_ref[...], go_ref[...], TN)).astype(bf16)


def outer(x, go, gain):
    spots, depth = x.shape
    outs = go.shape[1]
    return call(
        functools.partial(outer_body, gain),
        "outer",
        [
            (pl.BlockSpec((spots, 256), lambda k: (0, k)), x),
            (pl.BlockSpec((spots, outs), lambda k: (0, 0)), go),
        ],
        [(pl.BlockSpec((256, outs), lambda k: (k, 0)), struct((depth, outs), bf16))],
        flops=2 * spots * depth * outs,
        grid=(depth // 256,),
    )


def start_body(idx_ref, valid_ref, cot_ref, outk_ref, go_ref, bias_ref, own_ref, give_ref):
    zl = idx_ref[3]
    masked = cot_ref[...].astype(f32) * valid_ref[0]
    go_ref[...] = masked.astype(bf16)
    bias_ref[...] = jnp.sum(masked, axis=0, keepdims=True).astype(bf16)
    chans = outk_ref.shape[0] // 4
    block = cot_ref.shape[0] // 4
    for target, along in ((give_ref, 1 - zl), (own_ref, zl)):
        weights = jnp.concatenate(
            [outk_ref[at((2 * up + along) * chans, chans, chans), :] for up in range(2)], axis=0
        )
        for begin in range(0, cot_ref.shape[0], block):
            part = post_gain * dot(go_ref[begin : begin + block, :], weights, NT)
            target[begin : begin + block, :] = part.astype(target.dtype)


def start_back(idx, valid, cot, outk):
    spots, outs = cot.shape
    half = outk.shape[0] // 2
    return call(
        start_body,
        "start_back",
        [(SMEM, idx), (SMEM, valid), (VMEM, cot), (VMEM, outk)],
        [
            (VMEM, struct(cot.shape, bf16)),
            (VMEM, struct((1, outs), bf16)),
            (VMEM, struct((spots, half), f32)),
            (VMEM, struct((spots, half), bf16)),
        ],
        flops=4 * spots * outs * half,
    )


def identity_body(idx_ref, go_ref, idk_ref, own_ref, give_ref):
    zl = idx_ref[3]
    chans = idk_ref.shape[0] // 4
    block = go_ref.shape[0] // 4
    for target, along in ((give_ref, 1 - zl), (own_ref, zl)):
        for up in range(2):
            weights = idk_ref[at((2 * up + along) * chans, chans, chans), :]
            for begin in range(0, go_ref.shape[0], block):
                part = dot(go_ref[begin : begin + block, :], weights, NT)
                target[up, begin : begin + block, :] = part.astype(target.dtype)


def identity_back(idx, go, idk):
    spots, outs = go.shape
    chans = idk.shape[0] // 4
    return call(
        identity_body,
        "identity_back",
        [(SMEM, idx), (VMEM, go), (VMEM, idk)],
        [(VMEM, struct((2, spots, chans), f32)), (VMEM, struct((2, spots, chans), bf16))],
        flops=8 * spots * outs * chans,
    )


def rows_body(side, idx_ref, own_ref, recv_ref, keep_ref, give_ref):
    zh = idx_ref[2]
    spots = keep_ref.shape[0]
    apart = own_ref.shape[0] - spots
    for target, begin in ((give_ref, (1 - zh) * apart), (keep_ref, zh * apart)):
        spot = at(begin, spots, side)
        total = own_ref[spot, :] + recv_ref[spot, :].astype(f32)
        target[...] = total.astype(target.dtype)


def rows_sum(side, idx, own, recv, spots):
    shape = (spots, own.shape[1])
    return call(
        functools.partial(rows_body, side),
        "rows_sum",
        [(SMEM, idx), (VMEM, own), (VMEM, recv)],
        [(VMEM, struct(shape, f32)), (VMEM, struct(shape, bf16))],
    )


def slots_body(idx_ref, own_ref, recv_ref, keep_ref, give_ref):
    zh = idx_ref[2]
    for target, slot in ((give_ref, 1 - zh), (keep_ref, zh)):
        total = own_ref[slot] + recv_ref[slot].astype(f32)
        target[...] = total.astype(target.dtype)


def slots_sum(idx, own, recv):
    shape = own.shape[1:]
    return call(
        slots_body,
        "slots_sum",
        [(SMEM, idx), (VMEM, own), (VMEM, recv)],
        [(VMEM, struct(shape, f32)), (VMEM, struct(shape, bf16))],
    )


def input_body(idx_ref, x_ref, keep_ref, recv_ref, id_ref, id_recv_ref, out_ref):
    zh = idx_ref[2]
    half = keep_ref.shape[0]
    for part in range(2):
        rows = slice(part * half, (part + 1) * half)
        conv = jnp.where(zh == part, keep_ref[...], recv_ref[...].astype(f32))
        straight = id_ref[rows, :] + id_recv_ref[rows, :].astype(f32)
        total = conv * gelu_slope(x_ref[rows, :].astype(f32)) + straight
        out_ref[rows, :] = total.astype(bf16)


def input_grad(idx, x, keep, recv, id_keep, id_recv):
    return call(
        input_body,
        "input_grad",
        [(SMEM, idx)] + [(VMEM, a) for a in (x, keep, recv, id_keep, id_recv)],
        [(VMEM, struct(x.shape, bf16))],
    )


def whole_body(side, idx_ref, xl, xa, xh, xd, rh, rl, x_ref, act_ref, sems):
    zh, zl = idx_ref[2], idx_ref[3]
    chans = xl.shape[1]
    spots = xa.shape[0]
    rest = xl.shape[0] - spots
    window, outside = at(zh * rest, spots, side), at((1 - zh) * spots, rest, side)

    def cols(up, along):
        return at((2 * up + along) * chans, chans, chans)

    run_copies(
        [
            (xl, x_ref.at[:, cols(zh, zl)]),
            (xa, x_ref.at[window, cols(zh, 1 - zl)]),
            (xh, x_ref.at[window, cols(1 - zh, zl)]),
            (xd, x_ref.at[window, cols(1 - zh, 1 - zl)]),
            (rl.at[0], x_ref.at[outside, cols(zh, 1 - zl)]),
            (rh, x_ref.at[outside, cols(1 - zh, zl)]),
            (rl.at[1], x_ref.at[outside, cols(1 - zh, 1 - zl)]),
        ],
        sems,
    )
    block = x_ref.shape[0] // 8
    for begin in range(0, x_ref.shape[0], block):
        rows = slice(begin, begin + block)
        act_ref[rows, :] = gelu(x_ref[rows, :].astype(f32)).astype(bf16)


def whole_input(side, idx, *parts):
    spots, chans = parts[0].shape
    return call(
        functools.partial(whole_body, side),
        "whole_input",
        [(SMEM, idx)] + [(FAR, p) for p in parts],
        [(VMEM, struct((spots, 4 * chans), bf16))] * 2,
        [pltpu.SemaphoreType.DMA((7,))],
    )


def join_body(idx_ref, own, recv, out, sems):
    zh, zl = idx_ref[2], idx_ref[3]
    half = own.shape[1]
    chans = own.shape[2] // 2
    pairs = []
    for source, along in ((own, zl), (recv, 1 - zl)):
        for part, up in ((0, zh), (1, 1 - zh)):
            for slot in range(2):
                spot = at((2 * slot + along) * chans, chans, chans)
                pairs.append(
                    (
                        source.at[part, :, slot * chans : (slot + 1) * chans],
                        out.at[at(up * half, half, half), spot],
                    )
                )
    run_copies(pairs, sems)


def join(idx, own, recv):
    _, half, wide = own.shape
    return call(
        join_body,
        "join",
        [(SMEM, idx), (FAR, own), (FAR, recv)],
        [(VMEM, struct((2 * half, 2 * wide), bf16))],
        [pltpu.SemaphoreType.DMA((8,))],
    )


def finish_body(valid_ref, x_ref, act_ref, idk_ref, outk_ref, ib_ref, out_ref):
    identity = dot(x_ref[...], idk_ref[...]) + ib_ref[...]
    branch = dot(act_ref[...], outk_ref[...])
    out_ref[...] = ((identity + post_gain * branch) * valid_ref[0]).astype(bf16)


def finish(valid, x, act, idk, outk, ib):
    spots, depth = x.shape
    outs = idk.shape[1]
    block = spots // 4
    by_row = lambda wide: pl.BlockSpec((block, wide), lambda k: (k, 0))
    full = lambda a: pl.BlockSpec(a.shape, lambda k: (0, 0))
    ib = ib.reshape(1, outs)
    return call(
        finish_body,
        "finish",
        [(SMEM, valid), (by_row(depth), x), (by_row(act.shape[1]), act)]
        + [(full(a), a) for a in (idk, outk, ib)],
        [(by_row(outs), struct((spots, outs), bf16))],
        flops=2 * spots * outs * (depth + act.shape[1]),
        grid=(4,),
    )


def flip(value, axis):
    return lax.ppermute(value, axis, [(0, 1), (1, 0)])


def hop(value, j, chips):
    return lax.ppermute(value, "chip", [(i, i ^ j) for i in range(chips)])


def gather_chips(value, chips):
    return [value] + [hop(value, j, chips) for j in range(1, chips)]


def swap(pieces, axis):
    return lax.all_to_all(pieces, axis, split_axis=0, concat_axis=0, tiled=True)


def after(value, other):
    return lax.optimization_barrier((value, other))[0]


def rows_of(value, start, size):
    return lax.dynamic_slice_in_dim(value, start, size, 0)


def local(
    pixels,
    counts,
    kernel_one,
    bias_one,
    kernel_two,
    bias_two,
    kernel_three,
    bias_three,
    out_kernel,
    identity_kernel,
    identity_bias,
    cotangent,
):
    images, rows, width, chans = pixels.shape
    side = width // 2
    spots = side * side
    half = spots // 2
    window = half + halo * side
    outs = cotangent.shape[3]
    chips = lax.axis_size("chip")
    chip, core, zh, zl = [lax.axis_index(a) for a in ("chip", "core", "zh", "zl")]
    idx = jnp.stack([chip, core, zh, zl]).astype(jnp.int32)
    taps = lambda kernel: kernel.reshape((9,) + kernel.shape[2:])
    one, two, three = taps(kernel_one), taps(kernel_two), taps(kernel_three)

    own_count = lax.dynamic_index_in_dim(counts, 2 * chip + core, 0, keepdims=True)
    valid = (own_count > 0).astype(f32)

    def block_of(kernel):
        size = kernel.shape[1] // (2 * chips)
        return lax.dynamic_slice_in_dim(kernel, (2 * chip + core) * size, size, 1)

    def other_half(*kernels):
        return jnp.stack([block_of(kernel) for kernel in kernels])

    def around(piece):
        own = jnp.stack(gather_chips(piece, chips))
        return own, flip(own, "core")

    bias_other = flip(jnp.stack([bias_one, bias_two, bias_three]), "zh")
    first_piece = flip(other_half(one), "zh")
    pooled = pool(pixels)
    xl = swap(pooled, DP).reshape(spots, chans)
    begin = zh * (spots - window)
    begin_other = (1 - zh) * (spots - window)
    xa = flip(rows_of(xl, begin, window), "zl")
    xh = flip(rows_of(xl, begin_other, window), "zh")
    one_other = around(after(first_piece, xl))
    xd = flip(xh, "zl")
    both_other = around(flip(after(other_half(two, three), xh), "zh"))

    go, identity_bias_grad, ga_own, ga_give = start_back(
        idx, valid, after(cotangent.reshape(spots, outs), pooled), out_kernel
    )
    pre_one, act_one = conv(side, idx, (xl, xa, xh, xd), one, one_other, 0, bias_one, bias_other[0], True)
    act_one_other = flip(act_one, "zl")
    pre_two, act_two = conv(side, idx, (act_one, act_one_other), two, both_other, 0, bias_two, bias_other[1])
    act_two_other = flip(act_two, "zl")
    ga_keep, ga_give = rows_sum(side, idx, ga_own, flip(ga_give, "zl"), window)
    ga_recv = flip(ga_give, "zh")
    pre_three, act_three = conv(
        side, idx, (act_two, act_two_other), three, both_other, 1, bias_three, bias_other[2]
    )

    gp_three, ga_own, ga_give = back(side, idx, ga_keep, ga_recv, pre_three, three, both_other, 1)
    ga_recv = flip(ga_give, "zl")
    gp_two, ga_own, ga_give = back(side, idx, ga_own, ga_recv, pre_two, two, both_other, 0)
    ga_recv = flip(ga_give, "zl")
    gp_mine, gp_theirs, gx_own, gx_give = back(
        side, idx, ga_own, ga_recv, pre_one, one, one_other, 0, half
    )
    gp_theirs = flip(gp_theirs, "zh")

    rest = spots - window
    rest_own = rows_of(xl, (1 - zh) * window, rest)
    rest_high = flip(rows_of(xl, zh * window, rest), "zh")
    rest_low = flip(jnp.stack([rest_own, rest_high]), "zl")
    full_x, act_zero = whole_input(side, idx, xl, xa, xh, xd, rest_high, rest_low)

    own_rows = rows_of(act_three, zh * halo * side, half)
    own_rows = jnp.stack([own_rows, flip(own_rows, "zh")])
    full_three = join(idx, own_rows, flip(own_rows, "zl"))
    block_out = finish(valid, full_x, full_three, identity_kernel, out_kernel, identity_bias)

    id_own, id_give = identity_back(idx, go, identity_kernel)
    id_keep, id_give = slots_sum(idx, id_own, flip(id_give, "zl"))
    id_recv = flip(id_give, "zh")

    gx_keep, gx_give = slots_sum(idx, gx_own, flip(gx_give, "zl"))
    gx = input_grad(idx, xl, gx_keep, flip(gx_give, "zh"), id_keep, id_recv)
    gx = swap(gx.reshape(images, rows * width // 4, chans), DP)
    pixels_grad = widen(gx, rows, width)

    identity_kernel_grad = outer(full_x, go, 1.0)
    out_kernel_grad = outer(full_three, go, post_gain)
    bias_rows = jnp.broadcast_to(identity_bias_grad, (16, outs))
    identity_kernel_grad, out_kernel_grad = lax.psum(
        (identity_kernel_grad, jnp.concatenate([out_kernel_grad, bias_rows])), DP
    )
    identity_bias_grad = out_kernel_grad[-1:]
    out_kernel_grad = out_kernel_grad[:-16]

    keep_three, give_three = weight_grad(side, half, idx, gp_three, act_two, act_two_other, chips)
    recv_three = flip(give_three, "core")
    keep_two, give_two = weight_grad(side, half, idx, gp_two, act_one, act_one_other, chips)
    recv_two = flip(give_two, "core")
    parts = pair_sum(keep_two, recv_two, keep_three, recv_three)
    parts = [parts[0]] + [hop(parts[j], j, chips) for j in range(1, chips)]
    keep, give = chip_sum(idx, parts)
    total = (keep + flip(give, "zh").astype(f32)).astype(bf16)
    total = jnp.stack(gather_chips(total, chips))
    kernel_two_grad, bias_two_grad, kernel_three_grad, bias_three_grad = final_grads(
        idx, total, flip(total, "core")
    )

    keep_one, give_one = weight_one_grad(side, idx, gp_mine, gp_theirs, act_zero, chips)
    parts = pair_sum(keep_one, flip(give_one, "core"))
    total = parts[0].astype(f32)
    for j in range(1, chips):
        total = total + hop(parts[j], j, chips).astype(f32)
    total = jnp.stack(gather_chips(total.astype(bf16)[None], chips))
    kernel_one_grad, bias_one_grad = final_grads(idx, total, flip(total, "core"))

    return (
        block_out.reshape(cotangent.shape),
        pixels_grad,
        kernel_one_grad.reshape(kernel_one.shape),
        bias_one_grad[0],
        kernel_two_grad.reshape(kernel_two.shape),
        bias_two_grad[0],
        kernel_three_grad.reshape(kernel_three.shape),
        bias_three_grad[0],
        out_kernel_grad.astype(f32),
        identity_kernel_grad.astype(f32),
        identity_bias_grad.astype(f32)[0],
    )


def solution(mesh):
    members = mesh.devices.size // mesh.shape["mp"]
    fine = Mesh(
        mesh.devices.reshape(members // 2, 2, 2, mesh.shape["mp"] // 2),
        ("chip", "core", "zh", "zl"),
    )
    return jax.shard_map(
        local,
        mesh=fine,
        in_specs=(
            P(None, DP, None, MP),
            P(),
            P(None, None, None, MP),
            P(MP),
            P(None, None, None, MP),
            P(MP),
            P(None, None, None, MP),
            P(MP),
            P(None, MP),
            P(None, MP),
            P(MP),
            P(DP, None, None, MP),
        ),
        out_specs=(
            P(DP, None, None, MP),
            P(None, DP, None, MP),
            P(None, None, None, MP),
            P(MP),
            P(None, None, None, MP),
            P(MP),
            P(None, None, None, MP),
            P(MP),
            P(None, MP),
            P(None, MP),
            P(MP),
        ),
        check_vma=False,
    )
```

```python
import functools

import jax
import jax.numpy as jnp
from jax import lax
from jax.experimental import pallas as pl
from jax.experimental.pallas import tpu as pltpu
from jax.sharding import Mesh
from jax.sharding import PartitionSpec as P


post_gain = 0.015625
slope = 0.7978845608028654
cubic = 0.044715
halo = 6
bf16 = jnp.bfloat16
f32 = jnp.float32
NT = (((1,), (1,)), ((), ()))
TN = (((0,), (0,)), ((), ()))
NN = (((1,), (0,)), ((), ()))
DP = ("chip", "core")
MP = ("zh", "zl")


def dot(left, right, dims=NN):
    return lax.dot_general(left, right, dims, preferred_element_type=f32)


def gelu(value):
    inner = jnp.tanh(slope * (value + cubic * value * value * value))
    return 0.5 * value * (1.0 + inner)


def gelu_slope(value):
    square = value * value
    inner = jnp.tanh(slope * value * (1.0 + cubic * square))
    climb = slope * (1.0 + 3.0 * cubic * square)
    return 0.5 * (1.0 + inner) + 0.5 * value * (1.0 - inner * inner) * climb


def struct(shape, kind):
    return jax.ShapeDtypeStruct(shape, kind)


def lanes(blocks):
    return blocks[0] if len(blocks) == 1 else jnp.concatenate(blocks, axis=1)


VMEM = pl.BlockSpec(memory_space=pltpu.VMEM)
SMEM = pl.BlockSpec(memory_space=pltpu.SMEM)
FAR = pl.BlockSpec(memory_space=pl.ANY)


def call(body, name, ins, outs, scratch=(), vmem=14, **more):
    spaces = [space for space, _ in ins]
    arrays = [array for _, array in ins]
    out_specs = [space for space, _ in outs]
    out_shape = [shape for _, shape in outs]
    single = len(outs) == 1
    return pl.pallas_call(
        body,
        in_specs=spaces,
        out_specs=out_specs[0] if single else out_specs,
        out_shape=out_shape[0] if single else out_shape,
        scratch_shapes=list(scratch),
        compiler_params=pltpu.CompilerParams(vmem_limit_bytes=vmem << 20),
        cost_estimate=pl.CostEstimate(flops=0, bytes_accessed=0, transcendentals=0),
        name=name,
        **more,
    )(*arrays)


def run_copies(pairs, sems):
    copies = [pltpu.make_async_copy(a, b, sems.at[i]) for i, (a, b) in enumerate(pairs)]
    for copy in copies:
        copy.start()
    for copy in copies:
        copy.wait()


def slice_copies(group, idx_ref, own, blocks, sibling, wbuf):
    chip, core, zh = idx_ref[0], idx_ref[1], idx_ref[2]
    size = blocks.shape[-2]
    pairs = [(own, wbuf.at[zh])]
    for j in range(blocks.shape[0]):
        for source, owner in ((blocks, core), (sibling, 1 - core)):
            spot = at((2 * (chip ^ j) + owner) * size, size, size)
            pairs.append((source.at[j, group], wbuf.at[1 - zh, :, spot, :]))
    return pairs


def at(start, size, unit):
    return pl.ds(pl.multiple_of(start, unit), size)


def pool_body(x_ref, out_ref):
    rows, width, chans = x_ref.shape[1:]
    half = width // 2
    pixel = lax.broadcasted_iota(jnp.int32, (half, 2 * width), 1)
    place = lax.broadcasted_iota(jnp.int32, (half, 2 * width), 0)
    inside = (lax.rem(pixel, width) >= 2 * place) & (lax.rem(pixel, width) < 2 * place + 2)
    pick = jnp.where(inside, 0.25, 0.0).astype(bf16)
    for image in range(x_ref.shape[0]):
        for row in range(rows // 2):
            window = x_ref[image, 2 * row : 2 * row + 2].reshape(2 * width, chans)
            out_ref[image, row * half : (row + 1) * half, :] = dot(pick, window).astype(bf16)


def pool(pixels):
    images, rows, width, chans = pixels.shape
    spots = rows * width // 4
    step = images // 2
    block = pl.BlockSpec((step, rows, width, chans), lambda i: (i, 0, 0, 0))
    out = pl.BlockSpec((step, spots, chans), lambda i: (i, 0, 0))
    return call(
        pool_body,
        "pool",
        [(block, pixels)],
        [(out, struct((images, spots, chans), bf16))],
        grid=(2,),
    )


def widen_body(g_ref, out_ref):
    rows, width, chans = out_ref.shape[1:]
    half = width // 2
    pixel = lax.broadcasted_iota(jnp.int32, (width, half), 0)
    place = lax.broadcasted_iota(jnp.int32, (width, half), 1)
    inside = (pixel >= 2 * place) & (pixel < 2 * place + 2)
    pick = jnp.where(inside, 0.25, 0.0).astype(bf16)
    for image in range(g_ref.shape[0]):
        for row in range(rows // 2):
            wide = dot(pick, g_ref[image, row * half : (row + 1) * half, :]).astype(bf16)
            out_ref[image, 2 * row] = wide
            out_ref[image, 2 * row + 1] = wide


def widen(grad, rows, width):
    images, spots, chans = grad.shape
    step = images // 4
    block = pl.BlockSpec((step, spots, chans), lambda i: (i, 0, 0))
    out = pl.BlockSpec((step, rows, width, chans), lambda i: (i, 0, 0, 0))
    return call(
        widen_body,
        "widen",
        [(block, grad)],
        [(out, struct((images, rows, width, chans), bf16))],
        grid=(4,),
    )


def conv_body(side, first, group, idx_ref, *refs):
    zh, zl = idx_ref[2], idx_ref[3]
    if first:
        xl, xa, xh, xd, wl, wo, ws, bl, bo, pre_ref, act_ref, xbuf, wbuf, acc, sems = refs
        chans = xl.shape[1]
        spots = xbuf.shape[0]
        begin = zh * (xl.shape[0] - spots)
        pairs = []
        for source, up, along in ((xl, zh, zl), (xa, zh, 1 - zl), (xh, 1 - zh, zl), (xd, 1 - zh, 1 - zl)):
            if source is xl:
                source = xl.at[at(begin, spots, side), :]
            pairs.append((source, xbuf.at[:, at((2 * up + along) * chans, chans, chans)]))
    else:
        xl, xa, wl, wo, ws, bl, bo, pre_ref, act_ref, xbuf, wbuf, acc, sems = refs
        chans = xl.shape[1] // 2
        spots = xbuf.shape[0]
        pairs = []
        for source, along in ((xl, zl), (xa, 1 - zl)):
            for up in range(2):
                pairs.append(
                    (
                        source.at[:, up * chans : (up + 1) * chans],
                        xbuf.at[:, at((2 * up + along) * chans, chans, chans)],
                    )
                )
    run_copies(slice_copies(group, idx_ref, wl, wo, ws, wbuf) + pairs, sems)
    acc[...] = jnp.zeros_like(acc)
    outs = 2 * wl.shape[2]
    block = spots // 2
    for x in range(3):
        weights = lanes([wbuf[u, 3 * y + x] for y in range(3) for u in range(2)])
        for begin in range(0, spots, block):
            values = xbuf[begin : begin + block, :]
            if first:
                values = gelu(values.astype(f32)).astype(bf16)
            product = dot(values, weights)
            for y in range(3):
                place = begin + side * (2 - y)
                acc[x, place : place + block, :] += product[:, y * outs : (y + 1) * outs]
    spot = lax.broadcasted_iota(jnp.int32, (block, outs), 0)
    column = lax.rem(spot, side)
    own, other = bl[...], bo[...]
    bias = lanes([jnp.where(zh == 0, own, other), jnp.where(zh == 0, other, own)])
    for begin in range(0, spots, block):
        place = begin + side
        left = pltpu.roll(acc[0, place : place + block, :], 1, 0)
        right = pltpu.roll(acc[2, place : place + block, :], block - 1, 0)
        pre = acc[1, place : place + block, :] + bias
        pre = pre + jnp.where(column > 0, left, 0.0)
        pre = pre + jnp.where(column < side - 1, right, 0.0)
        pre_ref[begin : begin + block, :] = pre
        act_ref[begin : begin + block, :] = gelu(pre).astype(bf16)


def conv(side, idx, sources, own, other, group, bias, bias_other, first=False):
    taps, depth, outs = own.shape
    spots = sources[1].shape[0]
    return call(
        functools.partial(conv_body, side, first, group),
        "conv",
        [(SMEM, idx)]
        + [(FAR, s) for s in sources]
        + [(FAR, own), (FAR, other[0]), (FAR, other[1])]
        + [(VMEM, bias.reshape(1, outs)), (VMEM, bias_other.reshape(1, outs))],
        [(VMEM, struct((spots, 2 * outs), f32)), (VMEM, struct((spots, 2 * outs), bf16))],
        [
            pltpu.VMEM((spots, depth), bf16),
            pltpu.VMEM((2, taps, depth, outs), bf16),
            pltpu.VMEM((3, spots + 2 * side, 2 * outs), f32),
            pltpu.SemaphoreType.DMA((2 * other[0].shape[0] + 5,)),
        ],
        vmem=28 if first else 20,
    )


def spread_taps(side, grad, taps_ref):
    pixels, outs = grad.shape
    spot = lax.broadcasted_iota(jnp.int32, (pixels, outs), 0)
    column = lax.rem(spot, side)
    wide = grad.astype(f32)
    ahead = jnp.where(column < side - 1, pltpu.roll(wide, pixels - 1, 0), 0.0).astype(bf16)
    behind = jnp.where(column > 0, pltpu.roll(wide, 1, 0), 0.0).astype(bf16)
    edge = jnp.zeros((side, 3 * outs), bf16)
    taps_ref[:side, :] = edge
    taps_ref[side + pixels :, :] = edge
    taps_ref[side : side + pixels, :] = jnp.concatenate([ahead, grad, behind], axis=1)


def tap_block(side, taps_ref, begin, block):
    return lanes([taps_ref[at(begin + side * (2 - y), block, side), :] for y in range(3)])


def slope_body(side, idx_ref, keep_ref, recv_ref, pre_ref, mine_ref, theirs_ref, gp_ref):
    zh = idx_ref[2]
    half, outs = mine_ref.shape
    total = keep_ref[...] + recv_ref[...].astype(f32)
    gp_ref[...] = (total * gelu_slope(pre_ref[...])).astype(bf16)
    own = gp_ref[at(zh * halo * side, half, side), :]
    low, high = own[:, :outs], own[:, outs:]
    mine_ref[...] = jnp.where(zh == 0, low, high)
    theirs_ref[...] = jnp.where(zh == 0, high, low)


def slope_back(side, idx, keep, recv, pre, half):
    outs = pre.shape[1] // 2
    return call(
        functools.partial(slope_body, side),
        "slope_back",
        [(SMEM, idx), (VMEM, keep), (VMEM, recv), (VMEM, pre)],
        [
            (VMEM, struct((half, outs), bf16)),
            (VMEM, struct((half, outs), bf16)),
            (VMEM, struct(pre.shape, bf16)),
        ],
    )


def back_body(side, last, group, idx_ref, *refs):
    zh, zl = idx_ref[2], idx_ref[3]
    if last:
        grad_ref, wl, wo, ws, own_ref, give_ref, taps_ref, wbuf, sems = refs
    else:
        keep_ref, recv_ref, pre_ref, wl, wo, ws, gp_ref, own_ref, give_ref, taps_ref, wbuf, sems = refs
    pairs = slice_copies(group, idx_ref, wl, wo, ws, wbuf)
    copies = [pltpu.make_async_copy(a, b, sems.at[i]) for i, (a, b) in enumerate(pairs)]
    for copy in copies:
        copy.start()
    if last:
        grad = grad_ref[...]
    else:
        total = keep_ref[...] + recv_ref[...].astype(f32)
        grad = (total * gelu_slope(pre_ref[...])).astype(bf16)
        gp_ref[...] = grad
    spread_taps(side, grad, taps_ref)
    depth, outs = wl.shape[1:]
    pixels = own_ref.shape[-2]
    start = zh * halo * side
    for copy in copies:
        copy.wait()
    block = pixels // 2
    chans = depth // 4

    def rows(index):
        spot = at(index * chans, chans, chans)
        return lanes([wbuf[u, t, spot, :] for t in range(9) for u in range(2)])

    for target, along in ((give_ref, 1 - zl), (own_ref, zl)):
        if last:
            for up in range(2):
                weights = rows(2 * up + along)
                for begin in range(0, pixels, block):
                    part = dot(tap_block(side, taps_ref, start + begin, block), weights, NT)
                    target[up, begin : begin + block, :] = part.astype(target.dtype)
        else:
            weights = jnp.concatenate([rows(along), rows(2 + along)], axis=0)
            for begin in range(0, pixels, block):
                part = dot(tap_block(side, taps_ref, begin, block), weights, NT)
                target[begin : begin + block, :] = part.astype(target.dtype)


def back(side, idx, sources, own, other, group, half=0):
    taps, depth, outs = own.shape
    spots = sources[-1].shape[0]
    if half:
        shape = (2, half, depth // 4)
        results = []
    else:
        shape = (spots, depth // 2)
        results = [(VMEM, struct((spots, 2 * outs), bf16))]
    results += [(VMEM, struct(shape, f32)), (VMEM, struct(shape, bf16))]
    return call(
        functools.partial(back_body, side, bool(half), group),
        "back",
        [(SMEM, idx)]
        + [(VMEM, source) for source in sources]
        + [(FAR, own), (FAR, other[0]), (FAR, other[1])],
        results,
        [
            pltpu.VMEM((spots + 2 * side, 6 * outs), bf16),
            pltpu.VMEM((2, taps, depth, outs), bf16),
            pltpu.SemaphoreType.DMA((2 * other[0].shape[0] + 1,)),
        ],
        vmem=28 if half else 20,
    )


def put_blocks(idx_ref, keep_ref, give_ref, part, tap, first_block, size, *inner):
    chip, core = idx_ref[0], idx_ref[1]
    for b in range(0, part.shape[0] // size, 2):
        even = part[b * size : (b + 1) * size, :]
        odd = part[(b + 1) * size : (b + 2) * size, :]
        slot = chip ^ ((first_block + b) // 2)
        rows = slice(tap * size, (tap + 1) * size)
        keep_ref[(slot,) + inner + (rows, slice(None))] = jnp.where(core == 0, even, odd).astype(bf16)
        give_ref[(slot,) + inner + (rows, slice(None))] = jnp.where(core == 0, odd, even).astype(bf16)


def weight_body(side, half, idx_ref, gp_ref, xl, xa, keep_ref, give_ref, xbuf, taps_ref, sems):
    zh, zl = idx_ref[2], idx_ref[3]
    chans = xl.shape[1] // 2
    pairs = []
    for source, along in ((xl, zl), (xa, 1 - zl)):
        for up in range(2):
            pairs.append(
                (
                    source.at[:, up * chans : (up + 1) * chans],
                    xbuf.at[:, at((2 * up + along) * chans, chans, chans)],
                )
            )
    run_copies(pairs, sems)
    spots, wide = gp_ref.shape
    outs = wide // 2
    spot = lax.broadcasted_iota(jnp.int32, (spots, wide), 0) - zh * halo * side
    grad = jnp.where((spot >= 0) & (spot < half), gp_ref[...].astype(f32), 0.0)
    bias = jnp.sum(grad, axis=0, keepdims=True)
    spread_taps(side, grad.astype(bf16), taps_ref)
    blocks = 2 * keep_ref.shape[0]
    depth = xbuf.shape[1]
    size = depth // blocks
    for begin in range(0, depth, 256):
        values = xbuf[:, begin : begin + 256]
        for y in range(3):
            place = side * (2 - y)
            part = dot(values, taps_ref[place : place + spots, :], TN)
            for x in range(3):
                for u in range(2):
                    col = x * wide + u * outs
                    put_blocks(
                        idx_ref, keep_ref, give_ref, part[:, col : col + outs],
                        3 * y + x, begin // size, size, u,
                    )
    for u in range(2):
        row = jnp.broadcast_to(bias[:, u * outs : (u + 1) * outs], (16, outs)).astype(bf16)
        for j in range(keep_ref.shape[0]):
            keep_ref[j, u, 9 * size :, :] = row
            give_ref[j, u, 9 * size :, :] = row


def weight_grad(side, half, idx, grad, act, act_other, chips):
    spots, wide = grad.shape
    outs = wide // 2
    depth = 2 * act.shape[1]
    rows = 9 * depth // (2 * chips) + 16
    return call(
        functools.partial(weight_body, side, half),
        "weight_grad",
        [(SMEM, idx), (VMEM, grad), (FAR, act), (FAR, act_other)],
        [(VMEM, struct((chips, 2, rows, outs), bf16))] * 2,
        [
            pltpu.VMEM((spots, depth), bf16),
            pltpu.VMEM((spots + 2 * side, 3 * wide), bf16),
            pltpu.SemaphoreType.DMA((4,)),
        ],
        vmem=20,
    )


def weight_one_body(side, idx_ref, mine_ref, theirs_ref, x_ref, keep_ref, give_ref, gp_ref, taps_ref):
    zh = idx_ref[2]
    half, outs = mine_ref.shape
    gp_ref[at(zh * half, half, side), :] = mine_ref[...]
    gp_ref[at((1 - zh) * half, half, side), :] = theirs_ref[...]
    grad = gp_ref[...]
    bias = jnp.sum(grad.astype(f32), axis=0, keepdims=True)
    spread_taps(side, grad, taps_ref)
    blocks = 2 * keep_ref.shape[0]
    spots, depth = x_ref.shape
    size = depth // blocks
    right = tap_block(side, taps_ref, 0, spots)
    for begin in range(0, depth, 256):
        part = dot(x_ref[:, begin : begin + 256], right, TN)
        for tap in range(9):
            put_blocks(
                idx_ref, keep_ref, give_ref, part[:, tap * outs : (tap + 1) * outs],
                tap, begin // size, size,
            )
    row = jnp.broadcast_to(bias, (16, outs)).astype(bf16)
    for j in range(keep_ref.shape[0]):
        keep_ref[j, 9 * size :, :] = row
        give_ref[j, 9 * size :, :] = row


def weight_one_grad(side, idx, mine, theirs, act_zero, chips):
    spots, depth = act_zero.shape
    outs = mine.shape[1]
    rows = 9 * depth // (2 * chips) + 16
    return call(
        functools.partial(weight_one_body, side),
        "weight_one_grad",
        [(SMEM, idx), (VMEM, mine), (VMEM, theirs), (VMEM, act_zero)],
        [(VMEM, struct((chips, rows, outs), bf16))] * 2,
        [
            pltpu.VMEM((spots, outs), bf16),
            pltpu.VMEM((spots + 2 * side, 3 * outs), bf16),
        ],
        vmem=24,
    )


def pair_body(keep_ref, recv_ref, *outs):
    for j, out in enumerate(outs):
        out[...] = (keep_ref[j].astype(f32) + recv_ref[j].astype(f32)).astype(bf16)


def pair_sum(keep, recv):
    return call(
        pair_body,
        "pair_sum",
        [(VMEM, keep), (VMEM, recv)],
        [(VMEM, struct(keep.shape[1:], bf16))] * keep.shape[0],
    )


def chip_body(idx_ref, *refs):
    parts, (keep_ref, give_ref) = refs[:-2], refs[-2:]
    zh = idx_ref[2]
    for target, slot in ((keep_ref, zh), (give_ref, 1 - zh)):
        total = parts[0][slot].astype(f32)
        for part in parts[1:]:
            total = total + part[slot].astype(f32)
        target[...] = total.astype(target.dtype)


def chip_sum(idx, parts):
    shape = parts[0].shape[1:]
    return call(
        chip_body,
        "chip_sum",
        [(SMEM, idx)] + [(VMEM, p) for p in parts],
        [(VMEM, struct(shape, f32)), (VMEM, struct(shape, bf16))],
    )


def final_body(groups, idx_ref, own_ref, sib_ref, *outs):
    chip, core = idx_ref[0], idx_ref[1]
    size = (own_ref.shape[-2] - 16) // 9
    for g in range(groups):
        grad_ref, bias_ref = outs[2 * g : 2 * g + 2]
        bias_ref[...] = own_ref[0, g, 9 * size : 9 * size + 1, :].astype(f32)
        for j in range(own_ref.shape[0]):
            for source, owner in ((own_ref, core), (sib_ref, 1 - core)):
                spot = at((2 * (chip ^ j) + owner) * size, size, size)
                for tap in range(9):
                    grad_ref[tap, spot, :] = source[j, g, tap * size : (tap + 1) * size, :].astype(f32)


def final_grads(idx, own, sib):
    chips, groups, rows, outs = own.shape
    depth = 2 * chips * ((rows - 16) // 9)
    return call(
        functools.partial(final_body, groups),
        "final_grads",
        [(SMEM, idx), (VMEM, own), (VMEM, sib)],
        [(VMEM, struct((9, depth, outs), f32)), (VMEM, struct((1, outs), f32))] * groups,
    )


def outer_body(gain, x_ref, go_ref, out_ref):
    out_ref[...] = (gain * dot(x_ref[...], go_ref[...], TN)).astype(bf16)


def outer(x, go, gain):
    spots, depth = x.shape
    outs = go.shape[1]
    return call(
        functools.partial(outer_body, gain),
        "outer",
        [
            (pl.BlockSpec((spots, 256), lambda k: (0, k)), x),
            (pl.BlockSpec((spots, outs), lambda k: (0, 0)), go),
        ],
        [(pl.BlockSpec((256, outs), lambda k: (k, 0)), struct((depth, outs), bf16))],
        grid=(depth // 256,),
    )


def start_body(idx_ref, valid_ref, cot_ref, outk_ref, go_ref, bias_ref, own_ref, give_ref):
    zl = idx_ref[3]
    masked = cot_ref[...].astype(f32) * valid_ref[0]
    go_ref[...] = masked.astype(bf16)
    bias_ref[...] = jnp.sum(masked, axis=0, keepdims=True).astype(bf16)
    chans = outk_ref.shape[0] // 4
    block = cot_ref.shape[0] // 4
    for target, along in ((give_ref, 1 - zl), (own_ref, zl)):
        weights = jnp.concatenate(
            [outk_ref[at((2 * up + along) * chans, chans, chans), :] for up in range(2)], axis=0
        )
        for begin in range(0, cot_ref.shape[0], block):
            part = post_gain * dot(go_ref[begin : begin + block, :], weights, NT)
            target[begin : begin + block, :] = part.astype(target.dtype)


def start_back(idx, valid, cot, outk):
    spots, outs = cot.shape
    half = outk.shape[0] // 2
    return call(
        start_body,
        "start_back",
        [(SMEM, idx), (SMEM, valid), (VMEM, cot), (VMEM, outk)],
        [
            (VMEM, struct(cot.shape, bf16)),
            (VMEM, struct((1, outs), bf16)),
            (VMEM, struct((spots, half), f32)),
            (VMEM, struct((spots, half), bf16)),
        ],
    )


def identity_body(idx_ref, go_ref, idk_ref, own_ref, give_ref):
    zl = idx_ref[3]
    chans = idk_ref.shape[0] // 4
    block = go_ref.shape[0] // 4
    for target, along in ((give_ref, 1 - zl), (own_ref, zl)):
        for up in range(2):
            weights = idk_ref[at((2 * up + along) * chans, chans, chans), :]
            for begin in range(0, go_ref.shape[0], block):
                part = dot(go_ref[begin : begin + block, :], weights, NT)
                target[up, begin : begin + block, :] = part.astype(target.dtype)


def identity_back(idx, go, idk):
    spots, outs = go.shape
    chans = idk.shape[0] // 4
    return call(
        identity_body,
        "identity_back",
        [(SMEM, idx), (VMEM, go), (VMEM, idk)],
        [(VMEM, struct((2, spots, chans), f32)), (VMEM, struct((2, spots, chans), bf16))],
    )


def rows_body(side, idx_ref, own_ref, recv_ref, keep_ref, give_ref):
    zh = idx_ref[2]
    spots = keep_ref.shape[0]
    apart = own_ref.shape[0] - spots
    for target, begin in ((give_ref, (1 - zh) * apart), (keep_ref, zh * apart)):
        spot = at(begin, spots, side)
        total = own_ref[spot, :] + recv_ref[spot, :].astype(f32)
        target[...] = total.astype(target.dtype)


def rows_sum(side, idx, own, recv, spots):
    shape = (spots, own.shape[1])
    return call(
        functools.partial(rows_body, side),
        "rows_sum",
        [(SMEM, idx), (VMEM, own), (VMEM, recv)],
        [(VMEM, struct(shape, f32)), (VMEM, struct(shape, bf16))],
    )


def slots_body(idx_ref, own_ref, recv_ref, keep_ref, give_ref):
    zh = idx_ref[2]
    for target, slot in ((give_ref, 1 - zh), (keep_ref, zh)):
        total = own_ref[slot] + recv_ref[slot].astype(f32)
        target[...] = total.astype(target.dtype)


def slots_sum(idx, own, recv):
    shape = own.shape[1:]
    return call(
        slots_body,
        "slots_sum",
        [(SMEM, idx), (VMEM, own), (VMEM, recv)],
        [(VMEM, struct(shape, f32)), (VMEM, struct(shape, bf16))],
    )


def input_body(idx_ref, x_ref, keep_ref, recv_ref, id_ref, id_recv_ref, out_ref):
    zh = idx_ref[2]
    half = keep_ref.shape[0]
    for part in range(2):
        rows = slice(part * half, (part + 1) * half)
        conv = jnp.where(zh == part, keep_ref[...], recv_ref[...].astype(f32))
        straight = id_ref[rows, :] + id_recv_ref[rows, :].astype(f32)
        total = conv * gelu_slope(x_ref[rows, :].astype(f32)) + straight
        out_ref[rows, :] = total.astype(bf16)


def input_grad(idx, x, keep, recv, id_keep, id_recv):
    return call(
        input_body,
        "input_grad",
        [(SMEM, idx)] + [(VMEM, a) for a in (x, keep, recv, id_keep, id_recv)],
        [(VMEM, struct(x.shape, bf16))],
    )


def whole_body(side, idx_ref, xl, xa, xh, xd, rh, rl, x_ref, act_ref, sems):
    zh, zl = idx_ref[2], idx_ref[3]
    chans = xl.shape[1]
    spots = xa.shape[0]
    rest = xl.shape[0] - spots
    window, outside = at(zh * rest, spots, side), at((1 - zh) * spots, rest, side)

    def cols(up, along):
        return at((2 * up + along) * chans, chans, chans)

    run_copies(
        [
            (xl, x_ref.at[:, cols(zh, zl)]),
            (xa, x_ref.at[window, cols(zh, 1 - zl)]),
            (xh, x_ref.at[window, cols(1 - zh, zl)]),
            (xd, x_ref.at[window, cols(1 - zh, 1 - zl)]),
            (rl.at[0], x_ref.at[outside, cols(zh, 1 - zl)]),
            (rh, x_ref.at[outside, cols(1 - zh, zl)]),
            (rl.at[1], x_ref.at[outside, cols(1 - zh, 1 - zl)]),
        ],
        sems,
    )
    block = x_ref.shape[0] // 8
    for begin in range(0, x_ref.shape[0], block):
        rows = slice(begin, begin + block)
        act_ref[rows, :] = gelu(x_ref[rows, :].astype(f32)).astype(bf16)


def whole_input(side, idx, *parts):
    spots, chans = parts[0].shape
    return call(
        functools.partial(whole_body, side),
        "whole_input",
        [(SMEM, idx)] + [(FAR, p) for p in parts],
        [(VMEM, struct((spots, 4 * chans), bf16))] * 2,
        [pltpu.SemaphoreType.DMA((7,))],
    )


def join_body(idx_ref, own, recv, far_own, far_recv, out, sems):
    zh, zl = idx_ref[2], idx_ref[3]
    half = own.shape[0]
    chans = own.shape[1] // 2
    pairs = []
    for source, up, along in ((own, zh, zl), (recv, zh, 1 - zl), (far_own, 1 - zh, zl), (far_recv, 1 - zh, 1 - zl)):
        for slot in range(2):
            spot = at((2 * slot + along) * chans, chans, chans)
            target = out.at[at(up * half, half, half), spot]
            pairs.append((source.at[:, slot * chans : (slot + 1) * chans], target))
    run_copies(pairs, sems)


def join(idx, *parts):
    half, wide = parts[0].shape
    return call(
        join_body,
        "join",
        [(SMEM, idx)] + [(FAR, p) for p in parts],
        [(VMEM, struct((2 * half, 2 * wide), bf16))],
        [pltpu.SemaphoreType.DMA((8,))],
    )


def finish_body(valid_ref, x_ref, act_ref, idk_ref, outk_ref, ib_ref, out_ref):
    identity = dot(x_ref[...], idk_ref[...]) + ib_ref[...]
    branch = dot(act_ref[...], outk_ref[...])
    out_ref[...] = ((identity + post_gain * branch) * valid_ref[0]).astype(bf16)


def finish(valid, x, act, idk, outk, ib):
    spots, depth = x.shape
    outs = idk.shape[1]
    block = spots // 4
    by_row = lambda wide: pl.BlockSpec((block, wide), lambda k: (k, 0))
    full = lambda a: pl.BlockSpec(a.shape, lambda k: (0, 0))
    ib = ib.reshape(1, outs)
    return call(
        finish_body,
        "finish",
        [(SMEM, valid), (by_row(depth), x), (by_row(act.shape[1]), act)]
        + [(full(a), a) for a in (idk, outk, ib)],
        [(by_row(outs), struct((spots, outs), bf16))],
        grid=(4,),
    )


def flip(value, axis):
    return lax.ppermute(value, axis, [(0, 1), (1, 0)])


def hop(value, j, chips):
    return lax.ppermute(value, "chip", [(i, i ^ j) for i in range(chips)])


def gather_chips(value, chips):
    return [value] + [hop(value, j, chips) for j in range(1, chips)]


def swap(pieces, axis):
    return lax.all_to_all(pieces, axis, split_axis=0, concat_axis=0, tiled=True)


def after(value, other):
    return lax.optimization_barrier((value, other))[0]


def rows_of(value, start, size):
    return lax.dynamic_slice_in_dim(value, start, size, 0)


def local(
    pixels,
    counts,
    kernel_one,
    bias_one,
    kernel_two,
    bias_two,
    kernel_three,
    bias_three,
    out_kernel,
    identity_kernel,
    identity_bias,
    cotangent,
):
    images, rows, width, chans = pixels.shape
    side = width // 2
    spots = side * side
    half = spots // 2
    window = half + halo * side
    outs = cotangent.shape[3]
    chips = lax.axis_size("chip")
    chip, core, zh, zl = [lax.axis_index(a) for a in ("chip", "core", "zh", "zl")]
    idx = jnp.stack([chip, core, zh, zl]).astype(jnp.int32)
    taps = lambda kernel: kernel.reshape((9,) + kernel.shape[2:])
    one, two, three = taps(kernel_one), taps(kernel_two), taps(kernel_three)

    own_count = lax.dynamic_index_in_dim(counts, 2 * chip + core, 0, keepdims=True)
    valid = (own_count > 0).astype(f32)

    def block_of(kernel):
        size = kernel.shape[1] // (2 * chips)
        return lax.dynamic_slice_in_dim(kernel, (2 * chip + core) * size, size, 1)

    def other_half(*kernels):
        return jnp.stack([block_of(kernel) for kernel in kernels])

    def around(piece):
        own = jnp.stack(gather_chips(piece, chips))
        return own, flip(own, "core")

    bias_other = flip(jnp.stack([bias_one, bias_two, bias_three]), "zh")
    first_piece = flip(other_half(one), "zh")
    pooled = pool(pixels)
    xl = swap(pooled, DP).reshape(spots, chans)
    begin = zh * (spots - window)
    begin_other = (1 - zh) * (spots - window)
    xa = flip(rows_of(xl, begin, window), "zl")
    xh = flip(rows_of(xl, begin_other, window), "zh")
    both_piece = flip(after(other_half(two, three), first_piece), "zh")
    one_other = around(after(first_piece, (xa, bias_other)))
    xd = flip(xh, "zl")
    both_other = around(after(both_piece, xh))

    go, identity_bias_grad, ga_own, ga_give = start_back(
        idx, valid, after(cotangent.reshape(spots, outs), xl), out_kernel
    )
    pre_one, act_one = conv(side, idx, (xl, xa, xh, xd), one, one_other, 0, bias_one, bias_other[0], True)
    act_one_other = flip(act_one, "zl")
    pre_two, act_two = conv(side, idx, (act_one, act_one_other), two, both_other, 0, bias_two, bias_other[1])
    act_two_other = flip(act_two, "zl")

    rest = spots - window
    rest_own = rows_of(xl, (1 - zh) * window, rest)
    rest_high = flip(after(rows_of(xl, zh * window, rest), act_one), "zh")
    rest_low = flip(jnp.stack([rest_own, rest_high]), "zl")
    full_x, act_zero = whole_input(side, idx, xl, xa, xh, xd, rest_high, rest_low)

    identity_kernel_grad = outer(full_x, go, 1.0)

    ga_keep, ga_give = rows_sum(side, idx, ga_own, flip(ga_give, "zl"), window)
    ga_recv = flip(after(ga_give, act_one), "zh")
    pre_three, act_three = conv(
        side, idx, (after(act_two, full_x), act_two_other), three, both_other, 1, bias_three, bias_other[2]
    )

    own_rows = rows_of(act_three, zh * halo * side, half)

    gp_three, ga_own, ga_give = back(
        side, idx, (ga_keep, ga_recv, pre_three), three, both_other, 1
    )
    ga_recv = flip(ga_give, "zl")
    gp_two, ga_own, ga_give = back(
        side, idx, (after(ga_own, identity_kernel_grad), ga_recv, pre_two), two, both_other, 0
    )
    ga_recv = flip(ga_give, "zl")
    gp_mine, gp_theirs, gp_one = slope_back(side, idx, ga_own, ga_recv, pre_one, half)
    gp_theirs = flip(gp_theirs, "zh")
    gx_own, gx_give = back(side, idx, (gp_one,), one, one_other, 0, half)

    near_rows = flip(own_rows, "zl")
    far_rows = flip(after(own_rows, gp_three), "zh")
    far_near_rows = flip(after(near_rows, gp_two), "zh")
    full_three = join(idx, own_rows, near_rows, far_rows, far_near_rows)
    block_out = finish(valid, full_x, full_three, identity_kernel, out_kernel, identity_bias)

    id_own, id_give = identity_back(idx, go, identity_kernel)
    id_keep, id_give = slots_sum(idx, id_own, flip(after(id_give, xd), "zl"))
    id_recv = flip(after(id_give, act_two), "zh")

    gx_keep, gx_give = slots_sum(idx, gx_own, flip(gx_give, "zl"))
    gx = input_grad(idx, xl, gx_keep, flip(gx_give, "zh"), id_keep, id_recv)
    gx = swap(gx.reshape(images, rows * width // 4, chans), DP)
    pixels_grad = widen(gx, rows, width)

    identity_kernel_grad = lax.psum(identity_kernel_grad, DP)
    out_kernel_grad = outer(full_three, go, post_gain)
    bias_rows = jnp.broadcast_to(identity_bias_grad, (16, outs))
    out_kernel_grad = jnp.concatenate([out_kernel_grad, bias_rows])
    out_kernel_grad = lax.psum(after(out_kernel_grad, identity_kernel_grad), DP)
    identity_bias_grad = out_kernel_grad[-1:]
    out_kernel_grad = out_kernel_grad[:-16]

    def both_slices(grad, act, act_other):
        keep, give = weight_grad(side, half, idx, grad, act, act_other, chips)
        parts = pair_sum(keep, flip(give, "core"))
        keep, give = chip_sum(idx, [parts[0]] + [hop(parts[j], j, chips) for j in range(1, chips)])
        total = (keep + flip(give, "zh").astype(f32)).astype(bf16)
        total = jnp.stack(gather_chips(total[None], chips))
        return final_grads(idx, total, flip(total, "core"))

    kernel_three_grad, bias_three_grad = both_slices(gp_three, act_two, act_two_other)
    kernel_two_grad, bias_two_grad = both_slices(gp_two, act_one, act_one_other)

    keep_one, give_one = weight_one_grad(side, idx, gp_mine, gp_theirs, act_zero, chips)
    parts = pair_sum(keep_one, flip(give_one, "core"))
    total = parts[0].astype(f32)
    for j in range(1, chips):
        total = total + hop(parts[j], j, chips).astype(f32)
    total = jnp.stack(gather_chips(total.astype(bf16)[None], chips))
    kernel_one_grad, bias_one_grad = final_grads(idx, total, flip(total, "core"))

    return (
        block_out.reshape(cotangent.shape),
        pixels_grad,
        kernel_one_grad.reshape(kernel_one.shape),
        bias_one_grad[0],
        kernel_two_grad.reshape(kernel_two.shape),
        bias_two_grad[0],
        kernel_three_grad.reshape(kernel_three.shape),
        bias_three_grad[0],
        out_kernel_grad.astype(f32),
        identity_kernel_grad.astype(f32),
        identity_bias_grad.astype(f32)[0],
    )


def solution(mesh):
    members = mesh.devices.size // mesh.shape["mp"]
    fine = Mesh(
        mesh.devices.reshape(members // 2, 2, 2, mesh.shape["mp"] // 2),
        ("chip", "core", "zh", "zl"),
    )
    return jax.shard_map(
        local,
        mesh=fine,
        in_specs=(
            P(None, DP, None, MP),
            P(),
            P(None, None, None, MP),
            P(MP),
            P(None, None, None, MP),
            P(MP),
            P(None, None, None, MP),
            P(MP),
            P(None, MP),
            P(None, MP),
            P(MP),
            P(DP, None, None, MP),
        ),
        out_specs=(
            P(DP, None, None, MP),
            P(None, DP, None, MP),
            P(None, None, None, MP),
            P(MP),
            P(None, None, None, MP),
            P(MP),
            P(None, None, None, MP),
            P(MP),
            P(None, MP),
            P(None, MP),
            P(MP),
        ),
        check_vma=False,
    )
```

```python
import functools
import math

import jax
import jax.numpy as jnp
from jax import lax
from jax.experimental import pallas as pl
from jax.experimental.pallas import tpu as pltpu
from jax.sharding import Mesh
from jax.sharding import PartitionSpec as P


post_gain = 0.015625
slope = 0.7978845608028654
cubic = 0.044715
halo = 6
bf16 = jnp.bfloat16
f32 = jnp.float32
NT = (((1,), (1,)), ((), ()))
TN = (((0,), (0,)), ((), ()))
NN = (((1,), (0,)), ((), ()))
DP = ("chip", "core")
MP = ("zh", "zl")


def dot(left, right, dims=NN):
    return lax.dot_general(left, right, dims, preferred_element_type=f32)


def gelu(value):
    inner = jnp.tanh(slope * (value + cubic * value * value * value))
    return 0.5 * value * (1.0 + inner)


def gelu_slope(value):
    square = value * value
    inner = jnp.tanh(slope * value * (1.0 + cubic * square))
    climb = slope * (1.0 + 3.0 * cubic * square)
    return 0.5 * (1.0 + inner) + 0.5 * value * (1.0 - inner * inner) * climb


def struct(shape, kind):
    return jax.ShapeDtypeStruct(shape, kind)


def lanes(blocks):
    return blocks[0] if len(blocks) == 1 else jnp.concatenate(blocks, axis=1)


VMEM = pl.BlockSpec(memory_space=pltpu.VMEM)
SMEM = pl.BlockSpec(memory_space=pltpu.SMEM)
FAR = pl.BlockSpec(memory_space=pl.ANY)
HBM = pl.BlockSpec(memory_space=pltpu.HBM)
LOAD = "load"
STORE = "store"


def size_of(array):
    return math.prod(array.shape) * jnp.dtype(array.dtype).itemsize


def call(body, name, ins, outs, scratch=(), spare=6, **more):
    loads = [i for i, (space, _) in enumerate(ins) if space is LOAD]
    stores = [i for i, (space, _) in enumerate(outs) if space is STORE]
    spaces = [FAR if space is LOAD else space for space, _ in ins]
    arrays = [array for _, array in ins]
    out_specs = [HBM if space is STORE else space for space, _ in outs]
    out_shape = [shape for _, shape in outs]
    held = [arrays[i] for i in loads] + [out_shape[i] for i in stores]
    buffers = [pltpu.VMEM(array.shape, array.dtype) for array in held]
    count = len(held)
    sems = [pltpu.SemaphoreType.DMA((count,))] if count else []
    vmem = sum(size_of(array) for array in held)
    vmem += sum(size_of(a) for space, a in list(ins) + list(outs) if space is VMEM)
    vmem += sum(size_of(b) for b in scratch if b.memory_space == pltpu.VMEM)

    def wrapped(*refs):
        inputs = list(refs[: len(ins)])
        outputs = list(refs[len(ins) : len(ins) + len(outs)])
        rest = refs[len(ins) + len(outs) :]
        kept = rest[:count]
        tail = rest[count:]
        copies = []
        if count:
            sem, tail = tail[0], tail[1:]
            copies = [
                pltpu.make_async_copy(inputs[i], kept[n], sem.at[n]) for n, i in enumerate(loads)
            ]
        for copy in copies:
            copy.start()
        for n, i in enumerate(loads):
            inputs[i] = kept[n]
        targets = {}
        for n, i in enumerate(stores):
            targets[len(loads) + n] = outputs[i]
            outputs[i] = kept[len(loads) + n]

        def arrive():
            for copy in copies:
                copy.wait()

        body(arrive, *inputs, *outputs, *tail)
        copies_out = [pltpu.make_async_copy(kept[n], target, sem.at[n]) for n, target in targets.items()]
        for copy in copies_out:
            copy.start()
        for copy in copies_out:
            copy.wait()

    single = len(outs) == 1
    return pl.pallas_call(
        wrapped,
        in_specs=spaces,
        out_specs=out_specs[0] if single else out_specs,
        out_shape=out_shape[0] if single else out_shape,
        scratch_shapes=buffers + sems + list(scratch),
        compiler_params=pltpu.CompilerParams(vmem_limit_bytes=vmem + (spare << 20)),
        cost_estimate=pl.CostEstimate(flops=0, bytes_accessed=0, transcendentals=0),
        name=name,
        **more,
    )(*arrays)


def run_copies(pairs, sems):
    copies = [pltpu.make_async_copy(a, b, sems.at[i]) for i, (a, b) in enumerate(pairs)]
    for copy in copies:
        copy.start()
    for copy in copies:
        copy.wait()


def slice_copies(group, idx_ref, own, blocks, sibling, wbuf):
    chip, core, zh = idx_ref[0], idx_ref[1], idx_ref[2]
    size = blocks.shape[-2]
    pairs = [(own, wbuf.at[zh])]
    for j in range(blocks.shape[0]):
        for source, owner in ((blocks, core), (sibling, 1 - core)):
            spot = at((2 * (chip ^ j) + owner) * size, size, size)
            pairs.append((source.at[j, group], wbuf.at[1 - zh, :, spot, :]))
    return pairs


def at(start, size, unit):
    return pl.ds(pl.multiple_of(start, unit), size)


def pool_body(arrive, x_ref, out_ref):
    arrive()
    rows, width, chans = x_ref.shape[1:]
    half = width // 2
    pixel = lax.broadcasted_iota(jnp.int32, (half, 2 * width), 1)
    place = lax.broadcasted_iota(jnp.int32, (half, 2 * width), 0)
    inside = (lax.rem(pixel, width) >= 2 * place) & (lax.rem(pixel, width) < 2 * place + 2)
    pick = jnp.where(inside, 0.25, 0.0).astype(bf16)
    for image in range(x_ref.shape[0]):
        for row in range(rows // 2):
            window = x_ref[image, 2 * row : 2 * row + 2].reshape(2 * width, chans)
            out_ref[image, row * half : (row + 1) * half, :] = dot(pick, window).astype(bf16)


def pool(pixels):
    images, rows, width, chans = pixels.shape
    shape = struct((images, rows * width // 4, chans), bf16)
    return call(pool_body, "pool", [(LOAD, pixels)], [(VMEM, shape)])


def widen_body(arrive, g_ref, out_ref):
    arrive()
    rows, width, chans = out_ref.shape[1:]
    half = width // 2
    pixel = lax.broadcasted_iota(jnp.int32, (width, half), 0)
    place = lax.broadcasted_iota(jnp.int32, (width, half), 1)
    inside = (pixel >= 2 * place) & (pixel < 2 * place + 2)
    pick = jnp.where(inside, 0.25, 0.0).astype(bf16)
    for image in range(g_ref.shape[0]):
        for row in range(rows // 2):
            wide = dot(pick, g_ref[image, row * half : (row + 1) * half, :]).astype(bf16)
            out_ref[image, 2 * row] = wide
            out_ref[image, 2 * row + 1] = wide


def widen(grad, rows, width):
    images, spots, chans = grad.shape
    step = images // 4
    block = pl.BlockSpec((step, spots, chans), lambda i: (i, 0, 0))
    out = pl.BlockSpec((step, rows, width, chans), lambda i: (i, 0, 0, 0))
    return call(
        widen_body,
        "widen",
        [(block, grad)],
        [(out, struct((images, rows, width, chans), bf16))],
        grid=(4,),
    )


def conv_body(side, first, group, arrive, idx_ref, *refs):
    zh, zl = idx_ref[2], idx_ref[3]
    if first:
        xl, xa, xh, xd, wl, wo, ws, bl, bo, pre_ref, act_ref, xbuf, wbuf, acc, sems = refs
        chans = xl.shape[1]
        spots = xbuf.shape[0]
        begin = zh * (xl.shape[0] - spots)
        pairs = []
        for source, up, along in ((xl, zh, zl), (xa, zh, 1 - zl), (xh, 1 - zh, zl), (xd, 1 - zh, 1 - zl)):
            if source is xl:
                source = xl.at[at(begin, spots, side), :]
            pairs.append((source, xbuf.at[:, at((2 * up + along) * chans, chans, chans)]))
    else:
        xl, xa, wl, wo, ws, bl, bo, pre_ref, act_ref, xbuf, wbuf, acc, sems = refs
        chans = xl.shape[1] // 2
        spots = xbuf.shape[0]
        pairs = []
        for source, along in ((xl, zl), (xa, 1 - zl)):
            for up in range(2):
                pairs.append(
                    (
                        source.at[:, up * chans : (up + 1) * chans],
                        xbuf.at[:, at((2 * up + along) * chans, chans, chans)],
                    )
                )
    run_copies(slice_copies(group, idx_ref, wl, wo, ws, wbuf) + pairs, sems)
    arrive()
    acc[...] = jnp.zeros_like(acc)
    outs = 2 * wl.shape[2]
    block = spots // 2
    for x in range(3):
        weights = lanes([wbuf[u, 3 * y + x] for y in range(3) for u in range(2)])
        for begin in range(0, spots, block):
            values = xbuf[begin : begin + block, :]
            if first:
                values = gelu(values.astype(f32)).astype(bf16)
            product = dot(values, weights)
            for y in range(3):
                place = begin + side * (2 - y)
                acc[x, place : place + block, :] += product[:, y * outs : (y + 1) * outs]
    spot = lax.broadcasted_iota(jnp.int32, (block, outs), 0)
    column = lax.rem(spot, side)
    own, other = bl[...], bo[...]
    bias = lanes([jnp.where(zh == 0, own, other), jnp.where(zh == 0, other, own)])
    for begin in range(0, spots, block):
        place = begin + side
        left = pltpu.roll(acc[0, place : place + block, :], 1, 0)
        right = pltpu.roll(acc[2, place : place + block, :], block - 1, 0)
        pre = acc[1, place : place + block, :] + bias
        pre = pre + jnp.where(column > 0, left, 0.0)
        pre = pre + jnp.where(column < side - 1, right, 0.0)
        pre_ref[begin : begin + block, :] = pre
        act_ref[begin : begin + block, :] = gelu(pre).astype(bf16)


def conv(side, idx, sources, own, other, group, bias, bias_other, first=False):
    taps, depth, outs = own.shape
    spots = sources[1].shape[0]
    return call(
        functools.partial(conv_body, side, first, group),
        "conv",
        [(SMEM, idx)]
        + [(FAR, s) for s in sources]
        + [(HBM, own), (FAR, other[0]), (FAR, other[1])]
        + [(VMEM, bias.reshape(1, outs)), (VMEM, bias_other.reshape(1, outs))],
        [(STORE, struct((spots, 2 * outs), f32)), (VMEM, struct((spots, 2 * outs), bf16))],
        [
            pltpu.VMEM((spots, depth), bf16),
            pltpu.VMEM((2, taps, depth, outs), bf16),
            pltpu.VMEM((3, spots + 2 * side, 2 * outs), f32),
            pltpu.SemaphoreType.DMA((2 * other[0].shape[0] + 5,)),
        ],
        spare=14 if first else 8,
    )


def spread_taps(side, grad, taps_ref):
    pixels, outs = grad.shape
    spot = lax.broadcasted_iota(jnp.int32, (pixels, outs), 0)
    column = lax.rem(spot, side)
    wide = grad.astype(f32)
    ahead = jnp.where(column < side - 1, pltpu.roll(wide, pixels - 1, 0), 0.0).astype(bf16)
    behind = jnp.where(column > 0, pltpu.roll(wide, 1, 0), 0.0).astype(bf16)
    edge = jnp.zeros((side, 3 * outs), bf16)
    taps_ref[:side, :] = edge
    taps_ref[side + pixels :, :] = edge
    taps_ref[side : side + pixels, :] = jnp.concatenate([ahead, grad, behind], axis=1)


def tap_block(side, taps_ref, begin, block):
    return lanes([taps_ref[at(begin + side * (2 - y), block, side), :] for y in range(3)])


def slope_body(side, arrive, idx_ref, keep_ref, recv_ref, pre_ref, mine_ref, theirs_ref, gp_ref):
    arrive()
    zh = idx_ref[2]
    half, outs = mine_ref.shape
    total = keep_ref[...] + recv_ref[...].astype(f32)
    gp_ref[...] = (total * gelu_slope(pre_ref[...])).astype(bf16)
    own = gp_ref[at(zh * halo * side, half, side), :]
    low, high = own[:, :outs], own[:, outs:]
    mine_ref[...] = jnp.where(zh == 0, low, high)
    theirs_ref[...] = jnp.where(zh == 0, high, low)


def slope_back(side, idx, keep, recv, pre, half):
    outs = pre.shape[1] // 2
    return call(
        functools.partial(slope_body, side),
        "slope_back",
        [(SMEM, idx), (LOAD, keep), (LOAD, recv), (LOAD, pre)],
        [
            (VMEM, struct((half, outs), bf16)),
            (VMEM, struct((half, outs), bf16)),
            (VMEM, struct(pre.shape, bf16)),
        ],
    )


def back_body(side, last, group, arrive, idx_ref, *refs):
    zh, zl = idx_ref[2], idx_ref[3]
    if last:
        grad_ref, wl, wo, ws, own_ref, give_ref, taps_ref, wbuf, sems = refs
    else:
        keep_ref, recv_ref, pre_ref, wl, wo, ws, gp_ref, own_ref, give_ref, taps_ref, wbuf, sems = refs
    pairs = slice_copies(group, idx_ref, wl, wo, ws, wbuf)
    copies = [pltpu.make_async_copy(a, b, sems.at[i]) for i, (a, b) in enumerate(pairs)]
    for copy in copies:
        copy.start()
    arrive()
    if last:
        grad = grad_ref[...]
    else:
        total = keep_ref[...] + recv_ref[...].astype(f32)
        grad = (total * gelu_slope(pre_ref[...])).astype(bf16)
        gp_ref[...] = grad
    spread_taps(side, grad, taps_ref)
    depth, outs = wl.shape[1:]
    pixels = own_ref.shape[-2]
    start = zh * halo * side
    for copy in copies:
        copy.wait()
    block = pixels // 2
    chans = depth // 4

    def rows(index):
        spot = at(index * chans, chans, chans)
        return lanes([wbuf[u, t, spot, :] for t in range(9) for u in range(2)])

    for target, along in ((give_ref, 1 - zl), (own_ref, zl)):
        if last:
            for up in range(2):
                weights = rows(2 * up + along)
                for begin in range(0, pixels, block):
                    part = dot(tap_block(side, taps_ref, start + begin, block), weights, NT)
                    target[up, begin : begin + block, :] = part.astype(target.dtype)
        else:
            weights = jnp.concatenate([rows(along), rows(2 + along)], axis=0)
            for begin in range(0, pixels, block):
                part = dot(tap_block(side, taps_ref, begin, block), weights, NT)
                target[begin : begin + block, :] = part.astype(target.dtype)


def back(side, idx, sources, own, other, group, half=0):
    taps, depth, outs = own.shape
    spots = sources[-1].shape[0]
    if half:
        shape = (2, half, depth // 4)
        results = []
    else:
        shape = (spots, depth // 2)
        results = [(VMEM, struct((spots, 2 * outs), bf16))]
    results += [(VMEM, struct(shape, f32)), (VMEM, struct(shape, bf16))]
    return call(
        functools.partial(back_body, side, bool(half), group),
        "back",
        [(SMEM, idx)]
        + [(LOAD, source) for source in sources]
        + [(HBM, own), (FAR, other[0]), (FAR, other[1])],
        results,
        [
            pltpu.VMEM((spots + 2 * side, 6 * outs), bf16),
            pltpu.VMEM((2, taps, depth, outs), bf16),
            pltpu.SemaphoreType.DMA((2 * other[0].shape[0] + 1,)),
        ],
        spare=14 if half else 10,
    )


def put_blocks(idx_ref, keep_ref, give_ref, part, tap, first_block, size, *inner):
    chip, core = idx_ref[0], idx_ref[1]
    for b in range(0, part.shape[0] // size, 2):
        even = part[b * size : (b + 1) * size, :]
        odd = part[(b + 1) * size : (b + 2) * size, :]
        slot = chip ^ ((first_block + b) // 2)
        rows = slice(tap * size, (tap + 1) * size)
        keep_ref[(slot,) + inner + (rows, slice(None))] = jnp.where(core == 0, even, odd).astype(bf16)
        give_ref[(slot,) + inner + (rows, slice(None))] = jnp.where(core == 0, odd, even).astype(bf16)


def weight_body(side, half, arrive, idx_ref, gp_ref, xl, xa, keep_ref, give_ref, xbuf, taps_ref, sems):
    arrive()
    zh, zl = idx_ref[2], idx_ref[3]
    chans = xl.shape[1] // 2
    pairs = []
    for source, along in ((xl, zl), (xa, 1 - zl)):
        for up in range(2):
            pairs.append(
                (
                    source.at[:, up * chans : (up + 1) * chans],
                    xbuf.at[:, at((2 * up + along) * chans, chans, chans)],
                )
            )
    run_copies(pairs, sems)
    spots, wide = gp_ref.shape
    outs = wide // 2
    spot = lax.broadcasted_iota(jnp.int32, (spots, wide), 0) - zh * halo * side
    grad = jnp.where((spot >= 0) & (spot < half), gp_ref[...].astype(f32), 0.0)
    bias = jnp.sum(grad, axis=0, keepdims=True)
    spread_taps(side, grad.astype(bf16), taps_ref)
    blocks = 2 * keep_ref.shape[0]
    depth = xbuf.shape[1]
    size = depth // blocks
    for begin in range(0, depth, 256):
        values = xbuf[:, begin : begin + 256]
        for y in range(3):
            place = side * (2 - y)
            part = dot(values, taps_ref[place : place + spots, :], TN)
            for x in range(3):
                for u in range(2):
                    col = x * wide + u * outs
                    put_blocks(
                        idx_ref, keep_ref, give_ref, part[:, col : col + outs],
                        3 * y + x, begin // size, size, u,
                    )
    for u in range(2):
        row = jnp.broadcast_to(bias[:, u * outs : (u + 1) * outs], (16, outs)).astype(bf16)
        for j in range(keep_ref.shape[0]):
            keep_ref[j, u, 9 * size :, :] = row
            give_ref[j, u, 9 * size :, :] = row


def weight_grad(side, half, idx, grad, act, act_other, chips):
    spots, wide = grad.shape
    outs = wide // 2
    depth = 2 * act.shape[1]
    rows = 9 * depth // (2 * chips) + 16
    return call(
        functools.partial(weight_body, side, half),
        "weight_grad",
        [(SMEM, idx), (LOAD, grad), (FAR, act), (FAR, act_other)],
        [(VMEM, struct((chips, 2, rows, outs), bf16))] * 2,
        [
            pltpu.VMEM((spots, depth), bf16),
            pltpu.VMEM((spots + 2 * side, 3 * wide), bf16),
            pltpu.SemaphoreType.DMA((4,)),
        ],
        spare=10,
    )


def weight_one_body(side, arrive, idx_ref, mine_ref, theirs_ref, x_ref, keep_ref, give_ref, gp_ref, taps_ref):
    arrive()
    zh = idx_ref[2]
    half, outs = mine_ref.shape
    gp_ref[at(zh * half, half, side), :] = mine_ref[...]
    gp_ref[at((1 - zh) * half, half, side), :] = theirs_ref[...]
    grad = gp_ref[...]
    bias = jnp.sum(grad.astype(f32), axis=0, keepdims=True)
    spread_taps(side, grad, taps_ref)
    blocks = 2 * keep_ref.shape[0]
    spots, depth = x_ref.shape
    size = depth // blocks
    right = tap_block(side, taps_ref, 0, spots)
    for begin in range(0, depth, 256):
        part = dot(x_ref[:, begin : begin + 256], right, TN)
        for tap in range(9):
            put_blocks(
                idx_ref, keep_ref, give_ref, part[:, tap * outs : (tap + 1) * outs],
                tap, begin // size, size,
            )
    row = jnp.broadcast_to(bias, (16, outs)).astype(bf16)
    for j in range(keep_ref.shape[0]):
        keep_ref[j, 9 * size :, :] = row
        give_ref[j, 9 * size :, :] = row


def weight_one_grad(side, idx, mine, theirs, act_zero, chips):
    spots, depth = act_zero.shape
    outs = mine.shape[1]
    rows = 9 * depth // (2 * chips) + 16
    return call(
        functools.partial(weight_one_body, side),
        "weight_one_grad",
        [(SMEM, idx), (LOAD, mine), (LOAD, theirs), (LOAD, act_zero)],
        [(VMEM, struct((chips, rows, outs), bf16))] * 2,
        [
            pltpu.VMEM((spots, outs), bf16),
            pltpu.VMEM((spots + 2 * side, 3 * outs), bf16),
        ],
        spare=14,
    )


def pair_body(arrive, idx_ref, keep_ref, recv_ref, *outs):
    arrive()
    for j, out in enumerate(outs):
        out[...] = (keep_ref[j].astype(f32) + recv_ref[j].astype(f32)).astype(bf16)


def pair_sum(idx, keep, recv):
    return call(
        pair_body,
        "pair_sum",
        [(SMEM, idx), (LOAD, keep), (LOAD, recv)],
        [(VMEM, struct(keep.shape[1:], bf16))] * keep.shape[0],
    )


def chip_body(arrive, idx_ref, *refs):
    arrive()
    parts, (keep_ref, give_ref) = refs[:-2], refs[-2:]
    zh = idx_ref[2]
    for target, slot in ((keep_ref, zh), (give_ref, 1 - zh)):
        total = parts[0][slot].astype(f32)
        for part in parts[1:]:
            total = total + part[slot].astype(f32)
        target[...] = total.astype(target.dtype)


def chip_sum(idx, parts):
    shape = parts[0].shape[1:]
    return call(
        chip_body,
        "chip_sum",
        [(SMEM, idx)] + [(LOAD, p) for p in parts],
        [(STORE, struct(shape, f32)), (VMEM, struct(shape, bf16))],
    )


def final_body(groups, arrive, idx_ref, own_ref, sib_ref, *outs):
    arrive()
    chip, core = idx_ref[0], idx_ref[1]
    size = (own_ref.shape[-2] - 16) // 9
    for g in range(groups):
        grad_ref, bias_ref = outs[2 * g : 2 * g + 2]
        bias_ref[...] = own_ref[0, g, 9 * size : 9 * size + 1, :].astype(f32)
        for j in range(own_ref.shape[0]):
            for source, owner in ((own_ref, core), (sib_ref, 1 - core)):
                spot = at((2 * (chip ^ j) + owner) * size, size, size)
                for tap in range(9):
                    grad_ref[tap, spot, :] = source[j, g, tap * size : (tap + 1) * size, :].astype(f32)


def final_grads(idx, own, sib):
    chips, groups, rows, outs = own.shape
    depth = 2 * chips * ((rows - 16) // 9)
    return call(
        functools.partial(final_body, groups),
        "final_grads",
        [(SMEM, idx), (LOAD, own), (LOAD, sib)],
        [(STORE, struct((9, depth, outs), f32)), (VMEM, struct((1, outs), f32))] * groups,
    )


def outer_body(gain, arrive, idx_ref, x_ref, go_ref, out_ref):
    arrive()
    for begin in range(0, x_ref.shape[1], 256):
        part = gain * dot(x_ref[:, begin : begin + 256], go_ref[...], TN)
        out_ref[begin : begin + 256, :] = part.astype(bf16)


def outer(idx, x, go, gain):
    return call(
        functools.partial(outer_body, gain),
        "outer",
        [(SMEM, idx), (LOAD, x), (LOAD, go)],
        [(STORE, struct((x.shape[1], go.shape[1]), bf16))],
        spare=8,
    )


def start_body(arrive, idx_ref, valid_ref, cot_ref, outk_ref, go_ref, bias_ref, own_ref, give_ref):
    arrive()
    zl = idx_ref[3]
    masked = cot_ref[...].astype(f32) * valid_ref[0]
    go_ref[...] = masked.astype(bf16)
    bias_ref[...] = jnp.sum(masked, axis=0, keepdims=True).astype(bf16)
    chans = outk_ref.shape[0] // 4
    block = cot_ref.shape[0] // 4
    for target, along in ((give_ref, 1 - zl), (own_ref, zl)):
        weights = jnp.concatenate(
            [outk_ref[at((2 * up + along) * chans, chans, chans), :] for up in range(2)], axis=0
        )
        for begin in range(0, cot_ref.shape[0], block):
            part = post_gain * dot(go_ref[begin : begin + block, :], weights, NT)
            target[begin : begin + block, :] = part.astype(target.dtype)


def start_back(idx, valid, cot, outk):
    spots, outs = cot.shape
    half = outk.shape[0] // 2
    return call(
        start_body,
        "start_back",
        [(SMEM, idx), (SMEM, valid), (LOAD, cot), (LOAD, outk)],
        [
            (STORE, struct(cot.shape, bf16)),
            (STORE, struct((1, outs), bf16)),
            (STORE, struct((spots, half), f32)),
            (VMEM, struct((spots, half), bf16)),
        ],
    )


def identity_body(arrive, idx_ref, go_ref, idk_ref, own_ref, give_ref):
    arrive()
    zl = idx_ref[3]
    chans = idk_ref.shape[0] // 4
    block = go_ref.shape[0] // 4
    for target, along in ((give_ref, 1 - zl), (own_ref, zl)):
        for up in range(2):
            weights = idk_ref[at((2 * up + along) * chans, chans, chans), :]
            for begin in range(0, go_ref.shape[0], block):
                part = dot(go_ref[begin : begin + block, :], weights, NT)
                target[up, begin : begin + block, :] = part.astype(target.dtype)


def identity_back(idx, go, idk):
    spots, outs = go.shape
    chans = idk.shape[0] // 4
    return call(
        identity_body,
        "identity_back",
        [(SMEM, idx), (LOAD, go), (LOAD, idk)],
        [(STORE, struct((2, spots, chans), f32)), (VMEM, struct((2, spots, chans), bf16))],
    )


def rows_body(side, arrive, idx_ref, own_ref, recv_ref, keep_ref, give_ref):
    arrive()
    zh = idx_ref[2]
    spots = keep_ref.shape[0]
    apart = own_ref.shape[0] - spots
    for target, begin in ((give_ref, (1 - zh) * apart), (keep_ref, zh * apart)):
        spot = at(begin, spots, side)
        total = own_ref[spot, :] + recv_ref[spot, :].astype(f32)
        target[...] = total.astype(target.dtype)


def rows_sum(side, idx, own, recv, spots):
    shape = (spots, own.shape[1])
    return call(
        functools.partial(rows_body, side),
        "rows_sum",
        [(SMEM, idx), (LOAD, own), (LOAD, recv)],
        [(STORE, struct(shape, f32)), (VMEM, struct(shape, bf16))],
    )


def slots_body(arrive, idx_ref, own_ref, recv_ref, keep_ref, give_ref):
    arrive()
    zh = idx_ref[2]
    for target, slot in ((give_ref, 1 - zh), (keep_ref, zh)):
        total = own_ref[slot] + recv_ref[slot].astype(f32)
        target[...] = total.astype(target.dtype)


def slots_sum(idx, own, recv):
    shape = own.shape[1:]
    return call(
        slots_body,
        "slots_sum",
        [(SMEM, idx), (LOAD, own), (LOAD, recv)],
        [(STORE, struct(shape, f32)), (VMEM, struct(shape, bf16))],
    )


def input_body(arrive, idx_ref, x_ref, keep_ref, recv_ref, id_ref, id_recv_ref, out_ref):
    arrive()
    zh = idx_ref[2]
    half = keep_ref.shape[0]
    for part in range(2):
        rows = slice(part * half, (part + 1) * half)
        conv = jnp.where(zh == part, keep_ref[...], recv_ref[...].astype(f32))
        straight = id_ref[rows, :] + id_recv_ref[rows, :].astype(f32)
        total = conv * gelu_slope(x_ref[rows, :].astype(f32)) + straight
        out_ref[rows, :] = total.astype(bf16)


def input_grad(idx, x, keep, recv, id_keep, id_recv):
    return call(
        input_body,
        "input_grad",
        [(SMEM, idx)] + [(LOAD, a) for a in (x, keep, recv, id_keep, id_recv)],
        [(VMEM, struct(x.shape, bf16))],
    )


def whole_body(side, arrive, idx_ref, xl, xa, xh, xd, rh, rl, x_ref, act_ref, sems):
    arrive()
    zh, zl = idx_ref[2], idx_ref[3]
    chans = xl.shape[1]
    spots = xa.shape[0]
    rest = xl.shape[0] - spots
    window, outside = at(zh * rest, spots, side), at((1 - zh) * spots, rest, side)

    def cols(up, along):
        return at((2 * up + along) * chans, chans, chans)

    run_copies(
        [
            (xl, x_ref.at[:, cols(zh, zl)]),
            (xa, x_ref.at[window, cols(zh, 1 - zl)]),
            (xh, x_ref.at[window, cols(1 - zh, zl)]),
            (xd, x_ref.at[window, cols(1 - zh, 1 - zl)]),
            (rl.at[0], x_ref.at[outside, cols(zh, 1 - zl)]),
            (rh, x_ref.at[outside, cols(1 - zh, zl)]),
            (rl.at[1], x_ref.at[outside, cols(1 - zh, 1 - zl)]),
        ],
        sems,
    )
    block = x_ref.shape[0] // 8
    for begin in range(0, x_ref.shape[0], block):
        rows = slice(begin, begin + block)
        act_ref[rows, :] = gelu(x_ref[rows, :].astype(f32)).astype(bf16)


def whole_input(side, idx, *parts):
    spots, chans = parts[0].shape
    return call(
        functools.partial(whole_body, side),
        "whole_input",
        [(SMEM, idx)] + [(FAR, p) for p in parts],
        [(STORE, struct((spots, 4 * chans), bf16))] * 2,
        [pltpu.SemaphoreType.DMA((7,))],
    )


def join_body(arrive, idx_ref, own, recv, far_own, far_recv, out, sems):
    arrive()
    zh, zl = idx_ref[2], idx_ref[3]
    half = own.shape[0]
    chans = own.shape[1] // 2
    pairs = []
    for source, up, along in ((own, zh, zl), (recv, zh, 1 - zl), (far_own, 1 - zh, zl), (far_recv, 1 - zh, 1 - zl)):
        for slot in range(2):
            spot = at((2 * slot + along) * chans, chans, chans)
            target = out.at[at(up * half, half, half), spot]
            pairs.append((source.at[:, slot * chans : (slot + 1) * chans], target))
    run_copies(pairs, sems)


def join(idx, *parts):
    half, wide = parts[0].shape
    return call(
        join_body,
        "join",
        [(SMEM, idx)] + [(FAR, p) for p in parts],
        [(VMEM, struct((2 * half, 2 * wide), bf16))],
        [pltpu.SemaphoreType.DMA((8,))],
    )


def finish_body(arrive, idx_ref, valid_ref, x_ref, act_ref, idk_ref, outk_ref, ib_ref, out_ref):
    arrive()
    block = x_ref.shape[0] // 4
    for begin in range(0, x_ref.shape[0], block):
        rows = slice(begin, begin + block)
        identity = dot(x_ref[rows, :], idk_ref[...]) + ib_ref[...]
        branch = dot(act_ref[rows, :], outk_ref[...])
        out_ref[rows, :] = ((identity + post_gain * branch) * valid_ref[0]).astype(bf16)


def finish(idx, valid, x, act, idk, outk, ib):
    outs = idk.shape[1]
    return call(
        finish_body,
        "finish",
        [(SMEM, idx), (SMEM, valid), (LOAD, x), (LOAD, act), (LOAD, idk), (LOAD, outk)]
        + [(VMEM, ib.reshape(1, outs))],
        [(STORE, struct((x.shape[0], outs), bf16))],
        spare=8,
    )


def flip(value, axis):
    return lax.ppermute(value, axis, [(0, 1), (1, 0)])


def hop(value, j, chips):
    return lax.ppermute(value, "chip", [(i, i ^ j) for i in range(chips)])


def gather_chips(value, chips):
    return [value] + [hop(value, j, chips) for j in range(1, chips)]


def swap(pieces, axis):
    return lax.all_to_all(pieces, axis, split_axis=0, concat_axis=0, tiled=True)


def after(value, other):
    return lax.optimization_barrier((value, other))[0]


def rows_of(value, start, size):
    return lax.dynamic_slice_in_dim(value, start, size, 0)


def local(
    pixels,
    counts,
    kernel_one,
    bias_one,
    kernel_two,
    bias_two,
    kernel_three,
    bias_three,
    out_kernel,
    identity_kernel,
    identity_bias,
    cotangent,
):
    images, rows, width, chans = pixels.shape
    side = width // 2
    spots = side * side
    half = spots // 2
    window = half + halo * side
    outs = cotangent.shape[3]
    chips = lax.axis_size("chip")
    chip, core, zh, zl = [lax.axis_index(a) for a in ("chip", "core", "zh", "zl")]
    idx = jnp.stack([chip, core, zh, zl]).astype(jnp.int32)
    taps = lambda kernel: kernel.reshape((9,) + kernel.shape[2:])
    one, two, three = taps(kernel_one), taps(kernel_two), taps(kernel_three)

    own_count = lax.dynamic_index_in_dim(counts, 2 * chip + core, 0, keepdims=True)
    valid = (own_count > 0).astype(f32)

    def block_of(kernel):
        size = kernel.shape[1] // (2 * chips)
        return lax.dynamic_slice_in_dim(kernel, (2 * chip + core) * size, size, 1)

    def other_half(*kernels):
        return jnp.stack([block_of(kernel) for kernel in kernels])

    def around(piece):
        own = jnp.stack(gather_chips(piece, chips))
        return own, flip(own, "core")

    last = [idx]

    def turn(*others):
        return after(idx, (last[0],) + others)

    def ran(results):
        last[0] = results[-1] if isinstance(results, (list, tuple)) else results
        return results

    bias_other = flip(jnp.stack([bias_one, bias_two, bias_three]), "zh")
    first_piece = flip(other_half(one), "zh")
    pooled = ran(pool(pixels))
    go, identity_bias_grad, ga_own, ga_give = ran(
        start_back(turn(), valid, cotangent.reshape(spots, outs), out_kernel)
    )
    ga_recv = flip(ga_give, "zl")
    id_own, id_give = ran(identity_back(turn(), go, identity_kernel))
    id_recv = flip(id_give, "zl")

    xl = swap(after(pooled, (first_piece, bias_other, id_give)), DP).reshape(spots, chans)
    begin = zh * (spots - window)
    begin_other = (1 - zh) * (spots - window)
    xa = flip(rows_of(xl, begin, window), "zl")
    xh = flip(rows_of(xl, begin_other, window), "zh")
    one_other = around(first_piece)
    ga_keep, ga_give = ran(rows_sum(side, turn(xl), ga_own, ga_recv, window))
    xd = flip(after(xh, one_other[0]), "zl")
    both_piece = flip(after(other_half(two, three), first_piece), "zh")
    both_other = around(both_piece)

    pre_one, act_one = ran(
        conv(side, turn(both_other[0], xa), (xl, xa, xh, xd), one, one_other, 0, bias_one, bias_other[0], True)
    )
    act_one_other = flip(act_one, "zl")
    ga_recv = flip(after(ga_give, xh), "zh")
    rest = spots - window
    rest_own = rows_of(xl, (1 - zh) * window, rest)
    rest_high = flip(after(rows_of(xl, zh * window, rest), act_one), "zh")
    id_keep, id_give = ran(slots_sum(turn(), id_own, id_recv))
    pre_two, act_two = ran(
        conv(side, turn(), (act_one, act_one_other), two, both_other, 0, bias_two, bias_other[1])
    )
    act_two_other = flip(act_two, "zl")
    rest_low = flip(jnp.stack([rest_own, rest_high]), "zl")
    id_recv = flip(after(id_give, act_two), "zh")

    full_x, act_zero = ran(whole_input(side, turn(), xl, xa, xh, xd, rest_high, rest_low))
    identity_kernel_grad = ran(outer(turn(), full_x, go, 1.0))
    identity_kernel_grad = lax.psum(identity_kernel_grad, DP)
    pre_three, act_three = ran(
        conv(side, turn(), (act_two, act_two_other), three, both_other, 1, bias_three, bias_other[2])
    )
    own_rows = rows_of(act_three, zh * halo * side, half)
    near_rows = flip(own_rows, "zl")
    far_rows = flip(own_rows, "zh")

    gp_three, ga_own, ga_give = ran(
        back(side, turn(), (ga_keep, ga_recv, pre_three), three, both_other, 1)
    )
    ga_recv = flip(ga_give, "zl")
    keep_three, give_three = ran(weight_grad(side, half, turn(), gp_three, act_two, act_two_other, chips))
    recv_three = flip(give_three, "core")
    gp_two, ga_own, ga_give = ran(
        back(side, turn(near_rows), (ga_own, ga_recv, pre_two), two, both_other, 0)
    )
    ga_recv = flip(ga_give, "zl")
    keep_two, give_two = ran(weight_grad(side, half, turn(), gp_two, act_one, act_one_other, chips))
    recv_two = flip(give_two, "core")
    parts_three = ran(pair_sum(turn(), keep_three, recv_three))
    parts_three = [parts_three[0]] + [hop(parts_three[j], j, chips) for j in range(1, chips)]

    gp_mine, gp_theirs, gp_one = ran(slope_back(side, turn(), ga_own, ga_recv, pre_one, half))
    gp_theirs = flip(gp_theirs, "zh")
    gx_own, gx_give = ran(back(side, turn(), (gp_one,), one, one_other, 0, half))
    gx_recv = flip(gx_give, "zl")
    far_near_rows = flip(far_rows, "zl")
    parts_two = ran(pair_sum(turn(), keep_two, recv_two))
    parts_two = [parts_two[0]] + [hop(parts_two[j], j, chips) for j in range(1, chips)]

    keep_one, give_one = ran(weight_one_grad(side, turn(), gp_mine, gp_theirs, act_zero, chips))
    recv_one = flip(give_one, "core")
    keep_three, give_three = ran(chip_sum(turn(), parts_three))
    recv_three = flip(give_three, "zh")
    gx_keep, gx_give = ran(slots_sum(turn(), gx_own, gx_recv))
    gx_recv = flip(gx_give, "zh")
    parts_one = ran(pair_sum(turn(), keep_one, recv_one))
    parts_one = [parts_one[0]] + [hop(parts_one[j], j, chips) for j in range(1, chips)]

    full_three = ran(join(turn(), own_rows, near_rows, far_rows, far_near_rows))
    out_kernel_grad = ran(outer(turn(), full_three, go, post_gain))
    bias_rows = jnp.broadcast_to(identity_bias_grad, (16, outs))
    out_kernel_grad = jnp.concatenate([out_kernel_grad, bias_rows])
    out_kernel_grad = lax.psum(after(out_kernel_grad, identity_kernel_grad), DP)
    identity_bias_grad = out_kernel_grad[-1:]
    out_kernel_grad = out_kernel_grad[:-16]

    keep_two, give_two = ran(chip_sum(turn(), parts_two))
    recv_two = flip(give_two, "zh")
    gx = ran(input_grad(turn(), xl, gx_keep, gx_recv, id_keep, id_recv))
    gx = swap(gx.reshape(images, rows * width // 4, chans), DP)
    block_out = ran(finish(turn(), valid, full_x, full_three, identity_kernel, out_kernel, identity_bias))

    def spread(total):
        total = jnp.stack(gather_chips(total[None], chips))
        return total, flip(total, "core")

    all_three = spread((keep_three + recv_three.astype(f32)).astype(bf16))
    total = parts_one[0].astype(f32)
    for part in parts_one[1:]:
        total = total + part.astype(f32)
    all_one = spread(total.astype(bf16))
    all_two = spread((keep_two + recv_two.astype(f32)).astype(bf16))
    kernel_three_grad, bias_three_grad = ran(final_grads(turn(), *all_three))
    pixels_grad = widen(gx, rows, width)
    kernel_two_grad, bias_two_grad = ran(final_grads(turn(), *all_two))
    kernel_one_grad, bias_one_grad = ran(final_grads(turn(), *all_one))

    return (
        block_out.reshape(cotangent.shape),
        pixels_grad,
        kernel_one_grad.reshape(kernel_one.shape),
        bias_one_grad[0],
        kernel_two_grad.reshape(kernel_two.shape),
        bias_two_grad[0],
        kernel_three_grad.reshape(kernel_three.shape),
        bias_three_grad[0],
        out_kernel_grad.astype(f32),
        identity_kernel_grad.astype(f32),
        identity_bias_grad.astype(f32)[0],
    )


def solution(mesh):
    members = mesh.devices.size // mesh.shape["mp"]
    fine = Mesh(
        mesh.devices.reshape(members // 2, 2, 2, mesh.shape["mp"] // 2),
        ("chip", "core", "zh", "zl"),
    )
    return jax.shard_map(
        local,
        mesh=fine,
        in_specs=(
            P(None, DP, None, MP),
            P(),
            P(None, None, None, MP),
            P(MP),
            P(None, None, None, MP),
            P(MP),
            P(None, None, None, MP),
            P(MP),
            P(None, MP),
            P(None, MP),
            P(MP),
            P(DP, None, None, MP),
        ),
        out_specs=(
            P(DP, None, None, MP),
            P(None, DP, None, MP),
            P(None, None, None, MP),
            P(MP),
            P(None, None, None, MP),
            P(MP),
            P(None, None, None, MP),
            P(MP),
            P(None, MP),
            P(None, MP),
            P(MP),
        ),
        check_vma=False,
    )
```

```python
import functools
import math

import jax
import jax.numpy as jnp
from jax import lax
from jax.experimental import pallas as pl
from jax.experimental.pallas import tpu as pltpu
from jax.sharding import Mesh
from jax.sharding import PartitionSpec as P


post_gain = 0.015625
slope = 0.7978845608028654
cubic = 0.044715
halo = 6
bf16 = jnp.bfloat16
f32 = jnp.float32
NT = (((1,), (1,)), ((), ()))
TN = (((0,), (0,)), ((), ()))
NN = (((1,), (0,)), ((), ()))
DP = ("chip", "core")
MP = ("zh", "zl")


def dot(left, right, dims=NN):
    return lax.dot_general(left, right, dims, preferred_element_type=f32)


def gelu(value):
    inner = jnp.tanh(slope * (value + cubic * value * value * value))
    return 0.5 * value * (1.0 + inner)


def gelu_slope(value):
    square = value * value
    inner = jnp.tanh(slope * value * (1.0 + cubic * square))
    climb = slope * (1.0 + 3.0 * cubic * square)
    return 0.5 * (1.0 + inner) + 0.5 * value * (1.0 - inner * inner) * climb


def struct(shape, kind):
    return jax.ShapeDtypeStruct(shape, kind)


def lanes(blocks):
    return blocks[0] if len(blocks) == 1 else jnp.concatenate(blocks, axis=1)


VMEM = pl.BlockSpec(memory_space=pltpu.VMEM)
SMEM = pl.BlockSpec(memory_space=pltpu.SMEM)
FAR = pl.BlockSpec(memory_space=pl.ANY)
LOAD = "load"


def size_of(array):
    return math.prod(array.shape) * jnp.dtype(array.dtype).itemsize


def call(body, name, ins, outs, scratch=(), spare=6, **more):
    loads = [i for i, (space, _) in enumerate(ins) if space is LOAD]
    spaces = [FAR if space is LOAD else space for space, _ in ins]
    arrays = [array for _, array in ins]
    out_specs = [space for space, _ in outs]
    out_shape = [shape for _, shape in outs]
    held = [arrays[i] for i in loads]
    buffers = [pltpu.VMEM(array.shape, array.dtype) for array in held]
    sems = [pltpu.SemaphoreType.DMA((len(held),))] if held else []
    vmem = sum(size_of(array) for array in held)
    vmem += sum(size_of(a) for space, a in list(ins) + list(outs) if space is VMEM)
    vmem += sum(size_of(b) for b in scratch if b.memory_space == pltpu.VMEM)
    moved = sum(size_of(a) for a in arrays + out_shape)

    def wrapped(*refs):
        inputs = list(refs[: len(ins)])
        outputs = refs[len(ins) : len(ins) + len(outs)]
        rest = refs[len(ins) + len(outs) :]
        kept, tail = rest[: len(held)], rest[len(held) :]
        copies = []
        if held:
            sem, tail = tail[0], tail[1:]
            copies = [
                pltpu.make_async_copy(inputs[i], kept[n], sem.at[n]) for n, i in enumerate(loads)
            ]
        for copy in copies:
            copy.start()
        for n, i in enumerate(loads):
            inputs[i] = kept[n]

        def arrive():
            for copy in copies:
                copy.wait()

        body(arrive, *inputs, *outputs, *tail)

    single = len(outs) == 1
    return pl.pallas_call(
        wrapped,
        in_specs=spaces,
        out_specs=out_specs[0] if single else out_specs,
        out_shape=out_shape[0] if single else out_shape,
        scratch_shapes=buffers + sems + list(scratch),
        compiler_params=pltpu.CompilerParams(vmem_limit_bytes=vmem + (spare << 20)),
        cost_estimate=pl.CostEstimate(flops=0, bytes_accessed=moved, transcendentals=0),
        name=name,
        **more,
    )(*arrays)


def run_copies(pairs, sems):
    copies = [pltpu.make_async_copy(a, b, sems.at[i]) for i, (a, b) in enumerate(pairs)]
    for copy in copies:
        copy.start()
    for copy in copies:
        copy.wait()


def slice_copies(group, idx_ref, own, blocks, sibling, wbuf):
    chip, core, zh = idx_ref[0], idx_ref[1], idx_ref[2]
    size = blocks.shape[-2]
    pairs = [(own, wbuf.at[zh])]
    for j in range(blocks.shape[0]):
        for source, owner in ((blocks, core), (sibling, 1 - core)):
            spot = at((2 * (chip ^ j) + owner) * size, size, size)
            pairs.append((source.at[j, group], wbuf.at[1 - zh, :, spot, :]))
    return pairs


def at(start, size, unit):
    return pl.ds(pl.multiple_of(start, unit), size)


def pool_body(arrive, x_ref, out_ref):
    arrive()
    rows, width, chans = x_ref.shape[1:]
    half = width // 2
    pixel = lax.broadcasted_iota(jnp.int32, (half, 2 * width), 1)
    place = lax.broadcasted_iota(jnp.int32, (half, 2 * width), 0)
    inside = (lax.rem(pixel, width) >= 2 * place) & (lax.rem(pixel, width) < 2 * place + 2)
    pick = jnp.where(inside, 0.25, 0.0).astype(bf16)
    for image in range(x_ref.shape[0]):
        for row in range(rows // 2):
            window = x_ref[image, 2 * row : 2 * row + 2].reshape(2 * width, chans)
            out_ref[image, row * half : (row + 1) * half, :] = dot(pick, window).astype(bf16)


def pool(pixels):
    images, rows, width, chans = pixels.shape
    shape = struct((images, rows * width // 4, chans), bf16)
    return call(pool_body, "pool", [(LOAD, pixels)], [(VMEM, shape)])


def widen_body(arrive, g_ref, out_ref):
    arrive()
    rows, width, chans = out_ref.shape[1:]
    half = width // 2
    pixel = lax.broadcasted_iota(jnp.int32, (width, half), 0)
    place = lax.broadcasted_iota(jnp.int32, (width, half), 1)
    inside = (pixel >= 2 * place) & (pixel < 2 * place + 2)
    pick = jnp.where(inside, 0.25, 0.0).astype(bf16)
    for image in range(g_ref.shape[0]):
        for row in range(rows // 2):
            wide = dot(pick, g_ref[image, row * half : (row + 1) * half, :]).astype(bf16)
            out_ref[image, 2 * row] = wide
            out_ref[image, 2 * row + 1] = wide


def widen(grad, rows, width):
    images, spots, chans = grad.shape
    step = images // 4
    block = pl.BlockSpec((step, spots, chans), lambda i: (i, 0, 0))
    out = pl.BlockSpec((step, rows, width, chans), lambda i: (i, 0, 0, 0))
    return call(
        widen_body,
        "widen",
        [(block, grad)],
        [(out, struct((images, rows, width, chans), bf16))],
        grid=(4,),
    )


def conv_body(side, first, group, arrive, idx_ref, *refs):
    zh, zl = idx_ref[2], idx_ref[3]
    if first:
        xl, xa, xh, xd, wl, wo, ws, bl, bo, pre_ref, act_ref, xbuf, wbuf, acc, sems = refs
        chans = xl.shape[1]
        spots = xbuf.shape[0]
        begin = zh * (xl.shape[0] - spots)
        pairs = []
        for source, up, along in ((xl, zh, zl), (xa, zh, 1 - zl), (xh, 1 - zh, zl), (xd, 1 - zh, 1 - zl)):
            if source is xl:
                source = xl.at[at(begin, spots, side), :]
            pairs.append((source, xbuf.at[:, at((2 * up + along) * chans, chans, chans)]))
    else:
        xl, xa, wl, wo, ws, bl, bo, pre_ref, act_ref, xbuf, wbuf, acc, sems = refs
        chans = xl.shape[1] // 2
        spots = xbuf.shape[0]
        pairs = []
        for source, along in ((xl, zl), (xa, 1 - zl)):
            for up in range(2):
                pairs.append(
                    (
                        source.at[:, up * chans : (up + 1) * chans],
                        xbuf.at[:, at((2 * up + along) * chans, chans, chans)],
                    )
                )
    run_copies(slice_copies(group, idx_ref, wl, wo, ws, wbuf) + pairs, sems)
    arrive()
    acc[...] = jnp.zeros_like(acc)
    outs = 2 * wl.shape[2]
    block = spots // 2
    for x in range(3):
        weights = lanes([wbuf[u, 3 * y + x] for y in range(3) for u in range(2)])
        for begin in range(0, spots, block):
            values = xbuf[begin : begin + block, :]
            if first:
                values = gelu(values.astype(f32)).astype(bf16)
            product = dot(values, weights)
            for y in range(3):
                place = begin + side * (2 - y)
                acc[x, place : place + block, :] += product[:, y * outs : (y + 1) * outs]
    spot = lax.broadcasted_iota(jnp.int32, (block, outs), 0)
    column = lax.rem(spot, side)
    own, other = bl[...], bo[...]
    bias = lanes([jnp.where(zh == 0, own, other), jnp.where(zh == 0, other, own)])
    for begin in range(0, spots, block):
        place = begin + side
        left = pltpu.roll(acc[0, place : place + block, :], 1, 0)
        right = pltpu.roll(acc[2, place : place + block, :], block - 1, 0)
        pre = acc[1, place : place + block, :] + bias
        pre = pre + jnp.where(column > 0, left, 0.0)
        pre = pre + jnp.where(column < side - 1, right, 0.0)
        pre_ref[begin : begin + block, :] = pre
        act_ref[begin : begin + block, :] = gelu(pre).astype(bf16)


def conv(side, idx, sources, own, other, group, bias, bias_other, first=False):
    taps, depth, outs = own.shape
    spots = sources[1].shape[0]
    return call(
        functools.partial(conv_body, side, first, group),
        "conv",
        [(SMEM, idx)]
        + [(FAR, s) for s in sources]
        + [(FAR, own), (FAR, other[0]), (FAR, other[1])]
        + [(VMEM, bias.reshape(1, outs)), (VMEM, bias_other.reshape(1, outs))],
        [(VMEM, struct((spots, 2 * outs), f32)), (VMEM, struct((spots, 2 * outs), bf16))],
        [
            pltpu.VMEM((spots, depth), bf16),
            pltpu.VMEM((2, taps, depth, outs), bf16),
            pltpu.VMEM((3, spots + 2 * side, 2 * outs), f32),
            pltpu.SemaphoreType.DMA((2 * other[0].shape[0] + 5,)),
        ],
        spare=14 if first else 8,
    )


def spread_taps(side, grad, taps_ref):
    pixels, outs = grad.shape
    spot = lax.broadcasted_iota(jnp.int32, (pixels, outs), 0)
    column = lax.rem(spot, side)
    wide = grad.astype(f32)
    ahead = jnp.where(column < side - 1, pltpu.roll(wide, pixels - 1, 0), 0.0).astype(bf16)
    behind = jnp.where(column > 0, pltpu.roll(wide, 1, 0), 0.0).astype(bf16)
    edge = jnp.zeros((side, 3 * outs), bf16)
    taps_ref[:side, :] = edge
    taps_ref[side + pixels :, :] = edge
    taps_ref[side : side + pixels, :] = jnp.concatenate([ahead, grad, behind], axis=1)


def tap_block(side, taps_ref, begin, block):
    return lanes([taps_ref[at(begin + side * (2 - y), block, side), :] for y in range(3)])


def slope_body(side, arrive, idx_ref, keep_ref, recv_ref, pre_ref, mine_ref, theirs_ref, gp_ref):
    arrive()
    zh = idx_ref[2]
    half, outs = mine_ref.shape
    total = keep_ref[...] + recv_ref[...].astype(f32)
    gp_ref[...] = (total * gelu_slope(pre_ref[...])).astype(bf16)
    own = gp_ref[at(zh * halo * side, half, side), :]
    low, high = own[:, :outs], own[:, outs:]
    mine_ref[...] = jnp.where(zh == 0, low, high)
    theirs_ref[...] = jnp.where(zh == 0, high, low)


def slope_back(side, idx, keep, recv, pre, half):
    outs = pre.shape[1] // 2
    return call(
        functools.partial(slope_body, side),
        "slope_back",
        [(SMEM, idx), (LOAD, keep), (LOAD, recv), (LOAD, pre)],
        [
            (VMEM, struct((half, outs), bf16)),
            (VMEM, struct((half, outs), bf16)),
            (VMEM, struct(pre.shape, bf16)),
        ],
    )


def back_body(side, last, group, arrive, idx_ref, *refs):
    zh, zl = idx_ref[2], idx_ref[3]
    if last:
        grad_ref, wl, wo, ws, own_ref, give_ref, taps_ref, wbuf, sems = refs
    else:
        keep_ref, recv_ref, pre_ref, wl, wo, ws, gp_ref, own_ref, give_ref, taps_ref, wbuf, sems = refs
    pairs = slice_copies(group, idx_ref, wl, wo, ws, wbuf)
    copies = [pltpu.make_async_copy(a, b, sems.at[i]) for i, (a, b) in enumerate(pairs)]
    for copy in copies:
        copy.start()
    arrive()
    if last:
        grad = grad_ref[...]
    else:
        total = keep_ref[...] + recv_ref[...].astype(f32)
        grad = (total * gelu_slope(pre_ref[...])).astype(bf16)
        gp_ref[...] = grad
    spread_taps(side, grad, taps_ref)
    depth, outs = wl.shape[1:]
    pixels = own_ref.shape[-2]
    start = zh * halo * side
    for copy in copies:
        copy.wait()
    block = pixels // 2
    chans = depth // 4

    def rows(index):
        spot = at(index * chans, chans, chans)
        return lanes([wbuf[u, t, spot, :] for t in range(9) for u in range(2)])

    for target, along in ((give_ref, 1 - zl), (own_ref, zl)):
        if last:
            for up in range(2):
                weights = rows(2 * up + along)
                for begin in range(0, pixels, block):
                    part = dot(tap_block(side, taps_ref, start + begin, block), weights, NT)
                    target[up, begin : begin + block, :] = part.astype(target.dtype)
        else:
            weights = jnp.concatenate([rows(along), rows(2 + along)], axis=0)
            for begin in range(0, pixels, block):
                part = dot(tap_block(side, taps_ref, begin, block), weights, NT)
                target[begin : begin + block, :] = part.astype(target.dtype)


def back(side, idx, sources, own, other, group, half=0):
    taps, depth, outs = own.shape
    spots = sources[-1].shape[0]
    if half:
        shape = (2, half, depth // 4)
        results = []
    else:
        shape = (spots, depth // 2)
        results = [(VMEM, struct((spots, 2 * outs), bf16))]
    results += [(VMEM, struct(shape, f32)), (VMEM, struct(shape, bf16))]
    return call(
        functools.partial(back_body, side, bool(half), group),
        "back",
        [(SMEM, idx)]
        + [(LOAD, source) for source in sources]
        + [(FAR, own), (FAR, other[0]), (FAR, other[1])],
        results,
        [
            pltpu.VMEM((spots + 2 * side, 6 * outs), bf16),
            pltpu.VMEM((2, taps, depth, outs), bf16),
            pltpu.SemaphoreType.DMA((2 * other[0].shape[0] + 1,)),
        ],
        spare=14 if half else 10,
    )


def put_blocks(idx_ref, keep_ref, give_ref, part, tap, first_block, size, begin=0):
    chip, core = idx_ref[0], idx_ref[1]
    for b in range(0, part.shape[0] // size, 2):
        even = part[b * size : (b + 1) * size, :]
        odd = part[(b + 1) * size : (b + 2) * size, :]
        slot = chip ^ ((first_block + b) // 2)
        rows = slice(begin + tap * size, begin + (tap + 1) * size)
        keep_ref[slot, rows, :] = jnp.where(core == 0, even, odd).astype(bf16)
        give_ref[slot, rows, :] = jnp.where(core == 0, odd, even).astype(bf16)


def weight_body(side, half, arrive, idx_ref, gp_ref, xl, xa, keep_ref, give_ref, xbuf, taps_ref, sems):
    arrive()
    zh, zl = idx_ref[2], idx_ref[3]
    chans = xl.shape[1] // 2
    pairs = []
    for source, along in ((xl, zl), (xa, 1 - zl)):
        for up in range(2):
            pairs.append(
                (
                    source.at[:, up * chans : (up + 1) * chans],
                    xbuf.at[:, at((2 * up + along) * chans, chans, chans)],
                )
            )
    run_copies(pairs, sems)
    spots, wide = gp_ref.shape
    outs = wide // 2
    spot = lax.broadcasted_iota(jnp.int32, (spots, wide), 0) - zh * halo * side
    grad = jnp.where((spot >= 0) & (spot < half), gp_ref[...].astype(f32), 0.0)
    bias = jnp.sum(grad, axis=0, keepdims=True)
    spread_taps(side, grad.astype(bf16), taps_ref)
    blocks = 2 * keep_ref.shape[0]
    depth = xbuf.shape[1]
    size = depth // blocks
    for begin in range(0, depth, 256):
        values = xbuf[:, begin : begin + 256]
        for y in range(3):
            place = side * (2 - y)
            part = dot(values, taps_ref[place : place + spots, :], TN)
            for x in range(3):
                for u in range(2):
                    col = x * wide + u * outs
                    put_blocks(
                        idx_ref, keep_ref, give_ref, part[:, col : col + outs],
                        3 * y + x, begin // size, size, u * (9 * size + 16),
                    )
    for u in range(2):
        row = jnp.broadcast_to(bias[:, u * outs : (u + 1) * outs], (16, outs)).astype(bf16)
        for j in range(keep_ref.shape[0]):
            spot = slice(u * (9 * size + 16) + 9 * size, (u + 1) * (9 * size + 16))
            keep_ref[j, spot, :] = row
            give_ref[j, spot, :] = row


def weight_grad(side, half, idx, grad, act, act_other, chips):
    spots, wide = grad.shape
    outs = wide // 2
    depth = 2 * act.shape[1]
    rows = 9 * depth // (2 * chips) + 16
    return call(
        functools.partial(weight_body, side, half),
        "weight_grad",
        [(SMEM, idx), (LOAD, grad), (FAR, act), (FAR, act_other)],
        [(VMEM, struct((chips, 2 * rows, outs), bf16))] * 2,
        [
            pltpu.VMEM((spots, depth), bf16),
            pltpu.VMEM((spots + 2 * side, 3 * wide), bf16),
            pltpu.SemaphoreType.DMA((4,)),
        ],
        spare=10,
    )


def weight_one_body(side, arrive, idx_ref, mine_ref, theirs_ref, x_ref, keep_ref, give_ref, gp_ref, taps_ref):
    arrive()
    zh = idx_ref[2]
    half, outs = mine_ref.shape
    gp_ref[at(zh * half, half, side), :] = mine_ref[...]
    gp_ref[at((1 - zh) * half, half, side), :] = theirs_ref[...]
    grad = gp_ref[...]
    bias = jnp.sum(grad.astype(f32), axis=0, keepdims=True)
    spread_taps(side, grad, taps_ref)
    blocks = 2 * keep_ref.shape[0]
    spots, depth = x_ref.shape
    size = depth // blocks
    right = tap_block(side, taps_ref, 0, spots)
    for begin in range(0, depth, 256):
        part = dot(x_ref[:, begin : begin + 256], right, TN)
        for tap in range(9):
            put_blocks(
                idx_ref, keep_ref, give_ref, part[:, tap * outs : (tap + 1) * outs],
                tap, begin // size, size,
            )
    row = jnp.broadcast_to(bias, (16, outs)).astype(bf16)
    for j in range(keep_ref.shape[0]):
        keep_ref[j, 9 * size :, :] = row
        give_ref[j, 9 * size :, :] = row


def weight_one_grad(side, idx, mine, theirs, act_zero, chips):
    spots, depth = act_zero.shape
    outs = mine.shape[1]
    rows = 9 * depth // (2 * chips) + 16
    return call(
        functools.partial(weight_one_body, side),
        "weight_one_grad",
        [(SMEM, idx), (LOAD, mine), (LOAD, theirs), (LOAD, act_zero)],
        [(VMEM, struct((chips, rows, outs), bf16))] * 2,
        [
            pltpu.VMEM((spots, outs), bf16),
            pltpu.VMEM((spots + 2 * side, 3 * outs), bf16),
        ],
        spare=14,
    )


def pair_body(arrive, idx_ref, *refs):
    arrive()
    pairs, outs = refs[: -refs[0].shape[0]], refs[-refs[0].shape[0] :]
    for j, out in enumerate(outs):
        begin = 0
        for keep, recv in zip(pairs[0::2], pairs[1::2]):
            rows = keep.shape[1]
            total = keep[j].astype(f32) + recv[j].astype(f32)
            out[begin : begin + rows, :] = total.astype(bf16)
            begin += rows


def pair_sum(idx, *pairs):
    chips, _, wide = pairs[0].shape
    rows = sum(p.shape[1] for p in pairs[0::2])
    return call(
        pair_body,
        "pair_sum",
        [(SMEM, idx)] + [(LOAD, p) for p in pairs],
        [(VMEM, struct((rows, wide), bf16))] * chips,
    )


def chip_body(arrive, idx_ref, *refs):
    arrive()
    parts, (keep_ref, give_ref, extra_ref) = refs[:-3], refs[-3:]
    zh = idx_ref[2]
    rows = keep_ref.shape[0]
    for target, begin in ((keep_ref, zh * rows), (give_ref, (1 - zh) * rows), (extra_ref, 2 * rows)):
        spot = at(begin, target.shape[0], 16)
        total = parts[0][spot, :].astype(f32)
        for part in parts[1:]:
            total = total + part[spot, :].astype(f32)
        target[...] = total.astype(target.dtype)


def chip_sum(idx, parts, rows):
    wide = parts[0].shape[1]
    extra = parts[0].shape[0] - 2 * rows
    return call(
        chip_body,
        "chip_sum",
        [(SMEM, idx)] + [(LOAD, p) for p in parts],
        [
            (VMEM, struct((rows, wide), f32)),
            (VMEM, struct((rows, wide), bf16)),
            (VMEM, struct((extra, wide), bf16)),
        ],
    )


def final_body(depth, arrive, idx_ref, own_ref, sib_ref, grad_ref, bias_ref, *flat):
    arrive()
    chip, core = idx_ref[0], idx_ref[1]
    chips = own_ref.shape[0]
    size = depth // (2 * chips)
    bias_ref[...] = own_ref[0, 9 * size : 9 * size + 1, :].astype(f32)
    for j in range(chips):
        for source, owner in ((own_ref, core), (sib_ref, 1 - core)):
            spot = at((2 * (chip ^ j) + owner) * size, size, size)
            for tap in range(9):
                grad_ref[tap, spot, :] = source[j, tap * size : (tap + 1) * size, :].astype(f32)
    if flat:
        flat_ref, flat_bias_ref = flat
        first = 9 * size + 16
        wide = own_ref.shape[2]
        columns = flat_ref.shape[1] // wide
        size = flat_ref.shape[0] // (2 * chips)
        for c in range(columns):
            row = first + columns * size + c
            flat_bias_ref[:, c * wide : (c + 1) * wide] = own_ref[0, row : row + 1, :].astype(f32)
        for j in range(chips):
            for source, owner in ((own_ref, core), (sib_ref, 1 - core)):
                spot = at((2 * (chip ^ j) + owner) * size, size, size)
                for c in range(columns):
                    row = first + c * size
                    piece = source[j, row : row + size, :].astype(f32)
                    flat_ref[spot, c * wide : (c + 1) * wide] = piece


def final_grads(idx, own, sib, depth, flat_shape=None):
    outs = own.shape[2]
    results = [(VMEM, struct((9, depth, outs), f32)), (VMEM, struct((1, outs), f32))]
    if flat_shape:
        results += [(VMEM, struct(flat_shape, f32)), (VMEM, struct((1, flat_shape[1]), f32))]
    return call(
        functools.partial(final_body, depth),
        "final_grads",
        [(SMEM, idx), (LOAD, own), (LOAD, sib)],
        results,
    )


def outer_body(gain, arrive, idx_ref, x_ref, go_ref, bias_ref, keep_ref, give_ref):
    arrive()
    chip, core = idx_ref[0], idx_ref[1]
    chips, rows, wide = keep_ref.shape
    columns = go_ref.shape[1] // wide
    size = (rows - 16) // columns
    bias = jnp.concatenate(
        [bias_ref[:, c * wide : (c + 1) * wide] for c in range(columns)]
        + [jnp.zeros((16 - columns, wide), f32)],
        axis=0,
    ).astype(bf16)
    for j in range(chips):
        keep_ref[j, columns * size :, :] = bias
        give_ref[j, columns * size :, :] = bias
    for begin in range(0, x_ref.shape[1], 256):
        part = gain * dot(x_ref[:, begin : begin + 256], go_ref[...], TN)
        for b in range(0, 256 // size, 2):
            slot = chip ^ ((begin // size + b) // 2)
            for c in range(columns):
                even = part[b * size : (b + 1) * size, c * wide : (c + 1) * wide]
                odd = part[(b + 1) * size : (b + 2) * size, c * wide : (c + 1) * wide]
                spot = slice(c * size, (c + 1) * size)
                keep_ref[slot, spot, :] = jnp.where(core == 0, even, odd).astype(bf16)
                give_ref[slot, spot, :] = jnp.where(core == 0, odd, even).astype(bf16)


def outer(idx, x, go, gain, bias, chips):
    rows = (go.shape[1] // 128) * (x.shape[1] // (2 * chips)) + 16
    return call(
        functools.partial(outer_body, gain),
        "outer",
        [(SMEM, idx), (LOAD, x), (LOAD, go), (LOAD, bias)],
        [(VMEM, struct((chips, rows, 128), bf16))] * 2,
        spare=8,
    )


def start_body(arrive, idx_ref, valid_ref, cot_ref, outk_ref, go_ref, bias_ref, own_ref, give_ref):
    arrive()
    zl = idx_ref[3]
    masked = cot_ref[...].astype(f32) * valid_ref[0]
    go_ref[...] = masked.astype(bf16)
    bias_ref[...] = jnp.sum(masked, axis=0, keepdims=True)
    chans = outk_ref.shape[0] // 4
    block = cot_ref.shape[0] // 4
    for target, along in ((give_ref, 1 - zl), (own_ref, zl)):
        weights = jnp.concatenate(
            [outk_ref[at((2 * up + along) * chans, chans, chans), :] for up in range(2)], axis=0
        )
        for begin in range(0, cot_ref.shape[0], block):
            part = post_gain * dot(go_ref[begin : begin + block, :], weights, NT)
            target[begin : begin + block, :] = part.astype(target.dtype)


def start_back(idx, valid, cot, outk):
    spots, outs = cot.shape
    half = outk.shape[0] // 2
    return call(
        start_body,
        "start_back",
        [(SMEM, idx), (SMEM, valid), (LOAD, cot), (LOAD, outk)],
        [
            (VMEM, struct(cot.shape, bf16)),
            (VMEM, struct((1, outs), f32)),
            (VMEM, struct((spots, half), f32)),
            (VMEM, struct((spots, half), bf16)),
        ],
    )


def identity_body(arrive, idx_ref, go_ref, idk_ref, own_ref, give_ref):
    arrive()
    zl = idx_ref[3]
    chans = idk_ref.shape[0] // 4
    block = go_ref.shape[0] // 4
    for target, along in ((give_ref, 1 - zl), (own_ref, zl)):
        for up in range(2):
            weights = idk_ref[at((2 * up + along) * chans, chans, chans), :]
            for begin in range(0, go_ref.shape[0], block):
                part = dot(go_ref[begin : begin + block, :], weights, NT)
                target[up, begin : begin + block, :] = part.astype(target.dtype)


def identity_back(idx, go, idk):
    spots, outs = go.shape
    chans = idk.shape[0] // 4
    return call(
        identity_body,
        "identity_back",
        [(SMEM, idx), (LOAD, go), (LOAD, idk)],
        [(VMEM, struct((2, spots, chans), f32)), (VMEM, struct((2, spots, chans), bf16))],
    )


def rows_body(side, arrive, idx_ref, own_ref, recv_ref, keep_ref, give_ref):
    arrive()
    zh = idx_ref[2]
    spots = keep_ref.shape[0]
    apart = own_ref.shape[0] - spots
    for target, begin in ((give_ref, (1 - zh) * apart), (keep_ref, zh * apart)):
        spot = at(begin, spots, side)
        total = own_ref[spot, :] + recv_ref[spot, :].astype(f32)
        target[...] = total.astype(target.dtype)


def rows_sum(side, idx, own, recv, spots):
    shape = (spots, own.shape[1])
    return call(
        functools.partial(rows_body, side),
        "rows_sum",
        [(SMEM, idx), (LOAD, own), (LOAD, recv)],
        [(VMEM, struct(shape, f32)), (VMEM, struct(shape, bf16))],
    )


def slots_body(arrive, idx_ref, own_ref, recv_ref, keep_ref, give_ref):
    arrive()
    zh = idx_ref[2]
    for target, slot in ((give_ref, 1 - zh), (keep_ref, zh)):
        total = own_ref[slot] + recv_ref[slot].astype(f32)
        target[...] = total.astype(target.dtype)


def slots_sum(idx, own, recv):
    shape = own.shape[1:]
    return call(
        slots_body,
        "slots_sum",
        [(SMEM, idx), (LOAD, own), (LOAD, recv)],
        [(VMEM, struct(shape, f32)), (VMEM, struct(shape, bf16))],
    )


def input_body(arrive, idx_ref, x_ref, keep_ref, recv_ref, id_ref, id_recv_ref, out_ref):
    arrive()
    zh = idx_ref[2]
    half = keep_ref.shape[0]
    for part in range(2):
        rows = slice(part * half, (part + 1) * half)
        conv = jnp.where(zh == part, keep_ref[...], recv_ref[...].astype(f32))
        straight = id_ref[rows, :] + id_recv_ref[rows, :].astype(f32)
        total = conv * gelu_slope(x_ref[rows, :].astype(f32)) + straight
        out_ref[rows, :] = total.astype(bf16)


def input_grad(idx, x, keep, recv, id_keep, id_recv):
    return call(
        input_body,
        "input_grad",
        [(SMEM, idx)] + [(LOAD, a) for a in (x, keep, recv, id_keep, id_recv)],
        [(VMEM, struct(x.shape, bf16))],
    )


def whole_body(side, arrive, idx_ref, xl, xa, xh, xd, rh, rl, x_ref, act_ref, sems):
    arrive()
    zh, zl = idx_ref[2], idx_ref[3]
    chans = xl.shape[1]
    spots = xa.shape[0]
    rest = xl.shape[0] - spots
    window, outside = at(zh * rest, spots, side), at((1 - zh) * spots, rest, side)

    def cols(up, along):
        return at((2 * up + along) * chans, chans, chans)

    run_copies(
        [
            (xl, x_ref.at[:, cols(zh, zl)]),
            (xa, x_ref.at[window, cols(zh, 1 - zl)]),
            (xh, x_ref.at[window, cols(1 - zh, zl)]),
            (xd, x_ref.at[window, cols(1 - zh, 1 - zl)]),
            (rl.at[0], x_ref.at[outside, cols(zh, 1 - zl)]),
            (rh, x_ref.at[outside, cols(1 - zh, zl)]),
            (rl.at[1], x_ref.at[outside, cols(1 - zh, 1 - zl)]),
        ],
        sems,
    )
    block = x_ref.shape[0] // 8
    for begin in range(0, x_ref.shape[0], block):
        rows = slice(begin, begin + block)
        act_ref[rows, :] = gelu(x_ref[rows, :].astype(f32)).astype(bf16)


def whole_input(side, idx, *parts):
    spots, chans = parts[0].shape
    return call(
        functools.partial(whole_body, side),
        "whole_input",
        [(SMEM, idx)] + [(FAR, p) for p in parts],
        [(VMEM, struct((spots, 4 * chans), bf16))] * 2,
        [pltpu.SemaphoreType.DMA((7,))],
    )


def join_body(arrive, idx_ref, own, recv, far_own, far_recv, out, sems):
    arrive()
    zh, zl = idx_ref[2], idx_ref[3]
    half = own.shape[0]
    chans = own.shape[1] // 2
    pairs = []
    for source, up, along in ((own, zh, zl), (recv, zh, 1 - zl), (far_own, 1 - zh, zl), (far_recv, 1 - zh, 1 - zl)):
        for slot in range(2):
            spot = at((2 * slot + along) * chans, chans, chans)
            target = out.at[at(up * half, half, half), spot]
            pairs.append((source.at[:, slot * chans : (slot + 1) * chans], target))
    run_copies(pairs, sems)


def join(idx, *parts):
    half, wide = parts[0].shape
    return call(
        join_body,
        "join",
        [(SMEM, idx)] + [(FAR, p) for p in parts],
        [(VMEM, struct((2 * half, 2 * wide), bf16))],
        [pltpu.SemaphoreType.DMA((8,))],
    )


def finish_body(arrive, idx_ref, valid_ref, x_ref, act_ref, idk_ref, outk_ref, ib_ref, out_ref):
    arrive()
    block = x_ref.shape[0] // 4
    for begin in range(0, x_ref.shape[0], block):
        rows = slice(begin, begin + block)
        identity = dot(x_ref[rows, :], idk_ref[...]) + ib_ref[...]
        branch = dot(act_ref[rows, :], outk_ref[...])
        out_ref[rows, :] = ((identity + post_gain * branch) * valid_ref[0]).astype(bf16)


def finish(idx, valid, x, act, idk, outk, ib):
    outs = idk.shape[1]
    return call(
        finish_body,
        "finish",
        [(SMEM, idx), (SMEM, valid), (LOAD, x), (LOAD, act), (LOAD, idk), (LOAD, outk)]
        + [(VMEM, ib.reshape(1, outs))],
        [(VMEM, struct((x.shape[0], outs), bf16))],
        spare=8,
    )


def flip(value, axis):
    return lax.ppermute(value, axis, [(0, 1), (1, 0)])


def hop(value, j, chips):
    return lax.ppermute(value, "chip", [(i, i ^ j) for i in range(chips)])


def gather_chips(value, chips):
    return [value] + [hop(value, j, chips) for j in range(1, chips)]


def swap(pieces, axis):
    return lax.all_to_all(pieces, axis, split_axis=0, concat_axis=0, tiled=True)


def after(value, other):
    return lax.optimization_barrier((value, other))[0]


def rows_of(value, start, size):
    return lax.dynamic_slice_in_dim(value, start, size, 0)


def local(
    pixels,
    counts,
    kernel_one,
    bias_one,
    kernel_two,
    bias_two,
    kernel_three,
    bias_three,
    out_kernel,
    identity_kernel,
    identity_bias,
    cotangent,
):
    images, rows, width, chans = pixels.shape
    side = width // 2
    spots = side * side
    half = spots // 2
    window = half + halo * side
    outs = cotangent.shape[3]
    chips = lax.axis_size("chip")
    chip, core, zh, zl = [lax.axis_index(a) for a in ("chip", "core", "zh", "zl")]
    idx = jnp.stack([chip, core, zh, zl]).astype(jnp.int32)
    taps = lambda kernel: kernel.reshape((9,) + kernel.shape[2:])
    one, two, three = taps(kernel_one), taps(kernel_two), taps(kernel_three)

    own_count = lax.dynamic_index_in_dim(counts, 2 * chip + core, 0, keepdims=True)
    valid = (own_count > 0).astype(f32)

    def block_of(kernel):
        size = kernel.shape[1] // (2 * chips)
        return lax.dynamic_slice_in_dim(kernel, (2 * chip + core) * size, size, 1)

    def other_half(*kernels):
        return jnp.stack([block_of(kernel) for kernel in kernels])

    def around(piece, *others):
        own = jnp.stack(after(gather_chips(piece, chips), others))
        return own, flip(own, "core")

    last = [idx]

    def turn(*others):
        return after(idx, (last[0],) + others)

    def ran(results):
        last[0] = results[-1] if isinstance(results, (list, tuple)) else results
        return results

    bias_other = flip(jnp.stack([bias_one, bias_two, bias_three]), "zh")
    first_piece = flip(other_half(one), "zh")
    pooled = ran(pool(pixels))
    go, identity_bias_grad, ga_own, ga_give = ran(
        start_back(turn(), valid, cotangent.reshape(spots, outs), out_kernel)
    )
    ga_recv = flip(ga_give, "zl")
    id_own, id_give = ran(identity_back(turn(), go, identity_kernel))
    id_recv = flip(id_give, "zl")

    xl = swap(after(pooled, (first_piece, bias_other, id_give)), DP).reshape(spots, chans)
    begin = zh * (spots - window)
    begin_other = (1 - zh) * (spots - window)
    xa = flip(rows_of(xl, begin, window), "zl")
    xh = flip(rows_of(xl, begin_other, window), "zh")
    one_other = around(first_piece)
    ga_keep, ga_give = ran(rows_sum(side, turn(xa), ga_own, ga_recv, window))
    xd = flip(after(xh, one_other[0]), "zl")
    both_piece = flip(after(other_half(two, three), first_piece), "zh")
    both_other = around(both_piece, xh)

    pre_one, act_one = ran(
        conv(side, turn(both_other[0], xa), (xl, xa, xh, xd), one, one_other, 0, bias_one, bias_other[0], True)
    )
    act_one_other = flip(act_one, "zl")
    ga_recv = flip(after(ga_give, xh), "zh")
    rest = spots - window
    rest_own = rows_of(xl, (1 - zh) * window, rest)
    rest_high = flip(after(rows_of(xl, zh * window, rest), act_one), "zh")
    id_keep, id_give = ran(slots_sum(turn(), id_own, id_recv))
    pre_two, act_two = ran(
        conv(side, turn(), (act_one, act_one_other), two, both_other, 0, bias_two, bias_other[1])
    )
    act_two_other = flip(act_two, "zl")
    rest_low = flip(jnp.stack([rest_own, rest_high]), "zl")
    id_recv = flip(after(id_give, act_two), "zh")

    full_x, act_zero = ran(whole_input(side, turn(), xl, xa, xh, xd, rest_high, rest_low))
    keep_id, give_id = ran(outer(turn(), full_x, go, 1.0, identity_bias_grad, chips))
    recv_id = flip(give_id, "core")
    pre_three, act_three = ran(
        conv(side, turn(), (act_two, act_two_other), three, both_other, 1, bias_three, bias_other[2])
    )
    own_rows = rows_of(act_three, zh * halo * side, half)
    near_rows = flip(own_rows, "zl")
    far_rows = flip(own_rows, "zh")

    gp_three, ga_own, ga_give = ran(
        back(side, turn(), (ga_keep, ga_recv, pre_three), three, both_other, 1)
    )
    ga_recv = flip(ga_give, "zl")
    keep_three, give_three = ran(weight_grad(side, half, turn(), gp_three, act_two, act_two_other, chips))
    recv_three = flip(give_three, "core")
    gp_two, ga_own, ga_give = ran(
        back(side, turn(near_rows), (ga_own, ga_recv, pre_two), two, both_other, 0)
    )
    ga_recv = flip(ga_give, "zl")
    parts_three = ran(pair_sum(turn(), keep_three, recv_three, keep_id, recv_id))
    parts_three = [parts_three[0]] + [hop(parts_three[j], j, chips) for j in range(1, chips)]
    keep_two, give_two = ran(weight_grad(side, half, turn(), gp_two, act_one, act_one_other, chips))
    recv_two = flip(give_two, "core")
    far_near_rows = flip(far_rows, "zl")

    gp_mine, gp_theirs, gp_one = ran(slope_back(side, turn(), ga_own, ga_recv, pre_one, half))
    gp_theirs = flip(gp_theirs, "zh")
    gx_own, gx_give = ran(back(side, turn(), (gp_one,), one, one_other, 0, half))
    gx_recv = flip(gx_give, "zl")

    keep_one, give_one = ran(weight_one_grad(side, turn(), gp_mine, gp_theirs, act_zero, chips))
    recv_one = flip(give_one, "core")
    full_three = ran(join(turn(), own_rows, near_rows, far_rows, far_near_rows))
    keep_out, give_out = ran(outer(turn(), full_three, go, post_gain, identity_bias_grad, chips))
    recv_out = flip(give_out, "core")
    gx_keep, gx_give = ran(slots_sum(turn(), gx_own, gx_recv))
    gx_recv = flip(gx_give, "zh")
    parts_one = ran(pair_sum(turn(), keep_one, recv_one))
    parts_one = [parts_one[0]] + [hop(parts_one[j], j, chips) for j in range(1, chips)]
    parts_two = ran(pair_sum(turn(), keep_two, recv_two, keep_out, recv_out))
    parts_two = [parts_two[0]] + [hop(parts_two[j], j, chips) for j in range(1, chips)]
    deep = two.shape[1]
    slot_rows = 9 * deep // (2 * chips) + 16
    keep_three, give_three, id_rows = ran(chip_sum(turn(), parts_three, slot_rows))
    recv_three = flip(give_three, "zh")

    gx = ran(input_grad(turn(), xl, gx_keep, gx_recv, id_keep, id_recv))
    gx = swap(gx.reshape(images, rows * width // 4, chans), DP)
    block_out = ran(finish(turn(), valid, full_x, full_three, identity_kernel, out_kernel, identity_bias))

    def spread(total):
        total = jnp.stack(gather_chips(total, chips))
        return total, flip(total, "core")

    def both(keep, recv, rows):
        return jnp.concatenate([(keep + recv.astype(f32)).astype(bf16), rows])

    total = parts_one[0].astype(f32)
    for part in parts_one[1:]:
        total = total + part.astype(f32)
    all_one = spread(total.astype(bf16))
    all_three = spread(both(keep_three, recv_three, id_rows))
    keep_two, give_two, out_rows = ran(chip_sum(turn(), parts_two, slot_rows))
    recv_two = flip(give_two, "zh")
    all_two = spread(both(keep_two, recv_two, out_rows))
    pixels_grad = widen(gx, rows, width)
    kernel_three_grad, bias_three_grad, identity_kernel_grad, identity_bias_grad = ran(
        final_grads(turn(), *all_three, deep, identity_kernel.shape)
    )
    kernel_one_grad, bias_one_grad = ran(final_grads(turn(), *all_one, one.shape[1]))
    kernel_two_grad, bias_two_grad, out_kernel_grad, _ = ran(
        final_grads(turn(), *all_two, deep, out_kernel.shape)
    )

    return (
        block_out.reshape(cotangent.shape),
        pixels_grad,
        kernel_one_grad.reshape(kernel_one.shape),
        bias_one_grad[0],
        kernel_two_grad.reshape(kernel_two.shape),
        bias_two_grad[0],
        kernel_three_grad.reshape(kernel_three.shape),
        bias_three_grad[0],
        out_kernel_grad,
        identity_kernel_grad,
        identity_bias_grad[0],
    )


def solution(mesh):
    members = mesh.devices.size // mesh.shape["mp"]
    fine = Mesh(
        mesh.devices.reshape(members // 2, 2, 2, mesh.shape["mp"] // 2),
        ("chip", "core", "zh", "zl"),
    )
    return jax.shard_map(
        local,
        mesh=fine,
        in_specs=(
            P(None, DP, None, MP),
            P(),
            P(None, None, None, MP),
            P(MP),
            P(None, None, None, MP),
            P(MP),
            P(None, None, None, MP),
            P(MP),
            P(None, MP),
            P(None, MP),
            P(MP),
            P(DP, None, None, MP),
        ),
        out_specs=(
            P(DP, None, None, MP),
            P(None, DP, None, MP),
            P(None, None, None, MP),
            P(MP),
            P(None, None, None, MP),
            P(MP),
            P(None, None, None, MP),
            P(MP),
            P(None, MP),
            P(None, MP),
            P(MP),
        ),
        check_vma=False,
    )
```

```python
import functools
import math

import jax
import jax.numpy as jnp
from jax import lax
from jax.experimental import pallas as pl
from jax.experimental.pallas import tpu as pltpu
from jax.sharding import Mesh
from jax.sharding import PartitionSpec as P


post_gain = 0.015625
slope = 0.7978845608028654
cubic = 0.044715
halo = 6
bf16 = jnp.bfloat16
f32 = jnp.float32
NT = (((1,), (1,)), ((), ()))
TN = (((0,), (0,)), ((), ()))
NN = (((1,), (0,)), ((), ()))
DP = ("chip", "core")
MP = ("zh", "zl")


def dot(left, right, dims=NN):
    return lax.dot_general(left, right, dims, preferred_element_type=f32)


def gelu(value):
    inner = jnp.tanh(slope * (value + cubic * value * value * value))
    return 0.5 * value * (1.0 + inner)


def gelu_slope(value):
    square = value * value
    inner = jnp.tanh(slope * value * (1.0 + cubic * square))
    climb = slope * (1.0 + 3.0 * cubic * square)
    return 0.5 * (1.0 + inner) + 0.5 * value * (1.0 - inner * inner) * climb


def struct(shape, kind):
    return jax.ShapeDtypeStruct(shape, kind)


def lanes(blocks):
    return blocks[0] if len(blocks) == 1 else jnp.concatenate(blocks, axis=1)


VMEM = pl.BlockSpec(memory_space=pltpu.VMEM)
SMEM = pl.BlockSpec(memory_space=pltpu.SMEM)
FAR = pl.BlockSpec(memory_space=pl.ANY)
LOAD = "load"


def size_of(array):
    return math.prod(array.shape) * jnp.dtype(array.dtype).itemsize


def call(body, name, ins, outs, scratch=(), spare=6, **more):
    loads = [i for i, (space, _) in enumerate(ins) if space is LOAD]
    spaces = [FAR if space is LOAD else space for space, _ in ins]
    arrays = [array for _, array in ins]
    out_specs = [space for space, _ in outs]
    out_shape = [shape for _, shape in outs]
    held = [arrays[i] for i in loads]
    buffers = [pltpu.VMEM(array.shape, array.dtype) for array in held]
    sems = [pltpu.SemaphoreType.DMA((len(held),))] if held else []
    vmem = sum(size_of(array) for array in held)
    vmem += sum(size_of(a) for space, a in list(ins) + list(outs) if space is VMEM)
    vmem += sum(size_of(b) for b in scratch if b.memory_space == pltpu.VMEM)
    moved = sum(size_of(a) for a in arrays + out_shape) // 16

    def wrapped(*refs):
        inputs = list(refs[: len(ins)])
        outputs = refs[len(ins) : len(ins) + len(outs)]
        rest = refs[len(ins) + len(outs) :]
        kept, tail = rest[: len(held)], rest[len(held) :]
        copies = []
        if held:
            sem, tail = tail[0], tail[1:]
            copies = [
                pltpu.make_async_copy(inputs[i], kept[n], sem.at[n]) for n, i in enumerate(loads)
            ]
        for copy in copies:
            copy.start()
        for n, i in enumerate(loads):
            inputs[i] = kept[n]

        def arrive():
            for copy in copies:
                copy.wait()

        body(arrive, *inputs, *outputs, *tail)

    single = len(outs) == 1
    return pl.pallas_call(
        wrapped,
        in_specs=spaces,
        out_specs=out_specs[0] if single else out_specs,
        out_shape=out_shape[0] if single else out_shape,
        scratch_shapes=buffers + sems + list(scratch),
        compiler_params=pltpu.CompilerParams(vmem_limit_bytes=vmem + (spare << 20)),
        cost_estimate=pl.CostEstimate(flops=0, bytes_accessed=moved, transcendentals=0),
        name=name,
        **more,
    )(*arrays)


def run_copies(pairs, sems):
    for copy in start_copies(pairs, sems):
        copy.wait()


def slice_copies(group, idx_ref, own, blocks, sibling, wbuf):
    chip, core, zh = idx_ref[0], idx_ref[1], idx_ref[2]
    size = blocks.shape[-2]
    pairs = [(own, wbuf.at[zh])]
    for j in range(blocks.shape[0]):
        for source, owner in ((blocks, core), (sibling, 1 - core)):
            spot = at((2 * (chip ^ j) + owner) * size, size, size)
            pairs.append((source.at[j, 9 * group : 9 * group + 9], wbuf.at[1 - zh, :, spot, :]))
    return pairs


def flat_copies(first, idx_ref, blocks, sibling, buffer):
    chip, core = idx_ref[0], idx_ref[1]
    columns, units = buffer.shape[:2]
    chips = blocks.shape[0]
    count = units // (2 * chips)
    pairs = []
    for j in range(chips):
        for source, owner in ((blocks, core), (sibling, 1 - core)):
            spot = pl.ds((2 * (chip ^ j) + owner) * count, count)
            for c in range(columns):
                begin = first + c * count
                pairs.append((source.at[j, begin : begin + count], buffer.at[c, spot]))
    return pairs


def start_copies(pairs, sems):
    copies = [pltpu.make_async_copy(a, b, sems.at[i]) for i, (a, b) in enumerate(pairs)]
    for copy in copies:
        copy.start()
    return copies


def flat_rows(buffer, begin, count):
    columns, _, size, wide = buffer.shape
    return lanes([buffer[c, pl.ds(begin, count)].reshape(count * size, wide) for c in range(columns)])


def at(start, size, unit):
    return pl.ds(pl.multiple_of(start, unit), size)


def pool_body(arrive, x_ref, out_ref):
    arrive()
    rows, width, chans = x_ref.shape[1:]
    half = width // 2
    pixel = lax.broadcasted_iota(jnp.int32, (half, 2 * width), 1)
    place = lax.broadcasted_iota(jnp.int32, (half, 2 * width), 0)
    inside = (lax.rem(pixel, width) >= 2 * place) & (lax.rem(pixel, width) < 2 * place + 2)
    pick = jnp.where(inside, 0.25, 0.0).astype(bf16)
    for image in range(x_ref.shape[0]):
        for row in range(rows // 2):
            window = x_ref[image, 2 * row : 2 * row + 2].reshape(2 * width, chans)
            out_ref[image, row * half : (row + 1) * half, :] = dot(pick, window).astype(bf16)


def pool(pixels):
    images, rows, width, chans = pixels.shape
    shape = struct((images, rows * width // 4, chans), bf16)
    return call(pool_body, "pool", [(LOAD, pixels)], [(VMEM, shape)])


def widen_body(arrive, g_ref, out_ref):
    arrive()
    rows, width, chans = out_ref.shape[1:]
    half = width // 2
    pixel = lax.broadcasted_iota(jnp.int32, (width, half), 0)
    place = lax.broadcasted_iota(jnp.int32, (width, half), 1)
    inside = (pixel >= 2 * place) & (pixel < 2 * place + 2)
    pick = jnp.where(inside, 0.25, 0.0).astype(bf16)
    for image in range(g_ref.shape[0]):
        for row in range(rows // 2):
            wide = dot(pick, g_ref[image, row * half : (row + 1) * half, :]).astype(bf16)
            out_ref[image, 2 * row] = wide
            out_ref[image, 2 * row + 1] = wide


def widen(grad, rows, width):
    images, spots, chans = grad.shape
    step = images // 4
    block = pl.BlockSpec((step, spots, chans), lambda i: (i, 0, 0))
    out = pl.BlockSpec((step, rows, width, chans), lambda i: (i, 0, 0, 0))
    return call(
        widen_body,
        "widen",
        [(block, grad)],
        [(out, struct((images, rows, width, chans), bf16))],
        grid=(4,),
    )


def conv_body(side, first, group, arrive, idx_ref, *refs):
    zh, zl = idx_ref[2], idx_ref[3]
    if first:
        xl, xa, xh, xd, wl, wo, ws, bl, bo, pre_ref, act_ref, xbuf, wbuf, acc, sems = refs
        chans = xl.shape[1]
        spots = xbuf.shape[0]
        begin = zh * (xl.shape[0] - spots)
        pairs = []
        for source, up, along in ((xl, zh, zl), (xa, zh, 1 - zl), (xh, 1 - zh, zl), (xd, 1 - zh, 1 - zl)):
            if source is xl:
                source = xl.at[at(begin, spots, side), :]
            pairs.append((source, xbuf.at[:, at((2 * up + along) * chans, chans, chans)]))
    else:
        xl, xa, wl, wo, ws, bl, bo, pre_ref, act_ref, xbuf, wbuf, acc, sems = refs
        chans = xl.shape[1] // 2
        spots = xbuf.shape[0]
        pairs = []
        for source, along in ((xl, zl), (xa, 1 - zl)):
            for up in range(2):
                pairs.append(
                    (
                        source.at[:, up * chans : (up + 1) * chans],
                        xbuf.at[:, at((2 * up + along) * chans, chans, chans)],
                    )
                )
    run_copies(slice_copies(group, idx_ref, wl, wo, ws, wbuf) + pairs, sems)
    arrive()
    acc[...] = jnp.zeros_like(acc)
    outs = 2 * wl.shape[2]
    block = spots // 2
    for x in range(3):
        weights = lanes([wbuf[u, 3 * y + x] for y in range(3) for u in range(2)])
        for begin in range(0, spots, block):
            values = xbuf[begin : begin + block, :]
            if first:
                values = gelu(values.astype(f32)).astype(bf16)
            product = dot(values, weights)
            for y in range(3):
                place = begin + side * (2 - y)
                acc[x, place : place + block, :] += product[:, y * outs : (y + 1) * outs]
    spot = lax.broadcasted_iota(jnp.int32, (block, outs), 0)
    column = lax.rem(spot, side)
    own, other = bl[...], bo[...]
    bias = lanes([jnp.where(zh == 0, own, other), jnp.where(zh == 0, other, own)])
    for begin in range(0, spots, block):
        place = begin + side
        left = pltpu.roll(acc[0, place : place + block, :], 1, 0)
        right = pltpu.roll(acc[2, place : place + block, :], block - 1, 0)
        pre = acc[1, place : place + block, :] + bias
        pre = pre + jnp.where(column > 0, left, 0.0)
        pre = pre + jnp.where(column < side - 1, right, 0.0)
        pre_ref[begin : begin + block, :] = pre
        act_ref[begin : begin + block, :] = gelu(pre).astype(bf16)


def conv(side, idx, sources, own, other, group, bias, bias_other, first=False):
    taps, depth, outs = own.shape
    spots = sources[1].shape[0]
    return call(
        functools.partial(conv_body, side, first, group),
        "conv",
        [(SMEM, idx)]
        + [(FAR, s) for s in sources]
        + [(FAR, own), (FAR, other[0]), (FAR, other[1])]
        + [(VMEM, bias.reshape(1, outs)), (VMEM, bias_other.reshape(1, outs))],
        [(VMEM, struct((spots, 2 * outs), f32)), (VMEM, struct((spots, 2 * outs), bf16))],
        [
            pltpu.VMEM((spots, depth), bf16),
            pltpu.VMEM((2, taps, depth, outs), bf16),
            pltpu.VMEM((3, spots + 2 * side, 2 * outs), f32),
            pltpu.SemaphoreType.DMA((2 * other[0].shape[0] + 5,)),
        ],
        spare=14 if first else 8,
    )


def spread_taps(side, grad, taps_ref):
    pixels, outs = grad.shape
    spot = lax.broadcasted_iota(jnp.int32, (pixels, outs), 0)
    column = lax.rem(spot, side)
    wide = grad.astype(f32)
    ahead = jnp.where(column < side - 1, pltpu.roll(wide, pixels - 1, 0), 0.0).astype(bf16)
    behind = jnp.where(column > 0, pltpu.roll(wide, 1, 0), 0.0).astype(bf16)
    edge = jnp.zeros((side, 3 * outs), bf16)
    taps_ref[:side, :] = edge
    taps_ref[side + pixels :, :] = edge
    taps_ref[side : side + pixels, :] = jnp.concatenate([ahead, grad, behind], axis=1)


def tap_block(side, taps_ref, begin, block):
    return lanes([taps_ref[at(begin + side * (2 - y), block, side), :] for y in range(3)])


def slope_body(side, arrive, idx_ref, keep_ref, recv_ref, pre_ref, mine_ref, theirs_ref, gp_ref):
    arrive()
    zh = idx_ref[2]
    half, outs = mine_ref.shape
    total = keep_ref[...] + recv_ref[...].astype(f32)
    gp_ref[...] = (total * gelu_slope(pre_ref[...])).astype(bf16)
    own = gp_ref[at(zh * halo * side, half, side), :]
    low, high = own[:, :outs], own[:, outs:]
    mine_ref[...] = jnp.where(zh == 0, low, high)
    theirs_ref[...] = jnp.where(zh == 0, high, low)


def slope_back(side, idx, keep, recv, pre, half):
    outs = pre.shape[1] // 2
    return call(
        functools.partial(slope_body, side),
        "slope_back",
        [(SMEM, idx), (LOAD, keep), (LOAD, recv), (LOAD, pre)],
        [
            (VMEM, struct((half, outs), bf16)),
            (VMEM, struct((half, outs), bf16)),
            (VMEM, struct(pre.shape, bf16)),
        ],
    )


def back_body(side, last, group, arrive, idx_ref, *refs):
    zh, zl = idx_ref[2], idx_ref[3]
    if last:
        grad_ref, x_ref, go_ref, far_ref, idk_ref, wl, wo, ws, po, ps = refs[:10]
        own_ref, give_ref, taps_ref, wbuf, idk_far, sems = refs[10:]
    else:
        keep_ref, recv_ref, pre_ref, wl, wo, ws, gp_ref, own_ref, give_ref, taps_ref, wbuf, sems = refs
    pairs = slice_copies(group, idx_ref, wl, wo, ws, wbuf)
    if last:
        pairs += flat_copies(18, idx_ref, po, ps, idk_far)
    copies = start_copies(pairs, sems)
    arrive()
    if last:
        grad = grad_ref[...]
    else:
        total = keep_ref[...].astype(f32) + recv_ref[...].astype(f32)
        grad = (total * gelu_slope(pre_ref[...])).astype(bf16)
        gp_ref[...] = grad
    spread_taps(side, grad, taps_ref)
    depth, outs = wl.shape[1:]
    pixels = own_ref.shape[-2]
    start = zh * halo * side
    for copy in copies:
        copy.wait()
    block = pixels // 2
    chans = depth // 4

    def rows(index):
        spot = at(index * chans, chans, chans)
        return lanes([wbuf[u, t, spot, :] for t in range(9) for u in range(2)])

    for target, along in ((give_ref, 1 - zl), (own_ref, zl)):
        if last:
            units = chans // idk_far.shape[2]
            for up in range(2):
                index = 2 * up + along
                weights = rows(index)
                near = idk_ref[at(index * chans, chans, chans), :]
                far = flat_rows(idk_far, index * units, units)
                for begin in range(0, pixels, block):
                    here = at(zh * pixels + begin, block, side)
                    part = dot(tap_block(side, taps_ref, start + begin, block), weights, NT)
                    x = x_ref[here, at(index * chans, chans, chans)]
                    part = part * gelu_slope(x.astype(f32))
                    part = part + dot(go_ref[here, :], near, NT)
                    part = part + dot(far_ref[at(start + begin, block, side), :], far, NT)
                    target[up, begin : begin + block, :] = part.astype(target.dtype)
        else:
            weights = jnp.concatenate([rows(along), rows(2 + along)], axis=0)
            for begin in range(0, pixels, block):
                part = dot(tap_block(side, taps_ref, begin, block), weights, NT)
                target[begin : begin + block, :] = part.astype(target.dtype)


def back(side, idx, sources, own, other, group, last=None):
    taps, depth, outs = own.shape
    spots = sources[0].shape[0]
    copies = 2 * other[0].shape[0] + 1
    extra = []
    scratch = []
    if last:
        full_x, go, go_far, idk, pieces, half = last
        chans = depth // 4
        shape = (2, half, chans)
        results = []
        extra = [(FAR, pieces[0]), (FAR, pieces[1])]
        sources = list(sources) + [full_x, go, go_far, idk]
        columns, size = idk.shape[1] // 128, pieces[0].shape[2]
        scratch = [pltpu.VMEM((columns, depth // size, size, 128), bf16)]
        copies += 2 * other[0].shape[0] * columns
    else:
        shape = (spots, depth // 2)
        results = [(VMEM, struct((spots, 2 * outs), bf16))]
    results += [(VMEM, struct(shape, f32)), (VMEM, struct(shape, bf16))]
    return call(
        functools.partial(back_body, side, bool(last), group),
        "back",
        [(SMEM, idx)]
        + [(LOAD, source) for source in sources]
        + [(FAR, own), (FAR, other[0]), (FAR, other[1])]
        + extra,
        results,
        [pltpu.VMEM((spots + 2 * side, 6 * outs), bf16), pltpu.VMEM((2, taps, depth, outs), bf16)]
        + scratch
        + [pltpu.SemaphoreType.DMA((copies,))],
        spare=14 if last else 10,
    )


def put_blocks(idx_ref, keep_ref, give_ref, part, tap, first_block, size, begin=0):
    chip, core = idx_ref[0], idx_ref[1]
    for b in range(0, part.shape[0] // size, 2):
        even = part[b * size : (b + 1) * size, :]
        odd = part[(b + 1) * size : (b + 2) * size, :]
        slot = chip ^ ((first_block + b) // 2)
        rows = slice(begin + tap * size, begin + (tap + 1) * size)
        keep_ref[slot, rows, :] = jnp.where(core == 0, even, odd).astype(bf16)
        give_ref[slot, rows, :] = jnp.where(core == 0, odd, even).astype(bf16)


def weight_body(side, half, flat, arrive, idx_ref, gp_ref, *refs):
    if flat:
        full_ref, go_ref, bias_ref = refs[:3]
        refs = refs[3:]
    xl, xa, keep_ref, give_ref, xbuf, taps_ref, sems = refs
    arrive()
    zh, zl = idx_ref[2], idx_ref[3]
    chans = xl.shape[1] // 2
    pairs = []
    for source, along in ((xl, zl), (xa, 1 - zl)):
        for up in range(2):
            pairs.append(
                (
                    source.at[:, up * chans : (up + 1) * chans],
                    xbuf.at[:, at((2 * up + along) * chans, chans, chans)],
                )
            )
    run_copies(pairs, sems)
    spots, wide = gp_ref.shape
    outs = wide // 2
    spot = lax.broadcasted_iota(jnp.int32, (spots, wide), 0) - zh * halo * side
    grad = jnp.where((spot >= 0) & (spot < half), gp_ref[...].astype(f32), 0.0)
    bias = jnp.sum(grad, axis=0, keepdims=True)
    spread_taps(side, grad.astype(bf16), taps_ref)
    blocks = 2 * keep_ref.shape[0]
    depth = xbuf.shape[1]
    size = depth // blocks
    for begin in range(0, depth, 256):
        values = xbuf[:, begin : begin + 256]
        for y in range(3):
            place = side * (2 - y)
            part = dot(values, taps_ref[place : place + spots, :], TN)
            for x in range(3):
                for u in range(2):
                    col = x * wide + u * outs
                    put_blocks(
                        idx_ref, keep_ref, give_ref, part[:, col : col + outs],
                        3 * y + x, begin // size, size, u * (9 * size + 16),
                    )
    for u in range(2):
        row = jnp.broadcast_to(bias[:, u * outs : (u + 1) * outs], (16, outs)).astype(bf16)
        for j in range(keep_ref.shape[0]):
            spot = slice(u * (9 * size + 16) + 9 * size, (u + 1) * (9 * size + 16))
            keep_ref[j, spot, :] = row
            give_ref[j, spot, :] = row
    if flat:
        first = 2 * (9 * size + 16)
        flat_pieces(1.0, idx_ref, full_ref, go_ref, bias_ref, keep_ref, give_ref, first)


def weight_grad(side, half, idx, grad, act, act_other, chips, flat=()):
    spots, wide = grad.shape
    outs = wide // 2
    depth = 2 * act.shape[1]
    rows = 2 * (9 * depth // (2 * chips) + 16)
    if flat:
        rows += flat_size(flat[0], flat[1], chips)
    return call(
        functools.partial(weight_body, side, half, bool(flat)),
        "weight_grad",
        [(SMEM, idx), (LOAD, grad)] + [(LOAD, a) for a in flat] + [(FAR, act), (FAR, act_other)],
        [(VMEM, struct((chips, rows, outs), bf16))] * 2,
        [
            pltpu.VMEM((spots, depth), bf16),
            pltpu.VMEM((spots + 2 * side, 3 * wide), bf16),
            pltpu.SemaphoreType.DMA((4,)),
        ],
        spare=10,
    )


def weight_one_body(side, arrive, idx_ref, mine_ref, theirs_ref, x_ref, *refs):
    act_ref, go_ref, out_bias_ref, keep_ref, give_ref, gp_ref, taps_ref = refs
    arrive()
    zh = idx_ref[2]
    half, outs = mine_ref.shape
    gp_ref[at(zh * half, half, side), :] = mine_ref[...]
    gp_ref[at((1 - zh) * half, half, side), :] = theirs_ref[...]
    grad = gp_ref[...]
    bias = jnp.sum(grad.astype(f32), axis=0, keepdims=True)
    spread_taps(side, grad, taps_ref)
    blocks = 2 * keep_ref.shape[0]
    spots, depth = x_ref.shape
    size = depth // blocks
    right = tap_block(side, taps_ref, 0, spots)
    for begin in range(0, depth, 256):
        part = dot(x_ref[:, begin : begin + 256], right, TN)
        for tap in range(9):
            put_blocks(
                idx_ref, keep_ref, give_ref, part[:, tap * outs : (tap + 1) * outs],
                tap, begin // size, size,
            )
    row = jnp.broadcast_to(bias, (16, outs)).astype(bf16)
    first = 9 * size + 16
    for j in range(keep_ref.shape[0]):
        keep_ref[j, 9 * size : first, :] = row
        give_ref[j, 9 * size : first, :] = row
    flat_pieces(post_gain, idx_ref, act_ref, go_ref, out_bias_ref, keep_ref, give_ref, first)


def weight_one_grad(side, idx, mine, theirs, act_zero, chips, flat):
    spots, depth = act_zero.shape
    outs = mine.shape[1]
    rows = 9 * depth // (2 * chips) + 16 + flat_size(flat[0], flat[1], chips)
    return call(
        functools.partial(weight_one_body, side),
        "weight_one_grad",
        [(SMEM, idx), (LOAD, mine), (LOAD, theirs), (LOAD, act_zero)]
        + [(LOAD, a) for a in flat],
        [(VMEM, struct((chips, rows, outs), bf16))] * 2,
        [
            pltpu.VMEM((spots, outs), bf16),
            pltpu.VMEM((spots + 2 * side, 3 * outs), bf16),
        ],
        spare=14,
    )


def pair_body(arrive, idx_ref, *refs):
    arrive()
    pairs, outs = refs[: -refs[0].shape[0]], refs[-refs[0].shape[0] :]
    for j, out in enumerate(outs):
        begin = 0
        for keep, recv in zip(pairs[0::2], pairs[1::2]):
            rows = keep.shape[1]
            total = keep[j].astype(f32) + recv[j].astype(f32)
            out[begin : begin + rows, :] = total.astype(bf16)
            begin += rows


def pair_sum(idx, *pairs):
    chips, _, wide = pairs[0].shape
    rows = sum(p.shape[1] for p in pairs[0::2])
    return call(
        pair_body,
        "pair_sum",
        [(SMEM, idx)] + [(LOAD, p) for p in pairs],
        [(VMEM, struct((rows, wide), bf16))] * chips,
    )


def chip_body(parts, arrive, idx_ref, *refs):
    arrive()
    parts, targets = refs[:parts], refs[parts:]
    zh = idx_ref[2]
    rows = targets[0].shape[0]
    for target, begin in zip(targets, (zh * rows, (1 - zh) * rows, 2 * rows)):
        spot = at(begin, target.shape[0], 16)
        total = parts[0][spot, :].astype(f32)
        for part in parts[1:]:
            total = total + part[spot, :].astype(f32)
        target[...] = total.astype(target.dtype)


def chip_sum(idx, parts, rows):
    wide = parts[0].shape[1]
    extra = parts[0].shape[0] - 2 * rows
    results = [(VMEM, struct((rows, wide), f32)), (VMEM, struct((rows, wide), bf16))]
    if extra:
        results.append((VMEM, struct((extra, wide), bf16)))
    return call(
        functools.partial(chip_body, len(parts)),
        "chip_sum",
        [(SMEM, idx)] + [(LOAD, p) for p in parts],
        results,
    )


def final_body(depth, arrive, idx_ref, own_ref, sib_ref, grad_ref, bias_ref, *flat):
    arrive()
    chip, core = idx_ref[0], idx_ref[1]
    chips = own_ref.shape[0]
    size = depth // (2 * chips)
    bias_ref[...] = own_ref[0, 9 * size : 9 * size + 1, :].astype(f32)
    for j in range(chips):
        for source, owner in ((own_ref, core), (sib_ref, 1 - core)):
            spot = at((2 * (chip ^ j) + owner) * size, size, size)
            for tap in range(9):
                grad_ref[tap, spot, :] = source[j, tap * size : (tap + 1) * size, :].astype(f32)
    if flat:
        flat_ref, flat_bias_ref = flat
        first = 9 * size + 16
        wide = own_ref.shape[2]
        columns = flat_ref.shape[1] // wide
        size = flat_ref.shape[0] // (2 * chips)
        for c in range(columns):
            row = first + columns * size + c
            flat_bias_ref[:, c * wide : (c + 1) * wide] = own_ref[0, row : row + 1, :].astype(f32)
        for j in range(chips):
            for source, owner in ((own_ref, core), (sib_ref, 1 - core)):
                spot = at((2 * (chip ^ j) + owner) * size, size, size)
                for c in range(columns):
                    row = first + c * size
                    piece = source[j, row : row + size, :].astype(f32)
                    flat_ref[spot, c * wide : (c + 1) * wide] = piece


def final_grads(idx, own, sib, depth, flat_shape=None):
    outs = own.shape[2]
    results = [(VMEM, struct((9, depth, outs), f32)), (VMEM, struct((1, outs), f32))]
    if flat_shape:
        results += [(VMEM, struct(flat_shape, f32)), (VMEM, struct((1, flat_shape[1]), f32))]
    return call(
        functools.partial(final_body, depth),
        "final_grads",
        [(SMEM, idx), (LOAD, own), (LOAD, sib)],
        results,
    )


def flat_pieces(gain, idx_ref, x_ref, go_ref, bias_ref, keep_ref, give_ref, first):
    chip, core = idx_ref[0], idx_ref[1]
    chips, _, wide = keep_ref.shape
    columns = go_ref.shape[1] // wide
    size = x_ref.shape[1] // (2 * chips)
    bias = jnp.concatenate(
        [bias_ref[:, c * wide : (c + 1) * wide] for c in range(columns)]
        + [jnp.zeros((16 - columns, wide), f32)],
        axis=0,
    ).astype(bf16)
    for j in range(chips):
        keep_ref[j, first + columns * size :, :] = bias
        give_ref[j, first + columns * size :, :] = bias
    for begin in range(0, x_ref.shape[1], 256):
        part = gain * dot(x_ref[:, begin : begin + 256], go_ref[...], TN)
        for b in range(0, 256 // size, 2):
            slot = chip ^ ((begin // size + b) // 2)
            for c in range(columns):
                even = part[b * size : (b + 1) * size, c * wide : (c + 1) * wide]
                odd = part[(b + 1) * size : (b + 2) * size, c * wide : (c + 1) * wide]
                spot = slice(first + c * size, first + (c + 1) * size)
                keep_ref[slot, spot, :] = jnp.where(core == 0, even, odd).astype(bf16)
                give_ref[slot, spot, :] = jnp.where(core == 0, odd, even).astype(bf16)


def flat_size(x, go, chips):
    return (go.shape[1] // 128) * (x.shape[1] // (2 * chips)) + 16


def start_body(side, arrive, idx_ref, valid_ref, cot_ref, far_ref, outk_ref, po, ps, *refs):
    go_ref, go_far_ref, bias_ref, own_ref, give_ref, outk_far, sems = refs
    zh, zl = idx_ref[2], idx_ref[3]
    first = po.shape[1] - outk_far.shape[0] * (outk_far.shape[1] // (2 * po.shape[0]))
    copies = start_copies(flat_copies(first, idx_ref, po, ps, outk_far), sems)
    arrive()
    masked = cot_ref[...].astype(f32) * valid_ref[0]
    go_ref[...] = masked.astype(bf16)
    bias_ref[...] = jnp.sum(masked, axis=0, keepdims=True)
    go_far_ref[...] = (far_ref[...].astype(f32) * valid_ref[0]).astype(bf16)
    for copy in copies:
        copy.wait()
    chans = outk_ref.shape[0] // 4
    units = chans // outk_far.shape[2]
    spots = far_ref.shape[0]
    start = zh * (cot_ref.shape[0] - spots)
    block = spots // 2
    for target, along in ((give_ref, 1 - zl), (own_ref, zl)):
        near, far = [], []
        for up in range(2):
            index = 2 * up + along
            near.append(outk_ref[at(index * chans, chans, chans), :])
            far.append(flat_rows(outk_far, index * units, units))
        near = jnp.concatenate(near, axis=0)
        far = jnp.concatenate(far, axis=0)
        for begin in range(0, spots, block):
            part = dot(go_ref[at(start + begin, block, side), :], near, NT)
            part = part + dot(go_far_ref[begin : begin + block, :], far, NT)
            target[begin : begin + block, :] = (post_gain * part).astype(target.dtype)


def start_back(side, idx, valid, cot, cot_far, outk, pieces):
    spots, outs = cot_far.shape
    depth = outk.shape[0]
    columns, size = outs // 128, pieces[0].shape[2]
    shape = (spots, depth // 2)
    return call(
        functools.partial(start_body, side),
        "start_back",
        [(SMEM, idx), (SMEM, valid), (LOAD, cot), (LOAD, cot_far), (LOAD, outk)]
        + [(FAR, pieces[0]), (FAR, pieces[1])],
        [
            (VMEM, struct(cot.shape, bf16)),
            (VMEM, struct(cot_far.shape, bf16)),
            (VMEM, struct((1, outs), f32)),
            (VMEM, struct(shape, f32)),
            (VMEM, struct(shape, bf16)),
        ],
        [
            pltpu.VMEM((columns, depth // size, size, 128), bf16),
            pltpu.SemaphoreType.DMA((2 * pieces[0].shape[0] * columns,)),
        ],
        spare=8,
    )


def slots_body(arrive, idx_ref, own_ref, recv_ref, keep_ref, give_ref):
    arrive()
    zh = idx_ref[2]
    for target, slot in ((give_ref, 1 - zh), (keep_ref, zh)):
        total = own_ref[slot] + recv_ref[slot].astype(f32)
        target[...] = total.astype(bf16)


def slots_sum(idx, own, recv):
    shape = struct(own.shape[1:], bf16)
    return call(
        slots_body,
        "slots_sum",
        [(SMEM, idx), (LOAD, own), (LOAD, recv)],
        [(VMEM, shape), (VMEM, shape)],
    )


def input_body(arrive, idx_ref, keep_ref, recv_ref, out_ref):
    arrive()
    zh = idx_ref[2]
    half = keep_ref.shape[0]
    out_ref[at(zh * half, half, half), :] = keep_ref[...]
    out_ref[at((1 - zh) * half, half, half), :] = recv_ref[...]


def input_grad(idx, keep, recv):
    half, chans = keep.shape
    return call(
        input_body,
        "input_grad",
        [(SMEM, idx), (LOAD, keep), (LOAD, recv)],
        [(VMEM, struct((2 * half, chans), bf16))],
    )


def whole_body(side, arrive, idx_ref, xl, xa, xh, xd, rh, rl, x_ref, act_ref, sems):
    arrive()
    zh, zl = idx_ref[2], idx_ref[3]
    chans = xl.shape[1]
    spots = xa.shape[0]
    rest = xl.shape[0] - spots
    window, outside = at(zh * rest, spots, side), at((1 - zh) * spots, rest, side)

    def cols(up, along):
        return at((2 * up + along) * chans, chans, chans)

    run_copies(
        [
            (xl, x_ref.at[:, cols(zh, zl)]),
            (xa, x_ref.at[window, cols(zh, 1 - zl)]),
            (xh, x_ref.at[window, cols(1 - zh, zl)]),
            (xd, x_ref.at[window, cols(1 - zh, 1 - zl)]),
            (rl.at[0], x_ref.at[outside, cols(zh, 1 - zl)]),
            (rh, x_ref.at[outside, cols(1 - zh, zl)]),
            (rl.at[1], x_ref.at[outside, cols(1 - zh, 1 - zl)]),
        ],
        sems,
    )
    block = x_ref.shape[0] // 8
    for begin in range(0, x_ref.shape[0], block):
        rows = slice(begin, begin + block)
        act_ref[rows, :] = gelu(x_ref[rows, :].astype(f32)).astype(bf16)


def whole_input(side, idx, *parts):
    spots, chans = parts[0].shape
    return call(
        functools.partial(whole_body, side),
        "whole_input",
        [(SMEM, idx)] + [(FAR, p) for p in parts],
        [(VMEM, struct((spots, 4 * chans), bf16))] * 2,
        [pltpu.SemaphoreType.DMA((7,))],
    )


def join_body(arrive, idx_ref, own, recv, far_own, far_recv, out, sems):
    arrive()
    zh, zl = idx_ref[2], idx_ref[3]
    half = own.shape[0]
    chans = own.shape[1] // 2
    pairs = []
    for source, up, along in ((own, zh, zl), (recv, zh, 1 - zl), (far_own, 1 - zh, zl), (far_recv, 1 - zh, 1 - zl)):
        for slot in range(2):
            spot = at((2 * slot + along) * chans, chans, chans)
            target = out.at[at(up * half, half, half), spot]
            pairs.append((source.at[:, slot * chans : (slot + 1) * chans], target))
    run_copies(pairs, sems)


def join(idx, *parts):
    half, wide = parts[0].shape
    return call(
        join_body,
        "join",
        [(SMEM, idx)] + [(FAR, p) for p in parts],
        [(VMEM, struct((2 * half, 2 * wide), bf16))],
        [pltpu.SemaphoreType.DMA((8,))],
    )


def finish_body(arrive, idx_ref, valid_ref, x_ref, act_ref, idk_ref, outk_ref, ib_ref, out_ref):
    arrive()
    block = x_ref.shape[0] // 4
    for begin in range(0, x_ref.shape[0], block):
        rows = slice(begin, begin + block)
        identity = dot(x_ref[rows, :], idk_ref[...]) + ib_ref[...]
        branch = dot(act_ref[rows, :], outk_ref[...])
        out_ref[rows, :] = ((identity + post_gain * branch) * valid_ref[0]).astype(bf16)


def finish(idx, valid, x, act, idk, outk, ib):
    outs = idk.shape[1]
    return call(
        finish_body,
        "finish",
        [(SMEM, idx), (SMEM, valid), (LOAD, x), (LOAD, act), (LOAD, idk), (LOAD, outk)]
        + [(VMEM, ib.reshape(1, outs))],
        [(VMEM, struct((x.shape[0], outs), bf16))],
        spare=8,
    )


def flip(value, axis):
    return lax.ppermute(value, axis, [(0, 1), (1, 0)])


def hop(value, j, chips):
    return lax.ppermute(value, "chip", [(i, i ^ j) for i in range(chips)])


def gather_chips(value, chips):
    return [value] + [hop(value, j, chips) for j in range(1, chips)]


def swap(pieces, axis):
    return lax.all_to_all(pieces, axis, split_axis=0, concat_axis=0, tiled=True)


def after(value, other):
    return lax.optimization_barrier((value, other))[0]


def rows_of(value, start, size):
    return lax.dynamic_slice_in_dim(value, start, size, 0)


def local(
    pixels,
    counts,
    kernel_one,
    bias_one,
    kernel_two,
    bias_two,
    kernel_three,
    bias_three,
    out_kernel,
    identity_kernel,
    identity_bias,
    cotangent,
):
    images, rows, width, chans = pixels.shape
    side = width // 2
    spots = side * side
    half = spots // 2
    window = half + halo * side
    outs = cotangent.shape[3]
    chips = lax.axis_size("chip")
    chip, core, zh, zl = [lax.axis_index(a) for a in ("chip", "core", "zh", "zl")]
    idx = jnp.stack([chip, core, zh, zl]).astype(jnp.int32)
    taps = lambda kernel: kernel.reshape((9,) + kernel.shape[2:])
    one, two, three = taps(kernel_one), taps(kernel_two), taps(kernel_three)

    own_count = lax.dynamic_index_in_dim(counts, 2 * chip + core, 0, keepdims=True)
    valid = (own_count > 0).astype(f32)

    place = 2 * chip + core

    def units_of(kernel, size):
        if kernel.ndim == 3:
            block = kernel.shape[1] // (2 * chips)
            return lax.dynamic_slice_in_dim(kernel, place * block, block, 1)
        block = kernel.shape[0] // (2 * chips)
        block = lax.dynamic_slice_in_dim(kernel, place * block, block, 0)
        block = block.reshape(-1, size, block.shape[1] // 128, 128)
        return block.transpose(2, 0, 1, 3).reshape(-1, size, 128)

    def around(piece, *others):
        own = jnp.stack(after(gather_chips(piece, chips), others))
        return own, flip(own, "core")

    last = [idx]

    def turn(*others):
        return after(idx, (last[0],) + others)

    def ran(results):
        last[0] = results[-1] if isinstance(results, (list, tuple)) else results
        return results

    deep = two.shape[1]
    size = deep // (2 * chips)
    first_piece = units_of(one, size)
    bias_other = flip(after(jnp.stack([bias_one, bias_two, bias_three]), first_piece), "zh")
    first_piece = flip(first_piece, "zh")
    both_piece = jnp.concatenate(
        [units_of(kernel, size) for kernel in (two, three, identity_kernel, out_kernel)]
    )
    pooled = ran(pool(pixels))
    cot = cotangent.reshape(spots, outs)
    begin = zh * (spots - window)
    begin_other = (1 - zh) * (spots - window)
    cot_rows = rows_of(cot, begin_other, window)

    xl = swap(after(pooled, (first_piece, bias_other, both_piece, cot_rows)), DP).reshape(spots, chans)
    both_piece = flip(after(both_piece, first_piece), "zh")
    xa = flip(rows_of(xl, begin, window), "zl")
    xh = flip(rows_of(xl, begin_other, window), "zh")
    one_other = around(after(first_piece, xa))
    xd = flip(after(xh, one_other[0]), "zl")
    both_other = around(after(both_piece, one_other[0]), xh)
    cot_far = flip(after(cot_rows, xh), "zh")

    pre_one, act_one = ran(
        conv(side, turn(both_other[0], xa), (xl, xa, xh, xd), one, one_other, 0, bias_one, bias_other[0], True)
    )
    act_one_other = flip(act_one, "zl")
    pre_two, act_two = ran(
        conv(side, turn(), (act_one, act_one_other), two, both_other, 0, bias_two, bias_other[1])
    )
    act_two_other = flip(act_two, "zl")
    go, go_far, identity_bias_grad, ga_own, ga_give = ran(
        start_back(side, turn(), valid, cot, cot_far, out_kernel, both_other)
    )
    ga_recv = flip(ga_give, "zl")
    rest = spots - window
    rest_own = rows_of(xl, (1 - zh) * window, rest)
    rest_high = flip(after(rows_of(xl, zh * window, rest), go), "zh")
    pre_three, act_three = ran(
        conv(side, turn(), (act_two, act_two_other), three, both_other, 1, bias_three, bias_other[2])
    )
    own_rows = rows_of(act_three, zh * halo * side, half)
    near_rows = flip(own_rows, "zl")

    gp_three, ga_own, ga_give = ran(
        back(side, turn(), (ga_own, ga_recv, pre_three), three, both_other, 1)
    )
    ga_recv = flip(ga_give, "zl")
    rest_low = flip(after(jnp.stack([rest_own, rest_high]), gp_three), "zl")
    far_rows = flip(after(own_rows, gp_three), "zh")
    full_x, act_zero = ran(whole_input(side, turn(), xl, xa, xh, xd, rest_high, rest_low))
    keep_three, give_three = ran(
        weight_grad(
            side, half, turn(), gp_three, act_two, act_two_other, chips, (full_x, go, identity_bias_grad)
        )
    )
    recv_three = flip(give_three, "core")
    gp_two, ga_own, ga_give = ran(
        back(side, turn(near_rows), (ga_own, ga_recv, pre_two), two, both_other, 0)
    )
    ga_recv = flip(ga_give, "zl")
    parts_three = ran(pair_sum(turn(), keep_three, recv_three))
    parts_three = [parts_three[0]] + [hop(parts_three[j], j, chips) for j in range(1, chips)]
    keep_two, give_two = ran(weight_grad(side, half, turn(), gp_two, act_one, act_one_other, chips))
    recv_two = flip(give_two, "core")
    far_near_rows = flip(far_rows, "zl")

    gp_mine, gp_theirs, gp_one = ran(slope_back(side, turn(), ga_own, ga_recv, pre_one, half))
    gp_theirs = flip(gp_theirs, "zh")
    gx_own, gx_give = ran(
        back(
            side, turn(), (gp_one,), one, one_other, 0,
            (full_x, go, go_far, identity_kernel, both_other, half),
        )
    )
    gx_recv = flip(gx_give, "zl")
    parts_two = ran(pair_sum(turn(), keep_two, recv_two))
    parts_two = [parts_two[0]] + [hop(parts_two[j], j, chips) for j in range(1, chips)]
    full_three = ran(join(turn(), own_rows, near_rows, far_rows, far_near_rows))

    keep_one, give_one = ran(
        weight_one_grad(
            side, turn(), gp_mine, gp_theirs, act_zero, chips, (full_three, go, identity_bias_grad)
        )
    )
    recv_one = flip(give_one, "core")
    slot_rows = 9 * size + 16
    keep_three, give_three, id_rows = ran(chip_sum(turn(), parts_three, slot_rows))
    recv_three = flip(give_three, "zh")
    parts_one = ran(pair_sum(turn(), keep_one, recv_one))
    parts_one = [parts_one[0]] + [hop(parts_one[j], j, chips) for j in range(1, chips)]
    gx_keep, gx_give = ran(slots_sum(turn(), gx_own, gx_recv))
    gx_recv = flip(gx_give, "zh")
    keep_two, give_two = ran(chip_sum(turn(), parts_two, slot_rows))
    recv_two = flip(give_two, "zh")

    def spread(total):
        total = jnp.stack(gather_chips(total, chips))
        return total, flip(total, "core")

    def both(keep, recv):
        return (keep + recv.astype(f32)).astype(bf16)

    block_out = ran(finish(turn(), valid, full_x, full_three, identity_kernel, out_kernel, identity_bias))
    gx = ran(input_grad(turn(), gx_keep, gx_recv))
    gx = swap(gx.reshape(images, rows * width // 4, chans), DP)
    all_three = spread(jnp.concatenate([both(keep_three, recv_three), id_rows]))
    total = parts_one[0].astype(f32)
    for part in parts_one[1:]:
        total = total + part.astype(f32)
    all_one = spread(total.astype(bf16))
    all_two = spread(both(keep_two, recv_two))
    kernel_three_grad, bias_three_grad, identity_kernel_grad, identity_bias_grad = ran(
        final_grads(turn(), *all_three, deep, identity_kernel.shape)
    )
    pixels_grad = widen(gx, rows, width)
    kernel_two_grad, bias_two_grad = ran(final_grads(turn(), *all_two, deep))
    kernel_one_grad, bias_one_grad, out_kernel_grad, _ = ran(
        final_grads(turn(), *all_one, one.shape[1], out_kernel.shape)
    )

    return (
        block_out.reshape(cotangent.shape),
        pixels_grad,
        kernel_one_grad.reshape(kernel_one.shape),
        bias_one_grad[0],
        kernel_two_grad.reshape(kernel_two.shape),
        bias_two_grad[0],
        kernel_three_grad.reshape(kernel_three.shape),
        bias_three_grad[0],
        out_kernel_grad,
        identity_kernel_grad,
        identity_bias_grad[0],
    )


def solution(mesh):
    members = mesh.devices.size // mesh.shape["mp"]
    fine = Mesh(
        mesh.devices.reshape(members // 2, 2, 2, mesh.shape["mp"] // 2),
        ("chip", "core", "zh", "zl"),
    )
    return jax.shard_map(
        local,
        mesh=fine,
        in_specs=(
            P(None, DP, None, MP),
            P(),
            P(None, None, None, MP),
            P(MP),
            P(None, None, None, MP),
            P(MP),
            P(None, None, None, MP),
            P(MP),
            P(None, MP),
            P(None, MP),
            P(MP),
            P(DP, None, None, MP),
        ),
        out_specs=(
            P(DP, None, None, MP),
            P(None, DP, None, MP),
            P(None, None, None, MP),
            P(MP),
            P(None, None, None, MP),
            P(MP),
            P(None, None, None, MP),
            P(MP),
            P(None, MP),
            P(None, MP),
            P(MP),
        ),
        check_vma=False,
    )
```

```python
import functools
import math

import jax
import jax.numpy as jnp
from jax import lax
from jax.experimental import pallas as pl
from jax.experimental.pallas import tpu as pltpu
from jax.sharding import Mesh
from jax.sharding import PartitionSpec as P


post_gain = 0.015625
slope = 0.7978845608028654
cubic = 0.044715
halo = 6
bf16 = jnp.bfloat16
f32 = jnp.float32
NT = (((1,), (1,)), ((), ()))
TN = (((0,), (0,)), ((), ()))
NN = (((1,), (0,)), ((), ()))
DP = ("chip", "core")
MP = ("zh", "zl")


def dot(left, right, dims=NN):
    return lax.dot_general(left, right, dims, preferred_element_type=f32)


def gelu(value):
    inner = jnp.tanh(slope * (value + cubic * value * value * value))
    return 0.5 * value * (1.0 + inner)


def gelu_slope(value):
    square = value * value
    inner = jnp.tanh(slope * value * (1.0 + cubic * square))
    climb = slope * (1.0 + 3.0 * cubic * square)
    return 0.5 * (1.0 + inner) + 0.5 * value * (1.0 - inner * inner) * climb


def struct(shape, kind):
    return jax.ShapeDtypeStruct(shape, kind)


def lanes(blocks):
    return blocks[0] if len(blocks) == 1 else jnp.concatenate(blocks, axis=1)


def step_bits(core, chips):
    bits = [1 << n for n in range(chips.bit_length() - 1)]
    for n in range(0, len(bits) - 1, 2) if core else ():
        bits[n], bits[n + 1] = bits[n + 1], bits[n]
    return bits


def mask_of(i, core, chips):
    masks = []
    for which in range(2):
        bits = step_bits(which, chips)
        masks.append(sum(bit for n, bit in enumerate(bits) if i >> (len(bits) - 1 - n) & 1))
    return jnp.where(core == 0, masks[0], masks[1])


def slot_of(mask, core, chips):
    slots = []
    for which in range(2):
        bits = step_bits(which, chips)
        slot = 0
        for n, bit in enumerate(bits):
            slot = slot + ((mask >> (bit.bit_length() - 1)) & 1) * (1 << (len(bits) - 1 - n))
        slots.append(slot)
    return jnp.where(core == 0, slots[0], slots[1])


VMEM = pl.BlockSpec(memory_space=pltpu.VMEM)
SMEM = pl.BlockSpec(memory_space=pltpu.SMEM)
FAR = pl.BlockSpec(memory_space=pl.ANY)
LOAD = "load"


def size_of(array):
    return math.prod(array.shape) * jnp.dtype(array.dtype).itemsize


def call(body, name, ins, outs, scratch=(), spare=6, **more):
    loads = [i for i, (space, _) in enumerate(ins) if space is LOAD]
    spaces = [FAR if space is LOAD else space for space, _ in ins]
    arrays = [array for _, array in ins]
    out_specs = [space for space, _ in outs]
    out_shape = [shape for _, shape in outs]
    held = [arrays[i] for i in loads]
    buffers = [pltpu.VMEM(array.shape, array.dtype) for array in held]
    sems = [pltpu.SemaphoreType.DMA((len(held),))] if held else []
    vmem = sum(size_of(array) for array in held)
    vmem += sum(size_of(a) for space, a in list(ins) + list(outs) if space is VMEM)
    vmem += sum(size_of(b) for b in scratch if b.memory_space == pltpu.VMEM)
    moved = sum(size_of(a) for a in arrays + out_shape)

    def wrapped(*refs):
        inputs = list(refs[: len(ins)])
        outputs = refs[len(ins) : len(ins) + len(outs)]
        rest = refs[len(ins) + len(outs) :]
        kept, tail = rest[: len(held)], rest[len(held) :]
        copies = []
        if held:
            sem, tail = tail[0], tail[1:]
            copies = [
                pltpu.make_async_copy(inputs[i], kept[n], sem.at[n]) for n, i in enumerate(loads)
            ]
        for copy in copies:
            copy.start()
        for n, i in enumerate(loads):
            inputs[i] = kept[n]

        def arrive():
            for copy in copies:
                copy.wait()

        body(arrive, *inputs, *outputs, *tail)

    single = len(outs) == 1
    return pl.pallas_call(
        wrapped,
        in_specs=spaces,
        out_specs=out_specs[0] if single else out_specs,
        out_shape=out_shape[0] if single else out_shape,
        scratch_shapes=buffers + sems + list(scratch),
        compiler_params=pltpu.CompilerParams(vmem_limit_bytes=vmem + (spare << 20)),
        cost_estimate=pl.CostEstimate(flops=0, bytes_accessed=moved, transcendentals=0),
        name=name,
        **more,
    )(*arrays)


def run_copies(pairs, sems):
    for copy in start_copies(pairs, sems):
        copy.wait()


def slice_copies(group, idx_ref, own, blocks, sibling, wbuf):
    chip, core, zh = idx_ref[0], idx_ref[1], idx_ref[2]
    size = blocks.shape[-2]
    pairs = [(own, wbuf.at[zh])]
    for j in range(blocks.shape[0]):
        for source, owner in ((blocks, core), (sibling, 1 - core)):
            home = chip ^ mask_of(j, owner, blocks.shape[0])
            spot = at((2 * home + owner) * size, size, size)
            pairs.append((source.at[j, 9 * group : 9 * group + 9], wbuf.at[1 - zh, :, spot, :]))
    return pairs


def flat_copies(first, idx_ref, blocks, sibling, buffer):
    chip, core = idx_ref[0], idx_ref[1]
    columns, units = buffer.shape[:2]
    chips = blocks.shape[0]
    count = units // (2 * chips)
    pairs = []
    for j in range(chips):
        for source, owner in ((blocks, core), (sibling, 1 - core)):
            home = chip ^ mask_of(j, owner, chips)
            spot = pl.ds((2 * home + owner) * count, count)
            for c in range(columns):
                begin = first + c * count
                pairs.append((source.at[j, begin : begin + count], buffer.at[c, spot]))
    return pairs


def start_copies(pairs, sems):
    copies = [pltpu.make_async_copy(a, b, sems.at[i]) for i, (a, b) in enumerate(pairs)]
    for copy in copies:
        copy.start()
    return copies


def flat_rows(buffer, begin, count):
    columns, _, size, wide = buffer.shape
    return lanes([buffer[c, pl.ds(begin, count)].reshape(count * size, wide) for c in range(columns)])


def halves(spots, side):
    first = (spots // side + 1) // 2 * side
    return ((0, first), (first, spots - first))


def columns_of(size, wide, side):
    return lax.rem(lax.broadcasted_iota(jnp.int32, (size, wide), 0), side)


def at(start, size, unit):
    return pl.ds(pl.multiple_of(start, unit), size)


def pool_body(arrive, x_ref, out_ref):
    arrive()
    rows, width, chans = x_ref.shape[1:]
    half = width // 2
    pixel = lax.broadcasted_iota(jnp.int32, (half, 2 * width), 1)
    place = lax.broadcasted_iota(jnp.int32, (half, 2 * width), 0)
    inside = (lax.rem(pixel, width) >= 2 * place) & (lax.rem(pixel, width) < 2 * place + 2)
    pick = jnp.where(inside, 0.25, 0.0).astype(bf16)
    for image in range(x_ref.shape[0]):
        for row in range(rows // 2):
            window = x_ref[image, 2 * row : 2 * row + 2].reshape(2 * width, chans)
            out_ref[image, row * half : (row + 1) * half, :] = dot(pick, window).astype(bf16)


def pool(pixels):
    images, rows, width, chans = pixels.shape
    shape = struct((images, rows * width // 4, chans), bf16)
    return call(pool_body, "pool", [(LOAD, pixels)], [(VMEM, shape)])


def widen_body(arrive, g_ref, out_ref):
    arrive()
    rows, width, chans = out_ref.shape[1:]
    half = width // 2
    pixel = lax.broadcasted_iota(jnp.int32, (width, half), 0)
    place = lax.broadcasted_iota(jnp.int32, (width, half), 1)
    inside = (pixel >= 2 * place) & (pixel < 2 * place + 2)
    pick = jnp.where(inside, 0.25, 0.0).astype(bf16)
    for image in range(g_ref.shape[0]):
        for row in range(rows // 2):
            wide = dot(pick, g_ref[image, row * half : (row + 1) * half, :]).astype(bf16)
            out_ref[image, 2 * row] = wide
            out_ref[image, 2 * row + 1] = wide


def widen(grad, rows, width):
    images, spots, chans = grad.shape
    step = images // 4
    block = pl.BlockSpec((step, spots, chans), lambda i: (i, 0, 0))
    out = pl.BlockSpec((step, rows, width, chans), lambda i: (i, 0, 0, 0))
    return call(
        widen_body,
        "widen",
        [(block, grad)],
        [(out, struct((images, rows, width, chans), bf16))],
        grid=(4,),
    )


def conv_body(side, first, group, arrive, idx_ref, *refs):
    zh, zl = idx_ref[2], idx_ref[3]
    if first:
        xl, xa, xh, xd, wl, wo, ws, bl, bo, pre_ref, act_ref, xbuf, wbuf, acc, sems = refs
        chans = xl.shape[1]
        spots = xbuf.shape[0]
        begin = zh * (xl.shape[0] - spots)
        pairs = []
        for source, up, along in ((xl, zh, zl), (xa, zh, 1 - zl), (xh, 1 - zh, zl), (xd, 1 - zh, 1 - zl)):
            if source is xl:
                source = xl.at[at(begin, spots, side), :]
            pairs.append((source, xbuf.at[:, at((2 * up + along) * chans, chans, chans)]))
    else:
        xl, xa, wl, wo, ws, bl, bo, pre_ref, act_ref, xbuf, wbuf, acc, sems = refs
        chans = xl.shape[1] // 2
        spots = xbuf.shape[0]
        pairs = []
        for source, along in ((xl, zl), (xa, 1 - zl)):
            for up in range(2):
                pairs.append(
                    (
                        source.at[:, up * chans : (up + 1) * chans],
                        xbuf.at[:, at((2 * up + along) * chans, chans, chans)],
                    )
                )
    run_copies(slice_copies(group, idx_ref, wl, wo, ws, wbuf) + pairs, sems)
    arrive()
    acc[...] = jnp.zeros_like(acc)
    outs = 2 * wl.shape[2]
    for x in range(3):
        weights = lanes([wbuf[u, 3 * y + x] for y in range(3) for u in range(2)])
        for begin, block in halves(spots, side):
            values = xbuf[begin : begin + block, :]
            if first:
                values = gelu(values.astype(f32)).astype(bf16)
            product = dot(values, weights)
            for y in range(3):
                place = begin + side * (2 - y)
                acc[x, place : place + block, :] += product[:, y * outs : (y + 1) * outs]
    own, other = bl[...], bo[...]
    bias = lanes([jnp.where(zh == 0, own, other), jnp.where(zh == 0, other, own)])
    for begin, block in halves(act_ref.shape[0], side):
        column = columns_of(block, outs, side)
        spot = at(begin + side + zh * side, block, side)
        left = pltpu.roll(acc[0, spot, :], 1, 0)
        right = pltpu.roll(acc[2, spot, :], block - 1, 0)
        pre = acc[1, spot, :] + bias
        pre = pre + jnp.where(column > 0, left, 0.0)
        pre = pre + jnp.where(column < side - 1, right, 0.0)
        pre_ref[begin : begin + block, :] = pre
        act_ref[begin : begin + block, :] = gelu(pre).astype(bf16)


def conv(side, idx, sources, own, other, group, bias, bias_other, first=False):
    taps, depth, outs = own.shape
    spots = sources[1].shape[0]
    rows = spots - side
    return call(
        functools.partial(conv_body, side, first, group),
        "conv",
        [(SMEM, idx)]
        + [(FAR, s) for s in sources]
        + [(FAR, own), (FAR, other[0]), (FAR, other[1])]
        + [(VMEM, bias.reshape(1, outs)), (VMEM, bias_other.reshape(1, outs))],
        [(VMEM, struct((rows, 2 * outs), f32)), (VMEM, struct((rows, 2 * outs), bf16))],
        [
            pltpu.VMEM((spots, depth), bf16),
            pltpu.VMEM((2, taps, depth, outs), bf16),
            pltpu.VMEM((3, spots + 2 * side, 2 * outs), f32),
            pltpu.SemaphoreType.DMA((2 * other[0].shape[0] + 5,)),
        ],
        spare=14 if first else 8,
    )


def spread_taps(side, grad, taps_ref):
    pixels, outs = grad.shape
    column = columns_of(pixels, outs, side)
    wide = grad.astype(f32)
    ahead = jnp.where(column < side - 1, pltpu.roll(wide, pixels - 1, 0), 0.0).astype(bf16)
    behind = jnp.where(column > 0, pltpu.roll(wide, 1, 0), 0.0).astype(bf16)
    edge = jnp.zeros((side, 3 * outs), bf16)
    taps_ref[:side, :] = edge
    taps_ref[side + pixels :, :] = edge
    taps_ref[side : side + pixels, :] = jnp.concatenate([ahead, grad, behind], axis=1)


def tap_block(side, taps_ref, begin, block):
    return lanes([taps_ref[at(begin + side * (2 - y), block, side), :] for y in range(3)])


def slope_body(side, arrive, idx_ref, keep_ref, recv_ref, pre_ref, mine_ref, theirs_ref, gp_ref):
    arrive()
    zh = idx_ref[2]
    half, outs = mine_ref.shape
    total = keep_ref[...] + recv_ref[...].astype(f32)
    spots = keep_ref.shape[0]
    pre = pre_ref[at(zh * (pre_ref.shape[0] - spots), spots, side), :]
    gp_ref[...] = (total * gelu_slope(pre)).astype(bf16)
    own = gp_ref[at(zh * (gp_ref.shape[0] - half), half, side), :]
    low, high = own[:, :outs], own[:, outs:]
    mine_ref[...] = jnp.where(zh == 0, low, high)
    theirs_ref[...] = jnp.where(zh == 0, high, low)


def slope_back(side, idx, keep, recv, pre, half):
    outs = pre.shape[1] // 2
    return call(
        functools.partial(slope_body, side),
        "slope_back",
        [(SMEM, idx), (LOAD, keep), (LOAD, recv), (LOAD, pre)],
        [
            (VMEM, struct((half, outs), bf16)),
            (VMEM, struct((half, outs), bf16)),
            (VMEM, struct(keep.shape, bf16)),
        ],
    )


def back_body(side, last, group, arrive, idx_ref, *refs):
    zh, zl = idx_ref[2], idx_ref[3]
    if last:
        valid_ref, grad_ref, x_ref, go_ref, far_ref, idk_ref, wl, wo, ws, po, ps = refs[:11]
        own_ref, give_ref, taps_ref, wbuf, idk_far, sems = refs[11:]
    else:
        keep_ref, recv_ref, pre_ref, wl, wo, ws, gp_ref, own_ref, give_ref, taps_ref, wbuf, sems = refs
    pairs = slice_copies(group, idx_ref, wl, wo, ws, wbuf)
    if last:
        pairs += flat_copies(9, idx_ref, po, ps, idk_far)
    copies = start_copies(pairs, sems)
    arrive()
    if last:
        grad = grad_ref[...]
    else:
        total = keep_ref[...] + recv_ref[...].astype(f32)
        spots = keep_ref.shape[0]
        pre = pre_ref[at(zh * (pre_ref.shape[0] - spots), spots, side), :]
        grad = (total * gelu_slope(pre)).astype(bf16)
        gp_ref[...] = grad
    spread_taps(side, grad, taps_ref)
    depth, outs = wl.shape[1:]
    pixels = own_ref.shape[-2]
    start = zh * side
    for copy in copies:
        copy.wait()
    chans = depth // 4

    def rows(index):
        spot = at(index * chans, chans, chans)
        return lanes([wbuf[u, t, spot, :] for t in range(9) for u in range(2)])

    for target, along in ((give_ref, 1 - zl), (own_ref, zl)):
        if last:
            units = chans // idk_far.shape[2]
            for up in range(2):
                index = 2 * up + along
                weights = rows(index)
                near = idk_ref[at(index * chans, chans, chans), :]
                far = flat_rows(idk_far, index * units, units)
                apart = zh * (far_ref.shape[0] - pixels)
                for begin, block in halves(pixels, side):
                    here = at(zh * pixels + begin, block, side)
                    part = dot(tap_block(side, taps_ref, start + begin, block), weights, NT)
                    x = x_ref[here, at(index * chans, chans, chans)]
                    part = part * gelu_slope(x.astype(f32))
                    part = part + dot(go_ref[here, :], near, NT)
                    part = part + valid_ref[0] * dot(far_ref[at(apart + begin, block, side), :], far, NT)
                    target[up, begin : begin + block, :] = part.astype(target.dtype)
        else:
            weights = jnp.concatenate([rows(along), rows(2 + along)], axis=0)
            for begin, block in halves(pixels, side):
                part = dot(tap_block(side, taps_ref, start + begin, block), weights, NT)
                target[begin : begin + block, :] = part.astype(target.dtype)


def back(side, idx, sources, own, other, group, last=None):
    taps, depth, outs = own.shape
    spots = sources[0].shape[0]
    copies = 2 * other[0].shape[0] + 1
    extra = []
    scratch = []
    if last:
        valid, full_x, go, cot_far, idk, pieces, half = last
        chans = depth // 4
        shape = (2, half, chans)
        results = []
        extra = [(FAR, pieces[0]), (FAR, pieces[1])]
        sources = list(sources) + [full_x, go, cot_far, idk]
        columns, size = idk.shape[1] // 128, pieces[0].shape[2]
        scratch = [pltpu.VMEM((columns, depth // size, size, 128), bf16)]
        copies += 2 * other[0].shape[0] * columns
    else:
        shape = (spots - side, depth // 2)
        results = [(VMEM, struct((spots, 2 * outs), bf16))]
    results += [(VMEM, struct(shape, f32)), (VMEM, struct(shape, bf16))]
    return call(
        functools.partial(back_body, side, bool(last), group),
        "back",
        [(SMEM, idx)]
        + ([(SMEM, last[0])] if last else [])
        + [(LOAD, source) for source in sources]
        + [(FAR, own), (FAR, other[0]), (FAR, other[1])]
        + extra,
        results,
        [pltpu.VMEM((spots + 2 * side, 6 * outs), bf16), pltpu.VMEM((2, taps, depth, outs), bf16)]
        + scratch
        + [pltpu.SemaphoreType.DMA((copies,))],
        spare=14 if last else 10,
    )


def put_blocks(idx_ref, keep_ref, give_ref, part, tap, first_block, size, begin=0):
    chip, core = idx_ref[0], idx_ref[1]
    for b in range(0, part.shape[0] // size, 2):
        even = part[b * size : (b + 1) * size, :]
        odd = part[(b + 1) * size : (b + 2) * size, :]
        mask = chip ^ ((first_block + b) // 2)
        slot = slot_of(mask, core, keep_ref.shape[0])
        give_slot = slot_of(mask, 1 - core, keep_ref.shape[0])
        rows = slice(begin + tap * size, begin + (tap + 1) * size)
        keep_ref[slot, rows, :] = jnp.where(core == 0, even, odd).astype(bf16)
        give_ref[give_slot, rows, :] = jnp.where(core == 0, odd, even).astype(bf16)


def weight_body(side, half, flat, arrive, idx_ref, gp_ref, *refs):
    if flat:
        full_ref, go_ref, bias_ref = refs[:3]
        refs = refs[3:]
    xl, xa, keep_ref, give_ref, xbuf, taps_ref, sems = refs
    arrive()
    zh, zl = idx_ref[2], idx_ref[3]
    chans = xl.shape[1] // 2
    spots = xbuf.shape[0]
    window = at(zh * (xl.shape[0] - spots), spots, side)
    pairs = []
    for source, along in ((xl, zl), (xa, 1 - zl)):
        for up in range(2):
            pairs.append(
                (
                    source.at[window, up * chans : (up + 1) * chans],
                    xbuf.at[:, at((2 * up + along) * chans, chans, chans)],
                )
            )
    run_copies(pairs, sems)
    wide = gp_ref.shape[1]
    outs = wide // 2
    spot = lax.broadcasted_iota(jnp.int32, (spots, wide), 0) - zh * side
    grad = gp_ref[at(zh * (gp_ref.shape[0] - spots), spots, side), :].astype(f32)
    grad = jnp.where((spot >= 0) & (spot < half), grad, 0.0)
    bias = jnp.sum(grad, axis=0, keepdims=True)
    spread_taps(side, grad.astype(bf16), taps_ref)
    blocks = 2 * keep_ref.shape[0]
    depth = xbuf.shape[1]
    size = depth // blocks
    for begin in range(0, depth, 256):
        values = xbuf[:, begin : begin + 256]
        for y in range(3):
            place = side * (2 - y)
            part = dot(values, taps_ref[place : place + spots, :], TN)
            for x in range(3):
                for u in range(2):
                    col = x * wide + u * outs
                    put_blocks(
                        idx_ref, keep_ref, give_ref, part[:, col : col + outs],
                        3 * y + x, begin // size, size, u * (9 * size + 16),
                    )
    for u in range(2):
        row = jnp.broadcast_to(bias[:, u * outs : (u + 1) * outs], (16, outs)).astype(bf16)
        for j in range(keep_ref.shape[0]):
            spot = slice(u * (9 * size + 16) + 9 * size, (u + 1) * (9 * size + 16))
            keep_ref[j, spot, :] = row
            give_ref[j, spot, :] = row
    if flat:
        first = 2 * (9 * size + 16)
        flat_pieces(1.0, idx_ref, full_ref, go_ref, bias_ref, keep_ref, give_ref, first)


def weight_grad(side, half, idx, grad, act, act_other, chips, flat=()):
    spots = half + side
    wide = grad.shape[1]
    outs = wide // 2
    depth = 2 * act.shape[1]
    rows = 2 * (9 * depth // (2 * chips) + 16)
    if flat:
        rows += flat_size(flat[0], flat[1], chips)
    return call(
        functools.partial(weight_body, side, half, bool(flat)),
        "weight_grad",
        [(SMEM, idx), (LOAD, grad)] + [(LOAD, a) for a in flat] + [(FAR, act), (FAR, act_other)],
        [(VMEM, struct((chips, rows, outs), bf16))] * 2,
        [
            pltpu.VMEM((spots, depth), bf16),
            pltpu.VMEM((spots + 2 * side, 3 * wide), bf16),
            pltpu.SemaphoreType.DMA((4,)),
        ],
        spare=10,
    )


def weight_one_body(side, arrive, idx_ref, mine_ref, theirs_ref, x_ref, *refs):
    keep_ref, give_ref, gp_ref, taps_ref = refs
    arrive()
    zh = idx_ref[2]
    half, outs = mine_ref.shape
    gp_ref[at(zh * half, half, side), :] = mine_ref[...]
    gp_ref[at((1 - zh) * half, half, side), :] = theirs_ref[...]
    grad = gp_ref[...]
    bias = jnp.sum(grad.astype(f32), axis=0, keepdims=True)
    spread_taps(side, grad, taps_ref)
    blocks = 2 * keep_ref.shape[0]
    spots, depth = x_ref.shape
    size = depth // blocks
    right = tap_block(side, taps_ref, 0, spots)
    for begin in range(0, depth, 256):
        part = dot(x_ref[:, begin : begin + 256], right, TN)
        for tap in range(9):
            put_blocks(
                idx_ref, keep_ref, give_ref, part[:, tap * outs : (tap + 1) * outs],
                tap, begin // size, size,
            )
    row = jnp.broadcast_to(bias, (16, outs)).astype(bf16)
    first = 9 * size + 16
    for j in range(keep_ref.shape[0]):
        keep_ref[j, 9 * size : first, :] = row
        give_ref[j, 9 * size : first, :] = row


def weight_one_grad(side, idx, mine, theirs, act_zero, chips):
    spots, depth = act_zero.shape
    outs = mine.shape[1]
    rows = 9 * depth // (2 * chips) + 16
    return call(
        functools.partial(weight_one_body, side),
        "weight_one_grad",
        [(SMEM, idx), (LOAD, mine), (LOAD, theirs), (LOAD, act_zero)],
        [(VMEM, struct((chips, rows, outs), bf16))] * 2,
        [
            pltpu.VMEM((spots, outs), bf16),
            pltpu.VMEM((spots + 2 * side, 3 * outs), bf16),
        ],
        spare=14,
    )


def fold_body(pairs, arrive, idx_ref, *refs):
    arrive()
    ins, (keep_ref, give_ref) = refs[: 2 * pairs], refs[2 * pairs :]
    half = keep_ref.shape[0]
    for i in range(2 * half):
        target = keep_ref if i < half else give_ref
        begin = 0
        for keep, recv in zip(ins[0::2], ins[1::2]):
            rows = keep.shape[1]
            total = keep[i].astype(f32) + recv[i].astype(f32)
            target[i % half, begin : begin + rows, :] = total.astype(bf16)
            begin += rows


def fold(idx, *arrays):
    blocks, _, wide = arrays[0].shape
    rows = sum(a.shape[1] for a in arrays[0::2])
    return call(
        functools.partial(fold_body, len(arrays) // 2),
        "fold",
        [(SMEM, idx)] + [(LOAD, a) for a in arrays],
        [(VMEM, struct((blocks // 2, rows, wide), bf16))] * 2,
    )


def last_body(arrive, idx_ref, keep_in, recv_in, *targets):
    arrive()
    zh = idx_ref[2]
    rows = targets[0].shape[0]
    starts = (zh * rows, (1 - zh) * rows, 2 * rows) if len(targets) > 1 else (0,)
    for target, begin in zip(targets, starts):
        spot = at(begin, target.shape[0], 16)
        total = keep_in[0, spot, :].astype(f32) + recv_in[0, spot, :].astype(f32)
        target[...] = total.astype(bf16)


def last_fold(idx, keep, recv, rows=0):
    _, total, wide = keep.shape
    sizes = [rows, rows, total - 2 * rows] if rows else [total]
    return call(
        last_body,
        "last_fold",
        [(SMEM, idx), (LOAD, keep), (LOAD, recv)],
        [(VMEM, struct((size, wide), bf16)) for size in sizes if size],
    )


def final_body(depth, arrive, idx_ref, own_ref, sib_ref, grad_ref, bias_ref, *flat):
    arrive()
    chip, core = idx_ref[0], idx_ref[1]
    chips = own_ref.shape[0]
    size = depth // (2 * chips)
    bias_ref[...] = own_ref[0, 9 * size : 9 * size + 1, :].astype(f32)
    for j in range(chips):
        for source, owner in ((own_ref, core), (sib_ref, 1 - core)):
            home = chip ^ mask_of(j, owner, chips)
            spot = at((2 * home + owner) * size, size, size)
            for tap in range(9):
                grad_ref[tap, spot, :] = source[j, tap * size : (tap + 1) * size, :].astype(f32)
    if flat:
        flat_ref, flat_bias_ref = flat
        first = 9 * size + 16
        wide = own_ref.shape[2]
        columns = flat_ref.shape[1] // wide
        size = flat_ref.shape[0] // (2 * chips)
        for c in range(columns):
            row = first + columns * size + c
            flat_bias_ref[:, c * wide : (c + 1) * wide] = own_ref[0, row : row + 1, :].astype(f32)
        for j in range(chips):
            for source, owner in ((own_ref, core), (sib_ref, 1 - core)):
                home = chip ^ mask_of(j, owner, chips)
                spot = at((2 * home + owner) * size, size, size)
                for c in range(columns):
                    row = first + c * size
                    piece = source[j, row : row + size, :].astype(f32)
                    flat_ref[spot, c * wide : (c + 1) * wide] = piece


def final_grads(idx, own, sib, depth, flat_shape=None):
    outs = own.shape[2]
    results = [(VMEM, struct((9, depth, outs), f32)), (VMEM, struct((1, outs), f32))]
    if flat_shape:
        results += [(VMEM, struct(flat_shape, f32)), (VMEM, struct((1, flat_shape[1]), f32))]
    return call(
        functools.partial(final_body, depth),
        "final_grads",
        [(SMEM, idx), (LOAD, own), (LOAD, sib)],
        results,
    )


def flat_pieces(gain, idx_ref, x_ref, go_ref, bias_ref, keep_ref, give_ref, first):
    chip, core = idx_ref[0], idx_ref[1]
    chips, _, wide = keep_ref.shape
    columns = go_ref.shape[1] // wide
    size = x_ref.shape[1] // (2 * chips)
    bias = jnp.concatenate(
        [bias_ref[:, c * wide : (c + 1) * wide] for c in range(columns)]
        + [jnp.zeros((16 - columns, wide), f32)],
        axis=0,
    ).astype(bf16)
    for j in range(chips):
        keep_ref[j, first + columns * size :, :] = bias
        give_ref[j, first + columns * size :, :] = bias
    for begin in range(0, x_ref.shape[1], 256):
        part = gain * dot(x_ref[:, begin : begin + 256], go_ref[...], TN)
        for b in range(0, 256 // size, 2):
            mask = chip ^ ((begin // size + b) // 2)
            slot = slot_of(mask, core, chips)
            give_slot = slot_of(mask, 1 - core, chips)
            for c in range(columns):
                even = part[b * size : (b + 1) * size, c * wide : (c + 1) * wide]
                odd = part[(b + 1) * size : (b + 2) * size, c * wide : (c + 1) * wide]
                spot = slice(first + c * size, first + (c + 1) * size)
                keep_ref[slot, spot, :] = jnp.where(core == 0, even, odd).astype(bf16)
                give_ref[give_slot, spot, :] = jnp.where(core == 0, odd, even).astype(bf16)


def flat_size(x, go, chips):
    return (go.shape[1] // 128) * (x.shape[1] // (2 * chips)) + 16


def outer_body(gain, arrive, idx_ref, x_ref, go_ref, bias_ref, keep_ref, give_ref):
    arrive()
    flat_pieces(gain, idx_ref, x_ref, go_ref, bias_ref, keep_ref, give_ref, 0)


def outer(idx, x, go, gain, bias, chips):
    return call(
        functools.partial(outer_body, gain),
        "outer",
        [(SMEM, idx), (LOAD, x), (LOAD, go), (LOAD, bias)],
        [(VMEM, struct((chips, flat_size(x, go, chips), 128), bf16))] * 2,
        spare=8,
    )


def start_body(arrive, idx_ref, valid_ref, cot_ref, outk_ref, go_ref, bias_ref, own_ref, give_ref):
    arrive()
    zl = idx_ref[3]
    masked = cot_ref[...].astype(f32) * valid_ref[0]
    go_ref[...] = masked.astype(bf16)
    bias_ref[...] = jnp.sum(masked, axis=0, keepdims=True)
    chans = outk_ref.shape[0] // 4
    block = cot_ref.shape[0] // 4
    for target, along in ((give_ref, 1 - zl), (own_ref, zl)):
        weights = jnp.concatenate(
            [outk_ref[at((2 * up + along) * chans, chans, chans), :] for up in range(2)], axis=0
        )
        for begin in range(0, cot_ref.shape[0], block):
            part = post_gain * dot(go_ref[begin : begin + block, :], weights, NT)
            target[begin : begin + block, :] = part.astype(target.dtype)


def start_back(idx, valid, cot, outk):
    spots, outs = cot.shape
    half = outk.shape[0] // 2
    return call(
        start_body,
        "start_back",
        [(SMEM, idx), (SMEM, valid), (LOAD, cot), (LOAD, outk)],
        [
            (VMEM, struct(cot.shape, bf16)),
            (VMEM, struct((1, outs), f32)),
            (VMEM, struct((spots, half), f32)),
            (VMEM, struct((spots, half), bf16)),
        ],
    )


def rows_body(side, arrive, idx_ref, own_ref, recv_ref, keep_ref, give_ref):
    arrive()
    zh = idx_ref[2]
    spots = keep_ref.shape[0]
    apart = own_ref.shape[0] - spots
    for target, begin in ((give_ref, (1 - zh) * apart), (keep_ref, zh * apart)):
        spot = at(begin, spots, side)
        total = own_ref[spot, :] + recv_ref[spot, :].astype(f32)
        target[...] = total.astype(target.dtype)


def rows_sum(side, idx, own, recv, spots):
    shape = (spots, own.shape[1])
    return call(
        functools.partial(rows_body, side),
        "rows_sum",
        [(SMEM, idx), (LOAD, own), (LOAD, recv)],
        [(VMEM, struct(shape, f32)), (VMEM, struct(shape, bf16))],
    )


def slots_body(arrive, idx_ref, own_ref, recv_ref, keep_ref, give_ref):
    arrive()
    zh = idx_ref[2]
    for target, slot in ((give_ref, 1 - zh), (keep_ref, zh)):
        total = own_ref[slot] + recv_ref[slot].astype(f32)
        target[...] = total.astype(bf16)


def slots_sum(idx, own, recv):
    shape = struct(own.shape[1:], bf16)
    return call(
        slots_body,
        "slots_sum",
        [(SMEM, idx), (LOAD, own), (LOAD, recv)],
        [(VMEM, shape), (VMEM, shape)],
    )


def input_body(arrive, idx_ref, keep_ref, recv_ref, out_ref):
    arrive()
    zh = idx_ref[2]
    half = keep_ref.shape[0]
    out_ref[at(zh * half, half, half), :] = keep_ref[...]
    out_ref[at((1 - zh) * half, half, half), :] = recv_ref[...]


def input_grad(idx, keep, recv):
    half, chans = keep.shape
    return call(
        input_body,
        "input_grad",
        [(SMEM, idx), (LOAD, keep), (LOAD, recv)],
        [(VMEM, struct((2 * half, chans), bf16))],
    )


def whole_body(side, arrive, idx_ref, xl, xa, xh, xd, rh, rl, x_ref, act_ref, sems):
    arrive()
    zh, zl = idx_ref[2], idx_ref[3]
    chans = xl.shape[1]
    spots = xa.shape[0]
    rest = xl.shape[0] - spots
    window, outside = at(zh * rest, spots, side), at((1 - zh) * spots, rest, side)

    def cols(up, along):
        return at((2 * up + along) * chans, chans, chans)

    run_copies(
        [
            (xl, x_ref.at[:, cols(zh, zl)]),
            (xa, x_ref.at[window, cols(zh, 1 - zl)]),
            (xh, x_ref.at[window, cols(1 - zh, zl)]),
            (xd, x_ref.at[window, cols(1 - zh, 1 - zl)]),
            (rl.at[0], x_ref.at[outside, cols(zh, 1 - zl)]),
            (rh, x_ref.at[outside, cols(1 - zh, zl)]),
            (rl.at[1], x_ref.at[outside, cols(1 - zh, 1 - zl)]),
        ],
        sems,
    )
    block = x_ref.shape[0] // 8
    for begin in range(0, x_ref.shape[0], block):
        rows = slice(begin, begin + block)
        act_ref[rows, :] = gelu(x_ref[rows, :].astype(f32)).astype(bf16)


def whole_input(side, idx, *parts):
    spots, chans = parts[0].shape
    return call(
        functools.partial(whole_body, side),
        "whole_input",
        [(SMEM, idx)] + [(FAR, p) for p in parts],
        [(VMEM, struct((spots, 4 * chans), bf16))] * 2,
        [pltpu.SemaphoreType.DMA((7,))],
    )


def join_body(arrive, idx_ref, own, recv, far_own, far_recv, out, sems):
    arrive()
    zh, zl = idx_ref[2], idx_ref[3]
    half = own.shape[0]
    chans = own.shape[1] // 2
    pairs = []
    for source, up, along in ((own, zh, zl), (recv, zh, 1 - zl), (far_own, 1 - zh, zl), (far_recv, 1 - zh, 1 - zl)):
        for slot in range(2):
            spot = at((2 * slot + along) * chans, chans, chans)
            target = out.at[at(up * half, half, half), spot]
            pairs.append((source.at[:, slot * chans : (slot + 1) * chans], target))
    run_copies(pairs, sems)


def join(idx, *parts):
    half, wide = parts[0].shape
    return call(
        join_body,
        "join",
        [(SMEM, idx)] + [(FAR, p) for p in parts],
        [(VMEM, struct((2 * half, 2 * wide), bf16))],
        [pltpu.SemaphoreType.DMA((8,))],
    )


def finish_body(arrive, idx_ref, valid_ref, x_ref, act_ref, idk_ref, outk_ref, ib_ref, out_ref):
    arrive()
    block = x_ref.shape[0] // 4
    for begin in range(0, x_ref.shape[0], block):
        rows = slice(begin, begin + block)
        identity = dot(x_ref[rows, :], idk_ref[...]) + ib_ref[...]
        branch = dot(act_ref[rows, :], outk_ref[...])
        out_ref[rows, :] = ((identity + post_gain * branch) * valid_ref[0]).astype(bf16)


def finish(idx, valid, x, act, idk, outk, ib):
    outs = idk.shape[1]
    return call(
        finish_body,
        "finish",
        [(SMEM, idx), (SMEM, valid), (LOAD, x), (LOAD, act), (LOAD, idk), (LOAD, outk)]
        + [(VMEM, ib.reshape(1, outs))],
        [(VMEM, struct((x.shape[0], outs), bf16))],
        spare=8,
    )


def flip(value, axis):
    return lax.ppermute(value, axis, [(0, 1), (1, 0)])


def cross(value, step, chips):
    pairs = []
    for chip in range(chips):
        for core in range(2):
            other = chip ^ step_bits(core, chips)[step]
            pairs.append((2 * chip + core, 2 * other + core))
    return lax.ppermute(value, DP, pairs)


def swap(pieces, axis):
    return lax.all_to_all(pieces, axis, split_axis=0, concat_axis=0, tiled=True)


def after(value, other):
    return lax.optimization_barrier((value, other))[0]


def rows_of(value, start, size):
    return lax.dynamic_slice_in_dim(value, start, size, 0)


def local(
    pixels,
    counts,
    kernel_one,
    bias_one,
    kernel_two,
    bias_two,
    kernel_three,
    bias_three,
    out_kernel,
    identity_kernel,
    identity_bias,
    cotangent,
):
    images, rows, width, chans = pixels.shape
    side = width // 2
    spots = side * side
    half = spots // 2
    window = half + halo * side
    outs = cotangent.shape[3]
    chips = lax.axis_size("chip")
    chip, core, zh, zl = [lax.axis_index(a) for a in ("chip", "core", "zh", "zl")]
    idx = jnp.stack([chip, core, zh, zl]).astype(jnp.int32)
    taps = lambda kernel: kernel.reshape((9,) + kernel.shape[2:])
    one, two, three = taps(kernel_one), taps(kernel_two), taps(kernel_three)

    own_count = lax.dynamic_index_in_dim(counts, 2 * chip + core, 0, keepdims=True)
    valid = (own_count > 0).astype(f32)

    place = 2 * chip + core

    def units_of(kernel, size):
        if kernel.ndim == 3:
            block = kernel.shape[1] // (2 * chips)
            return lax.dynamic_slice_in_dim(kernel, place * block, block, 1)
        block = kernel.shape[0] // (2 * chips)
        block = lax.dynamic_slice_in_dim(kernel, place * block, block, 0)
        block = block.reshape(-1, size, block.shape[1] // 128, 128)
        return block.transpose(2, 0, 1, 3).reshape(-1, size, 128)

    steps = chips.bit_length() - 1

    def spread(piece, early=(), late=()):
        own = piece[None]
        for step in reversed(range(steps)):
            tie = late if step == 0 else early
            own = jnp.concatenate(after((own, cross(own, step, chips)), tie))
        return own, flip(own, "core")

    last = [idx]

    def turn(*others):
        return after(idx, (last[0],) + others)

    def ran(results):
        last[0] = results[-1] if isinstance(results, (list, tuple)) else results
        return results

    size = two.shape[1] // (2 * chips)
    deep = two.shape[1]
    two_piece = units_of(two, size)
    bias_other = flip(after(jnp.stack([bias_one, bias_two, bias_three]), two_piece), "zh")
    two_piece = flip(two_piece, "zh")
    pooled = ran(pool(pixels))
    xl = swap(after(pooled, (two_piece, bias_other)), DP).reshape(spots, chans)
    one_piece = flip(units_of(after(one, pooled), size), "zh")
    last_piece = jnp.concatenate([units_of(after(k, pooled), size) for k in (three, identity_kernel)])
    units = last_piece.shape[0]
    cot = cotangent.reshape(spots, outs)
    cot_rows = rows_of(after(cot, pooled), (1 - zh) * half, half)
    go, identity_bias_grad, ga_own, ga_give = ran(start_back(turn(), valid, cot, out_kernel))

    apart = spots - window
    xa = flip(rows_of(xl, zh * apart, window), "zl")
    xh = flip(rows_of(xl, (1 - zh) * apart, window), "zh")
    xd = flip(xh, "zl")
    rest = spots - window
    rest_own = rows_of(xl, (1 - zh) * window, rest)
    rest_high = rows_of(xl, zh * window, rest)
    rest_high = jnp.concatenate([rest_high[:, :128], rest_high[:, 128:]]).reshape(-1, size, 128)
    last_piece = jnp.concatenate([last_piece, rest_high])
    one_other = spread(after(one_piece, xl), (xh, xa, ga_give, last_piece, cot_rows), xd)
    last_piece = flip(after(last_piece, xh), "zh")
    rest_high = last_piece[units:].reshape(2, rest, 128)
    rest_high = jnp.concatenate([rest_high[0], rest_high[1]], axis=1)
    last_piece = last_piece[:units]
    two_other = spread(after(two_piece, xl), (xh, xa), xd)
    ga_recv = flip(after(ga_give, xd), "zl")

    pre_one, act_one = ran(
        conv(side, turn(), (xl, xa, xh, xd), one, one_other, 0, bias_one, bias_other[0], True)
    )
    act_one_other = flip(act_one, "zl")
    ga_own, ga_give = ran(rows_sum(side, turn(last_piece), ga_own, ga_recv, half + (halo - 3) * side))
    pre_two, act_two = ran(
        conv(side, turn(), (act_one, act_one_other), two, two_other, 0, bias_two, bias_other[1])
    )
    act_two_other = flip(act_two, "zl")
    last_other = spread(after(last_piece, xd), act_one_other, act_two)
    ga_recv = flip(after(ga_give, act_two), "zh")
    pre_three, act_three = ran(
        conv(side, turn(), (act_two, act_two_other), three, last_other, 0, bias_three, bias_other[2])
    )
    rest_low = flip(jnp.stack(after((rest_own, rest_high), act_three)), "zl")
    own_rows = rows_of(act_three, zh * (halo - 3) * side, half)

    gp_three, ga_own, ga_give = ran(
        back(side, turn(), (ga_own, ga_recv, pre_three), three, last_other, 0)
    )
    ga_recv = flip(ga_give, "zl")
    cot_far = flip(after(cot_rows, gp_three), "zh")
    full_x, act_zero = ran(whole_input(side, turn(), xl, xa, xh, xd, rest_high, rest_low))
    keep_three, give_three = ran(
        weight_grad(
            side, half, turn(), gp_three, act_two, act_two_other, chips, (full_x, go, identity_bias_grad)
        )
    )
    gp_two, ga_own, ga_give = ran(
        back(side, turn(), (ga_own, ga_recv, pre_two), two, two_other, 0)
    )
    ga_recv = flip(ga_give, "zl")
    keep_two, give_two = ran(weight_grad(side, half, turn(cot_far), gp_two, act_one, act_one_other, chips))

    gp_mine, gp_theirs, gp_one = ran(slope_back(side, turn(), ga_own, ga_recv, pre_one, half))
    gp_theirs = flip(gp_theirs, "zh")
    recv_three = flip(after(give_three, gp_one), "core")
    gx_own, gx_give = ran(
        back(
            side, turn(), (gp_one,), one, one_other, 0,
            (valid, full_x, go, cot_far, identity_kernel, last_other, half),
        )
    )
    gx_recv = flip(gx_give, "zl")

    def folds(keep, recv, first):
        for step in range(first, steps):
            keep, give = ran(fold(turn(), keep, recv))
            recv = cross(give, step, chips)
        return keep, recv

    keep_three, give_three = ran(fold(turn(), keep_three, recv_three))
    recv_three = cross(give_three, 0, chips)
    keep_one, give_one = ran(weight_one_grad(side, turn(), gp_mine, gp_theirs, act_zero, chips))
    recv_one = flip(give_one, "core")
    recv_two = flip(after(give_two, keep_one), "core")
    own_rows = after(own_rows, keep_one)
    near_rows = flip(own_rows, "zl")
    far_rows = flip(own_rows, "zh")
    keep_three, recv_three = folds(keep_three, recv_three, 1)
    keep_one, give_one = ran(fold(turn(), keep_one, recv_one))
    recv_one = cross(give_one, 0, chips)
    gx_keep, gx_give = ran(slots_sum(turn(), gx_own, gx_recv))
    gx_recv = flip(gx_give, "zh")
    far_near_rows = flip(after(far_rows, gx_keep), "zl")
    slot_rows = 9 * size + 16
    keep_three, give_three, id_rows = ran(last_fold(turn(), keep_three, recv_three, slot_rows))
    recv_three = flip(give_three, "zh")
    keep_one, recv_one = folds(keep_one, recv_one, 1)
    full_three = ran(join(turn(), own_rows, near_rows, far_rows, far_near_rows))
    keep_out, give_out = ran(outer(turn(), full_three, go, post_gain, identity_bias_grad, chips))
    recv_out = flip(give_out, "core")
    total = ran(last_fold(turn(), keep_one, recv_one))
    keep_two, give_two = ran(fold(turn(), keep_two, recv_two, keep_out, recv_out))
    recv_two = cross(give_two, 0, chips)

    def both(keep, recv):
        return (keep.astype(f32) + recv.astype(f32)).astype(bf16)

    all_three = spread(jnp.concatenate([both(after(keep_three, total), recv_three), id_rows]))
    keep_two, recv_two = folds(keep_two, recv_two, 1)
    all_one = spread(total)
    gx = ran(input_grad(turn(), gx_keep, gx_recv))
    gx = swap(gx.reshape(images, rows * width // 4, chans), DP)
    keep_two, give_two, out_rows = ran(last_fold(turn(), keep_two, recv_two, slot_rows))
    recv_two = flip(give_two, "zh")
    block_out = ran(finish(turn(), valid, full_x, full_three, identity_kernel, out_kernel, identity_bias))
    all_two = spread(jnp.concatenate([both(after(keep_two, block_out), recv_two), out_rows]))
    kernel_three_grad, bias_three_grad, identity_kernel_grad, identity_bias_grad = ran(
        final_grads(turn(), *all_three, deep, identity_kernel.shape)
    )
    pixels_grad = widen(gx, rows, width)
    kernel_one_grad, bias_one_grad = ran(final_grads(turn(), *all_one, one.shape[1]))
    kernel_two_grad, bias_two_grad, out_kernel_grad, _ = ran(
        final_grads(turn(), *all_two, deep, out_kernel.shape)
    )

    return (
        block_out.reshape(cotangent.shape),
        pixels_grad,
        kernel_one_grad.reshape(kernel_one.shape),
        bias_one_grad[0],
        kernel_two_grad.reshape(kernel_two.shape),
        bias_two_grad[0],
        kernel_three_grad.reshape(kernel_three.shape),
        bias_three_grad[0],
        out_kernel_grad,
        identity_kernel_grad,
        identity_bias_grad[0],
    )


def solution(mesh):
    members = mesh.devices.size // mesh.shape["mp"]
    fine = Mesh(
        mesh.devices.reshape(members // 2, 2, 2, mesh.shape["mp"] // 2),
        ("chip", "core", "zh", "zl"),
    )
    return jax.shard_map(
        local,
        mesh=fine,
        in_specs=(
            P(None, DP, None, MP),
            P(),
            P(None, None, None, MP),
            P(MP),
            P(None, None, None, MP),
            P(MP),
            P(None, None, None, MP),
            P(MP),
            P(None, MP),
            P(None, MP),
            P(MP),
            P(DP, None, None, MP),
        ),
        out_specs=(
            P(DP, None, None, MP),
            P(None, DP, None, MP),
            P(None, None, None, MP),
            P(MP),
            P(None, None, None, MP),
            P(MP),
            P(None, None, None, MP),
            P(MP),
            P(None, MP),
            P(None, MP),
            P(MP),
        ),
        check_vma=False,
    )
```

```python
import functools
import math

import jax
import jax.numpy as jnp
from jax import lax
from jax.experimental import pallas as pl
from jax.experimental.pallas import tpu as pltpu
from jax.sharding import Mesh
from jax.sharding import PartitionSpec as P


post_gain = 0.015625
slope = 0.7978845608028654
cubic = 0.044715
halo = 6
bf16 = jnp.bfloat16
f32 = jnp.float32
NT = (((1,), (1,)), ((), ()))
TN = (((0,), (0,)), ((), ()))
NN = (((1,), (0,)), ((), ()))
DP = ("chip", "core")
MP = ("zh", "zl")


def dot(left, right, dims=NN):
    return lax.dot_general(left, right, dims, preferred_element_type=f32)


def gelu(value):
    inner = jnp.tanh(slope * (value + cubic * value * value * value))
    return 0.5 * value * (1.0 + inner)


def gelu_slope(value):
    square = value * value
    inner = jnp.tanh(slope * value * (1.0 + cubic * square))
    climb = slope * (1.0 + 3.0 * cubic * square)
    return 0.5 * (1.0 + inner) + 0.5 * value * (1.0 - inner * inner) * climb


def struct(shape, kind):
    return jax.ShapeDtypeStruct(shape, kind)


def lanes(blocks):
    return blocks[0] if len(blocks) == 1 else jnp.concatenate(blocks, axis=1)


def step_bits(core, chips):
    bits = [1 << n for n in range(chips.bit_length() - 1)]
    for n in range(0, len(bits) - 1, 2) if core else ():
        bits[n], bits[n + 1] = bits[n + 1], bits[n]
    return bits


def mask_of(i, core, chips):
    masks = []
    for which in range(2):
        bits = step_bits(which, chips)
        masks.append(sum(bit for n, bit in enumerate(bits) if i >> (len(bits) - 1 - n) & 1))
    return jnp.where(core == 0, masks[0], masks[1])


def slot_of(mask, core, chips):
    slots = []
    for which in range(2):
        bits = step_bits(which, chips)
        slot = 0
        for n, bit in enumerate(bits):
            slot = slot + ((mask >> (bit.bit_length() - 1)) & 1) * (1 << (len(bits) - 1 - n))
        slots.append(slot)
    return jnp.where(core == 0, slots[0], slots[1])


VMEM = pl.BlockSpec(memory_space=pltpu.VMEM)
SMEM = pl.BlockSpec(memory_space=pltpu.SMEM)
FAR = pl.BlockSpec(memory_space=pl.ANY)
LOAD = "load"


def size_of(array):
    return math.prod(array.shape) * jnp.dtype(array.dtype).itemsize


def call(body, name, ins, outs, scratch=(), spare=6, **more):
    loads = [i for i, (space, _) in enumerate(ins) if space is LOAD]
    spaces = [FAR if space is LOAD else space for space, _ in ins]
    arrays = [array for _, array in ins]
    out_specs = [space for space, _ in outs]
    out_shape = [shape for _, shape in outs]
    held = [arrays[i] for i in loads]
    buffers = [pltpu.VMEM(array.shape, array.dtype) for array in held]
    sems = [pltpu.SemaphoreType.DMA((len(held),))] if held else []
    vmem = sum(size_of(array) for array in held)
    vmem += sum(size_of(a) for space, a in list(ins) + list(outs) if space is VMEM)
    vmem += sum(size_of(b) for b in scratch if b.memory_space == pltpu.VMEM)
    moved = sum(size_of(a) for a in arrays + out_shape)

    def wrapped(*refs):
        inputs = list(refs[: len(ins)])
        outputs = refs[len(ins) : len(ins) + len(outs)]
        rest = refs[len(ins) + len(outs) :]
        kept, tail = rest[: len(held)], rest[len(held) :]
        copies = []
        if held:
            sem, tail = tail[0], tail[1:]
            copies = [
                pltpu.make_async_copy(inputs[i], kept[n], sem.at[n]) for n, i in enumerate(loads)
            ]
        for copy in copies:
            copy.start()
        for n, i in enumerate(loads):
            inputs[i] = kept[n]

        def arrive():
            for copy in copies:
                copy.wait()

        body(arrive, *inputs, *outputs, *tail)

    single = len(outs) == 1
    return pl.pallas_call(
        wrapped,
        in_specs=spaces,
        out_specs=out_specs[0] if single else out_specs,
        out_shape=out_shape[0] if single else out_shape,
        scratch_shapes=buffers + sems + list(scratch),
        compiler_params=pltpu.CompilerParams(vmem_limit_bytes=vmem + (spare << 20)),
        cost_estimate=pl.CostEstimate(flops=0, bytes_accessed=moved, transcendentals=0),
        name=name,
        **more,
    )(*arrays)


def run_copies(pairs, sems):
    for copy in start_copies(pairs, sems):
        copy.wait()


def slice_copies(group, idx_ref, own, blocks, sibling, wbuf):
    chip, core, zh = idx_ref[0], idx_ref[1], idx_ref[2]
    size = blocks.shape[-2]
    pairs = [(own, wbuf.at[zh])]
    for j in range(blocks.shape[0]):
        for source, owner in ((blocks, core), (sibling, 1 - core)):
            home = chip ^ mask_of(j, owner, blocks.shape[0])
            spot = at((2 * home + owner) * size, size, size)
            pairs.append((source.at[j, 9 * group : 9 * group + 9], wbuf.at[1 - zh, :, spot, :]))
    return pairs


def flat_copies(first, idx_ref, blocks, sibling, buffer):
    chip, core = idx_ref[0], idx_ref[1]
    columns, units = buffer.shape[:2]
    chips = blocks.shape[0]
    count = units // (2 * chips)
    pairs = []
    for j in range(chips):
        for source, owner in ((blocks, core), (sibling, 1 - core)):
            home = chip ^ mask_of(j, owner, chips)
            spot = pl.ds((2 * home + owner) * count, count)
            for c in range(columns):
                begin = first + c * count
                pairs.append((source.at[j, begin : begin + count], buffer.at[c, spot]))
    return pairs


def start_copies(pairs, sems):
    copies = [pltpu.make_async_copy(a, b, sems.at[i]) for i, (a, b) in enumerate(pairs)]
    for copy in copies:
        copy.start()
    return copies


def flat_rows(buffer, begin, count):
    columns, _, size, wide = buffer.shape
    return lanes([buffer[c, pl.ds(begin, count)].reshape(count * size, wide) for c in range(columns)])


def halves(spots, side):
    first = (spots // side + 1) // 2 * side
    return ((0, first), (first, spots - first))


def columns_of(size, wide, side):
    return lax.rem(lax.broadcasted_iota(jnp.int32, (size, wide), 0), side)


def at(start, size, unit):
    return pl.ds(pl.multiple_of(start, unit), size)


def pool_body(arrive, x_ref, out_ref):
    arrive()
    rows, width, chans = x_ref.shape[1:]
    half = width // 2
    pixel = lax.broadcasted_iota(jnp.int32, (half, 2 * width), 1)
    place = lax.broadcasted_iota(jnp.int32, (half, 2 * width), 0)
    inside = (lax.rem(pixel, width) >= 2 * place) & (lax.rem(pixel, width) < 2 * place + 2)
    pick = jnp.where(inside, 0.25, 0.0).astype(bf16)
    for image in range(x_ref.shape[0]):
        for row in range(rows // 2):
            window = x_ref[image, 2 * row : 2 * row + 2].reshape(2 * width, chans)
            out_ref[image, row * half : (row + 1) * half, :] = dot(pick, window).astype(bf16)


def pool(pixels):
    images, rows, width, chans = pixels.shape
    shape = struct((images, rows * width // 4, chans), bf16)
    return call(pool_body, "pool", [(LOAD, pixels)], [(VMEM, shape)])


def widen_body(arrive, idx_ref, g_ref, out_ref):
    arrive()
    rows, width, chans = out_ref.shape[1:]
    half = width // 2
    pixel = lax.broadcasted_iota(jnp.int32, (width, half), 0)
    place = lax.broadcasted_iota(jnp.int32, (width, half), 1)
    inside = (pixel >= 2 * place) & (pixel < 2 * place + 2)
    pick = jnp.where(inside, 0.25, 0.0).astype(bf16)
    for image in range(g_ref.shape[0]):
        for row in range(rows // 2):
            wide = dot(pick, g_ref[image, row * half : (row + 1) * half, :]).astype(bf16)
            out_ref[image, 2 * row] = wide
            out_ref[image, 2 * row + 1] = wide


def widen(idx, grad, rows, width):
    images, spots, chans = grad.shape
    step = images // 4
    block = pl.BlockSpec((step, spots, chans), lambda i: (i, 0, 0))
    out = pl.BlockSpec((step, rows, width, chans), lambda i: (i, 0, 0, 0))
    return call(
        widen_body,
        "widen",
        [(SMEM, idx), (block, grad)],
        [(out, struct((images, rows, width, chans), bf16))],
        grid=(4,),
    )


def conv_body(side, first, group, arrive, idx_ref, *refs):
    zh, zl = idx_ref[2], idx_ref[3]
    if first:
        xl, xa, xh, xd, wl, wo, ws, bl, bo, pre_ref, act_ref, xbuf, wbuf, acc, sems = refs
        chans = xl.shape[1]
        spots = xbuf.shape[0]
        begin = zh * (xl.shape[0] - spots)
        pairs = []
        for source, up, along in ((xl, zh, zl), (xa, zh, 1 - zl), (xh, 1 - zh, zl), (xd, 1 - zh, 1 - zl)):
            if source is xl:
                source = xl.at[at(begin, spots, side), :]
            pairs.append((source, xbuf.at[:, at((2 * up + along) * chans, chans, chans)]))
    else:
        xl, xa, wl, wo, ws, bl, bo, pre_ref, act_ref, xbuf, wbuf, acc, sems = refs
        chans = xl.shape[1] // 2
        spots = xbuf.shape[0]
        pairs = []
        for source, along in ((xl, zl), (xa, 1 - zl)):
            for up in range(2):
                pairs.append(
                    (
                        source.at[:, up * chans : (up + 1) * chans],
                        xbuf.at[:, at((2 * up + along) * chans, chans, chans)],
                    )
                )
    run_copies(slice_copies(group, idx_ref, wl, wo, ws, wbuf) + pairs, sems)
    arrive()
    acc[...] = jnp.zeros_like(acc)
    outs = 2 * wl.shape[2]
    for x in range(3):
        weights = lanes([wbuf[u, 3 * y + x] for y in range(3) for u in range(2)])
        for begin, block in halves(spots, side):
            values = xbuf[begin : begin + block, :]
            if first:
                values = gelu(values.astype(f32)).astype(bf16)
            product = dot(values, weights)
            for y in range(3):
                place = begin + side * (2 - y)
                acc[x, place : place + block, :] += product[:, y * outs : (y + 1) * outs]
    own, other = bl[...], bo[...]
    bias = lanes([jnp.where(zh == 0, own, other), jnp.where(zh == 0, other, own)])
    for begin, block in halves(act_ref.shape[0], side):
        column = columns_of(block, outs, side)
        spot = at(begin + side + zh * side, block, side)
        left = pltpu.roll(acc[0, spot, :], 1, 0)
        right = pltpu.roll(acc[2, spot, :], block - 1, 0)
        pre = acc[1, spot, :] + bias
        pre = pre + jnp.where(column > 0, left, 0.0)
        pre = pre + jnp.where(column < side - 1, right, 0.0)
        pre_ref[begin : begin + block, :] = pre
        act_ref[begin : begin + block, :] = gelu(pre).astype(bf16)


def conv(side, idx, sources, own, other, group, bias, bias_other, first=False):
    taps, depth, outs = own.shape
    spots = sources[1].shape[0]
    rows = spots - side
    return call(
        functools.partial(conv_body, side, first, group),
        "conv",
        [(SMEM, idx)]
        + [(FAR, s) for s in sources]
        + [(FAR, own), (FAR, other[0]), (FAR, other[1])]
        + [(VMEM, bias.reshape(1, outs)), (VMEM, bias_other.reshape(1, outs))],
        [(VMEM, struct((rows, 2 * outs), f32)), (VMEM, struct((rows, 2 * outs), bf16))],
        [
            pltpu.VMEM((spots, depth), bf16),
            pltpu.VMEM((2, taps, depth, outs), bf16),
            pltpu.VMEM((3, spots + 2 * side, 2 * outs), f32),
            pltpu.SemaphoreType.DMA((2 * other[0].shape[0] + 5,)),
        ],
        spare=14 if first else 8,
    )


def spread_taps(side, grad, taps_ref):
    pixels, outs = grad.shape
    column = columns_of(pixels, outs, side)
    wide = grad.astype(f32)
    ahead = jnp.where(column < side - 1, pltpu.roll(wide, pixels - 1, 0), 0.0).astype(bf16)
    behind = jnp.where(column > 0, pltpu.roll(wide, 1, 0), 0.0).astype(bf16)
    edge = jnp.zeros((side, 3 * outs), bf16)
    taps_ref[:side, :] = edge
    taps_ref[side + pixels :, :] = edge
    taps_ref[side : side + pixels, :] = jnp.concatenate([ahead, grad, behind], axis=1)


def tap_block(side, taps_ref, begin, block):
    return lanes([taps_ref[at(begin + side * (2 - y), block, side), :] for y in range(3)])


def slope_body(side, arrive, idx_ref, keep_ref, recv_ref, pre_ref, mine_ref, theirs_ref, gp_ref):
    arrive()
    zh = idx_ref[2]
    half, outs = mine_ref.shape
    total = keep_ref[...] + recv_ref[...].astype(f32)
    spots = keep_ref.shape[0]
    pre = pre_ref[at(zh * (pre_ref.shape[0] - spots), spots, side), :]
    gp_ref[...] = (total * gelu_slope(pre)).astype(bf16)
    own = gp_ref[at(zh * (gp_ref.shape[0] - half), half, side), :]
    low, high = own[:, :outs], own[:, outs:]
    mine_ref[...] = jnp.where(zh == 0, low, high)
    theirs_ref[...] = jnp.where(zh == 0, high, low)


def slope_back(side, idx, keep, recv, pre, half):
    outs = pre.shape[1] // 2
    return call(
        functools.partial(slope_body, side),
        "slope_back",
        [(SMEM, idx), (LOAD, keep), (LOAD, recv), (LOAD, pre)],
        [
            (VMEM, struct((half, outs), bf16)),
            (VMEM, struct((half, outs), bf16)),
            (VMEM, struct(keep.shape, bf16)),
        ],
    )


def back_body(side, last, group, arrive, idx_ref, *refs):
    zh, zl = idx_ref[2], idx_ref[3]
    if last:
        valid_ref, grad_ref, x_ref, go_ref, far_ref, idk_ref, wl, wo, ws, po, ps = refs[:11]
        own_ref, give_ref, taps_ref, wbuf, idk_far, sems = refs[11:]
    else:
        keep_ref, recv_ref, pre_ref, wl, wo, ws, gp_ref, own_ref, give_ref, taps_ref, wbuf, sems = refs
    pairs = slice_copies(group, idx_ref, wl, wo, ws, wbuf)
    if last:
        pairs += flat_copies(9, idx_ref, po, ps, idk_far)
    copies = start_copies(pairs, sems)
    arrive()
    if last:
        grad = grad_ref[...]
    else:
        spots = gp_ref.shape[0]

        def window(ref):
            return ref[at(zh * (ref.shape[0] - spots), spots, side), :]

        total = window(keep_ref) + window(recv_ref).astype(f32)
        grad = (total * gelu_slope(window(pre_ref))).astype(bf16)
        gp_ref[...] = grad
    spread_taps(side, grad, taps_ref)
    depth, outs = wl.shape[1:]
    pixels = own_ref.shape[-2]
    start = zh * side
    for copy in copies:
        copy.wait()
    chans = depth // 4

    def rows(index):
        spot = at(index * chans, chans, chans)
        return lanes([wbuf[u, t, spot, :] for t in range(9) for u in range(2)])

    for target, along in ((give_ref, 1 - zl), (own_ref, zl)):
        if last:
            units = chans // idk_far.shape[2]
            for up in range(2):
                index = 2 * up + along
                weights = rows(index)
                near = idk_ref[at(index * chans, chans, chans), :]
                far = flat_rows(idk_far, index * units, units)
                apart = zh * (far_ref.shape[0] - pixels)
                for begin, block in halves(pixels, side):
                    here = at(zh * pixels + begin, block, side)
                    part = dot(tap_block(side, taps_ref, start + begin, block), weights, NT)
                    x = x_ref[here, at(index * chans, chans, chans)]
                    part = part * gelu_slope(x.astype(f32))
                    part = part + dot(go_ref[here, :], near, NT)
                    part = part + valid_ref[0] * dot(far_ref[at(apart + begin, block, side), :], far, NT)
                    target[up, begin : begin + block, :] = part.astype(target.dtype)
        else:
            weights = jnp.concatenate([rows(along), rows(2 + along)], axis=0)
            for begin, block in halves(pixels, side):
                part = dot(tap_block(side, taps_ref, start + begin, block), weights, NT)
                target[begin : begin + block, :] = part.astype(target.dtype)


def back(side, idx, sources, own, other, group, last=None):
    taps, depth, outs = own.shape
    spots = min(sources[0].shape[0], sources[-1].shape[0])
    copies = 2 * other[0].shape[0] + 1
    extra = []
    scratch = []
    if last:
        valid, full_x, go, cot_far, idk, pieces, half = last
        chans = depth // 4
        shape = (2, half, chans)
        results = []
        extra = [(FAR, pieces[0]), (FAR, pieces[1])]
        sources = list(sources) + [full_x, go, cot_far, idk]
        columns, size = idk.shape[1] // 128, pieces[0].shape[2]
        scratch = [pltpu.VMEM((columns, depth // size, size, 128), bf16)]
        copies += 2 * other[0].shape[0] * columns
    else:
        shape = (spots - side, depth // 2)
        results = [(VMEM, struct((spots, 2 * outs), bf16))]
    results += [(VMEM, struct(shape, f32)), (VMEM, struct(shape, bf16))]
    return call(
        functools.partial(back_body, side, bool(last), group),
        "back",
        [(SMEM, idx)]
        + ([(SMEM, last[0])] if last else [])
        + [(LOAD, source) for source in sources]
        + [(FAR, own), (FAR, other[0]), (FAR, other[1])]
        + extra,
        results,
        [pltpu.VMEM((spots + 2 * side, 6 * outs), bf16), pltpu.VMEM((2, taps, depth, outs), bf16)]
        + scratch
        + [pltpu.SemaphoreType.DMA((copies,))],
        spare=14 if last else 10,
    )


def put_blocks(idx_ref, keep_ref, give_ref, part, tap, first_block, size, begin=0):
    chip, core = idx_ref[0], idx_ref[1]
    for b in range(0, part.shape[0] // size, 2):
        even = part[b * size : (b + 1) * size, :]
        odd = part[(b + 1) * size : (b + 2) * size, :]
        mask = chip ^ ((first_block + b) // 2)
        slot = slot_of(mask, core, keep_ref.shape[0])
        give_slot = slot_of(mask, 1 - core, keep_ref.shape[0])
        rows = slice(begin + tap * size, begin + (tap + 1) * size)
        keep_ref[slot, rows, :] = jnp.where(core == 0, even, odd).astype(bf16)
        give_ref[give_slot, rows, :] = jnp.where(core == 0, odd, even).astype(bf16)


def weight_body(side, half, flat, arrive, idx_ref, gp_ref, *refs):
    if flat:
        full_ref, go_ref, bias_ref = refs[:3]
        refs = refs[3:]
    xl, xa, keep_ref, give_ref, xbuf, taps_ref, sems = refs
    arrive()
    zh, zl = idx_ref[2], idx_ref[3]
    chans = xl.shape[1] // 2
    spots = xbuf.shape[0]
    window = at(zh * (xl.shape[0] - spots), spots, side)
    pairs = []
    for source, along in ((xl, zl), (xa, 1 - zl)):
        for up in range(2):
            pairs.append(
                (
                    source.at[window, up * chans : (up + 1) * chans],
                    xbuf.at[:, at((2 * up + along) * chans, chans, chans)],
                )
            )
    run_copies(pairs, sems)
    wide = gp_ref.shape[1]
    outs = wide // 2
    spot = lax.broadcasted_iota(jnp.int32, (spots, wide), 0) - zh * side
    grad = gp_ref[at(zh * (gp_ref.shape[0] - spots), spots, side), :].astype(f32)
    grad = jnp.where((spot >= 0) & (spot < half), grad, 0.0)
    bias = jnp.sum(grad, axis=0, keepdims=True)
    spread_taps(side, grad.astype(bf16), taps_ref)
    blocks = 2 * keep_ref.shape[0]
    depth = xbuf.shape[1]
    size = depth // blocks
    for begin in range(0, depth, 256):
        values = xbuf[:, begin : begin + 256]
        for y in range(3):
            place = side * (2 - y)
            part = dot(values, taps_ref[place : place + spots, :], TN)
            for x in range(3):
                for u in range(2):
                    col = x * wide + u * outs
                    put_blocks(
                        idx_ref, keep_ref, give_ref, part[:, col : col + outs],
                        3 * y + x, begin // size, size, u * (9 * size + 16),
                    )
    for u in range(2):
        row = jnp.broadcast_to(bias[:, u * outs : (u + 1) * outs], (16, outs)).astype(bf16)
        for j in range(keep_ref.shape[0]):
            spot = slice(u * (9 * size + 16) + 9 * size, (u + 1) * (9 * size + 16))
            keep_ref[j, spot, :] = row
            give_ref[j, spot, :] = row
    if flat:
        first = 2 * (9 * size + 16)
        flat_pieces(1.0, idx_ref, full_ref, go_ref, bias_ref, keep_ref, give_ref, first)


def weight_grad(side, half, idx, grad, act, act_other, chips, flat=()):
    spots = half + side
    wide = grad.shape[1]
    outs = wide // 2
    depth = 2 * act.shape[1]
    rows = 2 * (9 * depth // (2 * chips) + 16)
    if flat:
        rows += flat_size(flat[0], flat[1], chips)
    return call(
        functools.partial(weight_body, side, half, bool(flat)),
        "weight_grad",
        [(SMEM, idx), (LOAD, grad)] + [(LOAD, a) for a in flat] + [(FAR, act), (FAR, act_other)],
        [(VMEM, struct((chips, rows, outs), bf16))] * 2,
        [
            pltpu.VMEM((spots, depth), bf16),
            pltpu.VMEM((spots + 2 * side, 3 * wide), bf16),
            pltpu.SemaphoreType.DMA((4,)),
        ],
        spare=10,
    )


def weight_one_body(side, arrive, idx_ref, mine_ref, theirs_ref, x_ref, *refs):
    keep_ref, give_ref, gp_ref, taps_ref = refs
    arrive()
    zh = idx_ref[2]
    half, outs = mine_ref.shape
    gp_ref[at(zh * half, half, side), :] = mine_ref[...]
    gp_ref[at((1 - zh) * half, half, side), :] = theirs_ref[...]
    grad = gp_ref[...]
    bias = jnp.sum(grad.astype(f32), axis=0, keepdims=True)
    spread_taps(side, grad, taps_ref)
    blocks = 2 * keep_ref.shape[0]
    spots, depth = x_ref.shape
    size = depth // blocks
    right = tap_block(side, taps_ref, 0, spots)
    for begin in range(0, depth, 256):
        part = dot(x_ref[:, begin : begin + 256], right, TN)
        for tap in range(9):
            put_blocks(
                idx_ref, keep_ref, give_ref, part[:, tap * outs : (tap + 1) * outs],
                tap, begin // size, size,
            )
    row = jnp.broadcast_to(bias, (16, outs)).astype(bf16)
    first = 9 * size + 16
    for j in range(keep_ref.shape[0]):
        keep_ref[j, 9 * size : first, :] = row
        give_ref[j, 9 * size : first, :] = row


def weight_one_grad(side, idx, mine, theirs, act_zero, chips):
    spots, depth = act_zero.shape
    outs = mine.shape[1]
    rows = 9 * depth // (2 * chips) + 16
    return call(
        functools.partial(weight_one_body, side),
        "weight_one_grad",
        [(SMEM, idx), (LOAD, mine), (LOAD, theirs), (LOAD, act_zero)],
        [(VMEM, struct((chips, rows, outs), bf16))] * 2,
        [
            pltpu.VMEM((spots, outs), bf16),
            pltpu.VMEM((spots + 2 * side, 3 * outs), bf16),
        ],
        spare=14,
    )


def fold_body(pairs, arrive, idx_ref, *refs):
    arrive()
    ins, (keep_ref, give_ref) = refs[: 2 * pairs], refs[2 * pairs :]
    half = keep_ref.shape[0]
    for i in range(2 * half):
        target = keep_ref if i < half else give_ref
        begin = 0
        for keep, recv in zip(ins[0::2], ins[1::2]):
            rows = keep.shape[1]
            total = keep[i].astype(f32) + recv[i].astype(f32)
            target[i % half, begin : begin + rows, :] = total.astype(bf16)
            begin += rows


def fold(idx, *arrays):
    blocks, _, wide = arrays[0].shape
    rows = sum(a.shape[1] for a in arrays[0::2])
    return call(
        functools.partial(fold_body, len(arrays) // 2),
        "fold",
        [(SMEM, idx)] + [(LOAD, a) for a in arrays],
        [(VMEM, struct((blocks // 2, rows, wide), bf16))] * 2,
    )


def last_body(slotted, rest, arrive, idx_ref, keep_in, recv_in, *targets):
    arrive()
    zh = idx_ref[2]

    def put(target, place, begin, rows):
        spot = at(begin, rows, 16)
        total = keep_in[0, spot, :].astype(f32) + recv_in[0, spot, :].astype(f32)
        target[place : place + rows, :] = total.astype(bf16)

    place = 0
    for begin, rows in slotted:
        put(targets[0], place, begin + zh * rows, rows)
        put(targets[1], place, begin + (1 - zh) * rows, rows)
        place += rows
    begin, rows = rest
    put(targets[-1], 0, begin, rows)


def last_fold(idx, keep, recv, slotted=(), rest=None):
    wide = keep.shape[2]
    rest = rest or (0, keep.shape[1])
    rows = sum(size for _, size in slotted)
    sizes = ([rows, rows] if slotted else []) + [rest[1]]
    return call(
        functools.partial(last_body, slotted, rest),
        "last_fold",
        [(SMEM, idx), (LOAD, keep), (LOAD, recv)],
        [(VMEM, struct((size, wide), bf16)) for size in sizes],
    )


def final_body(parts, arrive, idx_ref, own_ref, sib_ref, *refs):
    arrive()
    outs, stages, sems = refs[: 2 * len(parts)], refs[2 * len(parts) : -1], refs[-1]
    chip, core = idx_ref[0], idx_ref[1]
    chips, _, wide = own_ref.shape
    first = 0
    copies = []

    def store(source, target):
        copies.append(pltpu.make_async_copy(source, target, sems.at[len(copies)]))
        copies[-1].start()

    for n, part in enumerate(parts):
        grad_ref, bias_ref, stage = outs[2 * n], outs[2 * n + 1], stages[n]
        size = part[0] // (2 * chips)
        columns = 1 if len(part) == 1 else part[1] // wide
        end = first + size * (9 if len(part) == 1 else columns)
        for c in range(columns):
            row = own_ref[0, end + c : end + c + 1, :].astype(f32)
            bias_ref[:, c * wide : (c + 1) * wide] = row
        for n_row, begin in enumerate(range(first, end, size)):
            for j in range(chips):
                for source, owner in ((own_ref, core), (sib_ref, 1 - core)):
                    home = chip ^ mask_of(j, owner, chips)
                    spot = at((2 * home + owner) * size, size, size)
                    piece = source[j, begin : begin + size, :].astype(f32)
                    if len(part) == 1:
                        stage[n_row, spot, :] = piece
                    else:
                        stage[spot, n_row * wide : (n_row + 1) * wide] = piece
            if len(part) == 1:
                store(stage.at[n_row], grad_ref.at[n_row])
        if len(part) > 1:
            store(stage, grad_ref)
        first = end + 16
    for copy in copies:
        copy.wait()


def final_grads(idx, own, sib, parts):
    wide = own.shape[2]
    results, stages = [], []
    for part in parts:
        shape = (9, part[0], wide) if len(part) == 1 else part
        results += [(FAR, struct(shape, f32)), (VMEM, struct((1, shape[-1]), f32))]
        stages.append(pltpu.VMEM(shape, f32))
    copies = sum(9 if len(part) == 1 else 1 for part in parts)
    return call(
        functools.partial(final_body, parts),
        "final_grads",
        [(SMEM, idx), (LOAD, own), (LOAD, sib)],
        results,
        stages + [pltpu.SemaphoreType.DMA((copies,))],
    )


def flat_pieces(gain, idx_ref, x_ref, go_ref, bias_ref, keep_ref, give_ref, first):
    chip, core = idx_ref[0], idx_ref[1]
    chips, _, wide = keep_ref.shape
    columns = go_ref.shape[1] // wide
    size = x_ref.shape[1] // (2 * chips)
    bias = jnp.concatenate(
        [bias_ref[:, c * wide : (c + 1) * wide] for c in range(columns)]
        + [jnp.zeros((16 - columns, wide), f32)],
        axis=0,
    ).astype(bf16)
    for j in range(chips):
        keep_ref[j, first + columns * size :, :] = bias
        give_ref[j, first + columns * size :, :] = bias
    for begin in range(0, x_ref.shape[1], 256):
        part = gain * dot(x_ref[:, begin : begin + 256], go_ref[...], TN)
        for b in range(0, 256 // size, 2):
            mask = chip ^ ((begin // size + b) // 2)
            slot = slot_of(mask, core, chips)
            give_slot = slot_of(mask, 1 - core, chips)
            for c in range(columns):
                even = part[b * size : (b + 1) * size, c * wide : (c + 1) * wide]
                odd = part[(b + 1) * size : (b + 2) * size, c * wide : (c + 1) * wide]
                spot = slice(first + c * size, first + (c + 1) * size)
                keep_ref[slot, spot, :] = jnp.where(core == 0, even, odd).astype(bf16)
                give_ref[give_slot, spot, :] = jnp.where(core == 0, odd, even).astype(bf16)


def flat_size(x, go, chips):
    return (go.shape[1] // 128) * (x.shape[1] // (2 * chips)) + 16


def outer_body(gain, arrive, idx_ref, x_ref, go_ref, bias_ref, keep_ref, give_ref):
    arrive()
    flat_pieces(gain, idx_ref, x_ref, go_ref, bias_ref, keep_ref, give_ref, 0)


def outer(idx, x, go, gain, bias, chips):
    return call(
        functools.partial(outer_body, gain),
        "outer",
        [(SMEM, idx), (LOAD, x), (LOAD, go), (LOAD, bias)],
        [(VMEM, struct((chips, flat_size(x, go, chips), 128), bf16))] * 2,
        spare=8,
    )


def start_body(arrive, idx_ref, valid_ref, cot_ref, outk_ref, go_ref, bias_ref, own_ref, give_ref):
    arrive()
    zl = idx_ref[3]
    masked = cot_ref[...].astype(f32) * valid_ref[0]
    go_ref[...] = masked.astype(bf16)
    bias_ref[...] = jnp.sum(masked, axis=0, keepdims=True)
    chans = outk_ref.shape[0] // 4
    block = cot_ref.shape[0] // 4
    for target, along in ((give_ref, 1 - zl), (own_ref, zl)):
        weights = jnp.concatenate(
            [outk_ref[at((2 * up + along) * chans, chans, chans), :] for up in range(2)], axis=0
        )
        for begin in range(0, cot_ref.shape[0], block):
            part = post_gain * dot(go_ref[begin : begin + block, :], weights, NT)
            target[begin : begin + block, :] = part.astype(target.dtype)


def start_back(idx, valid, cot, outk):
    spots, outs = cot.shape
    half = outk.shape[0] // 2
    return call(
        start_body,
        "start_back",
        [(SMEM, idx), (SMEM, valid), (LOAD, cot), (LOAD, outk)],
        [
            (VMEM, struct(cot.shape, bf16)),
            (VMEM, struct((1, outs), f32)),
            (VMEM, struct((spots, half), f32)),
            (VMEM, struct((spots, half), bf16)),
        ],
    )


def rows_body(side, arrive, idx_ref, own_ref, recv_ref, keep_ref, give_ref):
    arrive()
    zh = idx_ref[2]
    spots = keep_ref.shape[0]
    apart = own_ref.shape[0] - spots
    for target, begin in ((give_ref, (1 - zh) * apart), (keep_ref, zh * apart)):
        spot = at(begin, spots, side)
        total = own_ref[spot, :] + recv_ref[spot, :].astype(f32)
        target[...] = total.astype(target.dtype)


def rows_sum(side, idx, own, recv, spots):
    shape = (spots, own.shape[1])
    return call(
        functools.partial(rows_body, side),
        "rows_sum",
        [(SMEM, idx), (LOAD, own), (LOAD, recv)],
        [(VMEM, struct(shape, f32)), (VMEM, struct(shape, bf16))],
    )


def slots_body(arrive, idx_ref, own_ref, recv_ref, keep_ref, give_ref):
    arrive()
    zh = idx_ref[2]
    for target, slot in ((give_ref, 1 - zh), (keep_ref, zh)):
        total = own_ref[slot] + recv_ref[slot].astype(f32)
        target[...] = total.astype(bf16)


def slots_sum(idx, own, recv):
    shape = struct(own.shape[1:], bf16)
    return call(
        slots_body,
        "slots_sum",
        [(SMEM, idx), (LOAD, own), (LOAD, recv)],
        [(VMEM, shape), (VMEM, shape)],
    )


def input_body(arrive, idx_ref, keep_ref, recv_ref, out_ref):
    arrive()
    zh = idx_ref[2]
    half = keep_ref.shape[0]
    out_ref[at(zh * half, half, half), :] = keep_ref[...]
    out_ref[at((1 - zh) * half, half, half), :] = recv_ref[...]


def input_grad(idx, keep, recv):
    half, chans = keep.shape
    return call(
        input_body,
        "input_grad",
        [(SMEM, idx), (LOAD, keep), (LOAD, recv)],
        [(VMEM, struct((2 * half, chans), bf16))],
    )


def whole_body(side, arrive, idx_ref, xl, xa, xh, xd, rh, rl, x_ref, act_ref, sems):
    arrive()
    zh, zl = idx_ref[2], idx_ref[3]
    chans = xl.shape[1]
    spots = xa.shape[0]
    rest = xl.shape[0] - spots
    window, outside = at(zh * rest, spots, side), at((1 - zh) * spots, rest, side)

    def cols(up, along):
        return at((2 * up + along) * chans, chans, chans)

    run_copies(
        [
            (xl, x_ref.at[:, cols(zh, zl)]),
            (xa, x_ref.at[window, cols(zh, 1 - zl)]),
            (xh, x_ref.at[window, cols(1 - zh, zl)]),
            (xd, x_ref.at[window, cols(1 - zh, 1 - zl)]),
            (rl.at[0], x_ref.at[outside, cols(zh, 1 - zl)]),
            (rh, x_ref.at[outside, cols(1 - zh, zl)]),
            (rl.at[1], x_ref.at[outside, cols(1 - zh, 1 - zl)]),
        ],
        sems,
    )
    block = x_ref.shape[0] // 8
    for begin in range(0, x_ref.shape[0], block):
        rows = slice(begin, begin + block)
        act_ref[rows, :] = gelu(x_ref[rows, :].astype(f32)).astype(bf16)


def whole_input(side, idx, *parts):
    spots, chans = parts[0].shape
    return call(
        functools.partial(whole_body, side),
        "whole_input",
        [(SMEM, idx)] + [(FAR, p) for p in parts],
        [(VMEM, struct((spots, 4 * chans), bf16))] * 2,
        [pltpu.SemaphoreType.DMA((7,))],
    )


def join_body(arrive, idx_ref, own, recv, far_own, far_recv, out, sems):
    arrive()
    zh, zl = idx_ref[2], idx_ref[3]
    half = own.shape[0]
    chans = own.shape[1] // 2
    pairs = []
    for source, up, along in ((own, zh, zl), (recv, zh, 1 - zl), (far_own, 1 - zh, zl), (far_recv, 1 - zh, 1 - zl)):
        for slot in range(2):
            spot = at((2 * slot + along) * chans, chans, chans)
            target = out.at[at(up * half, half, half), spot]
            pairs.append((source.at[:, slot * chans : (slot + 1) * chans], target))
    run_copies(pairs, sems)


def join(idx, *parts):
    half, wide = parts[0].shape
    return call(
        join_body,
        "join",
        [(SMEM, idx)] + [(FAR, p) for p in parts],
        [(VMEM, struct((2 * half, 2 * wide), bf16))],
        [pltpu.SemaphoreType.DMA((8,))],
    )


def finish_body(arrive, idx_ref, valid_ref, x_ref, act_ref, idk_ref, outk_ref, ib_ref, out_ref):
    arrive()
    block = x_ref.shape[0] // 4
    for begin in range(0, x_ref.shape[0], block):
        rows = slice(begin, begin + block)
        identity = dot(x_ref[rows, :], idk_ref[...]) + ib_ref[...]
        branch = dot(act_ref[rows, :], outk_ref[...])
        out_ref[rows, :] = ((identity + post_gain * branch) * valid_ref[0]).astype(bf16)


def finish(idx, valid, x, act, idk, outk, ib):
    outs = idk.shape[1]
    return call(
        finish_body,
        "finish",
        [(SMEM, idx), (SMEM, valid), (LOAD, x), (LOAD, act), (LOAD, idk), (LOAD, outk)]
        + [(VMEM, ib.reshape(1, outs))],
        [(VMEM, struct((x.shape[0], outs), bf16))],
        spare=8,
    )


def flip(value, axis):
    return lax.ppermute(value, axis, [(0, 1), (1, 0)])


def cross(value, step, chips):
    pairs = []
    for chip in range(chips):
        for core in range(2):
            other = chip ^ step_bits(core, chips)[step]
            pairs.append((2 * chip + core, 2 * other + core))
    return lax.ppermute(value, DP, pairs)


def hops(value, chips):
    blocks = [value]
    for i in range(1, chips):
        pairs = []
        for chip in range(chips):
            for core in range(2):
                bits = step_bits(core, chips)
                mask = sum(bit for n, bit in enumerate(bits) if i >> (len(bits) - 1 - n) & 1)
                pairs.append((2 * (chip ^ mask) + core, 2 * chip + core))
        blocks.append(lax.ppermute(value, DP, pairs))
    return blocks


def swap(pieces, axis):
    return lax.all_to_all(pieces, axis, split_axis=0, concat_axis=0, tiled=True)


def after(value, other):
    return lax.optimization_barrier((value, other))[0]


def rows_of(value, start, size):
    return lax.dynamic_slice_in_dim(value, start, size, 0)


def local(
    pixels,
    counts,
    kernel_one,
    bias_one,
    kernel_two,
    bias_two,
    kernel_three,
    bias_three,
    out_kernel,
    identity_kernel,
    identity_bias,
    cotangent,
):
    images, rows, width, chans = pixels.shape
    side = width // 2
    spots = side * side
    half = spots // 2
    window = half + halo * side
    outs = cotangent.shape[3]
    chips = lax.axis_size("chip")
    chip, core, zh, zl = [lax.axis_index(a) for a in ("chip", "core", "zh", "zl")]
    idx = jnp.stack([chip, core, zh, zl]).astype(jnp.int32)
    taps = lambda kernel: kernel.reshape((9,) + kernel.shape[2:])
    one, two, three = taps(kernel_one), taps(kernel_two), taps(kernel_three)

    own_count = lax.dynamic_index_in_dim(counts, 2 * chip + core, 0, keepdims=True)
    valid = (own_count > 0).astype(f32)

    place = 2 * chip + core

    def units_of(kernel, size):
        if kernel.ndim == 3:
            block = kernel.shape[1] // (2 * chips)
            return lax.dynamic_slice_in_dim(kernel, place * block, block, 1)
        block = kernel.shape[0] // (2 * chips)
        block = lax.dynamic_slice_in_dim(kernel, place * block, block, 0)
        block = block.reshape(-1, size, block.shape[1] // 128, 128)
        return block.transpose(2, 0, 1, 3).reshape(-1, size, 128)

    steps = chips.bit_length() - 1

    def start_spread(piece, *others):
        return jnp.concatenate(after((piece[None], cross(piece[None], steps - 1, chips)), others))

    def end_spread(own, *others):
        for step in reversed(range(steps - 1)):
            own = jnp.concatenate(after((own, cross(own, step, chips)), others))
        return own, flip(own, "core")

    last = [idx]

    def turn(*others):
        return after(idx, (last[0],) + others)

    def ran(results):
        last[0] = results[-1] if isinstance(results, (list, tuple)) else results
        return results

    size = two.shape[1] // (2 * chips)
    deep = two.shape[1]
    cot = cotangent.reshape(spots, outs)
    two_piece = flip(units_of(two, size), "zh")
    pooled = ran(pool(pixels))
    xl = swap(after(pooled, two_piece), DP).reshape(spots, chans)
    one_piece = flip(units_of(after(one, pooled), size), "zh")
    go, identity_bias_grad, ga_own, ga_give = ran(start_back(turn(), valid, cot, out_kernel))
    ga_recv = flip(ga_give, "zl")
    bias_other = flip(after(jnp.stack([bias_one, bias_two, bias_three]), go), "zh")
    last_piece = jnp.concatenate([units_of(after(k, pooled), size) for k in (three, identity_kernel)])
    cot_rows = rows_of(after(cot, pooled), (1 - zh) * half, half)

    apart = spots - window
    xa = flip(rows_of(xl, zh * apart, window), "zl")
    xh = flip(rows_of(xl, (1 - zh) * apart, window), "zh")
    two_near = start_spread(two_piece)
    ga_own, ga_give = ran(rows_sum(side, turn(bias_other), ga_own, ga_recv, window))
    rest = spots - window
    rest_own = rows_of(xl, (1 - zh) * window, rest)
    rest_high = rows_of(xl, zh * window, rest)
    one_near = start_spread(one_piece, xh, xa, two_near, last_piece, cot_rows, ga_own)
    xd = flip(xh, "zl")
    last_piece = flip(after(last_piece, xh), "zh")
    two_other = end_spread(two_near, xd)
    one_other = end_spread(one_near, xd, two_other[0], last_piece)
    ga_recv = flip(after(ga_give, xd), "zh")
    rest_high = flip(after(rest_high, xd), "zh")

    pre_one, act_one = ran(
        conv(
            side, turn(), (xl, xa, xh, xd), one, one_other, 0, bias_one, bias_other[0], True
        )
    )
    act_one_other = flip(act_one, "zl")
    pre_two, act_two = ran(
        conv(side, turn(ga_recv), (act_one, act_one_other), two, two_other, 0, bias_two, bias_other[1])
    )
    act_two_other = flip(act_two, "zl")
    last_other = jnp.stack(after(hops(after(last_piece, act_one), chips), act_two))
    last_other = last_other, flip(last_other, "core")
    pre_three, act_three = ran(
        conv(side, turn(), (act_two, act_two_other), three, last_other, 0, bias_three, bias_other[2])
    )
    rest_low = flip(jnp.stack(after((rest_own, rest_high), act_three)), "zl")
    cot_far = flip(after(cot_rows, act_three), "zh")
    own_rows = rows_of(act_three, zh * (halo - 3) * side, half)

    gp_three, ga_own, ga_give = ran(
        back(side, turn(), (ga_own, ga_recv, pre_three), three, last_other, 0)
    )
    ga_recv = flip(ga_give, "zl")
    full_x, act_zero = ran(whole_input(side, turn(), xl, xa, xh, xd, rest_high, rest_low))
    keep_three, give_three = ran(
        weight_grad(
            side, half, turn(), gp_three, act_two, act_two_other, chips, (full_x, go, identity_bias_grad)
        )
    )
    gp_two, ga_own, ga_give = ran(
        back(side, turn(), (ga_own, ga_recv, pre_two), two, two_other, 0)
    )
    ga_recv = flip(ga_give, "zl")
    keep_two, give_two = ran(weight_grad(side, half, turn(cot_far), gp_two, act_one, act_one_other, chips))

    gp_mine, gp_theirs, gp_one = ran(slope_back(side, turn(), ga_own, ga_recv, pre_one, half))
    gp_theirs = flip(gp_theirs, "zh")
    recv_three = flip(after(give_three, gp_one), "core")
    recv_two = flip(after(give_two, gp_one), "core")
    gx_own, gx_give = ran(
        back(
            side, turn(), (gp_one,), one, one_other, 0,
            (valid, full_x, go, cot_far, identity_kernel, last_other, half),
        )
    )

    def folds(keep, recv, first):
        for step in range(first, steps):
            keep, give = ran(fold(turn(), keep, recv))
            recv = cross(give, step, chips)
        return keep, recv

    keep_one, give_one = ran(weight_one_grad(side, turn(), gp_mine, gp_theirs, act_zero, chips))
    keep_deep, give_deep = ran(fold(turn(), keep_three, recv_three, keep_two, recv_two))
    recv_deep = cross(give_deep, 0, chips)
    recv_one = flip(give_one, "core")
    gx_recv = flip(after(gx_give, keep_one), "zl")
    own_rows = after(own_rows, keep_one)
    near_rows = flip(own_rows, "zl")
    far_rows = flip(own_rows, "zh")
    gx_keep, gx_give = ran(slots_sum(turn(), gx_own, gx_recv))
    gx_recv = flip(gx_give, "zh")
    far_near_rows = flip(after(far_rows, gx_keep), "zl")
    keep_deep, recv_deep = folds(keep_deep, recv_deep, 1)
    slot = 9 * size + 16
    flat = keep_three.shape[1] - 2 * slot
    keep_deep, give_deep, id_rows = ran(
        last_fold(
            turn(), keep_deep, recv_deep, ((0, slot), (2 * slot + flat, slot)), (2 * slot, flat)
        )
    )
    recv_deep = flip(give_deep, "zh")
    full_three = ran(join(turn(), own_rows, near_rows, far_rows, far_near_rows))
    keep_out, give_out = ran(outer(turn(), full_three, go, post_gain, identity_bias_grad, chips))
    recv_out = flip(give_out, "core")
    keep_one, give_one = ran(fold(turn(), keep_one, recv_one, keep_out, recv_out))
    recv_one = cross(give_one, 0, chips)
    block_out = ran(finish(turn(), valid, full_x, full_three, identity_kernel, out_kernel, identity_bias))
    keep_one, recv_one = folds(keep_one, recv_one, 1)
    deep_rows = (after(keep_deep, keep_one).astype(f32) + recv_deep.astype(f32)).astype(bf16)
    near_deep = start_spread(jnp.concatenate([deep_rows, id_rows]))
    (total_one,) = ran([last_fold(turn(), keep_one, recv_one)])
    near_one = start_spread(total_one)
    gx = ran(input_grad(turn(), gx_keep, gx_recv))
    gx = swap(gx.reshape(images, rows * width // 4, chans), DP)
    all_deep = end_spread(near_deep)
    pixels_grad = ran(widen(turn(near_one), gx, rows, width))
    all_one = end_spread(near_one, pixels_grad)
    kernel_one_grad, bias_one_grad, out_kernel_grad, _ = ran(
        final_grads(turn(), *all_one, ((one.shape[1],), out_kernel.shape))
    )
    (
        kernel_three_grad,
        bias_three_grad,
        kernel_two_grad,
        bias_two_grad,
        identity_kernel_grad,
        identity_bias_grad,
    ) = ran(final_grads(turn(), *all_deep, ((deep,), (deep,), identity_kernel.shape)))

    return (
        block_out.reshape(cotangent.shape),
        pixels_grad,
        kernel_one_grad.reshape(kernel_one.shape),
        bias_one_grad[0],
        kernel_two_grad.reshape(kernel_two.shape),
        bias_two_grad[0],
        kernel_three_grad.reshape(kernel_three.shape),
        bias_three_grad[0],
        out_kernel_grad,
        identity_kernel_grad,
        identity_bias_grad[0],
    )


def solution(mesh):
    members = mesh.devices.size // mesh.shape["mp"]
    fine = Mesh(
        mesh.devices.reshape(members // 2, 2, 2, mesh.shape["mp"] // 2),
        ("chip", "core", "zh", "zl"),
    )
    return jax.shard_map(
        local,
        mesh=fine,
        in_specs=(
            P(None, DP, None, MP),
            P(),
            P(None, None, None, MP),
            P(MP),
            P(None, None, None, MP),
            P(MP),
            P(None, None, None, MP),
            P(MP),
            P(None, MP),
            P(None, MP),
            P(MP),
            P(DP, None, None, MP),
        ),
        out_specs=(
            P(DP, None, None, MP),
            P(None, DP, None, MP),
            P(None, None, None, MP),
            P(MP),
            P(None, None, None, MP),
            P(MP),
            P(None, None, None, MP),
            P(MP),
            P(None, MP),
            P(None, MP),
            P(MP),
        ),
        check_vma=False,
    )
```

```python
import functools
import math

import jax
import jax.numpy as jnp
from jax import lax
from jax.experimental import pallas as pl
from jax.experimental.pallas import tpu as pltpu
from jax.sharding import Mesh
from jax.sharding import PartitionSpec as P


post_gain = 0.015625
slope = 0.7978845608028654
cubic = 0.044715
halo = 6
bf16 = jnp.bfloat16
f32 = jnp.float32
NT = (((1,), (1,)), ((), ()))
TN = (((0,), (0,)), ((), ()))
NN = (((1,), (0,)), ((), ()))
DP = ("chip", "core")
MP = ("zh", "zl")


def dot(left, right, dims=NN):
    return lax.dot_general(left, right, dims, preferred_element_type=f32)


def gelu(value):
    inner = jnp.tanh(slope * (value + cubic * value * value * value))
    return 0.5 * value * (1.0 + inner)


def gelu_slope(value):
    square = value * value
    inner = jnp.tanh(slope * value * (1.0 + cubic * square))
    climb = slope * (1.0 + 3.0 * cubic * square)
    return 0.5 * (1.0 + inner) + 0.5 * value * (1.0 - inner * inner) * climb


def struct(shape, kind):
    return jax.ShapeDtypeStruct(shape, kind)


def lanes(blocks):
    return blocks[0] if len(blocks) == 1 else jnp.concatenate(blocks, axis=1)


def step_bits(core, chips):
    bits = [1 << n for n in range(chips.bit_length() - 1)]
    for n in range(0, len(bits) - 1, 2) if core else ():
        bits[n], bits[n + 1] = bits[n + 1], bits[n]
    return bits


def mask_of(i, core, chips):
    masks = []
    for which in range(2):
        bits = step_bits(which, chips)
        masks.append(sum(bit for n, bit in enumerate(bits) if i >> (len(bits) - 1 - n) & 1))
    return jnp.where(core == 0, masks[0], masks[1])


def slot_of(mask, core, chips):
    slots = []
    for which in range(2):
        bits = step_bits(which, chips)
        slot = 0
        for n, bit in enumerate(bits):
            slot = slot + ((mask >> (bit.bit_length() - 1)) & 1) * (1 << (len(bits) - 1 - n))
        slots.append(slot)
    return jnp.where(core == 0, slots[0], slots[1])


VMEM = pl.BlockSpec(memory_space=pltpu.VMEM)
SMEM = pl.BlockSpec(memory_space=pltpu.SMEM)
FAR = pl.BlockSpec(memory_space=pl.ANY)
LOAD = "load"


def size_of(array):
    return math.prod(array.shape) * jnp.dtype(array.dtype).itemsize


def call(body, name, ins, outs, scratch=(), spare=6, **more):
    loads = [i for i, (space, _) in enumerate(ins) if space is LOAD]
    spaces = [FAR if space is LOAD else space for space, _ in ins]
    arrays = [array for _, array in ins]
    out_specs = [space for space, _ in outs]
    out_shape = [shape for _, shape in outs]
    held = [arrays[i] for i in loads]
    buffers = [pltpu.VMEM(array.shape, array.dtype) for array in held]
    sems = [pltpu.SemaphoreType.DMA((len(held),))] if held else []
    vmem = sum(size_of(array) for array in held)
    vmem += sum(size_of(a) for space, a in list(ins) + list(outs) if space is VMEM)
    vmem += sum(size_of(b) for b in scratch if b.memory_space == pltpu.VMEM)
    moved = sum(size_of(a) for a in arrays + out_shape)

    def wrapped(*refs):
        inputs = list(refs[: len(ins)])
        outputs = refs[len(ins) : len(ins) + len(outs)]
        rest = refs[len(ins) + len(outs) :]
        kept, tail = rest[: len(held)], rest[len(held) :]
        copies = []
        if held:
            sem, tail = tail[0], tail[1:]
            copies = [
                pltpu.make_async_copy(inputs[i], kept[n], sem.at[n]) for n, i in enumerate(loads)
            ]
        for copy in copies:
            copy.start()
        for n, i in enumerate(loads):
            inputs[i] = kept[n]

        def arrive():
            for copy in copies:
                copy.wait()

        body(arrive, *inputs, *outputs, *tail)

    single = len(outs) == 1
    return pl.pallas_call(
        wrapped,
        in_specs=spaces,
        out_specs=out_specs[0] if single else out_specs,
        out_shape=out_shape[0] if single else out_shape,
        scratch_shapes=buffers + sems + list(scratch),
        compiler_params=pltpu.CompilerParams(vmem_limit_bytes=vmem + (spare << 20)),
        cost_estimate=pl.CostEstimate(flops=0, bytes_accessed=moved, transcendentals=0),
        name=name,
        **more,
    )(*arrays)


def run_copies(pairs, sems):
    for copy in start_copies(pairs, sems):
        copy.wait()


def slice_copies(group, idx_ref, own, blocks, sibling, wbuf):
    chip, core, zh = idx_ref[0], idx_ref[1], idx_ref[2]
    size = blocks.shape[-2]
    pairs = [(own, wbuf.at[zh])]
    for j in range(blocks.shape[0]):
        for source, owner in ((blocks, core), (sibling, 1 - core)):
            home = chip ^ mask_of(j, owner, blocks.shape[0])
            spot = at((2 * home + owner) * size, size, size)
            pairs.append((source.at[j, 9 * group : 9 * group + 9], wbuf.at[1 - zh, :, spot, :]))
    return pairs


def flat_copies(first, idx_ref, blocks, sibling, buffer):
    chip, core = idx_ref[0], idx_ref[1]
    columns, units = buffer.shape[:2]
    chips = blocks.shape[0]
    count = units // (2 * chips)
    pairs = []
    for j in range(chips):
        for source, owner in ((blocks, core), (sibling, 1 - core)):
            home = chip ^ mask_of(j, owner, chips)
            spot = pl.ds((2 * home + owner) * count, count)
            for c in range(columns):
                begin = first + c * count
                pairs.append((source.at[j, begin : begin + count], buffer.at[c, spot]))
    return pairs


def start_copies(pairs, sems):
    copies = [pltpu.make_async_copy(a, b, sems.at[i]) for i, (a, b) in enumerate(pairs)]
    for copy in copies:
        copy.start()
    return copies


def flat_rows(buffer, begin, count):
    columns, _, size, wide = buffer.shape
    return lanes([buffer[c, pl.ds(begin, count)].reshape(count * size, wide) for c in range(columns)])


def halves(spots, side):
    first = (spots // side + 1) // 2 * side
    return ((0, first), (first, spots - first))


def columns_of(size, wide, side):
    return lax.rem(lax.broadcasted_iota(jnp.int32, (size, wide), 0), side)


def at(start, size, unit):
    return pl.ds(pl.multiple_of(start, unit), size)


def pool_body(arrive, x_ref, out_ref):
    arrive()
    rows, width, chans = x_ref.shape[1:]
    half = width // 2
    pixel = lax.broadcasted_iota(jnp.int32, (half, 2 * width), 1)
    place = lax.broadcasted_iota(jnp.int32, (half, 2 * width), 0)
    inside = (lax.rem(pixel, width) >= 2 * place) & (lax.rem(pixel, width) < 2 * place + 2)
    pick = jnp.where(inside, 0.25, 0.0).astype(bf16)
    for image in range(x_ref.shape[0]):
        for row in range(rows // 2):
            window = x_ref[image, 2 * row : 2 * row + 2].reshape(2 * width, chans)
            out_ref[image, row * half : (row + 1) * half, :] = dot(pick, window).astype(bf16)


def pool(pixels):
    images, rows, width, chans = pixels.shape
    shape = struct((images, rows * width // 4, chans), bf16)
    return call(pool_body, "pool", [(LOAD, pixels)], [(VMEM, shape)])


def widen_body(arrive, idx_ref, g_ref, out_ref):
    arrive()
    rows, width, chans = out_ref.shape[1:]
    half = width // 2
    pixel = lax.broadcasted_iota(jnp.int32, (width, half), 0)
    place = lax.broadcasted_iota(jnp.int32, (width, half), 1)
    inside = (pixel >= 2 * place) & (pixel < 2 * place + 2)
    pick = jnp.where(inside, 0.25, 0.0).astype(bf16)
    for image in range(g_ref.shape[0]):
        for row in range(rows // 2):
            wide = dot(pick, g_ref[image, row * half : (row + 1) * half, :]).astype(bf16)
            out_ref[image, 2 * row] = wide
            out_ref[image, 2 * row + 1] = wide


def widen(idx, grad, rows, width):
    images, spots, chans = grad.shape
    step = images // 4
    block = pl.BlockSpec((step, spots, chans), lambda i: (i, 0, 0))
    out = pl.BlockSpec((step, rows, width, chans), lambda i: (i, 0, 0, 0))
    return call(
        widen_body,
        "widen",
        [(SMEM, idx), (block, grad)],
        [(out, struct((images, rows, width, chans), bf16))],
        grid=(4,),
    )


def conv_body(side, first, group, arrive, idx_ref, *refs):
    zh, zl = idx_ref[2], idx_ref[3]
    if first:
        xl, xa, xh, xd, wl, wo, ws, bl, bo, pre_ref, act_ref, xbuf, wbuf, acc, sems = refs
        chans = xl.shape[1]
        spots = xbuf.shape[0]
        begin = zh * (xl.shape[0] - spots)
        pairs = []
        for source, up, along in ((xl, zh, zl), (xa, zh, 1 - zl), (xh, 1 - zh, zl), (xd, 1 - zh, 1 - zl)):
            if source is xl:
                source = xl.at[at(begin, spots, side), :]
            pairs.append((source, xbuf.at[:, at((2 * up + along) * chans, chans, chans)]))
    else:
        xl, xa, wl, wo, ws, bl, bo, pre_ref, act_ref, xbuf, wbuf, acc, sems = refs
        chans = xl.shape[1] // 2
        spots = xbuf.shape[0]
        pairs = []
        for source, along in ((xl, zl), (xa, 1 - zl)):
            for up in range(2):
                pairs.append(
                    (
                        source.at[:, up * chans : (up + 1) * chans],
                        xbuf.at[:, at((2 * up + along) * chans, chans, chans)],
                    )
                )
    run_copies(slice_copies(group, idx_ref, wl, wo, ws, wbuf) + pairs, sems)
    arrive()
    acc[...] = jnp.zeros_like(acc)
    outs = 2 * wl.shape[2]
    for x in range(3):
        weights = lanes([wbuf[u, 3 * y + x] for y in range(3) for u in range(2)])
        for begin, block in halves(spots, side):
            values = xbuf[begin : begin + block, :]
            if first:
                values = gelu(values.astype(f32)).astype(bf16)
            product = dot(values, weights)
            for y in range(3):
                place = begin + side * (2 - y)
                acc[x, place : place + block, :] += product[:, y * outs : (y + 1) * outs]
    own, other = bl[...], bo[...]
    bias = lanes([jnp.where(zh == 0, own, other), jnp.where(zh == 0, other, own)])
    for begin, block in halves(act_ref.shape[0], side):
        column = columns_of(block, outs, side)
        spot = at(begin + side + zh * side, block, side)
        left = pltpu.roll(acc[0, spot, :], 1, 0)
        right = pltpu.roll(acc[2, spot, :], block - 1, 0)
        pre = acc[1, spot, :] + bias
        pre = pre + jnp.where(column > 0, left, 0.0)
        pre = pre + jnp.where(column < side - 1, right, 0.0)
        pre_ref[begin : begin + block, :] = pre
        act_ref[begin : begin + block, :] = gelu(pre).astype(bf16)


def conv(side, idx, sources, own, other, group, bias, bias_other, first=False):
    taps, depth, outs = own.shape
    spots = sources[1].shape[0]
    rows = spots - side
    return call(
        functools.partial(conv_body, side, first, group),
        "conv",
        [(SMEM, idx)]
        + [(FAR, s) for s in sources]
        + [(FAR, own), (FAR, other[0]), (FAR, other[1])]
        + [(VMEM, bias.reshape(1, outs)), (VMEM, bias_other.reshape(1, outs))],
        [(VMEM, struct((rows, 2 * outs), f32)), (VMEM, struct((rows, 2 * outs), bf16))],
        [
            pltpu.VMEM((spots, depth), bf16),
            pltpu.VMEM((2, taps, depth, outs), bf16),
            pltpu.VMEM((3, spots + 2 * side, 2 * outs), f32),
            pltpu.SemaphoreType.DMA((2 * other[0].shape[0] + 5,)),
        ],
        spare=14 if first else 8,
    )


def spread_taps(side, grad, taps_ref):
    pixels, outs = grad.shape
    column = columns_of(pixels, outs, side)
    wide = grad.astype(f32)
    ahead = jnp.where(column < side - 1, pltpu.roll(wide, pixels - 1, 0), 0.0).astype(bf16)
    behind = jnp.where(column > 0, pltpu.roll(wide, 1, 0), 0.0).astype(bf16)
    edge = jnp.zeros((side, 3 * outs), bf16)
    taps_ref[:side, :] = edge
    taps_ref[side + pixels :, :] = edge
    taps_ref[side : side + pixels, :] = jnp.concatenate([ahead, grad, behind], axis=1)


def tap_block(side, taps_ref, begin, block):
    return lanes([taps_ref[at(begin + side * (2 - y), block, side), :] for y in range(3)])


def slope_body(side, arrive, idx_ref, keep_ref, recv_ref, pre_ref, mine_ref, theirs_ref, gp_ref):
    arrive()
    zh = idx_ref[2]
    half, outs = mine_ref.shape
    total = keep_ref[...] + recv_ref[...].astype(f32)
    spots = keep_ref.shape[0]
    pre = pre_ref[at(zh * (pre_ref.shape[0] - spots), spots, side), :]
    gp_ref[...] = (total * gelu_slope(pre)).astype(bf16)
    own = gp_ref[at(zh * (gp_ref.shape[0] - half), half, side), :]
    low, high = own[:, :outs], own[:, outs:]
    mine_ref[...] = jnp.where(zh == 0, low, high)
    theirs_ref[...] = jnp.where(zh == 0, high, low)


def slope_back(side, idx, keep, recv, pre, half):
    outs = pre.shape[1] // 2
    return call(
        functools.partial(slope_body, side),
        "slope_back",
        [(SMEM, idx), (LOAD, keep), (LOAD, recv), (LOAD, pre)],
        [
            (VMEM, struct((half, outs), bf16)),
            (VMEM, struct((half, outs), bf16)),
            (VMEM, struct(keep.shape, bf16)),
        ],
    )


def back_body(side, last, group, arrive, idx_ref, *refs):
    zh, zl = idx_ref[2], idx_ref[3]
    if last:
        valid_ref, grad_ref, x_ref, go_ref, far_ref, idk_ref, wl, wo, ws, po, ps = refs[:11]
        own_ref, give_ref, taps_ref, wbuf, idk_far, sems = refs[11:]
    else:
        keep_ref, recv_ref, pre_ref, wl, wo, ws, gp_ref, own_ref, give_ref, taps_ref, wbuf, sems = refs
    pairs = slice_copies(group, idx_ref, wl, wo, ws, wbuf)
    if last:
        pairs += flat_copies(9, idx_ref, po, ps, idk_far)
    copies = start_copies(pairs, sems)
    arrive()
    if last:
        grad = grad_ref[...]
    else:
        spots = gp_ref.shape[0]

        def window(ref):
            return ref[at(zh * (ref.shape[0] - spots), spots, side), :]

        total = window(keep_ref) + window(recv_ref).astype(f32)
        grad = (total * gelu_slope(window(pre_ref))).astype(bf16)
        gp_ref[...] = grad
    spread_taps(side, grad, taps_ref)
    depth, outs = wl.shape[1:]
    pixels = own_ref.shape[-2]
    start = zh * side
    for copy in copies:
        copy.wait()
    chans = depth // 4

    def rows(index):
        spot = at(index * chans, chans, chans)
        return lanes([wbuf[u, t, spot, :] for t in range(9) for u in range(2)])

    for target, along in ((give_ref, 1 - zl), (own_ref, zl)):
        if last:
            units = chans // idk_far.shape[2]
            for up in range(2):
                index = 2 * up + along
                weights = rows(index)
                near = idk_ref[at(index * chans, chans, chans), :]
                far = flat_rows(idk_far, index * units, units)
                apart = zh * (far_ref.shape[0] - pixels)
                for begin, block in halves(pixels, side):
                    here = at(zh * pixels + begin, block, side)
                    part = dot(tap_block(side, taps_ref, start + begin, block), weights, NT)
                    x = x_ref[here, at(index * chans, chans, chans)]
                    part = part * gelu_slope(x.astype(f32))
                    part = part + dot(go_ref[here, :], near, NT)
                    part = part + valid_ref[0] * dot(far_ref[at(apart + begin, block, side), :], far, NT)
                    target[up, begin : begin + block, :] = part.astype(target.dtype)
        else:
            weights = jnp.concatenate([rows(along), rows(2 + along)], axis=0)
            for begin, block in halves(pixels, side):
                part = dot(tap_block(side, taps_ref, start + begin, block), weights, NT)
                target[begin : begin + block, :] = part.astype(target.dtype)


def back(side, idx, sources, own, other, group, last=None):
    taps, depth, outs = own.shape
    spots = min(sources[0].shape[0], sources[-1].shape[0])
    copies = 2 * other[0].shape[0] + 1
    extra = []
    scratch = []
    if last:
        valid, full_x, go, cot_far, idk, pieces, half = last
        chans = depth // 4
        shape = (2, half, chans)
        results = []
        extra = [(FAR, pieces[0]), (FAR, pieces[1])]
        sources = list(sources) + [full_x, go, cot_far, idk]
        columns, size = idk.shape[1] // 128, pieces[0].shape[2]
        scratch = [pltpu.VMEM((columns, depth // size, size, 128), bf16)]
        copies += 2 * other[0].shape[0] * columns
    else:
        shape = (spots - side, depth // 2)
        results = [(VMEM, struct((spots, 2 * outs), bf16))]
    results += [(VMEM, struct(shape, f32)), (VMEM, struct(shape, bf16))]
    return call(
        functools.partial(back_body, side, bool(last), group),
        "back",
        [(SMEM, idx)]
        + ([(SMEM, last[0])] if last else [])
        + [(LOAD, source) for source in sources]
        + [(FAR, own), (FAR, other[0]), (FAR, other[1])]
        + extra,
        results,
        [pltpu.VMEM((spots + 2 * side, 6 * outs), bf16), pltpu.VMEM((2, taps, depth, outs), bf16)]
        + scratch
        + [pltpu.SemaphoreType.DMA((copies,))],
        spare=14 if last else 10,
    )


def put_blocks(idx_ref, keep_ref, give_ref, part, tap, first_block, size, begin=0):
    chip, core = idx_ref[0], idx_ref[1]
    for b in range(0, part.shape[0] // size, 2):
        even = part[b * size : (b + 1) * size, :]
        odd = part[(b + 1) * size : (b + 2) * size, :]
        mask = chip ^ ((first_block + b) // 2)
        slot = slot_of(mask, core, keep_ref.shape[0])
        give_slot = slot_of(mask, 1 - core, keep_ref.shape[0])
        rows = slice(begin + tap * size, begin + (tap + 1) * size)
        keep_ref[slot, rows, :] = jnp.where(core == 0, even, odd).astype(bf16)
        give_ref[give_slot, rows, :] = jnp.where(core == 0, odd, even).astype(bf16)


def weight_body(side, half, flat, arrive, idx_ref, gp_ref, *refs):
    if flat:
        full_ref, go_ref, bias_ref = refs[:3]
        refs = refs[3:]
    xl, xa, keep_ref, give_ref, xbuf, taps_ref, sems = refs
    arrive()
    zh, zl = idx_ref[2], idx_ref[3]
    chans = xl.shape[1] // 2
    spots = xbuf.shape[0]
    window = at(zh * (xl.shape[0] - spots), spots, side)
    pairs = []
    for source, along in ((xl, zl), (xa, 1 - zl)):
        for up in range(2):
            pairs.append(
                (
                    source.at[window, up * chans : (up + 1) * chans],
                    xbuf.at[:, at((2 * up + along) * chans, chans, chans)],
                )
            )
    run_copies(pairs, sems)
    wide = gp_ref.shape[1]
    outs = wide // 2
    spot = lax.broadcasted_iota(jnp.int32, (spots, wide), 0) - zh * side
    grad = gp_ref[at(zh * (gp_ref.shape[0] - spots), spots, side), :].astype(f32)
    grad = jnp.where((spot >= 0) & (spot < half), grad, 0.0)
    bias = jnp.sum(grad, axis=0, keepdims=True)
    spread_taps(side, grad.astype(bf16), taps_ref)
    blocks = 2 * keep_ref.shape[0]
    depth = xbuf.shape[1]
    size = depth // blocks
    for begin in range(0, depth, 256):
        values = xbuf[:, begin : begin + 256]
        for y in range(3):
            place = side * (2 - y)
            part = dot(values, taps_ref[place : place + spots, :], TN)
            for x in range(3):
                for u in range(2):
                    col = x * wide + u * outs
                    put_blocks(
                        idx_ref, keep_ref, give_ref, part[:, col : col + outs],
                        3 * y + x, begin // size, size, u * (9 * size + 16),
                    )
    for u in range(2):
        row = jnp.broadcast_to(bias[:, u * outs : (u + 1) * outs], (16, outs)).astype(bf16)
        for j in range(keep_ref.shape[0]):
            spot = slice(u * (9 * size + 16) + 9 * size, (u + 1) * (9 * size + 16))
            keep_ref[j, spot, :] = row
            give_ref[j, spot, :] = row
    if flat:
        first = 2 * (9 * size + 16)
        flat_pieces(1.0, idx_ref, full_ref, go_ref, bias_ref, keep_ref, give_ref, first)


def weight_grad(side, half, idx, grad, act, act_other, chips, flat=()):
    spots = half + side
    wide = grad.shape[1]
    outs = wide // 2
    depth = 2 * act.shape[1]
    rows = 2 * (9 * depth // (2 * chips) + 16)
    if flat:
        rows += flat_size(flat[0], flat[1], chips)
    return call(
        functools.partial(weight_body, side, half, bool(flat)),
        "weight_grad",
        [(SMEM, idx), (LOAD, grad)] + [(LOAD, a) for a in flat] + [(FAR, act), (FAR, act_other)],
        [(VMEM, struct((chips, rows, outs), bf16))] * 2,
        [
            pltpu.VMEM((spots, depth), bf16),
            pltpu.VMEM((spots + 2 * side, 3 * wide), bf16),
            pltpu.SemaphoreType.DMA((4,)),
        ],
        spare=10,
    )


def weight_one_body(side, arrive, idx_ref, mine_ref, theirs_ref, x_ref, *refs):
    keep_ref, give_ref, gp_ref, taps_ref = refs
    arrive()
    zh = idx_ref[2]
    half, outs = mine_ref.shape
    gp_ref[at(zh * half, half, side), :] = mine_ref[...]
    gp_ref[at((1 - zh) * half, half, side), :] = theirs_ref[...]
    grad = gp_ref[...]
    bias = jnp.sum(grad.astype(f32), axis=0, keepdims=True)
    spread_taps(side, grad, taps_ref)
    blocks = 2 * keep_ref.shape[0]
    spots, depth = x_ref.shape
    size = depth // blocks
    right = tap_block(side, taps_ref, 0, spots)
    for begin in range(0, depth, 256):
        part = dot(x_ref[:, begin : begin + 256], right, TN)
        for tap in range(9):
            put_blocks(
                idx_ref, keep_ref, give_ref, part[:, tap * outs : (tap + 1) * outs],
                tap, begin // size, size,
            )
    row = jnp.broadcast_to(bias, (16, outs)).astype(bf16)
    first = 9 * size + 16
    for j in range(keep_ref.shape[0]):
        keep_ref[j, 9 * size : first, :] = row
        give_ref[j, 9 * size : first, :] = row


def weight_one_grad(side, idx, mine, theirs, act_zero, chips):
    spots, depth = act_zero.shape
    outs = mine.shape[1]
    rows = 9 * depth // (2 * chips) + 16
    return call(
        functools.partial(weight_one_body, side),
        "weight_one_grad",
        [(SMEM, idx), (LOAD, mine), (LOAD, theirs), (LOAD, act_zero)],
        [(VMEM, struct((chips, rows, outs), bf16))] * 2,
        [
            pltpu.VMEM((spots, outs), bf16),
            pltpu.VMEM((spots + 2 * side, 3 * outs), bf16),
        ],
        spare=14,
    )


def fold_body(pairs, arrive, idx_ref, *refs):
    arrive()
    ins, (keep_ref, give_ref) = refs[: 2 * pairs], refs[2 * pairs :]
    half = keep_ref.shape[0]
    for i in range(2 * half):
        target = keep_ref if i < half else give_ref
        begin = 0
        for keep, recv in zip(ins[0::2], ins[1::2]):
            rows = keep.shape[1]
            total = keep[i].astype(f32) + recv[i].astype(f32)
            target[i % half, begin : begin + rows, :] = total.astype(bf16)
            begin += rows


def fold(idx, *arrays):
    blocks, _, wide = arrays[0].shape
    rows = sum(a.shape[1] for a in arrays[0::2])
    return call(
        functools.partial(fold_body, len(arrays) // 2),
        "fold",
        [(SMEM, idx)] + [(LOAD, a) for a in arrays],
        [(VMEM, struct((blocks // 2, rows, wide), bf16))] * 2,
    )


def last_body(slotted, rest, arrive, idx_ref, keep_in, recv_in, *targets):
    arrive()
    zh = idx_ref[2]

    def put(target, place, begin, rows):
        spot = at(begin, rows, 16)
        total = keep_in[0, spot, :].astype(f32) + recv_in[0, spot, :].astype(f32)
        target[place : place + rows, :] = total.astype(bf16)

    place = 0
    for begin, rows in slotted:
        put(targets[0], place, begin + zh * rows, rows)
        put(targets[1], place, begin + (1 - zh) * rows, rows)
        place += rows
    begin, rows = rest
    put(targets[-1], 0, begin, rows)


def last_fold(idx, keep, recv, slotted=(), rest=None):
    wide = keep.shape[2]
    rest = rest or (0, keep.shape[1])
    rows = sum(size for _, size in slotted)
    sizes = ([rows, rows] if slotted else []) + [rest[1]]
    return call(
        functools.partial(last_body, slotted, rest),
        "last_fold",
        [(SMEM, idx), (LOAD, keep), (LOAD, recv)],
        [(VMEM, struct((size, wide), bf16)) for size in sizes],
    )


def final_body(parts, arrive, idx_ref, own_ref, sib_ref, *refs):
    arrive()
    outs, stages, sems = refs[: 2 * len(parts)], refs[2 * len(parts) : -1], refs[-1]
    chip, core = idx_ref[0], idx_ref[1]
    chips, _, wide = own_ref.shape
    first = 0
    copies = []

    def store(source, target):
        copies.append(pltpu.make_async_copy(source, target, sems.at[len(copies)]))
        copies[-1].start()

    for n, part in enumerate(parts):
        grad_ref, bias_ref, stage = outs[2 * n], outs[2 * n + 1], stages[n]
        size = part[0] // (2 * chips)
        columns = 1 if len(part) == 1 else part[1] // wide
        end = first + size * (9 if len(part) == 1 else columns)
        for c in range(columns):
            row = own_ref[0, end + c : end + c + 1, :].astype(f32)
            bias_ref[:, c * wide : (c + 1) * wide] = row
        for n_row, begin in enumerate(range(first, end, size)):
            for j in range(chips):
                for source, owner in ((own_ref, core), (sib_ref, 1 - core)):
                    home = chip ^ mask_of(j, owner, chips)
                    spot = at((2 * home + owner) * size, size, size)
                    piece = source[j, begin : begin + size, :].astype(f32)
                    if len(part) == 1:
                        stage[n_row, spot, :] = piece
                    else:
                        stage[spot, n_row * wide : (n_row + 1) * wide] = piece
            if len(part) == 1:
                store(stage.at[n_row], grad_ref.at[n_row])
        if len(part) > 1:
            store(stage, grad_ref)
        first = end + 16
    for copy in copies:
        copy.wait()


def final_grads(idx, own, sib, parts):
    wide = own.shape[2]
    results, stages = [], []
    for part in parts:
        shape = (9, part[0], wide) if len(part) == 1 else part
        results += [(FAR, struct(shape, f32)), (VMEM, struct((1, shape[-1]), f32))]
        stages.append(pltpu.VMEM(shape, f32))
    copies = sum(9 if len(part) == 1 else 1 for part in parts)
    return call(
        functools.partial(final_body, parts),
        "final_grads",
        [(SMEM, idx), (LOAD, own), (LOAD, sib)],
        results,
        stages + [pltpu.SemaphoreType.DMA((copies,))],
    )


def flat_pieces(gain, idx_ref, x_ref, go_ref, bias_ref, keep_ref, give_ref, first):
    chip, core = idx_ref[0], idx_ref[1]
    chips, _, wide = keep_ref.shape
    columns = go_ref.shape[1] // wide
    size = x_ref.shape[1] // (2 * chips)
    bias = jnp.concatenate(
        [bias_ref[:, c * wide : (c + 1) * wide] for c in range(columns)]
        + [jnp.zeros((16 - columns, wide), f32)],
        axis=0,
    ).astype(bf16)
    for j in range(chips):
        keep_ref[j, first + columns * size :, :] = bias
        give_ref[j, first + columns * size :, :] = bias
    for begin in range(0, x_ref.shape[1], 256):
        part = gain * dot(x_ref[:, begin : begin + 256], go_ref[...], TN)
        for b in range(0, 256 // size, 2):
            mask = chip ^ ((begin // size + b) // 2)
            slot = slot_of(mask, core, chips)
            give_slot = slot_of(mask, 1 - core, chips)
            for c in range(columns):
                even = part[b * size : (b + 1) * size, c * wide : (c + 1) * wide]
                odd = part[(b + 1) * size : (b + 2) * size, c * wide : (c + 1) * wide]
                spot = slice(first + c * size, first + (c + 1) * size)
                keep_ref[slot, spot, :] = jnp.where(core == 0, even, odd).astype(bf16)
                give_ref[give_slot, spot, :] = jnp.where(core == 0, odd, even).astype(bf16)


def flat_size(x, go, chips):
    return (go.shape[1] // 128) * (x.shape[1] // (2 * chips)) + 16


def outer_body(gain, arrive, idx_ref, x_ref, go_ref, bias_ref, keep_ref, give_ref):
    arrive()
    flat_pieces(gain, idx_ref, x_ref, go_ref, bias_ref, keep_ref, give_ref, 0)


def outer(idx, x, go, gain, bias, chips):
    return call(
        functools.partial(outer_body, gain),
        "outer",
        [(SMEM, idx), (LOAD, x), (LOAD, go), (LOAD, bias)],
        [(VMEM, struct((chips, flat_size(x, go, chips), 128), bf16))] * 2,
        spare=8,
    )


def start_body(arrive, idx_ref, valid_ref, cot_ref, outk_ref, go_ref, bias_ref, own_ref, give_ref):
    arrive()
    zl = idx_ref[3]
    masked = cot_ref[...].astype(f32) * valid_ref[0]
    go_ref[...] = masked.astype(bf16)
    bias_ref[...] = jnp.sum(masked, axis=0, keepdims=True)
    chans = outk_ref.shape[0] // 4
    block = cot_ref.shape[0] // 4
    for target, along in ((give_ref, 1 - zl), (own_ref, zl)):
        weights = jnp.concatenate(
            [outk_ref[at((2 * up + along) * chans, chans, chans), :] for up in range(2)], axis=0
        )
        for begin in range(0, cot_ref.shape[0], block):
            part = post_gain * dot(go_ref[begin : begin + block, :], weights, NT)
            target[begin : begin + block, :] = part.astype(target.dtype)


def start_back(idx, valid, cot, outk):
    spots, outs = cot.shape
    half = outk.shape[0] // 2
    return call(
        start_body,
        "start_back",
        [(SMEM, idx), (SMEM, valid), (LOAD, cot), (LOAD, outk)],
        [
            (VMEM, struct(cot.shape, bf16)),
            (VMEM, struct((1, outs), f32)),
            (VMEM, struct((spots, half), f32)),
            (VMEM, struct((spots, half), bf16)),
        ],
    )


def rows_body(side, arrive, idx_ref, own_ref, recv_ref, keep_ref, give_ref):
    arrive()
    zh = idx_ref[2]
    spots = keep_ref.shape[0]
    apart = own_ref.shape[0] - spots
    for target, begin in ((give_ref, (1 - zh) * apart), (keep_ref, zh * apart)):
        spot = at(begin, spots, side)
        total = own_ref[spot, :] + recv_ref[spot, :].astype(f32)
        target[...] = total.astype(target.dtype)


def rows_sum(side, idx, own, recv, spots):
    shape = (spots, own.shape[1])
    return call(
        functools.partial(rows_body, side),
        "rows_sum",
        [(SMEM, idx), (LOAD, own), (LOAD, recv)],
        [(VMEM, struct(shape, f32)), (VMEM, struct(shape, bf16))],
    )


def slots_body(arrive, idx_ref, own_ref, recv_ref, keep_ref, give_ref):
    arrive()
    zh = idx_ref[2]
    for target, slot in ((give_ref, 1 - zh), (keep_ref, zh)):
        total = own_ref[slot] + recv_ref[slot].astype(f32)
        target[...] = total.astype(bf16)


def slots_sum(idx, own, recv):
    shape = struct(own.shape[1:], bf16)
    return call(
        slots_body,
        "slots_sum",
        [(SMEM, idx), (LOAD, own), (LOAD, recv)],
        [(VMEM, shape), (VMEM, shape)],
    )


def input_body(arrive, idx_ref, keep_ref, recv_ref, out_ref):
    arrive()
    zh = idx_ref[2]
    half = keep_ref.shape[0]
    out_ref[at(zh * half, half, half), :] = keep_ref[...]
    out_ref[at((1 - zh) * half, half, half), :] = recv_ref[...]


def input_grad(idx, keep, recv):
    half, chans = keep.shape
    return call(
        input_body,
        "input_grad",
        [(SMEM, idx), (LOAD, keep), (LOAD, recv)],
        [(VMEM, struct((2 * half, chans), bf16))],
    )


def whole_body(side, arrive, idx_ref, xl, xa, xh, xd, rh, rl, x_ref, act_ref, sems):
    arrive()
    zh, zl = idx_ref[2], idx_ref[3]
    chans = xl.shape[1]
    spots = xa.shape[0]
    rest = xl.shape[0] - spots
    window, outside = at(zh * rest, spots, side), at((1 - zh) * spots, rest, side)

    def cols(up, along):
        return at((2 * up + along) * chans, chans, chans)

    run_copies(
        [
            (xl, x_ref.at[:, cols(zh, zl)]),
            (xa, x_ref.at[window, cols(zh, 1 - zl)]),
            (xh, x_ref.at[window, cols(1 - zh, zl)]),
            (xd, x_ref.at[window, cols(1 - zh, 1 - zl)]),
            (rl.at[0], x_ref.at[outside, cols(zh, 1 - zl)]),
            (rh, x_ref.at[outside, cols(1 - zh, zl)]),
            (rl.at[1], x_ref.at[outside, cols(1 - zh, 1 - zl)]),
        ],
        sems,
    )
    block = x_ref.shape[0] // 8
    for begin in range(0, x_ref.shape[0], block):
        rows = slice(begin, begin + block)
        act_ref[rows, :] = gelu(x_ref[rows, :].astype(f32)).astype(bf16)


def whole_input(side, idx, *parts):
    spots, chans = parts[0].shape
    return call(
        functools.partial(whole_body, side),
        "whole_input",
        [(SMEM, idx)] + [(FAR, p) for p in parts],
        [(VMEM, struct((spots, 4 * chans), bf16))] * 2,
        [pltpu.SemaphoreType.DMA((7,))],
    )


def join_body(arrive, idx_ref, own, recv, far_own, far_recv, out, sems):
    arrive()
    zh, zl = idx_ref[2], idx_ref[3]
    half = own.shape[0]
    chans = own.shape[1] // 2
    pairs = []
    for source, up, along in ((own, zh, zl), (recv, zh, 1 - zl), (far_own, 1 - zh, zl), (far_recv, 1 - zh, 1 - zl)):
        for slot in range(2):
            spot = at((2 * slot + along) * chans, chans, chans)
            target = out.at[at(up * half, half, half), spot]
            pairs.append((source.at[:, slot * chans : (slot + 1) * chans], target))
    run_copies(pairs, sems)


def join(idx, *parts):
    half, wide = parts[0].shape
    return call(
        join_body,
        "join",
        [(SMEM, idx)] + [(FAR, p) for p in parts],
        [(VMEM, struct((2 * half, 2 * wide), bf16))],
        [pltpu.SemaphoreType.DMA((8,))],
    )


def finish_body(arrive, idx_ref, valid_ref, x_ref, act_ref, idk_ref, outk_ref, ib_ref, out_ref):
    arrive()
    block = x_ref.shape[0] // 4
    for begin in range(0, x_ref.shape[0], block):
        rows = slice(begin, begin + block)
        identity = dot(x_ref[rows, :], idk_ref[...]) + ib_ref[...]
        branch = dot(act_ref[rows, :], outk_ref[...])
        out_ref[rows, :] = ((identity + post_gain * branch) * valid_ref[0]).astype(bf16)


def finish(idx, valid, x, act, idk, outk, ib):
    outs = idk.shape[1]
    return call(
        finish_body,
        "finish",
        [(SMEM, idx), (SMEM, valid), (LOAD, x), (LOAD, act), (LOAD, idk), (LOAD, outk)]
        + [(VMEM, ib.reshape(1, outs))],
        [(VMEM, struct((x.shape[0], outs), bf16))],
        spare=8,
    )


def flip(value, axis):
    return lax.ppermute(value, axis, [(0, 1), (1, 0)])


def cross(value, step, chips):
    pairs = []
    for chip in range(chips):
        for core in range(2):
            other = chip ^ step_bits(core, chips)[step]
            pairs.append((2 * chip + core, 2 * other + core))
    return lax.ppermute(value, DP, pairs)


def hops(value, chips):
    blocks = [value]
    for i in range(1, chips):
        pairs = []
        for chip in range(chips):
            for core in range(2):
                bits = step_bits(core, chips)
                mask = sum(bit for n, bit in enumerate(bits) if i >> (len(bits) - 1 - n) & 1)
                pairs.append((2 * (chip ^ mask) + core, 2 * chip + core))
        blocks.append(lax.ppermute(value, DP, pairs))
    return blocks


def swap(pieces, axis):
    return lax.all_to_all(pieces, axis, split_axis=0, concat_axis=0, tiled=True)


def after(value, other):
    return lax.optimization_barrier((value, other))[0]


def rows_of(value, start, size):
    return lax.dynamic_slice_in_dim(value, start, size, 0)


def local(
    pixels,
    counts,
    kernel_one,
    bias_one,
    kernel_two,
    bias_two,
    kernel_three,
    bias_three,
    out_kernel,
    identity_kernel,
    identity_bias,
    cotangent,
):
    images, rows, width, chans = pixels.shape
    side = width // 2
    spots = side * side
    half = spots // 2
    window = half + halo * side
    outs = cotangent.shape[3]
    chips = lax.axis_size("chip")
    chip, core, zh, zl = [lax.axis_index(a) for a in ("chip", "core", "zh", "zl")]
    idx = jnp.stack([chip, core, zh, zl]).astype(jnp.int32)
    taps = lambda kernel: kernel.reshape((9,) + kernel.shape[2:])
    one, two, three = taps(kernel_one), taps(kernel_two), taps(kernel_three)

    own_count = lax.dynamic_index_in_dim(counts, 2 * chip + core, 0, keepdims=True)
    valid = (own_count > 0).astype(f32)

    place = 2 * chip + core

    def units_of(kernel, size):
        if kernel.ndim == 3:
            block = kernel.shape[1] // (2 * chips)
            return lax.dynamic_slice_in_dim(kernel, place * block, block, 1)
        block = kernel.shape[0] // (2 * chips)
        block = lax.dynamic_slice_in_dim(kernel, place * block, block, 0)
        block = block.reshape(-1, size, block.shape[1] // 128, 128)
        return block.transpose(2, 0, 1, 3).reshape(-1, size, 128)

    steps = chips.bit_length() - 1

    def start_spread(piece, *others):
        return jnp.concatenate(after((piece[None], cross(piece[None], steps - 1, chips)), others))

    def end_spread(own, *others):
        for step in reversed(range(steps - 1)):
            own = jnp.concatenate(after((own, cross(own, step, chips)), others))
        return own, flip(own, "core")

    last = [idx]

    def turn(*others):
        return after(idx, (last[0],) + others)

    def ran(results):
        last[0] = results[-1] if isinstance(results, (list, tuple)) else results
        return results

    size = two.shape[1] // (2 * chips)
    deep = two.shape[1]
    cot = cotangent.reshape(spots, outs)
    two_piece = flip(units_of(two, size), "zh")
    pooled = ran(pool(pixels))
    xl = swap(after(pooled, two_piece), DP).reshape(spots, chans)
    one_piece = flip(units_of(after(one, two_piece), size), "zh")
    go, identity_bias_grad, ga_own, ga_give = ran(start_back(turn(), valid, cot, out_kernel))
    bias_other = flip(after(jnp.stack([bias_one, bias_two, bias_three]), go), "zh")
    last_piece = jnp.concatenate([units_of(after(k, pooled), size) for k in (three, identity_kernel)])
    cot_rows = rows_of(after(cot, pooled), (1 - zh) * half, half)

    apart = spots - window
    xa = flip(rows_of(xl, zh * apart, window), "zl")
    xh = flip(rows_of(xl, (1 - zh) * apart, window), "zh")
    two_near = start_spread(two_piece)
    rest = spots - window
    rest_own = rows_of(xl, (1 - zh) * window, rest)
    rest_high = rows_of(xl, zh * window, rest)
    one_near = start_spread(one_piece, xh, xa, two_near, last_piece, cot_rows, ga_give, bias_other)
    xd = flip(xh, "zl")
    last_piece = flip(after(last_piece, xh), "zh")
    two_other = end_spread(two_near, xd)
    one_other = end_spread(one_near, xd, two_other[0])
    ga_recv = flip(after(ga_give, xd), "zl")
    rest_high = flip(after(rest_high, xd), "zh")

    pre_one, act_one = ran(
        conv(
            side, turn(), (xl, xa, xh, xd), one, one_other, 0, bias_one, bias_other[0], True
        )
    )
    act_one_other = flip(act_one, "zl")
    ga_own, ga_give = ran(rows_sum(side, turn(), ga_own, ga_recv, half + (halo - 3) * side))
    pre_two, act_two = ran(
        conv(side, turn(), (act_one, act_one_other), two, two_other, 0, bias_two, bias_other[1])
    )
    act_two_other = flip(act_two, "zl")
    ga_recv = flip(after(ga_give, act_two), "zh")
    last_other = jnp.stack(after(hops(after(last_piece, act_one), chips), act_two))
    last_other = last_other, flip(last_other, "core")
    pre_three, act_three = ran(
        conv(side, turn(), (act_two, act_two_other), three, last_other, 0, bias_three, bias_other[2])
    )
    rest_low = flip(jnp.stack(after((rest_own, rest_high), act_three)), "zl")
    cot_far = flip(after(cot_rows, act_three), "zh")
    own_rows = rows_of(act_three, zh * (halo - 3) * side, half)

    gp_three, ga_own, ga_give = ran(
        back(side, turn(), (ga_own, ga_recv, pre_three), three, last_other, 0)
    )
    ga_recv = flip(ga_give, "zl")
    full_x, act_zero = ran(whole_input(side, turn(), xl, xa, xh, xd, rest_high, rest_low))
    keep_three, give_three = ran(
        weight_grad(
            side, half, turn(), gp_three, act_two, act_two_other, chips, (full_x, go, identity_bias_grad)
        )
    )
    gp_two, ga_own, ga_give = ran(
        back(side, turn(), (ga_own, ga_recv, pre_two), two, two_other, 0)
    )
    ga_recv = flip(ga_give, "zl")
    keep_two, give_two = ran(weight_grad(side, half, turn(cot_far), gp_two, act_one, act_one_other, chips))

    gp_mine, gp_theirs, gp_one = ran(slope_back(side, turn(), ga_own, ga_recv, pre_one, half))
    gp_theirs = flip(gp_theirs, "zh")
    recv_three = flip(after(give_three, gp_one), "core")
    recv_two = flip(after(give_two, gp_one), "core")
    gx_own, gx_give = ran(
        back(
            side, turn(), (gp_one,), one, one_other, 0,
            (valid, full_x, go, cot_far, identity_kernel, last_other, half),
        )
    )

    def folds(keep, recv, first):
        for step in range(first, steps):
            keep, give = ran(fold(turn(), keep, recv))
            recv = cross(give, step, chips)
        return keep, recv

    keep_deep, give_deep = ran(fold(turn(gp_theirs), keep_three, recv_three, keep_two, recv_two))
    recv_deep = cross(give_deep, 0, chips)
    gx_recv = flip(after(gx_give, keep_deep), "zl")
    own_rows = after(own_rows, keep_deep)
    near_rows = flip(own_rows, "zl")
    far_rows = flip(own_rows, "zh")
    keep_one, give_one = ran(weight_one_grad(side, turn(), gp_mine, gp_theirs, act_zero, chips))
    recv_one = flip(give_one, "core")
    gx_keep, gx_give = ran(slots_sum(turn(), gx_own, gx_recv))
    gx_recv = flip(gx_give, "zh")
    keep_deep, recv_deep = folds(keep_deep, recv_deep, 1)
    far_near_rows = flip(after(far_rows, keep_deep), "zl")
    slot = 9 * size + 16
    flat = keep_three.shape[1] - 2 * slot
    keep_deep, give_deep, id_rows = ran(
        last_fold(
            turn(), keep_deep, recv_deep, ((0, slot), (2 * slot + flat, slot)), (2 * slot, flat)
        )
    )
    recv_deep = flip(give_deep, "zh")
    full_three = ran(join(turn(), own_rows, near_rows, far_rows, far_near_rows))
    keep_out, give_out = ran(outer(turn(), full_three, go, post_gain, identity_bias_grad, chips))
    recv_out = flip(give_out, "core")
    keep_one, give_one = ran(fold(turn(), keep_one, recv_one, keep_out, recv_out))
    recv_one = cross(give_one, 0, chips)
    deep_rows = (after(keep_deep, keep_one).astype(f32) + recv_deep.astype(f32)).astype(bf16)
    deep_rows = jnp.concatenate([deep_rows, id_rows])
    near_deep = start_spread(deep_rows)
    block_out = ran(
        finish(turn(deep_rows), valid, full_x, full_three, identity_kernel, out_kernel, identity_bias)
    )
    keep_one, recv_one = folds(keep_one, recv_one, 1)
    all_deep = end_spread(after(near_deep, keep_one))
    gx = ran(input_grad(turn(near_deep), gx_keep, gx_recv))
    gx = swap(gx.reshape(images, rows * width // 4, chans), DP)
    (total_one,) = ran([last_fold(turn(), keep_one, recv_one)])
    near_one = start_spread(total_one)
    pixels_grad = ran(widen(turn(near_one, all_deep[0]), gx, rows, width))
    all_one = end_spread(near_one, all_deep[0])
    (
        kernel_three_grad,
        bias_three_grad,
        kernel_two_grad,
        bias_two_grad,
        identity_kernel_grad,
        identity_bias_grad,
    ) = ran(final_grads(turn(), *all_deep, ((deep,), (deep,), identity_kernel.shape)))
    kernel_one_grad, bias_one_grad, out_kernel_grad, _ = ran(
        final_grads(turn(), *all_one, ((one.shape[1],), out_kernel.shape))
    )

    return (
        block_out.reshape(cotangent.shape),
        pixels_grad,
        kernel_one_grad.reshape(kernel_one.shape),
        bias_one_grad[0],
        kernel_two_grad.reshape(kernel_two.shape),
        bias_two_grad[0],
        kernel_three_grad.reshape(kernel_three.shape),
        bias_three_grad[0],
        out_kernel_grad,
        identity_kernel_grad,
        identity_bias_grad[0],
    )


def solution(mesh):
    members = mesh.devices.size // mesh.shape["mp"]
    fine = Mesh(
        mesh.devices.reshape(members // 2, 2, 2, mesh.shape["mp"] // 2),
        ("chip", "core", "zh", "zl"),
    )
    return jax.shard_map(
        local,
        mesh=fine,
        in_specs=(
            P(None, DP, None, MP),
            P(),
            P(None, None, None, MP),
            P(MP),
            P(None, None, None, MP),
            P(MP),
            P(None, None, None, MP),
            P(MP),
            P(None, MP),
            P(None, MP),
            P(MP),
            P(DP, None, None, MP),
        ),
        out_specs=(
            P(DP, None, None, MP),
            P(None, DP, None, MP),
            P(None, None, None, MP),
            P(MP),
            P(None, None, None, MP),
            P(MP),
            P(None, None, None, MP),
            P(MP),
            P(None, MP),
            P(None, MP),
            P(MP),
        ),
        check_vma=False,
    )
```

```python
import functools
import math

import jax
import jax.numpy as jnp
from jax import lax
from jax.experimental import pallas as pl
from jax.experimental.pallas import tpu as pltpu
from jax.sharding import Mesh
from jax.sharding import PartitionSpec as P


post_gain = 0.015625
slope = 0.7978845608028654
cubic = 0.044715
halo = 6
bf16 = jnp.bfloat16
f32 = jnp.float32
NT = (((1,), (1,)), ((), ()))
TN = (((0,), (0,)), ((), ()))
NN = (((1,), (0,)), ((), ()))
DP = ("chip", "core")
MP = ("zh", "zl")


def dot(left, right, dims=NN):
    return lax.dot_general(left, right, dims, preferred_element_type=f32)


def gelu(value):
    inner = jnp.tanh(slope * (value + cubic * value * value * value))
    return 0.5 * value * (1.0 + inner)


def gelu_slope(value):
    square = value * value
    inner = jnp.tanh(slope * value * (1.0 + cubic * square))
    climb = slope * (1.0 + 3.0 * cubic * square)
    return 0.5 * (1.0 + inner) + 0.5 * value * (1.0 - inner * inner) * climb


def struct(shape, kind):
    return jax.ShapeDtypeStruct(shape, kind)


def lanes(blocks):
    return blocks[0] if len(blocks) == 1 else jnp.concatenate(blocks, axis=1)


def step_bits(core, chips):
    bits = [1 << n for n in range(chips.bit_length() - 1)]
    for n in range(0, len(bits) - 1, 2) if core else ():
        bits[n], bits[n + 1] = bits[n + 1], bits[n]
    return bits


def mask_of(i, core, chips):
    masks = []
    for which in range(2):
        bits = step_bits(which, chips)
        masks.append(sum(bit for n, bit in enumerate(bits) if i >> (len(bits) - 1 - n) & 1))
    return jnp.where(core == 0, masks[0], masks[1])


def slot_of(mask, core, chips):
    slots = []
    for which in range(2):
        bits = step_bits(which, chips)
        slot = 0
        for n, bit in enumerate(bits):
            slot = slot + ((mask >> (bit.bit_length() - 1)) & 1) * (1 << (len(bits) - 1 - n))
        slots.append(slot)
    return jnp.where(core == 0, slots[0], slots[1])


VMEM = pl.BlockSpec(memory_space=pltpu.VMEM)
SMEM = pl.BlockSpec(memory_space=pltpu.SMEM)
FAR = pl.BlockSpec(memory_space=pl.ANY)
LOAD = "load"


def size_of(array):
    return math.prod(array.shape) * jnp.dtype(array.dtype).itemsize


def call(body, name, ins, outs, scratch=(), spare=6, **more):
    loads = [i for i, (space, _) in enumerate(ins) if space is LOAD]
    spaces = [FAR if space is LOAD else space for space, _ in ins]
    arrays = [array for _, array in ins]
    out_specs = [space for space, _ in outs]
    out_shape = [shape for _, shape in outs]
    held = [arrays[i] for i in loads]
    buffers = [pltpu.VMEM(array.shape, array.dtype) for array in held]
    sems = [pltpu.SemaphoreType.DMA((len(held),))] if held else []
    vmem = sum(size_of(array) for array in held)
    vmem += sum(size_of(a) for space, a in list(ins) + list(outs) if space is VMEM)
    vmem += sum(size_of(b) for b in scratch if b.memory_space == pltpu.VMEM)
    moved = sum(size_of(a) for a in arrays + out_shape)

    def wrapped(*refs):
        inputs = list(refs[: len(ins)])
        outputs = refs[len(ins) : len(ins) + len(outs)]
        rest = refs[len(ins) + len(outs) :]
        kept, tail = rest[: len(held)], rest[len(held) :]
        copies = []
        if held:
            sem, tail = tail[0], tail[1:]
            copies = [
                pltpu.make_async_copy(inputs[i], kept[n], sem.at[n]) for n, i in enumerate(loads)
            ]
        for copy in copies:
            copy.start()
        for n, i in enumerate(loads):
            inputs[i] = kept[n]

        def arrive():
            for copy in copies:
                copy.wait()

        body(arrive, *inputs, *outputs, *tail)

    single = len(outs) == 1
    return pl.pallas_call(
        wrapped,
        in_specs=spaces,
        out_specs=out_specs[0] if single else out_specs,
        out_shape=out_shape[0] if single else out_shape,
        scratch_shapes=buffers + sems + list(scratch),
        compiler_params=pltpu.CompilerParams(vmem_limit_bytes=vmem + (spare << 20)),
        cost_estimate=pl.CostEstimate(flops=0, bytes_accessed=moved, transcendentals=0),
        name=name,
        **more,
    )(*arrays)


def run_copies(pairs, sems):
    for copy in start_copies(pairs, sems):
        copy.wait()


def slice_copies(group, idx_ref, own, blocks, sibling, wbuf):
    chip, core, zh = idx_ref[0], idx_ref[1], idx_ref[2]
    size = blocks.shape[-2]
    pairs = [(own, wbuf.at[zh])]
    for j in range(blocks.shape[0]):
        for source, owner in ((blocks, core), (sibling, 1 - core)):
            home = chip ^ mask_of(j, owner, blocks.shape[0])
            spot = at((2 * home + owner) * size, size, size)
            pairs.append((source.at[j, 9 * group : 9 * group + 9], wbuf.at[1 - zh, :, spot, :]))
    return pairs


def flat_copies(first, idx_ref, blocks, sibling, buffer):
    chip, core = idx_ref[0], idx_ref[1]
    columns, units = buffer.shape[:2]
    chips = blocks.shape[0]
    count = units // (2 * chips)
    pairs = []
    for j in range(chips):
        for source, owner in ((blocks, core), (sibling, 1 - core)):
            home = chip ^ mask_of(j, owner, chips)
            spot = pl.ds((2 * home + owner) * count, count)
            for c in range(columns):
                begin = first + c * count
                pairs.append((source.at[j, begin : begin + count], buffer.at[c, spot]))
    return pairs


def start_copies(pairs, sems):
    copies = [pltpu.make_async_copy(a, b, sems.at[i]) for i, (a, b) in enumerate(pairs)]
    for copy in copies:
        copy.start()
    return copies


def flat_rows(buffer, begin, count):
    columns, _, size, wide = buffer.shape
    return lanes([buffer[c, pl.ds(begin, count)].reshape(count * size, wide) for c in range(columns)])


def halves(spots, side):
    first = (spots // side + 1) // 2 * side
    return ((0, first), (first, spots - first))


def columns_of(size, wide, side):
    return lax.rem(lax.broadcasted_iota(jnp.int32, (size, wide), 0), side)


def at(start, size, unit):
    return pl.ds(pl.multiple_of(start, unit), size)


def pool_body(arrive, x_ref, out_ref):
    arrive()
    rows, width, chans = x_ref.shape[1:]
    half = width // 2
    pixel = lax.broadcasted_iota(jnp.int32, (half, 2 * width), 1)
    place = lax.broadcasted_iota(jnp.int32, (half, 2 * width), 0)
    inside = (lax.rem(pixel, width) >= 2 * place) & (lax.rem(pixel, width) < 2 * place + 2)
    pick = jnp.where(inside, 0.25, 0.0).astype(bf16)
    for image in range(x_ref.shape[0]):
        for row in range(rows // 2):
            window = x_ref[image, 2 * row : 2 * row + 2].reshape(2 * width, chans)
            out_ref[image, row * half : (row + 1) * half, :] = dot(pick, window).astype(bf16)


def pool(pixels):
    images, rows, width, chans = pixels.shape
    shape = struct((images, rows * width // 4, chans), bf16)
    return call(pool_body, "pool", [(LOAD, pixels)], [(VMEM, shape)])


def widen_body(arrive, idx_ref, g_ref, out_ref):
    arrive()
    rows, width, chans = out_ref.shape[1:]
    half = width // 2
    pixel = lax.broadcasted_iota(jnp.int32, (width, half), 0)
    place = lax.broadcasted_iota(jnp.int32, (width, half), 1)
    inside = (pixel >= 2 * place) & (pixel < 2 * place + 2)
    pick = jnp.where(inside, 0.25, 0.0).astype(bf16)
    for image in range(g_ref.shape[0]):
        for row in range(rows // 2):
            wide = dot(pick, g_ref[image, row * half : (row + 1) * half, :]).astype(bf16)
            out_ref[image, 2 * row] = wide
            out_ref[image, 2 * row + 1] = wide


def widen(idx, grad, rows, width):
    images, spots, chans = grad.shape
    step = images // 4
    block = pl.BlockSpec((step, spots, chans), lambda i: (i, 0, 0))
    out = pl.BlockSpec((step, rows, width, chans), lambda i: (i, 0, 0, 0))
    return call(
        widen_body,
        "widen",
        [(SMEM, idx), (block, grad)],
        [(out, struct((images, rows, width, chans), bf16))],
        grid=(4,),
    )


def conv_body(side, first, group, arrive, idx_ref, *refs):
    zh, zl = idx_ref[2], idx_ref[3]
    if first:
        xl, xa, xh, xd, wl, wo, ws, bl, bo, pre_ref, act_ref, xbuf, wbuf, acc, sems = refs
        chans = xl.shape[1]
        spots = xbuf.shape[0]
        begin = zh * (xl.shape[0] - spots)
        pairs = []
        for source, up, along in ((xl, zh, zl), (xa, zh, 1 - zl), (xh, 1 - zh, zl), (xd, 1 - zh, 1 - zl)):
            if source is xl:
                source = xl.at[at(begin, spots, side), :]
            pairs.append((source, xbuf.at[:, at((2 * up + along) * chans, chans, chans)]))
    else:
        xl, xa, wl, wo, ws, bl, bo, pre_ref, act_ref, xbuf, wbuf, acc, sems = refs
        chans = xl.shape[1] // 2
        spots = xbuf.shape[0]
        pairs = []
        for source, along in ((xl, zl), (xa, 1 - zl)):
            for up in range(2):
                pairs.append(
                    (
                        source.at[:, up * chans : (up + 1) * chans],
                        xbuf.at[:, at((2 * up + along) * chans, chans, chans)],
                    )
                )
    run_copies(slice_copies(group, idx_ref, wl, wo, ws, wbuf) + pairs, sems)
    arrive()
    acc[...] = jnp.zeros_like(acc)
    outs = 2 * wl.shape[2]
    for x in range(3):
        weights = lanes([wbuf[u, 3 * y + x] for y in range(3) for u in range(2)])
        for begin, block in halves(spots, side):
            values = xbuf[begin : begin + block, :]
            if first:
                values = gelu(values.astype(f32)).astype(bf16)
            product = dot(values, weights)
            for y in range(3):
                place = begin + side * (2 - y)
                acc[x, place : place + block, :] += product[:, y * outs : (y + 1) * outs]
    own, other = bl[...], bo[...]
    bias = lanes([jnp.where(zh == 0, own, other), jnp.where(zh == 0, other, own)])
    for begin, block in halves(act_ref.shape[0], side):
        column = columns_of(block, outs, side)
        spot = at(begin + side + zh * side, block, side)
        left = pltpu.roll(acc[0, spot, :], 1, 0)
        right = pltpu.roll(acc[2, spot, :], block - 1, 0)
        pre = acc[1, spot, :] + bias
        pre = pre + jnp.where(column > 0, left, 0.0)
        pre = pre + jnp.where(column < side - 1, right, 0.0)
        pre_ref[begin : begin + block, :] = pre
        act_ref[begin : begin + block, :] = gelu(pre).astype(bf16)


def conv(side, idx, sources, own, other, group, bias, bias_other, first=False):
    taps, depth, outs = own.shape
    spots = sources[1].shape[0]
    rows = spots - side
    return call(
        functools.partial(conv_body, side, first, group),
        "conv",
        [(SMEM, idx)]
        + [(FAR, s) for s in sources]
        + [(FAR, own), (FAR, other[0]), (FAR, other[1])]
        + [(VMEM, bias.reshape(1, outs)), (VMEM, bias_other.reshape(1, outs))],
        [(VMEM, struct((rows, 2 * outs), f32)), (VMEM, struct((rows, 2 * outs), bf16))],
        [
            pltpu.VMEM((spots, depth), bf16),
            pltpu.VMEM((2, taps, depth, outs), bf16),
            pltpu.VMEM((3, spots + 2 * side, 2 * outs), f32),
            pltpu.SemaphoreType.DMA((2 * other[0].shape[0] + 5,)),
        ],
        spare=14 if first else 8,
    )


def spread_taps(side, grad, taps_ref):
    pixels, outs = grad.shape
    column = columns_of(pixels, outs, side)
    wide = grad.astype(f32)
    ahead = jnp.where(column < side - 1, pltpu.roll(wide, pixels - 1, 0), 0.0).astype(bf16)
    behind = jnp.where(column > 0, pltpu.roll(wide, 1, 0), 0.0).astype(bf16)
    edge = jnp.zeros((side, 3 * outs), bf16)
    taps_ref[:side, :] = edge
    taps_ref[side + pixels :, :] = edge
    taps_ref[side : side + pixels, :] = jnp.concatenate([ahead, grad, behind], axis=1)


def tap_block(side, taps_ref, begin, block):
    return lanes([taps_ref[at(begin + side * (2 - y), block, side), :] for y in range(3)])


def slope_body(side, arrive, idx_ref, keep_ref, recv_ref, pre_ref, mine_ref, theirs_ref, gp_ref):
    arrive()
    zh = idx_ref[2]
    half, outs = mine_ref.shape
    total = keep_ref[...] + recv_ref[...].astype(f32)
    spots = keep_ref.shape[0]
    pre = pre_ref[at(zh * (pre_ref.shape[0] - spots), spots, side), :]
    gp_ref[...] = (total * gelu_slope(pre)).astype(bf16)
    own = gp_ref[at(zh * (gp_ref.shape[0] - half), half, side), :]
    low, high = own[:, :outs], own[:, outs:]
    mine_ref[...] = jnp.where(zh == 0, low, high)
    theirs_ref[...] = jnp.where(zh == 0, high, low)


def slope_back(side, idx, keep, recv, pre, half):
    outs = pre.shape[1] // 2
    return call(
        functools.partial(slope_body, side),
        "slope_back",
        [(SMEM, idx), (VMEM, keep), (VMEM, recv), (LOAD, pre)],
        [
            (VMEM, struct((half, outs), bf16)),
            (VMEM, struct((half, outs), bf16)),
            (VMEM, struct(keep.shape, bf16)),
        ],
    )


def back_body(side, last, group, arrive, idx_ref, *refs):
    zh, zl = idx_ref[2], idx_ref[3]
    if last:
        valid_ref, grad_ref, x_ref, go_ref, far_ref, idk_ref, wl, wo, ws, po, ps = refs[:11]
        own_ref, give_ref, taps_ref, wbuf, idk_far, sems = refs[11:]
    else:
        keep_ref, recv_ref, pre_ref, wl, wo, ws, gp_ref, own_ref, give_ref, taps_ref, wbuf, sems = refs
    pairs = slice_copies(group, idx_ref, wl, wo, ws, wbuf)
    if last:
        pairs += flat_copies(9, idx_ref, po, ps, idk_far)
    copies = start_copies(pairs, sems)
    arrive()
    if last:
        grad = grad_ref[...]
    else:
        spots = gp_ref.shape[0]

        def window(ref):
            return ref[at(zh * (ref.shape[0] - spots), spots, side), :]

        total = window(keep_ref) + window(recv_ref).astype(f32)
        grad = (total * gelu_slope(window(pre_ref))).astype(bf16)
        gp_ref[...] = grad
    spread_taps(side, grad, taps_ref)
    depth, outs = wl.shape[1:]
    pixels = own_ref.shape[-2]
    start = zh * side
    for copy in copies:
        copy.wait()
    chans = depth // 4

    def rows(index):
        spot = at(index * chans, chans, chans)
        return lanes([wbuf[u, t, spot, :] for t in range(9) for u in range(2)])

    for target, along in ((give_ref, 1 - zl), (own_ref, zl)):
        if last:
            units = chans // idk_far.shape[2]
            for up in range(2):
                index = 2 * up + along
                weights = rows(index)
                near = idk_ref[at(index * chans, chans, chans), :]
                far = flat_rows(idk_far, index * units, units)
                apart = zh * (far_ref.shape[0] - pixels)
                for begin, block in halves(pixels, side):
                    here = at(zh * pixels + begin, block, side)
                    part = dot(tap_block(side, taps_ref, start + begin, block), weights, NT)
                    x = x_ref[here, at(index * chans, chans, chans)]
                    part = part * gelu_slope(x.astype(f32))
                    part = part + dot(go_ref[here, :], near, NT)
                    part = part + valid_ref[0] * dot(far_ref[at(apart + begin, block, side), :], far, NT)
                    target[up, begin : begin + block, :] = part.astype(target.dtype)
        else:
            weights = jnp.concatenate([rows(along), rows(2 + along)], axis=0)
            for begin, block in halves(pixels, side):
                part = dot(tap_block(side, taps_ref, start + begin, block), weights, NT)
                target[begin : begin + block, :] = part.astype(target.dtype)


def back(side, idx, sources, own, other, group, last=None):
    taps, depth, outs = own.shape
    spots = min(sources[0].shape[0], sources[-1].shape[0])
    copies = 2 * other[0].shape[0] + 1
    extra = []
    scratch = []
    if last:
        valid, full_x, go, cot_far, idk, pieces, half = last
        chans = depth // 4
        shape = (2, half, chans)
        results = []
        extra = [(FAR, pieces[0]), (FAR, pieces[1])]
        sources = list(sources) + [full_x, go, cot_far, idk]
        columns, size = idk.shape[1] // 128, pieces[0].shape[2]
        scratch = [pltpu.VMEM((columns, depth // size, size, 128), bf16)]
        copies += 2 * other[0].shape[0] * columns
    else:
        shape = (spots - side, depth // 2)
        results = [(VMEM, struct((spots, 2 * outs), bf16))]
    results += [(VMEM, struct(shape, f32)), (VMEM, struct(shape, bf16))]
    return call(
        functools.partial(back_body, side, bool(last), group),
        "back",
        [(SMEM, idx)]
        + ([(SMEM, last[0])] if last else [])
        + [(LOAD, source) for source in sources]
        + [(FAR, own), (FAR, other[0]), (FAR, other[1])]
        + extra,
        results,
        [pltpu.VMEM((spots + 2 * side, 6 * outs), bf16), pltpu.VMEM((2, taps, depth, outs), bf16)]
        + scratch
        + [pltpu.SemaphoreType.DMA((copies,))],
        spare=14 if last else 10,
    )


def put_blocks(idx_ref, keep_ref, give_ref, part, tap, first_block, size, begin=0):
    chip, core = idx_ref[0], idx_ref[1]
    for b in range(0, part.shape[0] // size, 2):
        even = part[b * size : (b + 1) * size, :]
        odd = part[(b + 1) * size : (b + 2) * size, :]
        mask = chip ^ ((first_block + b) // 2)
        slot = slot_of(mask, core, keep_ref.shape[0])
        give_slot = slot_of(mask, 1 - core, keep_ref.shape[0])
        rows = slice(begin + tap * size, begin + (tap + 1) * size)
        keep_ref[slot, rows, :] = jnp.where(core == 0, even, odd).astype(bf16)
        give_ref[give_slot, rows, :] = jnp.where(core == 0, odd, even).astype(bf16)


def weight_body(side, half, flat, arrive, idx_ref, gp_ref, *refs):
    if flat:
        full_ref, go_ref, bias_ref = refs[:3]
        refs = refs[3:]
    xl, xa, keep_ref, give_ref, xbuf, taps_ref, sems = refs
    arrive()
    zh, zl = idx_ref[2], idx_ref[3]
    chans = xl.shape[1] // 2
    spots = xbuf.shape[0]
    window = at(zh * (xl.shape[0] - spots), spots, side)
    pairs = []
    for source, along in ((xl, zl), (xa, 1 - zl)):
        for up in range(2):
            pairs.append(
                (
                    source.at[window, up * chans : (up + 1) * chans],
                    xbuf.at[:, at((2 * up + along) * chans, chans, chans)],
                )
            )
    run_copies(pairs, sems)
    wide = gp_ref.shape[1]
    outs = wide // 2
    spot = lax.broadcasted_iota(jnp.int32, (spots, wide), 0) - zh * side
    grad = gp_ref[at(zh * (gp_ref.shape[0] - spots), spots, side), :].astype(f32)
    grad = jnp.where((spot >= 0) & (spot < half), grad, 0.0)
    bias = jnp.sum(grad, axis=0, keepdims=True)
    spread_taps(side, grad.astype(bf16), taps_ref)
    blocks = 2 * keep_ref.shape[0]
    depth = xbuf.shape[1]
    size = depth // blocks
    for begin in range(0, depth, 256):
        values = xbuf[:, begin : begin + 256]
        for y in range(3):
            place = side * (2 - y)
            part = dot(values, taps_ref[place : place + spots, :], TN)
            for x in range(3):
                for u in range(2):
                    col = x * wide + u * outs
                    put_blocks(
                        idx_ref, keep_ref, give_ref, part[:, col : col + outs],
                        3 * y + x, begin // size, size, u * (9 * size + 16),
                    )
    for u in range(2):
        row = jnp.broadcast_to(bias[:, u * outs : (u + 1) * outs], (16, outs)).astype(bf16)
        for j in range(keep_ref.shape[0]):
            spot = slice(u * (9 * size + 16) + 9 * size, (u + 1) * (9 * size + 16))
            keep_ref[j, spot, :] = row
            give_ref[j, spot, :] = row
    if flat:
        first = 2 * (9 * size + 16)
        flat_pieces(1.0, idx_ref, full_ref, go_ref, bias_ref, keep_ref, give_ref, first)


def weight_grad(side, half, idx, grad, act, act_other, chips, flat=()):
    spots = half + side
    wide = grad.shape[1]
    outs = wide // 2
    depth = 2 * act.shape[1]
    rows = 2 * (9 * depth // (2 * chips) + 16)
    if flat:
        rows += flat_size(flat[0], flat[1], chips)
    return call(
        functools.partial(weight_body, side, half, bool(flat)),
        "weight_grad",
        [(SMEM, idx), (LOAD, grad)] + [(LOAD, a) for a in flat] + [(FAR, act), (FAR, act_other)],
        [(VMEM, struct((chips, rows, outs), bf16))] * 2,
        [
            pltpu.VMEM((spots, depth), bf16),
            pltpu.VMEM((spots + 2 * side, 3 * wide), bf16),
            pltpu.SemaphoreType.DMA((4,)),
        ],
        spare=10,
    )


def weight_one_body(side, arrive, idx_ref, mine_ref, theirs_ref, x_ref, *refs):
    keep_ref, give_ref, gp_ref, taps_ref = refs
    arrive()
    zh = idx_ref[2]
    half, outs = mine_ref.shape
    gp_ref[at(zh * half, half, side), :] = mine_ref[...]
    gp_ref[at((1 - zh) * half, half, side), :] = theirs_ref[...]
    grad = gp_ref[...]
    bias = jnp.sum(grad.astype(f32), axis=0, keepdims=True)
    spread_taps(side, grad, taps_ref)
    blocks = 2 * keep_ref.shape[0]
    spots, depth = x_ref.shape
    size = depth // blocks
    right = tap_block(side, taps_ref, 0, spots)
    for begin in range(0, depth, 256):
        part = dot(x_ref[:, begin : begin + 256], right, TN)
        for tap in range(9):
            put_blocks(
                idx_ref, keep_ref, give_ref, part[:, tap * outs : (tap + 1) * outs],
                tap, begin // size, size,
            )
    row = jnp.broadcast_to(bias, (16, outs)).astype(bf16)
    first = 9 * size + 16
    for j in range(keep_ref.shape[0]):
        keep_ref[j, 9 * size : first, :] = row
        give_ref[j, 9 * size : first, :] = row


def weight_one_grad(side, idx, mine, theirs, act_zero, chips):
    spots, depth = act_zero.shape
    outs = mine.shape[1]
    rows = 9 * depth // (2 * chips) + 16
    return call(
        functools.partial(weight_one_body, side),
        "weight_one_grad",
        [(SMEM, idx), (LOAD, mine), (LOAD, theirs), (LOAD, act_zero)],
        [(VMEM, struct((chips, rows, outs), bf16))] * 2,
        [
            pltpu.VMEM((spots, outs), bf16),
            pltpu.VMEM((spots + 2 * side, 3 * outs), bf16),
        ],
        spare=14,
    )


def fold_body(pairs, arrive, idx_ref, *refs):
    arrive()
    ins, (keep_ref, give_ref) = refs[: 2 * pairs], refs[2 * pairs :]
    half = keep_ref.shape[0]
    for i in range(2 * half):
        target = keep_ref if i < half else give_ref
        begin = 0
        for keep, recv in zip(ins[0::2], ins[1::2]):
            rows = keep.shape[1]
            total = keep[i].astype(f32) + recv[i].astype(f32)
            target[i % half, begin : begin + rows, :] = total.astype(bf16)
            begin += rows


def fold(idx, *arrays):
    blocks, _, wide = arrays[0].shape
    rows = sum(a.shape[1] for a in arrays[0::2])
    return call(
        functools.partial(fold_body, len(arrays) // 2),
        "fold",
        [(SMEM, idx)] + [(VMEM, a) for a in arrays],
        [(VMEM, struct((blocks // 2, rows, wide), bf16))] * 2,
    )


def last_body(slotted, rest, arrive, idx_ref, keep_in, recv_in, *targets):
    arrive()
    zh = idx_ref[2]

    def put(target, place, begin, rows):
        spot = at(begin, rows, 16)
        total = keep_in[0, spot, :].astype(f32) + recv_in[0, spot, :].astype(f32)
        target[place : place + rows, :] = total.astype(bf16)

    place = 0
    for begin, rows in slotted:
        put(targets[0], place, begin + zh * rows, rows)
        put(targets[1], place, begin + (1 - zh) * rows, rows)
        place += rows
    begin, rows = rest
    put(targets[-1], 0, begin, rows)


def last_fold(idx, keep, recv, slotted=(), rest=None):
    wide = keep.shape[2]
    rest = rest or (0, keep.shape[1])
    rows = sum(size for _, size in slotted)
    sizes = ([rows, rows] if slotted else []) + [rest[1]]
    return call(
        functools.partial(last_body, slotted, rest),
        "last_fold",
        [(SMEM, idx), (VMEM, keep), (VMEM, recv)],
        [(VMEM, struct((size, wide), bf16)) for size in sizes],
    )


def final_body(parts, arrive, idx_ref, own_ref, sib_ref, *refs):
    arrive()
    outs, stages, sems = refs[: 2 * len(parts)], refs[2 * len(parts) : -1], refs[-1]
    chip, core = idx_ref[0], idx_ref[1]
    chips, _, wide = own_ref.shape
    first = 0
    copies = []

    def store(source, target):
        copies.append(pltpu.make_async_copy(source, target, sems.at[len(copies)]))
        copies[-1].start()

    for n, part in enumerate(parts):
        grad_ref, bias_ref, stage = outs[2 * n], outs[2 * n + 1], stages[n]
        size = part[0] // (2 * chips)
        columns = 1 if len(part) == 1 else part[1] // wide
        end = first + size * (9 if len(part) == 1 else columns)
        for c in range(columns):
            row = own_ref[0, end + c : end + c + 1, :].astype(f32)
            bias_ref[:, c * wide : (c + 1) * wide] = row
        for n_row, begin in enumerate(range(first, end, size)):
            for j in range(chips):
                for source, owner in ((own_ref, core), (sib_ref, 1 - core)):
                    home = chip ^ mask_of(j, owner, chips)
                    spot = at((2 * home + owner) * size, size, size)
                    piece = source[j, begin : begin + size, :].astype(f32)
                    if len(part) == 1:
                        stage[n_row, spot, :] = piece
                    else:
                        stage[spot, n_row * wide : (n_row + 1) * wide] = piece
            if len(part) == 1:
                store(stage.at[n_row], grad_ref.at[n_row])
        if len(part) > 1:
            store(stage, grad_ref)
        first = end + 16
    for copy in copies:
        copy.wait()


def final_grads(idx, own, sib, parts):
    wide = own.shape[2]
    results, stages = [], []
    for part in parts:
        shape = (9, part[0], wide) if len(part) == 1 else part
        results += [(FAR, struct(shape, f32)), (VMEM, struct((1, shape[-1]), f32))]
        stages.append(pltpu.VMEM(shape, f32))
    copies = sum(9 if len(part) == 1 else 1 for part in parts)
    return call(
        functools.partial(final_body, parts),
        "final_grads",
        [(SMEM, idx), (VMEM, own), (VMEM, sib)],
        results,
        stages + [pltpu.SemaphoreType.DMA((copies,))],
    )


def flat_pieces(gain, idx_ref, x_ref, go_ref, bias_ref, keep_ref, give_ref, first):
    chip, core = idx_ref[0], idx_ref[1]
    chips, _, wide = keep_ref.shape
    columns = go_ref.shape[1] // wide
    size = x_ref.shape[1] // (2 * chips)
    bias = jnp.concatenate(
        [bias_ref[:, c * wide : (c + 1) * wide] for c in range(columns)]
        + [jnp.zeros((16 - columns, wide), f32)],
        axis=0,
    ).astype(bf16)
    for j in range(chips):
        keep_ref[j, first + columns * size :, :] = bias
        give_ref[j, first + columns * size :, :] = bias
    for begin in range(0, x_ref.shape[1], 256):
        part = gain * dot(x_ref[:, begin : begin + 256], go_ref[...], TN)
        for b in range(0, 256 // size, 2):
            mask = chip ^ ((begin // size + b) // 2)
            slot = slot_of(mask, core, chips)
            give_slot = slot_of(mask, 1 - core, chips)
            for c in range(columns):
                even = part[b * size : (b + 1) * size, c * wide : (c + 1) * wide]
                odd = part[(b + 1) * size : (b + 2) * size, c * wide : (c + 1) * wide]
                spot = slice(first + c * size, first + (c + 1) * size)
                keep_ref[slot, spot, :] = jnp.where(core == 0, even, odd).astype(bf16)
                give_ref[give_slot, spot, :] = jnp.where(core == 0, odd, even).astype(bf16)


def flat_size(x, go, chips):
    return (go.shape[1] // 128) * (x.shape[1] // (2 * chips)) + 16


def outer_body(gain, arrive, idx_ref, x_ref, go_ref, bias_ref, keep_ref, give_ref):
    arrive()
    flat_pieces(gain, idx_ref, x_ref, go_ref, bias_ref, keep_ref, give_ref, 0)


def outer(idx, x, go, gain, bias, chips):
    return call(
        functools.partial(outer_body, gain),
        "outer",
        [(SMEM, idx), (LOAD, x), (LOAD, go), (LOAD, bias)],
        [(VMEM, struct((chips, flat_size(x, go, chips), 128), bf16))] * 2,
        spare=8,
    )


def start_body(arrive, idx_ref, valid_ref, cot_ref, outk_ref, go_ref, bias_ref, own_ref, give_ref):
    arrive()
    zl = idx_ref[3]
    masked = cot_ref[...].astype(f32) * valid_ref[0]
    go_ref[...] = masked.astype(bf16)
    bias_ref[...] = jnp.sum(masked, axis=0, keepdims=True)
    chans = outk_ref.shape[0] // 4
    block = cot_ref.shape[0] // 4
    for target, along in ((give_ref, 1 - zl), (own_ref, zl)):
        weights = jnp.concatenate(
            [outk_ref[at((2 * up + along) * chans, chans, chans), :] for up in range(2)], axis=0
        )
        for begin in range(0, cot_ref.shape[0], block):
            part = post_gain * dot(go_ref[begin : begin + block, :], weights, NT)
            target[begin : begin + block, :] = part.astype(target.dtype)


def start_back(idx, valid, cot, outk):
    spots, outs = cot.shape
    half = outk.shape[0] // 2
    return call(
        start_body,
        "start_back",
        [(SMEM, idx), (SMEM, valid), (LOAD, cot), (LOAD, outk)],
        [
            (VMEM, struct(cot.shape, bf16)),
            (VMEM, struct((1, outs), f32)),
            (VMEM, struct((spots, half), f32)),
            (VMEM, struct((spots, half), bf16)),
        ],
    )


def rows_body(side, arrive, idx_ref, own_ref, recv_ref, keep_ref, give_ref):
    arrive()
    zh = idx_ref[2]
    spots = keep_ref.shape[0]
    apart = own_ref.shape[0] - spots
    for target, begin in ((give_ref, (1 - zh) * apart), (keep_ref, zh * apart)):
        spot = at(begin, spots, side)
        total = own_ref[spot, :] + recv_ref[spot, :].astype(f32)
        target[...] = total.astype(target.dtype)


def rows_sum(side, idx, own, recv, spots):
    shape = (spots, own.shape[1])
    return call(
        functools.partial(rows_body, side),
        "rows_sum",
        [(SMEM, idx), (LOAD, own), (LOAD, recv)],
        [(VMEM, struct(shape, f32)), (VMEM, struct(shape, bf16))],
    )


def slots_body(arrive, idx_ref, own_ref, recv_ref, keep_ref, give_ref):
    arrive()
    zh = idx_ref[2]
    for target, slot in ((give_ref, 1 - zh), (keep_ref, zh)):
        total = own_ref[slot] + recv_ref[slot].astype(f32)
        target[...] = total.astype(bf16)


def slots_sum(idx, own, recv):
    shape = struct(own.shape[1:], bf16)
    return call(
        slots_body,
        "slots_sum",
        [(SMEM, idx), (VMEM, own), (VMEM, recv)],
        [(VMEM, shape), (VMEM, shape)],
    )


def input_body(arrive, idx_ref, keep_ref, recv_ref, out_ref):
    arrive()
    zh = idx_ref[2]
    half = keep_ref.shape[0]
    out_ref[at(zh * half, half, half), :] = keep_ref[...]
    out_ref[at((1 - zh) * half, half, half), :] = recv_ref[...]


def input_grad(idx, keep, recv):
    half, chans = keep.shape
    return call(
        input_body,
        "input_grad",
        [(SMEM, idx), (VMEM, keep), (VMEM, recv)],
        [(VMEM, struct((2 * half, chans), bf16))],
    )


def whole_body(side, arrive, idx_ref, xl, xa, xh, xd, rh, rl, x_ref, act_ref, sems):
    arrive()
    zh, zl = idx_ref[2], idx_ref[3]
    chans = xl.shape[1]
    spots = xa.shape[0]
    rest = xl.shape[0] - spots
    window, outside = at(zh * rest, spots, side), at((1 - zh) * spots, rest, side)

    def cols(up, along):
        return at((2 * up + along) * chans, chans, chans)

    run_copies(
        [
            (xl, x_ref.at[:, cols(zh, zl)]),
            (xa, x_ref.at[window, cols(zh, 1 - zl)]),
            (xh, x_ref.at[window, cols(1 - zh, zl)]),
            (xd, x_ref.at[window, cols(1 - zh, 1 - zl)]),
            (rl.at[0], x_ref.at[outside, cols(zh, 1 - zl)]),
            (rh, x_ref.at[outside, cols(1 - zh, zl)]),
            (rl.at[1], x_ref.at[outside, cols(1 - zh, 1 - zl)]),
        ],
        sems,
    )
    block = x_ref.shape[0] // 8
    for begin in range(0, x_ref.shape[0], block):
        rows = slice(begin, begin + block)
        act_ref[rows, :] = gelu(x_ref[rows, :].astype(f32)).astype(bf16)


def whole_input(side, idx, *parts):
    spots, chans = parts[0].shape
    return call(
        functools.partial(whole_body, side),
        "whole_input",
        [(SMEM, idx)] + [(FAR, p) for p in parts],
        [(VMEM, struct((spots, 4 * chans), bf16))] * 2,
        [pltpu.SemaphoreType.DMA((7,))],
    )


def join_body(arrive, idx_ref, own, recv, far_own, far_recv, out, sems):
    arrive()
    zh, zl = idx_ref[2], idx_ref[3]
    half = own.shape[0]
    chans = own.shape[1] // 2
    pairs = []
    for source, up, along in ((own, zh, zl), (recv, zh, 1 - zl), (far_own, 1 - zh, zl), (far_recv, 1 - zh, 1 - zl)):
        for slot in range(2):
            spot = at((2 * slot + along) * chans, chans, chans)
            target = out.at[at(up * half, half, half), spot]
            pairs.append((source.at[:, slot * chans : (slot + 1) * chans], target))
    run_copies(pairs, sems)


def join(idx, *parts):
    half, wide = parts[0].shape
    return call(
        join_body,
        "join",
        [(SMEM, idx)] + [(FAR, p) for p in parts],
        [(VMEM, struct((2 * half, 2 * wide), bf16))],
        [pltpu.SemaphoreType.DMA((8,))],
    )


def finish_body(arrive, idx_ref, valid_ref, x_ref, act_ref, idk_ref, outk_ref, ib_ref, out_ref):
    arrive()
    block = x_ref.shape[0] // 4
    for begin in range(0, x_ref.shape[0], block):
        rows = slice(begin, begin + block)
        identity = dot(x_ref[rows, :], idk_ref[...]) + ib_ref[...]
        branch = dot(act_ref[rows, :], outk_ref[...])
        out_ref[rows, :] = ((identity + post_gain * branch) * valid_ref[0]).astype(bf16)


def finish(idx, valid, x, act, idk, outk, ib):
    outs = idk.shape[1]
    return call(
        finish_body,
        "finish",
        [(SMEM, idx), (SMEM, valid), (LOAD, x), (LOAD, act), (LOAD, idk), (LOAD, outk)]
        + [(VMEM, ib.reshape(1, outs))],
        [(VMEM, struct((x.shape[0], outs), bf16))],
        spare=8,
    )


def flip(value, axis):
    return lax.ppermute(value, axis, [(0, 1), (1, 0)])


def cross(value, step, chips):
    pairs = []
    for chip in range(chips):
        for core in range(2):
            other = chip ^ step_bits(core, chips)[step]
            pairs.append((2 * chip + core, 2 * other + core))
    return lax.ppermute(value, DP, pairs)


def hops(value, chips):
    blocks = [value]
    for i in range(1, chips):
        pairs = []
        for chip in range(chips):
            for core in range(2):
                bits = step_bits(core, chips)
                mask = sum(bit for n, bit in enumerate(bits) if i >> (len(bits) - 1 - n) & 1)
                pairs.append((2 * (chip ^ mask) + core, 2 * chip + core))
        blocks.append(lax.ppermute(value, DP, pairs))
    return blocks


def swap(pieces, axis):
    return lax.all_to_all(pieces, axis, split_axis=0, concat_axis=0, tiled=True)


def after(value, other):
    return lax.optimization_barrier((value, other))[0]


def rows_of(value, start, size):
    return lax.dynamic_slice_in_dim(value, start, size, 0)


def local(
    pixels,
    counts,
    kernel_one,
    bias_one,
    kernel_two,
    bias_two,
    kernel_three,
    bias_three,
    out_kernel,
    identity_kernel,
    identity_bias,
    cotangent,
):
    images, rows, width, chans = pixels.shape
    side = width // 2
    spots = side * side
    half = spots // 2
    window = half + halo * side
    outs = cotangent.shape[3]
    chips = lax.axis_size("chip")
    chip, core, zh, zl = [lax.axis_index(a) for a in ("chip", "core", "zh", "zl")]
    idx = jnp.stack([chip, core, zh, zl]).astype(jnp.int32)
    taps = lambda kernel: kernel.reshape((9,) + kernel.shape[2:])
    one, two, three = taps(kernel_one), taps(kernel_two), taps(kernel_three)

    own_count = lax.dynamic_index_in_dim(counts, 2 * chip + core, 0, keepdims=True)
    valid = (own_count > 0).astype(f32)

    place = 2 * chip + core

    def units_of(kernel, size):
        if kernel.ndim == 3:
            block = kernel.shape[1] // (2 * chips)
            return lax.dynamic_slice_in_dim(kernel, place * block, block, 1)
        block = kernel.shape[0] // (2 * chips)
        block = lax.dynamic_slice_in_dim(kernel, place * block, block, 0)
        block = block.reshape(-1, size, block.shape[1] // 128, 128)
        return block.transpose(2, 0, 1, 3).reshape(-1, size, 128)

    steps = chips.bit_length() - 1

    def start_spread(piece, *others):
        return jnp.concatenate(after((piece[None], cross(piece[None], steps - 1, chips)), others))

    def end_spread(own, *others):
        for step in reversed(range(steps - 1)):
            own = jnp.concatenate(after((own, cross(own, step, chips)), others))
        return own, flip(own, "core")

    last = [idx]

    def turn(*others):
        return after(idx, (last[0],) + others)

    def ran(results):
        last[0] = results[-1] if isinstance(results, (list, tuple)) else results
        return results

    size = two.shape[1] // (2 * chips)
    deep = two.shape[1]
    cot = cotangent.reshape(spots, outs)
    one_piece = flip(units_of(one, size), "zh")
    pooled = ran(pool(pixels))
    go, identity_bias_grad, ga_own, ga_give = ran(start_back(turn(), valid, cot, out_kernel))
    bias_other = flip(after(jnp.stack([bias_one, bias_two, bias_three]), go), "zh")
    two_piece = units_of(after(two, pooled), size)
    last_piece = jnp.concatenate([units_of(after(k, pooled), size) for k in (three, identity_kernel)])
    cot_rows = rows_of(after(cot, pooled), (1 - zh) * half, half)
    xl = swap(after(pooled, (one_piece, two_piece, last_piece, cot_rows, ga_give)), DP)
    xl = xl.reshape(spots, chans)
    two_piece = flip(after(two_piece, one_piece), "zh")

    apart = spots - window
    xa = flip(rows_of(xl, zh * apart, window), "zl")
    xh = flip(rows_of(xl, (1 - zh) * apart, window), "zh")
    rest = spots - window
    rest_own = rows_of(xl, (1 - zh) * window, rest)
    rest_high = rows_of(xl, zh * window, rest)
    two_near = start_spread(after(two_piece, xl))
    one_near = start_spread(after(one_piece, xl), xh, xa, two_near, bias_other)
    xd = flip(xh, "zl")
    last_piece = flip(after(last_piece, xh), "zh")
    two_other = end_spread(two_near, xd)
    one_other = end_spread(one_near, xd, two_other[0])
    ga_recv = flip(after(ga_give, xd), "zl")
    rest_high = flip(after(rest_high, xd), "zh")

    pre_one, act_one = ran(
        conv(
            side, turn(), (xl, xa, xh, xd), one, one_other, 0, bias_one, bias_other[0], True
        )
    )
    act_one_other = flip(act_one, "zl")
    ga_own, ga_give = ran(rows_sum(side, turn(), ga_own, ga_recv, half + (halo - 3) * side))
    pre_two, act_two = ran(
        conv(side, turn(), (act_one, act_one_other), two, two_other, 0, bias_two, bias_other[1])
    )
    act_two_other = flip(act_two, "zl")
    ga_recv = flip(after(ga_give, act_two), "zh")
    last_other = jnp.stack(after(hops(after(last_piece, act_one), chips), act_two))
    last_other = last_other, flip(last_other, "core")
    pre_three, act_three = ran(
        conv(side, turn(), (act_two, act_two_other), three, last_other, 0, bias_three, bias_other[2])
    )
    rest_low = flip(jnp.stack(after((rest_own, rest_high), act_three)), "zl")
    cot_far = flip(after(cot_rows, act_three), "zh")
    own_rows = rows_of(act_three, zh * (halo - 3) * side, half)

    gp_three, ga_own, ga_give = ran(
        back(side, turn(), (ga_own, ga_recv, pre_three), three, last_other, 0)
    )
    ga_recv = flip(ga_give, "zl")
    full_x, act_zero = ran(whole_input(side, turn(), xl, xa, xh, xd, rest_high, rest_low))
    keep_three, give_three = ran(
        weight_grad(
            side, half, turn(), gp_three, act_two, act_two_other, chips, (full_x, go, identity_bias_grad)
        )
    )
    gp_two, ga_own, ga_give = ran(
        back(side, turn(), (ga_own, ga_recv, pre_two), two, two_other, 0)
    )
    ga_recv = flip(ga_give, "zl")
    keep_two, give_two = ran(weight_grad(side, half, turn(cot_far), gp_two, act_one, act_one_other, chips))

    gp_mine, gp_theirs, gp_one = ran(slope_back(side, turn(), ga_own, ga_recv, pre_one, half))
    gp_theirs = flip(gp_theirs, "zh")
    recv_three = flip(after(give_three, gp_one), "core")
    recv_two = flip(after(give_two, gp_one), "core")
    gx_own, gx_give = ran(
        back(
            side, turn(), (gp_one,), one, one_other, 0,
            (valid, full_x, go, cot_far, identity_kernel, last_other, half),
        )
    )

    def folds(keep, recv, first, *others):
        for step in range(first, steps):
            keep, give = ran(fold(turn(*others), keep, recv))
            recv = cross(give, step, chips)
        return keep, recv

    keep_deep, give_deep = ran(fold(turn(gp_theirs), keep_three, recv_three, keep_two, recv_two))
    recv_deep = cross(give_deep, 0, chips)
    gx_recv = flip(after(gx_give, keep_deep), "zl")
    own_rows = after(own_rows, keep_deep)
    near_rows = flip(own_rows, "zl")
    far_rows = flip(own_rows, "zh")
    keep_one, give_one = ran(weight_one_grad(side, turn(), gp_mine, gp_theirs, act_zero, chips))
    recv_one = flip(give_one, "core")
    gx_keep, gx_give = ran(slots_sum(turn(), gx_own, gx_recv))
    gx_recv = flip(gx_give, "zh")
    keep_deep, recv_deep = folds(keep_deep, recv_deep, 1)
    keep_one, give_one = ran(fold(turn(), keep_one, recv_one))
    recv_one = cross(give_one, 0, chips)
    slot = 9 * size + 16
    flat = keep_three.shape[1] - 2 * slot
    keep_deep, give_deep, id_rows = ran(
        last_fold(
            turn(), keep_deep, recv_deep, ((0, slot), (2 * slot + flat, slot)), (2 * slot, flat)
        )
    )
    recv_deep = flip(give_deep, "zh")
    far_near_rows = flip(after(far_rows, keep_deep), "zl")
    keep_one, recv_one = folds(keep_one, recv_one, 1)
    full_three = ran(join(turn(), own_rows, near_rows, far_rows, far_near_rows))
    keep_out, give_out = ran(outer(turn(), full_three, go, post_gain, identity_bias_grad, chips))
    recv_out = flip(give_out, "core")
    (total_one,) = ran([last_fold(turn(), keep_one, recv_one)])
    keep_out, give_out = ran(fold(turn(), keep_out, recv_out))
    recv_out = cross(give_out, 0, chips)
    deep_rows = (after(keep_deep, keep_out).astype(f32) + recv_deep.astype(f32)).astype(bf16)
    deep_rows = jnp.concatenate([deep_rows, id_rows])
    near_deep = start_spread(deep_rows)
    block_out = ran(
        finish(turn(deep_rows), valid, full_x, full_three, identity_kernel, out_kernel, identity_bias)
    )
    keep_out, recv_out = folds(keep_out, recv_out, 1)
    gx = ran(input_grad(turn(), gx_keep, gx_recv))
    gx = swap(gx.reshape(images, rows * width // 4, chans), DP)
    (total_out,) = ran([last_fold(turn(), keep_out, recv_out)])
    near_one = start_spread(jnp.concatenate([total_one, total_out]))
    pixels_grad = ran(widen(turn(near_one), gx, rows, width))
    all_deep = end_spread(near_deep, pixels_grad)
    all_one = end_spread(near_one)
    (
        kernel_three_grad,
        bias_three_grad,
        kernel_two_grad,
        bias_two_grad,
        identity_kernel_grad,
        identity_bias_grad,
    ) = ran(final_grads(turn(), *all_deep, ((deep,), (deep,), identity_kernel.shape)))
    kernel_one_grad, bias_one_grad, out_kernel_grad, _ = ran(
        final_grads(turn(), *all_one, ((one.shape[1],), out_kernel.shape))
    )

    return (
        block_out.reshape(cotangent.shape),
        pixels_grad,
        kernel_one_grad.reshape(kernel_one.shape),
        bias_one_grad[0],
        kernel_two_grad.reshape(kernel_two.shape),
        bias_two_grad[0],
        kernel_three_grad.reshape(kernel_three.shape),
        bias_three_grad[0],
        out_kernel_grad,
        identity_kernel_grad,
        identity_bias_grad[0],
    )


def solution(mesh):
    members = mesh.devices.size // mesh.shape["mp"]
    fine = Mesh(
        mesh.devices.reshape(members // 2, 2, 2, mesh.shape["mp"] // 2),
        ("chip", "core", "zh", "zl"),
    )
    return jax.shard_map(
        local,
        mesh=fine,
        in_specs=(
            P(None, DP, None, MP),
            P(),
            P(None, None, None, MP),
            P(MP),
            P(None, None, None, MP),
            P(MP),
            P(None, None, None, MP),
            P(MP),
            P(None, MP),
            P(None, MP),
            P(MP),
            P(DP, None, None, MP),
        ),
        out_specs=(
            P(DP, None, None, MP),
            P(None, DP, None, MP),
            P(None, None, None, MP),
            P(MP),
            P(None, None, None, MP),
            P(MP),
            P(None, None, None, MP),
            P(MP),
            P(None, MP),
            P(None, MP),
            P(MP),
        ),
        check_vma=False,
    )
```

```python
import functools
import math

import jax
import jax.numpy as jnp
from jax import lax
from jax.experimental import pallas as pl
from jax.experimental.pallas import tpu as pltpu
from jax.sharding import Mesh
from jax.sharding import PartitionSpec as P


post_gain = 0.015625
slope = 0.7978845608028654
cubic = 0.044715
halo = 6
bf16 = jnp.bfloat16
f32 = jnp.float32
NT = (((1,), (1,)), ((), ()))
TN = (((0,), (0,)), ((), ()))
NN = (((1,), (0,)), ((), ()))
DP = ("chip", "core")
MP = ("zh", "zl")


def dot(left, right, dims=NN):
    return lax.dot_general(left, right, dims, preferred_element_type=f32)


def gelu(value):
    inner = jnp.tanh(slope * (value + cubic * value * value * value))
    return 0.5 * value * (1.0 + inner)


def gelu_slope(value):
    square = value * value
    inner = jnp.tanh(slope * value * (1.0 + cubic * square))
    climb = slope * (1.0 + 3.0 * cubic * square)
    return 0.5 * (1.0 + inner) + 0.5 * value * (1.0 - inner * inner) * climb


def struct(shape, kind):
    return jax.ShapeDtypeStruct(shape, kind)


def lanes(blocks):
    return blocks[0] if len(blocks) == 1 else jnp.concatenate(blocks, axis=1)


def step_bits(core, chips):
    bits = [1 << n for n in range(chips.bit_length() - 1)]
    for n in range(0, len(bits) - 1, 2) if core else ():
        bits[n], bits[n + 1] = bits[n + 1], bits[n]
    return bits


def mask_of(i, core, chips):
    masks = []
    for which in range(2):
        bits = step_bits(which, chips)
        masks.append(sum(bit for n, bit in enumerate(bits) if i >> (len(bits) - 1 - n) & 1))
    return jnp.where(core == 0, masks[0], masks[1])


def slot_of(mask, core, chips):
    slots = []
    for which in range(2):
        bits = step_bits(which, chips)
        slot = 0
        for n, bit in enumerate(bits):
            slot = slot + ((mask >> (bit.bit_length() - 1)) & 1) * (1 << (len(bits) - 1 - n))
        slots.append(slot)
    return jnp.where(core == 0, slots[0], slots[1])


VMEM = pl.BlockSpec(memory_space=pltpu.VMEM)
SMEM = pl.BlockSpec(memory_space=pltpu.SMEM)
FAR = pl.BlockSpec(memory_space=pl.ANY)
LOAD = "load"


def size_of(array):
    return math.prod(array.shape) * jnp.dtype(array.dtype).itemsize


def call(body, name, ins, outs, scratch=(), spare=6, **more):
    loads = [i for i, (space, _) in enumerate(ins) if space is LOAD]
    spaces = [FAR if space is LOAD else space for space, _ in ins]
    arrays = [array for _, array in ins]
    out_specs = [space for space, _ in outs]
    out_shape = [shape for _, shape in outs]
    held = [arrays[i] for i in loads]
    buffers = [pltpu.VMEM(array.shape, array.dtype) for array in held]
    sems = [pltpu.SemaphoreType.DMA((len(held),))] if held else []
    vmem = sum(size_of(array) for array in held)
    vmem += sum(size_of(a) for space, a in list(ins) + list(outs) if space is VMEM)
    vmem += sum(size_of(b) for b in scratch if b.memory_space == pltpu.VMEM)
    moved = sum(size_of(a) for a in arrays + out_shape)

    def wrapped(*refs):
        inputs = list(refs[: len(ins)])
        outputs = refs[len(ins) : len(ins) + len(outs)]
        rest = refs[len(ins) + len(outs) :]
        kept, tail = rest[: len(held)], rest[len(held) :]
        copies = []
        if held:
            sem, tail = tail[0], tail[1:]
            copies = [
                pltpu.make_async_copy(inputs[i], kept[n], sem.at[n]) for n, i in enumerate(loads)
            ]
        for copy in copies:
            copy.start()
        for n, i in enumerate(loads):
            inputs[i] = kept[n]

        def arrive():
            for copy in copies:
                copy.wait()

        body(arrive, *inputs, *outputs, *tail)

    single = len(outs) == 1
    return pl.pallas_call(
        wrapped,
        in_specs=spaces,
        out_specs=out_specs[0] if single else out_specs,
        out_shape=out_shape[0] if single else out_shape,
        scratch_shapes=buffers + sems + list(scratch),
        compiler_params=pltpu.CompilerParams(vmem_limit_bytes=vmem + (spare << 20)),
        cost_estimate=pl.CostEstimate(flops=0, bytes_accessed=moved, transcendentals=0),
        name=name,
        **more,
    )(*arrays)


def run_copies(pairs, sems):
    for copy in start_copies(pairs, sems):
        copy.wait()


def slice_copies(group, idx_ref, own, blocks, sibling, wbuf):
    chip, core, zh = idx_ref[0], idx_ref[1], idx_ref[2]
    size = blocks.shape[-2]
    pairs = [(own, wbuf.at[zh])]
    for j in range(blocks.shape[0]):
        for source, owner in ((blocks, core), (sibling, 1 - core)):
            home = chip ^ mask_of(j, owner, blocks.shape[0])
            spot = at((2 * home + owner) * size, size, size)
            pairs.append((source.at[j, 9 * group : 9 * group + 9], wbuf.at[1 - zh, :, spot, :]))
    return pairs


def flat_copies(first, idx_ref, blocks, sibling, buffer):
    chip, core = idx_ref[0], idx_ref[1]
    columns, units = buffer.shape[:2]
    chips = blocks.shape[0]
    count = units // (2 * chips)
    pairs = []
    for j in range(chips):
        for source, owner in ((blocks, core), (sibling, 1 - core)):
            home = chip ^ mask_of(j, owner, chips)
            spot = pl.ds((2 * home + owner) * count, count)
            for c in range(columns):
                begin = first + c * count
                pairs.append((source.at[j, begin : begin + count], buffer.at[c, spot]))
    return pairs


def start_copies(pairs, sems):
    copies = [pltpu.make_async_copy(a, b, sems.at[i]) for i, (a, b) in enumerate(pairs)]
    for copy in copies:
        copy.start()
    return copies


def flat_rows(buffer, begin, count):
    columns, _, size, wide = buffer.shape
    return lanes([buffer[c, pl.ds(begin, count)].reshape(count * size, wide) for c in range(columns)])


def halves(spots, side):
    first = (spots // side + 1) // 2 * side
    return ((0, first), (first, spots - first))


def columns_of(size, wide, side):
    return lax.rem(lax.broadcasted_iota(jnp.int32, (size, wide), 0), side)


def at(start, size, unit):
    return pl.ds(pl.multiple_of(start, unit), size)


def pool_body(arrive, x_ref, out_ref):
    arrive()
    rows, width, chans = x_ref.shape[1:]
    half = width // 2
    pixel = lax.broadcasted_iota(jnp.int32, (half, 2 * width), 1)
    place = lax.broadcasted_iota(jnp.int32, (half, 2 * width), 0)
    inside = (lax.rem(pixel, width) >= 2 * place) & (lax.rem(pixel, width) < 2 * place + 2)
    pick = jnp.where(inside, 0.25, 0.0).astype(bf16)
    for image in range(x_ref.shape[0]):
        for row in range(rows // 2):
            window = x_ref[image, 2 * row : 2 * row + 2].reshape(2 * width, chans)
            out_ref[image, row * half : (row + 1) * half, :] = dot(pick, window).astype(bf16)


def pool(pixels):
    images, rows, width, chans = pixels.shape
    shape = struct((images, rows * width // 4, chans), bf16)
    return call(pool_body, "pool", [(LOAD, pixels)], [(VMEM, shape)])


def widen_body(arrive, idx_ref, g_ref, out_ref):
    arrive()
    rows, width, chans = out_ref.shape[1:]
    half = width // 2
    pixel = lax.broadcasted_iota(jnp.int32, (width, half), 0)
    place = lax.broadcasted_iota(jnp.int32, (width, half), 1)
    inside = (pixel >= 2 * place) & (pixel < 2 * place + 2)
    pick = jnp.where(inside, 0.25, 0.0).astype(bf16)
    for image in range(g_ref.shape[0]):
        for row in range(rows // 2):
            wide = dot(pick, g_ref[image, row * half : (row + 1) * half, :]).astype(bf16)
            out_ref[image, 2 * row] = wide
            out_ref[image, 2 * row + 1] = wide


def widen(idx, grad, rows, width):
    images, spots, chans = grad.shape
    step = images // 4
    block = pl.BlockSpec((step, spots, chans), lambda i: (i, 0, 0))
    out = pl.BlockSpec((step, rows, width, chans), lambda i: (i, 0, 0, 0))
    return call(
        widen_body,
        "widen",
        [(SMEM, idx), (block, grad)],
        [(out, struct((images, rows, width, chans), bf16))],
        grid=(4,),
    )


def conv_body(side, first, group, arrive, idx_ref, *refs):
    zh, zl = idx_ref[2], idx_ref[3]
    if first:
        xl, xa, xh, xd, wl, wo, ws, bl, bo, pre_ref, act_ref, xbuf, wbuf, acc, sems = refs
        chans = xl.shape[1]
        spots = xbuf.shape[0]
        begin = zh * (xl.shape[0] - spots)
        pairs = []
        for source, up, along in ((xl, zh, zl), (xa, zh, 1 - zl), (xh, 1 - zh, zl), (xd, 1 - zh, 1 - zl)):
            if source is xl:
                source = xl.at[at(begin, spots, side), :]
            pairs.append((source, xbuf.at[:, at((2 * up + along) * chans, chans, chans)]))
    else:
        xl, xa, wl, wo, ws, bl, bo, pre_ref, act_ref, xbuf, wbuf, acc, sems = refs
        chans = xl.shape[1] // 2
        spots = xbuf.shape[0]
        pairs = []
        for source, along in ((xl, zl), (xa, 1 - zl)):
            for up in range(2):
                pairs.append(
                    (
                        source.at[:, up * chans : (up + 1) * chans],
                        xbuf.at[:, at((2 * up + along) * chans, chans, chans)],
                    )
                )
    run_copies(slice_copies(group, idx_ref, wl, wo, ws, wbuf) + pairs, sems)
    arrive()
    acc[...] = jnp.zeros_like(acc)
    outs = 2 * wl.shape[2]
    for x in range(3):
        weights = lanes([wbuf[u, 3 * y + x] for y in range(3) for u in range(2)])
        for begin, block in halves(spots, side):
            values = xbuf[begin : begin + block, :]
            if first:
                values = gelu(values.astype(f32)).astype(bf16)
            product = dot(values, weights)
            for y in range(3):
                place = begin + side * (2 - y)
                acc[x, place : place + block, :] += product[:, y * outs : (y + 1) * outs]
    own, other = bl[...], bo[...]
    bias = lanes([jnp.where(zh == 0, own, other), jnp.where(zh == 0, other, own)])
    for begin, block in halves(act_ref.shape[0], side):
        column = columns_of(block, outs, side)
        spot = at(begin + side + zh * side, block, side)
        left = pltpu.roll(acc[0, spot, :], 1, 0)
        right = pltpu.roll(acc[2, spot, :], block - 1, 0)
        pre = acc[1, spot, :] + bias
        pre = pre + jnp.where(column > 0, left, 0.0)
        pre = pre + jnp.where(column < side - 1, right, 0.0)
        pre_ref[begin : begin + block, :] = pre
        act_ref[begin : begin + block, :] = gelu(pre).astype(bf16)


def conv(side, idx, sources, own, other, group, bias, bias_other, first=False):
    taps, depth, outs = own.shape
    spots = sources[1].shape[0]
    rows = spots - side
    return call(
        functools.partial(conv_body, side, first, group),
        "conv",
        [(SMEM, idx)]
        + [(FAR, s) for s in sources]
        + [(FAR, own), (FAR, other[0]), (FAR, other[1])]
        + [(VMEM, bias.reshape(1, outs)), (VMEM, bias_other.reshape(1, outs))],
        [(VMEM, struct((rows, 2 * outs), f32)), (VMEM, struct((rows, 2 * outs), bf16))],
        [
            pltpu.VMEM((spots, depth), bf16),
            pltpu.VMEM((2, taps, depth, outs), bf16),
            pltpu.VMEM((3, spots + 2 * side, 2 * outs), f32),
            pltpu.SemaphoreType.DMA((2 * other[0].shape[0] + 5,)),
        ],
        spare=14 if first else 8,
    )


def spread_taps(side, grad, taps_ref):
    pixels, outs = grad.shape
    column = columns_of(pixels, outs, side)
    wide = grad.astype(f32)
    ahead = jnp.where(column < side - 1, pltpu.roll(wide, pixels - 1, 0), 0.0).astype(bf16)
    behind = jnp.where(column > 0, pltpu.roll(wide, 1, 0), 0.0).astype(bf16)
    edge = jnp.zeros((side, 3 * outs), bf16)
    taps_ref[:side, :] = edge
    taps_ref[side + pixels :, :] = edge
    taps_ref[side : side + pixels, :] = jnp.concatenate([ahead, grad, behind], axis=1)


def tap_block(side, taps_ref, begin, block):
    return lanes([taps_ref[at(begin + side * (2 - y), block, side), :] for y in range(3)])


def slope_body(side, arrive, idx_ref, keep_ref, recv_ref, pre_ref, mine_ref, theirs_ref, gp_ref):
    arrive()
    zh = idx_ref[2]
    half, outs = mine_ref.shape
    total = keep_ref[...] + recv_ref[...].astype(f32)
    spots = keep_ref.shape[0]
    pre = pre_ref[at(zh * (pre_ref.shape[0] - spots), spots, side), :]
    gp_ref[...] = (total * gelu_slope(pre)).astype(bf16)
    own = gp_ref[at(zh * (gp_ref.shape[0] - half), half, side), :]
    low, high = own[:, :outs], own[:, outs:]
    mine_ref[...] = jnp.where(zh == 0, low, high)
    theirs_ref[...] = jnp.where(zh == 0, high, low)


def slope_back(side, idx, keep, recv, pre, half):
    outs = pre.shape[1] // 2
    return call(
        functools.partial(slope_body, side),
        "slope_back",
        [(SMEM, idx), (VMEM, keep), (VMEM, recv), (LOAD, pre)],
        [
            (VMEM, struct((half, outs), bf16)),
            (VMEM, struct((half, outs), bf16)),
            (VMEM, struct(keep.shape, bf16)),
        ],
    )


def back_body(side, last, group, arrive, idx_ref, *refs):
    zh, zl = idx_ref[2], idx_ref[3]
    if last:
        valid_ref, grad_ref, x_ref, go_ref, far_ref, idk_ref, wl, wo, ws, po, ps = refs[:11]
        own_ref, give_ref, taps_ref, wbuf, idk_far, sems = refs[11:]
    else:
        keep_ref, recv_ref, pre_ref, wl, wo, ws, gp_ref, own_ref, give_ref, taps_ref, wbuf, sems = refs
    pairs = slice_copies(group, idx_ref, wl, wo, ws, wbuf)
    if last:
        pairs += flat_copies(9, idx_ref, po, ps, idk_far)
    copies = start_copies(pairs, sems)
    arrive()
    if last:
        grad = grad_ref[...]
    else:
        spots = gp_ref.shape[0]

        def window(ref):
            return ref[at(zh * (ref.shape[0] - spots), spots, side), :]

        total = window(keep_ref) + window(recv_ref).astype(f32)
        grad = (total * gelu_slope(window(pre_ref))).astype(bf16)
        gp_ref[...] = grad
    spread_taps(side, grad, taps_ref)
    depth, outs = wl.shape[1:]
    pixels = own_ref.shape[-2]
    start = zh * side
    for copy in copies:
        copy.wait()
    chans = depth // 4

    def rows(index):
        spot = at(index * chans, chans, chans)
        return lanes([wbuf[u, t, spot, :] for t in range(9) for u in range(2)])

    for target, along in ((give_ref, 1 - zl), (own_ref, zl)):
        if last:
            units = chans // idk_far.shape[2]
            for up in range(2):
                index = 2 * up + along
                weights = rows(index)
                near = idk_ref[at(index * chans, chans, chans), :]
                far = flat_rows(idk_far, index * units, units)
                apart = zh * (far_ref.shape[0] - pixels)
                for begin, block in halves(pixels, side):
                    here = at(zh * pixels + begin, block, side)
                    part = dot(tap_block(side, taps_ref, start + begin, block), weights, NT)
                    x = x_ref[here, at(index * chans, chans, chans)]
                    part = part * gelu_slope(x.astype(f32))
                    part = part + dot(go_ref[here, :], near, NT)
                    part = part + valid_ref[0] * dot(far_ref[at(apart + begin, block, side), :], far, NT)
                    target[up, begin : begin + block, :] = part.astype(target.dtype)
        else:
            weights = jnp.concatenate([rows(along), rows(2 + along)], axis=0)
            for begin, block in halves(pixels, side):
                part = dot(tap_block(side, taps_ref, start + begin, block), weights, NT)
                target[begin : begin + block, :] = part.astype(target.dtype)


def back(side, idx, sources, own, other, group, last=None):
    taps, depth, outs = own.shape
    spots = min(sources[0].shape[0], sources[-1].shape[0])
    copies = 2 * other[0].shape[0] + 1
    extra = []
    scratch = []
    if last:
        valid, full_x, go, cot_far, idk, pieces, half = last
        chans = depth // 4
        shape = (2, half, chans)
        results = []
        extra = [(FAR, pieces[0]), (FAR, pieces[1])]
        sources = list(sources) + [full_x, go, cot_far, idk]
        columns, size = idk.shape[1] // 128, pieces[0].shape[2]
        scratch = [pltpu.VMEM((columns, depth // size, size, 128), bf16)]
        copies += 2 * other[0].shape[0] * columns
    else:
        shape = (spots - side, depth // 2)
        results = [(VMEM, struct((spots, 2 * outs), bf16))]
    results += [(VMEM, struct(shape, f32)), (VMEM, struct(shape, bf16))]
    return call(
        functools.partial(back_body, side, bool(last), group),
        "back",
        [(SMEM, idx)]
        + ([(SMEM, last[0])] if last else [])
        + [(LOAD, source) for source in sources]
        + [(FAR, own), (FAR, other[0]), (FAR, other[1])]
        + extra,
        results,
        [pltpu.VMEM((spots + 2 * side, 6 * outs), bf16), pltpu.VMEM((2, taps, depth, outs), bf16)]
        + scratch
        + [pltpu.SemaphoreType.DMA((copies,))],
        spare=14 if last else 10,
    )


def put_blocks(idx_ref, keep_ref, give_ref, part, tap, first_block, size, begin=0):
    chip, core = idx_ref[0], idx_ref[1]
    for b in range(0, part.shape[0] // size, 2):
        even = part[b * size : (b + 1) * size, :]
        odd = part[(b + 1) * size : (b + 2) * size, :]
        mask = chip ^ ((first_block + b) // 2)
        slot = slot_of(mask, core, keep_ref.shape[0])
        give_slot = slot_of(mask, 1 - core, keep_ref.shape[0])
        rows = slice(begin + tap * size, begin + (tap + 1) * size)
        keep_ref[slot, rows, :] = jnp.where(core == 0, even, odd).astype(bf16)
        give_ref[give_slot, rows, :] = jnp.where(core == 0, odd, even).astype(bf16)


def weight_body(side, half, flat, arrive, idx_ref, gp_ref, *refs):
    if flat:
        full_ref, go_ref, bias_ref = refs[:3]
        refs = refs[3:]
    xl, xa, keep_ref, give_ref, xbuf, taps_ref, sems = refs
    arrive()
    zh, zl = idx_ref[2], idx_ref[3]
    chans = xl.shape[1] // 2
    spots = xbuf.shape[0]
    window = at(zh * (xl.shape[0] - spots), spots, side)
    pairs = []
    for source, along in ((xl, zl), (xa, 1 - zl)):
        for up in range(2):
            pairs.append(
                (
                    source.at[window, up * chans : (up + 1) * chans],
                    xbuf.at[:, at((2 * up + along) * chans, chans, chans)],
                )
            )
    run_copies(pairs, sems)
    wide = gp_ref.shape[1]
    outs = wide // 2
    spot = lax.broadcasted_iota(jnp.int32, (spots, wide), 0) - zh * side
    grad = gp_ref[at(zh * (gp_ref.shape[0] - spots), spots, side), :].astype(f32)
    grad = jnp.where((spot >= 0) & (spot < half), grad, 0.0)
    bias = jnp.sum(grad, axis=0, keepdims=True)
    spread_taps(side, grad.astype(bf16), taps_ref)
    blocks = 2 * keep_ref.shape[0]
    depth = xbuf.shape[1]
    size = depth // blocks
    for begin in range(0, depth, 256):
        values = xbuf[:, begin : begin + 256]
        for y in range(3):
            place = side * (2 - y)
            part = dot(values, taps_ref[place : place + spots, :], TN)
            for x in range(3):
                for u in range(2):
                    col = x * wide + u * outs
                    put_blocks(
                        idx_ref, keep_ref, give_ref, part[:, col : col + outs],
                        3 * y + x, begin // size, size, u * (9 * size + 16),
                    )
    for u in range(2):
        row = jnp.broadcast_to(bias[:, u * outs : (u + 1) * outs], (16, outs)).astype(bf16)
        for j in range(keep_ref.shape[0]):
            spot = slice(u * (9 * size + 16) + 9 * size, (u + 1) * (9 * size + 16))
            keep_ref[j, spot, :] = row
            give_ref[j, spot, :] = row
    if flat:
        first = 2 * (9 * size + 16)
        flat_pieces(1.0, idx_ref, full_ref, go_ref, bias_ref, keep_ref, give_ref, first)


def weight_grad(side, half, idx, grad, act, act_other, chips, flat=()):
    spots = half + side
    wide = grad.shape[1]
    outs = wide // 2
    depth = 2 * act.shape[1]
    rows = 2 * (9 * depth // (2 * chips) + 16)
    if flat:
        rows += flat_size(flat[0], flat[1], chips)
    return call(
        functools.partial(weight_body, side, half, bool(flat)),
        "weight_grad",
        [(SMEM, idx), (LOAD, grad)] + [(LOAD, a) for a in flat] + [(FAR, act), (FAR, act_other)],
        [(VMEM, struct((chips, rows, outs), bf16))] * 2,
        [
            pltpu.VMEM((spots, depth), bf16),
            pltpu.VMEM((spots + 2 * side, 3 * wide), bf16),
            pltpu.SemaphoreType.DMA((4,)),
        ],
        spare=10,
    )


def weight_one_body(side, arrive, idx_ref, mine_ref, theirs_ref, x_ref, *refs):
    keep_ref, give_ref, gp_ref, taps_ref = refs
    arrive()
    zh = idx_ref[2]
    half, outs = mine_ref.shape
    gp_ref[at(zh * half, half, side), :] = mine_ref[...]
    gp_ref[at((1 - zh) * half, half, side), :] = theirs_ref[...]
    grad = gp_ref[...]
    bias = jnp.sum(grad.astype(f32), axis=0, keepdims=True)
    spread_taps(side, grad, taps_ref)
    blocks = 2 * keep_ref.shape[0]
    spots, depth = x_ref.shape
    size = depth // blocks
    right = tap_block(side, taps_ref, 0, spots)
    for begin in range(0, depth, 256):
        part = dot(x_ref[:, begin : begin + 256], right, TN)
        for tap in range(9):
            put_blocks(
                idx_ref, keep_ref, give_ref, part[:, tap * outs : (tap + 1) * outs],
                tap, begin // size, size,
            )
    row = jnp.broadcast_to(bias, (16, outs)).astype(bf16)
    first = 9 * size + 16
    for j in range(keep_ref.shape[0]):
        keep_ref[j, 9 * size : first, :] = row
        give_ref[j, 9 * size : first, :] = row


def weight_one_grad(side, idx, mine, theirs, act_zero, chips):
    spots, depth = act_zero.shape
    outs = mine.shape[1]
    rows = 9 * depth // (2 * chips) + 16
    return call(
        functools.partial(weight_one_body, side),
        "weight_one_grad",
        [(SMEM, idx), (LOAD, mine), (LOAD, theirs), (LOAD, act_zero)],
        [(VMEM, struct((chips, rows, outs), bf16))] * 2,
        [
            pltpu.VMEM((spots, outs), bf16),
            pltpu.VMEM((spots + 2 * side, 3 * outs), bf16),
        ],
        spare=14,
    )


def fold_body(pairs, arrive, idx_ref, *refs):
    arrive()
    ins, (keep_ref, give_ref) = refs[: 2 * pairs], refs[2 * pairs :]
    half = keep_ref.shape[0]
    for i in range(2 * half):
        target = keep_ref if i < half else give_ref
        begin = 0
        for keep, recv in zip(ins[0::2], ins[1::2]):
            rows = keep.shape[1]
            total = keep[i].astype(f32) + recv[i].astype(f32)
            target[i % half, begin : begin + rows, :] = total.astype(bf16)
            begin += rows


def fold(idx, *arrays):
    blocks, _, wide = arrays[0].shape
    rows = sum(a.shape[1] for a in arrays[0::2])
    return call(
        functools.partial(fold_body, len(arrays) // 2),
        "fold",
        [(SMEM, idx)] + [(VMEM, a) for a in arrays],
        [(VMEM, struct((blocks // 2, rows, wide), bf16))] * 2,
    )


def last_body(slotted, rest, arrive, idx_ref, keep_in, recv_in, *targets):
    arrive()
    zh = idx_ref[2]

    def put(target, place, begin, rows):
        spot = at(begin, rows, 16)
        total = keep_in[0, spot, :].astype(f32) + recv_in[0, spot, :].astype(f32)
        target[place : place + rows, :] = total.astype(bf16)

    place = 0
    for begin, rows in slotted:
        put(targets[0], place, begin + zh * rows, rows)
        put(targets[1], place, begin + (1 - zh) * rows, rows)
        place += rows
    begin, rows = rest
    put(targets[-1], 0, begin, rows)


def last_fold(idx, keep, recv, slotted=(), rest=None):
    wide = keep.shape[2]
    rest = rest or (0, keep.shape[1])
    rows = sum(size for _, size in slotted)
    sizes = ([rows, rows] if slotted else []) + [rest[1]]
    return call(
        functools.partial(last_body, slotted, rest),
        "last_fold",
        [(SMEM, idx), (VMEM, keep), (VMEM, recv)],
        [(VMEM, struct((size, wide), bf16)) for size in sizes],
    )


def final_body(parts, arrive, idx_ref, own_ref, sib_ref, *refs):
    arrive()
    outs, stages, sems = refs[: 2 * len(parts)], refs[2 * len(parts) : -1], refs[-1]
    chip, core = idx_ref[0], idx_ref[1]
    chips, _, wide = own_ref.shape
    first = 0
    copies = []

    def store(source, target):
        copies.append(pltpu.make_async_copy(source, target, sems.at[len(copies)]))
        copies[-1].start()

    for n, part in enumerate(parts):
        grad_ref, bias_ref, stage = outs[2 * n], outs[2 * n + 1], stages[n]
        size = part[0] // (2 * chips)
        columns = 1 if len(part) == 1 else part[1] // wide
        end = first + size * (9 if len(part) == 1 else columns)
        for c in range(columns):
            row = own_ref[0, end + c : end + c + 1, :].astype(f32)
            bias_ref[:, c * wide : (c + 1) * wide] = row
        for n_row, begin in enumerate(range(first, end, size)):
            for j in range(chips):
                for source, owner in ((own_ref, core), (sib_ref, 1 - core)):
                    home = chip ^ mask_of(j, owner, chips)
                    spot = at((2 * home + owner) * size, size, size)
                    piece = source[j, begin : begin + size, :].astype(f32)
                    if len(part) == 1:
                        stage[n_row, spot, :] = piece
                    else:
                        stage[spot, n_row * wide : (n_row + 1) * wide] = piece
            if len(part) == 1:
                store(stage.at[n_row], grad_ref.at[n_row])
        if len(part) > 1:
            store(stage, grad_ref)
        first = end + 16
    for copy in copies:
        copy.wait()


def final_grads(idx, own, sib, parts):
    wide = own.shape[2]
    results, stages = [], []
    for part in parts:
        shape = (9, part[0], wide) if len(part) == 1 else part
        results += [(FAR, struct(shape, f32)), (VMEM, struct((1, shape[-1]), f32))]
        stages.append(pltpu.VMEM(shape, f32))
    copies = sum(9 if len(part) == 1 else 1 for part in parts)
    return call(
        functools.partial(final_body, parts),
        "final_grads",
        [(SMEM, idx), (VMEM, own), (VMEM, sib)],
        results,
        stages + [pltpu.SemaphoreType.DMA((copies,))],
    )


def flat_pieces(gain, idx_ref, x_ref, go_ref, bias_ref, keep_ref, give_ref, first):
    chip, core = idx_ref[0], idx_ref[1]
    chips, _, wide = keep_ref.shape
    columns = go_ref.shape[1] // wide
    size = x_ref.shape[1] // (2 * chips)
    bias = jnp.concatenate(
        [bias_ref[:, c * wide : (c + 1) * wide] for c in range(columns)]
        + [jnp.zeros((16 - columns, wide), f32)],
        axis=0,
    ).astype(bf16)
    for j in range(chips):
        keep_ref[j, first + columns * size :, :] = bias
        give_ref[j, first + columns * size :, :] = bias
    for begin in range(0, x_ref.shape[1], 256):
        part = gain * dot(x_ref[:, begin : begin + 256], go_ref[...], TN)
        for b in range(0, 256 // size, 2):
            mask = chip ^ ((begin // size + b) // 2)
            slot = slot_of(mask, core, chips)
            give_slot = slot_of(mask, 1 - core, chips)
            for c in range(columns):
                even = part[b * size : (b + 1) * size, c * wide : (c + 1) * wide]
                odd = part[(b + 1) * size : (b + 2) * size, c * wide : (c + 1) * wide]
                spot = slice(first + c * size, first + (c + 1) * size)
                keep_ref[slot, spot, :] = jnp.where(core == 0, even, odd).astype(bf16)
                give_ref[give_slot, spot, :] = jnp.where(core == 0, odd, even).astype(bf16)


def flat_size(x, go, chips):
    return (go.shape[1] // 128) * (x.shape[1] // (2 * chips)) + 16


def outer_body(gain, arrive, idx_ref, x_ref, go_ref, bias_ref, keep_ref, give_ref):
    arrive()
    flat_pieces(gain, idx_ref, x_ref, go_ref, bias_ref, keep_ref, give_ref, 0)


def outer(idx, x, go, gain, bias, chips):
    return call(
        functools.partial(outer_body, gain),
        "outer",
        [(SMEM, idx), (LOAD, x), (LOAD, go), (LOAD, bias)],
        [(VMEM, struct((chips, flat_size(x, go, chips), 128), bf16))] * 2,
        spare=8,
    )


def start_body(arrive, idx_ref, valid_ref, cot_ref, outk_ref, go_ref, bias_ref, own_ref, give_ref):
    arrive()
    zl = idx_ref[3]
    masked = cot_ref[...].astype(f32) * valid_ref[0]
    go_ref[...] = masked.astype(bf16)
    bias_ref[...] = jnp.sum(masked, axis=0, keepdims=True)
    chans = outk_ref.shape[0] // 4
    block = cot_ref.shape[0] // 4
    for target, along in ((give_ref, 1 - zl), (own_ref, zl)):
        weights = jnp.concatenate(
            [outk_ref[at((2 * up + along) * chans, chans, chans), :] for up in range(2)], axis=0
        )
        for begin in range(0, cot_ref.shape[0], block):
            part = post_gain * dot(go_ref[begin : begin + block, :], weights, NT)
            target[begin : begin + block, :] = part.astype(target.dtype)


def start_back(idx, valid, cot, outk):
    spots, outs = cot.shape
    half = outk.shape[0] // 2
    return call(
        start_body,
        "start_back",
        [(SMEM, idx), (SMEM, valid), (LOAD, cot), (LOAD, outk)],
        [
            (VMEM, struct(cot.shape, bf16)),
            (VMEM, struct((1, outs), f32)),
            (VMEM, struct((spots, half), f32)),
            (VMEM, struct((spots, half), bf16)),
        ],
    )


def rows_body(side, arrive, idx_ref, own_ref, recv_ref, keep_ref, give_ref):
    arrive()
    zh = idx_ref[2]
    spots = keep_ref.shape[0]
    apart = own_ref.shape[0] - spots
    for target, begin in ((give_ref, (1 - zh) * apart), (keep_ref, zh * apart)):
        spot = at(begin, spots, side)
        total = own_ref[spot, :] + recv_ref[spot, :].astype(f32)
        target[...] = total.astype(target.dtype)


def rows_sum(side, idx, own, recv, spots):
    shape = (spots, own.shape[1])
    return call(
        functools.partial(rows_body, side),
        "rows_sum",
        [(SMEM, idx), (LOAD, own), (LOAD, recv)],
        [(VMEM, struct(shape, f32)), (VMEM, struct(shape, bf16))],
    )


def slots_body(arrive, idx_ref, own_ref, recv_ref, keep_ref, give_ref):
    arrive()
    zh = idx_ref[2]
    for target, slot in ((give_ref, 1 - zh), (keep_ref, zh)):
        total = own_ref[slot] + recv_ref[slot].astype(f32)
        target[...] = total.astype(bf16)


def slots_sum(idx, own, recv):
    shape = struct(own.shape[1:], bf16)
    return call(
        slots_body,
        "slots_sum",
        [(SMEM, idx), (VMEM, own), (VMEM, recv)],
        [(VMEM, shape), (VMEM, shape)],
    )


def input_body(arrive, idx_ref, keep_ref, recv_ref, out_ref):
    arrive()
    zh = idx_ref[2]
    half = keep_ref.shape[0]
    out_ref[at(zh * half, half, half), :] = keep_ref[...]
    out_ref[at((1 - zh) * half, half, half), :] = recv_ref[...]


def input_grad(idx, keep, recv):
    half, chans = keep.shape
    return call(
        input_body,
        "input_grad",
        [(SMEM, idx), (VMEM, keep), (VMEM, recv)],
        [(VMEM, struct((2 * half, chans), bf16))],
    )


def whole_body(side, arrive, idx_ref, xl, xa, xh, xd, rh, rl, x_ref, act_ref, sems):
    arrive()
    zh, zl = idx_ref[2], idx_ref[3]
    chans = xl.shape[1]
    spots = xa.shape[0]
    rest = xl.shape[0] - spots
    window, outside = at(zh * rest, spots, side), at((1 - zh) * spots, rest, side)

    def cols(up, along):
        return at((2 * up + along) * chans, chans, chans)

    run_copies(
        [
            (xl, x_ref.at[:, cols(zh, zl)]),
            (xa, x_ref.at[window, cols(zh, 1 - zl)]),
            (xh, x_ref.at[window, cols(1 - zh, zl)]),
            (xd, x_ref.at[window, cols(1 - zh, 1 - zl)]),
            (rl.at[0], x_ref.at[outside, cols(zh, 1 - zl)]),
            (rh, x_ref.at[outside, cols(1 - zh, zl)]),
            (rl.at[1], x_ref.at[outside, cols(1 - zh, 1 - zl)]),
        ],
        sems,
    )
    block = x_ref.shape[0] // 8
    for begin in range(0, x_ref.shape[0], block):
        rows = slice(begin, begin + block)
        act_ref[rows, :] = gelu(x_ref[rows, :].astype(f32)).astype(bf16)


def whole_input(side, idx, *parts):
    spots, chans = parts[0].shape
    return call(
        functools.partial(whole_body, side),
        "whole_input",
        [(SMEM, idx)] + [(FAR, p) for p in parts],
        [(VMEM, struct((spots, 4 * chans), bf16))] * 2,
        [pltpu.SemaphoreType.DMA((7,))],
    )


def join_body(arrive, idx_ref, own, recv, far_own, far_recv, out, sems):
    arrive()
    zh, zl = idx_ref[2], idx_ref[3]
    half = own.shape[0]
    chans = own.shape[1] // 2
    pairs = []
    for source, up, along in ((own, zh, zl), (recv, zh, 1 - zl), (far_own, 1 - zh, zl), (far_recv, 1 - zh, 1 - zl)):
        for slot in range(2):
            spot = at((2 * slot + along) * chans, chans, chans)
            target = out.at[at(up * half, half, half), spot]
            pairs.append((source.at[:, slot * chans : (slot + 1) * chans], target))
    run_copies(pairs, sems)


def join(idx, *parts):
    half, wide = parts[0].shape
    return call(
        join_body,
        "join",
        [(SMEM, idx)] + [(FAR, p) for p in parts],
        [(VMEM, struct((2 * half, 2 * wide), bf16))],
        [pltpu.SemaphoreType.DMA((8,))],
    )


def finish_body(arrive, idx_ref, valid_ref, x_ref, act_ref, idk_ref, outk_ref, ib_ref, out_ref):
    arrive()
    block = x_ref.shape[0] // 4
    for begin in range(0, x_ref.shape[0], block):
        rows = slice(begin, begin + block)
        identity = dot(x_ref[rows, :], idk_ref[...]) + ib_ref[...]
        branch = dot(act_ref[rows, :], outk_ref[...])
        out_ref[rows, :] = ((identity + post_gain * branch) * valid_ref[0]).astype(bf16)


def finish(idx, valid, x, act, idk, outk, ib):
    outs = idk.shape[1]
    return call(
        finish_body,
        "finish",
        [(SMEM, idx), (SMEM, valid), (LOAD, x), (LOAD, act), (LOAD, idk), (LOAD, outk)]
        + [(VMEM, ib.reshape(1, outs))],
        [(VMEM, struct((x.shape[0], outs), bf16))],
        spare=8,
    )


def flip(value, axis):
    return lax.ppermute(value, axis, [(0, 1), (1, 0)])


def cross(value, step, chips):
    pairs = []
    for chip in range(chips):
        for core in range(2):
            other = chip ^ step_bits(core, chips)[step]
            pairs.append((2 * chip + core, 2 * other + core))
    return lax.ppermute(value, DP, pairs)


def hops(value, chips):
    blocks = [value]
    for i in range(1, chips):
        pairs = []
        for chip in range(chips):
            for core in range(2):
                bits = step_bits(core, chips)
                mask = sum(bit for n, bit in enumerate(bits) if i >> (len(bits) - 1 - n) & 1)
                pairs.append((2 * (chip ^ mask) + core, 2 * chip + core))
        blocks.append(lax.ppermute(value, DP, pairs))
    return blocks


def swap(pieces, axis):
    return lax.all_to_all(pieces, axis, split_axis=0, concat_axis=0, tiled=True)


def after(value, other):
    return lax.optimization_barrier((value, other))[0]


def rows_of(value, start, size):
    return lax.dynamic_slice_in_dim(value, start, size, 0)


def local(
    pixels,
    counts,
    kernel_one,
    bias_one,
    kernel_two,
    bias_two,
    kernel_three,
    bias_three,
    out_kernel,
    identity_kernel,
    identity_bias,
    cotangent,
):
    images, rows, width, chans = pixels.shape
    side = width // 2
    spots = side * side
    half = spots // 2
    window = half + halo * side
    outs = cotangent.shape[3]
    chips = lax.axis_size("chip")
    chip, core, zh, zl = [lax.axis_index(a) for a in ("chip", "core", "zh", "zl")]
    idx = jnp.stack([chip, core, zh, zl]).astype(jnp.int32)
    taps = lambda kernel: kernel.reshape((9,) + kernel.shape[2:])
    one, two, three = taps(kernel_one), taps(kernel_two), taps(kernel_three)

    own_count = lax.dynamic_index_in_dim(counts, 2 * chip + core, 0, keepdims=True)
    valid = (own_count > 0).astype(f32)

    place = 2 * chip + core

    def units_of(kernel, size):
        if kernel.ndim == 3:
            block = kernel.shape[1] // (2 * chips)
            return lax.dynamic_slice_in_dim(kernel, place * block, block, 1)
        block = kernel.shape[0] // (2 * chips)
        block = lax.dynamic_slice_in_dim(kernel, place * block, block, 0)
        block = block.reshape(-1, size, block.shape[1] // 128, 128)
        return block.transpose(2, 0, 1, 3).reshape(-1, size, 128)

    steps = chips.bit_length() - 1

    def start_spread(piece, *others):
        return jnp.concatenate(after((piece[None], cross(piece[None], steps - 1, chips)), others))

    def end_spread(own, *others):
        for step in reversed(range(steps - 1)):
            own = jnp.concatenate(after((own, cross(own, step, chips)), others))
        return own, flip(own, "core")

    last = [idx]

    def turn(*others):
        return after(idx, (last[0],) + others)

    def ran(results):
        last[0] = results[-1] if isinstance(results, (list, tuple)) else results
        return results

    size = two.shape[1] // (2 * chips)
    deep = two.shape[1]
    cot = cotangent.reshape(spots, outs)
    one_piece = flip(units_of(one, size), "zh")
    pooled = ran(pool(pixels))
    go, identity_bias_grad, ga_own, ga_give = ran(start_back(turn(), valid, cot, out_kernel))
    bias_other = flip(after(jnp.stack([bias_one, bias_two, bias_three]), go), "zh")
    two_piece = units_of(after(two, pooled), size)
    last_piece = jnp.concatenate([units_of(after(k, pooled), size) for k in (three, identity_kernel)])
    cot_rows = rows_of(after(cot, pooled), (1 - zh) * half, half)
    xl = swap(after(pooled, (one_piece, two_piece, last_piece, cot_rows, ga_give)), DP)
    xl = xl.reshape(spots, chans)
    two_piece = flip(after(two_piece, one_piece), "zh")

    apart = spots - window
    xa = flip(rows_of(xl, zh * apart, window), "zl")
    xh = flip(rows_of(xl, (1 - zh) * apart, window), "zh")
    rest = spots - window
    rest_own = rows_of(xl, (1 - zh) * window, rest)
    rest_high = rows_of(xl, zh * window, rest)
    two_near = start_spread(after(two_piece, xl))
    one_near = start_spread(after(one_piece, xl), xh, xa, two_near, bias_other)
    xd = flip(xh, "zl")
    last_piece = flip(after(last_piece, xh), "zh")
    two_other = end_spread(two_near, xd)
    one_other = end_spread(one_near, xd, two_other[0], last_piece)
    ga_recv = flip(after(ga_give, xd), "zl")
    rest_high = flip(after(rest_high, xd), "zh")

    pre_one, act_one = ran(
        conv(
            side, turn(), (xl, xa, xh, xd), one, one_other, 0, bias_one, bias_other[0], True
        )
    )
    act_one_other = flip(act_one, "zl")
    ga_own, ga_give = ran(rows_sum(side, turn(), ga_own, ga_recv, half + (halo - 3) * side))
    pre_two, act_two = ran(
        conv(side, turn(), (act_one, act_one_other), two, two_other, 0, bias_two, bias_other[1])
    )
    act_two_other = flip(act_two, "zl")
    ga_recv = flip(after(ga_give, act_two), "zh")
    last_other = jnp.stack(after(hops(after(last_piece, act_one), chips), act_two))
    last_other = last_other, flip(last_other, "core")
    pre_three, act_three = ran(
        conv(side, turn(), (act_two, act_two_other), three, last_other, 0, bias_three, bias_other[2])
    )
    rest_low = flip(jnp.stack(after((rest_own, rest_high), act_three)), "zl")
    cot_far = flip(after(cot_rows, act_three), "zh")
    own_rows = rows_of(act_three, zh * (halo - 3) * side, half)

    gp_three, ga_own, ga_give = ran(
        back(side, turn(), (ga_own, ga_recv, pre_three), three, last_other, 0)
    )
    ga_recv = flip(ga_give, "zl")
    full_x, act_zero = ran(whole_input(side, turn(), xl, xa, xh, xd, rest_high, rest_low))
    keep_three, give_three = ran(
        weight_grad(
            side, half, turn(), gp_three, act_two, act_two_other, chips, (full_x, go, identity_bias_grad)
        )
    )
    gp_two, ga_own, ga_give = ran(
        back(side, turn(), (ga_own, ga_recv, pre_two), two, two_other, 0)
    )
    ga_recv = flip(ga_give, "zl")
    keep_two, give_two = ran(weight_grad(side, half, turn(cot_far), gp_two, act_one, act_one_other, chips))

    gp_mine, gp_theirs, gp_one = ran(slope_back(side, turn(), ga_own, ga_recv, pre_one, half))
    gp_theirs = flip(gp_theirs, "zh")
    recv_three = flip(after(give_three, gp_one), "core")
    recv_two = flip(after(give_two, gp_one), "core")
    gx_own, gx_give = ran(
        back(
            side, turn(), (gp_one,), one, one_other, 0,
            (valid, full_x, go, cot_far, identity_kernel, last_other, half),
        )
    )

    def folds(keep, recv, first, *others):
        for step in range(first, steps):
            keep, give = ran(fold(turn(*others), keep, recv))
            recv = cross(give, step, chips)
        return keep, recv

    keep_deep, give_deep = ran(fold(turn(gp_theirs), keep_three, recv_three, keep_two, recv_two))
    recv_deep = cross(give_deep, 0, chips)
    gx_recv = flip(after(gx_give, keep_deep), "zl")
    own_rows = after(own_rows, keep_deep)
    near_rows = flip(own_rows, "zl")
    far_rows = flip(own_rows, "zh")
    keep_one, give_one = ran(weight_one_grad(side, turn(), gp_mine, gp_theirs, act_zero, chips))
    recv_one = flip(give_one, "core")
    keep_deep, recv_deep = folds(keep_deep, recv_deep, 1, far_rows)
    gx_keep, gx_give = ran(slots_sum(turn(), gx_own, gx_recv))
    gx_recv = flip(gx_give, "zh")
    keep_one, give_one = ran(fold(turn(), keep_one, recv_one))
    recv_one = cross(give_one, 0, chips)
    slot = 9 * size + 16
    flat = keep_three.shape[1] - 2 * slot
    keep_deep, give_deep, id_rows = ran(
        last_fold(
            turn(), keep_deep, recv_deep, ((0, slot), (2 * slot + flat, slot)), (2 * slot, flat)
        )
    )
    recv_deep = flip(give_deep, "zh")
    far_near_rows = flip(after(far_rows, keep_deep), "zl")
    keep_one, recv_one = folds(keep_one, recv_one, 1)
    full_three = ran(join(turn(), own_rows, near_rows, far_rows, far_near_rows))
    keep_out, give_out = ran(outer(turn(), full_three, go, post_gain, identity_bias_grad, chips))
    recv_out = flip(give_out, "core")
    (total_one,) = ran([last_fold(turn(), keep_one, recv_one)])
    keep_out, give_out = ran(fold(turn(), keep_out, recv_out))
    recv_out = cross(give_out, 0, chips)
    gx = ran(input_grad(turn(), gx_keep, gx_recv))
    gx = swap(gx.reshape(images, rows * width // 4, chans), DP)
    deep_rows = (after(keep_deep, keep_out).astype(f32) + recv_deep.astype(f32)).astype(bf16)
    deep_rows = jnp.concatenate([deep_rows, id_rows])
    near_deep = start_spread(deep_rows)
    block_out = ran(
        finish(turn(deep_rows), valid, full_x, full_three, identity_kernel, out_kernel, identity_bias)
    )
    keep_out, recv_out = folds(keep_out, recv_out, 1)
    (total_out,) = ran([last_fold(turn(), keep_out, recv_out)])
    near_one = start_spread(jnp.concatenate([total_one, total_out]))
    pixels_grad = ran(widen(turn(near_one, near_deep), gx, rows, width))
    all_deep = end_spread(near_deep, pixels_grad)
    all_one = end_spread(near_one)
    (
        kernel_three_grad,
        bias_three_grad,
        kernel_two_grad,
        bias_two_grad,
        identity_kernel_grad,
        identity_bias_grad,
    ) = ran(final_grads(turn(), *all_deep, ((deep,), (deep,), identity_kernel.shape)))
    kernel_one_grad, bias_one_grad, out_kernel_grad, _ = ran(
        final_grads(turn(), *all_one, ((one.shape[1],), out_kernel.shape))
    )

    return (
        block_out.reshape(cotangent.shape),
        pixels_grad,
        kernel_one_grad.reshape(kernel_one.shape),
        bias_one_grad[0],
        kernel_two_grad.reshape(kernel_two.shape),
        bias_two_grad[0],
        kernel_three_grad.reshape(kernel_three.shape),
        bias_three_grad[0],
        out_kernel_grad,
        identity_kernel_grad,
        identity_bias_grad[0],
    )


def solution(mesh):
    members = mesh.devices.size // mesh.shape["mp"]
    fine = Mesh(
        mesh.devices.reshape(members // 2, 2, 2, mesh.shape["mp"] // 2),
        ("chip", "core", "zh", "zl"),
    )
    return jax.shard_map(
        local,
        mesh=fine,
        in_specs=(
            P(None, DP, None, MP),
            P(),
            P(None, None, None, MP),
            P(MP),
            P(None, None, None, MP),
            P(MP),
            P(None, None, None, MP),
            P(MP),
            P(None, MP),
            P(None, MP),
            P(MP),
            P(DP, None, None, MP),
        ),
        out_specs=(
            P(DP, None, None, MP),
            P(None, DP, None, MP),
            P(None, None, None, MP),
            P(MP),
            P(None, None, None, MP),
            P(MP),
            P(None, None, None, MP),
            P(MP),
            P(None, MP),
            P(None, MP),
            P(MP),
        ),
        check_vma=False,
    )
```

```python
import functools
import math

import jax
import jax.numpy as jnp
from jax import lax
from jax.experimental import pallas as pl
from jax.experimental.pallas import tpu as pltpu
from jax.sharding import Mesh
from jax.sharding import PartitionSpec as P


post_gain = 0.015625
slope = 0.7978845608028654
cubic = 0.044715
halo = 6
bf16 = jnp.bfloat16
f32 = jnp.float32
NT = (((1,), (1,)), ((), ()))
TN = (((0,), (0,)), ((), ()))
NN = (((1,), (0,)), ((), ()))
DP = ("chip", "core")
MP = ("zh", "zl")


def dot(left, right, dims=NN):
    return lax.dot_general(left, right, dims, preferred_element_type=f32)


def gelu(value):
    inner = jnp.tanh(slope * (value + cubic * value * value * value))
    return 0.5 * value * (1.0 + inner)


def gelu_slope(value):
    square = value * value
    inner = jnp.tanh(slope * value * (1.0 + cubic * square))
    climb = slope * (1.0 + 3.0 * cubic * square)
    return 0.5 * (1.0 + inner) + 0.5 * value * (1.0 - inner * inner) * climb


def struct(shape, kind):
    return jax.ShapeDtypeStruct(shape, kind)


def lanes(blocks):
    return blocks[0] if len(blocks) == 1 else jnp.concatenate(blocks, axis=1)


def step_bits(core, chips):
    bits = [1 << n for n in range(chips.bit_length() - 1)]
    for n in range(0, len(bits) - 1, 2) if core else ():
        bits[n], bits[n + 1] = bits[n + 1], bits[n]
    return bits


def mask_of(i, core, chips):
    masks = []
    for which in range(2):
        bits = step_bits(which, chips)
        masks.append(sum(bit for n, bit in enumerate(bits) if i >> (len(bits) - 1 - n) & 1))
    return jnp.where(core == 0, masks[0], masks[1])


def slot_of(mask, core, chips):
    slots = []
    for which in range(2):
        bits = step_bits(which, chips)
        slot = 0
        for n, bit in enumerate(bits):
            slot = slot + ((mask >> (bit.bit_length() - 1)) & 1) * (1 << (len(bits) - 1 - n))
        slots.append(slot)
    return jnp.where(core == 0, slots[0], slots[1])


VMEM = pl.BlockSpec(memory_space=pltpu.VMEM)
SMEM = pl.BlockSpec(memory_space=pltpu.SMEM)
FAR = pl.BlockSpec(memory_space=pl.ANY)
LOAD = "load"


def size_of(array):
    return math.prod(array.shape) * jnp.dtype(array.dtype).itemsize


def call(body, name, ins, outs, scratch=(), spare=6, **more):
    loads = [i for i, (space, _) in enumerate(ins) if space is LOAD]
    spaces = [FAR if space is LOAD else space for space, _ in ins]
    arrays = [array for _, array in ins]
    out_specs = [space for space, _ in outs]
    out_shape = [shape for _, shape in outs]
    held = [arrays[i] for i in loads]
    buffers = [pltpu.VMEM(array.shape, array.dtype) for array in held]
    sems = [pltpu.SemaphoreType.DMA((len(held),))] if held else []
    vmem = sum(size_of(array) for array in held)
    vmem += sum(size_of(a) for space, a in list(ins) + list(outs) if space is VMEM)
    vmem += sum(size_of(b) for b in scratch if b.memory_space == pltpu.VMEM)
    moved = sum(size_of(a) for a in arrays + out_shape)

    def wrapped(*refs):
        inputs = list(refs[: len(ins)])
        outputs = refs[len(ins) : len(ins) + len(outs)]
        rest = refs[len(ins) + len(outs) :]
        kept, tail = rest[: len(held)], rest[len(held) :]
        copies = []
        if held:
            sem, tail = tail[0], tail[1:]
            copies = [
                pltpu.make_async_copy(inputs[i], kept[n], sem.at[n]) for n, i in enumerate(loads)
            ]
        for copy in copies:
            copy.start()
        for n, i in enumerate(loads):
            inputs[i] = kept[n]

        def arrive():
            for copy in copies:
                copy.wait()

        body(arrive, *inputs, *outputs, *tail)

    single = len(outs) == 1
    return pl.pallas_call(
        wrapped,
        in_specs=spaces,
        out_specs=out_specs[0] if single else out_specs,
        out_shape=out_shape[0] if single else out_shape,
        scratch_shapes=buffers + sems + list(scratch),
        compiler_params=pltpu.CompilerParams(vmem_limit_bytes=vmem + (spare << 20)),
        cost_estimate=pl.CostEstimate(flops=0, bytes_accessed=moved, transcendentals=0),
        name=name,
        **more,
    )(*arrays)


def run_copies(pairs, sems):
    for copy in start_copies(pairs, sems):
        copy.wait()


def slice_copies(group, idx_ref, own, blocks, sibling, wbuf):
    chip, core, zh = idx_ref[0], idx_ref[1], idx_ref[2]
    size = blocks.shape[-2]
    pairs = [(own, wbuf.at[zh])]
    for j in range(blocks.shape[0]):
        for source, owner in ((blocks, core), (sibling, 1 - core)):
            home = chip ^ mask_of(j, owner, blocks.shape[0])
            spot = at((2 * home + owner) * size, size, size)
            pairs.append((source.at[j, 9 * group : 9 * group + 9], wbuf.at[1 - zh, :, spot, :]))
    return pairs


def flat_copies(first, idx_ref, blocks, sibling, buffer):
    chip, core = idx_ref[0], idx_ref[1]
    columns, units = buffer.shape[:2]
    chips = blocks.shape[0]
    count = units // (2 * chips)
    pairs = []
    for j in range(chips):
        for source, owner in ((blocks, core), (sibling, 1 - core)):
            home = chip ^ mask_of(j, owner, chips)
            spot = pl.ds((2 * home + owner) * count, count)
            for c in range(columns):
                begin = first + c * count
                pairs.append((source.at[j, begin : begin + count], buffer.at[c, spot]))
    return pairs


def start_copies(pairs, sems):
    copies = [pltpu.make_async_copy(a, b, sems.at[i]) for i, (a, b) in enumerate(pairs)]
    for copy in copies:
        copy.start()
    return copies


def flat_rows(buffer, begin, count):
    columns, _, size, wide = buffer.shape
    return lanes([buffer[c, pl.ds(begin, count)].reshape(count * size, wide) for c in range(columns)])


def halves(spots, side):
    first = (spots // side + 1) // 2 * side
    return ((0, first), (first, spots - first))


def columns_of(size, wide, side):
    return lax.rem(lax.broadcasted_iota(jnp.int32, (size, wide), 0), side)


def at(start, size, unit):
    return pl.ds(pl.multiple_of(start, unit), size)


def pool_body(arrive, x_ref, out_ref):
    arrive()
    rows, width, chans = x_ref.shape[1:]
    half = width // 2
    pixel = lax.broadcasted_iota(jnp.int32, (half, 2 * width), 1)
    place = lax.broadcasted_iota(jnp.int32, (half, 2 * width), 0)
    inside = (lax.rem(pixel, width) >= 2 * place) & (lax.rem(pixel, width) < 2 * place + 2)
    pick = jnp.where(inside, 0.25, 0.0).astype(bf16)
    for image in range(x_ref.shape[0]):
        for row in range(rows // 2):
            window = x_ref[image, 2 * row : 2 * row + 2].reshape(2 * width, chans)
            out_ref[image, row * half : (row + 1) * half, :] = dot(pick, window).astype(bf16)


def pool(pixels):
    images, rows, width, chans = pixels.shape
    shape = struct((images, rows * width // 4, chans), bf16)
    return call(pool_body, "pool", [(LOAD, pixels)], [(VMEM, shape)])


def widen_body(arrive, idx_ref, g_ref, out_ref):
    arrive()
    rows, width, chans = out_ref.shape[1:]
    half = width // 2
    pixel = lax.broadcasted_iota(jnp.int32, (width, half), 0)
    place = lax.broadcasted_iota(jnp.int32, (width, half), 1)
    inside = (pixel >= 2 * place) & (pixel < 2 * place + 2)
    pick = jnp.where(inside, 0.25, 0.0).astype(bf16)
    for image in range(g_ref.shape[0]):
        for row in range(rows // 2):
            wide = dot(pick, g_ref[image, row * half : (row + 1) * half, :]).astype(bf16)
            out_ref[image, 2 * row] = wide
            out_ref[image, 2 * row + 1] = wide


def widen(idx, grad, rows, width):
    images, spots, chans = grad.shape
    step = images // 4
    block = pl.BlockSpec((step, spots, chans), lambda i: (i, 0, 0))
    out = pl.BlockSpec((step, rows, width, chans), lambda i: (i, 0, 0, 0))
    return call(
        widen_body,
        "widen",
        [(SMEM, idx), (block, grad)],
        [(out, struct((images, rows, width, chans), bf16))],
        grid=(4,),
    )


def conv_body(side, first, group, arrive, idx_ref, *refs):
    zh, zl = idx_ref[2], idx_ref[3]
    if first:
        xl, xa, xh, xd, wl, wo, ws, bl, bo, pre_ref, act_ref, xbuf, wbuf, acc, sems = refs
        chans = xl.shape[1]
        spots = xbuf.shape[0]
        begin = zh * (xl.shape[0] - spots)
        pairs = []
        for source, up, along in ((xl, zh, zl), (xa, zh, 1 - zl), (xh, 1 - zh, zl), (xd, 1 - zh, 1 - zl)):
            if source is xl:
                source = xl.at[at(begin, spots, side), :]
            pairs.append((source, xbuf.at[:, at((2 * up + along) * chans, chans, chans)]))
    else:
        xl, xa, wl, wo, ws, bl, bo, pre_ref, act_ref, xbuf, wbuf, acc, sems = refs
        chans = xl.shape[1] // 2
        spots = xbuf.shape[0]
        pairs = []
        for source, along in ((xl, zl), (xa, 1 - zl)):
            for up in range(2):
                pairs.append(
                    (
                        source.at[:, up * chans : (up + 1) * chans],
                        xbuf.at[:, at((2 * up + along) * chans, chans, chans)],
                    )
                )
    run_copies(slice_copies(group, idx_ref, wl, wo, ws, wbuf) + pairs, sems)
    arrive()
    acc[...] = jnp.zeros_like(acc)
    outs = 2 * wl.shape[2]
    for x in range(3):
        weights = lanes([wbuf[u, 3 * y + x] for y in range(3) for u in range(2)])
        for begin, block in halves(spots, side):
            values = xbuf[begin : begin + block, :]
            if first:
                values = gelu(values.astype(f32)).astype(bf16)
            product = dot(values, weights)
            for y in range(3):
                place = begin + side * (2 - y)
                acc[x, place : place + block, :] += product[:, y * outs : (y + 1) * outs]
    own, other = bl[...], bo[...]
    bias = lanes([jnp.where(zh == 0, own, other), jnp.where(zh == 0, other, own)])
    for begin, block in halves(act_ref.shape[0], side):
        column = columns_of(block, outs, side)
        spot = at(begin + side + zh * side, block, side)
        left = pltpu.roll(acc[0, spot, :], 1, 0)
        right = pltpu.roll(acc[2, spot, :], block - 1, 0)
        pre = acc[1, spot, :] + bias
        pre = pre + jnp.where(column > 0, left, 0.0)
        pre = pre + jnp.where(column < side - 1, right, 0.0)
        pre_ref[begin : begin + block, :] = pre
        act_ref[begin : begin + block, :] = gelu(pre).astype(bf16)


def conv(side, idx, sources, own, other, group, bias, bias_other, first=False):
    taps, depth, outs = own.shape
    spots = sources[1].shape[0]
    rows = spots - side
    return call(
        functools.partial(conv_body, side, first, group),
        "conv",
        [(SMEM, idx)]
        + [(FAR, s) for s in sources]
        + [(FAR, own), (FAR, other[0]), (FAR, other[1])]
        + [(VMEM, bias.reshape(1, outs)), (VMEM, bias_other.reshape(1, outs))],
        [(VMEM, struct((rows, 2 * outs), f32)), (VMEM, struct((rows, 2 * outs), bf16))],
        [
            pltpu.VMEM((spots, depth), bf16),
            pltpu.VMEM((2, taps, depth, outs), bf16),
            pltpu.VMEM((3, spots + 2 * side, 2 * outs), f32),
            pltpu.SemaphoreType.DMA((2 * other[0].shape[0] + 5,)),
        ],
        spare=14 if first else 8,
    )


def spread_taps(side, grad, taps_ref):
    pixels, outs = grad.shape
    column = columns_of(pixels, outs, side)
    wide = grad.astype(f32)
    ahead = jnp.where(column < side - 1, pltpu.roll(wide, pixels - 1, 0), 0.0).astype(bf16)
    behind = jnp.where(column > 0, pltpu.roll(wide, 1, 0), 0.0).astype(bf16)
    edge = jnp.zeros((side, 3 * outs), bf16)
    taps_ref[:side, :] = edge
    taps_ref[side + pixels :, :] = edge
    taps_ref[side : side + pixels, :] = jnp.concatenate([ahead, grad, behind], axis=1)


def tap_block(side, taps_ref, begin, block):
    return lanes([taps_ref[at(begin + side * (2 - y), block, side), :] for y in range(3)])


def slope_body(side, arrive, idx_ref, keep_ref, recv_ref, pre_ref, mine_ref, theirs_ref, gp_ref):
    arrive()
    zh = idx_ref[2]
    half, outs = mine_ref.shape
    total = keep_ref[...] + recv_ref[...].astype(f32)
    spots = keep_ref.shape[0]
    pre = pre_ref[at(zh * (pre_ref.shape[0] - spots), spots, side), :]
    gp_ref[...] = (total * gelu_slope(pre)).astype(bf16)
    own = gp_ref[at(zh * (gp_ref.shape[0] - half), half, side), :]
    low, high = own[:, :outs], own[:, outs:]
    mine_ref[...] = jnp.where(zh == 0, low, high)
    theirs_ref[...] = jnp.where(zh == 0, high, low)


def slope_back(side, idx, keep, recv, pre, half):
    outs = pre.shape[1] // 2
    return call(
        functools.partial(slope_body, side),
        "slope_back",
        [(SMEM, idx), (VMEM, keep), (VMEM, recv), (LOAD, pre)],
        [
            (VMEM, struct((half, outs), bf16)),
            (VMEM, struct((half, outs), bf16)),
            (VMEM, struct(keep.shape, bf16)),
        ],
    )


def back_body(side, last, group, arrive, idx_ref, *refs):
    zh, zl = idx_ref[2], idx_ref[3]
    if last:
        valid_ref, grad_ref, x_ref, go_ref, far_ref, idk_ref, wl, wo, ws, po, ps = refs[:11]
        own_ref, give_ref, taps_ref, wbuf, idk_far, sems = refs[11:]
    else:
        keep_ref, recv_ref, pre_ref, wl, wo, ws, gp_ref, own_ref, give_ref, taps_ref, wbuf, sems = refs
    pairs = slice_copies(group, idx_ref, wl, wo, ws, wbuf)
    if last:
        pairs += flat_copies(9, idx_ref, po, ps, idk_far)
    copies = start_copies(pairs, sems)
    arrive()
    if last:
        grad = grad_ref[...]
    else:
        spots = gp_ref.shape[0]

        def window(ref):
            return ref[at(zh * (ref.shape[0] - spots), spots, side), :]

        total = window(keep_ref) + window(recv_ref).astype(f32)
        grad = (total * gelu_slope(window(pre_ref))).astype(bf16)
        gp_ref[...] = grad
    spread_taps(side, grad, taps_ref)
    depth, outs = wl.shape[1:]
    pixels = own_ref.shape[-2]
    start = zh * side
    for copy in copies:
        copy.wait()
    chans = depth // 4

    def rows(index):
        spot = at(index * chans, chans, chans)
        return lanes([wbuf[u, t, spot, :] for t in range(9) for u in range(2)])

    for target, along in ((give_ref, 1 - zl), (own_ref, zl)):
        if last:
            units = chans // idk_far.shape[2]
            for up in range(2):
                index = 2 * up + along
                weights = rows(index)
                near = idk_ref[at(index * chans, chans, chans), :]
                far = flat_rows(idk_far, index * units, units)
                apart = zh * (far_ref.shape[0] - pixels)
                for begin, block in halves(pixels, side):
                    here = at(zh * pixels + begin, block, side)
                    part = dot(tap_block(side, taps_ref, start + begin, block), weights, NT)
                    x = x_ref[here, at(index * chans, chans, chans)]
                    part = part * gelu_slope(x.astype(f32))
                    part = part + dot(go_ref[here, :], near, NT)
                    part = part + valid_ref[0] * dot(far_ref[at(apart + begin, block, side), :], far, NT)
                    target[up, begin : begin + block, :] = part.astype(target.dtype)
        else:
            weights = jnp.concatenate([rows(along), rows(2 + along)], axis=0)
            for begin, block in halves(pixels, side):
                part = dot(tap_block(side, taps_ref, start + begin, block), weights, NT)
                target[begin : begin + block, :] = part.astype(target.dtype)


def back(side, idx, sources, own, other, group, last=None):
    taps, depth, outs = own.shape
    spots = min(sources[0].shape[0], sources[-1].shape[0])
    copies = 2 * other[0].shape[0] + 1
    extra = []
    scratch = []
    if last:
        valid, full_x, go, cot_far, idk, pieces, half = last
        chans = depth // 4
        shape = (2, half, chans)
        results = []
        extra = [(FAR, pieces[0]), (FAR, pieces[1])]
        sources = list(sources) + [full_x, go, cot_far, idk]
        columns, size = idk.shape[1] // 128, pieces[0].shape[2]
        scratch = [pltpu.VMEM((columns, depth // size, size, 128), bf16)]
        copies += 2 * other[0].shape[0] * columns
    else:
        shape = (spots - side, depth // 2)
        results = [(VMEM, struct((spots, 2 * outs), bf16))]
    results += [(VMEM, struct(shape, f32)), (VMEM, struct(shape, bf16))]
    return call(
        functools.partial(back_body, side, bool(last), group),
        "back",
        [(SMEM, idx)]
        + ([(SMEM, last[0])] if last else [])
        + [(LOAD, source) for source in sources]
        + [(FAR, own), (FAR, other[0]), (FAR, other[1])]
        + extra,
        results,
        [pltpu.VMEM((spots + 2 * side, 6 * outs), bf16), pltpu.VMEM((2, taps, depth, outs), bf16)]
        + scratch
        + [pltpu.SemaphoreType.DMA((copies,))],
        spare=14 if last else 10,
    )


def put_blocks(idx_ref, keep_ref, give_ref, part, tap, first_block, size, begin=0):
    chip, core = idx_ref[0], idx_ref[1]
    for b in range(0, part.shape[0] // size, 2):
        even = part[b * size : (b + 1) * size, :]
        odd = part[(b + 1) * size : (b + 2) * size, :]
        mask = chip ^ ((first_block + b) // 2)
        slot = slot_of(mask, core, keep_ref.shape[0])
        give_slot = slot_of(mask, 1 - core, keep_ref.shape[0])
        rows = slice(begin + tap * size, begin + (tap + 1) * size)
        keep_ref[slot, rows, :] = jnp.where(core == 0, even, odd).astype(bf16)
        give_ref[give_slot, rows, :] = jnp.where(core == 0, odd, even).astype(bf16)


def weight_body(side, half, flat, arrive, idx_ref, gp_ref, *refs):
    if flat:
        full_ref, go_ref, bias_ref = refs[:3]
        refs = refs[3:]
    xl, xa, keep_ref, give_ref, xbuf, taps_ref, sems = refs
    arrive()
    zh, zl = idx_ref[2], idx_ref[3]
    chans = xl.shape[1] // 2
    spots = xbuf.shape[0]
    window = at(zh * (xl.shape[0] - spots), spots, side)
    pairs = []
    for source, along in ((xl, zl), (xa, 1 - zl)):
        for up in range(2):
            pairs.append(
                (
                    source.at[window, up * chans : (up + 1) * chans],
                    xbuf.at[:, at((2 * up + along) * chans, chans, chans)],
                )
            )
    run_copies(pairs, sems)
    wide = gp_ref.shape[1]
    outs = wide // 2
    spot = lax.broadcasted_iota(jnp.int32, (spots, wide), 0) - zh * side
    grad = gp_ref[at(zh * (gp_ref.shape[0] - spots), spots, side), :].astype(f32)
    grad = jnp.where((spot >= 0) & (spot < half), grad, 0.0)
    bias = jnp.sum(grad, axis=0, keepdims=True)
    spread_taps(side, grad.astype(bf16), taps_ref)
    blocks = 2 * keep_ref.shape[0]
    depth = xbuf.shape[1]
    size = depth // blocks
    for begin in range(0, depth, 256):
        values = xbuf[:, begin : begin + 256]
        for y in range(3):
            place = side * (2 - y)
            part = dot(values, taps_ref[place : place + spots, :], TN)
            for x in range(3):
                for u in range(2):
                    col = x * wide + u * outs
                    put_blocks(
                        idx_ref, keep_ref, give_ref, part[:, col : col + outs],
                        3 * y + x, begin // size, size, u * (9 * size + 16),
                    )
    for u in range(2):
        row = jnp.broadcast_to(bias[:, u * outs : (u + 1) * outs], (16, outs)).astype(bf16)
        for j in range(keep_ref.shape[0]):
            spot = slice(u * (9 * size + 16) + 9 * size, (u + 1) * (9 * size + 16))
            keep_ref[j, spot, :] = row
            give_ref[j, spot, :] = row
    if flat:
        first = 2 * (9 * size + 16)
        flat_pieces(1.0, idx_ref, full_ref, go_ref, bias_ref, keep_ref, give_ref, first)


def weight_grad(side, half, idx, grad, act, act_other, chips, flat=()):
    spots = half + side
    wide = grad.shape[1]
    outs = wide // 2
    depth = 2 * act.shape[1]
    rows = 2 * (9 * depth // (2 * chips) + 16)
    if flat:
        rows += flat_size(flat[0], flat[1], chips)
    return call(
        functools.partial(weight_body, side, half, bool(flat)),
        "weight_grad",
        [(SMEM, idx), (LOAD, grad)] + [(LOAD, a) for a in flat] + [(FAR, act), (FAR, act_other)],
        [(VMEM, struct((chips, rows, outs), bf16))] * 2,
        [
            pltpu.VMEM((spots, depth), bf16),
            pltpu.VMEM((spots + 2 * side, 3 * wide), bf16),
            pltpu.SemaphoreType.DMA((4,)),
        ],
        spare=10,
    )


def weight_one_body(side, arrive, idx_ref, mine_ref, theirs_ref, x_ref, *refs):
    keep_ref, give_ref, gp_ref, taps_ref = refs
    arrive()
    zh = idx_ref[2]
    half, outs = mine_ref.shape
    gp_ref[at(zh * half, half, side), :] = mine_ref[...]
    gp_ref[at((1 - zh) * half, half, side), :] = theirs_ref[...]
    grad = gp_ref[...]
    bias = jnp.sum(grad.astype(f32), axis=0, keepdims=True)
    spread_taps(side, grad, taps_ref)
    blocks = 2 * keep_ref.shape[0]
    spots, depth = x_ref.shape
    size = depth // blocks
    right = tap_block(side, taps_ref, 0, spots)
    for begin in range(0, depth, 256):
        part = dot(x_ref[:, begin : begin + 256], right, TN)
        for tap in range(9):
            put_blocks(
                idx_ref, keep_ref, give_ref, part[:, tap * outs : (tap + 1) * outs],
                tap, begin // size, size,
            )
    row = jnp.broadcast_to(bias, (16, outs)).astype(bf16)
    first = 9 * size + 16
    for j in range(keep_ref.shape[0]):
        keep_ref[j, 9 * size : first, :] = row
        give_ref[j, 9 * size : first, :] = row


def weight_one_grad(side, idx, mine, theirs, act_zero, chips):
    spots, depth = act_zero.shape
    outs = mine.shape[1]
    rows = 9 * depth // (2 * chips) + 16
    return call(
        functools.partial(weight_one_body, side),
        "weight_one_grad",
        [(SMEM, idx), (LOAD, mine), (LOAD, theirs), (LOAD, act_zero)],
        [(VMEM, struct((chips, rows, outs), bf16))] * 2,
        [
            pltpu.VMEM((spots, outs), bf16),
            pltpu.VMEM((spots + 2 * side, 3 * outs), bf16),
        ],
        spare=14,
    )


def fold_body(pairs, arrive, idx_ref, *refs):
    arrive()
    ins, (keep_ref, give_ref) = refs[: 2 * pairs], refs[2 * pairs :]
    half = keep_ref.shape[0]
    for i in range(2 * half):
        target = keep_ref if i < half else give_ref
        begin = 0
        for keep, recv in zip(ins[0::2], ins[1::2]):
            rows = keep.shape[1]
            total = keep[i].astype(f32) + recv[i].astype(f32)
            target[i % half, begin : begin + rows, :] = total.astype(bf16)
            begin += rows


def fold(idx, *arrays):
    blocks, _, wide = arrays[0].shape
    rows = sum(a.shape[1] for a in arrays[0::2])
    return call(
        functools.partial(fold_body, len(arrays) // 2),
        "fold",
        [(SMEM, idx)] + [(VMEM, a) for a in arrays],
        [(VMEM, struct((blocks // 2, rows, wide), bf16))] * 2,
    )


def last_body(slotted, rest, arrive, idx_ref, keep_in, recv_in, *targets):
    arrive()
    zh = idx_ref[2]

    def put(target, place, begin, rows):
        spot = at(begin, rows, 16)
        total = keep_in[0, spot, :].astype(f32) + recv_in[0, spot, :].astype(f32)
        target[place : place + rows, :] = total.astype(bf16)

    place = 0
    for begin, rows in slotted:
        put(targets[0], place, begin + zh * rows, rows)
        put(targets[1], place, begin + (1 - zh) * rows, rows)
        place += rows
    begin, rows = rest
    put(targets[-1], 0, begin, rows)


def last_fold(idx, keep, recv, slotted=(), rest=None):
    wide = keep.shape[2]
    rest = rest or (0, keep.shape[1])
    rows = sum(size for _, size in slotted)
    sizes = ([rows, rows] if slotted else []) + [rest[1]]
    return call(
        functools.partial(last_body, slotted, rest),
        "last_fold",
        [(SMEM, idx), (VMEM, keep), (VMEM, recv)],
        [(VMEM, struct((size, wide), bf16)) for size in sizes],
    )


def final_body(parts, arrive, idx_ref, own_ref, sib_ref, *refs):
    arrive()
    outs, stages, sems = refs[: 2 * len(parts)], refs[2 * len(parts) : -1], refs[-1]
    chip, core = idx_ref[0], idx_ref[1]
    chips, _, wide = own_ref.shape
    first = 0
    copies = []

    def store(source, target):
        copies.append(pltpu.make_async_copy(source, target, sems.at[len(copies)]))
        copies[-1].start()

    for n, part in enumerate(parts):
        grad_ref, bias_ref, stage = outs[2 * n], outs[2 * n + 1], stages[n]
        size = part[0] // (2 * chips)
        columns = 1 if len(part) == 1 else part[1] // wide
        end = first + size * (9 if len(part) == 1 else columns)
        for c in range(columns):
            row = own_ref[0, end + c : end + c + 1, :].astype(f32)
            bias_ref[:, c * wide : (c + 1) * wide] = row
        for n_row, begin in enumerate(range(first, end, size)):
            for j in range(chips):
                for source, owner in ((own_ref, core), (sib_ref, 1 - core)):
                    home = chip ^ mask_of(j, owner, chips)
                    spot = at((2 * home + owner) * size, size, size)
                    piece = source[j, begin : begin + size, :].astype(f32)
                    if len(part) == 1:
                        stage[n_row, spot, :] = piece
                    else:
                        stage[spot, n_row * wide : (n_row + 1) * wide] = piece
            if len(part) == 1:
                store(stage.at[n_row], grad_ref.at[n_row])
        if len(part) > 1:
            store(stage, grad_ref)
        first = end + 16
    for copy in copies:
        copy.wait()


def final_grads(idx, own, sib, parts):
    wide = own.shape[2]
    results, stages = [], []
    for part in parts:
        shape = (9, part[0], wide) if len(part) == 1 else part
        results += [(FAR, struct(shape, f32)), (VMEM, struct((1, shape[-1]), f32))]
        stages.append(pltpu.VMEM(shape, f32))
    copies = sum(9 if len(part) == 1 else 1 for part in parts)
    return call(
        functools.partial(final_body, parts),
        "final_grads",
        [(SMEM, idx), (VMEM, own), (VMEM, sib)],
        results,
        stages + [pltpu.SemaphoreType.DMA((copies,))],
    )


def flat_pieces(gain, idx_ref, x_ref, go_ref, bias_ref, keep_ref, give_ref, first):
    chip, core = idx_ref[0], idx_ref[1]
    chips, _, wide = keep_ref.shape
    columns = go_ref.shape[1] // wide
    size = x_ref.shape[1] // (2 * chips)
    bias = jnp.concatenate(
        [bias_ref[:, c * wide : (c + 1) * wide] for c in range(columns)]
        + [jnp.zeros((16 - columns, wide), f32)],
        axis=0,
    ).astype(bf16)
    for j in range(chips):
        keep_ref[j, first + columns * size :, :] = bias
        give_ref[j, first + columns * size :, :] = bias
    for begin in range(0, x_ref.shape[1], 256):
        part = gain * dot(x_ref[:, begin : begin + 256], go_ref[...], TN)
        for b in range(0, 256 // size, 2):
            mask = chip ^ ((begin // size + b) // 2)
            slot = slot_of(mask, core, chips)
            give_slot = slot_of(mask, 1 - core, chips)
            for c in range(columns):
                even = part[b * size : (b + 1) * size, c * wide : (c + 1) * wide]
                odd = part[(b + 1) * size : (b + 2) * size, c * wide : (c + 1) * wide]
                spot = slice(first + c * size, first + (c + 1) * size)
                keep_ref[slot, spot, :] = jnp.where(core == 0, even, odd).astype(bf16)
                give_ref[give_slot, spot, :] = jnp.where(core == 0, odd, even).astype(bf16)


def flat_size(x, go, chips):
    return (go.shape[1] // 128) * (x.shape[1] // (2 * chips)) + 16


def outer_body(gain, arrive, idx_ref, x_ref, go_ref, bias_ref, keep_ref, give_ref):
    arrive()
    flat_pieces(gain, idx_ref, x_ref, go_ref, bias_ref, keep_ref, give_ref, 0)


def outer(idx, x, go, gain, bias, chips):
    return call(
        functools.partial(outer_body, gain),
        "outer",
        [(SMEM, idx), (LOAD, x), (LOAD, go), (LOAD, bias)],
        [(VMEM, struct((chips, flat_size(x, go, chips), 128), bf16))] * 2,
        spare=8,
    )


def start_body(arrive, idx_ref, valid_ref, cot_ref, outk_ref, go_ref, bias_ref, own_ref, give_ref):
    arrive()
    zl = idx_ref[3]
    masked = cot_ref[...].astype(f32) * valid_ref[0]
    go_ref[...] = masked.astype(bf16)
    bias_ref[...] = jnp.sum(masked, axis=0, keepdims=True)
    chans = outk_ref.shape[0] // 4
    block = cot_ref.shape[0] // 4
    for target, along in ((give_ref, 1 - zl), (own_ref, zl)):
        weights = jnp.concatenate(
            [outk_ref[at((2 * up + along) * chans, chans, chans), :] for up in range(2)], axis=0
        )
        for begin in range(0, cot_ref.shape[0], block):
            part = post_gain * dot(go_ref[begin : begin + block, :], weights, NT)
            target[begin : begin + block, :] = part.astype(target.dtype)


def start_back(idx, valid, cot, outk):
    spots, outs = cot.shape
    half = outk.shape[0] // 2
    return call(
        start_body,
        "start_back",
        [(SMEM, idx), (SMEM, valid), (LOAD, cot), (LOAD, outk)],
        [
            (VMEM, struct(cot.shape, bf16)),
            (VMEM, struct((1, outs), f32)),
            (VMEM, struct((spots, half), f32)),
            (VMEM, struct((spots, half), bf16)),
        ],
    )


def rows_body(side, arrive, idx_ref, own_ref, recv_ref, keep_ref, give_ref):
    arrive()
    zh = idx_ref[2]
    spots = keep_ref.shape[0]
    apart = own_ref.shape[0] - spots
    for target, begin in ((give_ref, (1 - zh) * apart), (keep_ref, zh * apart)):
        spot = at(begin, spots, side)
        total = own_ref[spot, :] + recv_ref[spot, :].astype(f32)
        target[...] = total.astype(target.dtype)


def rows_sum(side, idx, own, recv, spots):
    shape = (spots, own.shape[1])
    return call(
        functools.partial(rows_body, side),
        "rows_sum",
        [(SMEM, idx), (LOAD, own), (LOAD, recv)],
        [(VMEM, struct(shape, f32)), (VMEM, struct(shape, bf16))],
    )


def slots_body(arrive, idx_ref, own_ref, recv_ref, keep_ref, give_ref):
    arrive()
    zh = idx_ref[2]
    for target, slot in ((give_ref, 1 - zh), (keep_ref, zh)):
        total = own_ref[slot] + recv_ref[slot].astype(f32)
        target[...] = total.astype(bf16)


def slots_sum(idx, own, recv):
    shape = struct(own.shape[1:], bf16)
    return call(
        slots_body,
        "slots_sum",
        [(SMEM, idx), (VMEM, own), (VMEM, recv)],
        [(VMEM, shape), (VMEM, shape)],
    )


def input_body(arrive, idx_ref, keep_ref, recv_ref, out_ref):
    arrive()
    zh = idx_ref[2]
    half = keep_ref.shape[0]
    out_ref[at(zh * half, half, half), :] = keep_ref[...]
    out_ref[at((1 - zh) * half, half, half), :] = recv_ref[...]


def input_grad(idx, keep, recv):
    half, chans = keep.shape
    return call(
        input_body,
        "input_grad",
        [(SMEM, idx), (VMEM, keep), (VMEM, recv)],
        [(VMEM, struct((2 * half, chans), bf16))],
    )


def whole_body(side, arrive, idx_ref, xl, xa, xh, xd, rh, rl, x_ref, act_ref, sems):
    arrive()
    zh, zl = idx_ref[2], idx_ref[3]
    chans = xl.shape[1]
    spots = xa.shape[0]
    rest = xl.shape[0] - spots
    window, outside = at(zh * rest, spots, side), at((1 - zh) * spots, rest, side)

    def cols(up, along):
        return at((2 * up + along) * chans, chans, chans)

    run_copies(
        [
            (xl, x_ref.at[:, cols(zh, zl)]),
            (xa, x_ref.at[window, cols(zh, 1 - zl)]),
            (xh, x_ref.at[window, cols(1 - zh, zl)]),
            (xd, x_ref.at[window, cols(1 - zh, 1 - zl)]),
            (rl.at[0], x_ref.at[outside, cols(zh, 1 - zl)]),
            (rh, x_ref.at[outside, cols(1 - zh, zl)]),
            (rl.at[1], x_ref.at[outside, cols(1 - zh, 1 - zl)]),
        ],
        sems,
    )
    block = x_ref.shape[0] // 8
    for begin in range(0, x_ref.shape[0], block):
        rows = slice(begin, begin + block)
        act_ref[rows, :] = gelu(x_ref[rows, :].astype(f32)).astype(bf16)


def whole_input(side, idx, *parts):
    spots, chans = parts[0].shape
    return call(
        functools.partial(whole_body, side),
        "whole_input",
        [(SMEM, idx)] + [(FAR, p) for p in parts],
        [(VMEM, struct((spots, 4 * chans), bf16))] * 2,
        [pltpu.SemaphoreType.DMA((7,))],
    )


def join_body(arrive, idx_ref, own, recv, far_own, far_recv, out, sems):
    arrive()
    zh, zl = idx_ref[2], idx_ref[3]
    half = own.shape[0]
    chans = own.shape[1] // 2
    pairs = []
    for source, up, along in ((own, zh, zl), (recv, zh, 1 - zl), (far_own, 1 - zh, zl), (far_recv, 1 - zh, 1 - zl)):
        for slot in range(2):
            spot = at((2 * slot + along) * chans, chans, chans)
            target = out.at[at(up * half, half, half), spot]
            pairs.append((source.at[:, slot * chans : (slot + 1) * chans], target))
    run_copies(pairs, sems)


def join(idx, *parts):
    half, wide = parts[0].shape
    return call(
        join_body,
        "join",
        [(SMEM, idx)] + [(FAR, p) for p in parts],
        [(VMEM, struct((2 * half, 2 * wide), bf16))],
        [pltpu.SemaphoreType.DMA((8,))],
    )


def finish_body(arrive, idx_ref, valid_ref, x_ref, act_ref, idk_ref, outk_ref, ib_ref, out_ref):
    arrive()
    block = x_ref.shape[0] // 4
    for begin in range(0, x_ref.shape[0], block):
        rows = slice(begin, begin + block)
        identity = dot(x_ref[rows, :], idk_ref[...]) + ib_ref[...]
        branch = dot(act_ref[rows, :], outk_ref[...])
        out_ref[rows, :] = ((identity + post_gain * branch) * valid_ref[0]).astype(bf16)


def finish(idx, valid, x, act, idk, outk, ib):
    outs = idk.shape[1]
    return call(
        finish_body,
        "finish",
        [(SMEM, idx), (SMEM, valid), (LOAD, x), (LOAD, act), (LOAD, idk), (LOAD, outk)]
        + [(VMEM, ib.reshape(1, outs))],
        [(VMEM, struct((x.shape[0], outs), bf16))],
        spare=8,
    )


def flip(value, axis):
    return lax.ppermute(value, axis, [(0, 1), (1, 0)])


def cross(value, step, chips):
    pairs = []
    for chip in range(chips):
        for core in range(2):
            other = chip ^ step_bits(core, chips)[step]
            pairs.append((2 * chip + core, 2 * other + core))
    return lax.ppermute(value, DP, pairs)


def hops(value, chips):
    blocks = [value]
    for i in range(1, chips):
        pairs = []
        for chip in range(chips):
            for core in range(2):
                bits = step_bits(core, chips)
                mask = sum(bit for n, bit in enumerate(bits) if i >> (len(bits) - 1 - n) & 1)
                pairs.append((2 * (chip ^ mask) + core, 2 * chip + core))
        blocks.append(lax.ppermute(value, DP, pairs))
    return blocks


def swap(pieces, axis):
    return lax.all_to_all(pieces, axis, split_axis=0, concat_axis=0, tiled=True)


def after(value, other):
    return lax.optimization_barrier((value, other))[0]


def rows_of(value, start, size):
    return lax.dynamic_slice_in_dim(value, start, size, 0)


def local(
    pixels,
    counts,
    kernel_one,
    bias_one,
    kernel_two,
    bias_two,
    kernel_three,
    bias_three,
    out_kernel,
    identity_kernel,
    identity_bias,
    cotangent,
):
    images, rows, width, chans = pixels.shape
    side = width // 2
    spots = side * side
    half = spots // 2
    window = half + halo * side
    outs = cotangent.shape[3]
    chips = lax.axis_size("chip")
    chip, core, zh, zl = [lax.axis_index(a) for a in ("chip", "core", "zh", "zl")]
    idx = jnp.stack([chip, core, zh, zl]).astype(jnp.int32)
    taps = lambda kernel: kernel.reshape((9,) + kernel.shape[2:])
    one, two, three = taps(kernel_one), taps(kernel_two), taps(kernel_three)

    own_count = lax.dynamic_index_in_dim(counts, 2 * chip + core, 0, keepdims=True)
    valid = (own_count > 0).astype(f32)

    place = 2 * chip + core

    def units_of(kernel, size):
        if kernel.ndim == 3:
            block = kernel.shape[1] // (2 * chips)
            return lax.dynamic_slice_in_dim(kernel, place * block, block, 1)
        block = kernel.shape[0] // (2 * chips)
        block = lax.dynamic_slice_in_dim(kernel, place * block, block, 0)
        block = block.reshape(-1, size, block.shape[1] // 128, 128)
        return block.transpose(2, 0, 1, 3).reshape(-1, size, 128)

    steps = chips.bit_length() - 1

    def start_spread(piece, *others):
        return jnp.concatenate(after((piece[None], cross(piece[None], steps - 1, chips)), others))

    def end_spread(own, *others):
        for step in reversed(range(steps - 1)):
            own = jnp.concatenate(after((own, cross(own, step, chips)), others))
        return own, flip(own, "core")

    last = [idx]

    def turn(*others):
        return after(idx, (last[0],) + others)

    def ran(results):
        last[0] = results[-1] if isinstance(results, (list, tuple)) else results
        return results

    size = two.shape[1] // (2 * chips)
    deep = two.shape[1]
    cot = cotangent.reshape(spots, outs)
    one_piece = flip(units_of(one, size), "zh")
    pooled = ran(pool(pixels))
    go, identity_bias_grad, ga_own, ga_give = ran(start_back(turn(), valid, cot, out_kernel))
    bias_other = flip(after(jnp.stack([bias_one, bias_two, bias_three]), go), "zh")
    two_piece = units_of(after(two, pooled), size)
    last_piece = jnp.concatenate([units_of(after(k, pooled), size) for k in (three, identity_kernel)])
    cot_rows = rows_of(after(cot, pooled), (1 - zh) * half, half)
    xl = swap(after(pooled, (one_piece, two_piece, last_piece, cot_rows, ga_give)), DP)
    xl = xl.reshape(spots, chans)
    two_piece = flip(after(two_piece, one_piece), "zh")

    apart = spots - window
    xa = flip(rows_of(xl, zh * apart, window), "zl")
    xh = flip(rows_of(xl, (1 - zh) * apart, window), "zh")
    rest = spots - window
    rest_own = rows_of(xl, (1 - zh) * window, rest)
    rest_high = rows_of(xl, zh * window, rest)
    two_near = start_spread(after(two_piece, xl))
    one_near = start_spread(after(one_piece, xl), xh, xa, two_near, bias_other)
    xd = flip(xh, "zl")
    last_piece = flip(after(last_piece, xh), "zh")
    two_other = end_spread(two_near, xd)
    one_other = end_spread(one_near, xd, two_other[0], last_piece)
    ga_recv = flip(after(ga_give, xd), "zl")
    rest_high = flip(after(rest_high, xd), "zh")

    pre_one, act_one = ran(
        conv(
            side, turn(), (xl, xa, xh, xd), one, one_other, 0, bias_one, bias_other[0], True
        )
    )
    act_one_other = flip(act_one, "zl")
    ga_own, ga_give = ran(rows_sum(side, turn(), ga_own, ga_recv, half + (halo - 3) * side))
    pre_two, act_two = ran(
        conv(side, turn(), (act_one, act_one_other), two, two_other, 0, bias_two, bias_other[1])
    )
    act_two_other = flip(act_two, "zl")
    ga_recv = flip(after(ga_give, act_two), "zh")
    last_other = jnp.stack(after(hops(after(last_piece, act_one), chips), act_two))
    last_other = last_other, flip(last_other, "core")
    pre_three, act_three = ran(
        conv(side, turn(), (act_two, act_two_other), three, last_other, 0, bias_three, bias_other[2])
    )
    rest_low = flip(jnp.stack(after((rest_own, rest_high), act_three)), "zl")
    cot_far = flip(after(cot_rows, act_three), "zh")
    own_rows = rows_of(act_three, zh * (halo - 3) * side, half)

    gp_three, ga_own, ga_give = ran(
        back(side, turn(), (ga_own, ga_recv, pre_three), three, last_other, 0)
    )
    ga_recv = flip(ga_give, "zl")
    full_x, act_zero = ran(whole_input(side, turn(), xl, xa, xh, xd, rest_high, rest_low))
    keep_three, give_three = ran(
        weight_grad(
            side, half, turn(), gp_three, act_two, act_two_other, chips, (full_x, go, identity_bias_grad)
        )
    )
    gp_two, ga_own, ga_give = ran(
        back(side, turn(), (ga_own, ga_recv, pre_two), two, two_other, 0)
    )
    ga_recv = flip(ga_give, "zl")
    keep_two, give_two = ran(weight_grad(side, half, turn(cot_far), gp_two, act_one, act_one_other, chips))

    gp_mine, gp_theirs, gp_one = ran(slope_back(side, turn(), ga_own, ga_recv, pre_one, half))
    gp_theirs = flip(gp_theirs, "zh")
    recv_three = flip(after(give_three, gp_one), "core")
    recv_two = flip(after(give_two, gp_one), "core")
    gx_own, gx_give = ran(
        back(
            side, turn(), (gp_one,), one, one_other, 0,
            (valid, full_x, go, cot_far, identity_kernel, last_other, half),
        )
    )

    def folds(keep, recv, first, *others):
        for step in range(first, steps):
            keep, give = ran(fold(turn(*others), keep, recv))
            recv = cross(give, step, chips)
        return keep, recv

    keep_deep, give_deep = ran(fold(turn(gp_theirs), keep_three, recv_three, keep_two, recv_two))
    recv_deep = cross(give_deep, 0, chips)
    gx_recv = flip(after(gx_give, keep_deep), "zl")
    own_rows = after(own_rows, keep_deep)
    near_rows = flip(own_rows, "zl")
    far_rows = flip(own_rows, "zh")
    keep_one, give_one = ran(weight_one_grad(side, turn(), gp_mine, gp_theirs, act_zero, chips))
    recv_one = flip(give_one, "core")
    keep_deep, recv_deep = folds(keep_deep, recv_deep, 1, far_rows)
    gx_keep, gx_give = ran(slots_sum(turn(), gx_own, gx_recv))
    gx_recv = flip(gx_give, "zh")
    keep_one, give_one = ran(fold(turn(), keep_one, recv_one))
    recv_one = cross(give_one, 0, chips)
    slot = 9 * size + 16
    flat = keep_three.shape[1] - 2 * slot
    keep_deep, give_deep, id_rows = ran(
        last_fold(
            turn(), keep_deep, recv_deep, ((0, slot), (2 * slot + flat, slot)), (2 * slot, flat)
        )
    )
    recv_deep = flip(give_deep, "zh")
    far_near_rows = flip(after(far_rows, keep_deep), "zl")
    keep_one, recv_one = folds(keep_one, recv_one, 1)
    full_three = ran(join(turn(), own_rows, near_rows, far_rows, far_near_rows))
    keep_out, give_out = ran(outer(turn(), full_three, go, post_gain, identity_bias_grad, chips))
    recv_out = flip(give_out, "core")
    (total_one,) = ran([last_fold(turn(), keep_one, recv_one)])
    keep_out, give_out = ran(fold(turn(), keep_out, recv_out))
    recv_out = cross(give_out, 0, chips)
    deep_rows = (after(keep_deep, keep_out).astype(f32) + recv_deep.astype(f32)).astype(bf16)
    deep_rows = jnp.concatenate([deep_rows, id_rows])
    near_deep = start_spread(deep_rows)
    block_out = ran(
        finish(turn(deep_rows), valid, full_x, full_three, identity_kernel, out_kernel, identity_bias)
    )
    keep_out, recv_out = folds(keep_out, recv_out, 1, near_deep)
    gx = ran(input_grad(turn(), gx_keep, gx_recv))
    gx = swap(gx.reshape(images, rows * width // 4, chans), DP)
    all_deep = end_spread(near_deep)
    (total_out,) = ran([last_fold(turn(all_deep[0]), keep_out, recv_out)])
    near_one = start_spread(jnp.concatenate([total_one, total_out]))
    pixels_grad = ran(widen(turn(near_one), gx, rows, width))
    (
        kernel_three_grad,
        bias_three_grad,
        kernel_two_grad,
        bias_two_grad,
        identity_kernel_grad,
        identity_bias_grad,
    ) = ran(final_grads(turn(), *all_deep, ((deep,), (deep,), identity_kernel.shape)))
    all_one = end_spread(near_one, bias_three_grad)
    kernel_one_grad, bias_one_grad, out_kernel_grad, _ = ran(
        final_grads(turn(), *all_one, ((one.shape[1],), out_kernel.shape))
    )

    return (
        block_out.reshape(cotangent.shape),
        pixels_grad,
        kernel_one_grad.reshape(kernel_one.shape),
        bias_one_grad[0],
        kernel_two_grad.reshape(kernel_two.shape),
        bias_two_grad[0],
        kernel_three_grad.reshape(kernel_three.shape),
        bias_three_grad[0],
        out_kernel_grad,
        identity_kernel_grad,
        identity_bias_grad[0],
    )


def solution(mesh):
    members = mesh.devices.size // mesh.shape["mp"]
    fine = Mesh(
        mesh.devices.reshape(members // 2, 2, 2, mesh.shape["mp"] // 2),
        ("chip", "core", "zh", "zl"),
    )
    return jax.shard_map(
        local,
        mesh=fine,
        in_specs=(
            P(None, DP, None, MP),
            P(),
            P(None, None, None, MP),
            P(MP),
            P(None, None, None, MP),
            P(MP),
            P(None, None, None, MP),
            P(MP),
            P(None, MP),
            P(None, MP),
            P(MP),
            P(DP, None, None, MP),
        ),
        out_specs=(
            P(DP, None, None, MP),
            P(None, DP, None, MP),
            P(None, None, None, MP),
            P(MP),
            P(None, None, None, MP),
            P(MP),
            P(None, None, None, MP),
            P(MP),
            P(None, MP),
            P(None, MP),
            P(MP),
        ),
        check_vma=False,
    )
```

```python
import functools
import math

import jax
import jax.numpy as jnp
from jax import lax
from jax.experimental import pallas as pl
from jax.experimental.pallas import tpu as pltpu
from jax.sharding import Mesh
from jax.sharding import PartitionSpec as P


post_gain = 0.015625
slope = 0.7978845608028654
cubic = 0.044715
halo = 6
bf16 = jnp.bfloat16
f32 = jnp.float32
NT = (((1,), (1,)), ((), ()))
TN = (((0,), (0,)), ((), ()))
NN = (((1,), (0,)), ((), ()))
DP = ("chip", "core")
MP = ("zh", "zl")


def dot(left, right, dims=NN):
    return lax.dot_general(left, right, dims, preferred_element_type=f32)


def gelu(value):
    inner = jnp.tanh(slope * (value + cubic * value * value * value))
    return 0.5 * value * (1.0 + inner)


def gelu_slope(value):
    square = value * value
    inner = jnp.tanh(slope * value * (1.0 + cubic * square))
    climb = slope * (1.0 + 3.0 * cubic * square)
    return 0.5 * (1.0 + inner) + 0.5 * value * (1.0 - inner * inner) * climb


def struct(shape, kind):
    return jax.ShapeDtypeStruct(shape, kind)


def lanes(blocks):
    return blocks[0] if len(blocks) == 1 else jnp.concatenate(blocks, axis=1)


def step_bits(core, chips):
    bits = [1 << n for n in range(chips.bit_length() - 1)]
    for n in range(0, len(bits) - 1, 2) if core else ():
        bits[n], bits[n + 1] = bits[n + 1], bits[n]
    return bits


def mask_of(i, core, chips):
    masks = []
    for which in range(2):
        bits = step_bits(which, chips)
        masks.append(sum(bit for n, bit in enumerate(bits) if i >> (len(bits) - 1 - n) & 1))
    return jnp.where(core == 0, masks[0], masks[1])


def slot_of(mask, core, chips):
    slots = []
    for which in range(2):
        bits = step_bits(which, chips)
        slot = 0
        for n, bit in enumerate(bits):
            slot = slot + ((mask >> (bit.bit_length() - 1)) & 1) * (1 << (len(bits) - 1 - n))
        slots.append(slot)
    return jnp.where(core == 0, slots[0], slots[1])


VMEM = pl.BlockSpec(memory_space=pltpu.VMEM)
SMEM = pl.BlockSpec(memory_space=pltpu.SMEM)
FAR = pl.BlockSpec(memory_space=pl.ANY)
LOAD = "load"


def size_of(array):
    return math.prod(array.shape) * jnp.dtype(array.dtype).itemsize


def call(body, name, ins, outs, scratch=(), spare=6, **more):
    loads = [i for i, (space, _) in enumerate(ins) if space is LOAD]
    spaces = [FAR if space is LOAD else space for space, _ in ins]
    arrays = [array for _, array in ins]
    out_specs = [space for space, _ in outs]
    out_shape = [shape for _, shape in outs]
    held = [arrays[i] for i in loads]
    buffers = [pltpu.VMEM(array.shape, array.dtype) for array in held]
    sems = [pltpu.SemaphoreType.DMA((len(held),))] if held else []
    vmem = sum(size_of(array) for array in held)
    vmem += sum(size_of(a) for space, a in list(ins) + list(outs) if space is VMEM)
    vmem += sum(size_of(b) for b in scratch if b.memory_space == pltpu.VMEM)
    moved = sum(size_of(a) for a in arrays + out_shape)

    def wrapped(*refs):
        inputs = list(refs[: len(ins)])
        outputs = refs[len(ins) : len(ins) + len(outs)]
        rest = refs[len(ins) + len(outs) :]
        kept, tail = rest[: len(held)], rest[len(held) :]
        copies = []
        if held:
            sem, tail = tail[0], tail[1:]
            copies = [
                pltpu.make_async_copy(inputs[i], kept[n], sem.at[n]) for n, i in enumerate(loads)
            ]
        for copy in copies:
            copy.start()
        for n, i in enumerate(loads):
            inputs[i] = kept[n]

        def arrive():
            for copy in copies:
                copy.wait()

        body(arrive, *inputs, *outputs, *tail)

    single = len(outs) == 1
    return pl.pallas_call(
        wrapped,
        in_specs=spaces,
        out_specs=out_specs[0] if single else out_specs,
        out_shape=out_shape[0] if single else out_shape,
        scratch_shapes=buffers + sems + list(scratch),
        compiler_params=pltpu.CompilerParams(vmem_limit_bytes=vmem + (spare << 20)),
        cost_estimate=pl.CostEstimate(flops=0, bytes_accessed=moved, transcendentals=0),
        name=name,
        **more,
    )(*arrays)


def run_copies(pairs, sems):
    for copy in start_copies(pairs, sems):
        copy.wait()


def slice_copies(group, idx_ref, own, blocks, sibling, wbuf):
    chip, core, zh = idx_ref[0], idx_ref[1], idx_ref[2]
    size = blocks.shape[-2]
    pairs = [(own, wbuf.at[zh])]
    for j in range(blocks.shape[0]):
        for source, owner in ((blocks, core), (sibling, 1 - core)):
            home = chip ^ mask_of(j, owner, blocks.shape[0])
            spot = at((2 * home + owner) * size, size, size)
            pairs.append((source.at[j, 9 * group : 9 * group + 9], wbuf.at[1 - zh, :, spot, :]))
    return pairs


def flat_copies(first, idx_ref, blocks, sibling, buffer):
    chip, core = idx_ref[0], idx_ref[1]
    columns, units = buffer.shape[:2]
    chips = blocks.shape[0]
    count = units // (2 * chips)
    pairs = []
    for j in range(chips):
        for source, owner in ((blocks, core), (sibling, 1 - core)):
            home = chip ^ mask_of(j, owner, chips)
            spot = pl.ds((2 * home + owner) * count, count)
            for c in range(columns):
                begin = first + c * count
                pairs.append((source.at[j, begin : begin + count], buffer.at[c, spot]))
    return pairs


def start_copies(pairs, sems):
    copies = [pltpu.make_async_copy(a, b, sems.at[i]) for i, (a, b) in enumerate(pairs)]
    for copy in copies:
        copy.start()
    return copies


def flat_rows(buffer, begin, count):
    columns, _, size, wide = buffer.shape
    return lanes([buffer[c, pl.ds(begin, count)].reshape(count * size, wide) for c in range(columns)])


def halves(spots, side):
    first = (spots // side + 1) // 2 * side
    return ((0, first), (first, spots - first))


def columns_of(size, wide, side):
    return lax.rem(lax.broadcasted_iota(jnp.int32, (size, wide), 0), side)


def at(start, size, unit):
    return pl.ds(pl.multiple_of(start, unit), size)


def pool_body(arrive, x_ref, out_ref):
    arrive()
    rows, width, chans = x_ref.shape[1:]
    half = width // 2
    pixel = lax.broadcasted_iota(jnp.int32, (half, 2 * width), 1)
    place = lax.broadcasted_iota(jnp.int32, (half, 2 * width), 0)
    inside = (lax.rem(pixel, width) >= 2 * place) & (lax.rem(pixel, width) < 2 * place + 2)
    pick = jnp.where(inside, 0.25, 0.0).astype(bf16)
    for image in range(x_ref.shape[0]):
        for row in range(rows // 2):
            window = x_ref[image, 2 * row : 2 * row + 2].reshape(2 * width, chans)
            out_ref[image, row * half : (row + 1) * half, :] = dot(pick, window).astype(bf16)


def pool(pixels):
    images, rows, width, chans = pixels.shape
    shape = struct((images, rows * width // 4, chans), bf16)
    return call(pool_body, "pool", [(LOAD, pixels)], [(VMEM, shape)])


def widen_body(arrive, idx_ref, g_ref, out_ref):
    arrive()
    rows, width, chans = out_ref.shape[1:]
    half = width // 2
    pixel = lax.broadcasted_iota(jnp.int32, (width, half), 0)
    place = lax.broadcasted_iota(jnp.int32, (width, half), 1)
    inside = (pixel >= 2 * place) & (pixel < 2 * place + 2)
    pick = jnp.where(inside, 0.25, 0.0).astype(bf16)
    for image in range(g_ref.shape[0]):
        for row in range(rows // 2):
            wide = dot(pick, g_ref[image, row * half : (row + 1) * half, :]).astype(bf16)
            out_ref[image, 2 * row] = wide
            out_ref[image, 2 * row + 1] = wide


def widen(idx, grad, rows, width):
    images, spots, chans = grad.shape
    step = images // 4
    block = pl.BlockSpec((step, spots, chans), lambda i: (i, 0, 0))
    out = pl.BlockSpec((step, rows, width, chans), lambda i: (i, 0, 0, 0))
    return call(
        widen_body,
        "widen",
        [(SMEM, idx), (block, grad)],
        [(out, struct((images, rows, width, chans), bf16))],
        grid=(4,),
    )


def conv_body(side, first, group, arrive, idx_ref, *refs):
    zh, zl = idx_ref[2], idx_ref[3]
    if first:
        xl, xa, xh, xd, wl, wo, ws, bl, bo, pre_ref, act_ref, xbuf, wbuf, acc, sems = refs
        chans = xl.shape[1]
        spots = xbuf.shape[0]
        begin = zh * (xl.shape[0] - spots)
        pairs = []
        for source, up, along in ((xl, zh, zl), (xa, zh, 1 - zl), (xh, 1 - zh, zl), (xd, 1 - zh, 1 - zl)):
            if source is xl:
                source = xl.at[at(begin, spots, side), :]
            pairs.append((source, xbuf.at[:, at((2 * up + along) * chans, chans, chans)]))
    else:
        xl, xa, wl, wo, ws, bl, bo, pre_ref, act_ref, xbuf, wbuf, acc, sems = refs
        chans = xl.shape[1] // 2
        spots = xbuf.shape[0]
        pairs = []
        for source, along in ((xl, zl), (xa, 1 - zl)):
            for up in range(2):
                pairs.append(
                    (
                        source.at[:, up * chans : (up + 1) * chans],
                        xbuf.at[:, at((2 * up + along) * chans, chans, chans)],
                    )
                )
    run_copies(slice_copies(group, idx_ref, wl, wo, ws, wbuf) + pairs, sems)
    arrive()
    acc[...] = jnp.zeros_like(acc)
    outs = 2 * wl.shape[2]
    for x in range(3):
        weights = lanes([wbuf[u, 3 * y + x] for y in range(3) for u in range(2)])
        for begin, block in halves(spots, side):
            values = xbuf[begin : begin + block, :]
            if first:
                values = gelu(values.astype(f32)).astype(bf16)
            product = dot(values, weights)
            for y in range(3):
                place = begin + side * (2 - y)
                acc[x, place : place + block, :] += product[:, y * outs : (y + 1) * outs]
    own, other = bl[...], bo[...]
    bias = lanes([jnp.where(zh == 0, own, other), jnp.where(zh == 0, other, own)])
    for begin, block in halves(act_ref.shape[0], side):
        column = columns_of(block, outs, side)
        spot = at(begin + side + zh * side, block, side)
        left = pltpu.roll(acc[0, spot, :], 1, 0)
        right = pltpu.roll(acc[2, spot, :], block - 1, 0)
        pre = acc[1, spot, :] + bias
        pre = pre + jnp.where(column > 0, left, 0.0)
        pre = pre + jnp.where(column < side - 1, right, 0.0)
        pre_ref[begin : begin + block, :] = pre
        act_ref[begin : begin + block, :] = gelu(pre).astype(bf16)


def conv(side, idx, sources, own, other, group, bias, bias_other, first=False):
    taps, depth, outs = own.shape
    spots = sources[1].shape[0]
    rows = spots - side
    return call(
        functools.partial(conv_body, side, first, group),
        "conv",
        [(SMEM, idx)]
        + [(FAR, s) for s in sources]
        + [(FAR, own), (FAR, other[0]), (FAR, other[1])]
        + [(VMEM, bias.reshape(1, outs)), (VMEM, bias_other.reshape(1, outs))],
        [(VMEM, struct((rows, 2 * outs), f32)), (VMEM, struct((rows, 2 * outs), bf16))],
        [
            pltpu.VMEM((spots, depth), bf16),
            pltpu.VMEM((2, taps, depth, outs), bf16),
            pltpu.VMEM((3, spots + 2 * side, 2 * outs), f32),
            pltpu.SemaphoreType.DMA((2 * other[0].shape[0] + 5,)),
        ],
        spare=14 if first else 8,
    )


def spread_taps(side, grad, taps_ref):
    pixels, outs = grad.shape
    column = columns_of(pixels, outs, side)
    wide = grad.astype(f32)
    ahead = jnp.where(column < side - 1, pltpu.roll(wide, pixels - 1, 0), 0.0).astype(bf16)
    behind = jnp.where(column > 0, pltpu.roll(wide, 1, 0), 0.0).astype(bf16)
    edge = jnp.zeros((side, 3 * outs), bf16)
    taps_ref[:side, :] = edge
    taps_ref[side + pixels :, :] = edge
    taps_ref[side : side + pixels, :] = jnp.concatenate([ahead, grad, behind], axis=1)


def tap_block(side, taps_ref, begin, block):
    return lanes([taps_ref[at(begin + side * (2 - y), block, side), :] for y in range(3)])


def slope_body(side, arrive, idx_ref, keep_ref, recv_ref, pre_ref, mine_ref, theirs_ref, gp_ref):
    arrive()
    zh = idx_ref[2]
    half, outs = mine_ref.shape
    total = keep_ref[...] + recv_ref[...].astype(f32)
    spots = keep_ref.shape[0]
    pre = pre_ref[at(zh * (pre_ref.shape[0] - spots), spots, side), :]
    gp_ref[...] = (total * gelu_slope(pre)).astype(bf16)
    own = gp_ref[at(zh * (gp_ref.shape[0] - half), half, side), :]
    low, high = own[:, :outs], own[:, outs:]
    mine_ref[...] = jnp.where(zh == 0, low, high)
    theirs_ref[...] = jnp.where(zh == 0, high, low)


def slope_back(side, idx, keep, recv, pre, half):
    outs = pre.shape[1] // 2
    return call(
        functools.partial(slope_body, side),
        "slope_back",
        [(SMEM, idx), (VMEM, keep), (VMEM, recv), (LOAD, pre)],
        [
            (VMEM, struct((half, outs), bf16)),
            (VMEM, struct((half, outs), bf16)),
            (VMEM, struct(keep.shape, bf16)),
        ],
    )


def back_body(side, last, group, arrive, idx_ref, *refs):
    zh, zl = idx_ref[2], idx_ref[3]
    if last:
        valid_ref, grad_ref, x_ref, go_ref, far_ref, idk_ref, wl, wo, ws, po, ps = refs[:11]
        own_ref, give_ref, taps_ref, wbuf, idk_far, sems = refs[11:]
    else:
        keep_ref, recv_ref, pre_ref, wl, wo, ws, gp_ref, own_ref, give_ref, taps_ref, wbuf, sems = refs
    pairs = slice_copies(group, idx_ref, wl, wo, ws, wbuf)
    if last:
        pairs += flat_copies(9, idx_ref, po, ps, idk_far)
    copies = start_copies(pairs, sems)
    arrive()
    if last:
        grad = grad_ref[...]
    else:
        spots = gp_ref.shape[0]

        def window(ref):
            return ref[at(zh * (ref.shape[0] - spots), spots, side), :]

        total = window(keep_ref) + window(recv_ref).astype(f32)
        grad = (total * gelu_slope(window(pre_ref))).astype(bf16)
        gp_ref[...] = grad
    spread_taps(side, grad, taps_ref)
    depth, outs = wl.shape[1:]
    pixels = own_ref.shape[-2]
    start = zh * side
    for copy in copies:
        copy.wait()
    chans = depth // 4

    def rows(index):
        spot = at(index * chans, chans, chans)
        return lanes([wbuf[u, t, spot, :] for t in range(9) for u in range(2)])

    for target, along in ((give_ref, 1 - zl), (own_ref, zl)):
        if last:
            units = chans // idk_far.shape[2]
            for up in range(2):
                index = 2 * up + along
                weights = rows(index)
                near = idk_ref[at(index * chans, chans, chans), :]
                far = flat_rows(idk_far, index * units, units)
                apart = zh * (far_ref.shape[0] - pixels)
                for begin, block in halves(pixels, side):
                    here = at(zh * pixels + begin, block, side)
                    part = dot(tap_block(side, taps_ref, start + begin, block), weights, NT)
                    x = x_ref[here, at(index * chans, chans, chans)]
                    part = part * gelu_slope(x.astype(f32))
                    part = part + dot(go_ref[here, :], near, NT)
                    part = part + valid_ref[0] * dot(far_ref[at(apart + begin, block, side), :], far, NT)
                    target[up, begin : begin + block, :] = part.astype(target.dtype)
        else:
            weights = jnp.concatenate([rows(along), rows(2 + along)], axis=0)
            for begin, block in halves(pixels, side):
                part = dot(tap_block(side, taps_ref, start + begin, block), weights, NT)
                target[begin : begin + block, :] = part.astype(target.dtype)


def back(side, idx, sources, own, other, group, last=None):
    taps, depth, outs = own.shape
    spots = min(sources[0].shape[0], sources[-1].shape[0])
    copies = 2 * other[0].shape[0] + 1
    extra = []
    scratch = []
    if last:
        valid, full_x, go, cot_far, idk, pieces, half = last
        chans = depth // 4
        shape = (2, half, chans)
        results = []
        extra = [(FAR, pieces[0]), (FAR, pieces[1])]
        sources = list(sources) + [full_x, go, cot_far, idk]
        columns, size = idk.shape[1] // 128, pieces[0].shape[2]
        scratch = [pltpu.VMEM((columns, depth // size, size, 128), bf16)]
        copies += 2 * other[0].shape[0] * columns
    else:
        shape = (spots - side, depth // 2)
        results = [(VMEM, struct((spots, 2 * outs), bf16))]
    results += [(VMEM, struct(shape, f32)), (VMEM, struct(shape, bf16))]
    return call(
        functools.partial(back_body, side, bool(last), group),
        "back",
        [(SMEM, idx)]
        + ([(SMEM, last[0])] if last else [])
        + [(LOAD, source) for source in sources]
        + [(FAR, own), (FAR, other[0]), (FAR, other[1])]
        + extra,
        results,
        [pltpu.VMEM((spots + 2 * side, 6 * outs), bf16), pltpu.VMEM((2, taps, depth, outs), bf16)]
        + scratch
        + [pltpu.SemaphoreType.DMA((copies,))],
        spare=14 if last else 10,
    )


def put_blocks(idx_ref, keep_ref, give_ref, part, tap, first_block, size, begin=0):
    chip, core = idx_ref[0], idx_ref[1]
    for b in range(0, part.shape[0] // size, 2):
        even = part[b * size : (b + 1) * size, :]
        odd = part[(b + 1) * size : (b + 2) * size, :]
        mask = chip ^ ((first_block + b) // 2)
        slot = slot_of(mask, core, keep_ref.shape[0])
        give_slot = slot_of(mask, 1 - core, keep_ref.shape[0])
        rows = slice(begin + tap * size, begin + (tap + 1) * size)
        keep_ref[slot, rows, :] = jnp.where(core == 0, even, odd).astype(bf16)
        give_ref[give_slot, rows, :] = jnp.where(core == 0, odd, even).astype(bf16)


def weight_body(side, half, flat, arrive, idx_ref, gp_ref, *refs):
    if flat:
        full_ref, go_ref, bias_ref = refs[:3]
        refs = refs[3:]
    xl, xa, keep_ref, give_ref, xbuf, taps_ref, sems = refs
    arrive()
    zh, zl = idx_ref[2], idx_ref[3]
    chans = xl.shape[1] // 2
    spots = xbuf.shape[0]
    window = at(zh * (xl.shape[0] - spots), spots, side)
    pairs = []
    for source, along in ((xl, zl), (xa, 1 - zl)):
        for up in range(2):
            pairs.append(
                (
                    source.at[window, up * chans : (up + 1) * chans],
                    xbuf.at[:, at((2 * up + along) * chans, chans, chans)],
                )
            )
    run_copies(pairs, sems)
    wide = gp_ref.shape[1]
    outs = wide // 2
    spot = lax.broadcasted_iota(jnp.int32, (spots, wide), 0) - zh * side
    grad = gp_ref[at(zh * (gp_ref.shape[0] - spots), spots, side), :].astype(f32)
    grad = jnp.where((spot >= 0) & (spot < half), grad, 0.0)
    bias = jnp.sum(grad, axis=0, keepdims=True)
    spread_taps(side, grad.astype(bf16), taps_ref)
    blocks = 2 * keep_ref.shape[0]
    depth = xbuf.shape[1]
    size = depth // blocks
    for begin in range(0, depth, 256):
        values = xbuf[:, begin : begin + 256]
        for y in range(3):
            place = side * (2 - y)
            part = dot(values, taps_ref[place : place + spots, :], TN)
            for x in range(3):
                for u in range(2):
                    col = x * wide + u * outs
                    put_blocks(
                        idx_ref, keep_ref, give_ref, part[:, col : col + outs],
                        3 * y + x, begin // size, size, u * (9 * size + 16),
                    )
    for u in range(2):
        row = jnp.broadcast_to(bias[:, u * outs : (u + 1) * outs], (16, outs)).astype(bf16)
        for j in range(keep_ref.shape[0]):
            spot = slice(u * (9 * size + 16) + 9 * size, (u + 1) * (9 * size + 16))
            keep_ref[j, spot, :] = row
            give_ref[j, spot, :] = row
    if flat:
        first = 2 * (9 * size + 16)
        flat_pieces(1.0, idx_ref, full_ref, go_ref, bias_ref, keep_ref, give_ref, first)


def weight_grad(side, half, idx, grad, act, act_other, chips, flat=()):
    spots = half + side
    wide = grad.shape[1]
    outs = wide // 2
    depth = 2 * act.shape[1]
    rows = 2 * (9 * depth // (2 * chips) + 16)
    if flat:
        rows += flat_size(flat[0], flat[1], chips)
    return call(
        functools.partial(weight_body, side, half, bool(flat)),
        "weight_grad",
        [(SMEM, idx), (LOAD, grad)] + [(LOAD, a) for a in flat] + [(FAR, act), (FAR, act_other)],
        [(VMEM, struct((chips, rows, outs), bf16))] * 2,
        [
            pltpu.VMEM((spots, depth), bf16),
            pltpu.VMEM((spots + 2 * side, 3 * wide), bf16),
            pltpu.SemaphoreType.DMA((4,)),
        ],
        spare=10,
    )


def weight_one_body(side, arrive, idx_ref, mine_ref, theirs_ref, x_ref, *refs):
    keep_ref, give_ref, gp_ref, taps_ref = refs
    arrive()
    zh = idx_ref[2]
    half, outs = mine_ref.shape
    gp_ref[at(zh * half, half, side), :] = mine_ref[...]
    gp_ref[at((1 - zh) * half, half, side), :] = theirs_ref[...]
    grad = gp_ref[...]
    bias = jnp.sum(grad.astype(f32), axis=0, keepdims=True)
    spread_taps(side, grad, taps_ref)
    blocks = 2 * keep_ref.shape[0]
    spots, depth = x_ref.shape
    size = depth // blocks
    right = tap_block(side, taps_ref, 0, spots)
    for begin in range(0, depth, 256):
        part = dot(x_ref[:, begin : begin + 256], right, TN)
        for tap in range(9):
            put_blocks(
                idx_ref, keep_ref, give_ref, part[:, tap * outs : (tap + 1) * outs],
                tap, begin // size, size,
            )
    row = jnp.broadcast_to(bias, (16, outs)).astype(bf16)
    first = 9 * size + 16
    for j in range(keep_ref.shape[0]):
        keep_ref[j, 9 * size : first, :] = row
        give_ref[j, 9 * size : first, :] = row


def weight_one_grad(side, idx, mine, theirs, act_zero, chips):
    spots, depth = act_zero.shape
    outs = mine.shape[1]
    rows = 9 * depth // (2 * chips) + 16
    return call(
        functools.partial(weight_one_body, side),
        "weight_one_grad",
        [(SMEM, idx), (LOAD, mine), (LOAD, theirs), (LOAD, act_zero)],
        [(VMEM, struct((chips, rows, outs), bf16))] * 2,
        [
            pltpu.VMEM((spots, outs), bf16),
            pltpu.VMEM((spots + 2 * side, 3 * outs), bf16),
        ],
        spare=14,
    )


def fold_body(pairs, arrive, idx_ref, *refs):
    arrive()
    ins, (keep_ref, give_ref) = refs[: 2 * pairs], refs[2 * pairs :]
    half = keep_ref.shape[0]
    for i in range(2 * half):
        target = keep_ref if i < half else give_ref
        begin = 0
        for keep, recv in zip(ins[0::2], ins[1::2]):
            rows = keep.shape[1]
            total = keep[i].astype(f32) + recv[i].astype(f32)
            target[i % half, begin : begin + rows, :] = total.astype(bf16)
            begin += rows


def fold(idx, *arrays):
    blocks, _, wide = arrays[0].shape
    rows = sum(a.shape[1] for a in arrays[0::2])
    return call(
        functools.partial(fold_body, len(arrays) // 2),
        "fold",
        [(SMEM, idx)] + [(VMEM, a) for a in arrays],
        [(VMEM, struct((blocks // 2, rows, wide), bf16))] * 2,
    )


def last_body(slotted, rest, arrive, idx_ref, keep_in, recv_in, *targets):
    arrive()
    zh = idx_ref[2]

    def put(target, place, begin, rows):
        spot = at(begin, rows, 16)
        total = keep_in[0, spot, :].astype(f32) + recv_in[0, spot, :].astype(f32)
        target[place : place + rows, :] = total.astype(bf16)

    place = 0
    for begin, rows in slotted:
        put(targets[0], place, begin + zh * rows, rows)
        put(targets[1], place, begin + (1 - zh) * rows, rows)
        place += rows
    begin, rows = rest
    put(targets[-1], 0, begin, rows)


def last_fold(idx, keep, recv, slotted=(), rest=None):
    wide = keep.shape[2]
    rest = rest or (0, keep.shape[1])
    rows = sum(size for _, size in slotted)
    sizes = ([rows, rows] if slotted else []) + [rest[1]]
    return call(
        functools.partial(last_body, slotted, rest),
        "last_fold",
        [(SMEM, idx), (VMEM, keep), (VMEM, recv)],
        [(VMEM, struct((size, wide), bf16)) for size in sizes],
    )


def final_body(parts, arrive, idx_ref, own_ref, sib_ref, *refs):
    arrive()
    outs, stages, sems = refs[: 2 * len(parts)], refs[2 * len(parts) : -1], refs[-1]
    chip, core = idx_ref[0], idx_ref[1]
    chips, _, wide = own_ref.shape
    first = 0
    copies = []

    def store(source, target):
        copies.append(pltpu.make_async_copy(source, target, sems.at[len(copies)]))
        copies[-1].start()

    for n, part in enumerate(parts):
        grad_ref, bias_ref, stage = outs[2 * n], outs[2 * n + 1], stages[n]
        size = part[0] // (2 * chips)
        columns = 1 if len(part) == 1 else part[1] // wide
        end = first + size * (9 if len(part) == 1 else columns)
        for c in range(columns):
            row = own_ref[0, end + c : end + c + 1, :].astype(f32)
            bias_ref[:, c * wide : (c + 1) * wide] = row
        for n_row, begin in enumerate(range(first, end, size)):
            for j in range(chips):
                for source, owner in ((own_ref, core), (sib_ref, 1 - core)):
                    home = chip ^ mask_of(j, owner, chips)
                    spot = at((2 * home + owner) * size, size, size)
                    piece = source[j, begin : begin + size, :].astype(f32)
                    if len(part) == 1:
                        stage[n_row, spot, :] = piece
                    else:
                        stage[spot, n_row * wide : (n_row + 1) * wide] = piece
            if len(part) == 1:
                store(stage.at[n_row], grad_ref.at[n_row])
        if len(part) > 1:
            store(stage, grad_ref)
        first = end + 16
    for copy in copies:
        copy.wait()


def final_grads(idx, own, sib, parts):
    wide = own.shape[2]
    results, stages = [], []
    for part in parts:
        shape = (9, part[0], wide) if len(part) == 1 else part
        results += [(FAR, struct(shape, f32)), (VMEM, struct((1, shape[-1]), f32))]
        stages.append(pltpu.VMEM(shape, f32))
    copies = sum(9 if len(part) == 1 else 1 for part in parts)
    return call(
        functools.partial(final_body, parts),
        "final_grads",
        [(SMEM, idx), (VMEM, own), (VMEM, sib)],
        results,
        stages + [pltpu.SemaphoreType.DMA((copies,))],
    )


def flat_pieces(gain, idx_ref, x_ref, go_ref, bias_ref, keep_ref, give_ref, first):
    chip, core = idx_ref[0], idx_ref[1]
    chips, _, wide = keep_ref.shape
    columns = go_ref.shape[1] // wide
    size = x_ref.shape[1] // (2 * chips)
    bias = jnp.concatenate(
        [bias_ref[:, c * wide : (c + 1) * wide] for c in range(columns)]
        + [jnp.zeros((16 - columns, wide), f32)],
        axis=0,
    ).astype(bf16)
    for j in range(chips):
        keep_ref[j, first + columns * size :, :] = bias
        give_ref[j, first + columns * size :, :] = bias
    for begin in range(0, x_ref.shape[1], 256):
        part = gain * dot(x_ref[:, begin : begin + 256], go_ref[...], TN)
        for b in range(0, 256 // size, 2):
            mask = chip ^ ((begin // size + b) // 2)
            slot = slot_of(mask, core, chips)
            give_slot = slot_of(mask, 1 - core, chips)
            for c in range(columns):
                even = part[b * size : (b + 1) * size, c * wide : (c + 1) * wide]
                odd = part[(b + 1) * size : (b + 2) * size, c * wide : (c + 1) * wide]
                spot = slice(first + c * size, first + (c + 1) * size)
                keep_ref[slot, spot, :] = jnp.where(core == 0, even, odd).astype(bf16)
                give_ref[give_slot, spot, :] = jnp.where(core == 0, odd, even).astype(bf16)


def flat_size(x, go, chips):
    return (go.shape[1] // 128) * (x.shape[1] // (2 * chips)) + 16


def outer_body(gain, arrive, idx_ref, x_ref, go_ref, bias_ref, keep_ref, give_ref):
    arrive()
    flat_pieces(gain, idx_ref, x_ref, go_ref, bias_ref, keep_ref, give_ref, 0)


def outer(idx, x, go, gain, bias, chips):
    return call(
        functools.partial(outer_body, gain),
        "outer",
        [(SMEM, idx), (LOAD, x), (LOAD, go), (LOAD, bias)],
        [(VMEM, struct((chips, flat_size(x, go, chips), 128), bf16))] * 2,
        spare=8,
    )


def start_body(arrive, idx_ref, valid_ref, cot_ref, outk_ref, go_ref, bias_ref, own_ref, give_ref):
    arrive()
    zl = idx_ref[3]
    masked = cot_ref[...].astype(f32) * valid_ref[0]
    go_ref[...] = masked.astype(bf16)
    bias_ref[...] = jnp.sum(masked, axis=0, keepdims=True)
    chans = outk_ref.shape[0] // 4
    block = cot_ref.shape[0] // 4
    for target, along in ((give_ref, 1 - zl), (own_ref, zl)):
        weights = jnp.concatenate(
            [outk_ref[at((2 * up + along) * chans, chans, chans), :] for up in range(2)], axis=0
        )
        for begin in range(0, cot_ref.shape[0], block):
            part = post_gain * dot(go_ref[begin : begin + block, :], weights, NT)
            target[begin : begin + block, :] = part.astype(target.dtype)


def start_back(idx, valid, cot, outk):
    spots, outs = cot.shape
    half = outk.shape[0] // 2
    return call(
        start_body,
        "start_back",
        [(SMEM, idx), (SMEM, valid), (LOAD, cot), (LOAD, outk)],
        [
            (VMEM, struct(cot.shape, bf16)),
            (VMEM, struct((1, outs), f32)),
            (VMEM, struct((spots, half), f32)),
            (VMEM, struct((spots, half), bf16)),
        ],
    )


def rows_body(side, arrive, idx_ref, own_ref, recv_ref, keep_ref, give_ref):
    arrive()
    zh = idx_ref[2]
    spots = keep_ref.shape[0]
    apart = own_ref.shape[0] - spots
    for target, begin in ((give_ref, (1 - zh) * apart), (keep_ref, zh * apart)):
        spot = at(begin, spots, side)
        total = own_ref[spot, :] + recv_ref[spot, :].astype(f32)
        target[...] = total.astype(target.dtype)


def rows_sum(side, idx, own, recv, spots):
    shape = (spots, own.shape[1])
    return call(
        functools.partial(rows_body, side),
        "rows_sum",
        [(SMEM, idx), (LOAD, own), (LOAD, recv)],
        [(VMEM, struct(shape, f32)), (VMEM, struct(shape, bf16))],
    )


def slots_body(arrive, idx_ref, own_ref, recv_ref, keep_ref, give_ref):
    arrive()
    zh = idx_ref[2]
    for target, slot in ((give_ref, 1 - zh), (keep_ref, zh)):
        total = own_ref[slot] + recv_ref[slot].astype(f32)
        target[...] = total.astype(bf16)


def slots_sum(idx, own, recv):
    shape = struct(own.shape[1:], bf16)
    return call(
        slots_body,
        "slots_sum",
        [(SMEM, idx), (VMEM, own), (VMEM, recv)],
        [(VMEM, shape), (VMEM, shape)],
    )


def input_body(arrive, idx_ref, keep_ref, recv_ref, out_ref):
    arrive()
    zh = idx_ref[2]
    half = keep_ref.shape[0]
    out_ref[at(zh * half, half, half), :] = keep_ref[...]
    out_ref[at((1 - zh) * half, half, half), :] = recv_ref[...]


def input_grad(idx, keep, recv):
    half, chans = keep.shape
    return call(
        input_body,
        "input_grad",
        [(SMEM, idx), (VMEM, keep), (VMEM, recv)],
        [(VMEM, struct((2 * half, chans), bf16))],
    )


def whole_body(side, arrive, idx_ref, xl, xa, xh, xd, rh, rl, x_ref, act_ref, sems):
    arrive()
    zh, zl = idx_ref[2], idx_ref[3]
    chans = xl.shape[1]
    spots = xa.shape[0]
    rest = xl.shape[0] - spots
    window, outside = at(zh * rest, spots, side), at((1 - zh) * spots, rest, side)

    def cols(up, along):
        return at((2 * up + along) * chans, chans, chans)

    run_copies(
        [
            (xl, x_ref.at[:, cols(zh, zl)]),
            (xa, x_ref.at[window, cols(zh, 1 - zl)]),
            (xh, x_ref.at[window, cols(1 - zh, zl)]),
            (xd, x_ref.at[window, cols(1 - zh, 1 - zl)]),
            (rl.at[0], x_ref.at[outside, cols(zh, 1 - zl)]),
            (rh, x_ref.at[outside, cols(1 - zh, zl)]),
            (rl.at[1], x_ref.at[outside, cols(1 - zh, 1 - zl)]),
        ],
        sems,
    )
    block = x_ref.shape[0] // 8
    for begin in range(0, x_ref.shape[0], block):
        rows = slice(begin, begin + block)
        act_ref[rows, :] = gelu(x_ref[rows, :].astype(f32)).astype(bf16)


def whole_input(side, idx, *parts):
    spots, chans = parts[0].shape
    return call(
        functools.partial(whole_body, side),
        "whole_input",
        [(SMEM, idx)] + [(FAR, p) for p in parts],
        [(VMEM, struct((spots, 4 * chans), bf16))] * 2,
        [pltpu.SemaphoreType.DMA((7,))],
    )


def join_body(arrive, idx_ref, own, recv, far_own, far_recv, out, sems):
    arrive()
    zh, zl = idx_ref[2], idx_ref[3]
    half = own.shape[0]
    chans = own.shape[1] // 2
    pairs = []
    for source, up, along in ((own, zh, zl), (recv, zh, 1 - zl), (far_own, 1 - zh, zl), (far_recv, 1 - zh, 1 - zl)):
        for slot in range(2):
            spot = at((2 * slot + along) * chans, chans, chans)
            target = out.at[at(up * half, half, half), spot]
            pairs.append((source.at[:, slot * chans : (slot + 1) * chans], target))
    run_copies(pairs, sems)


def join(idx, *parts):
    half, wide = parts[0].shape
    return call(
        join_body,
        "join",
        [(SMEM, idx)] + [(FAR, p) for p in parts],
        [(VMEM, struct((2 * half, 2 * wide), bf16))],
        [pltpu.SemaphoreType.DMA((8,))],
    )


def finish_body(arrive, idx_ref, valid_ref, x_ref, act_ref, idk_ref, outk_ref, ib_ref, out_ref):
    arrive()
    block = x_ref.shape[0] // 4
    for begin in range(0, x_ref.shape[0], block):
        rows = slice(begin, begin + block)
        identity = dot(x_ref[rows, :], idk_ref[...]) + ib_ref[...]
        branch = dot(act_ref[rows, :], outk_ref[...])
        out_ref[rows, :] = ((identity + post_gain * branch) * valid_ref[0]).astype(bf16)


def finish(idx, valid, x, act, idk, outk, ib):
    outs = idk.shape[1]
    return call(
        finish_body,
        "finish",
        [(SMEM, idx), (SMEM, valid), (LOAD, x), (LOAD, act), (LOAD, idk), (LOAD, outk)]
        + [(VMEM, ib.reshape(1, outs))],
        [(VMEM, struct((x.shape[0], outs), bf16))],
        spare=8,
    )


def flip(value, axis):
    return lax.ppermute(value, axis, [(0, 1), (1, 0)])


def cross(value, step, chips):
    pairs = []
    for chip in range(chips):
        for core in range(2):
            other = chip ^ step_bits(core, chips)[step]
            pairs.append((2 * chip + core, 2 * other + core))
    return lax.ppermute(value, DP, pairs)


def hops(value, chips):
    blocks = [value]
    for i in range(1, chips):
        pairs = []
        for chip in range(chips):
            for core in range(2):
                bits = step_bits(core, chips)
                mask = sum(bit for n, bit in enumerate(bits) if i >> (len(bits) - 1 - n) & 1)
                pairs.append((2 * (chip ^ mask) + core, 2 * chip + core))
        blocks.append(lax.ppermute(value, DP, pairs))
    return blocks


def swap(pieces, axis):
    return lax.all_to_all(pieces, axis, split_axis=0, concat_axis=0, tiled=True)


def after(value, other):
    return lax.optimization_barrier((value, other))[0]


def rows_of(value, start, size):
    return lax.dynamic_slice_in_dim(value, start, size, 0)


def local(
    pixels,
    counts,
    kernel_one,
    bias_one,
    kernel_two,
    bias_two,
    kernel_three,
    bias_three,
    out_kernel,
    identity_kernel,
    identity_bias,
    cotangent,
):
    images, rows, width, chans = pixels.shape
    side = width // 2
    spots = side * side
    half = spots // 2
    window = half + halo * side
    outs = cotangent.shape[3]
    chips = lax.axis_size("chip")
    chip, core, zh, zl = [lax.axis_index(a) for a in ("chip", "core", "zh", "zl")]
    idx = jnp.stack([chip, core, zh, zl]).astype(jnp.int32)
    taps = lambda kernel: kernel.reshape((9,) + kernel.shape[2:])
    one, two, three = taps(kernel_one), taps(kernel_two), taps(kernel_three)

    own_count = lax.dynamic_index_in_dim(counts, 2 * chip + core, 0, keepdims=True)
    valid = (own_count > 0).astype(f32)

    place = 2 * chip + core

    def units_of(kernel, size):
        if kernel.ndim == 3:
            block = kernel.shape[1] // (2 * chips)
            return lax.dynamic_slice_in_dim(kernel, place * block, block, 1)
        block = kernel.shape[0] // (2 * chips)
        block = lax.dynamic_slice_in_dim(kernel, place * block, block, 0)
        block = block.reshape(-1, size, block.shape[1] // 128, 128)
        return block.transpose(2, 0, 1, 3).reshape(-1, size, 128)

    steps = chips.bit_length() - 1

    def start_spread(piece, *others):
        return jnp.concatenate(after((piece[None], cross(piece[None], steps - 1, chips)), others))

    def end_spread(own, *others):
        for step in reversed(range(steps - 1)):
            own = jnp.concatenate(after((own, cross(own, step, chips)), others))
        return own, flip(own, "core")

    last = [idx]

    def turn(*others):
        return after(idx, (last[0],) + others)

    def ran(results):
        last[0] = results[-1] if isinstance(results, (list, tuple)) else results
        return results

    size = two.shape[1] // (2 * chips)
    deep = two.shape[1]
    cot = cotangent.reshape(spots, outs)
    one_piece = flip(units_of(one, size), "zh")
    pooled = ran(pool(pixels))
    go, identity_bias_grad, ga_own, ga_give = ran(start_back(turn(), valid, cot, out_kernel))
    bias_other = flip(after(jnp.stack([bias_one, bias_two, bias_three]), go), "zh")
    two_piece = units_of(after(two, pooled), size)
    last_piece = jnp.concatenate([units_of(after(k, pooled), size) for k in (three, identity_kernel)])
    cot_rows = rows_of(after(cot, pooled), (1 - zh) * half, half)
    xl = swap(after(pooled, (one_piece, two_piece, last_piece, cot_rows, ga_give)), DP)
    xl = xl.reshape(spots, chans)
    two_piece = flip(after(two_piece, one_piece), "zh")

    apart = spots - window
    xa = flip(rows_of(xl, zh * apart, window), "zl")
    xh = flip(rows_of(xl, (1 - zh) * apart, window), "zh")
    rest = spots - window
    rest_own = rows_of(xl, (1 - zh) * window, rest)
    rest_high = rows_of(xl, zh * window, rest)
    two_near = start_spread(after(two_piece, xl))
    one_near = start_spread(after(one_piece, xl), xh, xa, two_near, bias_other)
    xd = flip(xh, "zl")
    last_piece = flip(after(last_piece, xh), "zh")
    two_other = end_spread(two_near, xd)
    one_other = end_spread(one_near, xd, two_other[0], last_piece)
    ga_recv = flip(after(ga_give, xd), "zl")
    rest_high = flip(after(rest_high, xd), "zh")

    pre_one, act_one = ran(
        conv(
            side, turn(), (xl, xa, xh, xd), one, one_other, 0, bias_one, bias_other[0], True
        )
    )
    act_one_other = flip(act_one, "zl")
    ga_own, ga_give = ran(rows_sum(side, turn(), ga_own, ga_recv, half + (halo - 3) * side))
    pre_two, act_two = ran(
        conv(side, turn(), (act_one, act_one_other), two, two_other, 0, bias_two, bias_other[1])
    )
    act_two_other = flip(act_two, "zl")
    ga_recv = flip(after(ga_give, act_two), "zh")
    last_other = jnp.stack(after(hops(after(last_piece, act_one), chips), act_two))
    last_other = last_other, flip(last_other, "core")
    pre_three, act_three = ran(
        conv(side, turn(), (act_two, act_two_other), three, last_other, 0, bias_three, bias_other[2])
    )
    rest_low = flip(jnp.stack(after((rest_own, rest_high), act_three)), "zl")
    cot_far = flip(after(cot_rows, act_three), "zh")
    own_rows = rows_of(act_three, zh * (halo - 3) * side, half)

    gp_three, ga_own, ga_give = ran(
        back(side, turn(), (ga_own, ga_recv, pre_three), three, last_other, 0)
    )
    ga_recv = flip(ga_give, "zl")
    full_x, act_zero = ran(whole_input(side, turn(), xl, xa, xh, xd, rest_high, rest_low))
    keep_three, give_three = ran(
        weight_grad(
            side, half, turn(), gp_three, act_two, act_two_other, chips, (full_x, go, identity_bias_grad)
        )
    )
    gp_two, ga_own, ga_give = ran(
        back(side, turn(), (ga_own, ga_recv, pre_two), two, two_other, 0)
    )
    ga_recv = flip(ga_give, "zl")
    keep_two, give_two = ran(weight_grad(side, half, turn(cot_far), gp_two, act_one, act_one_other, chips))

    gp_mine, gp_theirs, gp_one = ran(slope_back(side, turn(), ga_own, ga_recv, pre_one, half))
    gp_theirs = flip(gp_theirs, "zh")
    recv_three = flip(after(give_three, gp_one), "core")
    recv_two = flip(after(give_two, gp_one), "core")
    gx_own, gx_give = ran(
        back(
            side, turn(), (gp_one,), one, one_other, 0,
            (valid, full_x, go, cot_far, identity_kernel, last_other, half),
        )
    )

    def folds(keep, recv, first, *others):
        for step in range(first, steps):
            keep, give = ran(fold(turn(*others), keep, recv))
            recv = cross(give, step, chips)
        return keep, recv

    keep_deep, give_deep = ran(fold(turn(gp_theirs), keep_three, recv_three, keep_two, recv_two))
    recv_deep = cross(give_deep, 0, chips)
    gx_recv = flip(after(gx_give, keep_deep), "zl")
    own_rows = after(own_rows, keep_deep)
    near_rows = flip(own_rows, "zl")
    far_rows = flip(own_rows, "zh")
    keep_one, give_one = ran(weight_one_grad(side, turn(), gp_mine, gp_theirs, act_zero, chips))
    recv_one = flip(give_one, "core")
    keep_deep, recv_deep = folds(keep_deep, recv_deep, 1)
    gx_keep, gx_give = ran(slots_sum(turn(), gx_own, gx_recv))
    gx_recv = flip(gx_give, "zh")
    keep_one, give_one = ran(fold(turn(far_rows), keep_one, recv_one))
    recv_one = cross(give_one, 0, chips)
    slot = 9 * size + 16
    flat = keep_three.shape[1] - 2 * slot
    keep_deep, give_deep, id_rows = ran(
        last_fold(
            turn(), keep_deep, recv_deep, ((0, slot), (2 * slot + flat, slot)), (2 * slot, flat)
        )
    )
    recv_deep = flip(give_deep, "zh")
    keep_one, recv_one = folds(keep_one, recv_one, 1)
    far_near_rows = flip(after(far_rows, keep_one), "zl")
    gx = ran(input_grad(turn(), gx_keep, gx_recv))
    gx = swap(gx.reshape(images, rows * width // 4, chans), DP)
    full_three = ran(join(turn(), own_rows, near_rows, far_rows, far_near_rows))
    keep_out, give_out = ran(outer(turn(), full_three, go, post_gain, identity_bias_grad, chips))
    recv_out = flip(give_out, "core")
    (total_one,) = ran([last_fold(turn(), keep_one, recv_one)])
    keep_out, give_out = ran(fold(turn(), keep_out, recv_out))
    recv_out = cross(give_out, 0, chips)
    deep_rows = (after(keep_deep, keep_out).astype(f32) + recv_deep.astype(f32)).astype(bf16)
    deep_rows = jnp.concatenate([deep_rows, id_rows])
    near_deep = start_spread(deep_rows)
    block_out = ran(
        finish(turn(deep_rows), valid, full_x, full_three, identity_kernel, out_kernel, identity_bias)
    )
    pixels_grad = ran(widen(turn(), gx, rows, width))
    keep_out, recv_out = folds(keep_out, recv_out, 1)
    (total_out,) = ran([last_fold(turn(), keep_out, recv_out)])
    near_one = start_spread(jnp.concatenate([total_one, total_out]))
    all_deep = end_spread(near_deep)
    all_one = end_spread(near_one)
    (
        kernel_three_grad,
        bias_three_grad,
        kernel_two_grad,
        bias_two_grad,
        identity_kernel_grad,
        identity_bias_grad,
    ) = ran(final_grads(turn(), *all_deep, ((deep,), (deep,), identity_kernel.shape)))
    kernel_one_grad, bias_one_grad, out_kernel_grad, _ = ran(
        final_grads(turn(), *all_one, ((one.shape[1],), out_kernel.shape))
    )

    return (
        block_out.reshape(cotangent.shape),
        pixels_grad,
        kernel_one_grad.reshape(kernel_one.shape),
        bias_one_grad[0],
        kernel_two_grad.reshape(kernel_two.shape),
        bias_two_grad[0],
        kernel_three_grad.reshape(kernel_three.shape),
        bias_three_grad[0],
        out_kernel_grad,
        identity_kernel_grad,
        identity_bias_grad[0],
    )


def solution(mesh):
    members = mesh.devices.size // mesh.shape["mp"]
    fine = Mesh(
        mesh.devices.reshape(members // 2, 2, 2, mesh.shape["mp"] // 2),
        ("chip", "core", "zh", "zl"),
    )
    return jax.shard_map(
        local,
        mesh=fine,
        in_specs=(
            P(None, DP, None, MP),
            P(),
            P(None, None, None, MP),
            P(MP),
            P(None, None, None, MP),
            P(MP),
            P(None, None, None, MP),
            P(MP),
            P(None, MP),
            P(None, MP),
            P(MP),
            P(DP, None, None, MP),
        ),
        out_specs=(
            P(DP, None, None, MP),
            P(None, DP, None, MP),
            P(None, None, None, MP),
            P(MP),
            P(None, None, None, MP),
            P(MP),
            P(None, None, None, MP),
            P(MP),
            P(None, MP),
            P(None, MP),
            P(MP),
        ),
        check_vma=False,
    )
```

```python
import functools
import math

import jax
import jax.numpy as jnp
from jax import lax
from jax.experimental import pallas as pl
from jax.experimental.pallas import tpu as pltpu
from jax.sharding import Mesh
from jax.sharding import PartitionSpec as P


post_gain = 0.015625
slope = 0.7978845608028654
cubic = 0.044715
halo = 6
bf16 = jnp.bfloat16
f32 = jnp.float32
NT = (((1,), (1,)), ((), ()))
TN = (((0,), (0,)), ((), ()))
NN = (((1,), (0,)), ((), ()))
DP = ("chip", "core")
MP = ("zh", "zl")


def dot(left, right, dims=NN):
    return lax.dot_general(left, right, dims, preferred_element_type=f32)


def gelu(value):
    inner = jnp.tanh(slope * (value + cubic * value * value * value))
    return 0.5 * value * (1.0 + inner)


def gelu_slope(value):
    square = value * value
    inner = jnp.tanh(slope * value * (1.0 + cubic * square))
    climb = slope * (1.0 + 3.0 * cubic * square)
    return 0.5 * (1.0 + inner) + 0.5 * value * (1.0 - inner * inner) * climb


def struct(shape, kind):
    return jax.ShapeDtypeStruct(shape, kind)


def lanes(blocks):
    return blocks[0] if len(blocks) == 1 else jnp.concatenate(blocks, axis=1)


def step_bits(core, chips):
    bits = [1 << n for n in range(chips.bit_length() - 1)]
    for n in range(0, len(bits) - 1, 2) if core else ():
        bits[n], bits[n + 1] = bits[n + 1], bits[n]
    return bits


def mask_of(i, core, chips):
    masks = []
    for which in range(2):
        bits = step_bits(which, chips)
        masks.append(sum(bit for n, bit in enumerate(bits) if i >> (len(bits) - 1 - n) & 1))
    return jnp.where(core == 0, masks[0], masks[1])


def slot_of(mask, core, chips):
    slots = []
    for which in range(2):
        bits = step_bits(which, chips)
        slot = 0
        for n, bit in enumerate(bits):
            slot = slot + ((mask >> (bit.bit_length() - 1)) & 1) * (1 << (len(bits) - 1 - n))
        slots.append(slot)
    return jnp.where(core == 0, slots[0], slots[1])


VMEM = pl.BlockSpec(memory_space=pltpu.VMEM)
SMEM = pl.BlockSpec(memory_space=pltpu.SMEM)
FAR = pl.BlockSpec(memory_space=pl.ANY)
LOAD = "load"


def size_of(array):
    return math.prod(array.shape) * jnp.dtype(array.dtype).itemsize


def call(body, name, ins, outs, scratch=(), spare=6, **more):
    loads = [i for i, (space, _) in enumerate(ins) if space is LOAD]
    spaces = [FAR if space is LOAD else space for space, _ in ins]
    arrays = [array for _, array in ins]
    out_specs = [space for space, _ in outs]
    out_shape = [shape for _, shape in outs]
    held = [arrays[i] for i in loads]
    buffers = [pltpu.VMEM(array.shape, array.dtype) for array in held]
    sems = [pltpu.SemaphoreType.DMA((len(held),))] if held else []
    vmem = sum(size_of(array) for array in held)
    vmem += sum(size_of(a) for space, a in list(ins) + list(outs) if space is VMEM)
    vmem += sum(size_of(b) for b in scratch if b.memory_space == pltpu.VMEM)
    moved = sum(size_of(a) for a in arrays + out_shape)

    def wrapped(*refs):
        inputs = list(refs[: len(ins)])
        outputs = refs[len(ins) : len(ins) + len(outs)]
        rest = refs[len(ins) + len(outs) :]
        kept, tail = rest[: len(held)], rest[len(held) :]
        copies = []
        if held:
            sem, tail = tail[0], tail[1:]
            copies = [
                pltpu.make_async_copy(inputs[i], kept[n], sem.at[n]) for n, i in enumerate(loads)
            ]
        for copy in copies:
            copy.start()
        for n, i in enumerate(loads):
            inputs[i] = kept[n]

        def arrive():
            for copy in copies:
                copy.wait()

        body(arrive, *inputs, *outputs, *tail)

    single = len(outs) == 1
    return pl.pallas_call(
        wrapped,
        in_specs=spaces,
        out_specs=out_specs[0] if single else out_specs,
        out_shape=out_shape[0] if single else out_shape,
        scratch_shapes=buffers + sems + list(scratch),
        compiler_params=pltpu.CompilerParams(vmem_limit_bytes=vmem + (spare << 20)),
        cost_estimate=pl.CostEstimate(flops=0, bytes_accessed=moved, transcendentals=0),
        name=name,
        **more,
    )(*arrays)


def run_copies(pairs, sems):
    for copy in start_copies(pairs, sems):
        copy.wait()


def slice_copies(group, idx_ref, own, blocks, sibling, wbuf):
    chip, core, zh = idx_ref[0], idx_ref[1], idx_ref[2]
    size = blocks.shape[-2]
    pairs = [(own, wbuf.at[zh])]
    for j in range(blocks.shape[0]):
        for source, owner in ((blocks, core), (sibling, 1 - core)):
            home = chip ^ mask_of(j, owner, blocks.shape[0])
            spot = at((2 * home + owner) * size, size, size)
            pairs.append((source.at[j, 9 * group : 9 * group + 9], wbuf.at[1 - zh, :, spot, :]))
    return pairs


def flat_copies(first, idx_ref, blocks, sibling, buffer):
    chip, core = idx_ref[0], idx_ref[1]
    columns, units = buffer.shape[:2]
    chips = blocks.shape[0]
    count = units // (2 * chips)
    pairs = []
    for j in range(chips):
        for source, owner in ((blocks, core), (sibling, 1 - core)):
            home = chip ^ mask_of(j, owner, chips)
            spot = pl.ds((2 * home + owner) * count, count)
            for c in range(columns):
                begin = first + c * count
                pairs.append((source.at[j, begin : begin + count], buffer.at[c, spot]))
    return pairs


def start_copies(pairs, sems):
    copies = [pltpu.make_async_copy(a, b, sems.at[i]) for i, (a, b) in enumerate(pairs)]
    for copy in copies:
        copy.start()
    return copies


def flat_rows(buffer, begin, count):
    columns, _, size, wide = buffer.shape
    return lanes([buffer[c, pl.ds(begin, count)].reshape(count * size, wide) for c in range(columns)])


def halves(spots, side):
    first = (spots // side + 1) // 2 * side
    return ((0, first), (first, spots - first))


def columns_of(size, wide, side):
    return lax.rem(lax.broadcasted_iota(jnp.int32, (size, wide), 0), side)


def at(start, size, unit):
    return pl.ds(pl.multiple_of(start, unit), size)


def pool_body(arrive, x_ref, out_ref):
    arrive()
    rows, width, chans = x_ref.shape[1:]
    half = width // 2
    pixel = lax.broadcasted_iota(jnp.int32, (half, 2 * width), 1)
    place = lax.broadcasted_iota(jnp.int32, (half, 2 * width), 0)
    inside = (lax.rem(pixel, width) >= 2 * place) & (lax.rem(pixel, width) < 2 * place + 2)
    pick = jnp.where(inside, 0.25, 0.0).astype(bf16)
    for image in range(x_ref.shape[0]):
        for row in range(rows // 2):
            window = x_ref[image, 2 * row : 2 * row + 2].reshape(2 * width, chans)
            out_ref[image, row * half : (row + 1) * half, :] = dot(pick, window).astype(bf16)


def pool(pixels):
    images, rows, width, chans = pixels.shape
    shape = struct((images, rows * width // 4, chans), bf16)
    return call(pool_body, "pool", [(LOAD, pixels)], [(VMEM, shape)])


def widen_body(arrive, idx_ref, g_ref, out_ref):
    arrive()
    rows, width, chans = out_ref.shape[1:]
    half = width // 2
    pixel = lax.broadcasted_iota(jnp.int32, (width, half), 0)
    place = lax.broadcasted_iota(jnp.int32, (width, half), 1)
    inside = (pixel >= 2 * place) & (pixel < 2 * place + 2)
    pick = jnp.where(inside, 0.25, 0.0).astype(bf16)
    for image in range(g_ref.shape[0]):
        for row in range(rows // 2):
            wide = dot(pick, g_ref[image, row * half : (row + 1) * half, :]).astype(bf16)
            out_ref[image, 2 * row] = wide
            out_ref[image, 2 * row + 1] = wide


def widen(idx, grad, rows, width):
    images, spots, chans = grad.shape
    step = images // 4
    block = pl.BlockSpec((step, spots, chans), lambda i: (i, 0, 0))
    out = pl.BlockSpec((step, rows, width, chans), lambda i: (i, 0, 0, 0))
    return call(
        widen_body,
        "widen",
        [(SMEM, idx), (block, grad)],
        [(out, struct((images, rows, width, chans), bf16))],
        grid=(4,),
    )


def conv_body(side, first, group, arrive, idx_ref, *refs):
    zh, zl = idx_ref[2], idx_ref[3]
    if first:
        xl, xa, xh, xd, wl, wo, ws, bl, bo, pre_ref, act_ref, xbuf, wbuf, acc, sems = refs
        chans = xl.shape[1]
        spots = xbuf.shape[0]
        begin = zh * (xl.shape[0] - spots)
        pairs = []
        for source, up, along in ((xl, zh, zl), (xa, zh, 1 - zl), (xh, 1 - zh, zl), (xd, 1 - zh, 1 - zl)):
            if source is xl:
                source = xl.at[at(begin, spots, side), :]
            pairs.append((source, xbuf.at[:, at((2 * up + along) * chans, chans, chans)]))
    else:
        xl, xa, wl, wo, ws, bl, bo, pre_ref, act_ref, xbuf, wbuf, acc, sems = refs
        chans = xl.shape[1] // 2
        spots = xbuf.shape[0]
        pairs = []
        for source, along in ((xl, zl), (xa, 1 - zl)):
            for up in range(2):
                pairs.append(
                    (
                        source.at[:, up * chans : (up + 1) * chans],
                        xbuf.at[:, at((2 * up + along) * chans, chans, chans)],
                    )
                )
    run_copies(slice_copies(group, idx_ref, wl, wo, ws, wbuf) + pairs, sems)
    arrive()
    acc[...] = jnp.zeros_like(acc)
    outs = 2 * wl.shape[2]
    for x in range(3):
        weights = lanes([wbuf[u, 3 * y + x] for y in range(3) for u in range(2)])
        for begin, block in halves(spots, side):
            values = xbuf[begin : begin + block, :]
            if first:
                values = gelu(values.astype(f32)).astype(bf16)
            product = dot(values, weights)
            for y in range(3):
                place = begin + side * (2 - y)
                acc[x, place : place + block, :] += product[:, y * outs : (y + 1) * outs]
    own, other = bl[...], bo[...]
    bias = lanes([jnp.where(zh == 0, own, other), jnp.where(zh == 0, other, own)])
    for begin, block in halves(act_ref.shape[0], side):
        column = columns_of(block, outs, side)
        spot = at(begin + side + zh * side, block, side)
        left = pltpu.roll(acc[0, spot, :], 1, 0)
        right = pltpu.roll(acc[2, spot, :], block - 1, 0)
        pre = acc[1, spot, :] + bias
        pre = pre + jnp.where(column > 0, left, 0.0)
        pre = pre + jnp.where(column < side - 1, right, 0.0)
        pre_ref[begin : begin + block, :] = pre
        act_ref[begin : begin + block, :] = gelu(pre).astype(bf16)


def conv(side, idx, sources, own, other, group, bias, bias_other, first=False):
    taps, depth, outs = own.shape
    spots = sources[1].shape[0]
    rows = spots - side
    return call(
        functools.partial(conv_body, side, first, group),
        "conv",
        [(SMEM, idx)]
        + [(FAR, s) for s in sources]
        + [(FAR, own), (FAR, other[0]), (FAR, other[1])]
        + [(VMEM, bias.reshape(1, outs)), (VMEM, bias_other.reshape(1, outs))],
        [(VMEM, struct((rows, 2 * outs), f32)), (VMEM, struct((rows, 2 * outs), bf16))],
        [
            pltpu.VMEM((spots, depth), bf16),
            pltpu.VMEM((2, taps, depth, outs), bf16),
            pltpu.VMEM((3, spots + 2 * side, 2 * outs), f32),
            pltpu.SemaphoreType.DMA((2 * other[0].shape[0] + 5,)),
        ],
        spare=14 if first else 8,
    )


def spread_taps(side, grad, taps_ref):
    pixels, outs = grad.shape
    column = columns_of(pixels, outs, side)
    wide = grad.astype(f32)
    ahead = jnp.where(column < side - 1, pltpu.roll(wide, pixels - 1, 0), 0.0).astype(bf16)
    behind = jnp.where(column > 0, pltpu.roll(wide, 1, 0), 0.0).astype(bf16)
    edge = jnp.zeros((side, 3 * outs), bf16)
    taps_ref[:side, :] = edge
    taps_ref[side + pixels :, :] = edge
    taps_ref[side : side + pixels, :] = jnp.concatenate([ahead, grad, behind], axis=1)


def tap_block(side, taps_ref, begin, block):
    return lanes([taps_ref[at(begin + side * (2 - y), block, side), :] for y in range(3)])


def slope_body(side, arrive, idx_ref, keep_ref, recv_ref, pre_ref, mine_ref, theirs_ref, gp_ref):
    arrive()
    zh = idx_ref[2]
    half, outs = mine_ref.shape
    total = keep_ref[...] + recv_ref[...].astype(f32)
    spots = keep_ref.shape[0]
    pre = pre_ref[at(zh * (pre_ref.shape[0] - spots), spots, side), :]
    gp_ref[...] = (total * gelu_slope(pre)).astype(bf16)
    own = gp_ref[at(zh * (gp_ref.shape[0] - half), half, side), :]
    low, high = own[:, :outs], own[:, outs:]
    mine_ref[...] = jnp.where(zh == 0, low, high)
    theirs_ref[...] = jnp.where(zh == 0, high, low)


def slope_back(side, idx, keep, recv, pre, half):
    outs = pre.shape[1] // 2
    return call(
        functools.partial(slope_body, side),
        "slope_back",
        [(SMEM, idx), (VMEM, keep), (VMEM, recv), (LOAD, pre)],
        [
            (VMEM, struct((half, outs), bf16)),
            (VMEM, struct((half, outs), bf16)),
            (VMEM, struct(keep.shape, bf16)),
        ],
    )


def back_body(side, last, group, arrive, idx_ref, *refs):
    zh, zl = idx_ref[2], idx_ref[3]
    if last:
        valid_ref, grad_ref, x_ref, go_ref, far_ref, idk_ref, wl, wo, ws, po, ps = refs[:11]
        own_ref, give_ref, taps_ref, wbuf, idk_far, sems = refs[11:]
    else:
        keep_ref, recv_ref, pre_ref, wl, wo, ws, gp_ref, own_ref, give_ref, taps_ref, wbuf, sems = refs
    pairs = slice_copies(group, idx_ref, wl, wo, ws, wbuf)
    if last:
        pairs += flat_copies(9, idx_ref, po, ps, idk_far)
    copies = start_copies(pairs, sems)
    arrive()
    if last:
        grad = grad_ref[...]
    else:
        spots = gp_ref.shape[0]

        def window(ref):
            return ref[at(zh * (ref.shape[0] - spots), spots, side), :]

        total = window(keep_ref) + window(recv_ref).astype(f32)
        grad = (total * gelu_slope(window(pre_ref))).astype(bf16)
        gp_ref[...] = grad
    spread_taps(side, grad, taps_ref)
    depth, outs = wl.shape[1:]
    pixels = own_ref.shape[-2]
    start = zh * side
    for copy in copies:
        copy.wait()
    chans = depth // 4

    def rows(index):
        spot = at(index * chans, chans, chans)
        return lanes([wbuf[u, t, spot, :] for t in range(9) for u in range(2)])

    for target, along in ((give_ref, 1 - zl), (own_ref, zl)):
        if last:
            units = chans // idk_far.shape[2]
            for up in range(2):
                index = 2 * up + along
                weights = rows(index)
                near = idk_ref[at(index * chans, chans, chans), :]
                far = flat_rows(idk_far, index * units, units)
                apart = zh * (far_ref.shape[0] - pixels)
                for begin, block in halves(pixels, side):
                    here = at(zh * pixels + begin, block, side)
                    part = dot(tap_block(side, taps_ref, start + begin, block), weights, NT)
                    x = x_ref[here, at(index * chans, chans, chans)]
                    part = part * gelu_slope(x.astype(f32))
                    part = part + dot(go_ref[here, :], near, NT)
                    part = part + valid_ref[0] * dot(far_ref[at(apart + begin, block, side), :], far, NT)
                    target[up, begin : begin + block, :] = part.astype(target.dtype)
        else:
            weights = jnp.concatenate([rows(along), rows(2 + along)], axis=0)
            for begin, block in halves(pixels, side):
                part = dot(tap_block(side, taps_ref, start + begin, block), weights, NT)
                target[begin : begin + block, :] = part.astype(target.dtype)


def back(side, idx, sources, own, other, group, last=None):
    taps, depth, outs = own.shape
    spots = min(sources[0].shape[0], sources[-1].shape[0])
    copies = 2 * other[0].shape[0] + 1
    extra = []
    scratch = []
    if last:
        valid, full_x, go, cot_far, idk, pieces, half = last
        chans = depth // 4
        shape = (2, half, chans)
        results = []
        extra = [(FAR, pieces[0]), (FAR, pieces[1])]
        sources = list(sources) + [full_x, go, cot_far, idk]
        columns, size = idk.shape[1] // 128, pieces[0].shape[2]
        scratch = [pltpu.VMEM((columns, depth // size, size, 128), bf16)]
        copies += 2 * other[0].shape[0] * columns
    else:
        shape = (spots - side, depth // 2)
        results = [(VMEM, struct((spots, 2 * outs), bf16))]
    results += [(VMEM, struct(shape, f32)), (VMEM, struct(shape, bf16))]
    return call(
        functools.partial(back_body, side, bool(last), group),
        "back",
        [(SMEM, idx)]
        + ([(SMEM, last[0])] if last else [])
        + [(LOAD, source) for source in sources]
        + [(FAR, own), (FAR, other[0]), (FAR, other[1])]
        + extra,
        results,
        [pltpu.VMEM((spots + 2 * side, 6 * outs), bf16), pltpu.VMEM((2, taps, depth, outs), bf16)]
        + scratch
        + [pltpu.SemaphoreType.DMA((copies,))],
        spare=14 if last else 10,
    )


def put_blocks(idx_ref, keep_ref, give_ref, part, tap, first_block, size, begin=0):
    chip, core = idx_ref[0], idx_ref[1]
    for b in range(0, part.shape[0] // size, 2):
        even = part[b * size : (b + 1) * size, :]
        odd = part[(b + 1) * size : (b + 2) * size, :]
        mask = chip ^ ((first_block + b) // 2)
        slot = slot_of(mask, core, keep_ref.shape[0])
        give_slot = slot_of(mask, 1 - core, keep_ref.shape[0])
        rows = slice(begin + tap * size, begin + (tap + 1) * size)
        keep_ref[slot, rows, :] = jnp.where(core == 0, even, odd).astype(bf16)
        give_ref[give_slot, rows, :] = jnp.where(core == 0, odd, even).astype(bf16)


def weight_body(side, half, flat, arrive, idx_ref, gp_ref, *refs):
    if flat:
        full_ref, go_ref, bias_ref = refs[:3]
        refs = refs[3:]
    xl, xa, keep_ref, give_ref, xbuf, taps_ref, sems = refs
    arrive()
    zh, zl = idx_ref[2], idx_ref[3]
    chans = xl.shape[1] // 2
    spots = xbuf.shape[0]
    window = at(zh * (xl.shape[0] - spots), spots, side)
    pairs = []
    for source, along in ((xl, zl), (xa, 1 - zl)):
        for up in range(2):
            pairs.append(
                (
                    source.at[window, up * chans : (up + 1) * chans],
                    xbuf.at[:, at((2 * up + along) * chans, chans, chans)],
                )
            )
    run_copies(pairs, sems)
    wide = gp_ref.shape[1]
    outs = wide // 2
    spot = lax.broadcasted_iota(jnp.int32, (spots, wide), 0) - zh * side
    grad = gp_ref[at(zh * (gp_ref.shape[0] - spots), spots, side), :].astype(f32)
    grad = jnp.where((spot >= 0) & (spot < half), grad, 0.0)
    bias = jnp.sum(grad, axis=0, keepdims=True)
    spread_taps(side, grad.astype(bf16), taps_ref)
    blocks = 2 * keep_ref.shape[0]
    depth = xbuf.shape[1]
    size = depth // blocks
    for begin in range(0, depth, 256):
        values = xbuf[:, begin : begin + 256]
        for y in range(3):
            place = side * (2 - y)
            part = dot(values, taps_ref[place : place + spots, :], TN)
            for x in range(3):
                for u in range(2):
                    col = x * wide + u * outs
                    put_blocks(
                        idx_ref, keep_ref, give_ref, part[:, col : col + outs],
                        3 * y + x, begin // size, size, u * (9 * size + 16),
                    )
    for u in range(2):
        row = jnp.broadcast_to(bias[:, u * outs : (u + 1) * outs], (16, outs)).astype(bf16)
        for j in range(keep_ref.shape[0]):
            spot = slice(u * (9 * size + 16) + 9 * size, (u + 1) * (9 * size + 16))
            keep_ref[j, spot, :] = row
            give_ref[j, spot, :] = row
    if flat:
        first = 2 * (9 * size + 16)
        flat_pieces(1.0, idx_ref, full_ref, go_ref, bias_ref, keep_ref, give_ref, first)


def weight_grad(side, half, idx, grad, act, act_other, chips, flat=()):
    spots = half + side
    wide = grad.shape[1]
    outs = wide // 2
    depth = 2 * act.shape[1]
    rows = 2 * (9 * depth // (2 * chips) + 16)
    if flat:
        rows += flat_size(flat[0], flat[1], chips)
    return call(
        functools.partial(weight_body, side, half, bool(flat)),
        "weight_grad",
        [(SMEM, idx), (LOAD, grad)] + [(LOAD, a) for a in flat] + [(FAR, act), (FAR, act_other)],
        [(VMEM, struct((chips, rows, outs), bf16))] * 2,
        [
            pltpu.VMEM((spots, depth), bf16),
            pltpu.VMEM((spots + 2 * side, 3 * wide), bf16),
            pltpu.SemaphoreType.DMA((4,)),
        ],
        spare=10,
    )


def weight_one_body(side, arrive, idx_ref, mine_ref, theirs_ref, x_ref, *refs):
    keep_ref, give_ref, gp_ref, taps_ref = refs
    arrive()
    zh = idx_ref[2]
    half, outs = mine_ref.shape
    gp_ref[at(zh * half, half, side), :] = mine_ref[...]
    gp_ref[at((1 - zh) * half, half, side), :] = theirs_ref[...]
    grad = gp_ref[...]
    bias = jnp.sum(grad.astype(f32), axis=0, keepdims=True)
    spread_taps(side, grad, taps_ref)
    blocks = 2 * keep_ref.shape[0]
    spots, depth = x_ref.shape
    size = depth // blocks
    right = tap_block(side, taps_ref, 0, spots)
    for begin in range(0, depth, 256):
        part = dot(x_ref[:, begin : begin + 256], right, TN)
        for tap in range(9):
            put_blocks(
                idx_ref, keep_ref, give_ref, part[:, tap * outs : (tap + 1) * outs],
                tap, begin // size, size,
            )
    row = jnp.broadcast_to(bias, (16, outs)).astype(bf16)
    first = 9 * size + 16
    for j in range(keep_ref.shape[0]):
        keep_ref[j, 9 * size : first, :] = row
        give_ref[j, 9 * size : first, :] = row


def weight_one_grad(side, idx, mine, theirs, act_zero, chips):
    spots, depth = act_zero.shape
    outs = mine.shape[1]
    rows = 9 * depth // (2 * chips) + 16
    return call(
        functools.partial(weight_one_body, side),
        "weight_one_grad",
        [(SMEM, idx), (LOAD, mine), (LOAD, theirs), (LOAD, act_zero)],
        [(VMEM, struct((chips, rows, outs), bf16))] * 2,
        [
            pltpu.VMEM((spots, outs), bf16),
            pltpu.VMEM((spots + 2 * side, 3 * outs), bf16),
        ],
        spare=14,
    )


def fold_body(pairs, arrive, idx_ref, *refs):
    arrive()
    ins, (keep_ref, give_ref) = refs[: 2 * pairs], refs[2 * pairs :]
    half = keep_ref.shape[0]
    for i in range(2 * half):
        target = keep_ref if i < half else give_ref
        begin = 0
        for keep, recv in zip(ins[0::2], ins[1::2]):
            rows = keep.shape[1]
            total = keep[i].astype(f32) + recv[i].astype(f32)
            target[i % half, begin : begin + rows, :] = total.astype(bf16)
            begin += rows


def fold(idx, *arrays):
    blocks, _, wide = arrays[0].shape
    rows = sum(a.shape[1] for a in arrays[0::2])
    return call(
        functools.partial(fold_body, len(arrays) // 2),
        "fold",
        [(SMEM, idx)] + [(VMEM, a) for a in arrays],
        [(VMEM, struct((blocks // 2, rows, wide), bf16))] * 2,
    )


def last_body(slotted, rest, arrive, idx_ref, keep_in, recv_in, *targets):
    arrive()
    zh = idx_ref[2]

    def put(target, place, begin, rows):
        spot = at(begin, rows, 16)
        total = keep_in[0, spot, :].astype(f32) + recv_in[0, spot, :].astype(f32)
        target[place : place + rows, :] = total.astype(bf16)

    place = 0
    for begin, rows in slotted:
        put(targets[0], place, begin + zh * rows, rows)
        put(targets[1], place, begin + (1 - zh) * rows, rows)
        place += rows
    begin, rows = rest
    put(targets[-1], 0, begin, rows)


def last_fold(idx, keep, recv, slotted=(), rest=None):
    wide = keep.shape[2]
    rest = rest or (0, keep.shape[1])
    rows = sum(size for _, size in slotted)
    sizes = ([rows, rows] if slotted else []) + [rest[1]]
    return call(
        functools.partial(last_body, slotted, rest),
        "last_fold",
        [(SMEM, idx), (VMEM, keep), (VMEM, recv)],
        [(VMEM, struct((size, wide), bf16)) for size in sizes],
    )


def final_body(parts, arrive, idx_ref, own_ref, sib_ref, *refs):
    arrive()
    outs, stages, sems = refs[: 2 * len(parts)], refs[2 * len(parts) : -1], refs[-1]
    chip, core = idx_ref[0], idx_ref[1]
    chips, _, wide = own_ref.shape
    first = 0
    copies = []

    def store(source, target):
        copies.append(pltpu.make_async_copy(source, target, sems.at[len(copies)]))
        copies[-1].start()

    for n, part in enumerate(parts):
        grad_ref, bias_ref, stage = outs[2 * n], outs[2 * n + 1], stages[n]
        size = part[0] // (2 * chips)
        columns = 1 if len(part) == 1 else part[1] // wide
        end = first + size * (9 if len(part) == 1 else columns)
        for c in range(columns):
            row = own_ref[0, end + c : end + c + 1, :].astype(f32)
            bias_ref[:, c * wide : (c + 1) * wide] = row
        for n_row, begin in enumerate(range(first, end, size)):
            for j in range(chips):
                for source, owner in ((own_ref, core), (sib_ref, 1 - core)):
                    home = chip ^ mask_of(j, owner, chips)
                    spot = at((2 * home + owner) * size, size, size)
                    piece = source[j, begin : begin + size, :].astype(f32)
                    if len(part) == 1:
                        stage[n_row, spot, :] = piece
                    else:
                        stage[spot, n_row * wide : (n_row + 1) * wide] = piece
            if len(part) == 1:
                store(stage.at[n_row], grad_ref.at[n_row])
        if len(part) > 1:
            store(stage, grad_ref)
        first = end + 16
    for copy in copies:
        copy.wait()


def final_grads(idx, own, sib, parts):
    wide = own.shape[2]
    results, stages = [], []
    for part in parts:
        shape = (9, part[0], wide) if len(part) == 1 else part
        results += [(FAR, struct(shape, f32)), (VMEM, struct((1, shape[-1]), f32))]
        stages.append(pltpu.VMEM(shape, f32))
    copies = sum(9 if len(part) == 1 else 1 for part in parts)
    return call(
        functools.partial(final_body, parts),
        "final_grads",
        [(SMEM, idx), (VMEM, own), (VMEM, sib)],
        results,
        stages + [pltpu.SemaphoreType.DMA((copies,))],
    )


def flat_pieces(gain, idx_ref, x_ref, go_ref, bias_ref, keep_ref, give_ref, first):
    chip, core = idx_ref[0], idx_ref[1]
    chips, _, wide = keep_ref.shape
    columns = go_ref.shape[1] // wide
    size = x_ref.shape[1] // (2 * chips)
    bias = jnp.concatenate(
        [bias_ref[:, c * wide : (c + 1) * wide] for c in range(columns)]
        + [jnp.zeros((16 - columns, wide), f32)],
        axis=0,
    ).astype(bf16)
    for j in range(chips):
        keep_ref[j, first + columns * size :, :] = bias
        give_ref[j, first + columns * size :, :] = bias
    for begin in range(0, x_ref.shape[1], 256):
        part = gain * dot(x_ref[:, begin : begin + 256], go_ref[...], TN)
        for b in range(0, 256 // size, 2):
            mask = chip ^ ((begin // size + b) // 2)
            slot = slot_of(mask, core, chips)
            give_slot = slot_of(mask, 1 - core, chips)
            for c in range(columns):
                even = part[b * size : (b + 1) * size, c * wide : (c + 1) * wide]
                odd = part[(b + 1) * size : (b + 2) * size, c * wide : (c + 1) * wide]
                spot = slice(first + c * size, first + (c + 1) * size)
                keep_ref[slot, spot, :] = jnp.where(core == 0, even, odd).astype(bf16)
                give_ref[give_slot, spot, :] = jnp.where(core == 0, odd, even).astype(bf16)


def flat_size(x, go, chips):
    return (go.shape[1] // 128) * (x.shape[1] // (2 * chips)) + 16


def outer_body(gain, arrive, idx_ref, x_ref, go_ref, bias_ref, keep_ref, give_ref):
    arrive()
    flat_pieces(gain, idx_ref, x_ref, go_ref, bias_ref, keep_ref, give_ref, 0)


def outer(idx, x, go, gain, bias, chips):
    return call(
        functools.partial(outer_body, gain),
        "outer",
        [(SMEM, idx), (LOAD, x), (LOAD, go), (LOAD, bias)],
        [(VMEM, struct((chips, flat_size(x, go, chips), 128), bf16))] * 2,
        spare=8,
    )


def start_body(arrive, idx_ref, valid_ref, cot_ref, outk_ref, go_ref, bias_ref, own_ref, give_ref):
    arrive()
    zl = idx_ref[3]
    masked = cot_ref[...].astype(f32) * valid_ref[0]
    go_ref[...] = masked.astype(bf16)
    bias_ref[...] = jnp.sum(masked, axis=0, keepdims=True)
    chans = outk_ref.shape[0] // 4
    block = cot_ref.shape[0] // 4
    for target, along in ((give_ref, 1 - zl), (own_ref, zl)):
        weights = jnp.concatenate(
            [outk_ref[at((2 * up + along) * chans, chans, chans), :] for up in range(2)], axis=0
        )
        for begin in range(0, cot_ref.shape[0], block):
            part = post_gain * dot(go_ref[begin : begin + block, :], weights, NT)
            target[begin : begin + block, :] = part.astype(target.dtype)


def start_back(idx, valid, cot, outk):
    spots, outs = cot.shape
    half = outk.shape[0] // 2
    return call(
        start_body,
        "start_back",
        [(SMEM, idx), (SMEM, valid), (LOAD, cot), (LOAD, outk)],
        [
            (VMEM, struct(cot.shape, bf16)),
            (VMEM, struct((1, outs), f32)),
            (VMEM, struct((spots, half), f32)),
            (VMEM, struct((spots, half), bf16)),
        ],
    )


def rows_body(side, arrive, idx_ref, own_ref, recv_ref, keep_ref, give_ref):
    arrive()
    zh = idx_ref[2]
    spots = keep_ref.shape[0]
    apart = own_ref.shape[0] - spots
    for target, begin in ((give_ref, (1 - zh) * apart), (keep_ref, zh * apart)):
        spot = at(begin, spots, side)
        total = own_ref[spot, :] + recv_ref[spot, :].astype(f32)
        target[...] = total.astype(target.dtype)


def rows_sum(side, idx, own, recv, spots):
    shape = (spots, own.shape[1])
    return call(
        functools.partial(rows_body, side),
        "rows_sum",
        [(SMEM, idx), (LOAD, own), (LOAD, recv)],
        [(VMEM, struct(shape, f32)), (VMEM, struct(shape, bf16))],
    )


def slots_body(arrive, idx_ref, own_ref, recv_ref, keep_ref, give_ref):
    arrive()
    zh = idx_ref[2]
    for target, slot in ((give_ref, 1 - zh), (keep_ref, zh)):
        total = own_ref[slot] + recv_ref[slot].astype(f32)
        target[...] = total.astype(bf16)


def slots_sum(idx, own, recv):
    shape = struct(own.shape[1:], bf16)
    return call(
        slots_body,
        "slots_sum",
        [(SMEM, idx), (VMEM, own), (VMEM, recv)],
        [(VMEM, shape), (VMEM, shape)],
    )


def input_body(arrive, idx_ref, keep_ref, recv_ref, out_ref):
    arrive()
    zh = idx_ref[2]
    half = keep_ref.shape[0]
    out_ref[at(zh * half, half, half), :] = keep_ref[...]
    out_ref[at((1 - zh) * half, half, half), :] = recv_ref[...]


def input_grad(idx, keep, recv):
    half, chans = keep.shape
    return call(
        input_body,
        "input_grad",
        [(SMEM, idx), (VMEM, keep), (VMEM, recv)],
        [(VMEM, struct((2 * half, chans), bf16))],
    )


def whole_body(side, arrive, idx_ref, xl, xa, xh, xd, rh, rl, x_ref, act_ref, sems):
    arrive()
    zh, zl = idx_ref[2], idx_ref[3]
    chans = xl.shape[1]
    spots = xa.shape[0]
    rest = xl.shape[0] - spots
    window, outside = at(zh * rest, spots, side), at((1 - zh) * spots, rest, side)

    def cols(up, along):
        return at((2 * up + along) * chans, chans, chans)

    run_copies(
        [
            (xl, x_ref.at[:, cols(zh, zl)]),
            (xa, x_ref.at[window, cols(zh, 1 - zl)]),
            (xh, x_ref.at[window, cols(1 - zh, zl)]),
            (xd, x_ref.at[window, cols(1 - zh, 1 - zl)]),
            (rl.at[0], x_ref.at[outside, cols(zh, 1 - zl)]),
            (rh, x_ref.at[outside, cols(1 - zh, zl)]),
            (rl.at[1], x_ref.at[outside, cols(1 - zh, 1 - zl)]),
        ],
        sems,
    )
    block = x_ref.shape[0] // 8
    for begin in range(0, x_ref.shape[0], block):
        rows = slice(begin, begin + block)
        act_ref[rows, :] = gelu(x_ref[rows, :].astype(f32)).astype(bf16)


def whole_input(side, idx, *parts):
    spots, chans = parts[0].shape
    return call(
        functools.partial(whole_body, side),
        "whole_input",
        [(SMEM, idx)] + [(FAR, p) for p in parts],
        [(VMEM, struct((spots, 4 * chans), bf16))] * 2,
        [pltpu.SemaphoreType.DMA((7,))],
    )


def join_body(arrive, idx_ref, own, recv, far_own, far_recv, out, sems):
    arrive()
    zh, zl = idx_ref[2], idx_ref[3]
    half = own.shape[0]
    chans = own.shape[1] // 2
    pairs = []
    for source, up, along in ((own, zh, zl), (recv, zh, 1 - zl), (far_own, 1 - zh, zl), (far_recv, 1 - zh, 1 - zl)):
        for slot in range(2):
            spot = at((2 * slot + along) * chans, chans, chans)
            target = out.at[at(up * half, half, half), spot]
            pairs.append((source.at[:, slot * chans : (slot + 1) * chans], target))
    run_copies(pairs, sems)


def join(idx, *parts):
    half, wide = parts[0].shape
    return call(
        join_body,
        "join",
        [(SMEM, idx)] + [(FAR, p) for p in parts],
        [(VMEM, struct((2 * half, 2 * wide), bf16))],
        [pltpu.SemaphoreType.DMA((8,))],
    )


def finish_body(arrive, idx_ref, valid_ref, x_ref, act_ref, idk_ref, outk_ref, ib_ref, out_ref):
    arrive()
    block = x_ref.shape[0] // 4
    for begin in range(0, x_ref.shape[0], block):
        rows = slice(begin, begin + block)
        identity = dot(x_ref[rows, :], idk_ref[...]) + ib_ref[...]
        branch = dot(act_ref[rows, :], outk_ref[...])
        out_ref[rows, :] = ((identity + post_gain * branch) * valid_ref[0]).astype(bf16)


def finish(idx, valid, x, act, idk, outk, ib):
    outs = idk.shape[1]
    return call(
        finish_body,
        "finish",
        [(SMEM, idx), (SMEM, valid), (LOAD, x), (LOAD, act), (LOAD, idk), (LOAD, outk)]
        + [(VMEM, ib.reshape(1, outs))],
        [(VMEM, struct((x.shape[0], outs), bf16))],
        spare=8,
    )


def flip(value, axis):
    return lax.ppermute(value, axis, [(0, 1), (1, 0)])


def cross(value, step, chips):
    pairs = []
    for chip in range(chips):
        for core in range(2):
            other = chip ^ step_bits(core, chips)[step]
            pairs.append((2 * chip + core, 2 * other + core))
    return lax.ppermute(value, DP, pairs)


def hops(value, chips):
    blocks = [value]
    for i in range(1, chips):
        pairs = []
        for chip in range(chips):
            for core in range(2):
                bits = step_bits(core, chips)
                mask = sum(bit for n, bit in enumerate(bits) if i >> (len(bits) - 1 - n) & 1)
                pairs.append((2 * (chip ^ mask) + core, 2 * chip + core))
        blocks.append(lax.ppermute(value, DP, pairs))
    return blocks


def swap(pieces, axis):
    return lax.all_to_all(pieces, axis, split_axis=0, concat_axis=0, tiled=True)


def after(value, other):
    return lax.optimization_barrier((value, other))[0]


def rows_of(value, start, size):
    return lax.dynamic_slice_in_dim(value, start, size, 0)


def local(
    pixels,
    counts,
    kernel_one,
    bias_one,
    kernel_two,
    bias_two,
    kernel_three,
    bias_three,
    out_kernel,
    identity_kernel,
    identity_bias,
    cotangent,
):
    images, rows, width, chans = pixels.shape
    side = width // 2
    spots = side * side
    half = spots // 2
    window = half + halo * side
    outs = cotangent.shape[3]
    chips = lax.axis_size("chip")
    chip, core, zh, zl = [lax.axis_index(a) for a in ("chip", "core", "zh", "zl")]
    idx = jnp.stack([chip, core, zh, zl]).astype(jnp.int32)
    taps = lambda kernel: kernel.reshape((9,) + kernel.shape[2:])
    one, two, three = taps(kernel_one), taps(kernel_two), taps(kernel_three)

    own_count = lax.dynamic_index_in_dim(counts, 2 * chip + core, 0, keepdims=True)
    valid = (own_count > 0).astype(f32)

    place = 2 * chip + core

    def units_of(kernel, size):
        if kernel.ndim == 3:
            block = kernel.shape[1] // (2 * chips)
            return lax.dynamic_slice_in_dim(kernel, place * block, block, 1)
        block = kernel.shape[0] // (2 * chips)
        block = lax.dynamic_slice_in_dim(kernel, place * block, block, 0)
        block = block.reshape(-1, size, block.shape[1] // 128, 128)
        return block.transpose(2, 0, 1, 3).reshape(-1, size, 128)

    steps = chips.bit_length() - 1

    def start_spread(piece, *others):
        return jnp.concatenate(after((piece[None], cross(piece[None], steps - 1, chips)), others))

    def end_spread(own, *others):
        for step in reversed(range(steps - 1)):
            own = jnp.concatenate(after((own, cross(own, step, chips)), others))
        return own, flip(own, "core")

    last = [idx]

    def turn(*others):
        return after(idx, (last[0],) + others)

    def ran(results):
        last[0] = results[-1] if isinstance(results, (list, tuple)) else results
        return results

    size = two.shape[1] // (2 * chips)
    deep = two.shape[1]
    cot = cotangent.reshape(spots, outs)
    one_piece = flip(units_of(one, size), "zh")
    pooled = ran(pool(pixels))
    go, identity_bias_grad, ga_own, ga_give = ran(start_back(turn(), valid, cot, out_kernel))
    bias_other = flip(after(jnp.stack([bias_one, bias_two, bias_three]), go), "zh")
    two_piece = units_of(after(two, pooled), size)
    last_piece = jnp.concatenate([units_of(after(k, pooled), size) for k in (three, identity_kernel)])
    cot_rows = rows_of(after(cot, pooled), (1 - zh) * half, half)
    xl = swap(after(pooled, (one_piece, two_piece, last_piece, cot_rows, ga_give)), DP)
    xl = xl.reshape(spots, chans)
    two_piece = flip(after(two_piece, one_piece), "zh")

    apart = spots - window
    xa = flip(rows_of(xl, zh * apart, window), "zl")
    xh = flip(rows_of(xl, (1 - zh) * apart, window), "zh")
    rest = spots - window
    rest_own = rows_of(xl, (1 - zh) * window, rest)
    rest_high = rows_of(xl, zh * window, rest)
    two_near = start_spread(after(two_piece, xl))
    one_near = start_spread(after(one_piece, xl), xh, xa, two_near, bias_other)
    xd = flip(xh, "zl")
    last_piece = flip(after(last_piece, xh), "zh")
    two_other = end_spread(two_near, xd)
    one_other = end_spread(one_near, xd, two_other[0], last_piece)
    ga_recv = flip(after(ga_give, xd), "zl")
    rest_high = flip(after(rest_high, xd), "zh")

    pre_one, act_one = ran(
        conv(
            side, turn(), (xl, xa, xh, xd), one, one_other, 0, bias_one, bias_other[0], True
        )
    )
    act_one_other = flip(act_one, "zl")
    ga_own, ga_give = ran(rows_sum(side, turn(), ga_own, ga_recv, half + (halo - 3) * side))
    pre_two, act_two = ran(
        conv(side, turn(), (act_one, act_one_other), two, two_other, 0, bias_two, bias_other[1])
    )
    act_two_other = flip(act_two, "zl")
    ga_recv = flip(after(ga_give, act_two), "zh")
    last_other = jnp.stack(after(hops(after(last_piece, act_one), chips), act_two))
    last_other = last_other, flip(last_other, "core")
    pre_three, act_three = ran(
        conv(side, turn(), (act_two, act_two_other), three, last_other, 0, bias_three, bias_other[2])
    )
    rest_low = flip(jnp.stack(after((rest_own, rest_high), act_three)), "zl")
    cot_far = flip(after(cot_rows, act_three), "zh")
    own_rows = rows_of(act_three, zh * (halo - 3) * side, half)

    gp_three, ga_own, ga_give = ran(
        back(side, turn(), (ga_own, ga_recv, pre_three), three, last_other, 0)
    )
    ga_recv = flip(ga_give, "zl")
    full_x, act_zero = ran(whole_input(side, turn(), xl, xa, xh, xd, rest_high, rest_low))
    keep_three, give_three = ran(
        weight_grad(
            side, half, turn(), gp_three, act_two, act_two_other, chips, (full_x, go, identity_bias_grad)
        )
    )
    gp_two, ga_own, ga_give = ran(
        back(side, turn(), (ga_own, ga_recv, pre_two), two, two_other, 0)
    )
    ga_recv = flip(ga_give, "zl")
    keep_two, give_two = ran(weight_grad(side, half, turn(cot_far), gp_two, act_one, act_one_other, chips))

    gp_mine, gp_theirs, gp_one = ran(slope_back(side, turn(), ga_own, ga_recv, pre_one, half))
    gp_theirs = flip(gp_theirs, "zh")
    recv_three = flip(after(give_three, gp_one), "core")
    recv_two = flip(after(give_two, gp_one), "core")
    gx_own, gx_give = ran(
        back(
            side, turn(), (gp_one,), one, one_other, 0,
            (valid, full_x, go, cot_far, identity_kernel, last_other, half),
        )
    )

    def folds(keep, recv, first, *others):
        for step in range(first, steps):
            keep, give = ran(fold(turn(*others), keep, recv))
            recv = cross(give, step, chips)
        return keep, recv

    keep_deep, give_deep = ran(fold(turn(gp_theirs), keep_three, recv_three, keep_two, recv_two))
    recv_deep = cross(give_deep, 0, chips)
    gx_recv = flip(after(gx_give, keep_deep), "zl")
    own_rows = after(own_rows, keep_deep)
    near_rows = flip(own_rows, "zl")
    far_rows = flip(own_rows, "zh")
    keep_one, give_one = ran(weight_one_grad(side, turn(), gp_mine, gp_theirs, act_zero, chips))
    recv_one = flip(give_one, "core")
    keep_deep, recv_deep = folds(keep_deep, recv_deep, 1, far_rows)
    gx_keep, gx_give = ran(slots_sum(turn(), gx_own, gx_recv))
    gx_recv = flip(gx_give, "zh")
    keep_one, give_one = ran(fold(turn(), keep_one, recv_one))
    recv_one = cross(give_one, 0, chips)
    slot = 9 * size + 16
    flat = keep_three.shape[1] - 2 * slot
    keep_deep, give_deep, id_rows = ran(
        last_fold(
            turn(), keep_deep, recv_deep, ((0, slot), (2 * slot + flat, slot)), (2 * slot, flat)
        )
    )
    recv_deep = flip(give_deep, "zh")
    far_near_rows = flip(after(far_rows, keep_deep), "zl")
    keep_one, recv_one = folds(keep_one, recv_one, 1)
    gx = ran(input_grad(turn(), gx_keep, gx_recv))
    full_three = ran(join(turn(), own_rows, near_rows, far_rows, far_near_rows))
    keep_out, give_out = ran(outer(turn(), full_three, go, post_gain, identity_bias_grad, chips))
    recv_out = flip(give_out, "core")
    (total_one,) = ran([last_fold(turn(), keep_one, recv_one)])
    keep_out, give_out = ran(fold(turn(), keep_out, recv_out))
    recv_out = cross(give_out, 0, chips)
    deep_rows = (after(keep_deep, keep_out).astype(f32) + recv_deep.astype(f32)).astype(bf16)
    deep_rows = jnp.concatenate([deep_rows, id_rows])
    near_deep = start_spread(deep_rows)
    gx = after(gx, deep_rows)
    gx = swap(gx.reshape(images, rows * width // 4, chans), DP)
    block_out = ran(
        finish(turn(deep_rows), valid, full_x, full_three, identity_kernel, out_kernel, identity_bias)
    )
    keep_out, recv_out = folds(keep_out, recv_out, 1)
    (total_out,) = ran([last_fold(turn(), keep_out, recv_out)])
    near_one = start_spread(jnp.concatenate([total_one, total_out]))
    pixels_grad = ran(widen(turn(near_one, near_deep), gx, rows, width))
    all_deep = end_spread(near_deep)
    all_one = end_spread(near_one)
    (
        kernel_three_grad,
        bias_three_grad,
        kernel_two_grad,
        bias_two_grad,
        identity_kernel_grad,
        identity_bias_grad,
    ) = ran(final_grads(turn(), *all_deep, ((deep,), (deep,), identity_kernel.shape)))
    kernel_one_grad, bias_one_grad, out_kernel_grad, _ = ran(
        final_grads(turn(), *all_one, ((one.shape[1],), out_kernel.shape))
    )

    return (
        block_out.reshape(cotangent.shape),
        pixels_grad,
        kernel_one_grad.reshape(kernel_one.shape),
        bias_one_grad[0],
        kernel_two_grad.reshape(kernel_two.shape),
        bias_two_grad[0],
        kernel_three_grad.reshape(kernel_three.shape),
        bias_three_grad[0],
        out_kernel_grad,
        identity_kernel_grad,
        identity_bias_grad[0],
    )


def solution(mesh):
    members = mesh.devices.size // mesh.shape["mp"]
    fine = Mesh(
        mesh.devices.reshape(members // 2, 2, 2, mesh.shape["mp"] // 2),
        ("chip", "core", "zh", "zl"),
    )
    return jax.shard_map(
        local,
        mesh=fine,
        in_specs=(
            P(None, DP, None, MP),
            P(),
            P(None, None, None, MP),
            P(MP),
            P(None, None, None, MP),
            P(MP),
            P(None, None, None, MP),
            P(MP),
            P(None, MP),
            P(None, MP),
            P(MP),
            P(DP, None, None, MP),
        ),
        out_specs=(
            P(DP, None, None, MP),
            P(None, DP, None, MP),
            P(None, None, None, MP),
            P(MP),
            P(None, None, None, MP),
            P(MP),
            P(None, None, None, MP),
            P(MP),
            P(None, MP),
            P(None, MP),
            P(MP),
        ),
        check_vma=False,
    )
```

```python
import functools
import math

import jax
import jax.numpy as jnp
from jax import lax
from jax.experimental import pallas as pl
from jax.experimental.pallas import tpu as pltpu
from jax.sharding import Mesh
from jax.sharding import PartitionSpec as P


post_gain = 0.015625
slope = 0.7978845608028654
cubic = 0.044715
halo = 6
bf16 = jnp.bfloat16
f32 = jnp.float32
NT = (((1,), (1,)), ((), ()))
TN = (((0,), (0,)), ((), ()))
NN = (((1,), (0,)), ((), ()))
DP = ("chip", "core")
MP = ("zh", "zl")


def dot(left, right, dims=NN):
    return lax.dot_general(left, right, dims, preferred_element_type=f32)


def gelu(value):
    inner = jnp.tanh(slope * (value + cubic * value * value * value))
    return 0.5 * value * (1.0 + inner)


def gelu_slope(value):
    square = value * value
    inner = jnp.tanh(slope * value * (1.0 + cubic * square))
    climb = slope * (1.0 + 3.0 * cubic * square)
    return 0.5 * (1.0 + inner) + 0.5 * value * (1.0 - inner * inner) * climb


def struct(shape, kind):
    return jax.ShapeDtypeStruct(shape, kind)


def lanes(blocks):
    return blocks[0] if len(blocks) == 1 else jnp.concatenate(blocks, axis=1)


def step_bits(core, chips):
    bits = [1 << n for n in range(chips.bit_length() - 1)]
    for n in range(0, len(bits) - 1, 2) if core else ():
        bits[n], bits[n + 1] = bits[n + 1], bits[n]
    return bits


def mask_of(i, core, chips):
    masks = []
    for which in range(2):
        bits = step_bits(which, chips)
        masks.append(sum(bit for n, bit in enumerate(bits) if i >> (len(bits) - 1 - n) & 1))
    return jnp.where(core == 0, masks[0], masks[1])


def slot_of(mask, core, chips):
    slots = []
    for which in range(2):
        bits = step_bits(which, chips)
        slot = 0
        for n, bit in enumerate(bits):
            slot = slot + ((mask >> (bit.bit_length() - 1)) & 1) * (1 << (len(bits) - 1 - n))
        slots.append(slot)
    return jnp.where(core == 0, slots[0], slots[1])


VMEM = pl.BlockSpec(memory_space=pltpu.VMEM)
SMEM = pl.BlockSpec(memory_space=pltpu.SMEM)
FAR = pl.BlockSpec(memory_space=pl.ANY)
LOAD = "load"


def size_of(array):
    return math.prod(array.shape) * jnp.dtype(array.dtype).itemsize


def call(body, name, ins, outs, scratch=(), spare=6, **more):
    loads = [i for i, (space, _) in enumerate(ins) if space is LOAD]
    spaces = [FAR if space is LOAD else space for space, _ in ins]
    arrays = [array for _, array in ins]
    out_specs = [space for space, _ in outs]
    out_shape = [shape for _, shape in outs]
    held = [arrays[i] for i in loads]
    buffers = [pltpu.VMEM(array.shape, array.dtype) for array in held]
    sems = [pltpu.SemaphoreType.DMA((len(held),))] if held else []
    vmem = sum(size_of(array) for array in held)
    vmem += sum(size_of(a) for space, a in list(ins) + list(outs) if space is VMEM)
    vmem += sum(size_of(b) for b in scratch if b.memory_space == pltpu.VMEM)
    moved = sum(size_of(a) for a in arrays + out_shape)

    def wrapped(*refs):
        inputs = list(refs[: len(ins)])
        outputs = refs[len(ins) : len(ins) + len(outs)]
        rest = refs[len(ins) + len(outs) :]
        kept, tail = rest[: len(held)], rest[len(held) :]
        copies = []
        if held:
            sem, tail = tail[0], tail[1:]
            copies = [
                pltpu.make_async_copy(inputs[i], kept[n], sem.at[n]) for n, i in enumerate(loads)
            ]
        for copy in copies:
            copy.start()
        for n, i in enumerate(loads):
            inputs[i] = kept[n]

        def arrive():
            for copy in copies:
                copy.wait()

        body(arrive, *inputs, *outputs, *tail)

    single = len(outs) == 1
    return pl.pallas_call(
        wrapped,
        in_specs=spaces,
        out_specs=out_specs[0] if single else out_specs,
        out_shape=out_shape[0] if single else out_shape,
        scratch_shapes=buffers + sems + list(scratch),
        compiler_params=pltpu.CompilerParams(vmem_limit_bytes=vmem + (spare << 20)),
        cost_estimate=pl.CostEstimate(flops=0, bytes_accessed=moved, transcendentals=0),
        name=name,
        **more,
    )(*arrays)


def run_copies(pairs, sems):
    for copy in start_copies(pairs, sems):
        copy.wait()


def slice_copies(group, idx_ref, own, blocks, sibling, wbuf):
    chip, core, zh = idx_ref[0], idx_ref[1], idx_ref[2]
    size = blocks.shape[-2]
    pairs = [(own, wbuf.at[zh])]
    for j in range(blocks.shape[0]):
        for source, owner in ((blocks, core), (sibling, 1 - core)):
            home = chip ^ mask_of(j, owner, blocks.shape[0])
            spot = at((2 * home + owner) * size, size, size)
            pairs.append((source.at[j, 9 * group : 9 * group + 9], wbuf.at[1 - zh, :, spot, :]))
    return pairs


def flat_copies(first, idx_ref, blocks, sibling, buffer):
    chip, core = idx_ref[0], idx_ref[1]
    columns, units = buffer.shape[:2]
    chips = blocks.shape[0]
    count = units // (2 * chips)
    pairs = []
    for j in range(chips):
        for source, owner in ((blocks, core), (sibling, 1 - core)):
            home = chip ^ mask_of(j, owner, chips)
            spot = pl.ds((2 * home + owner) * count, count)
            for c in range(columns):
                begin = first + c * count
                pairs.append((source.at[j, begin : begin + count], buffer.at[c, spot]))
    return pairs


def start_copies(pairs, sems):
    copies = [pltpu.make_async_copy(a, b, sems.at[i]) for i, (a, b) in enumerate(pairs)]
    for copy in copies:
        copy.start()
    return copies


def flat_rows(buffer, begin, count):
    columns, _, size, wide = buffer.shape
    return lanes([buffer[c, pl.ds(begin, count)].reshape(count * size, wide) for c in range(columns)])


def halves(spots, side):
    first = (spots // side + 1) // 2 * side
    return ((0, first), (first, spots - first))


def columns_of(size, wide, side):
    return lax.rem(lax.broadcasted_iota(jnp.int32, (size, wide), 0), side)


def at(start, size, unit):
    return pl.ds(pl.multiple_of(start, unit), size)


def pool_body(arrive, x_ref, out_ref):
    arrive()
    rows, width, chans = x_ref.shape[1:]
    half = width // 2
    pixel = lax.broadcasted_iota(jnp.int32, (half, 2 * width), 1)
    place = lax.broadcasted_iota(jnp.int32, (half, 2 * width), 0)
    inside = (lax.rem(pixel, width) >= 2 * place) & (lax.rem(pixel, width) < 2 * place + 2)
    pick = jnp.where(inside, 0.25, 0.0).astype(bf16)
    for image in range(x_ref.shape[0]):
        for row in range(rows // 2):
            window = x_ref[image, 2 * row : 2 * row + 2].reshape(2 * width, chans)
            out_ref[image, row * half : (row + 1) * half, :] = dot(pick, window).astype(bf16)


def pool(pixels):
    images, rows, width, chans = pixels.shape
    shape = struct((images, rows * width // 4, chans), bf16)
    return call(pool_body, "pool", [(LOAD, pixels)], [(VMEM, shape)])


def widen_body(arrive, idx_ref, g_ref, out_ref):
    arrive()
    rows, width, chans = out_ref.shape[1:]
    half = width // 2
    pixel = lax.broadcasted_iota(jnp.int32, (width, half), 0)
    place = lax.broadcasted_iota(jnp.int32, (width, half), 1)
    inside = (pixel >= 2 * place) & (pixel < 2 * place + 2)
    pick = jnp.where(inside, 0.25, 0.0).astype(bf16)
    for image in range(g_ref.shape[0]):
        for row in range(rows // 2):
            wide = dot(pick, g_ref[image, row * half : (row + 1) * half, :]).astype(bf16)
            out_ref[image, 2 * row] = wide
            out_ref[image, 2 * row + 1] = wide


def widen(idx, grad, rows, width):
    images, spots, chans = grad.shape
    step = images // 4
    block = pl.BlockSpec((step, spots, chans), lambda i: (i, 0, 0))
    out = pl.BlockSpec((step, rows, width, chans), lambda i: (i, 0, 0, 0))
    return call(
        widen_body,
        "widen",
        [(SMEM, idx), (block, grad)],
        [(out, struct((images, rows, width, chans), bf16))],
        grid=(4,),
    )


def conv_body(side, first, group, arrive, idx_ref, *refs):
    zh, zl = idx_ref[2], idx_ref[3]
    if first:
        xl, xa, xh, xd, wl, wo, ws, bl, bo, pre_ref, act_ref, xbuf, wbuf, acc, sems = refs
        chans = xl.shape[1]
        spots = xbuf.shape[0]
        begin = zh * (xl.shape[0] - spots)
        pairs = []
        for source, up, along in ((xl, zh, zl), (xa, zh, 1 - zl), (xh, 1 - zh, zl), (xd, 1 - zh, 1 - zl)):
            if source is xl:
                source = xl.at[at(begin, spots, side), :]
            pairs.append((source, xbuf.at[:, at((2 * up + along) * chans, chans, chans)]))
    else:
        xl, xa, wl, wo, ws, bl, bo, pre_ref, act_ref, xbuf, wbuf, acc, sems = refs
        chans = xl.shape[1] // 2
        spots = xbuf.shape[0]
        pairs = []
        for source, along in ((xl, zl), (xa, 1 - zl)):
            for up in range(2):
                pairs.append(
                    (
                        source.at[:, up * chans : (up + 1) * chans],
                        xbuf.at[:, at((2 * up + along) * chans, chans, chans)],
                    )
                )
    run_copies(slice_copies(group, idx_ref, wl, wo, ws, wbuf) + pairs, sems)
    arrive()
    acc[...] = jnp.zeros_like(acc)
    outs = 2 * wl.shape[2]
    for x in range(3):
        weights = lanes([wbuf[u, 3 * y + x] for y in range(3) for u in range(2)])
        for begin, block in halves(spots, side):
            values = xbuf[begin : begin + block, :]
            if first:
                values = gelu(values.astype(f32)).astype(bf16)
            product = dot(values, weights)
            for y in range(3):
                place = begin + side * (2 - y)
                acc[x, place : place + block, :] += product[:, y * outs : (y + 1) * outs]
    own, other = bl[...], bo[...]
    bias = lanes([jnp.where(zh == 0, own, other), jnp.where(zh == 0, other, own)])
    for begin, block in halves(act_ref.shape[0], side):
        column = columns_of(block, outs, side)
        spot = at(begin + side + zh * side, block, side)
        left = pltpu.roll(acc[0, spot, :], 1, 0)
        right = pltpu.roll(acc[2, spot, :], block - 1, 0)
        pre = acc[1, spot, :] + bias
        pre = pre + jnp.where(column > 0, left, 0.0)
        pre = pre + jnp.where(column < side - 1, right, 0.0)
        pre_ref[begin : begin + block, :] = pre
        act_ref[begin : begin + block, :] = gelu(pre).astype(bf16)


def conv(side, idx, sources, own, other, group, bias, bias_other, first=False):
    taps, depth, outs = own.shape
    spots = sources[1].shape[0]
    rows = spots - side
    return call(
        functools.partial(conv_body, side, first, group),
        "conv",
        [(SMEM, idx)]
        + [(FAR, s) for s in sources]
        + [(FAR, own), (FAR, other[0]), (FAR, other[1])]
        + [(VMEM, bias.reshape(1, outs)), (VMEM, bias_other.reshape(1, outs))],
        [(VMEM, struct((rows, 2 * outs), f32)), (VMEM, struct((rows, 2 * outs), bf16))],
        [
            pltpu.VMEM((spots, depth), bf16),
            pltpu.VMEM((2, taps, depth, outs), bf16),
            pltpu.VMEM((3, spots + 2 * side, 2 * outs), f32),
            pltpu.SemaphoreType.DMA((2 * other[0].shape[0] + 5,)),
        ],
        spare=14 if first else 8,
    )


def spread_taps(side, grad, taps_ref):
    pixels, outs = grad.shape
    column = columns_of(pixels, outs, side)
    wide = grad.astype(f32)
    ahead = jnp.where(column < side - 1, pltpu.roll(wide, pixels - 1, 0), 0.0).astype(bf16)
    behind = jnp.where(column > 0, pltpu.roll(wide, 1, 0), 0.0).astype(bf16)
    edge = jnp.zeros((side, 3 * outs), bf16)
    taps_ref[:side, :] = edge
    taps_ref[side + pixels :, :] = edge
    taps_ref[side : side + pixels, :] = jnp.concatenate([ahead, grad, behind], axis=1)


def tap_block(side, taps_ref, begin, block):
    return lanes([taps_ref[at(begin + side * (2 - y), block, side), :] for y in range(3)])


def slope_body(side, arrive, idx_ref, keep_ref, recv_ref, pre_ref, mine_ref, theirs_ref, gp_ref):
    arrive()
    zh = idx_ref[2]
    half, outs = mine_ref.shape
    total = keep_ref[...] + recv_ref[...].astype(f32)
    spots = keep_ref.shape[0]
    pre = pre_ref[at(zh * (pre_ref.shape[0] - spots), spots, side), :]
    gp_ref[...] = (total * gelu_slope(pre)).astype(bf16)
    own = gp_ref[at(zh * (gp_ref.shape[0] - half), half, side), :]
    low, high = own[:, :outs], own[:, outs:]
    mine_ref[...] = jnp.where(zh == 0, low, high)
    theirs_ref[...] = jnp.where(zh == 0, high, low)


def slope_back(side, idx, keep, recv, pre, half):
    outs = pre.shape[1] // 2
    return call(
        functools.partial(slope_body, side),
        "slope_back",
        [(SMEM, idx), (VMEM, keep), (VMEM, recv), (LOAD, pre)],
        [
            (VMEM, struct((half, outs), bf16)),
            (VMEM, struct((half, outs), bf16)),
            (VMEM, struct(keep.shape, bf16)),
        ],
    )


def back_body(side, last, group, arrive, idx_ref, *refs):
    zh, zl = idx_ref[2], idx_ref[3]
    if last:
        valid_ref, grad_ref, x_ref, go_ref, far_ref, idk_ref, wl, wo, ws, po, ps = refs[:11]
        own_ref, give_ref, taps_ref, wbuf, idk_far, sems = refs[11:]
    else:
        keep_ref, recv_ref, pre_ref, wl, wo, ws, gp_ref, own_ref, give_ref, taps_ref, wbuf, sems = refs
    pairs = slice_copies(group, idx_ref, wl, wo, ws, wbuf)
    if last:
        pairs += flat_copies(9, idx_ref, po, ps, idk_far)
    copies = start_copies(pairs, sems)
    arrive()
    if last:
        grad = grad_ref[...]
    else:
        spots = gp_ref.shape[0]

        def window(ref):
            return ref[at(zh * (ref.shape[0] - spots), spots, side), :]

        total = window(keep_ref) + window(recv_ref).astype(f32)
        grad = (total * gelu_slope(window(pre_ref))).astype(bf16)
        gp_ref[...] = grad
    spread_taps(side, grad, taps_ref)
    depth, outs = wl.shape[1:]
    pixels = own_ref.shape[-2]
    start = zh * side
    for copy in copies:
        copy.wait()
    chans = depth // 4

    def rows(index):
        spot = at(index * chans, chans, chans)
        return lanes([wbuf[u, t, spot, :] for t in range(9) for u in range(2)])

    for target, along in ((give_ref, 1 - zl), (own_ref, zl)):
        if last:
            units = chans // idk_far.shape[2]
            for up in range(2):
                index = 2 * up + along
                weights = rows(index)
                near = idk_ref[at(index * chans, chans, chans), :]
                far = flat_rows(idk_far, index * units, units)
                apart = zh * (far_ref.shape[0] - pixels)
                for begin, block in halves(pixels, side):
                    here = at(zh * pixels + begin, block, side)
                    part = dot(tap_block(side, taps_ref, start + begin, block), weights, NT)
                    x = x_ref[here, at(index * chans, chans, chans)]
                    part = part * gelu_slope(x.astype(f32))
                    part = part + dot(go_ref[here, :], near, NT)
                    part = part + valid_ref[0] * dot(far_ref[at(apart + begin, block, side), :], far, NT)
                    target[up, begin : begin + block, :] = part.astype(target.dtype)
        else:
            weights = jnp.concatenate([rows(along), rows(2 + along)], axis=0)
            for begin, block in halves(pixels, side):
                part = dot(tap_block(side, taps_ref, start + begin, block), weights, NT)
                target[begin : begin + block, :] = part.astype(target.dtype)


def back(side, idx, sources, own, other, group, last=None):
    taps, depth, outs = own.shape
    spots = min(sources[0].shape[0], sources[-1].shape[0])
    copies = 2 * other[0].shape[0] + 1
    extra = []
    scratch = []
    if last:
        valid, full_x, go, cot_far, idk, pieces, half = last
        chans = depth // 4
        shape = (2, half, chans)
        results = []
        extra = [(FAR, pieces[0]), (FAR, pieces[1])]
        sources = list(sources) + [full_x, go, cot_far, idk]
        columns, size = idk.shape[1] // 128, pieces[0].shape[2]
        scratch = [pltpu.VMEM((columns, depth // size, size, 128), bf16)]
        copies += 2 * other[0].shape[0] * columns
    else:
        shape = (spots - side, depth // 2)
        results = [(VMEM, struct((spots, 2 * outs), bf16))]
    results += [(VMEM, struct(shape, f32)), (VMEM, struct(shape, bf16))]
    return call(
        functools.partial(back_body, side, bool(last), group),
        "back",
        [(SMEM, idx)]
        + ([(SMEM, last[0])] if last else [])
        + [(LOAD, source) for source in sources]
        + [(FAR, own), (FAR, other[0]), (FAR, other[1])]
        + extra,
        results,
        [pltpu.VMEM((spots + 2 * side, 6 * outs), bf16), pltpu.VMEM((2, taps, depth, outs), bf16)]
        + scratch
        + [pltpu.SemaphoreType.DMA((copies,))],
        spare=14 if last else 10,
    )


def put_blocks(idx_ref, keep_ref, give_ref, part, tap, first_block, size, begin=0):
    chip, core = idx_ref[0], idx_ref[1]
    for b in range(0, part.shape[0] // size, 2):
        even = part[b * size : (b + 1) * size, :]
        odd = part[(b + 1) * size : (b + 2) * size, :]
        mask = chip ^ ((first_block + b) // 2)
        slot = slot_of(mask, core, keep_ref.shape[0])
        give_slot = slot_of(mask, 1 - core, keep_ref.shape[0])
        rows = slice(begin + tap * size, begin + (tap + 1) * size)
        keep_ref[slot, rows, :] = jnp.where(core == 0, even, odd).astype(bf16)
        give_ref[give_slot, rows, :] = jnp.where(core == 0, odd, even).astype(bf16)


def weight_body(side, half, flat, arrive, idx_ref, gp_ref, *refs):
    if flat:
        full_ref, go_ref, bias_ref = refs[:3]
        refs = refs[3:]
    xl, xa, keep_ref, give_ref, xbuf, taps_ref, sems = refs
    arrive()
    zh, zl = idx_ref[2], idx_ref[3]
    chans = xl.shape[1] // 2
    spots = xbuf.shape[0]
    window = at(zh * (xl.shape[0] - spots), spots, side)
    pairs = []
    for source, along in ((xl, zl), (xa, 1 - zl)):
        for up in range(2):
            pairs.append(
                (
                    source.at[window, up * chans : (up + 1) * chans],
                    xbuf.at[:, at((2 * up + along) * chans, chans, chans)],
                )
            )
    run_copies(pairs, sems)
    wide = gp_ref.shape[1]
    outs = wide // 2
    spot = lax.broadcasted_iota(jnp.int32, (spots, wide), 0) - zh * side
    grad = gp_ref[at(zh * (gp_ref.shape[0] - spots), spots, side), :].astype(f32)
    grad = jnp.where((spot >= 0) & (spot < half), grad, 0.0)
    bias = jnp.sum(grad, axis=0, keepdims=True)
    spread_taps(side, grad.astype(bf16), taps_ref)
    blocks = 2 * keep_ref.shape[0]
    depth = xbuf.shape[1]
    size = depth // blocks
    for begin in range(0, depth, 256):
        values = xbuf[:, begin : begin + 256]
        for y in range(3):
            place = side * (2 - y)
            part = dot(values, taps_ref[place : place + spots, :], TN)
            for x in range(3):
                for u in range(2):
                    col = x * wide + u * outs
                    put_blocks(
                        idx_ref, keep_ref, give_ref, part[:, col : col + outs],
                        3 * y + x, begin // size, size, u * (9 * size + 16),
                    )
    for u in range(2):
        row = jnp.broadcast_to(bias[:, u * outs : (u + 1) * outs], (16, outs)).astype(bf16)
        for j in range(keep_ref.shape[0]):
            spot = slice(u * (9 * size + 16) + 9 * size, (u + 1) * (9 * size + 16))
            keep_ref[j, spot, :] = row
            give_ref[j, spot, :] = row
    if flat:
        first = 2 * (9 * size + 16)
        flat_pieces(1.0, idx_ref, full_ref, go_ref, bias_ref, keep_ref, give_ref, first)


def weight_grad(side, half, idx, grad, act, act_other, chips, flat=()):
    spots = half + side
    wide = grad.shape[1]
    outs = wide // 2
    depth = 2 * act.shape[1]
    rows = 2 * (9 * depth // (2 * chips) + 16)
    if flat:
        rows += flat_size(flat[0], flat[1], chips)
    return call(
        functools.partial(weight_body, side, half, bool(flat)),
        "weight_grad",
        [(SMEM, idx), (LOAD, grad)] + [(LOAD, a) for a in flat] + [(FAR, act), (FAR, act_other)],
        [(VMEM, struct((chips, rows, outs), bf16))] * 2,
        [
            pltpu.VMEM((spots, depth), bf16),
            pltpu.VMEM((spots + 2 * side, 3 * wide), bf16),
            pltpu.SemaphoreType.DMA((4,)),
        ],
        spare=10,
    )


def weight_one_body(side, arrive, idx_ref, mine_ref, theirs_ref, x_ref, *refs):
    keep_ref, give_ref, gp_ref, taps_ref = refs
    arrive()
    zh = idx_ref[2]
    half, outs = mine_ref.shape
    gp_ref[at(zh * half, half, side), :] = mine_ref[...]
    gp_ref[at((1 - zh) * half, half, side), :] = theirs_ref[...]
    grad = gp_ref[...]
    bias = jnp.sum(grad.astype(f32), axis=0, keepdims=True)
    spread_taps(side, grad, taps_ref)
    blocks = 2 * keep_ref.shape[0]
    spots, depth = x_ref.shape
    size = depth // blocks
    right = tap_block(side, taps_ref, 0, spots)
    for begin in range(0, depth, 256):
        part = dot(x_ref[:, begin : begin + 256], right, TN)
        for tap in range(9):
            put_blocks(
                idx_ref, keep_ref, give_ref, part[:, tap * outs : (tap + 1) * outs],
                tap, begin // size, size,
            )
    row = jnp.broadcast_to(bias, (16, outs)).astype(bf16)
    first = 9 * size + 16
    for j in range(keep_ref.shape[0]):
        keep_ref[j, 9 * size : first, :] = row
        give_ref[j, 9 * size : first, :] = row


def weight_one_grad(side, idx, mine, theirs, act_zero, chips):
    spots, depth = act_zero.shape
    outs = mine.shape[1]
    rows = 9 * depth // (2 * chips) + 16
    return call(
        functools.partial(weight_one_body, side),
        "weight_one_grad",
        [(SMEM, idx), (LOAD, mine), (LOAD, theirs), (LOAD, act_zero)],
        [(VMEM, struct((chips, rows, outs), bf16))] * 2,
        [
            pltpu.VMEM((spots, outs), bf16),
            pltpu.VMEM((spots + 2 * side, 3 * outs), bf16),
        ],
        spare=14,
    )


def fold_body(pairs, arrive, idx_ref, *refs):
    arrive()
    ins, (keep_ref, give_ref) = refs[: 2 * pairs], refs[2 * pairs :]
    half = keep_ref.shape[0]
    for i in range(2 * half):
        target = keep_ref if i < half else give_ref
        begin = 0
        for keep, recv in zip(ins[0::2], ins[1::2]):
            rows = keep.shape[1]
            total = keep[i].astype(f32) + recv[i].astype(f32)
            target[i % half, begin : begin + rows, :] = total.astype(bf16)
            begin += rows


def fold(idx, *arrays):
    blocks, _, wide = arrays[0].shape
    rows = sum(a.shape[1] for a in arrays[0::2])
    return call(
        functools.partial(fold_body, len(arrays) // 2),
        "fold",
        [(SMEM, idx)] + [(VMEM, a) for a in arrays],
        [(VMEM, struct((blocks // 2, rows, wide), bf16))] * 2,
    )


def last_body(slotted, rest, arrive, idx_ref, keep_in, recv_in, *targets):
    arrive()
    zh = idx_ref[2]

    def put(target, place, begin, rows):
        spot = at(begin, rows, 16)
        total = keep_in[0, spot, :].astype(f32) + recv_in[0, spot, :].astype(f32)
        target[place : place + rows, :] = total.astype(bf16)

    place = 0
    for begin, rows in slotted:
        put(targets[0], place, begin + zh * rows, rows)
        put(targets[1], place, begin + (1 - zh) * rows, rows)
        place += rows
    begin, rows = rest
    put(targets[-1], 0, begin, rows)


def last_fold(idx, keep, recv, slotted=(), rest=None):
    wide = keep.shape[2]
    rest = rest or (0, keep.shape[1])
    rows = sum(size for _, size in slotted)
    sizes = ([rows, rows] if slotted else []) + [rest[1]]
    return call(
        functools.partial(last_body, slotted, rest),
        "last_fold",
        [(SMEM, idx), (VMEM, keep), (VMEM, recv)],
        [(VMEM, struct((size, wide), bf16)) for size in sizes],
    )


def final_body(parts, arrive, idx_ref, own_ref, sib_ref, *refs):
    arrive()
    outs, stages, sems = refs[: 2 * len(parts)], refs[2 * len(parts) : -1], refs[-1]
    chip, core = idx_ref[0], idx_ref[1]
    chips, _, wide = own_ref.shape
    first = 0
    copies = []

    def store(source, target):
        copies.append(pltpu.make_async_copy(source, target, sems.at[len(copies)]))
        copies[-1].start()

    for n, part in enumerate(parts):
        grad_ref, bias_ref, stage = outs[2 * n], outs[2 * n + 1], stages[n]
        size = part[0] // (2 * chips)
        columns = 1 if len(part) == 1 else part[1] // wide
        end = first + size * (9 if len(part) == 1 else columns)
        for c in range(columns):
            row = own_ref[0, end + c : end + c + 1, :].astype(f32)
            bias_ref[:, c * wide : (c + 1) * wide] = row
        for n_row, begin in enumerate(range(first, end, size)):
            for j in range(chips):
                for source, owner in ((own_ref, core), (sib_ref, 1 - core)):
                    home = chip ^ mask_of(j, owner, chips)
                    spot = at((2 * home + owner) * size, size, size)
                    piece = source[j, begin : begin + size, :].astype(f32)
                    if len(part) == 1:
                        stage[n_row, spot, :] = piece
                    else:
                        stage[spot, n_row * wide : (n_row + 1) * wide] = piece
            if len(part) == 1:
                store(stage.at[n_row], grad_ref.at[n_row])
        if len(part) > 1:
            store(stage, grad_ref)
        first = end + 16
    for copy in copies:
        copy.wait()


def final_grads(idx, own, sib, parts):
    wide = own.shape[2]
    results, stages = [], []
    for part in parts:
        shape = (9, part[0], wide) if len(part) == 1 else part
        results += [(FAR, struct(shape, f32)), (VMEM, struct((1, shape[-1]), f32))]
        stages.append(pltpu.VMEM(shape, f32))
    copies = sum(9 if len(part) == 1 else 1 for part in parts)
    return call(
        functools.partial(final_body, parts),
        "final_grads",
        [(SMEM, idx), (VMEM, own), (VMEM, sib)],
        results,
        stages + [pltpu.SemaphoreType.DMA((copies,))],
    )


def flat_pieces(gain, idx_ref, x_ref, go_ref, bias_ref, keep_ref, give_ref, first):
    chip, core = idx_ref[0], idx_ref[1]
    chips, _, wide = keep_ref.shape
    columns = go_ref.shape[1] // wide
    size = x_ref.shape[1] // (2 * chips)
    bias = jnp.concatenate(
        [bias_ref[:, c * wide : (c + 1) * wide] for c in range(columns)]
        + [jnp.zeros((16 - columns, wide), f32)],
        axis=0,
    ).astype(bf16)
    for j in range(chips):
        keep_ref[j, first + columns * size :, :] = bias
        give_ref[j, first + columns * size :, :] = bias
    for begin in range(0, x_ref.shape[1], 256):
        part = gain * dot(x_ref[:, begin : begin + 256], go_ref[...], TN)
        for b in range(0, 256 // size, 2):
            mask = chip ^ ((begin // size + b) // 2)
            slot = slot_of(mask, core, chips)
            give_slot = slot_of(mask, 1 - core, chips)
            for c in range(columns):
                even = part[b * size : (b + 1) * size, c * wide : (c + 1) * wide]
                odd = part[(b + 1) * size : (b + 2) * size, c * wide : (c + 1) * wide]
                spot = slice(first + c * size, first + (c + 1) * size)
                keep_ref[slot, spot, :] = jnp.where(core == 0, even, odd).astype(bf16)
                give_ref[give_slot, spot, :] = jnp.where(core == 0, odd, even).astype(bf16)


def flat_size(x, go, chips):
    return (go.shape[1] // 128) * (x.shape[1] // (2 * chips)) + 16


def outer_body(gain, arrive, idx_ref, x_ref, go_ref, bias_ref, keep_ref, give_ref):
    arrive()
    flat_pieces(gain, idx_ref, x_ref, go_ref, bias_ref, keep_ref, give_ref, 0)


def outer(idx, x, go, gain, bias, chips):
    return call(
        functools.partial(outer_body, gain),
        "outer",
        [(SMEM, idx), (LOAD, x), (LOAD, go), (LOAD, bias)],
        [(VMEM, struct((chips, flat_size(x, go, chips), 128), bf16))] * 2,
        spare=8,
    )


def start_body(arrive, idx_ref, valid_ref, cot_ref, outk_ref, go_ref, bias_ref, own_ref, give_ref):
    arrive()
    zl = idx_ref[3]
    masked = cot_ref[...].astype(f32) * valid_ref[0]
    go_ref[...] = masked.astype(bf16)
    bias_ref[...] = jnp.sum(masked, axis=0, keepdims=True)
    chans = outk_ref.shape[0] // 4
    block = cot_ref.shape[0] // 4
    for target, along in ((give_ref, 1 - zl), (own_ref, zl)):
        weights = jnp.concatenate(
            [outk_ref[at((2 * up + along) * chans, chans, chans), :] for up in range(2)], axis=0
        )
        for begin in range(0, cot_ref.shape[0], block):
            part = post_gain * dot(go_ref[begin : begin + block, :], weights, NT)
            target[begin : begin + block, :] = part.astype(target.dtype)


def start_back(idx, valid, cot, outk):
    spots, outs = cot.shape
    half = outk.shape[0] // 2
    return call(
        start_body,
        "start_back",
        [(SMEM, idx), (SMEM, valid), (LOAD, cot), (LOAD, outk)],
        [
            (VMEM, struct(cot.shape, bf16)),
            (VMEM, struct((1, outs), f32)),
            (VMEM, struct((spots, half), f32)),
            (VMEM, struct((spots, half), bf16)),
        ],
    )


def rows_body(side, arrive, idx_ref, own_ref, recv_ref, keep_ref, give_ref):
    arrive()
    zh = idx_ref[2]
    spots = keep_ref.shape[0]
    apart = own_ref.shape[0] - spots
    for target, begin in ((give_ref, (1 - zh) * apart), (keep_ref, zh * apart)):
        spot = at(begin, spots, side)
        total = own_ref[spot, :] + recv_ref[spot, :].astype(f32)
        target[...] = total.astype(target.dtype)


def rows_sum(side, idx, own, recv, spots):
    shape = (spots, own.shape[1])
    return call(
        functools.partial(rows_body, side),
        "rows_sum",
        [(SMEM, idx), (LOAD, own), (LOAD, recv)],
        [(VMEM, struct(shape, f32)), (VMEM, struct(shape, bf16))],
    )


def slots_body(arrive, idx_ref, own_ref, recv_ref, keep_ref, give_ref):
    arrive()
    zh = idx_ref[2]
    for target, slot in ((give_ref, 1 - zh), (keep_ref, zh)):
        total = own_ref[slot] + recv_ref[slot].astype(f32)
        target[...] = total.astype(bf16)


def slots_sum(idx, own, recv):
    shape = struct(own.shape[1:], bf16)
    return call(
        slots_body,
        "slots_sum",
        [(SMEM, idx), (VMEM, own), (VMEM, recv)],
        [(VMEM, shape), (VMEM, shape)],
    )


def input_body(arrive, idx_ref, keep_ref, recv_ref, out_ref):
    arrive()
    zh = idx_ref[2]
    half = keep_ref.shape[0]
    out_ref[at(zh * half, half, half), :] = keep_ref[...]
    out_ref[at((1 - zh) * half, half, half), :] = recv_ref[...]


def input_grad(idx, keep, recv):
    half, chans = keep.shape
    return call(
        input_body,
        "input_grad",
        [(SMEM, idx), (VMEM, keep), (VMEM, recv)],
        [(VMEM, struct((2 * half, chans), bf16))],
    )


def whole_body(side, arrive, idx_ref, xl, xa, xh, xd, rh, rl, x_ref, act_ref, sems):
    arrive()
    zh, zl = idx_ref[2], idx_ref[3]
    chans = xl.shape[1]
    spots = xa.shape[0]
    rest = xl.shape[0] - spots
    window, outside = at(zh * rest, spots, side), at((1 - zh) * spots, rest, side)

    def cols(up, along):
        return at((2 * up + along) * chans, chans, chans)

    run_copies(
        [
            (xl, x_ref.at[:, cols(zh, zl)]),
            (xa, x_ref.at[window, cols(zh, 1 - zl)]),
            (xh, x_ref.at[window, cols(1 - zh, zl)]),
            (xd, x_ref.at[window, cols(1 - zh, 1 - zl)]),
            (rl.at[0], x_ref.at[outside, cols(zh, 1 - zl)]),
            (rh, x_ref.at[outside, cols(1 - zh, zl)]),
            (rl.at[1], x_ref.at[outside, cols(1 - zh, 1 - zl)]),
        ],
        sems,
    )
    block = x_ref.shape[0] // 8
    for begin in range(0, x_ref.shape[0], block):
        rows = slice(begin, begin + block)
        act_ref[rows, :] = gelu(x_ref[rows, :].astype(f32)).astype(bf16)


def whole_input(side, idx, *parts):
    spots, chans = parts[0].shape
    return call(
        functools.partial(whole_body, side),
        "whole_input",
        [(SMEM, idx)] + [(FAR, p) for p in parts],
        [(VMEM, struct((spots, 4 * chans), bf16))] * 2,
        [pltpu.SemaphoreType.DMA((7,))],
    )


def join_body(arrive, idx_ref, own, recv, far_own, far_recv, out, sems):
    arrive()
    zh, zl = idx_ref[2], idx_ref[3]
    half = own.shape[0]
    chans = own.shape[1] // 2
    pairs = []
    for source, up, along in ((own, zh, zl), (recv, zh, 1 - zl), (far_own, 1 - zh, zl), (far_recv, 1 - zh, 1 - zl)):
        for slot in range(2):
            spot = at((2 * slot + along) * chans, chans, chans)
            target = out.at[at(up * half, half, half), spot]
            pairs.append((source.at[:, slot * chans : (slot + 1) * chans], target))
    run_copies(pairs, sems)


def join(idx, *parts):
    half, wide = parts[0].shape
    return call(
        join_body,
        "join",
        [(SMEM, idx)] + [(FAR, p) for p in parts],
        [(VMEM, struct((2 * half, 2 * wide), bf16))],
        [pltpu.SemaphoreType.DMA((8,))],
    )


def finish_body(arrive, idx_ref, valid_ref, x_ref, act_ref, idk_ref, outk_ref, ib_ref, out_ref):
    arrive()
    block = x_ref.shape[0] // 4
    for begin in range(0, x_ref.shape[0], block):
        rows = slice(begin, begin + block)
        identity = dot(x_ref[rows, :], idk_ref[...]) + ib_ref[...]
        branch = dot(act_ref[rows, :], outk_ref[...])
        out_ref[rows, :] = ((identity + post_gain * branch) * valid_ref[0]).astype(bf16)


def finish(idx, valid, x, act, idk, outk, ib):
    outs = idk.shape[1]
    return call(
        finish_body,
        "finish",
        [(SMEM, idx), (SMEM, valid), (LOAD, x), (LOAD, act), (LOAD, idk), (LOAD, outk)]
        + [(VMEM, ib.reshape(1, outs))],
        [(VMEM, struct((x.shape[0], outs), bf16))],
        spare=8,
    )


def flip(value, axis):
    return lax.ppermute(value, axis, [(0, 1), (1, 0)])


def cross(value, step, chips):
    pairs = []
    for chip in range(chips):
        for core in range(2):
            other = chip ^ step_bits(core, chips)[step]
            pairs.append((2 * chip + core, 2 * other + core))
    return lax.ppermute(value, DP, pairs)


def hops(value, chips):
    blocks = [value]
    for i in range(1, chips):
        pairs = []
        for chip in range(chips):
            for core in range(2):
                bits = step_bits(core, chips)
                mask = sum(bit for n, bit in enumerate(bits) if i >> (len(bits) - 1 - n) & 1)
                pairs.append((2 * (chip ^ mask) + core, 2 * chip + core))
        blocks.append(lax.ppermute(value, DP, pairs))
    return blocks


def swap(pieces, axis):
    return lax.all_to_all(pieces, axis, split_axis=0, concat_axis=0, tiled=True)


def after(value, other):
    return lax.optimization_barrier((value, other))[0]


def rows_of(value, start, size):
    return lax.dynamic_slice_in_dim(value, start, size, 0)


def local(
    pixels,
    counts,
    kernel_one,
    bias_one,
    kernel_two,
    bias_two,
    kernel_three,
    bias_three,
    out_kernel,
    identity_kernel,
    identity_bias,
    cotangent,
):
    images, rows, width, chans = pixels.shape
    side = width // 2
    spots = side * side
    half = spots // 2
    window = half + halo * side
    outs = cotangent.shape[3]
    chips = lax.axis_size("chip")
    chip, core, zh, zl = [lax.axis_index(a) for a in ("chip", "core", "zh", "zl")]
    idx = jnp.stack([chip, core, zh, zl]).astype(jnp.int32)
    taps = lambda kernel: kernel.reshape((9,) + kernel.shape[2:])
    one, two, three = taps(kernel_one), taps(kernel_two), taps(kernel_three)

    own_count = lax.dynamic_index_in_dim(counts, 2 * chip + core, 0, keepdims=True)
    valid = (own_count > 0).astype(f32)

    place = 2 * chip + core

    def units_of(kernel, size):
        if kernel.ndim == 3:
            block = kernel.shape[1] // (2 * chips)
            return lax.dynamic_slice_in_dim(kernel, place * block, block, 1)
        block = kernel.shape[0] // (2 * chips)
        block = lax.dynamic_slice_in_dim(kernel, place * block, block, 0)
        block = block.reshape(-1, size, block.shape[1] // 128, 128)
        return block.transpose(2, 0, 1, 3).reshape(-1, size, 128)

    steps = chips.bit_length() - 1

    def start_spread(piece, *others):
        return jnp.concatenate(after((piece[None], cross(piece[None], steps - 1, chips)), others))

    def end_spread(own, *others):
        for step in reversed(range(steps - 1)):
            own = jnp.concatenate(after((own, cross(own, step, chips)), others))
        return own, flip(own, "core")

    last = [idx]

    def turn(*others):
        return after(idx, (last[0],) + others)

    def ran(results):
        last[0] = results[-1] if isinstance(results, (list, tuple)) else results
        return results

    size = two.shape[1] // (2 * chips)
    deep = two.shape[1]
    cot = cotangent.reshape(spots, outs)
    one_piece = flip(units_of(one, size), "zh")
    pooled = ran(pool(pixels))
    go, identity_bias_grad, ga_own, ga_give = ran(start_back(turn(), valid, cot, out_kernel))
    bias_other = flip(after(jnp.stack([bias_one, bias_two, bias_three]), go), "zh")
    two_piece = units_of(after(two, pooled), size)
    last_piece = jnp.concatenate([units_of(after(k, pooled), size) for k in (three, identity_kernel)])
    cot_rows = rows_of(after(cot, pooled), (1 - zh) * half, half)
    xl = swap(after(pooled, (one_piece, two_piece, last_piece, cot_rows, ga_give)), DP)
    xl = xl.reshape(spots, chans)
    two_piece = flip(after(two_piece, one_piece), "zh")

    apart = spots - window
    xa = flip(rows_of(xl, zh * apart, window), "zl")
    xh = flip(rows_of(xl, (1 - zh) * apart, window), "zh")
    rest = spots - window
    rest_own = rows_of(xl, (1 - zh) * window, rest)
    rest_high = rows_of(xl, zh * window, rest)
    two_near = start_spread(after(two_piece, xl))
    one_near = start_spread(after(one_piece, xl), xh, xa, two_near, bias_other)
    xd = flip(xh, "zl")
    last_piece = flip(after(last_piece, xh), "zh")
    two_other = end_spread(two_near, xd)
    one_other = end_spread(one_near, xd, two_other[0], last_piece)
    ga_recv = flip(after(ga_give, xd), "zl")
    rest_high = flip(after(rest_high, xd), "zh")

    pre_one, act_one = ran(
        conv(
            side, turn(), (xl, xa, xh, xd), one, one_other, 0, bias_one, bias_other[0], True
        )
    )
    act_one_other = flip(act_one, "zl")
    ga_own, ga_give = ran(rows_sum(side, turn(), ga_own, ga_recv, half + (halo - 3) * side))
    pre_two, act_two = ran(
        conv(side, turn(), (act_one, act_one_other), two, two_other, 0, bias_two, bias_other[1])
    )
    act_two_other = flip(act_two, "zl")
    ga_recv = flip(after(ga_give, act_two), "zh")
    last_other = jnp.stack(after(hops(after(last_piece, act_one), chips), act_two))
    last_other = last_other, flip(last_other, "core")
    pre_three, act_three = ran(
        conv(side, turn(), (act_two, act_two_other), three, last_other, 0, bias_three, bias_other[2])
    )
    rest_low = flip(jnp.stack(after((rest_own, rest_high), act_three)), "zl")
    cot_far = flip(after(cot_rows, act_three), "zh")
    own_rows = rows_of(act_three, zh * (halo - 3) * side, half)

    gp_three, ga_own, ga_give = ran(
        back(side, turn(), (ga_own, ga_recv, pre_three), three, last_other, 0)
    )
    ga_recv = flip(ga_give, "zl")
    full_x, act_zero = ran(whole_input(side, turn(), xl, xa, xh, xd, rest_high, rest_low))
    keep_three, give_three = ran(
        weight_grad(
            side, half, turn(), gp_three, act_two, act_two_other, chips, (full_x, go, identity_bias_grad)
        )
    )
    gp_two, ga_own, ga_give = ran(
        back(side, turn(), (ga_own, ga_recv, pre_two), two, two_other, 0)
    )
    ga_recv = flip(ga_give, "zl")
    keep_two, give_two = ran(weight_grad(side, half, turn(cot_far), gp_two, act_one, act_one_other, chips))

    gp_mine, gp_theirs, gp_one = ran(slope_back(side, turn(), ga_own, ga_recv, pre_one, half))
    gp_theirs = flip(gp_theirs, "zh")
    recv_three = flip(after(give_three, gp_one), "core")
    recv_two = flip(after(give_two, gp_one), "core")
    gx_own, gx_give = ran(
        back(
            side, turn(), (gp_one,), one, one_other, 0,
            (valid, full_x, go, cot_far, identity_kernel, last_other, half),
        )
    )

    def folds(keep, recv, first, *others):
        for step in range(first, steps):
            keep, give = ran(fold(turn(*others), keep, recv))
            recv = cross(give, step, chips)
        return keep, recv

    keep_deep, give_deep = ran(fold(turn(gp_theirs), keep_three, recv_three, keep_two, recv_two))
    recv_deep = cross(give_deep, 0, chips)
    gx_recv = flip(after(gx_give, keep_deep), "zl")
    own_rows = after(own_rows, keep_deep)
    near_rows = flip(own_rows, "zl")
    far_rows = flip(own_rows, "zh")
    keep_one, give_one = ran(weight_one_grad(side, turn(), gp_mine, gp_theirs, act_zero, chips))
    recv_one = flip(give_one, "core")
    keep_deep, recv_deep = folds(keep_deep, recv_deep, 1, far_rows)
    gx_keep, gx_give = ran(slots_sum(turn(), gx_own, gx_recv))
    gx_recv = flip(gx_give, "zh")
    keep_one, give_one = ran(fold(turn(), keep_one, recv_one))
    recv_one = cross(give_one, 0, chips)
    slot = 9 * size + 16
    flat = keep_three.shape[1] - 2 * slot
    keep_deep, give_deep, id_rows = ran(
        last_fold(
            turn(), keep_deep, recv_deep, ((0, slot), (2 * slot + flat, slot)), (2 * slot, flat)
        )
    )
    recv_deep = flip(give_deep, "zh")
    far_near_rows = flip(after(far_rows, keep_deep), "zl")
    keep_one, recv_one = folds(keep_one, recv_one, 1)
    gx = ran(input_grad(turn(), gx_keep, gx_recv))
    full_three = ran(join(turn(), own_rows, near_rows, far_rows, far_near_rows))
    keep_out, give_out = ran(outer(turn(), full_three, go, post_gain, identity_bias_grad, chips))
    recv_out = flip(give_out, "core")
    (total_one,) = ran([last_fold(turn(), keep_one, recv_one)])
    keep_out, give_out = ran(fold(turn(), keep_out, recv_out))
    recv_out = cross(give_out, 0, chips)
    deep_rows = (after(keep_deep, keep_out).astype(f32) + recv_deep.astype(f32)).astype(bf16)
    deep_rows = jnp.concatenate([deep_rows, id_rows])
    near_deep = start_spread(deep_rows)
    gx = after(gx, deep_rows)
    gx = swap(gx.reshape(images, rows * width // 4, chans), DP)
    block_out = ran(
        finish(turn(deep_rows), valid, full_x, full_three, identity_kernel, out_kernel, identity_bias)
    )
    keep_out, recv_out = folds(keep_out, recv_out, 1)
    pixels_grad = ran(widen(turn(), gx, rows, width))
    (total_out,) = ran([last_fold(turn(), keep_out, recv_out)])
    near_one = start_spread(jnp.concatenate([total_one, total_out]))
    all_deep = end_spread(near_deep)
    all_one = end_spread(near_one)
    (
        kernel_three_grad,
        bias_three_grad,
        kernel_two_grad,
        bias_two_grad,
        identity_kernel_grad,
        identity_bias_grad,
    ) = ran(final_grads(turn(), *all_deep, ((deep,), (deep,), identity_kernel.shape)))
    kernel_one_grad, bias_one_grad, out_kernel_grad, _ = ran(
        final_grads(turn(), *all_one, ((one.shape[1],), out_kernel.shape))
    )

    return (
        block_out.reshape(cotangent.shape),
        pixels_grad,
        kernel_one_grad.reshape(kernel_one.shape),
        bias_one_grad[0],
        kernel_two_grad.reshape(kernel_two.shape),
        bias_two_grad[0],
        kernel_three_grad.reshape(kernel_three.shape),
        bias_three_grad[0],
        out_kernel_grad,
        identity_kernel_grad,
        identity_bias_grad[0],
    )


def solution(mesh):
    members = mesh.devices.size // mesh.shape["mp"]
    fine = Mesh(
        mesh.devices.reshape(members // 2, 2, 2, mesh.shape["mp"] // 2),
        ("chip", "core", "zh", "zl"),
    )
    return jax.shard_map(
        local,
        mesh=fine,
        in_specs=(
            P(None, DP, None, MP),
            P(),
            P(None, None, None, MP),
            P(MP),
            P(None, None, None, MP),
            P(MP),
            P(None, None, None, MP),
            P(MP),
            P(None, MP),
            P(None, MP),
            P(MP),
            P(DP, None, None, MP),
        ),
        out_specs=(
            P(DP, None, None, MP),
            P(None, DP, None, MP),
            P(None, None, None, MP),
            P(MP),
            P(None, None, None, MP),
            P(MP),
            P(None, None, None, MP),
            P(MP),
            P(None, MP),
            P(None, MP),
            P(MP),
        ),
        check_vma=False,
    )
```

```python
import functools
import math

import jax
import jax.numpy as jnp
from jax import lax
from jax.experimental import pallas as pl
from jax.experimental.pallas import tpu as pltpu
from jax.sharding import Mesh
from jax.sharding import PartitionSpec as P


post_gain = 0.015625
slope = 0.7978845608028654
cubic = 0.044715
halo = 6
bf16 = jnp.bfloat16
f32 = jnp.float32
NT = (((1,), (1,)), ((), ()))
TN = (((0,), (0,)), ((), ()))
NN = (((1,), (0,)), ((), ()))
DP = ("chip", "core")
MP = ("zh", "zl")


def dot(left, right, dims=NN):
    return lax.dot_general(left, right, dims, preferred_element_type=f32)


def gelu(value):
    inner = jnp.tanh(slope * (value + cubic * value * value * value))
    return 0.5 * value * (1.0 + inner)


def gelu_slope(value):
    square = value * value
    inner = jnp.tanh(slope * value * (1.0 + cubic * square))
    climb = slope * (1.0 + 3.0 * cubic * square)
    return 0.5 * (1.0 + inner) + 0.5 * value * (1.0 - inner * inner) * climb


def struct(shape, kind):
    return jax.ShapeDtypeStruct(shape, kind)


def lanes(blocks):
    return blocks[0] if len(blocks) == 1 else jnp.concatenate(blocks, axis=1)


def step_bits(core, chips):
    bits = [1 << n for n in range(chips.bit_length() - 1)]
    for n in range(0, len(bits) - 1, 2) if core else ():
        bits[n], bits[n + 1] = bits[n + 1], bits[n]
    return bits


def mask_of(i, core, chips):
    masks = []
    for which in range(2):
        bits = step_bits(which, chips)
        masks.append(sum(bit for n, bit in enumerate(bits) if i >> (len(bits) - 1 - n) & 1))
    return jnp.where(core == 0, masks[0], masks[1])


def slot_of(mask, core, chips):
    slots = []
    for which in range(2):
        bits = step_bits(which, chips)
        slot = 0
        for n, bit in enumerate(bits):
            slot = slot + ((mask >> (bit.bit_length() - 1)) & 1) * (1 << (len(bits) - 1 - n))
        slots.append(slot)
    return jnp.where(core == 0, slots[0], slots[1])


VMEM = pl.BlockSpec(memory_space=pltpu.VMEM)
SMEM = pl.BlockSpec(memory_space=pltpu.SMEM)
FAR = pl.BlockSpec(memory_space=pl.ANY)
LOAD = "load"


def size_of(array):
    return math.prod(array.shape) * jnp.dtype(array.dtype).itemsize


def call(body, name, ins, outs, scratch=(), spare=6, **more):
    loads = [i for i, (space, _) in enumerate(ins) if space is LOAD]
    spaces = [FAR if space is LOAD else space for space, _ in ins]
    arrays = [array for _, array in ins]
    out_specs = [space for space, _ in outs]
    out_shape = [shape for _, shape in outs]
    held = [arrays[i] for i in loads]
    buffers = [pltpu.VMEM(array.shape, array.dtype) for array in held]
    sems = [pltpu.SemaphoreType.DMA((len(held),))] if held else []
    vmem = sum(size_of(array) for array in held)
    vmem += sum(size_of(a) for space, a in list(ins) + list(outs) if space is VMEM)
    vmem += sum(size_of(b) for b in scratch if b.memory_space == pltpu.VMEM)
    moved = sum(size_of(a) for a in arrays + out_shape)

    def wrapped(*refs):
        inputs = list(refs[: len(ins)])
        outputs = refs[len(ins) : len(ins) + len(outs)]
        rest = refs[len(ins) + len(outs) :]
        kept, tail = rest[: len(held)], rest[len(held) :]
        copies = []
        if held:
            sem, tail = tail[0], tail[1:]
            copies = [
                pltpu.make_async_copy(inputs[i], kept[n], sem.at[n]) for n, i in enumerate(loads)
            ]
        for copy in copies:
            copy.start()
        for n, i in enumerate(loads):
            inputs[i] = kept[n]

        def arrive():
            for copy in copies:
                copy.wait()

        body(arrive, *inputs, *outputs, *tail)

    single = len(outs) == 1
    return pl.pallas_call(
        wrapped,
        in_specs=spaces,
        out_specs=out_specs[0] if single else out_specs,
        out_shape=out_shape[0] if single else out_shape,
        scratch_shapes=buffers + sems + list(scratch),
        compiler_params=pltpu.CompilerParams(vmem_limit_bytes=vmem + (spare << 20)),
        cost_estimate=pl.CostEstimate(flops=0, bytes_accessed=moved, transcendentals=0),
        name=name,
        **more,
    )(*arrays)


def run_copies(pairs, sems):
    for copy in start_copies(pairs, sems):
        copy.wait()


def slice_copies(group, idx_ref, own, blocks, sibling, wbuf):
    chip, core, zh = idx_ref[0], idx_ref[1], idx_ref[2]
    size = blocks.shape[-2]
    pairs = [(own, wbuf.at[zh])]
    for j in range(blocks.shape[0]):
        for source, owner in ((blocks, core), (sibling, 1 - core)):
            home = chip ^ mask_of(j, owner, blocks.shape[0])
            spot = at((2 * home + owner) * size, size, size)
            pairs.append((source.at[j, 9 * group : 9 * group + 9], wbuf.at[1 - zh, :, spot, :]))
    return pairs


def flat_copies(first, idx_ref, blocks, sibling, buffer):
    chip, core = idx_ref[0], idx_ref[1]
    columns, units = buffer.shape[:2]
    chips = blocks.shape[0]
    count = units // (2 * chips)
    pairs = []
    for j in range(chips):
        for source, owner in ((blocks, core), (sibling, 1 - core)):
            home = chip ^ mask_of(j, owner, chips)
            spot = pl.ds((2 * home + owner) * count, count)
            for c in range(columns):
                begin = first + c * count
                pairs.append((source.at[j, begin : begin + count], buffer.at[c, spot]))
    return pairs


def start_copies(pairs, sems):
    copies = [pltpu.make_async_copy(a, b, sems.at[i]) for i, (a, b) in enumerate(pairs)]
    for copy in copies:
        copy.start()
    return copies


def flat_rows(buffer, begin, count):
    columns, _, size, wide = buffer.shape
    return lanes([buffer[c, pl.ds(begin, count)].reshape(count * size, wide) for c in range(columns)])


def halves(spots, side):
    first = (spots // side + 1) // 2 * side
    return ((0, first), (first, spots - first))


def columns_of(size, wide, side):
    return lax.rem(lax.broadcasted_iota(jnp.int32, (size, wide), 0), side)


def at(start, size, unit):
    return pl.ds(pl.multiple_of(start, unit), size)


def pool_body(arrive, x_ref, out_ref):
    arrive()
    rows, width, chans = x_ref.shape[1:]
    half = width // 2
    pixel = lax.broadcasted_iota(jnp.int32, (half, 2 * width), 1)
    place = lax.broadcasted_iota(jnp.int32, (half, 2 * width), 0)
    inside = (lax.rem(pixel, width) >= 2 * place) & (lax.rem(pixel, width) < 2 * place + 2)
    pick = jnp.where(inside, 0.25, 0.0).astype(bf16)
    for image in range(x_ref.shape[0]):
        for row in range(rows // 2):
            window = x_ref[image, 2 * row : 2 * row + 2].reshape(2 * width, chans)
            out_ref[image, row * half : (row + 1) * half, :] = dot(pick, window).astype(bf16)


def pool(pixels):
    images, rows, width, chans = pixels.shape
    shape = struct((images, rows * width // 4, chans), bf16)
    return call(pool_body, "pool", [(LOAD, pixels)], [(VMEM, shape)])


def widen_body(arrive, idx_ref, g_ref, out_ref):
    arrive()
    rows, width, chans = out_ref.shape[1:]
    half = width // 2
    pixel = lax.broadcasted_iota(jnp.int32, (width, half), 0)
    place = lax.broadcasted_iota(jnp.int32, (width, half), 1)
    inside = (pixel >= 2 * place) & (pixel < 2 * place + 2)
    pick = jnp.where(inside, 0.25, 0.0).astype(bf16)
    for image in range(g_ref.shape[0]):
        for row in range(rows // 2):
            wide = dot(pick, g_ref[image, row * half : (row + 1) * half, :]).astype(bf16)
            out_ref[image, 2 * row] = wide
            out_ref[image, 2 * row + 1] = wide


def widen(idx, grad, rows, width):
    images, spots, chans = grad.shape
    step = images // 4
    block = pl.BlockSpec((step, spots, chans), lambda i: (i, 0, 0))
    out = pl.BlockSpec((step, rows, width, chans), lambda i: (i, 0, 0, 0))
    return call(
        widen_body,
        "widen",
        [(SMEM, idx), (block, grad)],
        [(out, struct((images, rows, width, chans), bf16))],
        grid=(4,),
    )


def conv_body(side, first, group, arrive, idx_ref, *refs):
    zh, zl = idx_ref[2], idx_ref[3]
    if first:
        xl, xa, xh, xd, wl, wo, ws, bl, bo, pre_ref, act_ref, xbuf, wbuf, acc, sems = refs
        chans = xl.shape[1]
        spots = xbuf.shape[0]
        begin = zh * (xl.shape[0] - spots)
        pairs = []
        for source, up, along in ((xl, zh, zl), (xa, zh, 1 - zl), (xh, 1 - zh, zl), (xd, 1 - zh, 1 - zl)):
            if source is xl:
                source = xl.at[at(begin, spots, side), :]
            pairs.append((source, xbuf.at[:, at((2 * up + along) * chans, chans, chans)]))
    else:
        xl, xa, wl, wo, ws, bl, bo, pre_ref, act_ref, xbuf, wbuf, acc, sems = refs
        chans = xl.shape[1] // 2
        spots = xbuf.shape[0]
        pairs = []
        for source, along in ((xl, zl), (xa, 1 - zl)):
            for up in range(2):
                pairs.append(
                    (
                        source.at[:, up * chans : (up + 1) * chans],
                        xbuf.at[:, at((2 * up + along) * chans, chans, chans)],
                    )
                )
    run_copies(slice_copies(group, idx_ref, wl, wo, ws, wbuf) + pairs, sems)
    arrive()
    acc[...] = jnp.zeros_like(acc)
    outs = 2 * wl.shape[2]
    for x in range(3):
        weights = lanes([wbuf[u, 3 * y + x] for y in range(3) for u in range(2)])
        for begin, block in halves(spots, side):
            values = xbuf[begin : begin + block, :]
            if first:
                values = gelu(values.astype(f32)).astype(bf16)
            product = dot(values, weights)
            for y in range(3):
                place = begin + side * (2 - y)
                acc[x, place : place + block, :] += product[:, y * outs : (y + 1) * outs]
    own, other = bl[...], bo[...]
    bias = lanes([jnp.where(zh == 0, own, other), jnp.where(zh == 0, other, own)])
    for begin, block in halves(act_ref.shape[0], side):
        column = columns_of(block, outs, side)
        spot = at(begin + side + zh * side, block, side)
        left = pltpu.roll(acc[0, spot, :], 1, 0)
        right = pltpu.roll(acc[2, spot, :], block - 1, 0)
        pre = acc[1, spot, :] + bias
        pre = pre + jnp.where(column > 0, left, 0.0)
        pre = pre + jnp.where(column < side - 1, right, 0.0)
        pre_ref[begin : begin + block, :] = pre
        act_ref[begin : begin + block, :] = gelu(pre).astype(bf16)


def conv(side, idx, sources, own, other, group, bias, bias_other, first=False):
    taps, depth, outs = own.shape
    spots = sources[1].shape[0]
    rows = spots - side
    return call(
        functools.partial(conv_body, side, first, group),
        "conv",
        [(SMEM, idx)]
        + [(FAR, s) for s in sources]
        + [(FAR, own), (FAR, other[0]), (FAR, other[1])]
        + [(VMEM, bias.reshape(1, outs)), (VMEM, bias_other.reshape(1, outs))],
        [(VMEM, struct((rows, 2 * outs), f32)), (VMEM, struct((rows, 2 * outs), bf16))],
        [
            pltpu.VMEM((spots, depth), bf16),
            pltpu.VMEM((2, taps, depth, outs), bf16),
            pltpu.VMEM((3, spots + 2 * side, 2 * outs), f32),
            pltpu.SemaphoreType.DMA((2 * other[0].shape[0] + 5,)),
        ],
        spare=14 if first else 8,
    )


def spread_taps(side, grad, taps_ref):
    pixels, outs = grad.shape
    column = columns_of(pixels, outs, side)
    wide = grad.astype(f32)
    ahead = jnp.where(column < side - 1, pltpu.roll(wide, pixels - 1, 0), 0.0).astype(bf16)
    behind = jnp.where(column > 0, pltpu.roll(wide, 1, 0), 0.0).astype(bf16)
    edge = jnp.zeros((side, 3 * outs), bf16)
    taps_ref[:side, :] = edge
    taps_ref[side + pixels :, :] = edge
    taps_ref[side : side + pixels, :] = jnp.concatenate([ahead, grad, behind], axis=1)


def tap_block(side, taps_ref, begin, block):
    return lanes([taps_ref[at(begin + side * (2 - y), block, side), :] for y in range(3)])


def slope_body(side, arrive, idx_ref, keep_ref, recv_ref, pre_ref, mine_ref, theirs_ref, gp_ref):
    arrive()
    zh = idx_ref[2]
    half, outs = mine_ref.shape
    total = keep_ref[...] + recv_ref[...].astype(f32)
    spots = keep_ref.shape[0]
    pre = pre_ref[at(zh * (pre_ref.shape[0] - spots), spots, side), :]
    gp_ref[...] = (total * gelu_slope(pre)).astype(bf16)
    own = gp_ref[at(zh * (gp_ref.shape[0] - half), half, side), :]
    low, high = own[:, :outs], own[:, outs:]
    mine_ref[...] = jnp.where(zh == 0, low, high)
    theirs_ref[...] = jnp.where(zh == 0, high, low)


def slope_back(side, idx, keep, recv, pre, half):
    outs = pre.shape[1] // 2
    return call(
        functools.partial(slope_body, side),
        "slope_back",
        [(SMEM, idx), (VMEM, keep), (VMEM, recv), (LOAD, pre)],
        [
            (VMEM, struct((half, outs), bf16)),
            (VMEM, struct((half, outs), bf16)),
            (VMEM, struct(keep.shape, bf16)),
        ],
    )


def back_body(side, last, group, arrive, idx_ref, *refs):
    zh, zl = idx_ref[2], idx_ref[3]
    if last:
        valid_ref, grad_ref, x_ref, go_ref, far_ref, idk_ref, wl, wo, ws, po, ps = refs[:11]
        own_ref, give_ref, taps_ref, wbuf, idk_far, sems = refs[11:]
    else:
        keep_ref, recv_ref, pre_ref, wl, wo, ws, gp_ref, own_ref, give_ref, taps_ref, wbuf, sems = refs
    pairs = slice_copies(group, idx_ref, wl, wo, ws, wbuf)
    if last:
        pairs += flat_copies(9, idx_ref, po, ps, idk_far)
    copies = start_copies(pairs, sems)
    arrive()
    if last:
        grad = grad_ref[...]
    else:
        spots = gp_ref.shape[0]

        def window(ref):
            return ref[at(zh * (ref.shape[0] - spots), spots, side), :]

        total = window(keep_ref) + window(recv_ref).astype(f32)
        grad = (total * gelu_slope(window(pre_ref))).astype(bf16)
        gp_ref[...] = grad
    spread_taps(side, grad, taps_ref)
    depth, outs = wl.shape[1:]
    pixels = own_ref.shape[-2]
    start = zh * side
    for copy in copies:
        copy.wait()
    chans = depth // 4

    def rows(index):
        spot = at(index * chans, chans, chans)
        return lanes([wbuf[u, t, spot, :] for t in range(9) for u in range(2)])

    for target, along in ((give_ref, 1 - zl), (own_ref, zl)):
        if last:
            units = chans // idk_far.shape[2]
            for up in range(2):
                index = 2 * up + along
                weights = rows(index)
                near = idk_ref[at(index * chans, chans, chans), :]
                far = flat_rows(idk_far, index * units, units)
                apart = zh * (far_ref.shape[0] - pixels)
                for begin, block in halves(pixels, side):
                    here = at(zh * pixels + begin, block, side)
                    part = dot(tap_block(side, taps_ref, start + begin, block), weights, NT)
                    x = x_ref[here, at(index * chans, chans, chans)]
                    part = part * gelu_slope(x.astype(f32))
                    part = part + dot(go_ref[here, :], near, NT)
                    part = part + valid_ref[0] * dot(far_ref[at(apart + begin, block, side), :], far, NT)
                    target[up, begin : begin + block, :] = part.astype(target.dtype)
        else:
            weights = jnp.concatenate([rows(along), rows(2 + along)], axis=0)
            for begin, block in halves(pixels, side):
                part = dot(tap_block(side, taps_ref, start + begin, block), weights, NT)
                target[begin : begin + block, :] = part.astype(target.dtype)


def back(side, idx, sources, own, other, group, last=None):
    taps, depth, outs = own.shape
    spots = min(sources[0].shape[0], sources[-1].shape[0])
    copies = 2 * other[0].shape[0] + 1
    extra = []
    scratch = []
    if last:
        valid, full_x, go, cot_far, idk, pieces, half = last
        chans = depth // 4
        shape = (2, half, chans)
        results = []
        extra = [(FAR, pieces[0]), (FAR, pieces[1])]
        sources = list(sources) + [full_x, go, cot_far, idk]
        columns, size = idk.shape[1] // 128, pieces[0].shape[2]
        scratch = [pltpu.VMEM((columns, depth // size, size, 128), bf16)]
        copies += 2 * other[0].shape[0] * columns
    else:
        shape = (spots - side, depth // 2)
        results = [(VMEM, struct((spots, 2 * outs), bf16))]
    results += [(VMEM, struct(shape, f32)), (VMEM, struct(shape, bf16))]
    return call(
        functools.partial(back_body, side, bool(last), group),
        "back",
        [(SMEM, idx)]
        + ([(SMEM, last[0])] if last else [])
        + [(LOAD, source) for source in sources]
        + [(FAR, own), (FAR, other[0]), (FAR, other[1])]
        + extra,
        results,
        [pltpu.VMEM((spots + 2 * side, 6 * outs), bf16), pltpu.VMEM((2, taps, depth, outs), bf16)]
        + scratch
        + [pltpu.SemaphoreType.DMA((copies,))],
        spare=14 if last else 10,
    )


def put_blocks(idx_ref, keep_ref, give_ref, part, tap, first_block, size, begin=0):
    chip, core = idx_ref[0], idx_ref[1]
    for b in range(0, part.shape[0] // size, 2):
        even = part[b * size : (b + 1) * size, :]
        odd = part[(b + 1) * size : (b + 2) * size, :]
        mask = chip ^ ((first_block + b) // 2)
        slot = slot_of(mask, core, keep_ref.shape[0])
        give_slot = slot_of(mask, 1 - core, keep_ref.shape[0])
        rows = slice(begin + tap * size, begin + (tap + 1) * size)
        keep_ref[slot, rows, :] = jnp.where(core == 0, even, odd).astype(bf16)
        give_ref[give_slot, rows, :] = jnp.where(core == 0, odd, even).astype(bf16)


def weight_body(side, half, flat, arrive, idx_ref, gp_ref, *refs):
    if flat:
        full_ref, go_ref, bias_ref = refs[:3]
        refs = refs[3:]
    xl, xa, keep_ref, give_ref, xbuf, taps_ref, sems = refs
    arrive()
    zh, zl = idx_ref[2], idx_ref[3]
    chans = xl.shape[1] // 2
    spots = xbuf.shape[0]
    window = at(zh * (xl.shape[0] - spots), spots, side)
    pairs = []
    for source, along in ((xl, zl), (xa, 1 - zl)):
        for up in range(2):
            pairs.append(
                (
                    source.at[window, up * chans : (up + 1) * chans],
                    xbuf.at[:, at((2 * up + along) * chans, chans, chans)],
                )
            )
    run_copies(pairs, sems)
    wide = gp_ref.shape[1]
    outs = wide // 2
    spot = lax.broadcasted_iota(jnp.int32, (spots, wide), 0) - zh * side
    grad = gp_ref[at(zh * (gp_ref.shape[0] - spots), spots, side), :].astype(f32)
    grad = jnp.where((spot >= 0) & (spot < half), grad, 0.0)
    bias = jnp.sum(grad, axis=0, keepdims=True)
    spread_taps(side, grad.astype(bf16), taps_ref)
    blocks = 2 * keep_ref.shape[0]
    depth = xbuf.shape[1]
    size = depth // blocks
    for begin in range(0, depth, 256):
        values = xbuf[:, begin : begin + 256]
        for y in range(3):
            place = side * (2 - y)
            part = dot(values, taps_ref[place : place + spots, :], TN)
            for x in range(3):
                for u in range(2):
                    col = x * wide + u * outs
                    put_blocks(
                        idx_ref, keep_ref, give_ref, part[:, col : col + outs],
                        3 * y + x, begin // size, size, u * (9 * size + 16),
                    )
    for u in range(2):
        row = jnp.broadcast_to(bias[:, u * outs : (u + 1) * outs], (16, outs)).astype(bf16)
        for j in range(keep_ref.shape[0]):
            spot = slice(u * (9 * size + 16) + 9 * size, (u + 1) * (9 * size + 16))
            keep_ref[j, spot, :] = row
            give_ref[j, spot, :] = row
    if flat:
        first = 2 * (9 * size + 16)
        flat_pieces(1.0, idx_ref, full_ref, go_ref, bias_ref, keep_ref, give_ref, first)


def weight_grad(side, half, idx, grad, act, act_other, chips, flat=()):
    spots = half + side
    wide = grad.shape[1]
    outs = wide // 2
    depth = 2 * act.shape[1]
    rows = 2 * (9 * depth // (2 * chips) + 16)
    if flat:
        rows += flat_size(flat[0], flat[1], chips)
    return call(
        functools.partial(weight_body, side, half, bool(flat)),
        "weight_grad",
        [(SMEM, idx), (LOAD, grad)] + [(LOAD, a) for a in flat] + [(FAR, act), (FAR, act_other)],
        [(VMEM, struct((chips, rows, outs), bf16))] * 2,
        [
            pltpu.VMEM((spots, depth), bf16),
            pltpu.VMEM((spots + 2 * side, 3 * wide), bf16),
            pltpu.SemaphoreType.DMA((4,)),
        ],
        spare=10,
    )


def weight_one_body(side, arrive, idx_ref, mine_ref, theirs_ref, x_ref, *refs):
    keep_ref, give_ref, gp_ref, taps_ref = refs
    arrive()
    zh = idx_ref[2]
    half, outs = mine_ref.shape
    gp_ref[at(zh * half, half, side), :] = mine_ref[...]
    gp_ref[at((1 - zh) * half, half, side), :] = theirs_ref[...]
    grad = gp_ref[...]
    bias = jnp.sum(grad.astype(f32), axis=0, keepdims=True)
    spread_taps(side, grad, taps_ref)
    blocks = 2 * keep_ref.shape[0]
    spots, depth = x_ref.shape
    size = depth // blocks
    right = tap_block(side, taps_ref, 0, spots)
    for begin in range(0, depth, 256):
        part = dot(x_ref[:, begin : begin + 256], right, TN)
        for tap in range(9):
            put_blocks(
                idx_ref, keep_ref, give_ref, part[:, tap * outs : (tap + 1) * outs],
                tap, begin // size, size,
            )
    row = jnp.broadcast_to(bias, (16, outs)).astype(bf16)
    first = 9 * size + 16
    for j in range(keep_ref.shape[0]):
        keep_ref[j, 9 * size : first, :] = row
        give_ref[j, 9 * size : first, :] = row


def weight_one_grad(side, idx, mine, theirs, act_zero, chips):
    spots, depth = act_zero.shape
    outs = mine.shape[1]
    rows = 9 * depth // (2 * chips) + 16
    return call(
        functools.partial(weight_one_body, side),
        "weight_one_grad",
        [(SMEM, idx), (LOAD, mine), (LOAD, theirs), (LOAD, act_zero)],
        [(VMEM, struct((chips, rows, outs), bf16))] * 2,
        [
            pltpu.VMEM((spots, outs), bf16),
            pltpu.VMEM((spots + 2 * side, 3 * outs), bf16),
        ],
        spare=14,
    )


def fold_body(pairs, arrive, idx_ref, *refs):
    arrive()
    ins, (keep_ref, give_ref) = refs[: 2 * pairs], refs[2 * pairs :]
    half = keep_ref.shape[0]
    for i in range(2 * half):
        target = keep_ref if i < half else give_ref
        begin = 0
        for keep, recv in zip(ins[0::2], ins[1::2]):
            rows = keep.shape[1]
            total = keep[i].astype(f32) + recv[i].astype(f32)
            target[i % half, begin : begin + rows, :] = total.astype(bf16)
            begin += rows


def fold(idx, *arrays):
    blocks, _, wide = arrays[0].shape
    rows = sum(a.shape[1] for a in arrays[0::2])
    return call(
        functools.partial(fold_body, len(arrays) // 2),
        "fold",
        [(SMEM, idx)] + [(VMEM, a) for a in arrays],
        [(VMEM, struct((blocks // 2, rows, wide), bf16))] * 2,
    )


def last_body(slotted, rest, arrive, idx_ref, keep_in, recv_in, *targets):
    arrive()
    zh = idx_ref[2]

    def put(target, place, begin, rows):
        spot = at(begin, rows, 16)
        total = keep_in[0, spot, :].astype(f32) + recv_in[0, spot, :].astype(f32)
        target[place : place + rows, :] = total.astype(bf16)

    place = 0
    for begin, rows in slotted:
        put(targets[0], place, begin + zh * rows, rows)
        put(targets[1], place, begin + (1 - zh) * rows, rows)
        place += rows
    begin, rows = rest
    put(targets[-1], 0, begin, rows)


def last_fold(idx, keep, recv, slotted=(), rest=None):
    wide = keep.shape[2]
    rest = rest or (0, keep.shape[1])
    rows = sum(size for _, size in slotted)
    sizes = ([rows, rows] if slotted else []) + [rest[1]]
    return call(
        functools.partial(last_body, slotted, rest),
        "last_fold",
        [(SMEM, idx), (VMEM, keep), (VMEM, recv)],
        [(VMEM, struct((size, wide), bf16)) for size in sizes],
    )


def final_body(parts, arrive, idx_ref, own_ref, sib_ref, *refs):
    arrive()
    outs, stages, sems = refs[: 2 * len(parts)], refs[2 * len(parts) : -1], refs[-1]
    chip, core = idx_ref[0], idx_ref[1]
    chips, _, wide = own_ref.shape
    first = 0
    copies = []

    def store(source, target):
        copies.append(pltpu.make_async_copy(source, target, sems.at[len(copies)]))
        copies[-1].start()

    for n, part in enumerate(parts):
        grad_ref, bias_ref, stage = outs[2 * n], outs[2 * n + 1], stages[n]
        size = part[0] // (2 * chips)
        columns = 1 if len(part) == 1 else part[1] // wide
        end = first + size * (9 if len(part) == 1 else columns)
        for c in range(columns):
            row = own_ref[0, end + c : end + c + 1, :].astype(f32)
            bias_ref[:, c * wide : (c + 1) * wide] = row
        for n_row, begin in enumerate(range(first, end, size)):
            for j in range(chips):
                for source, owner in ((own_ref, core), (sib_ref, 1 - core)):
                    home = chip ^ mask_of(j, owner, chips)
                    spot = at((2 * home + owner) * size, size, size)
                    piece = source[j, begin : begin + size, :].astype(f32)
                    if len(part) == 1:
                        stage[n_row, spot, :] = piece
                    else:
                        stage[spot, n_row * wide : (n_row + 1) * wide] = piece
            if len(part) == 1:
                store(stage.at[n_row], grad_ref.at[n_row])
        if len(part) > 1:
            store(stage, grad_ref)
        first = end + 16
    for copy in copies:
        copy.wait()


def final_grads(idx, own, sib, parts):
    wide = own.shape[2]
    results, stages = [], []
    for part in parts:
        shape = (9, part[0], wide) if len(part) == 1 else part
        results += [(FAR, struct(shape, f32)), (VMEM, struct((1, shape[-1]), f32))]
        stages.append(pltpu.VMEM(shape, f32))
    copies = sum(9 if len(part) == 1 else 1 for part in parts)
    return call(
        functools.partial(final_body, parts),
        "final_grads",
        [(SMEM, idx), (VMEM, own), (VMEM, sib)],
        results,
        stages + [pltpu.SemaphoreType.DMA((copies,))],
    )


def flat_pieces(gain, idx_ref, x_ref, go_ref, bias_ref, keep_ref, give_ref, first):
    chip, core = idx_ref[0], idx_ref[1]
    chips, _, wide = keep_ref.shape
    columns = go_ref.shape[1] // wide
    size = x_ref.shape[1] // (2 * chips)
    bias = jnp.concatenate(
        [bias_ref[:, c * wide : (c + 1) * wide] for c in range(columns)]
        + [jnp.zeros((16 - columns, wide), f32)],
        axis=0,
    ).astype(bf16)
    for j in range(chips):
        keep_ref[j, first + columns * size :, :] = bias
        give_ref[j, first + columns * size :, :] = bias
    for begin in range(0, x_ref.shape[1], 256):
        part = gain * dot(x_ref[:, begin : begin + 256], go_ref[...], TN)
        for b in range(0, 256 // size, 2):
            mask = chip ^ ((begin // size + b) // 2)
            slot = slot_of(mask, core, chips)
            give_slot = slot_of(mask, 1 - core, chips)
            for c in range(columns):
                even = part[b * size : (b + 1) * size, c * wide : (c + 1) * wide]
                odd = part[(b + 1) * size : (b + 2) * size, c * wide : (c + 1) * wide]
                spot = slice(first + c * size, first + (c + 1) * size)
                keep_ref[slot, spot, :] = jnp.where(core == 0, even, odd).astype(bf16)
                give_ref[give_slot, spot, :] = jnp.where(core == 0, odd, even).astype(bf16)


def flat_size(x, go, chips):
    return (go.shape[1] // 128) * (x.shape[1] // (2 * chips)) + 16


def outer_body(gain, arrive, idx_ref, x_ref, go_ref, bias_ref, keep_ref, give_ref):
    arrive()
    flat_pieces(gain, idx_ref, x_ref, go_ref, bias_ref, keep_ref, give_ref, 0)


def outer(idx, x, go, gain, bias, chips):
    return call(
        functools.partial(outer_body, gain),
        "outer",
        [(SMEM, idx), (LOAD, x), (LOAD, go), (LOAD, bias)],
        [(VMEM, struct((chips, flat_size(x, go, chips), 128), bf16))] * 2,
        spare=8,
    )


def start_body(arrive, idx_ref, valid_ref, cot_ref, outk_ref, go_ref, bias_ref, own_ref, give_ref):
    arrive()
    zl = idx_ref[3]
    masked = cot_ref[...].astype(f32) * valid_ref[0]
    go_ref[...] = masked.astype(bf16)
    bias_ref[...] = jnp.sum(masked, axis=0, keepdims=True)
    chans = outk_ref.shape[0] // 4
    block = cot_ref.shape[0] // 4
    for target, along in ((give_ref, 1 - zl), (own_ref, zl)):
        weights = jnp.concatenate(
            [outk_ref[at((2 * up + along) * chans, chans, chans), :] for up in range(2)], axis=0
        )
        for begin in range(0, cot_ref.shape[0], block):
            part = post_gain * dot(go_ref[begin : begin + block, :], weights, NT)
            target[begin : begin + block, :] = part.astype(target.dtype)


def start_back(idx, valid, cot, outk):
    spots, outs = cot.shape
    half = outk.shape[0] // 2
    return call(
        start_body,
        "start_back",
        [(SMEM, idx), (SMEM, valid), (LOAD, cot), (LOAD, outk)],
        [
            (VMEM, struct(cot.shape, bf16)),
            (VMEM, struct((1, outs), f32)),
            (VMEM, struct((spots, half), f32)),
            (VMEM, struct((spots, half), bf16)),
        ],
    )


def rows_body(side, arrive, idx_ref, own_ref, recv_ref, keep_ref, give_ref):
    arrive()
    zh = idx_ref[2]
    spots = keep_ref.shape[0]
    apart = own_ref.shape[0] - spots
    for target, begin in ((give_ref, (1 - zh) * apart), (keep_ref, zh * apart)):
        spot = at(begin, spots, side)
        total = own_ref[spot, :] + recv_ref[spot, :].astype(f32)
        target[...] = total.astype(target.dtype)


def rows_sum(side, idx, own, recv, spots):
    shape = (spots, own.shape[1])
    return call(
        functools.partial(rows_body, side),
        "rows_sum",
        [(SMEM, idx), (LOAD, own), (LOAD, recv)],
        [(VMEM, struct(shape, f32)), (VMEM, struct(shape, bf16))],
    )


def slots_body(arrive, idx_ref, own_ref, recv_ref, keep_ref, give_ref):
    arrive()
    zh = idx_ref[2]
    for target, slot in ((give_ref, 1 - zh), (keep_ref, zh)):
        total = own_ref[slot] + recv_ref[slot].astype(f32)
        target[...] = total.astype(bf16)


def slots_sum(idx, own, recv):
    shape = struct(own.shape[1:], bf16)
    return call(
        slots_body,
        "slots_sum",
        [(SMEM, idx), (VMEM, own), (VMEM, recv)],
        [(VMEM, shape), (VMEM, shape)],
    )


def input_body(arrive, idx_ref, keep_ref, recv_ref, out_ref):
    arrive()
    zh = idx_ref[2]
    half = keep_ref.shape[0]
    out_ref[at(zh * half, half, half), :] = keep_ref[...]
    out_ref[at((1 - zh) * half, half, half), :] = recv_ref[...]


def input_grad(idx, keep, recv):
    half, chans = keep.shape
    return call(
        input_body,
        "input_grad",
        [(SMEM, idx), (VMEM, keep), (VMEM, recv)],
        [(VMEM, struct((2 * half, chans), bf16))],
    )


def whole_body(side, arrive, idx_ref, xl, xa, xh, xd, rh, rl, x_ref, act_ref, sems):
    arrive()
    zh, zl = idx_ref[2], idx_ref[3]
    chans = xl.shape[1]
    spots = xa.shape[0]
    rest = xl.shape[0] - spots
    window, outside = at(zh * rest, spots, side), at((1 - zh) * spots, rest, side)

    def cols(up, along):
        return at((2 * up + along) * chans, chans, chans)

    run_copies(
        [
            (xl, x_ref.at[:, cols(zh, zl)]),
            (xa, x_ref.at[window, cols(zh, 1 - zl)]),
            (xh, x_ref.at[window, cols(1 - zh, zl)]),
            (xd, x_ref.at[window, cols(1 - zh, 1 - zl)]),
            (rl.at[0], x_ref.at[outside, cols(zh, 1 - zl)]),
            (rh, x_ref.at[outside, cols(1 - zh, zl)]),
            (rl.at[1], x_ref.at[outside, cols(1 - zh, 1 - zl)]),
        ],
        sems,
    )
    block = x_ref.shape[0] // 8
    for begin in range(0, x_ref.shape[0], block):
        rows = slice(begin, begin + block)
        act_ref[rows, :] = gelu(x_ref[rows, :].astype(f32)).astype(bf16)


def whole_input(side, idx, *parts):
    spots, chans = parts[0].shape
    return call(
        functools.partial(whole_body, side),
        "whole_input",
        [(SMEM, idx)] + [(FAR, p) for p in parts],
        [(VMEM, struct((spots, 4 * chans), bf16))] * 2,
        [pltpu.SemaphoreType.DMA((7,))],
    )


def join_body(arrive, idx_ref, own, recv, far_own, far_recv, out, sems):
    arrive()
    zh, zl = idx_ref[2], idx_ref[3]
    half = own.shape[0]
    chans = own.shape[1] // 2
    pairs = []
    for source, up, along in ((own, zh, zl), (recv, zh, 1 - zl), (far_own, 1 - zh, zl), (far_recv, 1 - zh, 1 - zl)):
        for slot in range(2):
            spot = at((2 * slot + along) * chans, chans, chans)
            target = out.at[at(up * half, half, half), spot]
            pairs.append((source.at[:, slot * chans : (slot + 1) * chans], target))
    run_copies(pairs, sems)


def join(idx, *parts):
    half, wide = parts[0].shape
    return call(
        join_body,
        "join",
        [(SMEM, idx)] + [(FAR, p) for p in parts],
        [(VMEM, struct((2 * half, 2 * wide), bf16))],
        [pltpu.SemaphoreType.DMA((8,))],
    )


def finish_body(arrive, idx_ref, valid_ref, x_ref, act_ref, idk_ref, outk_ref, ib_ref, out_ref):
    arrive()
    block = x_ref.shape[0] // 4
    for begin in range(0, x_ref.shape[0], block):
        rows = slice(begin, begin + block)
        identity = dot(x_ref[rows, :], idk_ref[...]) + ib_ref[...]
        branch = dot(act_ref[rows, :], outk_ref[...])
        out_ref[rows, :] = ((identity + post_gain * branch) * valid_ref[0]).astype(bf16)


def finish(idx, valid, x, act, idk, outk, ib):
    outs = idk.shape[1]
    return call(
        finish_body,
        "finish",
        [(SMEM, idx), (SMEM, valid), (LOAD, x), (LOAD, act), (LOAD, idk), (LOAD, outk)]
        + [(VMEM, ib.reshape(1, outs))],
        [(VMEM, struct((x.shape[0], outs), bf16))],
        spare=8,
    )


def flip(value, axis):
    return lax.ppermute(value, axis, [(0, 1), (1, 0)])


def cross(value, step, chips):
    pairs = []
    for chip in range(chips):
        for core in range(2):
            other = chip ^ step_bits(core, chips)[step]
            pairs.append((2 * chip + core, 2 * other + core))
    return lax.ppermute(value, DP, pairs)


def hops(value, chips):
    blocks = [value]
    for i in range(1, chips):
        pairs = []
        for chip in range(chips):
            for core in range(2):
                bits = step_bits(core, chips)
                mask = sum(bit for n, bit in enumerate(bits) if i >> (len(bits) - 1 - n) & 1)
                pairs.append((2 * (chip ^ mask) + core, 2 * chip + core))
        blocks.append(lax.ppermute(value, DP, pairs))
    return blocks


def swap(pieces, axis):
    return lax.all_to_all(pieces, axis, split_axis=0, concat_axis=0, tiled=True)


def after(value, other):
    return lax.optimization_barrier((value, other))[0]


def rows_of(value, start, size):
    return lax.dynamic_slice_in_dim(value, start, size, 0)


def local(
    pixels,
    counts,
    kernel_one,
    bias_one,
    kernel_two,
    bias_two,
    kernel_three,
    bias_three,
    out_kernel,
    identity_kernel,
    identity_bias,
    cotangent,
):
    images, rows, width, chans = pixels.shape
    side = width // 2
    spots = side * side
    half = spots // 2
    window = half + halo * side
    outs = cotangent.shape[3]
    chips = lax.axis_size("chip")
    chip, core, zh, zl = [lax.axis_index(a) for a in ("chip", "core", "zh", "zl")]
    idx = jnp.stack([chip, core, zh, zl]).astype(jnp.int32)
    taps = lambda kernel: kernel.reshape((9,) + kernel.shape[2:])
    one, two, three = taps(kernel_one), taps(kernel_two), taps(kernel_three)

    own_count = lax.dynamic_index_in_dim(counts, 2 * chip + core, 0, keepdims=True)
    valid = (own_count > 0).astype(f32)

    place = 2 * chip + core

    def units_of(kernel, size):
        if kernel.ndim == 3:
            block = kernel.shape[1] // (2 * chips)
            return lax.dynamic_slice_in_dim(kernel, place * block, block, 1)
        block = kernel.shape[0] // (2 * chips)
        block = lax.dynamic_slice_in_dim(kernel, place * block, block, 0)
        block = block.reshape(-1, size, block.shape[1] // 128, 128)
        return block.transpose(2, 0, 1, 3).reshape(-1, size, 128)

    steps = chips.bit_length() - 1

    def start_spread(piece, *others):
        return jnp.concatenate(after((piece[None], cross(piece[None], steps - 1, chips)), others))

    def end_spread(own, *others):
        for step in reversed(range(steps - 1)):
            own = jnp.concatenate(after((own, cross(own, step, chips)), others))
        return own, flip(own, "core")

    last = [idx]

    def turn(*others):
        return after(idx, (last[0],) + others)

    def ran(results):
        last[0] = results[-1] if isinstance(results, (list, tuple)) else results
        return results

    size = two.shape[1] // (2 * chips)
    deep = two.shape[1]
    cot = cotangent.reshape(spots, outs)
    one_piece = flip(units_of(one, size), "zh")
    pooled = ran(pool(pixels))
    go, identity_bias_grad, ga_own, ga_give = ran(start_back(turn(), valid, cot, out_kernel))
    bias_other = flip(after(jnp.stack([bias_one, bias_two, bias_three]), go), "zh")
    two_piece = units_of(after(two, pooled), size)
    last_piece = jnp.concatenate([units_of(after(k, pooled), size) for k in (three, identity_kernel)])
    cot_rows = rows_of(after(cot, pooled), (1 - zh) * half, half)
    xl = swap(after(pooled, (one_piece, two_piece, last_piece, cot_rows, ga_give)), DP)
    xl = xl.reshape(spots, chans)
    two_piece = flip(after(two_piece, one_piece), "zh")

    apart = spots - window
    xa = flip(rows_of(xl, zh * apart, window), "zl")
    xh = flip(rows_of(xl, (1 - zh) * apart, window), "zh")
    rest = spots - window
    rest_own = rows_of(xl, (1 - zh) * window, rest)
    rest_high = rows_of(xl, zh * window, rest)
    two_near = start_spread(after(two_piece, xl))
    one_near = start_spread(after(one_piece, xl), xh, xa, two_near, bias_other)
    xd = flip(xh, "zl")
    last_piece = flip(after(last_piece, xh), "zh")
    two_other = end_spread(two_near, xd)
    one_other = end_spread(one_near, xd, two_other[0], last_piece)
    ga_recv = flip(after(ga_give, xd), "zl")
    rest_high = flip(after(rest_high, xd), "zh")

    pre_one, act_one = ran(
        conv(
            side, turn(), (xl, xa, xh, xd), one, one_other, 0, bias_one, bias_other[0], True
        )
    )
    act_one_other = flip(act_one, "zl")
    ga_own, ga_give = ran(rows_sum(side, turn(), ga_own, ga_recv, half + (halo - 3) * side))
    pre_two, act_two = ran(
        conv(side, turn(), (act_one, act_one_other), two, two_other, 0, bias_two, bias_other[1])
    )
    act_two_other = flip(act_two, "zl")
    ga_recv = flip(after(ga_give, act_two), "zh")
    last_other = jnp.stack(after(hops(after(last_piece, act_one), chips), act_two))
    last_other = last_other, flip(last_other, "core")
    pre_three, act_three = ran(
        conv(side, turn(), (act_two, act_two_other), three, last_other, 0, bias_three, bias_other[2])
    )
    rest_low = flip(jnp.stack(after((rest_own, rest_high), act_three)), "zl")
    cot_far = flip(after(cot_rows, act_three), "zh")
    own_rows = rows_of(act_three, zh * (halo - 3) * side, half)

    gp_three, ga_own, ga_give = ran(
        back(side, turn(), (ga_own, ga_recv, pre_three), three, last_other, 0)
    )
    ga_recv = flip(ga_give, "zl")
    full_x, act_zero = ran(whole_input(side, turn(), xl, xa, xh, xd, rest_high, rest_low))
    keep_three, give_three = ran(
        weight_grad(
            side, half, turn(), gp_three, act_two, act_two_other, chips, (full_x, go, identity_bias_grad)
        )
    )
    gp_two, ga_own, ga_give = ran(
        back(side, turn(), (ga_own, ga_recv, pre_two), two, two_other, 0)
    )
    ga_recv = flip(ga_give, "zl")
    keep_two, give_two = ran(weight_grad(side, half, turn(cot_far), gp_two, act_one, act_one_other, chips))

    gp_mine, gp_theirs, gp_one = ran(slope_back(side, turn(), ga_own, ga_recv, pre_one, half))
    gp_theirs = flip(gp_theirs, "zh")
    recv_three = flip(after(give_three, gp_one), "core")
    recv_two = flip(after(give_two, gp_one), "core")
    gx_own, gx_give = ran(
        back(
            side, turn(), (gp_one,), one, one_other, 0,
            (valid, full_x, go, cot_far, identity_kernel, last_other, half),
        )
    )

    def folds(keep, recv, first, *others):
        for step in range(first, steps):
            keep, give = ran(fold(turn(*others), keep, recv))
            recv = cross(give, step, chips)
        return keep, recv

    keep_deep, give_deep = ran(fold(turn(gp_theirs), keep_three, recv_three, keep_two, recv_two))
    recv_deep = cross(give_deep, 0, chips)
    gx_recv = flip(after(gx_give, keep_deep), "zl")
    own_rows = after(own_rows, keep_deep)
    near_rows = flip(own_rows, "zl")
    far_rows = flip(own_rows, "zh")
    keep_one, give_one = ran(weight_one_grad(side, turn(), gp_mine, gp_theirs, act_zero, chips))
    recv_one = flip(give_one, "core")
    keep_deep, recv_deep = folds(keep_deep, recv_deep, 1, far_rows)
    gx_keep, gx_give = ran(slots_sum(turn(), gx_own, gx_recv))
    gx_recv = flip(gx_give, "zh")
    keep_one, give_one = ran(fold(turn(), keep_one, recv_one))
    recv_one = cross(give_one, 0, chips)
    slot = 9 * size + 16
    flat = keep_three.shape[1] - 2 * slot
    keep_deep, give_deep, id_rows = ran(
        last_fold(
            turn(), keep_deep, recv_deep, ((0, slot), (2 * slot + flat, slot)), (2 * slot, flat)
        )
    )
    recv_deep = flip(give_deep, "zh")
    far_near_rows = flip(after(far_rows, keep_deep), "zl")
    keep_one, recv_one = folds(keep_one, recv_one, 1)
    gx = ran(input_grad(turn(), gx_keep, gx_recv))
    full_three = ran(join(turn(), own_rows, near_rows, far_rows, far_near_rows))
    keep_out, give_out = ran(outer(turn(), full_three, go, post_gain, identity_bias_grad, chips))
    recv_out = flip(give_out, "core")
    (total_one,) = ran([last_fold(turn(), keep_one, recv_one)])
    near_one = start_spread(total_one)
    keep_out, give_out = ran(fold(turn(), keep_out, recv_out))
    recv_out = cross(give_out, 0, chips)
    deep_part = (after(keep_deep, keep_out).astype(f32) + recv_deep.astype(f32)).astype(bf16)
    gx = after(gx, deep_part)
    gx = swap(gx.reshape(images, rows * width // 4, chans), DP)
    block_out = ran(
        finish(turn(deep_part), valid, full_x, full_three, identity_kernel, out_kernel, identity_bias)
    )
    keep_out, recv_out = folds(keep_out, recv_out, 1, near_one)
    pixels_grad = ran(widen(turn(), gx, rows, width))
    (total_out,) = ran([last_fold(turn(), keep_out, recv_out)])
    deep_rows = jnp.concatenate([deep_part, id_rows, total_out])
    all_one = end_spread(near_one)
    near_deep = start_spread(deep_rows, all_one[0])
    kernel_one_grad, bias_one_grad = ran(final_grads(turn(), *all_one, ((one.shape[1],),)))
    all_deep = end_spread(near_deep, bias_one_grad)
    (
        kernel_three_grad,
        bias_three_grad,
        kernel_two_grad,
        bias_two_grad,
        identity_kernel_grad,
        identity_bias_grad,
        out_kernel_grad,
        _,
    ) = ran(
        final_grads(turn(), *all_deep, ((deep,), (deep,), identity_kernel.shape, out_kernel.shape))
    )

    return (
        block_out.reshape(cotangent.shape),
        pixels_grad,
        kernel_one_grad.reshape(kernel_one.shape),
        bias_one_grad[0],
        kernel_two_grad.reshape(kernel_two.shape),
        bias_two_grad[0],
        kernel_three_grad.reshape(kernel_three.shape),
        bias_three_grad[0],
        out_kernel_grad,
        identity_kernel_grad,
        identity_bias_grad[0],
    )


def solution(mesh):
    members = mesh.devices.size // mesh.shape["mp"]
    fine = Mesh(
        mesh.devices.reshape(members // 2, 2, 2, mesh.shape["mp"] // 2),
        ("chip", "core", "zh", "zl"),
    )
    return jax.shard_map(
        local,
        mesh=fine,
        in_specs=(
            P(None, DP, None, MP),
            P(),
            P(None, None, None, MP),
            P(MP),
            P(None, None, None, MP),
            P(MP),
            P(None, None, None, MP),
            P(MP),
            P(None, MP),
            P(None, MP),
            P(MP),
            P(DP, None, None, MP),
        ),
        out_specs=(
            P(DP, None, None, MP),
            P(None, DP, None, MP),
            P(None, None, None, MP),
            P(MP),
            P(None, None, None, MP),
            P(MP),
            P(None, None, None, MP),
            P(MP),
            P(None, MP),
            P(None, MP),
            P(MP),
        ),
        check_vma=False,
    )
```

```python
import functools
import math

import jax
import jax.numpy as jnp
from jax import lax
from jax.experimental import pallas as pl
from jax.experimental.pallas import tpu as pltpu
from jax.sharding import Mesh
from jax.sharding import PartitionSpec as P


post_gain = 0.015625
slope = 0.7978845608028654
cubic = 0.044715
halo = 6
bf16 = jnp.bfloat16
f32 = jnp.float32
NT = (((1,), (1,)), ((), ()))
TN = (((0,), (0,)), ((), ()))
NN = (((1,), (0,)), ((), ()))
DP = ("chip", "core")
MP = ("zh", "zl")


def dot(left, right, dims=NN):
    return lax.dot_general(left, right, dims, preferred_element_type=f32)


def gelu(value):
    inner = jnp.tanh(slope * (value + cubic * value * value * value))
    return 0.5 * value * (1.0 + inner)


def gelu_slope(value):
    square = value * value
    inner = jnp.tanh(slope * value * (1.0 + cubic * square))
    climb = slope * (1.0 + 3.0 * cubic * square)
    return 0.5 * (1.0 + inner) + 0.5 * value * (1.0 - inner * inner) * climb


def struct(shape, kind):
    return jax.ShapeDtypeStruct(shape, kind)


def lanes(blocks):
    return blocks[0] if len(blocks) == 1 else jnp.concatenate(blocks, axis=1)


def step_bits(core, chips):
    bits = [1 << n for n in range(chips.bit_length() - 1)]
    for n in range(0, len(bits) - 1, 2) if core else ():
        bits[n], bits[n + 1] = bits[n + 1], bits[n]
    return bits


def mask_of(i, core, chips):
    masks = []
    for which in range(2):
        bits = step_bits(which, chips)
        masks.append(sum(bit for n, bit in enumerate(bits) if i >> (len(bits) - 1 - n) & 1))
    return jnp.where(core == 0, masks[0], masks[1])


def slot_of(mask, core, chips):
    slots = []
    for which in range(2):
        bits = step_bits(which, chips)
        slot = 0
        for n, bit in enumerate(bits):
            slot = slot + ((mask >> (bit.bit_length() - 1)) & 1) * (1 << (len(bits) - 1 - n))
        slots.append(slot)
    return jnp.where(core == 0, slots[0], slots[1])


VMEM = pl.BlockSpec(memory_space=pltpu.VMEM)
SMEM = pl.BlockSpec(memory_space=pltpu.SMEM)
FAR = pl.BlockSpec(memory_space=pl.ANY)
LOAD = "load"


def size_of(array):
    return math.prod(array.shape) * jnp.dtype(array.dtype).itemsize


def call(body, name, ins, outs, scratch=(), spare=6, **more):
    loads = [i for i, (space, _) in enumerate(ins) if space is LOAD]
    spaces = [FAR if space is LOAD else space for space, _ in ins]
    arrays = [array for _, array in ins]
    out_specs = [space for space, _ in outs]
    out_shape = [shape for _, shape in outs]
    held = [arrays[i] for i in loads]
    buffers = [pltpu.VMEM(array.shape, array.dtype) for array in held]
    sems = [pltpu.SemaphoreType.DMA((len(held),))] if held else []
    vmem = sum(size_of(array) for array in held)
    vmem += sum(size_of(a) for space, a in list(ins) + list(outs) if space is VMEM)
    vmem += sum(size_of(b) for b in scratch if b.memory_space == pltpu.VMEM)
    moved = sum(size_of(a) for a in arrays + out_shape)

    def wrapped(*refs):
        inputs = list(refs[: len(ins)])
        outputs = refs[len(ins) : len(ins) + len(outs)]
        rest = refs[len(ins) + len(outs) :]
        kept, tail = rest[: len(held)], rest[len(held) :]
        copies = []
        if held:
            sem, tail = tail[0], tail[1:]
            copies = [
                pltpu.make_async_copy(inputs[i], kept[n], sem.at[n]) for n, i in enumerate(loads)
            ]
        for copy in copies:
            copy.start()
        for n, i in enumerate(loads):
            inputs[i] = kept[n]

        def arrive():
            for copy in copies:
                copy.wait()

        body(arrive, *inputs, *outputs, *tail)

    single = len(outs) == 1
    return pl.pallas_call(
        wrapped,
        in_specs=spaces,
        out_specs=out_specs[0] if single else out_specs,
        out_shape=out_shape[0] if single else out_shape,
        scratch_shapes=buffers + sems + list(scratch),
        compiler_params=pltpu.CompilerParams(vmem_limit_bytes=vmem + (spare << 20)),
        cost_estimate=pl.CostEstimate(flops=0, bytes_accessed=moved, transcendentals=0),
        name=name,
        **more,
    )(*arrays)


def run_copies(pairs, sems):
    for copy in start_copies(pairs, sems):
        copy.wait()


def slice_copies(group, idx_ref, own, blocks, sibling, wbuf):
    chip, core, zh = idx_ref[0], idx_ref[1], idx_ref[2]
    size = blocks.shape[-2]
    pairs = [(own, wbuf.at[zh])]
    for j in range(blocks.shape[0]):
        for source, owner in ((blocks, core), (sibling, 1 - core)):
            home = chip ^ mask_of(j, owner, blocks.shape[0])
            spot = at((2 * home + owner) * size, size, size)
            pairs.append((source.at[j, 9 * group : 9 * group + 9], wbuf.at[1 - zh, :, spot, :]))
    return pairs


def flat_copies(first, idx_ref, blocks, sibling, buffer):
    chip, core = idx_ref[0], idx_ref[1]
    columns, units = buffer.shape[:2]
    chips = blocks.shape[0]
    count = units // (2 * chips)
    pairs = []
    for j in range(chips):
        for source, owner in ((blocks, core), (sibling, 1 - core)):
            home = chip ^ mask_of(j, owner, chips)
            spot = pl.ds((2 * home + owner) * count, count)
            for c in range(columns):
                begin = first + c * count
                pairs.append((source.at[j, begin : begin + count], buffer.at[c, spot]))
    return pairs


def start_copies(pairs, sems):
    copies = [pltpu.make_async_copy(a, b, sems.at[i]) for i, (a, b) in enumerate(pairs)]
    for copy in copies:
        copy.start()
    return copies


def flat_rows(buffer, begin, count):
    columns, _, size, wide = buffer.shape
    return lanes([buffer[c, pl.ds(begin, count)].reshape(count * size, wide) for c in range(columns)])


def halves(spots, side):
    first = (spots // side + 1) // 2 * side
    return ((0, first), (first, spots - first))


def columns_of(size, wide, side):
    return lax.rem(lax.broadcasted_iota(jnp.int32, (size, wide), 0), side)


def at(start, size, unit):
    return pl.ds(pl.multiple_of(start, unit), size)


def pool_body(arrive, x_ref, out_ref):
    arrive()
    rows, width, chans = x_ref.shape[1:]
    half = width // 2
    pixel = lax.broadcasted_iota(jnp.int32, (half, 2 * width), 1)
    place = lax.broadcasted_iota(jnp.int32, (half, 2 * width), 0)
    inside = (lax.rem(pixel, width) >= 2 * place) & (lax.rem(pixel, width) < 2 * place + 2)
    pick = jnp.where(inside, 0.25, 0.0).astype(bf16)
    for image in range(x_ref.shape[0]):
        for row in range(rows // 2):
            window = x_ref[image, 2 * row : 2 * row + 2].reshape(2 * width, chans)
            out_ref[image, row * half : (row + 1) * half, :] = dot(pick, window).astype(bf16)


def pool(pixels):
    images, rows, width, chans = pixels.shape
    shape = struct((images, rows * width // 4, chans), bf16)
    return call(pool_body, "pool", [(LOAD, pixels)], [(VMEM, shape)])


def widen_body(arrive, idx_ref, g_ref, out_ref):
    arrive()
    rows, width, chans = out_ref.shape[1:]
    half = width // 2
    pixel = lax.broadcasted_iota(jnp.int32, (width, half), 0)
    place = lax.broadcasted_iota(jnp.int32, (width, half), 1)
    inside = (pixel >= 2 * place) & (pixel < 2 * place + 2)
    pick = jnp.where(inside, 0.25, 0.0).astype(bf16)
    for image in range(g_ref.shape[0]):
        for row in range(rows // 2):
            wide = dot(pick, g_ref[image, row * half : (row + 1) * half, :]).astype(bf16)
            out_ref[image, 2 * row] = wide
            out_ref[image, 2 * row + 1] = wide


def widen(idx, grad, rows, width):
    images, spots, chans = grad.shape
    step = images // 4
    block = pl.BlockSpec((step, spots, chans), lambda i: (i, 0, 0))
    out = pl.BlockSpec((step, rows, width, chans), lambda i: (i, 0, 0, 0))
    return call(
        widen_body,
        "widen",
        [(SMEM, idx), (block, grad)],
        [(out, struct((images, rows, width, chans), bf16))],
        grid=(4,),
    )


def conv_body(side, first, group, arrive, idx_ref, *refs):
    zh, zl = idx_ref[2], idx_ref[3]
    if first:
        xl, xa, xh, xd, wl, wo, ws, bl, bo, pre_ref, act_ref, xbuf, wbuf, acc, sems = refs
        chans = xl.shape[1]
        spots = xbuf.shape[0]
        begin = zh * (xl.shape[0] - spots)
        pairs = []
        for source, up, along in ((xl, zh, zl), (xa, zh, 1 - zl), (xh, 1 - zh, zl), (xd, 1 - zh, 1 - zl)):
            if source is xl:
                source = xl.at[at(begin, spots, side), :]
            pairs.append((source, xbuf.at[:, at((2 * up + along) * chans, chans, chans)]))
    else:
        xl, xa, wl, wo, ws, bl, bo, pre_ref, act_ref, xbuf, wbuf, acc, sems = refs
        chans = xl.shape[1] // 2
        spots = xbuf.shape[0]
        pairs = []
        for source, along in ((xl, zl), (xa, 1 - zl)):
            for up in range(2):
                pairs.append(
                    (
                        source.at[:, up * chans : (up + 1) * chans],
                        xbuf.at[:, at((2 * up + along) * chans, chans, chans)],
                    )
                )
    run_copies(slice_copies(group, idx_ref, wl, wo, ws, wbuf) + pairs, sems)
    arrive()
    if first:
        for begin, block in halves(spots, side):
            rows = slice(begin, begin + block)
            xbuf[rows, :] = gelu(xbuf[rows, :].astype(f32)).astype(bf16)
    acc[...] = jnp.zeros_like(acc)
    outs = 2 * wl.shape[2]
    for x in range(3):
        weights = lanes([wbuf[u, 3 * y + x] for y in range(3) for u in range(2)])
        for begin, block in halves(spots, side):
            product = dot(xbuf[begin : begin + block, :], weights)
            for y in range(3):
                place = begin + side * (2 - y)
                acc[x, place : place + block, :] += product[:, y * outs : (y + 1) * outs]
    own, other = bl[...], bo[...]
    bias = lanes([jnp.where(zh == 0, own, other), jnp.where(zh == 0, other, own)])
    for begin, block in halves(act_ref.shape[0], side):
        column = columns_of(block, outs, side)
        spot = at(begin + side + zh * side, block, side)
        left = pltpu.roll(acc[0, spot, :], 1, 0)
        right = pltpu.roll(acc[2, spot, :], block - 1, 0)
        pre = acc[1, spot, :] + bias
        pre = pre + jnp.where(column > 0, left, 0.0)
        pre = pre + jnp.where(column < side - 1, right, 0.0)
        pre_ref[begin : begin + block, :] = pre
        act_ref[begin : begin + block, :] = gelu(pre).astype(bf16)


def conv(side, idx, sources, own, other, group, bias, bias_other, first=False):
    taps, depth, outs = own.shape
    spots = sources[1].shape[0]
    rows = spots - side
    return call(
        functools.partial(conv_body, side, first, group),
        "conv",
        [(SMEM, idx)]
        + [(FAR, s) for s in sources]
        + [(FAR, own), (FAR, other[0]), (FAR, other[1])]
        + [(VMEM, bias.reshape(1, outs)), (VMEM, bias_other.reshape(1, outs))],
        [(VMEM, struct((rows, 2 * outs), f32)), (VMEM, struct((rows, 2 * outs), bf16))],
        [
            pltpu.VMEM((spots, depth), bf16),
            pltpu.VMEM((2, taps, depth, outs), bf16),
            pltpu.VMEM((3, spots + 2 * side, 2 * outs), f32),
            pltpu.SemaphoreType.DMA((2 * other[0].shape[0] + 5,)),
        ],
        spare=14 if first else 8,
    )


def spread_taps(side, grad, taps_ref):
    pixels, outs = grad.shape
    column = columns_of(pixels, outs, side)
    wide = grad.astype(f32)
    ahead = jnp.where(column < side - 1, pltpu.roll(wide, pixels - 1, 0), 0.0).astype(bf16)
    behind = jnp.where(column > 0, pltpu.roll(wide, 1, 0), 0.0).astype(bf16)
    edge = jnp.zeros((side, 3 * outs), bf16)
    taps_ref[:side, :] = edge
    taps_ref[side + pixels :, :] = edge
    taps_ref[side : side + pixels, :] = jnp.concatenate([ahead, grad, behind], axis=1)


def tap_block(side, taps_ref, begin, block):
    return lanes([taps_ref[at(begin + side * (2 - y), block, side), :] for y in range(3)])


def slope_body(side, arrive, idx_ref, keep_ref, recv_ref, pre_ref, mine_ref, theirs_ref, gp_ref):
    arrive()
    zh = idx_ref[2]
    half, outs = mine_ref.shape
    total = keep_ref[...] + recv_ref[...].astype(f32)
    spots = keep_ref.shape[0]
    pre = pre_ref[at(zh * (pre_ref.shape[0] - spots), spots, side), :]
    gp_ref[...] = (total * gelu_slope(pre)).astype(bf16)
    own = gp_ref[at(zh * (gp_ref.shape[0] - half), half, side), :]
    low, high = own[:, :outs], own[:, outs:]
    mine_ref[...] = jnp.where(zh == 0, low, high)
    theirs_ref[...] = jnp.where(zh == 0, high, low)


def slope_back(side, idx, keep, recv, pre, half):
    outs = pre.shape[1] // 2
    return call(
        functools.partial(slope_body, side),
        "slope_back",
        [(SMEM, idx), (VMEM, keep), (VMEM, recv), (LOAD, pre)],
        [
            (VMEM, struct((half, outs), bf16)),
            (VMEM, struct((half, outs), bf16)),
            (VMEM, struct(keep.shape, bf16)),
        ],
    )


def back_body(side, last, group, arrive, idx_ref, *refs):
    zh, zl = idx_ref[2], idx_ref[3]
    if last:
        valid_ref, grad_ref, x_ref, go_ref, far_ref, idk_ref, wl, wo, ws, po, ps = refs[:11]
        own_ref, give_ref, taps_ref, wbuf, idk_far, sems = refs[11:]
    else:
        keep_ref, recv_ref, pre_ref, wl, wo, ws, gp_ref, own_ref, give_ref, taps_ref, wbuf, sems = refs
    pairs = slice_copies(group, idx_ref, wl, wo, ws, wbuf)
    if last:
        pairs += flat_copies(9, idx_ref, po, ps, idk_far)
    copies = start_copies(pairs, sems)
    arrive()
    if last:
        grad = grad_ref[...]
    else:
        spots = gp_ref.shape[0]

        def window(ref):
            return ref[at(zh * (ref.shape[0] - spots), spots, side), :]

        total = window(keep_ref) + window(recv_ref).astype(f32)
        grad = (total * gelu_slope(window(pre_ref))).astype(bf16)
        gp_ref[...] = grad
    spread_taps(side, grad, taps_ref)
    depth, outs = wl.shape[1:]
    pixels = own_ref.shape[-2]
    start = zh * side
    for copy in copies:
        copy.wait()
    chans = depth // 4

    def rows(index):
        spot = at(index * chans, chans, chans)
        return lanes([wbuf[u, t, spot, :] for t in range(9) for u in range(2)])

    for target, along in ((give_ref, 1 - zl), (own_ref, zl)):
        if last:
            units = chans // idk_far.shape[2]
            for up in range(2):
                index = 2 * up + along
                weights = rows(index)
                near = idk_ref[at(index * chans, chans, chans), :]
                far = flat_rows(idk_far, index * units, units)
                apart = zh * (far_ref.shape[0] - pixels)
                for begin, block in halves(pixels, side):
                    here = at(zh * pixels + begin, block, side)
                    part = dot(tap_block(side, taps_ref, start + begin, block), weights, NT)
                    x = x_ref[here, at(index * chans, chans, chans)]
                    part = part * gelu_slope(x.astype(f32))
                    part = part + dot(go_ref[here, :], near, NT)
                    part = part + valid_ref[0] * dot(far_ref[at(apart + begin, block, side), :], far, NT)
                    target[up, begin : begin + block, :] = part.astype(target.dtype)
        else:
            weights = jnp.concatenate([rows(along), rows(2 + along)], axis=0)
            for begin, block in halves(pixels, side):
                part = dot(tap_block(side, taps_ref, start + begin, block), weights, NT)
                target[begin : begin + block, :] = part.astype(target.dtype)


def back(side, idx, sources, own, other, group, last=None):
    taps, depth, outs = own.shape
    spots = min(sources[0].shape[0], sources[-1].shape[0])
    copies = 2 * other[0].shape[0] + 1
    extra = []
    scratch = []
    if last:
        valid, full_x, go, cot_far, idk, pieces, half = last
        chans = depth // 4
        shape = (2, half, chans)
        results = []
        extra = [(FAR, pieces[0]), (FAR, pieces[1])]
        sources = list(sources) + [full_x, go, cot_far, idk]
        columns, size = idk.shape[1] // 128, pieces[0].shape[2]
        scratch = [pltpu.VMEM((columns, depth // size, size, 128), bf16)]
        copies += 2 * other[0].shape[0] * columns
    else:
        shape = (spots - side, depth // 2)
        results = [(VMEM, struct((spots, 2 * outs), bf16))]
    results += [(VMEM, struct(shape, f32)), (VMEM, struct(shape, bf16))]
    return call(
        functools.partial(back_body, side, bool(last), group),
        "back",
        [(SMEM, idx)]
        + ([(SMEM, last[0])] if last else [])
        + [(LOAD, source) for source in sources]
        + [(FAR, own), (FAR, other[0]), (FAR, other[1])]
        + extra,
        results,
        [pltpu.VMEM((spots + 2 * side, 6 * outs), bf16), pltpu.VMEM((2, taps, depth, outs), bf16)]
        + scratch
        + [pltpu.SemaphoreType.DMA((copies,))],
        spare=14 if last else 10,
    )


def put_blocks(idx_ref, keep_ref, give_ref, part, tap, first_block, size, begin=0):
    chip, core = idx_ref[0], idx_ref[1]
    for b in range(0, part.shape[0] // size, 2):
        even = part[b * size : (b + 1) * size, :]
        odd = part[(b + 1) * size : (b + 2) * size, :]
        mask = chip ^ ((first_block + b) // 2)
        slot = slot_of(mask, core, keep_ref.shape[0])
        give_slot = slot_of(mask, 1 - core, keep_ref.shape[0])
        rows = slice(begin + tap * size, begin + (tap + 1) * size)
        keep_ref[slot, rows, :] = jnp.where(core == 0, even, odd).astype(bf16)
        give_ref[give_slot, rows, :] = jnp.where(core == 0, odd, even).astype(bf16)


def weight_body(side, half, flat, arrive, idx_ref, gp_ref, *refs):
    if flat:
        full_ref, go_ref, bias_ref = refs[:3]
        refs = refs[3:]
    xl, xa, keep_ref, give_ref, xbuf, taps_ref, sems = refs
    arrive()
    zh, zl = idx_ref[2], idx_ref[3]
    chans = xl.shape[1] // 2
    spots = xbuf.shape[0]
    window = at(zh * (xl.shape[0] - spots), spots, side)
    pairs = []
    for source, along in ((xl, zl), (xa, 1 - zl)):
        for up in range(2):
            pairs.append(
                (
                    source.at[window, up * chans : (up + 1) * chans],
                    xbuf.at[:, at((2 * up + along) * chans, chans, chans)],
                )
            )
    run_copies(pairs, sems)
    wide = gp_ref.shape[1]
    outs = wide // 2
    spot = lax.broadcasted_iota(jnp.int32, (spots, wide), 0) - zh * side
    grad = gp_ref[at(zh * (gp_ref.shape[0] - spots), spots, side), :].astype(f32)
    grad = jnp.where((spot >= 0) & (spot < half), grad, 0.0)
    bias = jnp.sum(grad, axis=0, keepdims=True)
    spread_taps(side, grad.astype(bf16), taps_ref)
    blocks = 2 * keep_ref.shape[0]
    depth = xbuf.shape[1]
    size = depth // blocks
    for begin in range(0, depth, 256):
        values = xbuf[:, begin : begin + 256]
        for y in range(3):
            place = side * (2 - y)
            part = dot(values, taps_ref[place : place + spots, :], TN)
            for x in range(3):
                for u in range(2):
                    col = x * wide + u * outs
                    put_blocks(
                        idx_ref, keep_ref, give_ref, part[:, col : col + outs],
                        3 * y + x, begin // size, size, u * (9 * size + 16),
                    )
    for u in range(2):
        row = jnp.broadcast_to(bias[:, u * outs : (u + 1) * outs], (16, outs)).astype(bf16)
        for j in range(keep_ref.shape[0]):
            spot = slice(u * (9 * size + 16) + 9 * size, (u + 1) * (9 * size + 16))
            keep_ref[j, spot, :] = row
            give_ref[j, spot, :] = row
    if flat:
        first = 2 * (9 * size + 16)
        flat_pieces(1.0, idx_ref, full_ref, go_ref, bias_ref, keep_ref, give_ref, first)


def weight_grad(side, half, idx, grad, act, act_other, chips, flat=()):
    spots = half + side
    wide = grad.shape[1]
    outs = wide // 2
    depth = 2 * act.shape[1]
    rows = 2 * (9 * depth // (2 * chips) + 16)
    if flat:
        rows += flat_size(flat[0], flat[1], chips)
    return call(
        functools.partial(weight_body, side, half, bool(flat)),
        "weight_grad",
        [(SMEM, idx), (LOAD, grad)] + [(LOAD, a) for a in flat] + [(FAR, act), (FAR, act_other)],
        [(VMEM, struct((chips, rows, outs), bf16))] * 2,
        [
            pltpu.VMEM((spots, depth), bf16),
            pltpu.VMEM((spots + 2 * side, 3 * wide), bf16),
            pltpu.SemaphoreType.DMA((4,)),
        ],
        spare=10,
    )


def weight_one_body(side, arrive, idx_ref, mine_ref, theirs_ref, x_ref, *refs):
    keep_ref, give_ref, gp_ref, taps_ref = refs
    arrive()
    zh = idx_ref[2]
    half, outs = mine_ref.shape
    gp_ref[at(zh * half, half, side), :] = mine_ref[...]
    gp_ref[at((1 - zh) * half, half, side), :] = theirs_ref[...]
    grad = gp_ref[...]
    bias = jnp.sum(grad.astype(f32), axis=0, keepdims=True)
    spread_taps(side, grad, taps_ref)
    blocks = 2 * keep_ref.shape[0]
    spots, depth = x_ref.shape
    size = depth // blocks
    right = tap_block(side, taps_ref, 0, spots)
    for begin in range(0, depth, 256):
        part = dot(x_ref[:, begin : begin + 256], right, TN)
        for tap in range(9):
            put_blocks(
                idx_ref, keep_ref, give_ref, part[:, tap * outs : (tap + 1) * outs],
                tap, begin // size, size,
            )
    row = jnp.broadcast_to(bias, (16, outs)).astype(bf16)
    first = 9 * size + 16
    for j in range(keep_ref.shape[0]):
        keep_ref[j, 9 * size : first, :] = row
        give_ref[j, 9 * size : first, :] = row


def weight_one_grad(side, idx, mine, theirs, act_zero, chips):
    spots, depth = act_zero.shape
    outs = mine.shape[1]
    rows = 9 * depth // (2 * chips) + 16
    return call(
        functools.partial(weight_one_body, side),
        "weight_one_grad",
        [(SMEM, idx), (LOAD, mine), (LOAD, theirs), (LOAD, act_zero)],
        [(VMEM, struct((chips, rows, outs), bf16))] * 2,
        [
            pltpu.VMEM((spots, outs), bf16),
            pltpu.VMEM((spots + 2 * side, 3 * outs), bf16),
        ],
        spare=14,
    )


def fold_body(pairs, arrive, idx_ref, *refs):
    arrive()
    ins, (keep_ref, give_ref) = refs[: 2 * pairs], refs[2 * pairs :]
    half = keep_ref.shape[0]
    for i in range(2 * half):
        target = keep_ref if i < half else give_ref
        begin = 0
        for keep, recv in zip(ins[0::2], ins[1::2]):
            rows = keep.shape[1]
            total = keep[i].astype(f32) + recv[i].astype(f32)
            target[i % half, begin : begin + rows, :] = total.astype(bf16)
            begin += rows


def fold(idx, *arrays):
    blocks, _, wide = arrays[0].shape
    rows = sum(a.shape[1] for a in arrays[0::2])
    return call(
        functools.partial(fold_body, len(arrays) // 2),
        "fold",
        [(SMEM, idx)] + [(VMEM, a) for a in arrays],
        [(VMEM, struct((blocks // 2, rows, wide), bf16))] * 2,
    )


def last_body(slotted, rest, arrive, idx_ref, keep_in, recv_in, *targets):
    arrive()
    zh = idx_ref[2]

    def put(target, place, begin, rows):
        spot = at(begin, rows, 16)
        total = keep_in[0, spot, :].astype(f32) + recv_in[0, spot, :].astype(f32)
        target[place : place + rows, :] = total.astype(bf16)

    place = 0
    for begin, rows in slotted:
        put(targets[0], place, begin + zh * rows, rows)
        put(targets[1], place, begin + (1 - zh) * rows, rows)
        place += rows
    begin, rows = rest
    put(targets[-1], 0, begin, rows)


def last_fold(idx, keep, recv, slotted=(), rest=None):
    wide = keep.shape[2]
    rest = rest or (0, keep.shape[1])
    rows = sum(size for _, size in slotted)
    sizes = ([rows, rows] if slotted else []) + [rest[1]]
    return call(
        functools.partial(last_body, slotted, rest),
        "last_fold",
        [(SMEM, idx), (VMEM, keep), (VMEM, recv)],
        [(VMEM, struct((size, wide), bf16)) for size in sizes],
    )


def final_body(parts, arrive, idx_ref, own_ref, sib_ref, *refs):
    arrive()
    outs, stages, sems = refs[: 2 * len(parts)], refs[2 * len(parts) : -1], refs[-1]
    chip, core = idx_ref[0], idx_ref[1]
    chips, _, wide = own_ref.shape
    first = 0
    copies = []

    def store(source, target):
        copies.append(pltpu.make_async_copy(source, target, sems.at[len(copies)]))
        copies[-1].start()

    for n, part in enumerate(parts):
        grad_ref, bias_ref, stage = outs[2 * n], outs[2 * n + 1], stages[n]
        size = part[0] // (2 * chips)
        columns = 1 if len(part) == 1 else part[1] // wide
        end = first + size * (9 if len(part) == 1 else columns)
        for c in range(columns):
            row = own_ref[0, end + c : end + c + 1, :].astype(f32)
            bias_ref[:, c * wide : (c + 1) * wide] = row
        for n_row, begin in enumerate(range(first, end, size)):
            for j in range(chips):
                for source, owner in ((own_ref, core), (sib_ref, 1 - core)):
                    home = chip ^ mask_of(j, owner, chips)
                    spot = at((2 * home + owner) * size, size, size)
                    piece = source[j, begin : begin + size, :].astype(f32)
                    if len(part) == 1:
                        stage[n_row, spot, :] = piece
                    else:
                        stage[spot, n_row * wide : (n_row + 1) * wide] = piece
            if len(part) == 1:
                store(stage.at[n_row], grad_ref.at[n_row])
        if len(part) > 1:
            store(stage, grad_ref)
        first = end + 16
    for copy in copies:
        copy.wait()


def final_grads(idx, own, sib, parts):
    wide = own.shape[2]
    results, stages = [], []
    for part in parts:
        shape = (9, part[0], wide) if len(part) == 1 else part
        results += [(FAR, struct(shape, f32)), (VMEM, struct((1, shape[-1]), f32))]
        stages.append(pltpu.VMEM(shape, f32))
    copies = sum(9 if len(part) == 1 else 1 for part in parts)
    return call(
        functools.partial(final_body, parts),
        "final_grads",
        [(SMEM, idx), (VMEM, own), (VMEM, sib)],
        results,
        stages + [pltpu.SemaphoreType.DMA((copies,))],
    )


def flat_pieces(gain, idx_ref, x_ref, go_ref, bias_ref, keep_ref, give_ref, first):
    chip, core = idx_ref[0], idx_ref[1]
    chips, _, wide = keep_ref.shape
    columns = go_ref.shape[1] // wide
    size = x_ref.shape[1] // (2 * chips)
    bias = jnp.concatenate(
        [bias_ref[:, c * wide : (c + 1) * wide] for c in range(columns)]
        + [jnp.zeros((16 - columns, wide), f32)],
        axis=0,
    ).astype(bf16)
    for j in range(chips):
        keep_ref[j, first + columns * size :, :] = bias
        give_ref[j, first + columns * size :, :] = bias
    for begin in range(0, x_ref.shape[1], 256):
        part = gain * dot(x_ref[:, begin : begin + 256], go_ref[...], TN)
        for b in range(0, 256 // size, 2):
            mask = chip ^ ((begin // size + b) // 2)
            slot = slot_of(mask, core, chips)
            give_slot = slot_of(mask, 1 - core, chips)
            for c in range(columns):
                even = part[b * size : (b + 1) * size, c * wide : (c + 1) * wide]
                odd = part[(b + 1) * size : (b + 2) * size, c * wide : (c + 1) * wide]
                spot = slice(first + c * size, first + (c + 1) * size)
                keep_ref[slot, spot, :] = jnp.where(core == 0, even, odd).astype(bf16)
                give_ref[give_slot, spot, :] = jnp.where(core == 0, odd, even).astype(bf16)


def flat_size(x, go, chips):
    return (go.shape[1] // 128) * (x.shape[1] // (2 * chips)) + 16


def outer_body(gain, arrive, idx_ref, x_ref, go_ref, bias_ref, keep_ref, give_ref):
    arrive()
    flat_pieces(gain, idx_ref, x_ref, go_ref, bias_ref, keep_ref, give_ref, 0)


def outer(idx, x, go, gain, bias, chips):
    return call(
        functools.partial(outer_body, gain),
        "outer",
        [(SMEM, idx), (LOAD, x), (LOAD, go), (LOAD, bias)],
        [(VMEM, struct((chips, flat_size(x, go, chips), 128), bf16))] * 2,
        spare=8,
    )


def start_body(arrive, idx_ref, valid_ref, cot_ref, outk_ref, go_ref, bias_ref, own_ref, give_ref):
    arrive()
    zl = idx_ref[3]
    masked = cot_ref[...].astype(f32) * valid_ref[0]
    go_ref[...] = masked.astype(bf16)
    bias_ref[...] = jnp.sum(masked, axis=0, keepdims=True)
    chans = outk_ref.shape[0] // 4
    block = cot_ref.shape[0] // 4
    for target, along in ((give_ref, 1 - zl), (own_ref, zl)):
        weights = jnp.concatenate(
            [outk_ref[at((2 * up + along) * chans, chans, chans), :] for up in range(2)], axis=0
        )
        for begin in range(0, cot_ref.shape[0], block):
            part = post_gain * dot(go_ref[begin : begin + block, :], weights, NT)
            target[begin : begin + block, :] = part.astype(target.dtype)


def start_back(idx, valid, cot, outk):
    spots, outs = cot.shape
    half = outk.shape[0] // 2
    return call(
        start_body,
        "start_back",
        [(SMEM, idx), (SMEM, valid), (LOAD, cot), (LOAD, outk)],
        [
            (VMEM, struct(cot.shape, bf16)),
            (VMEM, struct((1, outs), f32)),
            (VMEM, struct((spots, half), f32)),
            (VMEM, struct((spots, half), bf16)),
        ],
    )


def rows_body(side, arrive, idx_ref, own_ref, recv_ref, keep_ref, give_ref):
    arrive()
    zh = idx_ref[2]
    spots = keep_ref.shape[0]
    apart = own_ref.shape[0] - spots
    for target, begin in ((give_ref, (1 - zh) * apart), (keep_ref, zh * apart)):
        spot = at(begin, spots, side)
        total = own_ref[spot, :] + recv_ref[spot, :].astype(f32)
        target[...] = total.astype(target.dtype)


def rows_sum(side, idx, own, recv, spots):
    shape = (spots, own.shape[1])
    return call(
        functools.partial(rows_body, side),
        "rows_sum",
        [(SMEM, idx), (LOAD, own), (LOAD, recv)],
        [(VMEM, struct(shape, f32)), (VMEM, struct(shape, bf16))],
    )


def slots_body(arrive, idx_ref, own_ref, recv_ref, keep_ref, give_ref):
    arrive()
    zh = idx_ref[2]
    for target, slot in ((give_ref, 1 - zh), (keep_ref, zh)):
        total = own_ref[slot] + recv_ref[slot].astype(f32)
        target[...] = total.astype(bf16)


def slots_sum(idx, own, recv):
    shape = struct(own.shape[1:], bf16)
    return call(
        slots_body,
        "slots_sum",
        [(SMEM, idx), (VMEM, own), (VMEM, recv)],
        [(VMEM, shape), (VMEM, shape)],
    )


def input_body(arrive, idx_ref, keep_ref, recv_ref, out_ref):
    arrive()
    zh = idx_ref[2]
    half = keep_ref.shape[0]
    out_ref[at(zh * half, half, half), :] = keep_ref[...]
    out_ref[at((1 - zh) * half, half, half), :] = recv_ref[...]


def input_grad(idx, keep, recv):
    half, chans = keep.shape
    return call(
        input_body,
        "input_grad",
        [(SMEM, idx), (VMEM, keep), (VMEM, recv)],
        [(VMEM, struct((2 * half, chans), bf16))],
    )


def whole_body(side, arrive, idx_ref, xl, xa, xh, xd, rh, rl, x_ref, act_ref, sems):
    arrive()
    zh, zl = idx_ref[2], idx_ref[3]
    chans = xl.shape[1]
    spots = xa.shape[0]
    rest = xl.shape[0] - spots
    window, outside = at(zh * rest, spots, side), at((1 - zh) * spots, rest, side)

    def cols(up, along):
        return at((2 * up + along) * chans, chans, chans)

    run_copies(
        [
            (xl, x_ref.at[:, cols(zh, zl)]),
            (xa, x_ref.at[window, cols(zh, 1 - zl)]),
            (xh, x_ref.at[window, cols(1 - zh, zl)]),
            (xd, x_ref.at[window, cols(1 - zh, 1 - zl)]),
            (rl.at[0], x_ref.at[outside, cols(zh, 1 - zl)]),
            (rh, x_ref.at[outside, cols(1 - zh, zl)]),
            (rl.at[1], x_ref.at[outside, cols(1 - zh, 1 - zl)]),
        ],
        sems,
    )
    block = x_ref.shape[0] // 8
    for begin in range(0, x_ref.shape[0], block):
        rows = slice(begin, begin + block)
        act_ref[rows, :] = gelu(x_ref[rows, :].astype(f32)).astype(bf16)


def whole_input(side, idx, *parts):
    spots, chans = parts[0].shape
    return call(
        functools.partial(whole_body, side),
        "whole_input",
        [(SMEM, idx)] + [(FAR, p) for p in parts],
        [(VMEM, struct((spots, 4 * chans), bf16))] * 2,
        [pltpu.SemaphoreType.DMA((7,))],
    )


def join_body(arrive, idx_ref, own, recv, far_own, far_recv, out, sems):
    arrive()
    zh, zl = idx_ref[2], idx_ref[3]
    half = own.shape[0]
    chans = own.shape[1] // 2
    pairs = []
    for source, up, along in ((own, zh, zl), (recv, zh, 1 - zl), (far_own, 1 - zh, zl), (far_recv, 1 - zh, 1 - zl)):
        for slot in range(2):
            spot = at((2 * slot + along) * chans, chans, chans)
            target = out.at[at(up * half, half, half), spot]
            pairs.append((source.at[:, slot * chans : (slot + 1) * chans], target))
    run_copies(pairs, sems)


def join(idx, *parts):
    half, wide = parts[0].shape
    return call(
        join_body,
        "join",
        [(SMEM, idx)] + [(FAR, p) for p in parts],
        [(VMEM, struct((2 * half, 2 * wide), bf16))],
        [pltpu.SemaphoreType.DMA((8,))],
    )


def finish_body(arrive, idx_ref, valid_ref, x_ref, act_ref, idk_ref, outk_ref, ib_ref, out_ref):
    arrive()
    block = x_ref.shape[0] // 4
    for begin in range(0, x_ref.shape[0], block):
        rows = slice(begin, begin + block)
        identity = dot(x_ref[rows, :], idk_ref[...]) + ib_ref[...]
        branch = dot(act_ref[rows, :], outk_ref[...])
        out_ref[rows, :] = ((identity + post_gain * branch) * valid_ref[0]).astype(bf16)


def finish(idx, valid, x, act, idk, outk, ib):
    outs = idk.shape[1]
    return call(
        finish_body,
        "finish",
        [(SMEM, idx), (SMEM, valid), (LOAD, x), (LOAD, act), (LOAD, idk), (LOAD, outk)]
        + [(VMEM, ib.reshape(1, outs))],
        [(VMEM, struct((x.shape[0], outs), bf16))],
        spare=8,
    )


def flip(value, axis):
    return lax.ppermute(value, axis, [(0, 1), (1, 0)])


def cross(value, step, chips):
    pairs = []
    for chip in range(chips):
        for core in range(2):
            other = chip ^ step_bits(core, chips)[step]
            pairs.append((2 * chip + core, 2 * other + core))
    return lax.ppermute(value, DP, pairs)


def hops(value, chips):
    blocks = [value]
    for i in range(1, chips):
        pairs = []
        for chip in range(chips):
            for core in range(2):
                bits = step_bits(core, chips)
                mask = sum(bit for n, bit in enumerate(bits) if i >> (len(bits) - 1 - n) & 1)
                pairs.append((2 * (chip ^ mask) + core, 2 * chip + core))
        blocks.append(lax.ppermute(value, DP, pairs))
    return blocks


def swap(pieces, axis):
    return lax.all_to_all(pieces, axis, split_axis=0, concat_axis=0, tiled=True)


def after(value, other):
    return lax.optimization_barrier((value, other))[0]


def rows_of(value, start, size):
    return lax.dynamic_slice_in_dim(value, start, size, 0)


def local(
    pixels,
    counts,
    kernel_one,
    bias_one,
    kernel_two,
    bias_two,
    kernel_three,
    bias_three,
    out_kernel,
    identity_kernel,
    identity_bias,
    cotangent,
):
    images, rows, width, chans = pixels.shape
    side = width // 2
    spots = side * side
    half = spots // 2
    window = half + halo * side
    outs = cotangent.shape[3]
    chips = lax.axis_size("chip")
    chip, core, zh, zl = [lax.axis_index(a) for a in ("chip", "core", "zh", "zl")]
    idx = jnp.stack([chip, core, zh, zl]).astype(jnp.int32)
    taps = lambda kernel: kernel.reshape((9,) + kernel.shape[2:])
    one, two, three = taps(kernel_one), taps(kernel_two), taps(kernel_three)

    own_count = lax.dynamic_index_in_dim(counts, 2 * chip + core, 0, keepdims=True)
    valid = (own_count > 0).astype(f32)

    place = 2 * chip + core

    def units_of(kernel, size):
        if kernel.ndim == 3:
            block = kernel.shape[1] // (2 * chips)
            return lax.dynamic_slice_in_dim(kernel, place * block, block, 1)
        block = kernel.shape[0] // (2 * chips)
        block = lax.dynamic_slice_in_dim(kernel, place * block, block, 0)
        block = block.reshape(-1, size, block.shape[1] // 128, 128)
        return block.transpose(2, 0, 1, 3).reshape(-1, size, 128)

    steps = chips.bit_length() - 1

    def start_spread(piece, *others):
        return jnp.concatenate(after((piece[None], cross(piece[None], steps - 1, chips)), others))

    def end_spread(own, *others):
        for step in reversed(range(steps - 1)):
            own = jnp.concatenate(after((own, cross(own, step, chips)), others))
        return own, flip(own, "core")

    last = [idx]

    def turn(*others):
        return after(idx, (last[0],) + others)

    def ran(results):
        last[0] = results[-1] if isinstance(results, (list, tuple)) else results
        return results

    size = two.shape[1] // (2 * chips)
    deep = two.shape[1]
    cot = cotangent.reshape(spots, outs)
    one_piece = flip(units_of(one, size), "zh")
    pooled = ran(pool(pixels))
    go, identity_bias_grad, ga_own, ga_give = ran(start_back(turn(), valid, cot, out_kernel))
    bias_other = flip(after(jnp.stack([bias_one, bias_two, bias_three]), go), "zh")
    two_piece = units_of(after(two, pooled), size)
    last_piece = jnp.concatenate([units_of(after(k, pooled), size) for k in (three, identity_kernel)])
    cot_rows = rows_of(after(cot, pooled), (1 - zh) * half, half)
    xl = swap(after(pooled, (one_piece, two_piece, last_piece, cot_rows, ga_give)), DP)
    xl = xl.reshape(spots, chans)
    two_piece = flip(after(two_piece, one_piece), "zh")

    apart = spots - window
    xa = flip(rows_of(xl, zh * apart, window), "zl")
    xh = flip(rows_of(xl, (1 - zh) * apart, window), "zh")
    rest = spots - window
    rest_own = rows_of(xl, (1 - zh) * window, rest)
    rest_high = rows_of(xl, zh * window, rest)
    two_near = start_spread(after(two_piece, xl))
    one_near = start_spread(after(one_piece, xl), xh, xa, two_near, bias_other)
    xd = flip(xh, "zl")
    last_piece = flip(after(last_piece, xh), "zh")
    two_other = end_spread(two_near, xd)
    one_other = end_spread(one_near, xd, two_other[0], last_piece)
    ga_recv = flip(after(ga_give, xd), "zl")
    rest_high = flip(after(rest_high, xd), "zh")

    pre_one, act_one = ran(
        conv(
            side, turn(), (xl, xa, xh, xd), one, one_other, 0, bias_one, bias_other[0], True
        )
    )
    act_one_other = flip(act_one, "zl")
    ga_own, ga_give = ran(rows_sum(side, turn(), ga_own, ga_recv, half + (halo - 3) * side))
    pre_two, act_two = ran(
        conv(side, turn(), (act_one, act_one_other), two, two_other, 0, bias_two, bias_other[1])
    )
    act_two_other = flip(act_two, "zl")
    ga_recv = flip(after(ga_give, act_two), "zh")
    last_other = jnp.stack(after(hops(after(last_piece, act_one), chips), act_two))
    last_other = last_other, flip(last_other, "core")
    pre_three, act_three = ran(
        conv(side, turn(), (act_two, act_two_other), three, last_other, 0, bias_three, bias_other[2])
    )
    rest_low = flip(jnp.stack(after((rest_own, rest_high), act_three)), "zl")
    cot_far = flip(after(cot_rows, act_three), "zh")
    own_rows = rows_of(act_three, zh * (halo - 3) * side, half)

    gp_three, ga_own, ga_give = ran(
        back(side, turn(), (ga_own, ga_recv, pre_three), three, last_other, 0)
    )
    ga_recv = flip(ga_give, "zl")
    full_x, act_zero = ran(whole_input(side, turn(), xl, xa, xh, xd, rest_high, rest_low))
    keep_three, give_three = ran(
        weight_grad(
            side, half, turn(), gp_three, act_two, act_two_other, chips, (full_x, go, identity_bias_grad)
        )
    )
    gp_two, ga_own, ga_give = ran(
        back(side, turn(), (ga_own, ga_recv, pre_two), two, two_other, 0)
    )
    ga_recv = flip(ga_give, "zl")
    keep_two, give_two = ran(weight_grad(side, half, turn(cot_far), gp_two, act_one, act_one_other, chips))

    gp_mine, gp_theirs, gp_one = ran(slope_back(side, turn(), ga_own, ga_recv, pre_one, half))
    gp_theirs = flip(gp_theirs, "zh")
    recv_three = flip(after(give_three, gp_one), "core")
    recv_two = flip(after(give_two, gp_one), "core")
    gx_own, gx_give = ran(
        back(
            side, turn(), (gp_one,), one, one_other, 0,
            (valid, full_x, go, cot_far, identity_kernel, last_other, half),
        )
    )

    def folds(keep, recv, first, *others):
        for step in range(first, steps):
            keep, give = ran(fold(turn(*others), keep, recv))
            recv = cross(give, step, chips)
        return keep, recv

    keep_deep, give_deep = ran(fold(turn(gp_theirs), keep_three, recv_three, keep_two, recv_two))
    recv_deep = cross(give_deep, 0, chips)
    gx_recv = flip(after(gx_give, keep_deep), "zl")
    own_rows = after(own_rows, keep_deep)
    near_rows = flip(own_rows, "zl")
    far_rows = flip(own_rows, "zh")
    keep_one, give_one = ran(weight_one_grad(side, turn(), gp_mine, gp_theirs, act_zero, chips))
    recv_one = flip(give_one, "core")
    keep_deep, recv_deep = folds(keep_deep, recv_deep, 1, far_rows)
    gx_keep, gx_give = ran(slots_sum(turn(), gx_own, gx_recv))
    gx_recv = flip(gx_give, "zh")
    keep_one, give_one = ran(fold(turn(), keep_one, recv_one))
    recv_one = cross(give_one, 0, chips)
    slot = 9 * size + 16
    flat = keep_three.shape[1] - 2 * slot
    keep_deep, give_deep, id_rows = ran(
        last_fold(
            turn(), keep_deep, recv_deep, ((0, slot), (2 * slot + flat, slot)), (2 * slot, flat)
        )
    )
    recv_deep = flip(give_deep, "zh")
    far_near_rows = flip(after(far_rows, keep_deep), "zl")
    keep_one, recv_one = folds(keep_one, recv_one, 1)
    full_three = ran(join(turn(), own_rows, near_rows, far_rows, far_near_rows))
    keep_out, give_out = ran(outer(turn(), full_three, go, post_gain, identity_bias_grad, chips))
    recv_out = flip(give_out, "core")
    (total_one,) = ran([last_fold(turn(), keep_one, recv_one)])
    keep_out, give_out = ran(fold(turn(), keep_out, recv_out))
    recv_out = cross(give_out, 0, chips)
    gx = ran(input_grad(turn(), gx_keep, gx_recv))
    gx = swap(gx.reshape(images, rows * width // 4, chans), DP)
    deep_rows = (after(keep_deep, keep_out).astype(f32) + recv_deep.astype(f32)).astype(bf16)
    deep_rows = jnp.concatenate([deep_rows, id_rows])
    near_deep = start_spread(deep_rows)
    block_out = ran(
        finish(turn(deep_rows), valid, full_x, full_three, identity_kernel, out_kernel, identity_bias)
    )
    keep_out, recv_out = folds(keep_out, recv_out, 1)
    (total_out,) = ran([last_fold(turn(), keep_out, recv_out)])
    near_one = start_spread(jnp.concatenate([total_one, total_out]))
    pixels_grad = ran(widen(turn(near_one, near_deep), gx, rows, width))
    all_deep = end_spread(near_deep, pixels_grad)
    all_one = end_spread(near_one)
    (
        kernel_three_grad,
        bias_three_grad,
        kernel_two_grad,
        bias_two_grad,
        identity_kernel_grad,
        identity_bias_grad,
    ) = ran(final_grads(turn(), *all_deep, ((deep,), (deep,), identity_kernel.shape)))
    kernel_one_grad, bias_one_grad, out_kernel_grad, _ = ran(
        final_grads(turn(), *all_one, ((one.shape[1],), out_kernel.shape))
    )

    return (
        block_out.reshape(cotangent.shape),
        pixels_grad,
        kernel_one_grad.reshape(kernel_one.shape),
        bias_one_grad[0],
        kernel_two_grad.reshape(kernel_two.shape),
        bias_two_grad[0],
        kernel_three_grad.reshape(kernel_three.shape),
        bias_three_grad[0],
        out_kernel_grad,
        identity_kernel_grad,
        identity_bias_grad[0],
    )


def solution(mesh):
    members = mesh.devices.size // mesh.shape["mp"]
    fine = Mesh(
        mesh.devices.reshape(members // 2, 2, 2, mesh.shape["mp"] // 2),
        ("chip", "core", "zh", "zl"),
    )
    return jax.shard_map(
        local,
        mesh=fine,
        in_specs=(
            P(None, DP, None, MP),
            P(),
            P(None, None, None, MP),
            P(MP),
            P(None, None, None, MP),
            P(MP),
            P(None, None, None, MP),
            P(MP),
            P(None, MP),
            P(None, MP),
            P(MP),
            P(DP, None, None, MP),
        ),
        out_specs=(
            P(DP, None, None, MP),
            P(None, DP, None, MP),
            P(None, None, None, MP),
            P(MP),
            P(None, None, None, MP),
            P(MP),
            P(None, None, None, MP),
            P(MP),
            P(None, MP),
            P(None, MP),
            P(MP),
        ),
        check_vma=False,
    )
```

```python
import functools
import math

import jax
import jax.numpy as jnp
from jax import lax
from jax.experimental import pallas as pl
from jax.experimental.pallas import tpu as pltpu
from jax.sharding import Mesh
from jax.sharding import PartitionSpec as P


post_gain = 0.015625
slope = 0.7978845608028654
cubic = 0.044715
halo = 6
bf16 = jnp.bfloat16
f32 = jnp.float32
NT = (((1,), (1,)), ((), ()))
TN = (((0,), (0,)), ((), ()))
NN = (((1,), (0,)), ((), ()))
DP = ("chip", "core")
MP = ("zh", "zl")


def dot(left, right, dims=NN):
    return lax.dot_general(left, right, dims, preferred_element_type=f32)


def gelu(value):
    inner = jnp.tanh(slope * (value + cubic * value * value * value))
    return 0.5 * value * (1.0 + inner)


def gelu_slope(value):
    square = value * value
    inner = jnp.tanh(slope * value * (1.0 + cubic * square))
    climb = slope * (1.0 + 3.0 * cubic * square)
    return 0.5 * (1.0 + inner) + 0.5 * value * (1.0 - inner * inner) * climb


def struct(shape, kind):
    return jax.ShapeDtypeStruct(shape, kind)


def lanes(blocks):
    return blocks[0] if len(blocks) == 1 else jnp.concatenate(blocks, axis=1)


def step_bits(core, chips):
    bits = [1 << n for n in range(chips.bit_length() - 1)]
    for n in range(0, len(bits) - 1, 2) if core else ():
        bits[n], bits[n + 1] = bits[n + 1], bits[n]
    return bits


def mask_of(i, core, chips):
    masks = []
    for which in range(2):
        bits = step_bits(which, chips)
        masks.append(sum(bit for n, bit in enumerate(bits) if i >> (len(bits) - 1 - n) & 1))
    return jnp.where(core == 0, masks[0], masks[1])


def slot_of(mask, core, chips):
    slots = []
    for which in range(2):
        bits = step_bits(which, chips)
        slot = 0
        for n, bit in enumerate(bits):
            slot = slot + ((mask >> (bit.bit_length() - 1)) & 1) * (1 << (len(bits) - 1 - n))
        slots.append(slot)
    return jnp.where(core == 0, slots[0], slots[1])


VMEM = pl.BlockSpec(memory_space=pltpu.VMEM)
SMEM = pl.BlockSpec(memory_space=pltpu.SMEM)
FAR = pl.BlockSpec(memory_space=pl.ANY)
LOAD = "load"


def size_of(array):
    return math.prod(array.shape) * jnp.dtype(array.dtype).itemsize


def call(body, name, ins, outs, scratch=(), spare=6, **more):
    loads = [i for i, (space, _) in enumerate(ins) if space is LOAD]
    spaces = [FAR if space is LOAD else space for space, _ in ins]
    arrays = [array for _, array in ins]
    out_specs = [space for space, _ in outs]
    out_shape = [shape for _, shape in outs]
    held = [arrays[i] for i in loads]
    buffers = [pltpu.VMEM(array.shape, array.dtype) for array in held]
    sems = [pltpu.SemaphoreType.DMA((len(held),))] if held else []
    vmem = sum(size_of(array) for array in held)
    vmem += sum(size_of(a) for space, a in list(ins) + list(outs) if space is VMEM)
    vmem += sum(size_of(b) for b in scratch if b.memory_space == pltpu.VMEM)
    moved = sum(size_of(a) for a in arrays + out_shape)

    def wrapped(*refs):
        inputs = list(refs[: len(ins)])
        outputs = refs[len(ins) : len(ins) + len(outs)]
        rest = refs[len(ins) + len(outs) :]
        kept, tail = rest[: len(held)], rest[len(held) :]
        copies = []
        if held:
            sem, tail = tail[0], tail[1:]
            copies = [
                pltpu.make_async_copy(inputs[i], kept[n], sem.at[n]) for n, i in enumerate(loads)
            ]
        for copy in copies:
            copy.start()
        for n, i in enumerate(loads):
            inputs[i] = kept[n]

        def arrive():
            for copy in copies:
                copy.wait()

        body(arrive, *inputs, *outputs, *tail)

    single = len(outs) == 1
    return pl.pallas_call(
        wrapped,
        in_specs=spaces,
        out_specs=out_specs[0] if single else out_specs,
        out_shape=out_shape[0] if single else out_shape,
        scratch_shapes=buffers + sems + list(scratch),
        compiler_params=pltpu.CompilerParams(vmem_limit_bytes=vmem + (spare << 20)),
        cost_estimate=pl.CostEstimate(flops=0, bytes_accessed=moved, transcendentals=0),
        name=name,
        **more,
    )(*arrays)


def run_copies(pairs, sems):
    for copy in start_copies(pairs, sems):
        copy.wait()


def slice_copies(group, idx_ref, own, blocks, sibling, wbuf):
    chip, core, zh = idx_ref[0], idx_ref[1], idx_ref[2]
    size = blocks.shape[-2]
    pairs = [(own, wbuf.at[zh])]
    for j in range(blocks.shape[0]):
        for source, owner in ((blocks, core), (sibling, 1 - core)):
            home = chip ^ mask_of(j, owner, blocks.shape[0])
            spot = at((2 * home + owner) * size, size, size)
            pairs.append((source.at[j, 9 * group : 9 * group + 9], wbuf.at[1 - zh, :, spot, :]))
    return pairs


def flat_copies(first, idx_ref, blocks, sibling, buffer):
    chip, core = idx_ref[0], idx_ref[1]
    columns, units = buffer.shape[:2]
    chips = blocks.shape[0]
    count = units // (2 * chips)
    pairs = []
    for j in range(chips):
        for source, owner in ((blocks, core), (sibling, 1 - core)):
            home = chip ^ mask_of(j, owner, chips)
            spot = pl.ds((2 * home + owner) * count, count)
            for c in range(columns):
                begin = first + c * count
                pairs.append((source.at[j, begin : begin + count], buffer.at[c, spot]))
    return pairs


def start_copies(pairs, sems):
    copies = [pltpu.make_async_copy(a, b, sems.at[i]) for i, (a, b) in enumerate(pairs)]
    for copy in copies:
        copy.start()
    return copies


def flat_rows(buffer, begin, count):
    columns, _, size, wide = buffer.shape
    return lanes([buffer[c, pl.ds(begin, count)].reshape(count * size, wide) for c in range(columns)])


def halves(spots, side):
    first = (spots // side + 1) // 2 * side
    return ((0, first), (first, spots - first))


def columns_of(size, wide, side):
    return lax.rem(lax.broadcasted_iota(jnp.int32, (size, wide), 0), side)


def at(start, size, unit):
    return pl.ds(pl.multiple_of(start, unit), size)


def pool_body(arrive, x_ref, out_ref):
    arrive()
    rows, width, chans = x_ref.shape[1:]
    half = width // 2
    pixel = lax.broadcasted_iota(jnp.int32, (half, 2 * width), 1)
    place = lax.broadcasted_iota(jnp.int32, (half, 2 * width), 0)
    inside = (lax.rem(pixel, width) >= 2 * place) & (lax.rem(pixel, width) < 2 * place + 2)
    pick = jnp.where(inside, 0.25, 0.0).astype(bf16)
    for image in range(x_ref.shape[0]):
        for row in range(rows // 2):
            window = x_ref[image, 2 * row : 2 * row + 2].reshape(2 * width, chans)
            out_ref[image, row * half : (row + 1) * half, :] = dot(pick, window).astype(bf16)


def pool(pixels):
    images, rows, width, chans = pixels.shape
    shape = struct((images, rows * width // 4, chans), bf16)
    return call(pool_body, "pool", [(LOAD, pixels)], [(VMEM, shape)])


def widen_body(arrive, idx_ref, g_ref, out_ref):
    arrive()
    rows, width, chans = out_ref.shape[1:]
    half = width // 2
    pixel = lax.broadcasted_iota(jnp.int32, (width, half), 0)
    place = lax.broadcasted_iota(jnp.int32, (width, half), 1)
    inside = (pixel >= 2 * place) & (pixel < 2 * place + 2)
    pick = jnp.where(inside, 0.25, 0.0).astype(bf16)
    for image in range(g_ref.shape[0]):
        for row in range(rows // 2):
            wide = dot(pick, g_ref[image, row * half : (row + 1) * half, :]).astype(bf16)
            out_ref[image, 2 * row] = wide
            out_ref[image, 2 * row + 1] = wide


def widen(idx, grad, rows, width):
    images, spots, chans = grad.shape
    step = images // 4
    block = pl.BlockSpec((step, spots, chans), lambda i: (i, 0, 0))
    out = pl.BlockSpec((step, rows, width, chans), lambda i: (i, 0, 0, 0))
    return call(
        widen_body,
        "widen",
        [(SMEM, idx), (block, grad)],
        [(out, struct((images, rows, width, chans), bf16))],
        grid=(4,),
    )


def conv_body(side, first, group, arrive, idx_ref, *refs):
    zh, zl = idx_ref[2], idx_ref[3]
    if first:
        xl, xa, xh, xd, wl, wo, ws, bl, bo, pre_ref, act_ref, xbuf, wbuf, acc, sems = refs
        chans = xl.shape[1]
        spots = xbuf.shape[0]
        begin = zh * (xl.shape[0] - spots)
        pairs = []
        for source, up, along in ((xl, zh, zl), (xa, zh, 1 - zl), (xh, 1 - zh, zl), (xd, 1 - zh, 1 - zl)):
            if source is xl:
                source = xl.at[at(begin, spots, side), :]
            pairs.append((source, xbuf.at[:, at((2 * up + along) * chans, chans, chans)]))
    else:
        xl, xa, wl, wo, ws, bl, bo, pre_ref, act_ref, xbuf, wbuf, acc, sems = refs
        chans = xl.shape[1] // 2
        spots = xbuf.shape[0]
        pairs = []
        for source, along in ((xl, zl), (xa, 1 - zl)):
            for up in range(2):
                pairs.append(
                    (
                        source.at[:, up * chans : (up + 1) * chans],
                        xbuf.at[:, at((2 * up + along) * chans, chans, chans)],
                    )
                )
    run_copies(slice_copies(group, idx_ref, wl, wo, ws, wbuf) + pairs, sems)
    arrive()
    if first:
        for begin, block in halves(spots, side):
            rows = slice(begin, begin + block)
            xbuf[rows, :] = gelu(xbuf[rows, :].astype(f32)).astype(bf16)
    acc[...] = jnp.zeros_like(acc)
    outs = 2 * wl.shape[2]
    for x in range(3):
        weights = lanes([wbuf[u, 3 * y + x] for y in range(3) for u in range(2)])
        for begin, block in halves(spots, side):
            product = dot(xbuf[begin : begin + block, :], weights)
            for y in range(3):
                place = begin + side * (2 - y)
                acc[x, place : place + block, :] += product[:, y * outs : (y + 1) * outs]
    own, other = bl[...], bo[...]
    bias = lanes([jnp.where(zh == 0, own, other), jnp.where(zh == 0, other, own)])
    for begin, block in halves(act_ref.shape[0], side):
        column = columns_of(block, outs, side)
        spot = at(begin + side + zh * side, block, side)
        left = pltpu.roll(acc[0, spot, :], 1, 0)
        right = pltpu.roll(acc[2, spot, :], block - 1, 0)
        pre = acc[1, spot, :] + bias
        pre = pre + jnp.where(column > 0, left, 0.0)
        pre = pre + jnp.where(column < side - 1, right, 0.0)
        pre_ref[begin : begin + block, :] = pre
        act_ref[begin : begin + block, :] = gelu(pre).astype(bf16)


def conv(side, idx, sources, own, other, group, bias, bias_other, first=False):
    taps, depth, outs = own.shape
    spots = sources[1].shape[0]
    rows = spots - side
    return call(
        functools.partial(conv_body, side, first, group),
        "conv",
        [(SMEM, idx)]
        + [(FAR, s) for s in sources]
        + [(FAR, own), (FAR, other[0]), (FAR, other[1])]
        + [(VMEM, bias.reshape(1, outs)), (VMEM, bias_other.reshape(1, outs))],
        [(VMEM, struct((rows, 2 * outs), f32)), (VMEM, struct((rows, 2 * outs), bf16))],
        [
            pltpu.VMEM((spots, depth), bf16),
            pltpu.VMEM((2, taps, depth, outs), bf16),
            pltpu.VMEM((3, spots + 2 * side, 2 * outs), f32),
            pltpu.SemaphoreType.DMA((2 * other[0].shape[0] + 5,)),
        ],
        spare=14 if first else 8,
    )


def spread_taps(side, grad, taps_ref):
    pixels, outs = grad.shape
    column = columns_of(pixels, outs, side)
    wide = grad.astype(f32)
    ahead = jnp.where(column < side - 1, pltpu.roll(wide, pixels - 1, 0), 0.0).astype(bf16)
    behind = jnp.where(column > 0, pltpu.roll(wide, 1, 0), 0.0).astype(bf16)
    edge = jnp.zeros((side, 3 * outs), bf16)
    taps_ref[:side, :] = edge
    taps_ref[side + pixels :, :] = edge
    taps_ref[side : side + pixels, :] = jnp.concatenate([ahead, grad, behind], axis=1)


def tap_block(side, taps_ref, begin, block):
    return lanes([taps_ref[at(begin + side * (2 - y), block, side), :] for y in range(3)])


def slope_body(side, arrive, idx_ref, keep_ref, recv_ref, pre_ref, mine_ref, theirs_ref, gp_ref):
    arrive()
    zh = idx_ref[2]
    half, outs = mine_ref.shape
    total = keep_ref[...] + recv_ref[...].astype(f32)
    spots = keep_ref.shape[0]
    pre = pre_ref[at(zh * (pre_ref.shape[0] - spots), spots, side), :]
    gp_ref[...] = (total * gelu_slope(pre)).astype(bf16)
    own = gp_ref[at(zh * (gp_ref.shape[0] - half), half, side), :]
    low, high = own[:, :outs], own[:, outs:]
    mine_ref[...] = jnp.where(zh == 0, low, high)
    theirs_ref[...] = jnp.where(zh == 0, high, low)


def slope_back(side, idx, keep, recv, pre, half):
    outs = pre.shape[1] // 2
    return call(
        functools.partial(slope_body, side),
        "slope_back",
        [(SMEM, idx), (VMEM, keep), (VMEM, recv), (LOAD, pre)],
        [
            (VMEM, struct((half, outs), bf16)),
            (VMEM, struct((half, outs), bf16)),
            (VMEM, struct(keep.shape, bf16)),
        ],
    )


def back_body(side, last, group, arrive, idx_ref, *refs):
    zh, zl = idx_ref[2], idx_ref[3]
    if last:
        valid_ref, grad_ref, x_ref, go_ref, far_ref, idk_ref, wl, wo, ws, po, ps = refs[:11]
        own_ref, give_ref, taps_ref, wbuf, idk_far, sems = refs[11:]
    else:
        keep_ref, recv_ref, pre_ref, wl, wo, ws, gp_ref, own_ref, give_ref, taps_ref, wbuf, sems = refs
    pairs = slice_copies(group, idx_ref, wl, wo, ws, wbuf)
    if last:
        pairs += flat_copies(9, idx_ref, po, ps, idk_far)
    copies = start_copies(pairs, sems)
    arrive()
    if last:
        grad = grad_ref[...]
    else:
        spots = gp_ref.shape[0]

        def window(ref):
            return ref[at(zh * (ref.shape[0] - spots), spots, side), :]

        total = window(keep_ref) + window(recv_ref).astype(f32)
        grad = (total * gelu_slope(window(pre_ref))).astype(bf16)
        gp_ref[...] = grad
    spread_taps(side, grad, taps_ref)
    depth, outs = wl.shape[1:]
    pixels = own_ref.shape[-2]
    start = zh * side
    for copy in copies:
        copy.wait()
    chans = depth // 4

    def rows(index):
        spot = at(index * chans, chans, chans)
        return lanes([wbuf[u, t, spot, :] for t in range(9) for u in range(2)])

    for target, along in ((give_ref, 1 - zl), (own_ref, zl)):
        if last:
            units = chans // idk_far.shape[2]
            for up in range(2):
                index = 2 * up + along
                weights = rows(index)
                near = idk_ref[at(index * chans, chans, chans), :]
                far = flat_rows(idk_far, index * units, units)
                apart = zh * (far_ref.shape[0] - pixels)
                for begin, block in halves(pixels, side):
                    here = at(zh * pixels + begin, block, side)
                    part = dot(tap_block(side, taps_ref, start + begin, block), weights, NT)
                    x = x_ref[here, at(index * chans, chans, chans)]
                    part = part * gelu_slope(x.astype(f32))
                    part = part + dot(go_ref[here, :], near, NT)
                    part = part + valid_ref[0] * dot(far_ref[at(apart + begin, block, side), :], far, NT)
                    target[up, begin : begin + block, :] = part.astype(target.dtype)
        else:
            weights = jnp.concatenate([rows(along), rows(2 + along)], axis=0)
            for begin, block in halves(pixels, side):
                part = dot(tap_block(side, taps_ref, start + begin, block), weights, NT)
                target[begin : begin + block, :] = part.astype(target.dtype)


def back(side, idx, sources, own, other, group, last=None):
    taps, depth, outs = own.shape
    spots = min(sources[0].shape[0], sources[-1].shape[0])
    copies = 2 * other[0].shape[0] + 1
    extra = []
    scratch = []
    if last:
        valid, full_x, go, cot_far, idk, pieces, half = last
        chans = depth // 4
        shape = (2, half, chans)
        results = []
        extra = [(FAR, pieces[0]), (FAR, pieces[1])]
        sources = list(sources) + [full_x, go, cot_far, idk]
        columns, size = idk.shape[1] // 128, pieces[0].shape[2]
        scratch = [pltpu.VMEM((columns, depth // size, size, 128), bf16)]
        copies += 2 * other[0].shape[0] * columns
    else:
        shape = (spots - side, depth // 2)
        results = [(VMEM, struct((spots, 2 * outs), bf16))]
    results += [(VMEM, struct(shape, f32)), (VMEM, struct(shape, bf16))]
    return call(
        functools.partial(back_body, side, bool(last), group),
        "back",
        [(SMEM, idx)]
        + ([(SMEM, last[0])] if last else [])
        + [(LOAD, source) for source in sources]
        + [(FAR, own), (FAR, other[0]), (FAR, other[1])]
        + extra,
        results,
        [pltpu.VMEM((spots + 2 * side, 6 * outs), bf16), pltpu.VMEM((2, taps, depth, outs), bf16)]
        + scratch
        + [pltpu.SemaphoreType.DMA((copies,))],
        spare=14 if last else 10,
    )


def put_blocks(idx_ref, keep_ref, give_ref, part, tap, first_block, size, begin=0):
    chip, core = idx_ref[0], idx_ref[1]
    for b in range(0, part.shape[0] // size, 2):
        even = part[b * size : (b + 1) * size, :]
        odd = part[(b + 1) * size : (b + 2) * size, :]
        mask = chip ^ ((first_block + b) // 2)
        slot = slot_of(mask, core, keep_ref.shape[0])
        give_slot = slot_of(mask, 1 - core, keep_ref.shape[0])
        rows = slice(begin + tap * size, begin + (tap + 1) * size)
        keep_ref[slot, rows, :] = jnp.where(core == 0, even, odd).astype(bf16)
        give_ref[give_slot, rows, :] = jnp.where(core == 0, odd, even).astype(bf16)


def weight_body(side, half, flat, arrive, idx_ref, gp_ref, *refs):
    if flat:
        full_ref, go_ref, bias_ref = refs[:3]
        refs = refs[3:]
    xl, xa, keep_ref, give_ref, xbuf, taps_ref, sems = refs
    arrive()
    zh, zl = idx_ref[2], idx_ref[3]
    chans = xl.shape[1] // 2
    spots = xbuf.shape[0]
    window = at(zh * (xl.shape[0] - spots), spots, side)
    pairs = []
    for source, along in ((xl, zl), (xa, 1 - zl)):
        for up in range(2):
            pairs.append(
                (
                    source.at[window, up * chans : (up + 1) * chans],
                    xbuf.at[:, at((2 * up + along) * chans, chans, chans)],
                )
            )
    run_copies(pairs, sems)
    wide = gp_ref.shape[1]
    outs = wide // 2
    spot = lax.broadcasted_iota(jnp.int32, (spots, wide), 0) - zh * side
    grad = gp_ref[at(zh * (gp_ref.shape[0] - spots), spots, side), :].astype(f32)
    grad = jnp.where((spot >= 0) & (spot < half), grad, 0.0)
    bias = jnp.sum(grad, axis=0, keepdims=True)
    spread_taps(side, grad.astype(bf16), taps_ref)
    blocks = 2 * keep_ref.shape[0]
    depth = xbuf.shape[1]
    size = depth // blocks
    for begin in range(0, depth, 256):
        values = xbuf[:, begin : begin + 256]
        for y in range(3):
            place = side * (2 - y)
            part = dot(values, taps_ref[place : place + spots, :], TN)
            for x in range(3):
                for u in range(2):
                    col = x * wide + u * outs
                    put_blocks(
                        idx_ref, keep_ref, give_ref, part[:, col : col + outs],
                        3 * y + x, begin // size, size, u * (9 * size + 16),
                    )
    for u in range(2):
        row = jnp.broadcast_to(bias[:, u * outs : (u + 1) * outs], (16, outs)).astype(bf16)
        for j in range(keep_ref.shape[0]):
            spot = slice(u * (9 * size + 16) + 9 * size, (u + 1) * (9 * size + 16))
            keep_ref[j, spot, :] = row
            give_ref[j, spot, :] = row
    if flat:
        first = 2 * (9 * size + 16)
        flat_pieces(1.0, idx_ref, full_ref, go_ref, bias_ref, keep_ref, give_ref, first)


def weight_grad(side, half, idx, grad, act, act_other, chips, flat=()):
    spots = half + side
    wide = grad.shape[1]
    outs = wide // 2
    depth = 2 * act.shape[1]
    rows = 2 * (9 * depth // (2 * chips) + 16)
    if flat:
        rows += flat_size(flat[0], flat[1], chips)
    return call(
        functools.partial(weight_body, side, half, bool(flat)),
        "weight_grad",
        [(SMEM, idx), (LOAD, grad)] + [(LOAD, a) for a in flat] + [(FAR, act), (FAR, act_other)],
        [(VMEM, struct((chips, rows, outs), bf16))] * 2,
        [
            pltpu.VMEM((spots, depth), bf16),
            pltpu.VMEM((spots + 2 * side, 3 * wide), bf16),
            pltpu.SemaphoreType.DMA((4,)),
        ],
        spare=10,
    )


def weight_one_body(side, arrive, idx_ref, mine_ref, theirs_ref, x_ref, *refs):
    keep_ref, give_ref, gp_ref, taps_ref = refs
    arrive()
    zh = idx_ref[2]
    half, outs = mine_ref.shape
    gp_ref[at(zh * half, half, side), :] = mine_ref[...]
    gp_ref[at((1 - zh) * half, half, side), :] = theirs_ref[...]
    grad = gp_ref[...]
    bias = jnp.sum(grad.astype(f32), axis=0, keepdims=True)
    spread_taps(side, grad, taps_ref)
    blocks = 2 * keep_ref.shape[0]
    spots, depth = x_ref.shape
    size = depth // blocks
    right = tap_block(side, taps_ref, 0, spots)
    for begin in range(0, depth, 256):
        part = dot(x_ref[:, begin : begin + 256], right, TN)
        for tap in range(9):
            put_blocks(
                idx_ref, keep_ref, give_ref, part[:, tap * outs : (tap + 1) * outs],
                tap, begin // size, size,
            )
    row = jnp.broadcast_to(bias, (16, outs)).astype(bf16)
    first = 9 * size + 16
    for j in range(keep_ref.shape[0]):
        keep_ref[j, 9 * size : first, :] = row
        give_ref[j, 9 * size : first, :] = row


def weight_one_grad(side, idx, mine, theirs, act_zero, chips):
    spots, depth = act_zero.shape
    outs = mine.shape[1]
    rows = 9 * depth // (2 * chips) + 16
    return call(
        functools.partial(weight_one_body, side),
        "weight_one_grad",
        [(SMEM, idx), (LOAD, mine), (LOAD, theirs), (LOAD, act_zero)],
        [(VMEM, struct((chips, rows, outs), bf16))] * 2,
        [
            pltpu.VMEM((spots, outs), bf16),
            pltpu.VMEM((spots + 2 * side, 3 * outs), bf16),
        ],
        spare=14,
    )


def fold_body(pairs, arrive, idx_ref, *refs):
    arrive()
    ins, (keep_ref, give_ref) = refs[: 2 * pairs], refs[2 * pairs :]
    half = keep_ref.shape[0]
    for i in range(2 * half):
        target = keep_ref if i < half else give_ref
        begin = 0
        for keep, recv in zip(ins[0::2], ins[1::2]):
            rows = keep.shape[1]
            total = keep[i].astype(f32) + recv[i].astype(f32)
            target[i % half, begin : begin + rows, :] = total.astype(bf16)
            begin += rows


def fold(idx, *arrays):
    blocks, _, wide = arrays[0].shape
    rows = sum(a.shape[1] for a in arrays[0::2])
    return call(
        functools.partial(fold_body, len(arrays) // 2),
        "fold",
        [(SMEM, idx)] + [(VMEM, a) for a in arrays],
        [(VMEM, struct((blocks // 2, rows, wide), bf16))] * 2,
    )


def last_body(slotted, rest, arrive, idx_ref, keep_in, recv_in, *targets):
    arrive()
    zh = idx_ref[2]

    def put(target, place, begin, rows):
        spot = at(begin, rows, 16)
        total = keep_in[0, spot, :].astype(f32) + recv_in[0, spot, :].astype(f32)
        target[place : place + rows, :] = total.astype(bf16)

    place = 0
    for begin, rows in slotted:
        put(targets[0], place, begin + zh * rows, rows)
        put(targets[1], place, begin + (1 - zh) * rows, rows)
        place += rows
    begin, rows = rest
    put(targets[-1], 0, begin, rows)


def last_fold(idx, keep, recv, slotted=(), rest=None):
    wide = keep.shape[2]
    rest = rest or (0, keep.shape[1])
    rows = sum(size for _, size in slotted)
    sizes = ([rows, rows] if slotted else []) + [rest[1]]
    return call(
        functools.partial(last_body, slotted, rest),
        "last_fold",
        [(SMEM, idx), (VMEM, keep), (VMEM, recv)],
        [(VMEM, struct((size, wide), bf16)) for size in sizes],
    )


def final_body(parts, arrive, idx_ref, own_ref, sib_ref, *refs):
    arrive()
    outs, stages, sems = refs[: 2 * len(parts)], refs[2 * len(parts) : -1], refs[-1]
    chip, core = idx_ref[0], idx_ref[1]
    chips, _, wide = own_ref.shape
    first = 0
    copies = []

    def store(source, target):
        copies.append(pltpu.make_async_copy(source, target, sems.at[len(copies)]))
        copies[-1].start()

    for n, part in enumerate(parts):
        grad_ref, bias_ref, stage = outs[2 * n], outs[2 * n + 1], stages[n]
        size = part[0] // (2 * chips)
        columns = 1 if len(part) == 1 else part[1] // wide
        end = first + size * (9 if len(part) == 1 else columns)
        for c in range(columns):
            row = own_ref[0, end + c : end + c + 1, :].astype(f32)
            bias_ref[:, c * wide : (c + 1) * wide] = row
        for n_row, begin in enumerate(range(first, end, size)):
            for j in range(chips):
                for source, owner in ((own_ref, core), (sib_ref, 1 - core)):
                    home = chip ^ mask_of(j, owner, chips)
                    spot = at((2 * home + owner) * size, size, size)
                    piece = source[j, begin : begin + size, :].astype(f32)
                    if len(part) == 1:
                        stage[n_row, spot, :] = piece
                    else:
                        stage[spot, n_row * wide : (n_row + 1) * wide] = piece
            if len(part) == 1:
                store(stage.at[n_row], grad_ref.at[n_row])
        if len(part) > 1:
            store(stage, grad_ref)
        first = end + 16
    for copy in copies:
        copy.wait()


def final_grads(idx, own, sib, parts):
    wide = own.shape[2]
    results, stages = [], []
    for part in parts:
        shape = (9, part[0], wide) if len(part) == 1 else part
        results += [(FAR, struct(shape, f32)), (VMEM, struct((1, shape[-1]), f32))]
        stages.append(pltpu.VMEM(shape, f32))
    copies = sum(9 if len(part) == 1 else 1 for part in parts)
    return call(
        functools.partial(final_body, parts),
        "final_grads",
        [(SMEM, idx), (VMEM, own), (VMEM, sib)],
        results,
        stages + [pltpu.SemaphoreType.DMA((copies,))],
    )


def flat_pieces(gain, idx_ref, x_ref, go_ref, bias_ref, keep_ref, give_ref, first):
    chip, core = idx_ref[0], idx_ref[1]
    chips, _, wide = keep_ref.shape
    columns = go_ref.shape[1] // wide
    size = x_ref.shape[1] // (2 * chips)
    bias = jnp.concatenate(
        [bias_ref[:, c * wide : (c + 1) * wide] for c in range(columns)]
        + [jnp.zeros((16 - columns, wide), f32)],
        axis=0,
    ).astype(bf16)
    for j in range(chips):
        keep_ref[j, first + columns * size :, :] = bias
        give_ref[j, first + columns * size :, :] = bias
    for begin in range(0, x_ref.shape[1], 256):
        part = gain * dot(x_ref[:, begin : begin + 256], go_ref[...], TN)
        for b in range(0, 256 // size, 2):
            mask = chip ^ ((begin // size + b) // 2)
            slot = slot_of(mask, core, chips)
            give_slot = slot_of(mask, 1 - core, chips)
            for c in range(columns):
                even = part[b * size : (b + 1) * size, c * wide : (c + 1) * wide]
                odd = part[(b + 1) * size : (b + 2) * size, c * wide : (c + 1) * wide]
                spot = slice(first + c * size, first + (c + 1) * size)
                keep_ref[slot, spot, :] = jnp.where(core == 0, even, odd).astype(bf16)
                give_ref[give_slot, spot, :] = jnp.where(core == 0, odd, even).astype(bf16)


def flat_size(x, go, chips):
    return (go.shape[1] // 128) * (x.shape[1] // (2 * chips)) + 16


def outer_body(gain, arrive, idx_ref, x_ref, go_ref, bias_ref, keep_ref, give_ref):
    arrive()
    flat_pieces(gain, idx_ref, x_ref, go_ref, bias_ref, keep_ref, give_ref, 0)


def outer(idx, x, go, gain, bias, chips):
    return call(
        functools.partial(outer_body, gain),
        "outer",
        [(SMEM, idx), (LOAD, x), (LOAD, go), (LOAD, bias)],
        [(VMEM, struct((chips, flat_size(x, go, chips), 128), bf16))] * 2,
        spare=8,
    )


def start_body(arrive, idx_ref, valid_ref, cot_ref, outk_ref, go_ref, bias_ref, own_ref, give_ref):
    arrive()
    zl = idx_ref[3]
    masked = cot_ref[...].astype(f32) * valid_ref[0]
    go_ref[...] = masked.astype(bf16)
    bias_ref[...] = jnp.sum(masked, axis=0, keepdims=True)
    chans = outk_ref.shape[0] // 4
    block = cot_ref.shape[0] // 4
    for target, along in ((give_ref, 1 - zl), (own_ref, zl)):
        weights = jnp.concatenate(
            [outk_ref[at((2 * up + along) * chans, chans, chans), :] for up in range(2)], axis=0
        )
        for begin in range(0, cot_ref.shape[0], block):
            part = post_gain * dot(go_ref[begin : begin + block, :], weights, NT)
            target[begin : begin + block, :] = part.astype(target.dtype)


def start_back(idx, valid, cot, outk):
    spots, outs = cot.shape
    half = outk.shape[0] // 2
    return call(
        start_body,
        "start_back",
        [(SMEM, idx), (SMEM, valid), (LOAD, cot), (LOAD, outk)],
        [
            (VMEM, struct(cot.shape, bf16)),
            (VMEM, struct((1, outs), f32)),
            (VMEM, struct((spots, half), f32)),
            (VMEM, struct((spots, half), bf16)),
        ],
    )


def rows_body(side, arrive, idx_ref, own_ref, recv_ref, keep_ref, give_ref):
    arrive()
    zh = idx_ref[2]
    spots = keep_ref.shape[0]
    apart = own_ref.shape[0] - spots
    for target, begin in ((give_ref, (1 - zh) * apart), (keep_ref, zh * apart)):
        spot = at(begin, spots, side)
        total = own_ref[spot, :] + recv_ref[spot, :].astype(f32)
        target[...] = total.astype(target.dtype)


def rows_sum(side, idx, own, recv, spots):
    shape = (spots, own.shape[1])
    return call(
        functools.partial(rows_body, side),
        "rows_sum",
        [(SMEM, idx), (LOAD, own), (LOAD, recv)],
        [(VMEM, struct(shape, f32)), (VMEM, struct(shape, bf16))],
    )


def slots_body(arrive, idx_ref, own_ref, recv_ref, keep_ref, give_ref):
    arrive()
    zh = idx_ref[2]
    for target, slot in ((give_ref, 1 - zh), (keep_ref, zh)):
        total = own_ref[slot] + recv_ref[slot].astype(f32)
        target[...] = total.astype(bf16)


def slots_sum(idx, own, recv):
    shape = struct(own.shape[1:], bf16)
    return call(
        slots_body,
        "slots_sum",
        [(SMEM, idx), (VMEM, own), (VMEM, recv)],
        [(VMEM, shape), (VMEM, shape)],
    )


def input_body(arrive, idx_ref, keep_ref, recv_ref, out_ref):
    arrive()
    zh = idx_ref[2]
    half = keep_ref.shape[0]
    out_ref[at(zh * half, half, half), :] = keep_ref[...]
    out_ref[at((1 - zh) * half, half, half), :] = recv_ref[...]


def input_grad(idx, keep, recv):
    half, chans = keep.shape
    return call(
        input_body,
        "input_grad",
        [(SMEM, idx), (VMEM, keep), (VMEM, recv)],
        [(VMEM, struct((2 * half, chans), bf16))],
    )


def whole_body(side, arrive, idx_ref, xl, xa, xh, xd, rh, rl, x_ref, act_ref, sems):
    arrive()
    zh, zl = idx_ref[2], idx_ref[3]
    chans = xl.shape[1]
    spots = xa.shape[0]
    rest = xl.shape[0] - spots
    window, outside = at(zh * rest, spots, side), at((1 - zh) * spots, rest, side)

    def cols(up, along):
        return at((2 * up + along) * chans, chans, chans)

    run_copies(
        [
            (xl, x_ref.at[:, cols(zh, zl)]),
            (xa, x_ref.at[window, cols(zh, 1 - zl)]),
            (xh, x_ref.at[window, cols(1 - zh, zl)]),
            (xd, x_ref.at[window, cols(1 - zh, 1 - zl)]),
            (rl.at[0], x_ref.at[outside, cols(zh, 1 - zl)]),
            (rh, x_ref.at[outside, cols(1 - zh, zl)]),
            (rl.at[1], x_ref.at[outside, cols(1 - zh, 1 - zl)]),
        ],
        sems,
    )
    block = x_ref.shape[0] // 8
    for begin in range(0, x_ref.shape[0], block):
        rows = slice(begin, begin + block)
        act_ref[rows, :] = gelu(x_ref[rows, :].astype(f32)).astype(bf16)


def whole_input(side, idx, *parts):
    spots, chans = parts[0].shape
    return call(
        functools.partial(whole_body, side),
        "whole_input",
        [(SMEM, idx)] + [(FAR, p) for p in parts],
        [(VMEM, struct((spots, 4 * chans), bf16))] * 2,
        [pltpu.SemaphoreType.DMA((7,))],
    )


def join_body(arrive, idx_ref, own, recv, far_own, far_recv, out, sems):
    arrive()
    zh, zl = idx_ref[2], idx_ref[3]
    half = own.shape[0]
    chans = own.shape[1] // 2
    pairs = []
    for source, up, along in ((own, zh, zl), (recv, zh, 1 - zl), (far_own, 1 - zh, zl), (far_recv, 1 - zh, 1 - zl)):
        for slot in range(2):
            spot = at((2 * slot + along) * chans, chans, chans)
            target = out.at[at(up * half, half, half), spot]
            pairs.append((source.at[:, slot * chans : (slot + 1) * chans], target))
    run_copies(pairs, sems)


def join(idx, *parts):
    half, wide = parts[0].shape
    return call(
        join_body,
        "join",
        [(SMEM, idx)] + [(FAR, p) for p in parts],
        [(VMEM, struct((2 * half, 2 * wide), bf16))],
        [pltpu.SemaphoreType.DMA((8,))],
    )


def finish_body(arrive, idx_ref, valid_ref, x_ref, act_ref, idk_ref, outk_ref, ib_ref, out_ref):
    arrive()
    block = x_ref.shape[0] // 4
    for begin in range(0, x_ref.shape[0], block):
        rows = slice(begin, begin + block)
        identity = dot(x_ref[rows, :], idk_ref[...]) + ib_ref[...]
        branch = dot(act_ref[rows, :], outk_ref[...])
        out_ref[rows, :] = ((identity + post_gain * branch) * valid_ref[0]).astype(bf16)


def finish(idx, valid, x, act, idk, outk, ib):
    outs = idk.shape[1]
    return call(
        finish_body,
        "finish",
        [(SMEM, idx), (SMEM, valid), (LOAD, x), (LOAD, act), (LOAD, idk), (LOAD, outk)]
        + [(VMEM, ib.reshape(1, outs))],
        [(VMEM, struct((x.shape[0], outs), bf16))],
        spare=8,
    )


def flip(value, axis):
    return lax.ppermute(value, axis, [(0, 1), (1, 0)])


def cross(value, step, chips):
    pairs = []
    for chip in range(chips):
        for core in range(2):
            other = chip ^ step_bits(core, chips)[step]
            pairs.append((2 * chip + core, 2 * other + core))
    return lax.ppermute(value, DP, pairs)


def hops(value, chips):
    blocks = [value]
    for i in range(1, chips):
        pairs = []
        for chip in range(chips):
            for core in range(2):
                bits = step_bits(core, chips)
                mask = sum(bit for n, bit in enumerate(bits) if i >> (len(bits) - 1 - n) & 1)
                pairs.append((2 * (chip ^ mask) + core, 2 * chip + core))
        blocks.append(lax.ppermute(value, DP, pairs))
    return blocks


def swap(pieces, axis):
    return lax.all_to_all(pieces, axis, split_axis=0, concat_axis=0, tiled=True)


def after(value, other):
    return lax.optimization_barrier((value, other))[0]


def rows_of(value, start, size):
    return lax.dynamic_slice_in_dim(value, start, size, 0)


def local(
    pixels,
    counts,
    kernel_one,
    bias_one,
    kernel_two,
    bias_two,
    kernel_three,
    bias_three,
    out_kernel,
    identity_kernel,
    identity_bias,
    cotangent,
):
    images, rows, width, chans = pixels.shape
    side = width // 2
    spots = side * side
    half = spots // 2
    window = half + halo * side
    outs = cotangent.shape[3]
    chips = lax.axis_size("chip")
    chip, core, zh, zl = [lax.axis_index(a) for a in ("chip", "core", "zh", "zl")]
    idx = jnp.stack([chip, core, zh, zl]).astype(jnp.int32)
    taps = lambda kernel: kernel.reshape((9,) + kernel.shape[2:])
    one, two, three = taps(kernel_one), taps(kernel_two), taps(kernel_three)

    own_count = lax.dynamic_index_in_dim(counts, 2 * chip + core, 0, keepdims=True)
    valid = (own_count > 0).astype(f32)

    place = 2 * chip + core

    def units_of(kernel, size):
        if kernel.ndim == 3:
            block = kernel.shape[1] // (2 * chips)
            return lax.dynamic_slice_in_dim(kernel, place * block, block, 1)
        block = kernel.shape[0] // (2 * chips)
        block = lax.dynamic_slice_in_dim(kernel, place * block, block, 0)
        block = block.reshape(-1, size, block.shape[1] // 128, 128)
        return block.transpose(2, 0, 1, 3).reshape(-1, size, 128)

    steps = chips.bit_length() - 1

    def start_spread(piece, *others):
        return jnp.concatenate(after((piece[None], cross(piece[None], steps - 1, chips)), others))

    def end_spread(own, *others):
        for step in reversed(range(steps - 1)):
            own = jnp.concatenate(after((own, cross(own, step, chips)), others))
        return own, flip(own, "core")

    last = [idx]

    def turn(*others):
        return after(idx, (last[0],) + others)

    def ran(results):
        last[0] = results[-1] if isinstance(results, (list, tuple)) else results
        return results

    size = two.shape[1] // (2 * chips)
    deep = two.shape[1]
    cot = cotangent.reshape(spots, outs)
    one_piece = flip(units_of(one, size), "zh")
    pooled = ran(pool(pixels))
    go, identity_bias_grad, ga_own, ga_give = ran(start_back(turn(), valid, cot, out_kernel))
    bias_other = flip(after(jnp.stack([bias_one, bias_two, bias_three]), go), "zh")
    two_piece = units_of(after(two, pooled), size)
    last_piece = jnp.concatenate([units_of(after(k, pooled), size) for k in (three, identity_kernel)])
    cot_rows = rows_of(after(cot, pooled), (1 - zh) * half, half)
    xl = swap(after(pooled, (one_piece, two_piece, last_piece, cot_rows, ga_give)), DP)
    ga_recv = flip(ga_give, "zl")
    xl = xl.reshape(spots, chans)
    two_piece = flip(after(two_piece, one_piece), "zh")

    apart = spots - window
    xa = flip(rows_of(xl, zh * apart, window), "zl")
    xh = flip(rows_of(xl, (1 - zh) * apart, window), "zh")
    rest = spots - window
    rest_own = rows_of(xl, (1 - zh) * window, rest)
    rest_high = rows_of(xl, zh * window, rest)
    two_near = start_spread(after(two_piece, xl))
    one_near = start_spread(after(one_piece, xl), xh, xa, two_near, bias_other)
    ga_own, ga_give = ran(rows_sum(side, turn(bias_other), ga_own, ga_recv, half + (halo - 3) * side))
    xd = flip(after(xh, ga_own), "zl")
    last_piece = flip(after(last_piece, xh), "zh")
    two_other = end_spread(two_near, xd)
    one_other = end_spread(one_near, xd, two_other[0], last_piece)
    rest_high = flip(after(rest_high, xd), "zh")

    pre_one, act_one = ran(
        conv(
            side, turn(), (xl, xa, xh, xd), one, one_other, 0, bias_one, bias_other[0], True
        )
    )
    act_one_other = flip(act_one, "zl")
    pre_two, act_two = ran(
        conv(side, turn(), (act_one, act_one_other), two, two_other, 0, bias_two, bias_other[1])
    )
    act_two_other = flip(act_two, "zl")
    ga_recv = flip(after(ga_give, act_two), "zh")
    last_other = jnp.stack(after(hops(after(last_piece, act_one), chips), act_two))
    last_other = last_other, flip(last_other, "core")
    pre_three, act_three = ran(
        conv(side, turn(), (act_two, act_two_other), three, last_other, 0, bias_three, bias_other[2])
    )
    rest_low = flip(jnp.stack(after((rest_own, rest_high), act_three)), "zl")
    cot_far = flip(after(cot_rows, act_three), "zh")
    own_rows = rows_of(act_three, zh * (halo - 3) * side, half)

    gp_three, ga_own, ga_give = ran(
        back(side, turn(), (ga_own, ga_recv, pre_three), three, last_other, 0)
    )
    ga_recv = flip(ga_give, "zl")
    full_x, act_zero = ran(whole_input(side, turn(), xl, xa, xh, xd, rest_high, rest_low))
    keep_three, give_three = ran(
        weight_grad(
            side, half, turn(), gp_three, act_two, act_two_other, chips, (full_x, go, identity_bias_grad)
        )
    )
    gp_two, ga_own, ga_give = ran(
        back(side, turn(), (ga_own, ga_recv, pre_two), two, two_other, 0)
    )
    ga_recv = flip(ga_give, "zl")
    keep_two, give_two = ran(weight_grad(side, half, turn(cot_far), gp_two, act_one, act_one_other, chips))

    gp_mine, gp_theirs, gp_one = ran(slope_back(side, turn(), ga_own, ga_recv, pre_one, half))
    gp_theirs = flip(gp_theirs, "zh")
    recv_three = flip(after(give_three, gp_one), "core")
    recv_two = flip(after(give_two, gp_one), "core")
    gx_own, gx_give = ran(
        back(
            side, turn(), (gp_one,), one, one_other, 0,
            (valid, full_x, go, cot_far, identity_kernel, last_other, half),
        )
    )

    def folds(keep, recv, first, *others):
        for step in range(first, steps):
            keep, give = ran(fold(turn(*others), keep, recv))
            recv = cross(give, step, chips)
        return keep, recv

    keep_deep, give_deep = ran(fold(turn(gp_theirs), keep_three, recv_three, keep_two, recv_two))
    recv_deep = cross(give_deep, 0, chips)
    gx_recv = flip(after(gx_give, keep_deep), "zl")
    own_rows = after(own_rows, keep_deep)
    near_rows = flip(own_rows, "zl")
    far_rows = flip(own_rows, "zh")
    keep_one, give_one = ran(weight_one_grad(side, turn(), gp_mine, gp_theirs, act_zero, chips))
    recv_one = flip(give_one, "core")
    keep_deep, recv_deep = folds(keep_deep, recv_deep, 1, far_rows)
    gx_keep, gx_give = ran(slots_sum(turn(), gx_own, gx_recv))
    gx_recv = flip(gx_give, "zh")
    keep_one, give_one = ran(fold(turn(), keep_one, recv_one))
    recv_one = cross(give_one, 0, chips)
    slot = 9 * size + 16
    flat = keep_three.shape[1] - 2 * slot
    keep_deep, give_deep, id_rows = ran(
        last_fold(
            turn(), keep_deep, recv_deep, ((0, slot), (2 * slot + flat, slot)), (2 * slot, flat)
        )
    )
    recv_deep = flip(give_deep, "zh")
    far_near_rows = flip(after(far_rows, keep_deep), "zl")
    keep_one, recv_one = folds(keep_one, recv_one, 1)
    full_three = ran(join(turn(), own_rows, near_rows, far_rows, far_near_rows))
    keep_out, give_out = ran(outer(turn(), full_three, go, post_gain, identity_bias_grad, chips))
    recv_out = flip(give_out, "core")
    (total_one,) = ran([last_fold(turn(), keep_one, recv_one)])
    keep_out, give_out = ran(fold(turn(), keep_out, recv_out))
    recv_out = cross(give_out, 0, chips)
    gx = ran(input_grad(turn(), gx_keep, gx_recv))
    gx = swap(gx.reshape(images, rows * width // 4, chans), DP)
    deep_rows = (after(keep_deep, keep_out).astype(f32) + recv_deep.astype(f32)).astype(bf16)
    deep_rows = jnp.concatenate([deep_rows, id_rows])
    near_deep = start_spread(deep_rows)
    block_out = ran(
        finish(turn(deep_rows), valid, full_x, full_three, identity_kernel, out_kernel, identity_bias)
    )
    keep_out, recv_out = folds(keep_out, recv_out, 1)
    (total_out,) = ran([last_fold(turn(), keep_out, recv_out)])
    near_one = start_spread(jnp.concatenate([total_one, total_out]))
    pixels_grad = ran(widen(turn(near_one, near_deep), gx, rows, width))
    all_deep = end_spread(near_deep, pixels_grad)
    all_one = end_spread(near_one)
    (
        kernel_three_grad,
        bias_three_grad,
        kernel_two_grad,
        bias_two_grad,
        identity_kernel_grad,
        identity_bias_grad,
    ) = ran(final_grads(turn(), *all_deep, ((deep,), (deep,), identity_kernel.shape)))
    kernel_one_grad, bias_one_grad, out_kernel_grad, _ = ran(
        final_grads(turn(), *all_one, ((one.shape[1],), out_kernel.shape))
    )

    return (
        block_out.reshape(cotangent.shape),
        pixels_grad,
        kernel_one_grad.reshape(kernel_one.shape),
        bias_one_grad[0],
        kernel_two_grad.reshape(kernel_two.shape),
        bias_two_grad[0],
        kernel_three_grad.reshape(kernel_three.shape),
        bias_three_grad[0],
        out_kernel_grad,
        identity_kernel_grad,
        identity_bias_grad[0],
    )


def solution(mesh):
    members = mesh.devices.size // mesh.shape["mp"]
    fine = Mesh(
        mesh.devices.reshape(members // 2, 2, 2, mesh.shape["mp"] // 2),
        ("chip", "core", "zh", "zl"),
    )
    return jax.shard_map(
        local,
        mesh=fine,
        in_specs=(
            P(None, DP, None, MP),
            P(),
            P(None, None, None, MP),
            P(MP),
            P(None, None, None, MP),
            P(MP),
            P(None, None, None, MP),
            P(MP),
            P(None, MP),
            P(None, MP),
            P(MP),
            P(DP, None, None, MP),
        ),
        out_specs=(
            P(DP, None, None, MP),
            P(None, DP, None, MP),
            P(None, None, None, MP),
            P(MP),
            P(None, None, None, MP),
            P(MP),
            P(None, None, None, MP),
            P(MP),
            P(None, MP),
            P(None, MP),
            P(MP),
        ),
        check_vma=False,
    )
```

```python
import functools
import math

import jax
import jax.numpy as jnp
from jax import lax
from jax.experimental import pallas as pl
from jax.experimental.pallas import tpu as pltpu
from jax.sharding import Mesh
from jax.sharding import PartitionSpec as P


post_gain = 0.015625
slope = 0.7978845608028654
cubic = 0.044715
halo = 6
bf16 = jnp.bfloat16
f32 = jnp.float32
NT = (((1,), (1,)), ((), ()))
TN = (((0,), (0,)), ((), ()))
NN = (((1,), (0,)), ((), ()))
DP = ("chip", "core")
MP = ("zh", "zl")


def dot(left, right, dims=NN):
    return lax.dot_general(left, right, dims, preferred_element_type=f32)


def gelu(value):
    inner = jnp.tanh(slope * (value + cubic * value * value * value))
    return 0.5 * value * (1.0 + inner)


def gelu_slope(value):
    square = value * value
    inner = jnp.tanh(slope * value * (1.0 + cubic * square))
    climb = slope * (1.0 + 3.0 * cubic * square)
    return 0.5 * (1.0 + inner) + 0.5 * value * (1.0 - inner * inner) * climb


def struct(shape, kind):
    return jax.ShapeDtypeStruct(shape, kind)


def lanes(blocks):
    return blocks[0] if len(blocks) == 1 else jnp.concatenate(blocks, axis=1)


def step_bits(core, chips):
    bits = [1 << n for n in range(chips.bit_length() - 1)]
    for n in range(0, len(bits) - 1, 2) if core else ():
        bits[n], bits[n + 1] = bits[n + 1], bits[n]
    return bits


def mask_of(i, core, chips):
    masks = []
    for which in range(2):
        bits = step_bits(which, chips)
        masks.append(sum(bit for n, bit in enumerate(bits) if i >> (len(bits) - 1 - n) & 1))
    return jnp.where(core == 0, masks[0], masks[1])


def slot_of(mask, core, chips):
    slots = []
    for which in range(2):
        bits = step_bits(which, chips)
        slot = 0
        for n, bit in enumerate(bits):
            slot = slot + ((mask >> (bit.bit_length() - 1)) & 1) * (1 << (len(bits) - 1 - n))
        slots.append(slot)
    return jnp.where(core == 0, slots[0], slots[1])


VMEM = pl.BlockSpec(memory_space=pltpu.VMEM)
SMEM = pl.BlockSpec(memory_space=pltpu.SMEM)
FAR = pl.BlockSpec(memory_space=pl.ANY)
LOAD = "load"


def size_of(array):
    return math.prod(array.shape) * jnp.dtype(array.dtype).itemsize


def call(body, name, ins, outs, scratch=(), spare=6, **more):
    loads = [i for i, (space, _) in enumerate(ins) if space is LOAD]
    spaces = [FAR if space is LOAD else space for space, _ in ins]
    arrays = [array for _, array in ins]
    out_specs = [space for space, _ in outs]
    out_shape = [shape for _, shape in outs]
    held = [arrays[i] for i in loads]
    buffers = [pltpu.VMEM(array.shape, array.dtype) for array in held]
    sems = [pltpu.SemaphoreType.DMA((len(held),))] if held else []
    vmem = sum(size_of(array) for array in held)
    vmem += sum(size_of(a) for space, a in list(ins) + list(outs) if space is VMEM)
    vmem += sum(size_of(b) for b in scratch if b.memory_space == pltpu.VMEM)
    moved = sum(size_of(a) for a in arrays + out_shape)

    def wrapped(*refs):
        inputs = list(refs[: len(ins)])
        outputs = refs[len(ins) : len(ins) + len(outs)]
        rest = refs[len(ins) + len(outs) :]
        kept, tail = rest[: len(held)], rest[len(held) :]
        copies = []
        if held:
            sem, tail = tail[0], tail[1:]
            copies = [
                pltpu.make_async_copy(inputs[i], kept[n], sem.at[n]) for n, i in enumerate(loads)
            ]
        for copy in copies:
            copy.start()
        for n, i in enumerate(loads):
            inputs[i] = kept[n]

        def arrive():
            for copy in copies:
                copy.wait()

        body(arrive, *inputs, *outputs, *tail)

    single = len(outs) == 1
    return pl.pallas_call(
        wrapped,
        in_specs=spaces,
        out_specs=out_specs[0] if single else out_specs,
        out_shape=out_shape[0] if single else out_shape,
        scratch_shapes=buffers + sems + list(scratch),
        compiler_params=pltpu.CompilerParams(vmem_limit_bytes=vmem + (spare << 20)),
        cost_estimate=pl.CostEstimate(flops=0, bytes_accessed=moved, transcendentals=0),
        name=name,
        **more,
    )(*arrays)


def run_copies(pairs, sems):
    for copy in start_copies(pairs, sems):
        copy.wait()


def slice_copies(group, idx_ref, own, blocks, sibling, wbuf):
    chip, core, zh = idx_ref[0], idx_ref[1], idx_ref[2]
    size = blocks.shape[-2]
    pairs = [(own, wbuf.at[zh])]
    for j in range(blocks.shape[0]):
        for source, owner in ((blocks, core), (sibling, 1 - core)):
            home = chip ^ mask_of(j, owner, blocks.shape[0])
            spot = at((2 * home + owner) * size, size, size)
            pairs.append((source.at[j, 9 * group : 9 * group + 9], wbuf.at[1 - zh, :, spot, :]))
    return pairs


def flat_copies(first, idx_ref, blocks, sibling, buffer):
    chip, core = idx_ref[0], idx_ref[1]
    columns, units = buffer.shape[:2]
    chips = blocks.shape[0]
    count = units // (2 * chips)
    pairs = []
    for j in range(chips):
        for source, owner in ((blocks, core), (sibling, 1 - core)):
            home = chip ^ mask_of(j, owner, chips)
            spot = pl.ds((2 * home + owner) * count, count)
            for c in range(columns):
                begin = first + c * count
                pairs.append((source.at[j, begin : begin + count], buffer.at[c, spot]))
    return pairs


def start_copies(pairs, sems):
    copies = [pltpu.make_async_copy(a, b, sems.at[i]) for i, (a, b) in enumerate(pairs)]
    for copy in copies:
        copy.start()
    return copies


def flat_rows(buffer, begin, count):
    columns, _, size, wide = buffer.shape
    return lanes([buffer[c, pl.ds(begin, count)].reshape(count * size, wide) for c in range(columns)])


def halves(spots, side):
    first = (spots // side + 1) // 2 * side
    return ((0, first), (first, spots - first))


def columns_of(size, wide, side):
    return lax.rem(lax.broadcasted_iota(jnp.int32, (size, wide), 0), side)


def at(start, size, unit):
    return pl.ds(pl.multiple_of(start, unit), size)


def pool_body(arrive, x_ref, out_ref):
    arrive()
    rows, width, chans = x_ref.shape[1:]
    half = width // 2
    pixel = lax.broadcasted_iota(jnp.int32, (half, 2 * width), 1)
    place = lax.broadcasted_iota(jnp.int32, (half, 2 * width), 0)
    inside = (lax.rem(pixel, width) >= 2 * place) & (lax.rem(pixel, width) < 2 * place + 2)
    pick = jnp.where(inside, 0.25, 0.0).astype(bf16)
    for image in range(x_ref.shape[0]):
        for row in range(rows // 2):
            window = x_ref[image, 2 * row : 2 * row + 2].reshape(2 * width, chans)
            out_ref[image, row * half : (row + 1) * half, :] = dot(pick, window).astype(bf16)


def pool(pixels):
    images, rows, width, chans = pixels.shape
    shape = struct((images, rows * width // 4, chans), bf16)
    return call(pool_body, "pool", [(LOAD, pixels)], [(VMEM, shape)])


def widen_body(arrive, idx_ref, g_ref, out_ref):
    arrive()
    rows, width, chans = out_ref.shape[1:]
    half = width // 2
    pixel = lax.broadcasted_iota(jnp.int32, (width, half), 0)
    place = lax.broadcasted_iota(jnp.int32, (width, half), 1)
    inside = (pixel >= 2 * place) & (pixel < 2 * place + 2)
    pick = jnp.where(inside, 0.25, 0.0).astype(bf16)
    for image in range(g_ref.shape[0]):
        for row in range(rows // 2):
            wide = dot(pick, g_ref[image, row * half : (row + 1) * half, :]).astype(bf16)
            out_ref[image, 2 * row] = wide
            out_ref[image, 2 * row + 1] = wide


def widen(idx, grad, rows, width):
    images, spots, chans = grad.shape
    step = images // 4
    block = pl.BlockSpec((step, spots, chans), lambda i: (i, 0, 0))
    out = pl.BlockSpec((step, rows, width, chans), lambda i: (i, 0, 0, 0))
    return call(
        widen_body,
        "widen",
        [(SMEM, idx), (block, grad)],
        [(out, struct((images, rows, width, chans), bf16))],
        grid=(4,),
    )


def conv_body(side, first, group, arrive, idx_ref, *refs):
    zh, zl = idx_ref[2], idx_ref[3]
    if first:
        xl, xa, xh, xd, wl, wo, ws, bl, bo, pre_ref, act_ref, xbuf, wbuf, acc, sems = refs
        chans = xl.shape[1]
        spots = xbuf.shape[0]
        begin = zh * (xl.shape[0] - spots)
        pairs = []
        for source, up, along in ((xl, zh, zl), (xa, zh, 1 - zl), (xh, 1 - zh, zl), (xd, 1 - zh, 1 - zl)):
            if source is xl:
                source = xl.at[at(begin, spots, side), :]
            pairs.append((source, xbuf.at[:, at((2 * up + along) * chans, chans, chans)]))
    else:
        xl, xa, wl, wo, ws, bl, bo, pre_ref, act_ref, xbuf, wbuf, acc, sems = refs
        chans = xl.shape[1] // 2
        spots = xbuf.shape[0]
        pairs = []
        for source, along in ((xl, zl), (xa, 1 - zl)):
            for up in range(2):
                pairs.append(
                    (
                        source.at[:, up * chans : (up + 1) * chans],
                        xbuf.at[:, at((2 * up + along) * chans, chans, chans)],
                    )
                )
    run_copies(slice_copies(group, idx_ref, wl, wo, ws, wbuf) + pairs, sems)
    arrive()
    if first:
        for begin, block in halves(spots, side):
            rows = slice(begin, begin + block)
            xbuf[rows, :] = gelu(xbuf[rows, :].astype(f32)).astype(bf16)
    acc[...] = jnp.zeros_like(acc)
    outs = 2 * wl.shape[2]
    for x in range(3):
        weights = lanes([wbuf[u, 3 * y + x] for y in range(3) for u in range(2)])
        for begin, block in halves(spots, side):
            product = dot(xbuf[begin : begin + block, :], weights)
            for y in range(3):
                place = begin + side * (2 - y)
                acc[x, place : place + block, :] += product[:, y * outs : (y + 1) * outs]
    own, other = bl[...], bo[...]
    bias = lanes([jnp.where(zh == 0, own, other), jnp.where(zh == 0, other, own)])
    for begin, block in halves(act_ref.shape[0], side):
        column = columns_of(block, outs, side)
        spot = at(begin + side + zh * side, block, side)
        left = pltpu.roll(acc[0, spot, :], 1, 0)
        right = pltpu.roll(acc[2, spot, :], block - 1, 0)
        pre = acc[1, spot, :] + bias
        pre = pre + jnp.where(column > 0, left, 0.0)
        pre = pre + jnp.where(column < side - 1, right, 0.0)
        pre_ref[begin : begin + block, :] = pre
        act_ref[begin : begin + block, :] = gelu(pre).astype(bf16)


def conv(side, idx, sources, own, other, group, bias, bias_other, first=False):
    taps, depth, outs = own.shape
    spots = sources[1].shape[0]
    rows = spots - side
    return call(
        functools.partial(conv_body, side, first, group),
        "conv",
        [(SMEM, idx)]
        + [(FAR, s) for s in sources]
        + [(FAR, own), (FAR, other[0]), (FAR, other[1])]
        + [(VMEM, bias.reshape(1, outs)), (VMEM, bias_other.reshape(1, outs))],
        [(VMEM, struct((rows, 2 * outs), f32)), (VMEM, struct((rows, 2 * outs), bf16))],
        [
            pltpu.VMEM((spots, depth), bf16),
            pltpu.VMEM((2, taps, depth, outs), bf16),
            pltpu.VMEM((3, spots + 2 * side, 2 * outs), f32),
            pltpu.SemaphoreType.DMA((2 * other[0].shape[0] + 5,)),
        ],
        spare=14 if first else 8,
    )


def spread_taps(side, grad, taps_ref):
    pixels, outs = grad.shape
    column = columns_of(pixels, outs, side)
    wide = grad.astype(f32)
    ahead = jnp.where(column < side - 1, pltpu.roll(wide, pixels - 1, 0), 0.0).astype(bf16)
    behind = jnp.where(column > 0, pltpu.roll(wide, 1, 0), 0.0).astype(bf16)
    edge = jnp.zeros((side, 3 * outs), bf16)
    taps_ref[:side, :] = edge
    taps_ref[side + pixels :, :] = edge
    taps_ref[side : side + pixels, :] = jnp.concatenate([ahead, grad, behind], axis=1)


def tap_block(side, taps_ref, begin, block):
    return lanes([taps_ref[at(begin + side * (2 - y), block, side), :] for y in range(3)])


def slope_body(side, arrive, idx_ref, keep_ref, recv_ref, pre_ref, mine_ref, theirs_ref, gp_ref):
    arrive()
    zh = idx_ref[2]
    half, outs = mine_ref.shape
    total = keep_ref[...] + recv_ref[...].astype(f32)
    spots = keep_ref.shape[0]
    pre = pre_ref[at(zh * (pre_ref.shape[0] - spots), spots, side), :]
    gp_ref[...] = (total * gelu_slope(pre)).astype(bf16)
    own = gp_ref[at(zh * (gp_ref.shape[0] - half), half, side), :]
    low, high = own[:, :outs], own[:, outs:]
    mine_ref[...] = jnp.where(zh == 0, low, high)
    theirs_ref[...] = jnp.where(zh == 0, high, low)


def slope_back(side, idx, keep, recv, pre, half):
    outs = pre.shape[1] // 2
    return call(
        functools.partial(slope_body, side),
        "slope_back",
        [(SMEM, idx), (VMEM, keep), (VMEM, recv), (LOAD, pre)],
        [
            (VMEM, struct((half, outs), bf16)),
            (VMEM, struct((half, outs), bf16)),
            (VMEM, struct(keep.shape, bf16)),
        ],
    )


def back_body(side, last, group, arrive, idx_ref, *refs):
    zh, zl = idx_ref[2], idx_ref[3]
    if last:
        valid_ref, grad_ref, x_ref, go_ref, far_ref, idk_ref, wl, wo, ws, po, ps = refs[:11]
        own_ref, give_ref, taps_ref, wbuf, idk_far, sems = refs[11:]
    else:
        keep_ref, recv_ref, pre_ref, wl, wo, ws, gp_ref, own_ref, give_ref, taps_ref, wbuf, sems = refs
    pairs = slice_copies(group, idx_ref, wl, wo, ws, wbuf)
    if last:
        pairs += flat_copies(9, idx_ref, po, ps, idk_far)
    copies = start_copies(pairs, sems)
    arrive()
    if last:
        grad = grad_ref[...]
    else:
        spots = gp_ref.shape[0]

        def window(ref):
            return ref[at(zh * (ref.shape[0] - spots), spots, side), :]

        total = window(keep_ref) + window(recv_ref).astype(f32)
        grad = (total * gelu_slope(window(pre_ref))).astype(bf16)
        gp_ref[...] = grad
    spread_taps(side, grad, taps_ref)
    depth, outs = wl.shape[1:]
    pixels = own_ref.shape[-2]
    start = zh * side
    for copy in copies:
        copy.wait()
    chans = depth // 4

    def rows(index):
        spot = at(index * chans, chans, chans)
        return lanes([wbuf[u, t, spot, :] for t in range(9) for u in range(2)])

    for target, along in ((give_ref, 1 - zl), (own_ref, zl)):
        if last:
            units = chans // idk_far.shape[2]
            for up in range(2):
                index = 2 * up + along
                weights = rows(index)
                near = idk_ref[at(index * chans, chans, chans), :]
                far = flat_rows(idk_far, index * units, units)
                apart = zh * (far_ref.shape[0] - pixels)
                for begin, block in halves(pixels, side):
                    here = at(zh * pixels + begin, block, side)
                    part = dot(tap_block(side, taps_ref, start + begin, block), weights, NT)
                    x = x_ref[here, at(index * chans, chans, chans)]
                    part = part * gelu_slope(x.astype(f32))
                    part = part + dot(go_ref[here, :], near, NT)
                    part = part + valid_ref[0] * dot(far_ref[at(apart + begin, block, side), :], far, NT)
                    target[up, begin : begin + block, :] = part.astype(target.dtype)
        else:
            weights = jnp.concatenate([rows(along), rows(2 + along)], axis=0)
            for begin, block in halves(pixels, side):
                part = dot(tap_block(side, taps_ref, start + begin, block), weights, NT)
                target[begin : begin + block, :] = part.astype(target.dtype)


def back(side, idx, sources, own, other, group, last=None):
    taps, depth, outs = own.shape
    spots = min(sources[0].shape[0], sources[-1].shape[0])
    copies = 2 * other[0].shape[0] + 1
    extra = []
    scratch = []
    if last:
        valid, full_x, go, cot_far, idk, pieces, half = last
        chans = depth // 4
        shape = (2, half, chans)
        results = []
        extra = [(FAR, pieces[0]), (FAR, pieces[1])]
        sources = list(sources) + [full_x, go, cot_far, idk]
        columns, size = idk.shape[1] // 128, pieces[0].shape[2]
        scratch = [pltpu.VMEM((columns, depth // size, size, 128), bf16)]
        copies += 2 * other[0].shape[0] * columns
    else:
        shape = (spots - side, depth // 2)
        results = [(VMEM, struct((spots, 2 * outs), bf16))]
    results += [(VMEM, struct(shape, f32)), (VMEM, struct(shape, bf16))]
    return call(
        functools.partial(back_body, side, bool(last), group),
        "back",
        [(SMEM, idx)]
        + ([(SMEM, last[0])] if last else [])
        + [(LOAD, source) for source in sources]
        + [(FAR, own), (FAR, other[0]), (FAR, other[1])]
        + extra,
        results,
        [pltpu.VMEM((spots + 2 * side, 6 * outs), bf16), pltpu.VMEM((2, taps, depth, outs), bf16)]
        + scratch
        + [pltpu.SemaphoreType.DMA((copies,))],
        spare=14 if last else 10,
    )


def put_blocks(idx_ref, keep_ref, give_ref, part, tap, first_block, size, begin=0):
    chip, core = idx_ref[0], idx_ref[1]
    for b in range(0, part.shape[0] // size, 2):
        even = part[b * size : (b + 1) * size, :]
        odd = part[(b + 1) * size : (b + 2) * size, :]
        mask = chip ^ ((first_block + b) // 2)
        slot = slot_of(mask, core, keep_ref.shape[0])
        give_slot = slot_of(mask, 1 - core, keep_ref.shape[0])
        rows = slice(begin + tap * size, begin + (tap + 1) * size)
        keep_ref[slot, rows, :] = jnp.where(core == 0, even, odd).astype(bf16)
        give_ref[give_slot, rows, :] = jnp.where(core == 0, odd, even).astype(bf16)


def weight_body(side, half, flat, arrive, idx_ref, gp_ref, *refs):
    if flat:
        full_ref, go_ref, bias_ref = refs[:3]
        refs = refs[3:]
    xl, xa, keep_ref, give_ref, xbuf, taps_ref, sems = refs
    arrive()
    zh, zl = idx_ref[2], idx_ref[3]
    chans = xl.shape[1] // 2
    spots = xbuf.shape[0]
    window = at(zh * (xl.shape[0] - spots), spots, side)
    pairs = []
    for source, along in ((xl, zl), (xa, 1 - zl)):
        for up in range(2):
            pairs.append(
                (
                    source.at[window, up * chans : (up + 1) * chans],
                    xbuf.at[:, at((2 * up + along) * chans, chans, chans)],
                )
            )
    run_copies(pairs, sems)
    wide = gp_ref.shape[1]
    outs = wide // 2
    spot = lax.broadcasted_iota(jnp.int32, (spots, wide), 0) - zh * side
    grad = gp_ref[at(zh * (gp_ref.shape[0] - spots), spots, side), :].astype(f32)
    grad = jnp.where((spot >= 0) & (spot < half), grad, 0.0)
    bias = jnp.sum(grad, axis=0, keepdims=True)
    spread_taps(side, grad.astype(bf16), taps_ref)
    blocks = 2 * keep_ref.shape[0]
    depth = xbuf.shape[1]
    size = depth // blocks
    for begin in range(0, depth, 256):
        values = xbuf[:, begin : begin + 256]
        for y in range(3):
            place = side * (2 - y)
            part = dot(values, taps_ref[place : place + spots, :], TN)
            for x in range(3):
                for u in range(2):
                    col = x * wide + u * outs
                    put_blocks(
                        idx_ref, keep_ref, give_ref, part[:, col : col + outs],
                        3 * y + x, begin // size, size, u * (9 * size + 16),
                    )
    for u in range(2):
        row = jnp.broadcast_to(bias[:, u * outs : (u + 1) * outs], (16, outs)).astype(bf16)
        for j in range(keep_ref.shape[0]):
            spot = slice(u * (9 * size + 16) + 9 * size, (u + 1) * (9 * size + 16))
            keep_ref[j, spot, :] = row
            give_ref[j, spot, :] = row
    if flat:
        first = 2 * (9 * size + 16)
        flat_pieces(1.0, idx_ref, full_ref, go_ref, bias_ref, keep_ref, give_ref, first)


def weight_grad(side, half, idx, grad, act, act_other, chips, flat=()):
    spots = half + side
    wide = grad.shape[1]
    outs = wide // 2
    depth = 2 * act.shape[1]
    rows = 2 * (9 * depth // (2 * chips) + 16)
    if flat:
        rows += flat_size(flat[0], flat[1], chips)
    return call(
        functools.partial(weight_body, side, half, bool(flat)),
        "weight_grad",
        [(SMEM, idx), (LOAD, grad)] + [(LOAD, a) for a in flat] + [(FAR, act), (FAR, act_other)],
        [(VMEM, struct((chips, rows, outs), bf16))] * 2,
        [
            pltpu.VMEM((spots, depth), bf16),
            pltpu.VMEM((spots + 2 * side, 3 * wide), bf16),
            pltpu.SemaphoreType.DMA((4,)),
        ],
        spare=10,
    )


def weight_one_body(side, arrive, idx_ref, mine_ref, theirs_ref, x_ref, *refs):
    keep_ref, give_ref, gp_ref, taps_ref = refs
    arrive()
    zh = idx_ref[2]
    half, outs = mine_ref.shape
    gp_ref[at(zh * half, half, side), :] = mine_ref[...]
    gp_ref[at((1 - zh) * half, half, side), :] = theirs_ref[...]
    grad = gp_ref[...]
    bias = jnp.sum(grad.astype(f32), axis=0, keepdims=True)
    spread_taps(side, grad, taps_ref)
    blocks = 2 * keep_ref.shape[0]
    spots, depth = x_ref.shape
    size = depth // blocks
    right = tap_block(side, taps_ref, 0, spots)
    for begin in range(0, depth, 256):
        part = dot(x_ref[:, begin : begin + 256], right, TN)
        for tap in range(9):
            put_blocks(
                idx_ref, keep_ref, give_ref, part[:, tap * outs : (tap + 1) * outs],
                tap, begin // size, size,
            )
    row = jnp.broadcast_to(bias, (16, outs)).astype(bf16)
    first = 9 * size + 16
    for j in range(keep_ref.shape[0]):
        keep_ref[j, 9 * size : first, :] = row
        give_ref[j, 9 * size : first, :] = row


def weight_one_grad(side, idx, mine, theirs, act_zero, chips):
    spots, depth = act_zero.shape
    outs = mine.shape[1]
    rows = 9 * depth // (2 * chips) + 16
    return call(
        functools.partial(weight_one_body, side),
        "weight_one_grad",
        [(SMEM, idx), (LOAD, mine), (LOAD, theirs), (LOAD, act_zero)],
        [(VMEM, struct((chips, rows, outs), bf16))] * 2,
        [
            pltpu.VMEM((spots, outs), bf16),
            pltpu.VMEM((spots + 2 * side, 3 * outs), bf16),
        ],
        spare=14,
    )


def fold_body(pairs, arrive, idx_ref, *refs):
    arrive()
    ins, (keep_ref, give_ref) = refs[: 2 * pairs], refs[2 * pairs :]
    half = keep_ref.shape[0]
    for i in range(2 * half):
        target = keep_ref if i < half else give_ref
        begin = 0
        for keep, recv in zip(ins[0::2], ins[1::2]):
            rows = keep.shape[1]
            total = keep[i].astype(f32) + recv[i].astype(f32)
            target[i % half, begin : begin + rows, :] = total.astype(bf16)
            begin += rows


def fold(idx, *arrays):
    blocks, _, wide = arrays[0].shape
    rows = sum(a.shape[1] for a in arrays[0::2])
    return call(
        functools.partial(fold_body, len(arrays) // 2),
        "fold",
        [(SMEM, idx)] + [(VMEM, a) for a in arrays],
        [(VMEM, struct((blocks // 2, rows, wide), bf16))] * 2,
    )


def last_body(slotted, rest, arrive, idx_ref, keep_in, recv_in, *targets):
    arrive()
    zh = idx_ref[2]

    def put(target, place, begin, rows):
        spot = at(begin, rows, 16)
        total = keep_in[0, spot, :].astype(f32) + recv_in[0, spot, :].astype(f32)
        target[place : place + rows, :] = total.astype(bf16)

    place = 0
    for begin, rows in slotted:
        put(targets[0], place, begin + zh * rows, rows)
        put(targets[1], place, begin + (1 - zh) * rows, rows)
        place += rows
    begin, rows = rest
    put(targets[-1], 0, begin, rows)


def last_fold(idx, keep, recv, slotted=(), rest=None):
    wide = keep.shape[2]
    rest = rest or (0, keep.shape[1])
    rows = sum(size for _, size in slotted)
    sizes = ([rows, rows] if slotted else []) + [rest[1]]
    return call(
        functools.partial(last_body, slotted, rest),
        "last_fold",
        [(SMEM, idx), (VMEM, keep), (VMEM, recv)],
        [(VMEM, struct((size, wide), bf16)) for size in sizes],
    )


def final_body(parts, arrive, idx_ref, own_ref, sib_ref, *refs):
    arrive()
    outs, stages, sems = refs[: 2 * len(parts)], refs[2 * len(parts) : -1], refs[-1]
    chip, core = idx_ref[0], idx_ref[1]
    chips, _, wide = own_ref.shape
    first = 0
    copies = []

    def store(source, target):
        copies.append(pltpu.make_async_copy(source, target, sems.at[len(copies)]))
        copies[-1].start()

    for n, part in enumerate(parts):
        grad_ref, bias_ref, stage = outs[2 * n], outs[2 * n + 1], stages[n]
        size = part[0] // (2 * chips)
        columns = 1 if len(part) == 1 else part[1] // wide
        end = first + size * (9 if len(part) == 1 else columns)
        for c in range(columns):
            row = own_ref[0, end + c : end + c + 1, :].astype(f32)
            bias_ref[:, c * wide : (c + 1) * wide] = row
        for n_row, begin in enumerate(range(first, end, size)):
            for j in range(chips):
                for source, owner in ((own_ref, core), (sib_ref, 1 - core)):
                    home = chip ^ mask_of(j, owner, chips)
                    spot = at((2 * home + owner) * size, size, size)
                    piece = source[j, begin : begin + size, :].astype(f32)
                    if len(part) == 1:
                        stage[n_row, spot, :] = piece
                    else:
                        stage[spot, n_row * wide : (n_row + 1) * wide] = piece
            if len(part) == 1:
                store(stage.at[n_row], grad_ref.at[n_row])
        if len(part) > 1:
            store(stage, grad_ref)
        first = end + 16
    for copy in copies:
        copy.wait()


def final_grads(idx, own, sib, parts):
    wide = own.shape[2]
    results, stages = [], []
    for part in parts:
        shape = (9, part[0], wide) if len(part) == 1 else part
        results += [(FAR, struct(shape, f32)), (VMEM, struct((1, shape[-1]), f32))]
        stages.append(pltpu.VMEM(shape, f32))
    copies = sum(9 if len(part) == 1 else 1 for part in parts)
    return call(
        functools.partial(final_body, parts),
        "final_grads",
        [(SMEM, idx), (VMEM, own), (VMEM, sib)],
        results,
        stages + [pltpu.SemaphoreType.DMA((copies,))],
    )


def flat_pieces(gain, idx_ref, x_ref, go_ref, bias_ref, keep_ref, give_ref, first):
    chip, core = idx_ref[0], idx_ref[1]
    chips, _, wide = keep_ref.shape
    columns = go_ref.shape[1] // wide
    size = x_ref.shape[1] // (2 * chips)
    bias = jnp.concatenate(
        [bias_ref[:, c * wide : (c + 1) * wide] for c in range(columns)]
        + [jnp.zeros((16 - columns, wide), f32)],
        axis=0,
    ).astype(bf16)
    for j in range(chips):
        keep_ref[j, first + columns * size :, :] = bias
        give_ref[j, first + columns * size :, :] = bias
    for begin in range(0, x_ref.shape[1], 256):
        part = gain * dot(x_ref[:, begin : begin + 256], go_ref[...], TN)
        for b in range(0, 256 // size, 2):
            mask = chip ^ ((begin // size + b) // 2)
            slot = slot_of(mask, core, chips)
            give_slot = slot_of(mask, 1 - core, chips)
            for c in range(columns):
                even = part[b * size : (b + 1) * size, c * wide : (c + 1) * wide]
                odd = part[(b + 1) * size : (b + 2) * size, c * wide : (c + 1) * wide]
                spot = slice(first + c * size, first + (c + 1) * size)
                keep_ref[slot, spot, :] = jnp.where(core == 0, even, odd).astype(bf16)
                give_ref[give_slot, spot, :] = jnp.where(core == 0, odd, even).astype(bf16)


def flat_size(x, go, chips):
    return (go.shape[1] // 128) * (x.shape[1] // (2 * chips)) + 16


def outer_body(gain, arrive, idx_ref, x_ref, go_ref, bias_ref, keep_ref, give_ref):
    arrive()
    flat_pieces(gain, idx_ref, x_ref, go_ref, bias_ref, keep_ref, give_ref, 0)


def outer(idx, x, go, gain, bias, chips):
    return call(
        functools.partial(outer_body, gain),
        "outer",
        [(SMEM, idx), (LOAD, x), (LOAD, go), (LOAD, bias)],
        [(VMEM, struct((chips, flat_size(x, go, chips), 128), bf16))] * 2,
        spare=8,
    )


def start_body(arrive, idx_ref, valid_ref, cot_ref, outk_ref, go_ref, bias_ref, own_ref, give_ref):
    arrive()
    zl = idx_ref[3]
    masked = cot_ref[...].astype(f32) * valid_ref[0]
    go_ref[...] = masked.astype(bf16)
    bias_ref[...] = jnp.sum(masked, axis=0, keepdims=True)
    chans = outk_ref.shape[0] // 4
    block = cot_ref.shape[0] // 4
    for target, along in ((give_ref, 1 - zl), (own_ref, zl)):
        weights = jnp.concatenate(
            [outk_ref[at((2 * up + along) * chans, chans, chans), :] for up in range(2)], axis=0
        )
        for begin in range(0, cot_ref.shape[0], block):
            part = post_gain * dot(go_ref[begin : begin + block, :], weights, NT)
            target[begin : begin + block, :] = part.astype(target.dtype)


def start_back(idx, valid, cot, outk):
    spots, outs = cot.shape
    half = outk.shape[0] // 2
    return call(
        start_body,
        "start_back",
        [(SMEM, idx), (SMEM, valid), (LOAD, cot), (LOAD, outk)],
        [
            (VMEM, struct(cot.shape, bf16)),
            (VMEM, struct((1, outs), f32)),
            (VMEM, struct((spots, half), f32)),
            (VMEM, struct((spots, half), bf16)),
        ],
    )


def rows_body(side, arrive, idx_ref, own_ref, recv_ref, keep_ref, give_ref):
    arrive()
    zh = idx_ref[2]
    spots = keep_ref.shape[0]
    apart = own_ref.shape[0] - spots
    for target, begin in ((give_ref, (1 - zh) * apart), (keep_ref, zh * apart)):
        spot = at(begin, spots, side)
        total = own_ref[spot, :] + recv_ref[spot, :].astype(f32)
        target[...] = total.astype(target.dtype)


def rows_sum(side, idx, own, recv, spots):
    shape = (spots, own.shape[1])
    return call(
        functools.partial(rows_body, side),
        "rows_sum",
        [(SMEM, idx), (LOAD, own), (LOAD, recv)],
        [(VMEM, struct(shape, f32)), (VMEM, struct(shape, bf16))],
    )


def slots_body(arrive, idx_ref, own_ref, recv_ref, keep_ref, give_ref):
    arrive()
    zh = idx_ref[2]
    for target, slot in ((give_ref, 1 - zh), (keep_ref, zh)):
        total = own_ref[slot] + recv_ref[slot].astype(f32)
        target[...] = total.astype(bf16)


def slots_sum(idx, own, recv):
    shape = struct(own.shape[1:], bf16)
    return call(
        slots_body,
        "slots_sum",
        [(SMEM, idx), (VMEM, own), (VMEM, recv)],
        [(VMEM, shape), (VMEM, shape)],
    )


def input_body(arrive, idx_ref, keep_ref, recv_ref, out_ref):
    arrive()
    zh = idx_ref[2]
    half = keep_ref.shape[0]
    out_ref[at(zh * half, half, half), :] = keep_ref[...]
    out_ref[at((1 - zh) * half, half, half), :] = recv_ref[...]


def input_grad(idx, keep, recv):
    half, chans = keep.shape
    return call(
        input_body,
        "input_grad",
        [(SMEM, idx), (VMEM, keep), (VMEM, recv)],
        [(VMEM, struct((2 * half, chans), bf16))],
    )


def whole_body(side, arrive, idx_ref, xl, xa, xh, xd, rh, rl, x_ref, act_ref, sems):
    arrive()
    zh, zl = idx_ref[2], idx_ref[3]
    chans = xl.shape[1]
    spots = xa.shape[0]
    rest = xl.shape[0] - spots
    window, outside = at(zh * rest, spots, side), at((1 - zh) * spots, rest, side)

    def cols(up, along):
        return at((2 * up + along) * chans, chans, chans)

    run_copies(
        [
            (xl, x_ref.at[:, cols(zh, zl)]),
            (xa, x_ref.at[window, cols(zh, 1 - zl)]),
            (xh, x_ref.at[window, cols(1 - zh, zl)]),
            (xd, x_ref.at[window, cols(1 - zh, 1 - zl)]),
            (rl.at[0], x_ref.at[outside, cols(zh, 1 - zl)]),
            (rh, x_ref.at[outside, cols(1 - zh, zl)]),
            (rl.at[1], x_ref.at[outside, cols(1 - zh, 1 - zl)]),
        ],
        sems,
    )
    block = x_ref.shape[0] // 8
    for begin in range(0, x_ref.shape[0], block):
        rows = slice(begin, begin + block)
        act_ref[rows, :] = gelu(x_ref[rows, :].astype(f32)).astype(bf16)


def whole_input(side, idx, *parts):
    spots, chans = parts[0].shape
    return call(
        functools.partial(whole_body, side),
        "whole_input",
        [(SMEM, idx)] + [(FAR, p) for p in parts],
        [(VMEM, struct((spots, 4 * chans), bf16))] * 2,
        [pltpu.SemaphoreType.DMA((7,))],
    )


def join_body(arrive, idx_ref, own, recv, far_own, far_recv, out, sems):
    arrive()
    zh, zl = idx_ref[2], idx_ref[3]
    half = own.shape[0]
    chans = own.shape[1] // 2
    pairs = []
    for source, up, along in ((own, zh, zl), (recv, zh, 1 - zl), (far_own, 1 - zh, zl), (far_recv, 1 - zh, 1 - zl)):
        for slot in range(2):
            spot = at((2 * slot + along) * chans, chans, chans)
            target = out.at[at(up * half, half, half), spot]
            pairs.append((source.at[:, slot * chans : (slot + 1) * chans], target))
    run_copies(pairs, sems)


def join(idx, *parts):
    half, wide = parts[0].shape
    return call(
        join_body,
        "join",
        [(SMEM, idx)] + [(FAR, p) for p in parts],
        [(VMEM, struct((2 * half, 2 * wide), bf16))],
        [pltpu.SemaphoreType.DMA((8,))],
    )


def finish_body(arrive, idx_ref, valid_ref, x_ref, act_ref, idk_ref, outk_ref, ib_ref, out_ref):
    arrive()
    block = x_ref.shape[0] // 4
    for begin in range(0, x_ref.shape[0], block):
        rows = slice(begin, begin + block)
        identity = dot(x_ref[rows, :], idk_ref[...]) + ib_ref[...]
        branch = dot(act_ref[rows, :], outk_ref[...])
        out_ref[rows, :] = ((identity + post_gain * branch) * valid_ref[0]).astype(bf16)


def finish(idx, valid, x, act, idk, outk, ib):
    outs = idk.shape[1]
    return call(
        finish_body,
        "finish",
        [(SMEM, idx), (SMEM, valid), (LOAD, x), (LOAD, act), (LOAD, idk), (LOAD, outk)]
        + [(VMEM, ib.reshape(1, outs))],
        [(VMEM, struct((x.shape[0], outs), bf16))],
        spare=8,
    )


def flip(value, axis):
    return lax.ppermute(value, axis, [(0, 1), (1, 0)])


def cross(value, step, chips):
    pairs = []
    for chip in range(chips):
        for core in range(2):
            other = chip ^ step_bits(core, chips)[step]
            pairs.append((2 * chip + core, 2 * other + core))
    return lax.ppermute(value, DP, pairs)


def hops(value, chips):
    blocks = [value]
    for i in range(1, chips):
        pairs = []
        for chip in range(chips):
            for core in range(2):
                bits = step_bits(core, chips)
                mask = sum(bit for n, bit in enumerate(bits) if i >> (len(bits) - 1 - n) & 1)
                pairs.append((2 * (chip ^ mask) + core, 2 * chip + core))
        blocks.append(lax.ppermute(value, DP, pairs))
    return blocks


def swap(pieces, axis):
    return lax.all_to_all(pieces, axis, split_axis=0, concat_axis=0, tiled=True)


def after(value, other):
    return lax.optimization_barrier((value, other))[0]


def rows_of(value, start, size):
    return lax.dynamic_slice_in_dim(value, start, size, 0)


def local(
    pixels,
    counts,
    kernel_one,
    bias_one,
    kernel_two,
    bias_two,
    kernel_three,
    bias_three,
    out_kernel,
    identity_kernel,
    identity_bias,
    cotangent,
):
    images, rows, width, chans = pixels.shape
    side = width // 2
    spots = side * side
    half = spots // 2
    window = half + halo * side
    outs = cotangent.shape[3]
    chips = lax.axis_size("chip")
    chip, core, zh, zl = [lax.axis_index(a) for a in ("chip", "core", "zh", "zl")]
    idx = jnp.stack([chip, core, zh, zl]).astype(jnp.int32)
    taps = lambda kernel: kernel.reshape((9,) + kernel.shape[2:])
    one, two, three = taps(kernel_one), taps(kernel_two), taps(kernel_three)

    own_count = lax.dynamic_index_in_dim(counts, 2 * chip + core, 0, keepdims=True)
    valid = (own_count > 0).astype(f32)

    place = 2 * chip + core

    def units_of(kernel, size):
        if kernel.ndim == 3:
            block = kernel.shape[1] // (2 * chips)
            return lax.dynamic_slice_in_dim(kernel, place * block, block, 1)
        block = kernel.shape[0] // (2 * chips)
        block = lax.dynamic_slice_in_dim(kernel, place * block, block, 0)
        block = block.reshape(-1, size, block.shape[1] // 128, 128)
        return block.transpose(2, 0, 1, 3).reshape(-1, size, 128)

    steps = chips.bit_length() - 1

    def start_spread(piece, *others):
        return jnp.concatenate(after((piece[None], cross(piece[None], steps - 1, chips)), others))

    def end_spread(own, *others):
        for step in reversed(range(steps - 1)):
            own = jnp.concatenate(after((own, cross(own, step, chips)), others))
        return own, flip(own, "core")

    last = [idx]

    def turn(*others):
        return after(idx, (last[0],) + others)

    def ran(results):
        last[0] = results[-1] if isinstance(results, (list, tuple)) else results
        return results

    size = two.shape[1] // (2 * chips)
    deep = two.shape[1]
    cot = cotangent.reshape(spots, outs)
    one_piece = flip(units_of(one, size), "zh")
    pooled = ran(pool(pixels))
    go, identity_bias_grad, ga_own, ga_give = ran(start_back(turn(), valid, cot, out_kernel))
    bias_other = flip(after(jnp.stack([bias_one, bias_two, bias_three]), go), "zh")
    two_piece = units_of(after(two, pooled), size)
    last_piece = jnp.concatenate([units_of(after(k, pooled), size) for k in (three, identity_kernel)])
    cot_rows = rows_of(after(cot, pooled), (1 - zh) * half, half)
    xl = swap(after(pooled, (one_piece, two_piece, last_piece, cot_rows, ga_give)), DP)
    xl = xl.reshape(spots, chans)
    two_piece = flip(after(two_piece, one_piece), "zh")

    apart = spots - window
    xa = flip(rows_of(xl, zh * apart, window), "zl")
    xh = flip(rows_of(xl, (1 - zh) * apart, window), "zh")
    rest = spots - window
    rest_own = rows_of(xl, (1 - zh) * window, rest)
    rest_high = rows_of(xl, zh * window, rest)
    two_near = start_spread(after(two_piece, xl))
    one_near = start_spread(after(one_piece, xl), xh, xa, two_near, bias_other)
    xd = flip(xh, "zl")
    last_piece = flip(after(last_piece, xh), "zh")
    two_other = end_spread(two_near, xd)
    one_other = end_spread(one_near, xd, two_other[0], last_piece)
    ga_recv = flip(after(ga_give, xd), "zl")
    rest_high = flip(after(rest_high, xd), "zh")

    pre_one, act_one = ran(
        conv(
            side, turn(), (xl, xa, xh, xd), one, one_other, 0, bias_one, bias_other[0], True
        )
    )
    act_one_other = flip(act_one, "zl")
    ga_own, ga_give = ran(rows_sum(side, turn(), ga_own, ga_recv, half + (halo - 3) * side))
    pre_two, act_two = ran(
        conv(side, turn(), (act_one, act_one_other), two, two_other, 0, bias_two, bias_other[1])
    )
    act_two_other = flip(act_two, "zl")
    ga_recv = flip(after(ga_give, act_two), "zh")
    last_other = jnp.stack(after(hops(after(last_piece, act_one), chips), act_two))
    last_other = last_other, flip(last_other, "core")
    pre_three, act_three = ran(
        conv(side, turn(), (act_two, act_two_other), three, last_other, 0, bias_three, bias_other[2])
    )
    rest_low = flip(jnp.stack(after((rest_own, rest_high), act_three)), "zl")
    cot_far = flip(after(cot_rows, act_three), "zh")
    own_rows = rows_of(act_three, zh * (halo - 3) * side, half)

    gp_three, ga_own, ga_give = ran(
        back(side, turn(), (ga_own, ga_recv, pre_three), three, last_other, 0)
    )
    ga_recv = flip(ga_give, "zl")
    full_x, act_zero = ran(whole_input(side, turn(), xl, xa, xh, xd, rest_high, rest_low))
    keep_three, give_three = ran(
        weight_grad(
            side, half, turn(), gp_three, act_two, act_two_other, chips, (full_x, go, identity_bias_grad)
        )
    )
    gp_two, ga_own, ga_give = ran(
        back(side, turn(), (ga_own, ga_recv, pre_two), two, two_other, 0)
    )
    ga_recv = flip(ga_give, "zl")
    keep_two, give_two = ran(weight_grad(side, half, turn(cot_far), gp_two, act_one, act_one_other, chips))

    gp_mine, gp_theirs, gp_one = ran(slope_back(side, turn(), ga_own, ga_recv, pre_one, half))
    gp_theirs = flip(gp_theirs, "zh")
    recv_three = flip(after(give_three, gp_one), "core")
    recv_two = flip(after(give_two, gp_one), "core")
    gx_own, gx_give = ran(
        back(
            side, turn(), (gp_one,), one, one_other, 0,
            (valid, full_x, go, cot_far, identity_kernel, last_other, half),
        )
    )

    def folds(keep, recv, first, *others):
        for step in range(first, steps):
            keep, give = ran(fold(turn(*others), keep, recv))
            recv = cross(give, step, chips)
        return keep, recv

    keep_deep, give_deep = ran(fold(turn(gp_theirs), keep_three, recv_three, keep_two, recv_two))
    recv_deep = cross(give_deep, 0, chips)
    gx_recv = flip(after(gx_give, keep_deep), "zl")
    own_rows = after(own_rows, keep_deep)
    near_rows = flip(own_rows, "zl")
    far_rows = flip(own_rows, "zh")
    keep_one, give_one = ran(weight_one_grad(side, turn(), gp_mine, gp_theirs, act_zero, chips))
    recv_one = flip(give_one, "core")
    gx_keep, gx_give = ran(slots_sum(turn(), gx_own, gx_recv))
    gx_recv = flip(gx_give, "zh")
    keep_deep, recv_deep = folds(keep_deep, recv_deep, 1)
    keep_one, give_one = ran(fold(turn(), keep_one, recv_one))
    recv_one = cross(give_one, 0, chips)
    slot = 9 * size + 16
    flat = keep_three.shape[1] - 2 * slot
    keep_deep, give_deep, id_rows = ran(
        last_fold(
            turn(), keep_deep, recv_deep, ((0, slot), (2 * slot + flat, slot)), (2 * slot, flat)
        )
    )
    recv_deep = flip(give_deep, "zh")
    far_near_rows = flip(after(far_rows, keep_deep), "zl")
    keep_one, recv_one = folds(keep_one, recv_one, 1)
    full_three = ran(join(turn(), own_rows, near_rows, far_rows, far_near_rows))
    keep_out, give_out = ran(outer(turn(), full_three, go, post_gain, identity_bias_grad, chips))
    recv_out = flip(give_out, "core")
    (total_one,) = ran([last_fold(turn(), keep_one, recv_one)])
    keep_out, give_out = ran(fold(turn(), keep_out, recv_out))
    recv_out = cross(give_out, 0, chips)
    deep_rows = (after(keep_deep, keep_out).astype(f32) + recv_deep.astype(f32)).astype(bf16)
    deep_rows = jnp.concatenate([deep_rows, id_rows])
    near_deep = start_spread(deep_rows)
    block_out = ran(
        finish(turn(deep_rows), valid, full_x, full_three, identity_kernel, out_kernel, identity_bias)
    )
    keep_out, recv_out = folds(keep_out, recv_out, 1)
    gx = ran(input_grad(turn(), gx_keep, gx_recv))
    gx = swap(gx.reshape(images, rows * width // 4, chans), DP)
    (total_out,) = ran([last_fold(turn(), keep_out, recv_out)])
    near_one = start_spread(jnp.concatenate([total_one, total_out]))
    pixels_grad = ran(widen(turn(near_one), gx, rows, width))
    all_deep = end_spread(near_deep, pixels_grad)
    all_one = end_spread(near_one)
    (
        kernel_three_grad,
        bias_three_grad,
        kernel_two_grad,
        bias_two_grad,
        identity_kernel_grad,
        identity_bias_grad,
    ) = ran(final_grads(turn(), *all_deep, ((deep,), (deep,), identity_kernel.shape)))
    kernel_one_grad, bias_one_grad, out_kernel_grad, _ = ran(
        final_grads(turn(), *all_one, ((one.shape[1],), out_kernel.shape))
    )

    return (
        block_out.reshape(cotangent.shape),
        pixels_grad,
        kernel_one_grad.reshape(kernel_one.shape),
        bias_one_grad[0],
        kernel_two_grad.reshape(kernel_two.shape),
        bias_two_grad[0],
        kernel_three_grad.reshape(kernel_three.shape),
        bias_three_grad[0],
        out_kernel_grad,
        identity_kernel_grad,
        identity_bias_grad[0],
    )


def solution(mesh):
    members = mesh.devices.size // mesh.shape["mp"]
    fine = Mesh(
        mesh.devices.reshape(members // 2, 2, 2, mesh.shape["mp"] // 2),
        ("chip", "core", "zh", "zl"),
    )
    return jax.shard_map(
        local,
        mesh=fine,
        in_specs=(
            P(None, DP, None, MP),
            P(),
            P(None, None, None, MP),
            P(MP),
            P(None, None, None, MP),
            P(MP),
            P(None, None, None, MP),
            P(MP),
            P(None, MP),
            P(None, MP),
            P(MP),
            P(DP, None, None, MP),
        ),
        out_specs=(
            P(DP, None, None, MP),
            P(None, DP, None, MP),
            P(None, None, None, MP),
            P(MP),
            P(None, None, None, MP),
            P(MP),
            P(None, None, None, MP),
            P(MP),
            P(None, MP),
            P(None, MP),
            P(MP),
        ),
        check_vma=False,
    )
```

```python
import functools
import math

import jax
import jax.numpy as jnp
from jax import lax
from jax.experimental import pallas as pl
from jax.experimental.pallas import tpu as pltpu
from jax.sharding import Mesh
from jax.sharding import PartitionSpec as P


post_gain = 0.015625
slope = 0.7978845608028654
cubic = 0.044715
halo = 6
bf16 = jnp.bfloat16
f32 = jnp.float32
NT = (((1,), (1,)), ((), ()))
TN = (((0,), (0,)), ((), ()))
NN = (((1,), (0,)), ((), ()))
DP = ("chip", "core")
MP = ("zh", "zl")


def dot(left, right, dims=NN):
    return lax.dot_general(left, right, dims, preferred_element_type=f32)


def gelu(value):
    inner = jnp.tanh(slope * (value + cubic * value * value * value))
    return 0.5 * value * (1.0 + inner)


def gelu_slope(value):
    square = value * value
    inner = jnp.tanh(slope * value * (1.0 + cubic * square))
    climb = slope * (1.0 + 3.0 * cubic * square)
    return 0.5 * (1.0 + inner) + 0.5 * value * (1.0 - inner * inner) * climb


def struct(shape, kind):
    return jax.ShapeDtypeStruct(shape, kind)


def lanes(blocks):
    return blocks[0] if len(blocks) == 1 else jnp.concatenate(blocks, axis=1)


def step_bits(core, chips):
    bits = [1 << n for n in range(chips.bit_length() - 1)]
    for n in range(0, len(bits) - 1, 2) if core else ():
        bits[n], bits[n + 1] = bits[n + 1], bits[n]
    return bits


def mask_of(i, core, chips):
    masks = []
    for which in range(2):
        bits = step_bits(which, chips)
        masks.append(sum(bit for n, bit in enumerate(bits) if i >> (len(bits) - 1 - n) & 1))
    return jnp.where(core == 0, masks[0], masks[1])


def slot_of(mask, core, chips):
    slots = []
    for which in range(2):
        bits = step_bits(which, chips)
        slot = 0
        for n, bit in enumerate(bits):
            slot = slot + ((mask >> (bit.bit_length() - 1)) & 1) * (1 << (len(bits) - 1 - n))
        slots.append(slot)
    return jnp.where(core == 0, slots[0], slots[1])


VMEM = pl.BlockSpec(memory_space=pltpu.VMEM)
SMEM = pl.BlockSpec(memory_space=pltpu.SMEM)
FAR = pl.BlockSpec(memory_space=pl.ANY)
LOAD = "load"


def size_of(array):
    return math.prod(array.shape) * jnp.dtype(array.dtype).itemsize


def call(body, name, ins, outs, scratch=(), spare=6, **more):
    loads = [i for i, (space, _) in enumerate(ins) if space is LOAD]
    spaces = [FAR if space is LOAD else space for space, _ in ins]
    arrays = [array for _, array in ins]
    out_specs = [space for space, _ in outs]
    out_shape = [shape for _, shape in outs]
    held = [arrays[i] for i in loads]
    buffers = [pltpu.VMEM(array.shape, array.dtype) for array in held]
    sems = [pltpu.SemaphoreType.DMA((len(held),))] if held else []
    vmem = sum(size_of(array) for array in held)
    vmem += sum(size_of(a) for space, a in list(ins) + list(outs) if space is VMEM)
    vmem += sum(size_of(b) for b in scratch if b.memory_space == pltpu.VMEM)
    moved = sum(size_of(a) for a in arrays + out_shape)

    def wrapped(*refs):
        inputs = list(refs[: len(ins)])
        outputs = refs[len(ins) : len(ins) + len(outs)]
        rest = refs[len(ins) + len(outs) :]
        kept, tail = rest[: len(held)], rest[len(held) :]
        copies = []
        if held:
            sem, tail = tail[0], tail[1:]
            copies = [
                pltpu.make_async_copy(inputs[i], kept[n], sem.at[n]) for n, i in enumerate(loads)
            ]
        for copy in copies:
            copy.start()
        for n, i in enumerate(loads):
            inputs[i] = kept[n]

        def arrive():
            for copy in copies:
                copy.wait()

        body(arrive, *inputs, *outputs, *tail)

    single = len(outs) == 1
    return pl.pallas_call(
        wrapped,
        in_specs=spaces,
        out_specs=out_specs[0] if single else out_specs,
        out_shape=out_shape[0] if single else out_shape,
        scratch_shapes=buffers + sems + list(scratch),
        compiler_params=pltpu.CompilerParams(vmem_limit_bytes=vmem + (spare << 20)),
        cost_estimate=pl.CostEstimate(flops=0, bytes_accessed=moved, transcendentals=0),
        name=name,
        **more,
    )(*arrays)


def run_copies(pairs, sems):
    for copy in start_copies(pairs, sems):
        copy.wait()


def slice_copies(group, idx_ref, own, blocks, sibling, wbuf):
    chip, core, zh = idx_ref[0], idx_ref[1], idx_ref[2]
    size = blocks.shape[-2]
    pairs = [(own, wbuf.at[zh])]
    for j in range(blocks.shape[0]):
        for source, owner in ((blocks, core), (sibling, 1 - core)):
            home = chip ^ mask_of(j, owner, blocks.shape[0])
            spot = at((2 * home + owner) * size, size, size)
            pairs.append((source.at[j, 9 * group : 9 * group + 9], wbuf.at[1 - zh, :, spot, :]))
    return pairs


def flat_copies(first, idx_ref, blocks, sibling, buffer):
    chip, core = idx_ref[0], idx_ref[1]
    columns, units = buffer.shape[:2]
    chips = blocks.shape[0]
    count = units // (2 * chips)
    pairs = []
    for j in range(chips):
        for source, owner in ((blocks, core), (sibling, 1 - core)):
            home = chip ^ mask_of(j, owner, chips)
            spot = pl.ds((2 * home + owner) * count, count)
            for c in range(columns):
                begin = first + c * count
                pairs.append((source.at[j, begin : begin + count], buffer.at[c, spot]))
    return pairs


def start_copies(pairs, sems):
    copies = [pltpu.make_async_copy(a, b, sems.at[i]) for i, (a, b) in enumerate(pairs)]
    for copy in copies:
        copy.start()
    return copies


def flat_rows(buffer, begin, count):
    columns, _, size, wide = buffer.shape
    return lanes([buffer[c, pl.ds(begin, count)].reshape(count * size, wide) for c in range(columns)])


def halves(spots, side):
    first = (spots // side + 1) // 2 * side
    return ((0, first), (first, spots - first))


def columns_of(size, wide, side):
    return lax.rem(lax.broadcasted_iota(jnp.int32, (size, wide), 0), side)


def at(start, size, unit):
    return pl.ds(pl.multiple_of(start, unit), size)


def pool_body(arrive, x_ref, out_ref):
    arrive()
    rows, width, chans = x_ref.shape[1:]
    half = width // 2
    pixel = lax.broadcasted_iota(jnp.int32, (half, 2 * width), 1)
    place = lax.broadcasted_iota(jnp.int32, (half, 2 * width), 0)
    inside = (lax.rem(pixel, width) >= 2 * place) & (lax.rem(pixel, width) < 2 * place + 2)
    pick = jnp.where(inside, 0.25, 0.0).astype(bf16)
    for image in range(x_ref.shape[0]):
        for row in range(rows // 2):
            window = x_ref[image, 2 * row : 2 * row + 2].reshape(2 * width, chans)
            out_ref[image, row * half : (row + 1) * half, :] = dot(pick, window).astype(bf16)


def pool(pixels):
    images, rows, width, chans = pixels.shape
    shape = struct((images, rows * width // 4, chans), bf16)
    return call(pool_body, "pool", [(LOAD, pixels)], [(VMEM, shape)])


def widen_body(arrive, idx_ref, g_ref, out_ref):
    arrive()
    rows, width, chans = out_ref.shape[1:]
    half = width // 2
    pixel = lax.broadcasted_iota(jnp.int32, (width, half), 0)
    place = lax.broadcasted_iota(jnp.int32, (width, half), 1)
    inside = (pixel >= 2 * place) & (pixel < 2 * place + 2)
    pick = jnp.where(inside, 0.25, 0.0).astype(bf16)
    for image in range(g_ref.shape[0]):
        for row in range(rows // 2):
            wide = dot(pick, g_ref[image, row * half : (row + 1) * half, :]).astype(bf16)
            out_ref[image, 2 * row] = wide
            out_ref[image, 2 * row + 1] = wide


def widen(idx, grad, rows, width):
    images, spots, chans = grad.shape
    step = images // 4
    block = pl.BlockSpec((step, spots, chans), lambda i: (i, 0, 0))
    out = pl.BlockSpec((step, rows, width, chans), lambda i: (i, 0, 0, 0))
    return call(
        widen_body,
        "widen",
        [(SMEM, idx), (block, grad)],
        [(out, struct((images, rows, width, chans), bf16))],
        grid=(4,),
    )


def conv_body(side, first, group, arrive, idx_ref, *refs):
    zh, zl = idx_ref[2], idx_ref[3]
    if first:
        xl, xa, xh, xd, wl, wo, ws, bl, bo, pre_ref, act_ref, xbuf, wbuf, acc, sems = refs
        chans = xl.shape[1]
        spots = xbuf.shape[0]
        begin = zh * (xl.shape[0] - spots)
        pairs = []
        for source, up, along in ((xl, zh, zl), (xa, zh, 1 - zl), (xh, 1 - zh, zl), (xd, 1 - zh, 1 - zl)):
            if source is xl:
                source = xl.at[at(begin, spots, side), :]
            pairs.append((source, xbuf.at[:, at((2 * up + along) * chans, chans, chans)]))
    else:
        xl, xa, wl, wo, ws, bl, bo, pre_ref, act_ref, xbuf, wbuf, acc, sems = refs
        chans = xl.shape[1] // 2
        spots = xbuf.shape[0]
        pairs = []
        for source, along in ((xl, zl), (xa, 1 - zl)):
            for up in range(2):
                pairs.append(
                    (
                        source.at[:, up * chans : (up + 1) * chans],
                        xbuf.at[:, at((2 * up + along) * chans, chans, chans)],
                    )
                )
    run_copies(slice_copies(group, idx_ref, wl, wo, ws, wbuf) + pairs, sems)
    arrive()
    if first:
        for begin, block in halves(spots, side):
            rows = slice(begin, begin + block)
            xbuf[rows, :] = gelu(xbuf[rows, :].astype(f32)).astype(bf16)
    acc[...] = jnp.zeros_like(acc)
    outs = 2 * wl.shape[2]
    for x in range(3):
        weights = lanes([wbuf[u, 3 * y + x] for y in range(3) for u in range(2)])
        for begin, block in halves(spots, side):
            product = dot(xbuf[begin : begin + block, :], weights)
            for y in range(3):
                place = begin + side * (2 - y)
                acc[x, place : place + block, :] += product[:, y * outs : (y + 1) * outs]
    own, other = bl[...], bo[...]
    bias = lanes([jnp.where(zh == 0, own, other), jnp.where(zh == 0, other, own)])
    for begin, block in halves(act_ref.shape[0], side):
        column = columns_of(block, outs, side)
        spot = at(begin + side + zh * side, block, side)
        left = pltpu.roll(acc[0, spot, :], 1, 0)
        right = pltpu.roll(acc[2, spot, :], block - 1, 0)
        pre = acc[1, spot, :] + bias
        pre = pre + jnp.where(column > 0, left, 0.0)
        pre = pre + jnp.where(column < side - 1, right, 0.0)
        pre_ref[begin : begin + block, :] = pre
        act_ref[begin : begin + block, :] = gelu(pre).astype(bf16)


def conv(side, idx, sources, own, other, group, bias, bias_other, first=False):
    taps, depth, outs = own.shape
    spots = sources[1].shape[0]
    rows = spots - side
    return call(
        functools.partial(conv_body, side, first, group),
        "conv",
        [(SMEM, idx)]
        + [(FAR, s) for s in sources]
        + [(FAR, own), (FAR, other[0]), (FAR, other[1])]
        + [(VMEM, bias.reshape(1, outs)), (VMEM, bias_other.reshape(1, outs))],
        [(VMEM, struct((rows, 2 * outs), f32)), (VMEM, struct((rows, 2 * outs), bf16))],
        [
            pltpu.VMEM((spots, depth), bf16),
            pltpu.VMEM((2, taps, depth, outs), bf16),
            pltpu.VMEM((3, spots + 2 * side, 2 * outs), f32),
            pltpu.SemaphoreType.DMA((2 * other[0].shape[0] + 5,)),
        ],
        spare=14 if first else 8,
    )


def spread_taps(side, grad, taps_ref):
    pixels, outs = grad.shape
    column = columns_of(pixels, outs, side)
    wide = grad.astype(f32)
    ahead = jnp.where(column < side - 1, pltpu.roll(wide, pixels - 1, 0), 0.0).astype(bf16)
    behind = jnp.where(column > 0, pltpu.roll(wide, 1, 0), 0.0).astype(bf16)
    edge = jnp.zeros((side, 3 * outs), bf16)
    taps_ref[:side, :] = edge
    taps_ref[side + pixels :, :] = edge
    taps_ref[side : side + pixels, :] = jnp.concatenate([ahead, grad, behind], axis=1)


def tap_block(side, taps_ref, begin, block):
    return lanes([taps_ref[at(begin + side * (2 - y), block, side), :] for y in range(3)])


def slope_body(side, arrive, idx_ref, keep_ref, recv_ref, pre_ref, mine_ref, theirs_ref, gp_ref):
    arrive()
    zh = idx_ref[2]
    half, outs = mine_ref.shape
    total = keep_ref[...] + recv_ref[...].astype(f32)
    spots = keep_ref.shape[0]
    pre = pre_ref[at(zh * (pre_ref.shape[0] - spots), spots, side), :]
    gp_ref[...] = (total * gelu_slope(pre)).astype(bf16)
    own = gp_ref[at(zh * (gp_ref.shape[0] - half), half, side), :]
    low, high = own[:, :outs], own[:, outs:]
    mine_ref[...] = jnp.where(zh == 0, low, high)
    theirs_ref[...] = jnp.where(zh == 0, high, low)


def slope_back(side, idx, keep, recv, pre, half):
    outs = pre.shape[1] // 2
    return call(
        functools.partial(slope_body, side),
        "slope_back",
        [(SMEM, idx), (VMEM, keep), (VMEM, recv), (LOAD, pre)],
        [
            (VMEM, struct((half, outs), bf16)),
            (VMEM, struct((half, outs), bf16)),
            (VMEM, struct(keep.shape, bf16)),
        ],
    )


def back_body(side, last, group, arrive, idx_ref, *refs):
    zh, zl = idx_ref[2], idx_ref[3]
    if last:
        valid_ref, grad_ref, x_ref, go_ref, far_ref, idk_ref, wl, wo, ws, po, ps = refs[:11]
        own_ref, give_ref, taps_ref, wbuf, idk_far, sems = refs[11:]
    else:
        keep_ref, recv_ref, pre_ref, wl, wo, ws, gp_ref, own_ref, give_ref, taps_ref, wbuf, sems = refs
    pairs = slice_copies(group, idx_ref, wl, wo, ws, wbuf)
    if last:
        pairs += flat_copies(9, idx_ref, po, ps, idk_far)
    copies = start_copies(pairs, sems)
    arrive()
    if last:
        grad = grad_ref[...]
    else:
        spots = gp_ref.shape[0]

        def window(ref):
            return ref[at(zh * (ref.shape[0] - spots), spots, side), :]

        total = window(keep_ref) + window(recv_ref).astype(f32)
        grad = (total * gelu_slope(window(pre_ref))).astype(bf16)
        gp_ref[...] = grad
    spread_taps(side, grad, taps_ref)
    depth, outs = wl.shape[1:]
    pixels = own_ref.shape[-2]
    start = zh * side
    for copy in copies:
        copy.wait()
    chans = depth // 4

    def rows(index):
        spot = at(index * chans, chans, chans)
        return lanes([wbuf[u, t, spot, :] for t in range(9) for u in range(2)])

    for target, along in ((give_ref, 1 - zl), (own_ref, zl)):
        if last:
            units = chans // idk_far.shape[2]
            for up in range(2):
                index = 2 * up + along
                weights = rows(index)
                near = idk_ref[at(index * chans, chans, chans), :]
                far = flat_rows(idk_far, index * units, units)
                apart = zh * (far_ref.shape[0] - pixels)
                for begin, block in halves(pixels, side):
                    here = at(zh * pixels + begin, block, side)
                    part = dot(tap_block(side, taps_ref, start + begin, block), weights, NT)
                    x = x_ref[here, at(index * chans, chans, chans)]
                    part = part * gelu_slope(x.astype(f32))
                    part = part + dot(go_ref[here, :], near, NT)
                    part = part + valid_ref[0] * dot(far_ref[at(apart + begin, block, side), :], far, NT)
                    target[up, begin : begin + block, :] = part.astype(target.dtype)
        else:
            weights = jnp.concatenate([rows(along), rows(2 + along)], axis=0)
            for begin, block in halves(pixels, side):
                part = dot(tap_block(side, taps_ref, start + begin, block), weights, NT)
                target[begin : begin + block, :] = part.astype(target.dtype)


def back(side, idx, sources, own, other, group, last=None):
    taps, depth, outs = own.shape
    spots = min(sources[0].shape[0], sources[-1].shape[0])
    copies = 2 * other[0].shape[0] + 1
    extra = []
    scratch = []
    if last:
        valid, full_x, go, cot_far, idk, pieces, half = last
        chans = depth // 4
        shape = (2, half, chans)
        results = []
        extra = [(FAR, pieces[0]), (FAR, pieces[1])]
        sources = list(sources) + [full_x, go, cot_far, idk]
        columns, size = idk.shape[1] // 128, pieces[0].shape[2]
        scratch = [pltpu.VMEM((columns, depth // size, size, 128), bf16)]
        copies += 2 * other[0].shape[0] * columns
    else:
        shape = (spots - side, depth // 2)
        results = [(VMEM, struct((spots, 2 * outs), bf16))]
    results += [(VMEM, struct(shape, f32)), (VMEM, struct(shape, bf16))]
    return call(
        functools.partial(back_body, side, bool(last), group),
        "back",
        [(SMEM, idx)]
        + ([(SMEM, last[0])] if last else [])
        + [(LOAD, source) for source in sources]
        + [(FAR, own), (FAR, other[0]), (FAR, other[1])]
        + extra,
        results,
        [pltpu.VMEM((spots + 2 * side, 6 * outs), bf16), pltpu.VMEM((2, taps, depth, outs), bf16)]
        + scratch
        + [pltpu.SemaphoreType.DMA((copies,))],
        spare=14 if last else 10,
    )


def put_blocks(idx_ref, keep_ref, give_ref, part, tap, first_block, size, begin=0):
    chip, core = idx_ref[0], idx_ref[1]
    for b in range(0, part.shape[0] // size, 2):
        even = part[b * size : (b + 1) * size, :]
        odd = part[(b + 1) * size : (b + 2) * size, :]
        mask = chip ^ ((first_block + b) // 2)
        slot = slot_of(mask, core, keep_ref.shape[0])
        give_slot = slot_of(mask, 1 - core, keep_ref.shape[0])
        rows = slice(begin + tap * size, begin + (tap + 1) * size)
        keep_ref[slot, rows, :] = jnp.where(core == 0, even, odd).astype(bf16)
        give_ref[give_slot, rows, :] = jnp.where(core == 0, odd, even).astype(bf16)


def weight_body(side, half, flat, arrive, idx_ref, gp_ref, *refs):
    if flat:
        full_ref, go_ref, bias_ref = refs[:3]
        refs = refs[3:]
    xl, xa, keep_ref, give_ref, xbuf, taps_ref, sems = refs
    arrive()
    zh, zl = idx_ref[2], idx_ref[3]
    chans = xl.shape[1] // 2
    spots = xbuf.shape[0]
    window = at(zh * (xl.shape[0] - spots), spots, side)
    pairs = []
    for source, along in ((xl, zl), (xa, 1 - zl)):
        for up in range(2):
            pairs.append(
                (
                    source.at[window, up * chans : (up + 1) * chans],
                    xbuf.at[:, at((2 * up + along) * chans, chans, chans)],
                )
            )
    run_copies(pairs, sems)
    wide = gp_ref.shape[1]
    outs = wide // 2
    spot = lax.broadcasted_iota(jnp.int32, (spots, wide), 0) - zh * side
    grad = gp_ref[at(zh * (gp_ref.shape[0] - spots), spots, side), :].astype(f32)
    grad = jnp.where((spot >= 0) & (spot < half), grad, 0.0)
    bias = jnp.sum(grad, axis=0, keepdims=True)
    spread_taps(side, grad.astype(bf16), taps_ref)
    blocks = 2 * keep_ref.shape[0]
    depth = xbuf.shape[1]
    size = depth // blocks
    for begin in range(0, depth, 256):
        values = xbuf[:, begin : begin + 256]
        for y in range(3):
            place = side * (2 - y)
            part = dot(values, taps_ref[place : place + spots, :], TN)
            for x in range(3):
                for u in range(2):
                    col = x * wide + u * outs
                    put_blocks(
                        idx_ref, keep_ref, give_ref, part[:, col : col + outs],
                        3 * y + x, begin // size, size, u * (9 * size + 16),
                    )
    for u in range(2):
        row = jnp.broadcast_to(bias[:, u * outs : (u + 1) * outs], (16, outs)).astype(bf16)
        for j in range(keep_ref.shape[0]):
            spot = slice(u * (9 * size + 16) + 9 * size, (u + 1) * (9 * size + 16))
            keep_ref[j, spot, :] = row
            give_ref[j, spot, :] = row
    if flat:
        first = 2 * (9 * size + 16)
        flat_pieces(1.0, idx_ref, full_ref, go_ref, bias_ref, keep_ref, give_ref, first)


def weight_grad(side, half, idx, grad, act, act_other, chips, flat=()):
    spots = half + side
    wide = grad.shape[1]
    outs = wide // 2
    depth = 2 * act.shape[1]
    rows = 2 * (9 * depth // (2 * chips) + 16)
    if flat:
        rows += flat_size(flat[0], flat[1], chips)
    return call(
        functools.partial(weight_body, side, half, bool(flat)),
        "weight_grad",
        [(SMEM, idx), (LOAD, grad)] + [(LOAD, a) for a in flat] + [(FAR, act), (FAR, act_other)],
        [(VMEM, struct((chips, rows, outs), bf16))] * 2,
        [
            pltpu.VMEM((spots, depth), bf16),
            pltpu.VMEM((spots + 2 * side, 3 * wide), bf16),
            pltpu.SemaphoreType.DMA((4,)),
        ],
        spare=10,
    )


def weight_one_body(side, arrive, idx_ref, mine_ref, theirs_ref, x_ref, *refs):
    keep_ref, give_ref, gp_ref, taps_ref = refs
    arrive()
    zh = idx_ref[2]
    half, outs = mine_ref.shape
    gp_ref[at(zh * half, half, side), :] = mine_ref[...]
    gp_ref[at((1 - zh) * half, half, side), :] = theirs_ref[...]
    grad = gp_ref[...]
    bias = jnp.sum(grad.astype(f32), axis=0, keepdims=True)
    spread_taps(side, grad, taps_ref)
    blocks = 2 * keep_ref.shape[0]
    spots, depth = x_ref.shape
    size = depth // blocks
    right = tap_block(side, taps_ref, 0, spots)
    for begin in range(0, depth, 256):
        part = dot(x_ref[:, begin : begin + 256], right, TN)
        for tap in range(9):
            put_blocks(
                idx_ref, keep_ref, give_ref, part[:, tap * outs : (tap + 1) * outs],
                tap, begin // size, size,
            )
    row = jnp.broadcast_to(bias, (16, outs)).astype(bf16)
    first = 9 * size + 16
    for j in range(keep_ref.shape[0]):
        keep_ref[j, 9 * size : first, :] = row
        give_ref[j, 9 * size : first, :] = row


def weight_one_grad(side, idx, mine, theirs, act_zero, chips):
    spots, depth = act_zero.shape
    outs = mine.shape[1]
    rows = 9 * depth // (2 * chips) + 16
    return call(
        functools.partial(weight_one_body, side),
        "weight_one_grad",
        [(SMEM, idx), (LOAD, mine), (LOAD, theirs), (LOAD, act_zero)],
        [(VMEM, struct((chips, rows, outs), bf16))] * 2,
        [
            pltpu.VMEM((spots, outs), bf16),
            pltpu.VMEM((spots + 2 * side, 3 * outs), bf16),
        ],
        spare=14,
    )


def fold_body(pairs, arrive, idx_ref, *refs):
    arrive()
    ins, (keep_ref, give_ref) = refs[: 2 * pairs], refs[2 * pairs :]
    half = keep_ref.shape[0]
    for i in range(2 * half):
        target = keep_ref if i < half else give_ref
        begin = 0
        for keep, recv in zip(ins[0::2], ins[1::2]):
            rows = keep.shape[1]
            total = keep[i].astype(f32) + recv[i].astype(f32)
            target[i % half, begin : begin + rows, :] = total.astype(bf16)
            begin += rows


def fold(idx, *arrays):
    blocks, _, wide = arrays[0].shape
    rows = sum(a.shape[1] for a in arrays[0::2])
    return call(
        functools.partial(fold_body, len(arrays) // 2),
        "fold",
        [(SMEM, idx)] + [(VMEM, a) for a in arrays],
        [(VMEM, struct((blocks // 2, rows, wide), bf16))] * 2,
    )


def last_body(slotted, rest, arrive, idx_ref, keep_in, recv_in, *targets):
    arrive()
    zh = idx_ref[2]

    def put(target, place, begin, rows):
        spot = at(begin, rows, 16)
        total = keep_in[0, spot, :].astype(f32) + recv_in[0, spot, :].astype(f32)
        target[place : place + rows, :] = total.astype(bf16)

    place = 0
    for begin, rows in slotted:
        put(targets[0], place, begin + zh * rows, rows)
        put(targets[1], place, begin + (1 - zh) * rows, rows)
        place += rows
    begin, rows = rest
    put(targets[-1], 0, begin, rows)


def last_fold(idx, keep, recv, slotted=(), rest=None):
    wide = keep.shape[2]
    rest = rest or (0, keep.shape[1])
    rows = sum(size for _, size in slotted)
    sizes = ([rows, rows] if slotted else []) + [rest[1]]
    return call(
        functools.partial(last_body, slotted, rest),
        "last_fold",
        [(SMEM, idx), (VMEM, keep), (VMEM, recv)],
        [(VMEM, struct((size, wide), bf16)) for size in sizes],
    )


def final_body(parts, arrive, idx_ref, own_ref, sib_ref, *refs):
    arrive()
    outs, stages, sems = refs[: 2 * len(parts)], refs[2 * len(parts) : -1], refs[-1]
    chip, core = idx_ref[0], idx_ref[1]
    chips, _, wide = own_ref.shape
    first = 0
    copies = []

    def store(source, target):
        copies.append(pltpu.make_async_copy(source, target, sems.at[len(copies)]))
        copies[-1].start()

    for n, part in enumerate(parts):
        grad_ref, bias_ref, stage = outs[2 * n], outs[2 * n + 1], stages[n]
        size = part[0] // (2 * chips)
        columns = 1 if len(part) == 1 else part[1] // wide
        end = first + size * (9 if len(part) == 1 else columns)
        for c in range(columns):
            row = own_ref[0, end + c : end + c + 1, :].astype(f32)
            bias_ref[:, c * wide : (c + 1) * wide] = row
        for n_row, begin in enumerate(range(first, end, size)):
            for j in range(chips):
                for source, owner in ((own_ref, core), (sib_ref, 1 - core)):
                    home = chip ^ mask_of(j, owner, chips)
                    spot = at((2 * home + owner) * size, size, size)
                    piece = source[j, begin : begin + size, :].astype(f32)
                    if len(part) == 1:
                        stage[n_row, spot, :] = piece
                    else:
                        stage[spot, n_row * wide : (n_row + 1) * wide] = piece
            if len(part) == 1:
                store(stage.at[n_row], grad_ref.at[n_row])
        if len(part) > 1:
            store(stage, grad_ref)
        first = end + 16
    for copy in copies:
        copy.wait()


def final_grads(idx, own, sib, parts):
    wide = own.shape[2]
    results, stages = [], []
    for part in parts:
        shape = (9, part[0], wide) if len(part) == 1 else part
        results += [(FAR, struct(shape, f32)), (VMEM, struct((1, shape[-1]), f32))]
        stages.append(pltpu.VMEM(shape, f32))
    copies = sum(9 if len(part) == 1 else 1 for part in parts)
    return call(
        functools.partial(final_body, parts),
        "final_grads",
        [(SMEM, idx), (VMEM, own), (VMEM, sib)],
        results,
        stages + [pltpu.SemaphoreType.DMA((copies,))],
    )


def flat_pieces(gain, idx_ref, x_ref, go_ref, bias_ref, keep_ref, give_ref, first):
    chip, core = idx_ref[0], idx_ref[1]
    chips, _, wide = keep_ref.shape
    columns = go_ref.shape[1] // wide
    size = x_ref.shape[1] // (2 * chips)
    bias = jnp.concatenate(
        [bias_ref[:, c * wide : (c + 1) * wide] for c in range(columns)]
        + [jnp.zeros((16 - columns, wide), f32)],
        axis=0,
    ).astype(bf16)
    for j in range(chips):
        keep_ref[j, first + columns * size :, :] = bias
        give_ref[j, first + columns * size :, :] = bias
    for begin in range(0, x_ref.shape[1], 256):
        part = gain * dot(x_ref[:, begin : begin + 256], go_ref[...], TN)
        for b in range(0, 256 // size, 2):
            mask = chip ^ ((begin // size + b) // 2)
            slot = slot_of(mask, core, chips)
            give_slot = slot_of(mask, 1 - core, chips)
            for c in range(columns):
                even = part[b * size : (b + 1) * size, c * wide : (c + 1) * wide]
                odd = part[(b + 1) * size : (b + 2) * size, c * wide : (c + 1) * wide]
                spot = slice(first + c * size, first + (c + 1) * size)
                keep_ref[slot, spot, :] = jnp.where(core == 0, even, odd).astype(bf16)
                give_ref[give_slot, spot, :] = jnp.where(core == 0, odd, even).astype(bf16)


def flat_size(x, go, chips):
    return (go.shape[1] // 128) * (x.shape[1] // (2 * chips)) + 16


def outer_body(gain, arrive, idx_ref, x_ref, go_ref, bias_ref, keep_ref, give_ref):
    arrive()
    flat_pieces(gain, idx_ref, x_ref, go_ref, bias_ref, keep_ref, give_ref, 0)


def outer(idx, x, go, gain, bias, chips):
    return call(
        functools.partial(outer_body, gain),
        "outer",
        [(SMEM, idx), (LOAD, x), (LOAD, go), (LOAD, bias)],
        [(VMEM, struct((chips, flat_size(x, go, chips), 128), bf16))] * 2,
        spare=8,
    )


def start_body(arrive, idx_ref, valid_ref, cot_ref, outk_ref, go_ref, bias_ref, own_ref, give_ref):
    arrive()
    zl = idx_ref[3]
    masked = cot_ref[...].astype(f32) * valid_ref[0]
    go_ref[...] = masked.astype(bf16)
    bias_ref[...] = jnp.sum(masked, axis=0, keepdims=True)
    chans = outk_ref.shape[0] // 4
    block = cot_ref.shape[0] // 4
    for target, along in ((give_ref, 1 - zl), (own_ref, zl)):
        weights = jnp.concatenate(
            [outk_ref[at((2 * up + along) * chans, chans, chans), :] for up in range(2)], axis=0
        )
        for begin in range(0, cot_ref.shape[0], block):
            part = post_gain * dot(go_ref[begin : begin + block, :], weights, NT)
            target[begin : begin + block, :] = part.astype(target.dtype)


def start_back(idx, valid, cot, outk):
    spots, outs = cot.shape
    half = outk.shape[0] // 2
    return call(
        start_body,
        "start_back",
        [(SMEM, idx), (SMEM, valid), (LOAD, cot), (LOAD, outk)],
        [
            (VMEM, struct(cot.shape, bf16)),
            (VMEM, struct((1, outs), f32)),
            (VMEM, struct((spots, half), f32)),
            (VMEM, struct((spots, half), bf16)),
        ],
    )


def rows_body(side, arrive, idx_ref, own_ref, recv_ref, keep_ref, give_ref):
    arrive()
    zh = idx_ref[2]
    spots = keep_ref.shape[0]
    apart = own_ref.shape[0] - spots
    for target, begin in ((give_ref, (1 - zh) * apart), (keep_ref, zh * apart)):
        spot = at(begin, spots, side)
        total = own_ref[spot, :] + recv_ref[spot, :].astype(f32)
        target[...] = total.astype(target.dtype)


def rows_sum(side, idx, own, recv, spots):
    shape = (spots, own.shape[1])
    return call(
        functools.partial(rows_body, side),
        "rows_sum",
        [(SMEM, idx), (LOAD, own), (LOAD, recv)],
        [(VMEM, struct(shape, f32)), (VMEM, struct(shape, bf16))],
    )


def slots_body(arrive, idx_ref, own_ref, recv_ref, keep_ref, give_ref):
    arrive()
    zh = idx_ref[2]
    for target, slot in ((give_ref, 1 - zh), (keep_ref, zh)):
        total = own_ref[slot] + recv_ref[slot].astype(f32)
        target[...] = total.astype(bf16)


def slots_sum(idx, own, recv):
    shape = struct(own.shape[1:], bf16)
    return call(
        slots_body,
        "slots_sum",
        [(SMEM, idx), (VMEM, own), (VMEM, recv)],
        [(VMEM, shape), (VMEM, shape)],
    )


def input_body(arrive, idx_ref, keep_ref, recv_ref, out_ref):
    arrive()
    zh = idx_ref[2]
    half = keep_ref.shape[0]
    out_ref[at(zh * half, half, half), :] = keep_ref[...]
    out_ref[at((1 - zh) * half, half, half), :] = recv_ref[...]


def input_grad(idx, keep, recv):
    half, chans = keep.shape
    return call(
        input_body,
        "input_grad",
        [(SMEM, idx), (VMEM, keep), (VMEM, recv)],
        [(VMEM, struct((2 * half, chans), bf16))],
    )


def whole_body(side, arrive, idx_ref, xl, xa, xh, xd, rh, rl, x_ref, act_ref, sems):
    arrive()
    zh, zl = idx_ref[2], idx_ref[3]
    chans = xl.shape[1]
    spots = xa.shape[0]
    rest = xl.shape[0] - spots
    window, outside = at(zh * rest, spots, side), at((1 - zh) * spots, rest, side)

    def cols(up, along):
        return at((2 * up + along) * chans, chans, chans)

    run_copies(
        [
            (xl, x_ref.at[:, cols(zh, zl)]),
            (xa, x_ref.at[window, cols(zh, 1 - zl)]),
            (xh, x_ref.at[window, cols(1 - zh, zl)]),
            (xd, x_ref.at[window, cols(1 - zh, 1 - zl)]),
            (rl.at[0], x_ref.at[outside, cols(zh, 1 - zl)]),
            (rh, x_ref.at[outside, cols(1 - zh, zl)]),
            (rl.at[1], x_ref.at[outside, cols(1 - zh, 1 - zl)]),
        ],
        sems,
    )
    block = x_ref.shape[0] // 8
    for begin in range(0, x_ref.shape[0], block):
        rows = slice(begin, begin + block)
        act_ref[rows, :] = gelu(x_ref[rows, :].astype(f32)).astype(bf16)


def whole_input(side, idx, *parts):
    spots, chans = parts[0].shape
    return call(
        functools.partial(whole_body, side),
        "whole_input",
        [(SMEM, idx)] + [(FAR, p) for p in parts],
        [(VMEM, struct((spots, 4 * chans), bf16))] * 2,
        [pltpu.SemaphoreType.DMA((7,))],
    )


def join_body(arrive, idx_ref, own, recv, far_own, far_recv, out, sems):
    arrive()
    zh, zl = idx_ref[2], idx_ref[3]
    half = own.shape[0]
    chans = own.shape[1] // 2
    pairs = []
    for source, up, along in ((own, zh, zl), (recv, zh, 1 - zl), (far_own, 1 - zh, zl), (far_recv, 1 - zh, 1 - zl)):
        for slot in range(2):
            spot = at((2 * slot + along) * chans, chans, chans)
            target = out.at[at(up * half, half, half), spot]
            pairs.append((source.at[:, slot * chans : (slot + 1) * chans], target))
    run_copies(pairs, sems)


def join(idx, *parts):
    half, wide = parts[0].shape
    return call(
        join_body,
        "join",
        [(SMEM, idx)] + [(FAR, p) for p in parts],
        [(VMEM, struct((2 * half, 2 * wide), bf16))],
        [pltpu.SemaphoreType.DMA((8,))],
    )


def finish_body(arrive, idx_ref, valid_ref, x_ref, act_ref, idk_ref, outk_ref, ib_ref, out_ref):
    arrive()
    block = x_ref.shape[0] // 4
    for begin in range(0, x_ref.shape[0], block):
        rows = slice(begin, begin + block)
        identity = dot(x_ref[rows, :], idk_ref[...]) + ib_ref[...]
        branch = dot(act_ref[rows, :], outk_ref[...])
        out_ref[rows, :] = ((identity + post_gain * branch) * valid_ref[0]).astype(bf16)


def finish(idx, valid, x, act, idk, outk, ib):
    outs = idk.shape[1]
    return call(
        finish_body,
        "finish",
        [(SMEM, idx), (SMEM, valid), (LOAD, x), (LOAD, act), (LOAD, idk), (LOAD, outk)]
        + [(VMEM, ib.reshape(1, outs))],
        [(VMEM, struct((x.shape[0], outs), bf16))],
        spare=8,
    )


def flip(value, axis):
    return lax.ppermute(value, axis, [(0, 1), (1, 0)])


def cross(value, step, chips):
    pairs = []
    for chip in range(chips):
        for core in range(2):
            other = chip ^ step_bits(core, chips)[step]
            pairs.append((2 * chip + core, 2 * other + core))
    return lax.ppermute(value, DP, pairs)


def hops(value, chips):
    blocks = [value]
    for i in range(1, chips):
        pairs = []
        for chip in range(chips):
            for core in range(2):
                bits = step_bits(core, chips)
                mask = sum(bit for n, bit in enumerate(bits) if i >> (len(bits) - 1 - n) & 1)
                pairs.append((2 * (chip ^ mask) + core, 2 * chip + core))
        blocks.append(lax.ppermute(value, DP, pairs))
    return blocks


def swap(pieces, axis):
    return lax.all_to_all(pieces, axis, split_axis=0, concat_axis=0, tiled=True)


def after(value, other):
    return lax.optimization_barrier((value, other))[0]


def rows_of(value, start, size):
    return lax.dynamic_slice_in_dim(value, start, size, 0)


def local(
    pixels,
    counts,
    kernel_one,
    bias_one,
    kernel_two,
    bias_two,
    kernel_three,
    bias_three,
    out_kernel,
    identity_kernel,
    identity_bias,
    cotangent,
):
    images, rows, width, chans = pixels.shape
    side = width // 2
    spots = side * side
    half = spots // 2
    window = half + halo * side
    outs = cotangent.shape[3]
    chips = lax.axis_size("chip")
    chip, core, zh, zl = [lax.axis_index(a) for a in ("chip", "core", "zh", "zl")]
    idx = jnp.stack([chip, core, zh, zl]).astype(jnp.int32)
    taps = lambda kernel: kernel.reshape((9,) + kernel.shape[2:])
    one, two, three = taps(kernel_one), taps(kernel_two), taps(kernel_three)

    own_count = lax.dynamic_index_in_dim(counts, 2 * chip + core, 0, keepdims=True)
    valid = (own_count > 0).astype(f32)

    place = 2 * chip + core

    def units_of(kernel, size):
        if kernel.ndim == 3:
            block = kernel.shape[1] // (2 * chips)
            return lax.dynamic_slice_in_dim(kernel, place * block, block, 1)
        block = kernel.shape[0] // (2 * chips)
        block = lax.dynamic_slice_in_dim(kernel, place * block, block, 0)
        block = block.reshape(-1, size, block.shape[1] // 128, 128)
        return block.transpose(2, 0, 1, 3).reshape(-1, size, 128)

    steps = chips.bit_length() - 1

    def start_spread(piece, *others):
        return jnp.concatenate(after((piece[None], cross(piece[None], steps - 1, chips)), others))

    def end_spread(own, *others):
        for step in reversed(range(steps - 1)):
            own = jnp.concatenate(after((own, cross(own, step, chips)), others))
        return own, flip(own, "core")

    last = [idx]

    def turn(*others):
        return after(idx, (last[0],) + others)

    def ran(results):
        last[0] = results[-1] if isinstance(results, (list, tuple)) else results
        return results

    size = two.shape[1] // (2 * chips)
    deep = two.shape[1]
    cot = cotangent.reshape(spots, outs)
    one_piece = flip(units_of(one, size), "zh")
    pooled = ran(pool(pixels))
    go, identity_bias_grad, ga_own, ga_give = ran(start_back(turn(), valid, cot, out_kernel))
    bias_other = flip(after(jnp.stack([bias_one, bias_two, bias_three]), go), "zh")
    two_piece = units_of(after(two, pooled), size)
    last_piece = jnp.concatenate([units_of(after(k, pooled), size) for k in (three, identity_kernel)])
    cot_rows = rows_of(after(cot, pooled), (1 - zh) * half, half)
    xl = swap(after(pooled, (one_piece, two_piece, last_piece, cot_rows, ga_give)), DP)
    xl = xl.reshape(spots, chans)
    two_piece = flip(after(two_piece, one_piece), "zh")

    apart = spots - window
    xa = flip(rows_of(xl, zh * apart, window), "zl")
    xh = flip(rows_of(xl, (1 - zh) * apart, window), "zh")
    rest = spots - window
    rest_own = rows_of(xl, (1 - zh) * window, rest)
    rest_high = rows_of(xl, zh * window, rest)
    two_near = start_spread(after(two_piece, xl))
    one_near = start_spread(after(one_piece, xl), xh, xa, two_near, bias_other)
    xd = flip(xh, "zl")
    last_piece = flip(after(last_piece, xh), "zh")
    two_other = end_spread(two_near, xd)
    one_other = end_spread(one_near, xd, two_other[0], last_piece)
    ga_recv = flip(after(ga_give, xd), "zl")
    rest_high = flip(after(rest_high, xd), "zh")

    pre_one, act_one = ran(
        conv(
            side, turn(), (xl, xa, xh, xd), one, one_other, 0, bias_one, bias_other[0], True
        )
    )
    act_one_other = flip(act_one, "zl")
    ga_own, ga_give = ran(rows_sum(side, turn(), ga_own, ga_recv, half + (halo - 3) * side))
    pre_two, act_two = ran(
        conv(side, turn(), (act_one, act_one_other), two, two_other, 0, bias_two, bias_other[1])
    )
    act_two_other = flip(act_two, "zl")
    ga_recv = flip(after(ga_give, act_two), "zh")
    last_other = jnp.stack(after(hops(after(last_piece, act_one), chips), act_two))
    last_other = last_other, flip(last_other, "core")
    pre_three, act_three = ran(
        conv(side, turn(), (act_two, act_two_other), three, last_other, 0, bias_three, bias_other[2])
    )
    rest_low = flip(jnp.stack(after((rest_own, rest_high), act_three)), "zl")
    cot_far = flip(after(cot_rows, act_three), "zh")
    own_rows = rows_of(act_three, zh * (halo - 3) * side, half)

    gp_three, ga_own, ga_give = ran(
        back(side, turn(), (ga_own, ga_recv, pre_three), three, last_other, 0)
    )
    ga_recv = flip(ga_give, "zl")
    full_x, act_zero = ran(whole_input(side, turn(), xl, xa, xh, xd, rest_high, rest_low))
    keep_three, give_three = ran(
        weight_grad(
            side, half, turn(), gp_three, act_two, act_two_other, chips, (full_x, go, identity_bias_grad)
        )
    )
    gp_two, ga_own, ga_give = ran(
        back(side, turn(), (ga_own, ga_recv, pre_two), two, two_other, 0)
    )
    ga_recv = flip(ga_give, "zl")
    keep_two, give_two = ran(weight_grad(side, half, turn(cot_far), gp_two, act_one, act_one_other, chips))

    gp_mine, gp_theirs, gp_one = ran(slope_back(side, turn(), ga_own, ga_recv, pre_one, half))
    gp_theirs = flip(gp_theirs, "zh")
    recv_three = flip(after(give_three, gp_one), "core")
    recv_two = flip(after(give_two, gp_one), "core")
    gx_own, gx_give = ran(
        back(
            side, turn(), (gp_one,), one, one_other, 0,
            (valid, full_x, go, cot_far, identity_kernel, last_other, half),
        )
    )

    def folds(keep, recv, first, *others):
        for step in range(first, steps):
            keep, give = ran(fold(turn(*others), keep, recv))
            recv = cross(give, step, chips)
        return keep, recv

    keep_deep, give_deep = ran(fold(turn(gp_theirs), keep_three, recv_three, keep_two, recv_two))
    recv_deep = cross(give_deep, 0, chips)
    gx_recv = flip(after(gx_give, keep_deep), "zl")
    own_rows = after(own_rows, keep_deep)
    near_rows = flip(own_rows, "zl")
    far_rows = flip(own_rows, "zh")
    keep_one, give_one = ran(weight_one_grad(side, turn(), gp_mine, gp_theirs, act_zero, chips))
    recv_one = flip(give_one, "core")
    keep_deep, recv_deep = folds(keep_deep, recv_deep, 1, far_rows)
    gx_keep, gx_give = ran(slots_sum(turn(), gx_own, gx_recv))
    gx_recv = flip(gx_give, "zh")
    keep_one, give_one = ran(fold(turn(), keep_one, recv_one))
    recv_one = cross(give_one, 0, chips)
    slot = 9 * size + 16
    flat = keep_three.shape[1] - 2 * slot
    keep_deep, give_deep, id_rows = ran(
        last_fold(
            turn(), keep_deep, recv_deep, ((0, slot), (2 * slot + flat, slot)), (2 * slot, flat)
        )
    )
    recv_deep = flip(give_deep, "zh")
    far_near_rows = flip(after(far_rows, keep_deep), "zl")
    keep_one, recv_one = folds(keep_one, recv_one, 1)
    full_three = ran(join(turn(), own_rows, near_rows, far_rows, far_near_rows))
    keep_out, give_out = ran(outer(turn(), full_three, go, post_gain, identity_bias_grad, chips))
    recv_out = flip(give_out, "core")
    (total_one,) = ran([last_fold(turn(), keep_one, recv_one)])
    keep_out, give_out = ran(fold(turn(), keep_out, recv_out))
    recv_out = cross(give_out, 0, chips)
    deep_rows = (after(keep_deep, keep_out).astype(f32) + recv_deep.astype(f32)).astype(bf16)
    deep_rows = jnp.concatenate([deep_rows, id_rows])
    near_deep = start_spread(deep_rows)
    block_out = ran(
        finish(turn(deep_rows), valid, full_x, full_three, identity_kernel, out_kernel, identity_bias)
    )
    keep_out, recv_out = folds(keep_out, recv_out, 1)
    gx = ran(input_grad(turn(), gx_keep, gx_recv))
    gx = swap(gx.reshape(images, rows * width // 4, chans), DP)
    (total_out,) = ran([last_fold(turn(), keep_out, recv_out)])
    near_one = start_spread(jnp.concatenate([total_one, total_out]))
    pixels_grad = ran(widen(turn(near_one, near_deep), gx, rows, width))
    all_deep = end_spread(near_deep, pixels_grad)
    all_one = end_spread(near_one)
    (
        kernel_three_grad,
        bias_three_grad,
        kernel_two_grad,
        bias_two_grad,
        identity_kernel_grad,
        identity_bias_grad,
    ) = ran(final_grads(turn(), *all_deep, ((deep,), (deep,), identity_kernel.shape)))
    kernel_one_grad, bias_one_grad, out_kernel_grad, _ = ran(
        final_grads(turn(), *all_one, ((one.shape[1],), out_kernel.shape))
    )

    return (
        block_out.reshape(cotangent.shape),
        pixels_grad,
        kernel_one_grad.reshape(kernel_one.shape),
        bias_one_grad[0],
        kernel_two_grad.reshape(kernel_two.shape),
        bias_two_grad[0],
        kernel_three_grad.reshape(kernel_three.shape),
        bias_three_grad[0],
        out_kernel_grad,
        identity_kernel_grad,
        identity_bias_grad[0],
    )


def solution(mesh):
    members = mesh.devices.size // mesh.shape["mp"]
    fine = Mesh(
        mesh.devices.reshape(members // 2, 2, 2, mesh.shape["mp"] // 2),
        ("chip", "core", "zh", "zl"),
    )
    return jax.shard_map(
        local,
        mesh=fine,
        in_specs=(
            P(None, DP, None, MP),
            P(),
            P(None, None, None, MP),
            P(MP),
            P(None, None, None, MP),
            P(MP),
            P(None, None, None, MP),
            P(MP),
            P(None, MP),
            P(None, MP),
            P(MP),
            P(DP, None, None, MP),
        ),
        out_specs=(
            P(DP, None, None, MP),
            P(None, DP, None, MP),
            P(None, None, None, MP),
            P(MP),
            P(None, None, None, MP),
            P(MP),
            P(None, None, None, MP),
            P(MP),
            P(None, MP),
            P(None, MP),
            P(MP),
        ),
        check_vma=False,
    )
```
